32 devices in a mesh: groups: 2 (over y), expo: 4 (over z), tile: 4 (over x, core).
Axes of the slice: x: 2, y: 2, z: 4, core: 2. Of those that a mesh axis runs over, the one named last changes fastest.
Arguments:
- template: bfloat16 [8, 64, 4096], P(('groups', 'expo'), 'tile'), parts along dimension 0
- science: bfloat16 [8, 1, 64, 4096], P(('groups', 'expo'), None, 'tile'), parts along dimension 0
- plan: int32 [8], P('groups'), parts along dimension 0, may hold values from 0 to 3, as said below
- orders: int32 [6, 2], replicated, may hold values from 0 to 2
- coadd_weight: float32 [8, 1], P(('groups', 'expo')), parts along dimension 0, may hold values from 0.3 to 3
- intersection: int32 [8, 1], P(('groups', 'expo')), parts along dimension 0, may hold values 0 or 1
Outputs:
- coadd: float32 [2, 64, 4096], P('groups', 'tile', 'expo'), parts along dimension 0
- coeffs: float32 [8, 1, 13], P(('groups', 'expo')), parts along dimension 0
The draws below stay inside these ranges and needn't reach their ends.
There are 2 independent parts, one for each index of `groups`. The reference program is written for one: setup_inputs(seed, part) draws one part's arguments, and reference() takes and returns one part's arrays. A program takes and returns all parts, laid end to end along the dimension named above; an argument that names none is the same for every part. Nothing has to cross between parts.
Inputs may be any that keep to these rules, and one draw needn't show every extreme that they name: `plan`: a permutation of the group's patch indices.
All inputs are finite; a program needn't handle non-finite values. No bound on the sum of `intersection` on one device may be relied on, other than what follows from the above.
Results may differ from the reference program's by a relative error of at most 0.0061.
Values may be sent and summed in bfloat16 or wider, within the bound.
No kernel may reach another device: no remote copies, remote signals or barrier semaphores. Data moves between devices by JAX's collectives and lax.ppermute only.
A program may use at most 64 MiB of HBM per device.

```python
import math
import jax
import jax.numpy as jnp
from jax import lax

W = 4096
HALF = 15
NB = 6
NU = 13
ROWS = 64
EXPOS = 4
PATCHES = 4
STEPS = 1


def template_field(key):
    field = jax.random.normal(jax.random.fold_in(key, 11), (PATCHES, ROWS, W), jnp.float32)
    return jnp.clip(field, -6.0, 6.0)


def plan_ids(key):
    order_ids = jax.random.permutation(jax.random.fold_in(key, 41), PATCHES)
    return order_ids.astype(jnp.int32)


def draw_template(key, part):
    return template_field(key).astype(jnp.bfloat16)


def draw_plan(key, part):
    return plan_ids(key)


def draw_science(key, part):
    field = template_field(key)
    picked = field[plan_ids(key)[:STEPS]]
    gains = jnp.exp(jax.random.uniform(jax.random.fold_in(key, 13), (EXPOS, STEPS), jnp.float32, -0.7, 0.7))
    shifts = jax.random.randint(jax.random.fold_in(key, 14), (EXPOS, STEPS, 2), -1, 2)
    noise = 0.5 * jax.random.normal(jax.random.fold_in(key, 15), (EXPOS, STEPS, ROWS, W), jnp.float32)

    def one_image(image, shift_pair):
        moved = jnp.roll(image, shift_pair[0], axis=0)
        return jnp.roll(moved, shift_pair[1], axis=1)
    moved_all = jax.vmap(jax.vmap(one_image, in_axes=(0, 0)), in_axes=(None, 0))(picked, shifts)
    return (gains[:, :, None, None] * moved_all + noise).astype(jnp.bfloat16)


def touch_ends(drawn, stream_key, least, high):
    longest = drawn.shape.index(max(drawn.shape))
    spots = []
    for shift in (0, 1):
        where = [jax.random.randint(jax.random.fold_in(stream_key, axis), (), 0, length) for axis, length in enumerate(drawn.shape)]
        where[longest] = (where[longest] + shift) % drawn.shape[longest]
        spots.append(tuple(where))
    return drawn.at[spots[0]].set(least).at[spots[1]].set(high)


def levels(stream_key, dims, split, smallest, largest):
    level, own = 1.0, jax.random.fold_in(stream_key, 6)
    for axis_at, blocks in split:
        draws = jnp.exp(jax.random.uniform(jax.random.fold_in(own, axis_at), (blocks,), jnp.float32, smallest / len(split), largest / len(split)))
        level = level * jnp.repeat(draws, dims[axis_at] // blocks).reshape([-1 if axis == axis_at else 1 for axis in range(len(dims))])
    return level


def setup_inputs(seed: int = 0, part: int = 0) -> dict:
    keys = jax.random.split(jax.random.key(seed), 7)
    part_keys = jax.random.split(jax.random.fold_in(keys[6], part), 7)
    return {
        "template": draw_template(jax.random.fold_in(jax.random.fold_in(keys[6], part), 71), part),
        "science": draw_science(jax.random.fold_in(jax.random.fold_in(keys[6], part), 71), part),
        "plan": draw_plan(jax.random.fold_in(jax.random.fold_in(keys[6], part), 71), part),
        "orders": touch_ends(jax.random.randint(keys[3], (NB, 2), 0, 3), jax.random.fold_in(keys[3], 1), 0, 2).astype(jnp.int32),
        "coadd_weight": jnp.clip(jnp.exp(math.log(3.0) - 2.3025851 * jax.random.uniform(part_keys[4], (EXPOS, STEPS), jnp.float32) ** levels(part_keys[4], (EXPOS, STEPS), ((0, 4),), -0.2, 0.2)), 0.3, 3.0),
        "intersection": touch_ends((jax.random.randint(part_keys[5], (EXPOS, STEPS), 0, 4) < 3).astype(jnp.int32), jax.random.fold_in(part_keys[5], 1), 0, 1),
    }


SIGMAS = (0.8, 1.4, 2.2, 3.0, 4.0, 5.5)
RIDGE = 0.05

def make_filters(orders):
    taps_pos = jnp.arange(2 * HALF + 1).astype(jnp.float32) - HALF
    row_list = []
    col_list = []
    for basis in range(NB):
        sigma = SIGMAS[basis]
        envelope = jnp.exp(-taps_pos * taps_pos / (2.0 * sigma * sigma))

        def power(order):
            return jnp.where(order == 0, 1.0, jnp.where(order == 1, taps_pos, taps_pos * taps_pos))
        row_filter = envelope * power(orders[basis, 0])
        col_filter = envelope * power(orders[basis, 1])
        row_list.append(row_filter / jnp.sqrt(jnp.sum(row_filter * row_filter)))
        col_list.append(col_filter / jnp.sqrt(jnp.sum(col_filter * col_filter)))
    return (jnp.stack(row_list).astype(jnp.bfloat16), jnp.stack(col_list).astype(jnp.bfloat16))

def convolve(patch, row_filters, col_filters):
    padded = jnp.pad(patch, ((HALF, HALF), (0, 0))).astype(jnp.float32)
    row_taps = row_filters.astype(jnp.float32)
    col_taps = col_filters.astype(jnp.float32)
    rowconv = jnp.zeros((NB, ROWS, W), jnp.float32)
    for tap in range(2 * HALF + 1):
        rowconv = rowconv + row_taps[:, tap][:, None, None] * padded[None, tap:tap + ROWS, :]
    rowconv = rowconv.astype(jnp.bfloat16)
    padded_cols = jnp.pad(rowconv, ((0, 0), (0, 0), (HALF, HALF))).astype(jnp.float32)
    conv = jnp.zeros((NB, ROWS, W), jnp.float32)
    for tap in range(2 * HALF + 1):
        conv = conv + col_taps[:, tap][:, None, None] * padded_cols[:, :, tap:tap + W]
    return conv

def reference(template, science, plan, orders, coadd_weight, intersection):
    row_filters, col_filters = make_filters(orders)
    column_pos = 2.0 * (jnp.arange(W).astype(jnp.float32) + 0.5) / W - 1.0
    coadds = []
    fitted = []
    for step in range(STEPS):
        patch = template[plan[step]]
        conv = convolve(patch, row_filters, col_filters)
        fields = jnp.concatenate([conv, conv * column_pos, jnp.ones((1, ROWS, W), jnp.float32)], axis=0)
        fields = fields.reshape(NU, ROWS * W)
        normal_matrix = jnp.dot(fields, fields.T, precision=lax.Precision.HIGHEST)
        normal_matrix = normal_matrix + RIDGE * (jnp.trace(normal_matrix) / NU) * jnp.eye(NU, dtype=jnp.float32)
        exposure_image = science[:, step].astype(jnp.float32).reshape(EXPOS, ROWS * W)
        projections = jnp.dot(exposure_image, fields.T, precision=lax.Precision.HIGHEST)
        factor = jnp.linalg.cholesky(normal_matrix)
        coeffs = jax.scipy.linalg.cho_solve((factor, True), projections.T).T
        model = jnp.dot(coeffs, fields, precision=lax.Precision.HIGHEST)
        difference = exposure_image - model
        weights = coadd_weight[:, step] * intersection[:, step].astype(jnp.float32)
        coadds.append(jnp.dot(weights, difference, precision=lax.Precision.HIGHEST).reshape(ROWS, W))
        fitted.append(coeffs)
    return (jnp.stack(coadds), jnp.stack(fitted, axis=1))
```

```python
import functools

import jax
import jax.numpy as jnp
import numpy as np
from jax import lax
from jax.experimental import pallas as pl
from jax.experimental.pallas import tpu as pltpu
from jax.sharding import PartitionSpec as P

HALF = 15
NB = 6
NU = 13
LANES = 128
PAIRS = [(j, k) for j in range(NB) for k in range(j, NB)]

SIGMAS = (0.8, 1.4, 2.2, 3.0, 4.0, 5.5)
RIDGE = 0.05


def power_of(pos, order):
    return jnp.where(order == 0, 1.0, jnp.where(order == 1, pos, pos * pos))


def tap_values(pos, sigma, order):
    value = jnp.exp(-pos * pos / (2.0 * sigma * sigma)) * power_of(pos, order)
    return jnp.where(jnp.abs(pos) <= HALF, value, 0.0)


def tap_norm(sigma, order):
    pos = lax.broadcasted_iota(jnp.int32, (8, LANES), 1).astype(jnp.float32) - HALF
    value = tap_values(pos, sigma, order)
    return jnp.sqrt(jnp.sum(value * value, axis=1, keepdims=True))[:1]


def send_kernel(template_ref, science_ref, out_ref):
    parts, rows, wide = out_ref.shape
    width = template_ref.shape[1]
    chunk = width // parts
    ext = chunk + LANES
    blank = jnp.zeros((rows, LANES), template_ref.dtype)
    for part in range(parts):
        start = part * chunk
        left = template_ref[:, start - LANES : start] if part else blank
        right = template_ref[:, start + chunk : start + chunk + LANES] if part < parts - 1 else blank
        whole = jnp.concatenate([left, template_ref[:, start : start + chunk], right], axis=1)
        out_ref[part, :, :ext] = whole[:, LANES - HALF : LANES - HALF + ext]
        out_ref[part, :, ext:] = science_ref[:, start : start + chunk]


def pick_kernel(owner_ref, recv_ref, out_ref):
    ext = out_ref.shape[2]
    block = recv_ref[owner_ref[0], :, :ext]
    for part in range(out_ref.shape[0]):
        out_ref[part] = block


def column_positions(first_col, block, width):
    col = lax.broadcasted_iota(jnp.int32, (8, LANES), 1) + (first_col + block * LANES)
    return 2.0 * (col.astype(jnp.float32) + 0.5) / width - 1.0


def fit_kernel(where_ref, orders_ref, weight_ref, hits_ref, patch_ref, recv_ref, conv_ref, sums_ref,
               row_ref, parts_ref, *, width):
    tile_at = where_ref[0]
    expo_at = where_ref[1]
    tiles, rows, ext = patch_ref.shape
    expos = recv_ref.shape[0]
    chunk = ext - LANES
    blocks = chunk // LANES

    all_rows = tiles * rows
    offset = (
        lax.broadcasted_iota(jnp.int32, (rows, all_rows), 1)
        - lax.broadcasted_iota(jnp.int32, (rows, all_rows), 0)
        - tile_at * rows
    ).astype(jnp.float32)
    bands = []
    for k in range(NB):
        norm = tap_norm(SIGMAS[k], orders_ref[k, 0])
        bands.append((tap_values(offset, SIGMAS[k], orders_ref[k, 0]) / norm).astype(jnp.bfloat16))
    row_band = jnp.concatenate(bands, axis=0)
    patch = patch_ref[...].reshape(all_rows, ext)
    row_ref[...] = jnp.dot(row_band, patch, preferred_element_type=jnp.float32).astype(jnp.bfloat16)

    shift = (
        lax.broadcasted_iota(jnp.int32, (2 * LANES, LANES), 0)
        - lax.broadcasted_iota(jnp.int32, (2 * LANES, LANES), 1)
        - HALF
    ).astype(jnp.float32)
    for k in range(NB):
        norm = tap_norm(SIGMAS[k], orders_ref[k, 1])
        band = (tap_values(shift, SIGMAS[k], orders_ref[k, 1]) / norm).astype(jnp.bfloat16)
        window = jnp.concatenate(
            [
                row_ref[k * rows : (k + 1) * rows, b * LANES : (b + 2) * LANES]
                for b in range(blocks)
            ],
            axis=0,
        )
        out = jnp.dot(window, band, preferred_element_type=jnp.float32)
        conv_ref[k] = out.reshape(blocks, rows, LANES)

    first_col = expo_at * chunk
    xs = [column_positions(first_col, b, width) for b in range(blocks)]

    def fold(x):
        total = x[:8]
        for i in range(8, rows, 8):
            total = total + x[i : i + 8]
        return total

    def moments(at, left, right, count):
        total = [None] * count
        for b in range(blocks):
            term = fold(left(b) * right(b)) if right is not None else fold(left(b))
            for i in range(count):
                total[i] = term if total[i] is None else total[i] + term
                if i < count - 1:
                    term = term * xs[b]
        for i in range(count):
            parts_ref[at + i] = total[i]

    def conv(k):
        return lambda b: conv_ref[k, b]

    def sci(e):
        return lambda b: recv_ref[e, :, ext + b * LANES : ext + (b + 1) * LANES].astype(jnp.float32)

    at = 0
    for j, k in PAIRS:
        moments(at, conv(j), conv(k), 3)
        at += 3
    for k in range(NB):
        moments(at, conv(k), None, 2)
        at += 2
    parts_ref[at:LANES] = jnp.zeros((LANES - at, 8, LANES), jnp.float32)
    at = LANES
    for e in range(expos):
        for k in range(NB):
            moments(at, conv(k), sci(e), 2)
            at += 2
        moments(at, sci(e), None, 1)
        at += 1
    weight = weight_ref[0, 0] * hits_ref[0, 0].astype(jnp.float32)
    weight = jnp.where(tile_at == 0, weight, 0.0)
    spot = (
        (lax.broadcasted_iota(jnp.int32, (8, LANES), 0) == 0)
        & (lax.broadcasted_iota(jnp.int32, (8, LANES), 1) == 0)
    )
    for e in range(expos):
        parts_ref[at + e] = jnp.where(spot & (expo_at == e), weight, 0.0)
    at += expos
    parts_ref[at : 2 * LANES] = jnp.zeros((2 * LANES - at, 8, LANES), jnp.float32)
    lanes = jnp.sum(parts_ref[...], axis=1)
    ones = jnp.ones((8, LANES), jnp.float32)
    for i in range(2):
        sums_ref[i * 8 : (i + 1) * 8] = lax.dot_general(
            ones,
            lanes[i * LANES : (i + 1) * LANES],
            (((1,), (1,)), ((), ())),
            precision=lax.Precision.HIGHEST,
            preferred_element_type=jnp.float32,
        )


def table(expos):
    matrix = np.zeros((16, LANES), np.int32)
    for at, (j, k) in enumerate(PAIRS):
        for a, b in ((j, k), (k, j)):
            matrix[a, b] = 3 * at
            matrix[a, NB + b] = matrix[NB + a, b] = 3 * at + 1
            matrix[NB + a, NB + b] = 3 * at + 2
    for k in range(NB):
        for x in range(2):
            matrix[x * NB + k, NU - 1] = matrix[NU - 1, x * NB + k] = 3 * len(PAIRS) + 2 * k + x
    for e in range(expos):
        for k in range(NB):
            for x in range(2):
                matrix[x * NB + k, NU + e] = NU * e + 2 * k + x
        matrix[NU - 1, NU + e] = NU * e + NU - 1
        matrix[NU:, NU + e] = NU * expos + e
    return matrix


def solve_kernel(where_ref, table_ref, sums_ref, conv_ref, recv_ref, coadd_ref, coeffs_ref, *, width, pixels):
    expo_at = where_ref[1]
    expos, rows, wide = recv_ref.shape
    chunk = coadd_ref.shape[1]
    blocks = chunk // LANES
    ext = wide - chunk
    where = table_ref[...]
    sub = lax.broadcasted_iota(jnp.int32, (16, LANES), 0)
    lane = lax.broadcasted_iota(jnp.int32, (16, LANES), 1)
    first = jnp.broadcast_to(sums_ref[0:1], (16, LANES))
    second = jnp.broadcast_to(sums_ref[8:9], (16, LANES))
    picked = jnp.where(
        lane < NU,
        jnp.take_along_axis(first, where, axis=1),
        jnp.take_along_axis(second, where, axis=1),
    )
    weights = jnp.where((lane >= NU) & (lane < NU + expos), picked[15:16], 0.0)
    mine = (sub < NU) & (lane < NU + expos)
    system = jnp.where((sub == NU - 1) & (lane == NU - 1), float(pixels), picked)
    system = jnp.where(mine, system, 0.0)
    diagonal = (sub == lane) & (sub < NU)
    trace = jnp.sum(jnp.where(diagonal, system, 0.0))
    system = system + jnp.where(diagonal, RIDGE * (trace / NU), 0.0)
    for i in range(NU):
        column = jnp.sum(jnp.where(lane == i, system, 0.0), axis=1, keepdims=True)
        row = system[i : i + 1] / column[i : i + 1]
        system = jnp.where(sub == i, row, system - column * row)
    own = jnp.sum(jnp.where(lane == NU + expo_at, system, 0.0), axis=1, keepdims=True)
    coeffs_ref[...] = jnp.sum(jnp.where(diagonal, own, 0.0), axis=0, keepdims=True)[:, :NU]
    mixed = jnp.broadcast_to(jnp.sum(system * weights, axis=1, keepdims=True), (16, LANES))
    scale = [jnp.broadcast_to(mixed[u : u + 1], (8, LANES)) for u in range(NU)]
    weight = [
        jnp.broadcast_to(
            jnp.sum(jnp.where(lane[:8] == NU + e, weights[:8], 0.0), axis=1, keepdims=True), (8, LANES)
        )
        for e in range(expos)
    ]
    first_col = expo_at * chunk
    for b in range(blocks):
        x = column_positions(first_col, b, width)
        gains = [scale[k] + scale[NB + k] * x for k in range(NB)]
        image = [
            recv_ref[e, :, ext + b * LANES : ext + (b + 1) * LANES].astype(jnp.float32) for e in range(expos)
        ]
        for r in range(0, rows, 8):
            total = weight[0] * image[0][r : r + 8]
            for e in range(1, expos):
                total = total + weight[e] * image[e][r : r + 8]
            model = scale[NU - 1]
            for k in range(NB):
                model = model + gains[k] * conv_ref[k, b, r : r + 8]
            coadd_ref[r : r + 8, b * LANES : (b + 1) * LANES] = total - model


def tiled_device(template, science, plan, orders, coadd_weight, intersection):
    expos = lax.axis_size("expo")
    tiles = lax.axis_size("tile")
    _, rows, width = template.shape
    steps = science.shape[1]
    chunk = width // expos
    ext = chunk + LANES
    blocks = chunk // LANES
    where = jnp.stack([lax.axis_index("tile"), lax.axis_index("expo")]).astype(jnp.int32)
    smem = pl.BlockSpec(memory_space=pltpu.SMEM)
    vmem = pl.BlockSpec(memory_space=pltpu.VMEM)
    coadds = []
    fitted = []
    for step in range(steps):
        send = pl.pallas_call(
            send_kernel,
            out_shape=jax.ShapeDtypeStruct((expos, rows, ext + chunk), template.dtype),
            in_specs=[vmem, vmem],
            out_specs=vmem,
        )(template[0], science[0, step])
        recv = lax.all_to_all(send, "expo", split_axis=0, concat_axis=0, tiled=True)
        picked = pl.pallas_call(
            pick_kernel,
            out_shape=jax.ShapeDtypeStruct((tiles, rows, ext), template.dtype),
            in_specs=[smem, vmem],
            out_specs=vmem,
        )(plan[step : step + 1], recv)
        patch = lax.all_to_all(picked, "tile", split_axis=0, concat_axis=0, tiled=True)
        conv, sums = pl.pallas_call(
            functools.partial(fit_kernel, width=width),
            out_shape=(
                jax.ShapeDtypeStruct((NB, blocks, rows, LANES), jnp.float32),
                jax.ShapeDtypeStruct((16, LANES), jnp.float32),
            ),
            in_specs=[smem, smem, smem, smem, vmem, vmem],
            out_specs=(vmem, vmem),
            scratch_shapes=[
                pltpu.VMEM((NB * rows, ext), jnp.bfloat16),
                pltpu.VMEM((2 * LANES, 8, LANES), jnp.float32),
            ],
            compiler_params=pltpu.CompilerParams(vmem_limit_bytes=32 * 1024 * 1024),
        )(
            where,
            orders,
            coadd_weight[:, step : step + 1],
            intersection[:, step : step + 1],
            patch,
            recv,
        )
        sums = lax.psum(sums, ("tile", "expo"))
        coadd, coeffs = pl.pallas_call(
            functools.partial(solve_kernel, width=width, pixels=tiles * rows * width),
            out_shape=(
                jax.ShapeDtypeStruct((rows, chunk), jnp.float32),
                jax.ShapeDtypeStruct((1, NU), jnp.float32),
            ),
            in_specs=[smem, vmem, vmem, vmem, vmem],
            out_specs=(vmem, vmem),
            compiler_params=pltpu.CompilerParams(vmem_limit_bytes=32 * 1024 * 1024),
        )(where, jnp.asarray(table(expos)), sums, conv, recv)
        coadds.append(coadd[None])
        fitted.append(coeffs)
    return (jnp.concatenate(coadds), jnp.stack(fitted, axis=1))


def broadcast(block, axis, holder):
    block = jnp.where(lax.axis_index(axis) == holder, block, jnp.zeros_like(block))
    return lax.psum(block, axis)


def extended(x, sides, width):
    for axis, dim in sides:
        size, length = (lax.axis_size(axis), x.shape[dim])
        up = [(i, (i + 1) % size) for i in range(size - 1)]
        down = [(j, i) for i, j in up]
        last = lax.slice_in_dim(x, length - width, length, axis=dim)
        first = lax.slice_in_dim(x, 0, width, axis=dim)
        before = lax.ppermute(last, axis, up)
        after = lax.ppermute(first, axis, down)
        x = jnp.concatenate([before, x, after], axis=dim)
    return x


def make_filters(orders):
    taps_pos = jnp.arange(2 * HALF + 1).astype(jnp.float32) - HALF
    row_list = []
    col_list = []
    for basis in range(NB):
        sigma = SIGMAS[basis]
        envelope = jnp.exp(-taps_pos * taps_pos / (2.0 * sigma * sigma))
        row_filter = envelope * power_of(taps_pos, orders[basis, 0])
        col_filter = envelope * power_of(taps_pos, orders[basis, 1])
        row_list.append(row_filter / jnp.sqrt(jnp.sum(row_filter * row_filter)))
        col_list.append(col_filter / jnp.sqrt(jnp.sum(col_filter * col_filter)))
    return (jnp.stack(row_list).astype(jnp.bfloat16), jnp.stack(col_list).astype(jnp.bfloat16))


def band_matrix(filters, out_len, in_len):
    offset = jnp.arange(in_len)[None, :] - jnp.arange(out_len)[:, None]
    taps_idx = jnp.arange(2 * HALF + 1)
    picks = (offset[:, :, None] == taps_idx[None, None, :]).astype(jnp.float32)
    band = jnp.einsum("ijt,kt->kij", picks, filters.astype(jnp.float32))
    return band.astype(jnp.bfloat16)


def any_device(template, science, plan, orders, coadd_weight, intersection):
    row_filters, col_filters = make_filters(orders)
    rows = template.shape[1]
    width = template.shape[2]
    blocks_count = width // 128
    steps_count = science.shape[1]
    row_band = band_matrix(row_filters, rows, rows + 2 * HALF)
    col_band = jnp.transpose(band_matrix(col_filters, 128, 128 + 2 * HALF), (0, 2, 1))
    column_pos = 2.0 * (jnp.arange(width).astype(jnp.float32) + 0.5) / width - 1.0
    pieces = []
    fitted = []
    for step in range(steps_count):
        received = broadcast(template[0], "expo", plan[step])
        padded = extended(received, (("tile", 0),), HALF)
        rowconv = jnp.einsum(
            "kij,jw->kiw", row_band, padded, preferred_element_type=jnp.float32
        ).astype(jnp.bfloat16)
        blocks = rowconv.reshape(NB, rows, blocks_count, 128)
        empty_rim = jnp.zeros((NB, rows, 1, HALF), jnp.bfloat16)
        previous = jnp.concatenate([empty_rim, blocks[:, :, :-1, 128 - HALF :]], axis=2)
        following = jnp.concatenate([blocks[:, :, 1:, :HALF], empty_rim], axis=2)
        window = jnp.concatenate([previous, blocks, following], axis=3)
        conv = jnp.einsum("krbj,kjc->krbc", window, col_band, preferred_element_type=jnp.float32)
        conv = conv.reshape(NB, rows, width)
        fields = jnp.concatenate(
            [conv, conv * column_pos, jnp.ones((1, rows, width), jnp.float32)], axis=0
        )
        fields = fields.reshape(NU, rows * width)
        exposure_image = science[0, step].astype(jnp.float32).reshape(rows * width)
        normal_local = jnp.dot(fields, fields.T, precision=lax.Precision.HIGHEST)
        project_local = jnp.dot(fields, exposure_image, precision=lax.Precision.HIGHEST)
        normal_matrix, projections = lax.psum((normal_local, project_local), "tile")
        normal_matrix = normal_matrix + RIDGE * (jnp.trace(normal_matrix) / NU) * jnp.eye(
            NU, dtype=jnp.float32
        )
        factor = jnp.linalg.cholesky(normal_matrix)
        coeffs = jax.scipy.linalg.cho_solve((factor, True), projections)
        model = jnp.dot(coeffs, fields, precision=lax.Precision.HIGHEST)
        difference = exposure_image - model
        weight_now = coadd_weight[0, step] * intersection[0, step].astype(jnp.float32)
        pieces.append((weight_now * difference).reshape(rows, width))
        fitted.append(coeffs)
    weighted = jnp.stack(pieces)
    received_parts = lax.all_to_all(weighted[None], "expo", split_axis=3, concat_axis=0, tiled=True)
    coadd = jnp.sum(received_parts, axis=0)
    return (coadd, jnp.stack(fitted)[None])


def per_device(template, science, plan, orders, coadd_weight, intersection):
    expos = lax.axis_size("expo")
    rows, width = template.shape[1:]
    whole_lanes = width % (expos * LANES) == 0 and rows % 16 == 0
    few = (NU + 1) * expos <= LANES and NU + expos <= LANES
    body = tiled_device if whole_lanes and few else any_device
    return body(template, science, plan, orders, coadd_weight, intersection)


def solution(mesh):
    return jax.shard_map(
        per_device,
        mesh=mesh,
        in_specs=(
            P(("groups", "expo"), "tile", None),
            P(("groups", "expo"), None, "tile", None),
            P("groups"),
            P(),
            P(("groups", "expo"), None),
            P(("groups", "expo"), None),
        ),
        out_specs=(P("groups", "tile", "expo"), P(("groups", "expo"), None, None)),
        check_vma=False,
    )
```

```python
import functools

import jax
import jax.numpy as jnp
import numpy as np
from jax import lax
from jax.experimental import pallas as pl
from jax.experimental.pallas import tpu as pltpu
from jax.sharding import PartitionSpec as P

HALF = 15
NB = 6
NU = 13
LANES = 128
PAIRS = [(j, k) for j in range(NB) for k in range(j, NB)]

SIGMAS = (0.8, 1.4, 2.2, 3.0, 4.0, 5.5)
RIDGE = 0.05


def power_of(pos, order):
    return jnp.where(order == 0, 1.0, jnp.where(order == 1, pos, pos * pos))


def tap_values(pos, sigma, order):
    value = jnp.exp(-pos * pos / (2.0 * sigma * sigma)) * power_of(pos, order)
    return jnp.where(jnp.abs(pos) <= HALF, value, 0.0)


def tap_norm(sigma, order):
    pos = lax.broadcasted_iota(jnp.int32, (8, LANES), 1).astype(jnp.float32) - HALF
    value = tap_values(pos, sigma, order)
    return jnp.sqrt(jnp.sum(value * value, axis=1, keepdims=True))[:1]


def send_kernel(template_ref, science_ref, out_ref):
    parts, rows, wide = out_ref.shape
    width = template_ref.shape[1]
    chunk = width // parts
    ext = chunk + LANES
    blank = jnp.zeros((rows, LANES), template_ref.dtype)
    for part in range(parts):
        start = part * chunk
        left = template_ref[:, start - LANES : start] if part else blank
        right = template_ref[:, start + chunk : start + chunk + LANES] if part < parts - 1 else blank
        whole = jnp.concatenate([left, template_ref[:, start : start + chunk], right], axis=1)
        out_ref[part, :, :ext] = whole[:, LANES - HALF : LANES - HALF + ext]
        out_ref[part, :, ext:] = science_ref[:, start : start + chunk]


def pick_kernel(owner_ref, recv_ref, out_ref):
    ext = out_ref.shape[2]
    block = recv_ref[owner_ref[0], :, :ext]
    for part in range(out_ref.shape[0]):
        out_ref[part] = block


def column_positions(first_col, block, width):
    col = lax.broadcasted_iota(jnp.int32, (8, LANES), 1) + (first_col + block * LANES)
    return 2.0 * (col.astype(jnp.float32) + 0.5) / width - 1.0


def fit_kernel(where_ref, orders_ref, weight_ref, hits_ref, patch_ref, recv_ref, conv_ref, sums_ref,
               row_ref, parts_ref, *, width):
    tile_at = where_ref[0]
    expo_at = where_ref[1]
    tiles, rows, ext = patch_ref.shape
    expos = recv_ref.shape[0]
    chunk = ext - LANES
    blocks = chunk // LANES

    all_rows = tiles * rows
    offset = (
        lax.broadcasted_iota(jnp.int32, (rows, all_rows), 1)
        - lax.broadcasted_iota(jnp.int32, (rows, all_rows), 0)
        - tile_at * rows
    ).astype(jnp.float32)
    bands = []
    for k in range(NB):
        norm = tap_norm(SIGMAS[k], orders_ref[k, 0])
        bands.append((tap_values(offset, SIGMAS[k], orders_ref[k, 0]) / norm).astype(jnp.bfloat16))
    row_band = jnp.concatenate(bands, axis=0)
    patch = patch_ref[...].reshape(all_rows, ext)
    row_ref[...] = jnp.dot(row_band, patch, preferred_element_type=jnp.float32).astype(jnp.bfloat16)

    shift = (
        lax.broadcasted_iota(jnp.int32, (2 * LANES, LANES), 0)
        - lax.broadcasted_iota(jnp.int32, (2 * LANES, LANES), 1)
        - HALF
    ).astype(jnp.float32)
    for k in range(NB):
        norm = tap_norm(SIGMAS[k], orders_ref[k, 1])
        band = (tap_values(shift, SIGMAS[k], orders_ref[k, 1]) / norm).astype(jnp.bfloat16)
        window = jnp.concatenate(
            [
                row_ref[k * rows : (k + 1) * rows, b * LANES : (b + 2) * LANES]
                for b in range(blocks)
            ],
            axis=0,
        )
        out = jnp.dot(window, band, preferred_element_type=jnp.float32)
        conv_ref[k] = out.reshape(blocks, rows, LANES)

    first_col = expo_at * chunk
    xs = [column_positions(first_col, b, width) for b in range(blocks)]

    def fold(x):
        total = x[:8]
        for i in range(8, rows, 8):
            total = total + x[i : i + 8]
        return total

    def moments(at, left, right, count):
        total = [None] * count
        for b in range(blocks):
            term = fold(left(b) * right(b)) if right is not None else fold(left(b))
            for i in range(count):
                total[i] = term if total[i] is None else total[i] + term
                if i < count - 1:
                    term = term * xs[b]
        for i in range(count):
            parts_ref[at + i] = total[i]

    def conv(k):
        return lambda b: conv_ref[k, b]

    def sci(e):
        return lambda b: recv_ref[e, :, ext + b * LANES : ext + (b + 1) * LANES].astype(jnp.float32)

    at = 0
    for j, k in PAIRS:
        moments(at, conv(j), conv(k), 3)
        at += 3
    for k in range(NB):
        moments(at, conv(k), None, 2)
        at += 2
    parts_ref[at:LANES] = jnp.zeros((LANES - at, 8, LANES), jnp.float32)
    at = LANES
    for e in range(expos):
        for k in range(NB):
            moments(at, conv(k), sci(e), 2)
            at += 2
        moments(at, sci(e), None, 1)
        at += 1
    weight = weight_ref[0, 0] * hits_ref[0, 0].astype(jnp.float32)
    weight = jnp.where(tile_at == 0, weight, 0.0)
    spot = (
        (lax.broadcasted_iota(jnp.int32, (8, LANES), 0) == 0)
        & (lax.broadcasted_iota(jnp.int32, (8, LANES), 1) == 0)
    )
    for e in range(expos):
        parts_ref[at + e] = jnp.where(spot & (expo_at == e), weight, 0.0)
    at += expos
    parts_ref[at : 2 * LANES] = jnp.zeros((2 * LANES - at, 8, LANES), jnp.float32)
    lanes = jnp.sum(parts_ref[...], axis=1)
    ones = jnp.ones((8, LANES), jnp.float32)
    rows_of = [
        lax.dot_general(
            ones,
            lanes[i * LANES : (i + 1) * LANES],
            (((1,), (1,)), ((), ())),
            precision=lax.Precision.HIGHEST,
            preferred_element_type=jnp.float32,
        )
        for i in range(2)
    ]
    both = jnp.where(lax.broadcasted_iota(jnp.int32, (8, LANES), 0) < 4, rows_of[0], rows_of[1])
    for i in range(sums_ref.shape[0]):
        sums_ref[i] = both


def table(expos):
    matrix = np.zeros((16, LANES), np.int32)
    for at, (j, k) in enumerate(PAIRS):
        for a, b in ((j, k), (k, j)):
            matrix[a, b] = 3 * at
            matrix[a, NB + b] = matrix[NB + a, b] = 3 * at + 1
            matrix[NB + a, NB + b] = 3 * at + 2
    for k in range(NB):
        for x in range(2):
            matrix[x * NB + k, NU - 1] = matrix[NU - 1, x * NB + k] = 3 * len(PAIRS) + 2 * k + x
    for e in range(expos):
        for k in range(NB):
            for x in range(2):
                matrix[x * NB + k, NU + e] = NU * e + 2 * k + x
        matrix[NU - 1, NU + e] = NU * e + NU - 1
        matrix[NU:, NU + e] = NU * expos + e
    return matrix


def solve_kernel(where_ref, table_ref, sums_ref, conv_ref, recv_ref, coadd_ref, coeffs_ref, *, width, pixels):
    expo_at = where_ref[1]
    expos, rows, wide = recv_ref.shape
    chunk = coadd_ref.shape[1]
    blocks = chunk // LANES
    ext = wide - chunk
    where = table_ref[...]
    sub = lax.broadcasted_iota(jnp.int32, (16, LANES), 0)
    lane = lax.broadcasted_iota(jnp.int32, (16, LANES), 1)
    sums = sums_ref[0]
    for i in range(1, sums_ref.shape[0]):
        sums = sums + sums_ref[i]
    first = jnp.broadcast_to(sums[0:1], (16, LANES))
    second = jnp.broadcast_to(sums[4:5], (16, LANES))
    picked = jnp.where(
        lane < NU,
        jnp.take_along_axis(first, where, axis=1),
        jnp.take_along_axis(second, where, axis=1),
    )
    weights = jnp.where((lane >= NU) & (lane < NU + expos), picked[15:16], 0.0)
    mine = (sub < NU) & (lane < NU + expos)
    system = jnp.where((sub == NU - 1) & (lane == NU - 1), float(pixels), picked)
    system = jnp.where(mine, system, 0.0)
    diagonal = (sub == lane) & (sub < NU)
    trace = jnp.sum(jnp.where(diagonal, system, 0.0))
    system = system + jnp.where(diagonal, RIDGE * (trace / NU), 0.0)
    for i in range(NU):
        column = jnp.sum(jnp.where(lane == i, system, 0.0), axis=1, keepdims=True)
        row = system[i : i + 1] / column[i : i + 1]
        system = jnp.where(sub == i, row, system - column * row)
    own = jnp.sum(jnp.where(lane == NU + expo_at, system, 0.0), axis=1, keepdims=True)
    coeffs_ref[...] = jnp.sum(jnp.where(diagonal, own, 0.0), axis=0, keepdims=True)[:, :NU]
    mixed = jnp.broadcast_to(jnp.sum(system * weights, axis=1, keepdims=True), (16, LANES))
    scale = [jnp.broadcast_to(mixed[u : u + 1], (8, LANES)) for u in range(NU)]
    weight = [
        jnp.broadcast_to(
            jnp.sum(jnp.where(lane[:8] == NU + e, weights[:8], 0.0), axis=1, keepdims=True), (8, LANES)
        )
        for e in range(expos)
    ]
    first_col = expo_at * chunk
    for b in range(blocks):
        x = column_positions(first_col, b, width)
        gains = [scale[k] + scale[NB + k] * x for k in range(NB)]
        image = [
            recv_ref[e, :, ext + b * LANES : ext + (b + 1) * LANES].astype(jnp.float32) for e in range(expos)
        ]
        for r in range(0, rows, 8):
            total = weight[0] * image[0][r : r + 8]
            for e in range(1, expos):
                total = total + weight[e] * image[e][r : r + 8]
            model = scale[NU - 1]
            for k in range(NB):
                model = model + gains[k] * conv_ref[k, b, r : r + 8]
            coadd_ref[r : r + 8, b * LANES : (b + 1) * LANES] = total - model


def tiled_device(template, science, plan, orders, coadd_weight, intersection):
    expos = lax.axis_size("expo")
    tiles = lax.axis_size("tile")
    _, rows, width = template.shape
    steps = science.shape[1]
    chunk = width // expos
    ext = chunk + LANES
    blocks = chunk // LANES
    where = jnp.stack([lax.axis_index("tile"), lax.axis_index("expo")]).astype(jnp.int32)
    smem = pl.BlockSpec(memory_space=pltpu.SMEM)
    vmem = pl.BlockSpec(memory_space=pltpu.VMEM)
    small = pltpu.CompilerParams(vmem_limit_bytes=16 * 1024 * 1024)
    coadds = []
    fitted = []
    for step in range(steps):
        send = pl.pallas_call(
            send_kernel,
            out_shape=jax.ShapeDtypeStruct((expos, rows, ext + chunk), template.dtype),
            in_specs=[vmem, vmem],
            out_specs=vmem,
            compiler_params=small,
        )(template[0], science[0, step])
        recv = lax.all_to_all(send, "expo", split_axis=0, concat_axis=0, tiled=True)
        picked = pl.pallas_call(
            pick_kernel,
            out_shape=jax.ShapeDtypeStruct((tiles, rows, ext), template.dtype),
            in_specs=[smem, vmem],
            out_specs=vmem,
            compiler_params=small,
        )(plan[step : step + 1], recv)
        patch = lax.all_to_all(picked, "tile", split_axis=0, concat_axis=0, tiled=True)
        conv, sums = pl.pallas_call(
            functools.partial(fit_kernel, width=width),
            out_shape=(
                jax.ShapeDtypeStruct((NB, blocks, rows, LANES), jnp.float32),
                jax.ShapeDtypeStruct((tiles * expos, 8, LANES), jnp.float32),
            ),
            in_specs=[smem, smem, smem, smem, vmem, vmem],
            out_specs=(vmem, vmem),
            scratch_shapes=[
                pltpu.VMEM((NB * rows, ext), jnp.bfloat16),
                pltpu.VMEM((2 * LANES, 8, LANES), jnp.float32),
            ],
            compiler_params=small,
        )(
            where,
            orders,
            coadd_weight[:, step : step + 1],
            intersection[:, step : step + 1],
            patch,
            recv,
        )
        sums = lax.all_to_all(sums, ("tile", "expo"), split_axis=0, concat_axis=0, tiled=True)
        coadd, coeffs = pl.pallas_call(
            functools.partial(solve_kernel, width=width, pixels=tiles * rows * width),
            out_shape=(
                jax.ShapeDtypeStruct((rows, chunk), jnp.float32),
                jax.ShapeDtypeStruct((1, NU), jnp.float32),
            ),
            in_specs=[smem, vmem, vmem, vmem, vmem],
            out_specs=(vmem, vmem),
            compiler_params=small,
        )(where, jnp.asarray(table(expos)), sums, conv, recv)
        coadds.append(coadd[None])
        fitted.append(coeffs)
    return (jnp.concatenate(coadds), jnp.stack(fitted, axis=1))


def broadcast(block, axis, holder):
    block = jnp.where(lax.axis_index(axis) == holder, block, jnp.zeros_like(block))
    return lax.psum(block, axis)


def extended(x, sides, width):
    for axis, dim in sides:
        size, length = (lax.axis_size(axis), x.shape[dim])
        up = [(i, (i + 1) % size) for i in range(size - 1)]
        down = [(j, i) for i, j in up]
        last = lax.slice_in_dim(x, length - width, length, axis=dim)
        first = lax.slice_in_dim(x, 0, width, axis=dim)
        before = lax.ppermute(last, axis, up)
        after = lax.ppermute(first, axis, down)
        x = jnp.concatenate([before, x, after], axis=dim)
    return x


def make_filters(orders):
    taps_pos = jnp.arange(2 * HALF + 1).astype(jnp.float32) - HALF
    row_list = []
    col_list = []
    for basis in range(NB):
        sigma = SIGMAS[basis]
        envelope = jnp.exp(-taps_pos * taps_pos / (2.0 * sigma * sigma))
        row_filter = envelope * power_of(taps_pos, orders[basis, 0])
        col_filter = envelope * power_of(taps_pos, orders[basis, 1])
        row_list.append(row_filter / jnp.sqrt(jnp.sum(row_filter * row_filter)))
        col_list.append(col_filter / jnp.sqrt(jnp.sum(col_filter * col_filter)))
    return (jnp.stack(row_list).astype(jnp.bfloat16), jnp.stack(col_list).astype(jnp.bfloat16))


def band_matrix(filters, out_len, in_len):
    offset = jnp.arange(in_len)[None, :] - jnp.arange(out_len)[:, None]
    taps_idx = jnp.arange(2 * HALF + 1)
    picks = (offset[:, :, None] == taps_idx[None, None, :]).astype(jnp.float32)
    band = jnp.einsum("ijt,kt->kij", picks, filters.astype(jnp.float32))
    return band.astype(jnp.bfloat16)


def any_device(template, science, plan, orders, coadd_weight, intersection):
    row_filters, col_filters = make_filters(orders)
    rows = template.shape[1]
    width = template.shape[2]
    blocks_count = width // 128
    steps_count = science.shape[1]
    row_band = band_matrix(row_filters, rows, rows + 2 * HALF)
    col_band = jnp.transpose(band_matrix(col_filters, 128, 128 + 2 * HALF), (0, 2, 1))
    column_pos = 2.0 * (jnp.arange(width).astype(jnp.float32) + 0.5) / width - 1.0
    pieces = []
    fitted = []
    for step in range(steps_count):
        received = broadcast(template[0], "expo", plan[step])
        padded = extended(received, (("tile", 0),), HALF)
        rowconv = jnp.einsum(
            "kij,jw->kiw", row_band, padded, preferred_element_type=jnp.float32
        ).astype(jnp.bfloat16)
        blocks = rowconv.reshape(NB, rows, blocks_count, 128)
        empty_rim = jnp.zeros((NB, rows, 1, HALF), jnp.bfloat16)
        previous = jnp.concatenate([empty_rim, blocks[:, :, :-1, 128 - HALF :]], axis=2)
        following = jnp.concatenate([blocks[:, :, 1:, :HALF], empty_rim], axis=2)
        window = jnp.concatenate([previous, blocks, following], axis=3)
        conv = jnp.einsum("krbj,kjc->krbc", window, col_band, preferred_element_type=jnp.float32)
        conv = conv.reshape(NB, rows, width)
        fields = jnp.concatenate(
            [conv, conv * column_pos, jnp.ones((1, rows, width), jnp.float32)], axis=0
        )
        fields = fields.reshape(NU, rows * width)
        exposure_image = science[0, step].astype(jnp.float32).reshape(rows * width)
        normal_local = jnp.dot(fields, fields.T, precision=lax.Precision.HIGHEST)
        project_local = jnp.dot(fields, exposure_image, precision=lax.Precision.HIGHEST)
        normal_matrix, projections = lax.psum((normal_local, project_local), "tile")
        normal_matrix = normal_matrix + RIDGE * (jnp.trace(normal_matrix) / NU) * jnp.eye(
            NU, dtype=jnp.float32
        )
        factor = jnp.linalg.cholesky(normal_matrix)
        coeffs = jax.scipy.linalg.cho_solve((factor, True), projections)
        model = jnp.dot(coeffs, fields, precision=lax.Precision.HIGHEST)
        difference = exposure_image - model
        weight_now = coadd_weight[0, step] * intersection[0, step].astype(jnp.float32)
        pieces.append((weight_now * difference).reshape(rows, width))
        fitted.append(coeffs)
    weighted = jnp.stack(pieces)
    received_parts = lax.all_to_all(weighted[None], "expo", split_axis=3, concat_axis=0, tiled=True)
    coadd = jnp.sum(received_parts, axis=0)
    return (coadd, jnp.stack(fitted)[None])


def per_device(template, science, plan, orders, coadd_weight, intersection):
    expos = lax.axis_size("expo")
    rows, width = template.shape[1:]
    whole_lanes = width % (expos * LANES) == 0 and rows % 16 == 0
    few = (NU + 1) * expos <= LANES and NU + expos <= LANES
    body = tiled_device if whole_lanes and few else any_device
    return body(template, science, plan, orders, coadd_weight, intersection)


def solution(mesh):
    return jax.shard_map(
        per_device,
        mesh=mesh,
        in_specs=(
            P(("groups", "expo"), "tile", None),
            P(("groups", "expo"), None, "tile", None),
            P("groups"),
            P(),
            P(("groups", "expo"), None),
            P(("groups", "expo"), None),
        ),
        out_specs=(P("groups", "tile", "expo"), P(("groups", "expo"), None, None)),
        check_vma=False,
    )
```

```python
import functools

import jax
import jax.numpy as jnp
import numpy as np
from jax import lax
from jax.experimental import pallas as pl
from jax.experimental.pallas import tpu as pltpu
from jax.sharding import PartitionSpec as P

HALF = 15
NB = 6
NU = 13
LANES = 128
PAIRS = [(j, k) for j in range(NB) for k in range(j, NB)]

SIGMAS = (0.8, 1.4, 2.2, 3.0, 4.0, 5.5)
RIDGE = 0.05


def power_of(pos, order):
    return jnp.where(order == 0, 1.0, jnp.where(order == 1, pos, pos * pos))


def tap_values(pos, sigma, order):
    value = jnp.exp(-pos * pos / (2.0 * sigma * sigma)) * power_of(pos, order)
    return jnp.where(jnp.abs(pos) <= HALF, value, 0.0)


def tap_norm(sigma, order):
    pos = lax.broadcasted_iota(jnp.int32, (8, LANES), 1).astype(jnp.float32) - HALF
    value = tap_values(pos, sigma, order)
    return jnp.sqrt(jnp.sum(value * value, axis=1, keepdims=True))[:1]


def send_kernel(template_ref, science_ref, patch_ref, images_ref, held_ref, sems):
    parts, rows, ext = patch_ref.shape
    chunk = ext - LANES
    loads = []
    copies = []
    for part in range(parts):
        columns = pl.ds(part * chunk, chunk)
        loads.append(
            pltpu.make_async_copy(template_ref.at[:, columns], held_ref.at[:, columns], sems.at[0, part])
        )
        copies.append(
            pltpu.make_async_copy(science_ref.at[:, columns], images_ref.at[part], sems.at[1, part])
        )
    for copy in loads + copies:
        copy.start()
    for copy in loads:
        copy.wait()
    blank = jnp.zeros((rows, LANES), patch_ref.dtype)
    for part in range(parts):
        start = part * chunk
        left = held_ref[:, start - LANES : start] if part else blank
        right = held_ref[:, start + chunk : start + chunk + LANES] if part < parts - 1 else blank
        whole = jnp.concatenate([left, held_ref[:, start : start + chunk], right], axis=1)
        patch_ref[part] = whole[:, LANES - HALF : LANES - HALF + ext]
    for copy in copies:
        copy.wait()


def pick_kernel(owner_ref, recv_ref, out_ref):
    block = recv_ref[owner_ref[0]]
    for part in range(out_ref.shape[0]):
        out_ref[part] = block


def column_positions(first_col, block, width):
    col = lax.broadcasted_iota(jnp.int32, (8, LANES), 1) + (first_col + block * LANES)
    return 2.0 * (col.astype(jnp.float32) + 0.5) / width - 1.0


def band_kernel(where_ref, orders_ref, row_ref, col_ref):
    rows = row_ref.shape[0] // NB
    all_rows = row_ref.shape[1]
    offset = (
        lax.broadcasted_iota(jnp.int32, (rows, all_rows), 1)
        - lax.broadcasted_iota(jnp.int32, (rows, all_rows), 0)
        - where_ref[0] * rows
    ).astype(jnp.float32)
    shift = (
        lax.broadcasted_iota(jnp.int32, (2 * LANES, LANES), 0)
        - lax.broadcasted_iota(jnp.int32, (2 * LANES, LANES), 1)
        - HALF
    ).astype(jnp.float32)
    for k in range(NB):
        norm = tap_norm(SIGMAS[k], orders_ref[k, 0])
        row_ref[k * rows : (k + 1) * rows] = (
            tap_values(offset, SIGMAS[k], orders_ref[k, 0]) / norm
        ).astype(jnp.bfloat16)
        norm = tap_norm(SIGMAS[k], orders_ref[k, 1])
        col_ref[k] = (tap_values(shift, SIGMAS[k], orders_ref[k, 1]) / norm).astype(jnp.bfloat16)


def fit_kernel(where_ref, weight_ref, hits_ref, row_band_ref, col_band_ref, patch_ref, recv_ref, conv_ref,
               sums_ref, row_ref, parts_ref, *, width):
    tile_at = where_ref[0]
    expo_at = where_ref[1]
    tiles, rows, ext = patch_ref.shape
    expos = recv_ref.shape[0]
    chunk = ext - LANES
    blocks = chunk // LANES

    patch = patch_ref[...].reshape(tiles * rows, ext)
    row_ref[...] = jnp.dot(
        row_band_ref[...], patch, preferred_element_type=jnp.float32
    ).astype(jnp.bfloat16)
    for k in range(NB):
        window = jnp.concatenate(
            [
                row_ref[k * rows : (k + 1) * rows, b * LANES : (b + 2) * LANES]
                for b in range(blocks)
            ],
            axis=0,
        )
        out = jnp.dot(window, col_band_ref[k], preferred_element_type=jnp.float32)
        conv_ref[k] = out.reshape(blocks, rows, LANES)

    first_col = expo_at * chunk
    xs = [column_positions(first_col, b, width) for b in range(blocks)]

    def fold(x):
        total = x[:8]
        for i in range(8, rows, 8):
            total = total + x[i : i + 8]
        return total

    def moments(at, left, right, count):
        total = [None] * count
        for b in range(blocks):
            term = fold(left(b) * right(b)) if right is not None else fold(left(b))
            for i in range(count):
                total[i] = term if total[i] is None else total[i] + term
                if i < count - 1:
                    term = term * xs[b]
        for i in range(count):
            parts_ref[at + i] = total[i]

    def conv(k):
        return lambda b: conv_ref[k, b]

    def sci(e):
        return lambda b: recv_ref[e, :, b * LANES : (b + 1) * LANES].astype(jnp.float32)

    at = 0
    for j, k in PAIRS:
        moments(at, conv(j), conv(k), 3)
        at += 3
    for k in range(NB):
        moments(at, conv(k), None, 2)
        at += 2
    parts_ref[at:LANES] = jnp.zeros((LANES - at, 8, LANES), jnp.float32)
    at = LANES
    for e in range(expos):
        for k in range(NB):
            moments(at, conv(k), sci(e), 2)
            at += 2
        moments(at, sci(e), None, 1)
        at += 1
    weight = weight_ref[0, 0] * hits_ref[0, 0].astype(jnp.float32)
    weight = jnp.where(tile_at == 0, weight, 0.0)
    spot = (
        (lax.broadcasted_iota(jnp.int32, (8, LANES), 0) == 0)
        & (lax.broadcasted_iota(jnp.int32, (8, LANES), 1) == 0)
    )
    for e in range(expos):
        parts_ref[at + e] = jnp.where(spot & (expo_at == e), weight, 0.0)
    at += expos
    parts_ref[at : 2 * LANES] = jnp.zeros((2 * LANES - at, 8, LANES), jnp.float32)
    lanes = jnp.sum(parts_ref[...], axis=1)
    ones = jnp.ones((8, LANES), jnp.float32)
    rows_of = [
        lax.dot_general(
            ones,
            lanes[i * LANES : (i + 1) * LANES],
            (((1,), (1,)), ((), ())),
            precision=lax.Precision.HIGHEST,
            preferred_element_type=jnp.float32,
        )
        for i in range(2)
    ]
    both = jnp.where(lax.broadcasted_iota(jnp.int32, (8, LANES), 0) < 4, rows_of[0], rows_of[1])
    for i in range(sums_ref.shape[0]):
        sums_ref[i] = both


def table(expos):
    matrix = np.zeros((16, LANES), np.int32)
    for at, (j, k) in enumerate(PAIRS):
        for a, b in ((j, k), (k, j)):
            matrix[a, b] = 3 * at
            matrix[a, NB + b] = matrix[NB + a, b] = 3 * at + 1
            matrix[NB + a, NB + b] = 3 * at + 2
    for k in range(NB):
        for x in range(2):
            matrix[x * NB + k, NU - 1] = matrix[NU - 1, x * NB + k] = 3 * len(PAIRS) + 2 * k + x
    for e in range(expos):
        for k in range(NB):
            for x in range(2):
                matrix[x * NB + k, NU + e] = NU * e + 2 * k + x
        matrix[NU - 1, NU + e] = NU * e + NU - 1
        matrix[NU:, NU + e] = NU * expos + e
    return matrix


def solve_kernel(where_ref, table_ref, sums_ref, conv_ref, recv_ref, coadd_ref, coeffs_ref, *, width, pixels):
    expo_at = where_ref[1]
    expos, rows, chunk = recv_ref.shape
    blocks = chunk // LANES
    where = table_ref[...]
    sub = lax.broadcasted_iota(jnp.int32, (16, LANES), 0)
    lane = lax.broadcasted_iota(jnp.int32, (16, LANES), 1)
    sums = sums_ref[0]
    for i in range(1, sums_ref.shape[0]):
        sums = sums + sums_ref[i]
    first = jnp.broadcast_to(sums[0:1], (16, LANES))
    second = jnp.broadcast_to(sums[4:5], (16, LANES))
    picked = jnp.where(
        lane < NU,
        jnp.take_along_axis(first, where, axis=1),
        jnp.take_along_axis(second, where, axis=1),
    )
    weights = jnp.where((lane >= NU) & (lane < NU + expos), picked[15:16], 0.0)
    mine = (sub < NU) & (lane < NU + expos)
    system = jnp.where((sub == NU - 1) & (lane == NU - 1), float(pixels), picked)
    system = jnp.where(mine, system, 0.0)
    diagonal = (sub == lane) & (sub < NU)
    trace = jnp.sum(jnp.where(diagonal, system, 0.0))
    system = system + jnp.where(diagonal, RIDGE * (trace / NU), 0.0)
    for i in range(NU):
        column = system[:, i : i + 1]
        row = system[i : i + 1] / column[i : i + 1]
        system = jnp.where(sub == i, row, system - column * row)
    own = jnp.sum(jnp.where(lane == NU + expo_at, system, 0.0), axis=1, keepdims=True)
    coeffs_ref[...] = jnp.sum(jnp.where(diagonal, own, 0.0), axis=0, keepdims=True)[:, :NU]
    mixed = jnp.broadcast_to(jnp.sum(system * weights, axis=1, keepdims=True), (16, LANES))
    scale = [jnp.broadcast_to(mixed[u : u + 1], (8, LANES)) for u in range(NU)]
    weight = [
        jnp.broadcast_to(
            jnp.sum(jnp.where(lane[:8] == NU + e, weights[:8], 0.0), axis=1, keepdims=True), (8, LANES)
        )
        for e in range(expos)
    ]
    first_col = expo_at * chunk
    for b in range(blocks):
        x = column_positions(first_col, b, width)
        gains = [scale[k] + scale[NB + k] * x for k in range(NB)]
        image = [
            recv_ref[e, :, b * LANES : (b + 1) * LANES].astype(jnp.float32) for e in range(expos)
        ]
        for r in range(0, rows, 8):
            total = weight[0] * image[0][r : r + 8]
            for e in range(1, expos):
                total = total + weight[e] * image[e][r : r + 8]
            model = scale[NU - 1]
            for k in range(NB):
                model = model + gains[k] * conv_ref[k, b, r : r + 8]
            coadd_ref[r : r + 8, b * LANES : (b + 1) * LANES] = total - model


def tiled_device(template, science, plan, orders, coadd_weight, intersection):
    expos = lax.axis_size("expo")
    tiles = lax.axis_size("tile")
    _, rows, width = template.shape
    steps = science.shape[1]
    chunk = width // expos
    ext = chunk + LANES
    blocks = chunk // LANES
    where = jnp.stack([lax.axis_index("tile"), lax.axis_index("expo")]).astype(jnp.int32)
    smem = pl.BlockSpec(memory_space=pltpu.SMEM)
    vmem = pl.BlockSpec(memory_space=pltpu.VMEM)
    small = pltpu.CompilerParams(vmem_limit_bytes=16 * 1024 * 1024)
    hbm = pl.BlockSpec(memory_space=pltpu.HBM)
    row_band, col_band = pl.pallas_call(
        band_kernel,
        out_shape=(
            jax.ShapeDtypeStruct((NB * rows, tiles * rows), jnp.bfloat16),
            jax.ShapeDtypeStruct((NB, 2 * LANES, LANES), jnp.bfloat16),
        ),
        in_specs=[smem, smem],
        out_specs=(vmem, vmem),
        compiler_params=small,
        cost_estimate=pl.CostEstimate(flops=4_000_000, bytes_accessed=500_000, transcendentals=200_000),
    )(where, orders)
    coadds = []
    fitted = []
    for step in range(steps):
        patches, images = pl.pallas_call(
            send_kernel,
            out_shape=(
                jax.ShapeDtypeStruct((expos, rows, ext), template.dtype),
                jax.ShapeDtypeStruct((expos, rows, chunk), science.dtype),
            ),
            in_specs=[hbm, hbm],
            out_specs=(vmem, vmem),
            scratch_shapes=[
                pltpu.VMEM((rows, width), template.dtype),
                pltpu.SemaphoreType.DMA((2, expos)),
            ],
            compiler_params=small,
        )(template[0], science[0, step])
        patches = lax.all_to_all(patches, "expo", split_axis=0, concat_axis=0, tiled=True)
        recv = lax.all_to_all(images, "expo", split_axis=0, concat_axis=0, tiled=True)
        picked = pl.pallas_call(
            pick_kernel,
            out_shape=jax.ShapeDtypeStruct((tiles, rows, ext), template.dtype),
            in_specs=[smem, vmem],
            out_specs=vmem,
            compiler_params=small,
        )(plan[step : step + 1], patches)
        patch = lax.all_to_all(picked, "tile", split_axis=0, concat_axis=0, tiled=True)
        conv, sums = pl.pallas_call(
            functools.partial(fit_kernel, width=width),
            out_shape=(
                jax.ShapeDtypeStruct((NB, blocks, rows, LANES), jnp.float32),
                jax.ShapeDtypeStruct((tiles * expos, 8, LANES), jnp.float32),
            ),
            in_specs=[smem, smem, smem, vmem, vmem, vmem, vmem],
            out_specs=(vmem, vmem),
            scratch_shapes=[
                pltpu.VMEM((NB * rows, ext), jnp.bfloat16),
                pltpu.VMEM((2 * LANES, 8, LANES), jnp.float32),
            ],
            compiler_params=small,
        )(
            where,
            coadd_weight[:, step : step + 1],
            intersection[:, step : step + 1],
            row_band,
            col_band,
            patch,
            recv,
        )
        sums = lax.all_to_all(sums, ("tile", "expo"), split_axis=0, concat_axis=0, tiled=True)
        coadd, coeffs = pl.pallas_call(
            functools.partial(solve_kernel, width=width, pixels=tiles * rows * width),
            out_shape=(
                jax.ShapeDtypeStruct((rows, chunk), jnp.float32),
                jax.ShapeDtypeStruct((1, NU), jnp.float32),
            ),
            in_specs=[smem, vmem, vmem, vmem, vmem],
            out_specs=(vmem, vmem),
            compiler_params=small,
        )(where, jnp.asarray(table(expos)), sums, conv, recv)
        coadds.append(coadd[None])
        fitted.append(coeffs)
    return (jnp.concatenate(coadds), jnp.stack(fitted, axis=1))


def broadcast(block, axis, holder):
    block = jnp.where(lax.axis_index(axis) == holder, block, jnp.zeros_like(block))
    return lax.psum(block, axis)


def extended(x, sides, width):
    for axis, dim in sides:
        size, length = (lax.axis_size(axis), x.shape[dim])
        up = [(i, (i + 1) % size) for i in range(size - 1)]
        down = [(j, i) for i, j in up]
        last = lax.slice_in_dim(x, length - width, length, axis=dim)
        first = lax.slice_in_dim(x, 0, width, axis=dim)
        before = lax.ppermute(last, axis, up)
        after = lax.ppermute(first, axis, down)
        x = jnp.concatenate([before, x, after], axis=dim)
    return x


def make_filters(orders):
    taps_pos = jnp.arange(2 * HALF + 1).astype(jnp.float32) - HALF
    row_list = []
    col_list = []
    for basis in range(NB):
        sigma = SIGMAS[basis]
        envelope = jnp.exp(-taps_pos * taps_pos / (2.0 * sigma * sigma))
        row_filter = envelope * power_of(taps_pos, orders[basis, 0])
        col_filter = envelope * power_of(taps_pos, orders[basis, 1])
        row_list.append(row_filter / jnp.sqrt(jnp.sum(row_filter * row_filter)))
        col_list.append(col_filter / jnp.sqrt(jnp.sum(col_filter * col_filter)))
    return (jnp.stack(row_list).astype(jnp.bfloat16), jnp.stack(col_list).astype(jnp.bfloat16))


def band_matrix(filters, out_len, in_len):
    offset = jnp.arange(in_len)[None, :] - jnp.arange(out_len)[:, None]
    taps_idx = jnp.arange(2 * HALF + 1)
    picks = (offset[:, :, None] == taps_idx[None, None, :]).astype(jnp.float32)
    band = jnp.einsum("ijt,kt->kij", picks, filters.astype(jnp.float32))
    return band.astype(jnp.bfloat16)


def any_device(template, science, plan, orders, coadd_weight, intersection):
    row_filters, col_filters = make_filters(orders)
    rows = template.shape[1]
    width = template.shape[2]
    blocks_count = width // 128
    steps_count = science.shape[1]
    row_band = band_matrix(row_filters, rows, rows + 2 * HALF)
    col_band = jnp.transpose(band_matrix(col_filters, 128, 128 + 2 * HALF), (0, 2, 1))
    column_pos = 2.0 * (jnp.arange(width).astype(jnp.float32) + 0.5) / width - 1.0
    pieces = []
    fitted = []
    for step in range(steps_count):
        received = broadcast(template[0], "expo", plan[step])
        padded = extended(received, (("tile", 0),), HALF)
        rowconv = jnp.einsum(
            "kij,jw->kiw", row_band, padded, preferred_element_type=jnp.float32
        ).astype(jnp.bfloat16)
        blocks = rowconv.reshape(NB, rows, blocks_count, 128)
        empty_rim = jnp.zeros((NB, rows, 1, HALF), jnp.bfloat16)
        previous = jnp.concatenate([empty_rim, blocks[:, :, :-1, 128 - HALF :]], axis=2)
        following = jnp.concatenate([blocks[:, :, 1:, :HALF], empty_rim], axis=2)
        window = jnp.concatenate([previous, blocks, following], axis=3)
        conv = jnp.einsum("krbj,kjc->krbc", window, col_band, preferred_element_type=jnp.float32)
        conv = conv.reshape(NB, rows, width)
        fields = jnp.concatenate(
            [conv, conv * column_pos, jnp.ones((1, rows, width), jnp.float32)], axis=0
        )
        fields = fields.reshape(NU, rows * width)
        exposure_image = science[0, step].astype(jnp.float32).reshape(rows * width)
        normal_local = jnp.dot(fields, fields.T, precision=lax.Precision.HIGHEST)
        project_local = jnp.dot(fields, exposure_image, precision=lax.Precision.HIGHEST)
        normal_matrix, projections = lax.psum((normal_local, project_local), "tile")
        normal_matrix = normal_matrix + RIDGE * (jnp.trace(normal_matrix) / NU) * jnp.eye(
            NU, dtype=jnp.float32
        )
        factor = jnp.linalg.cholesky(normal_matrix)
        coeffs = jax.scipy.linalg.cho_solve((factor, True), projections)
        model = jnp.dot(coeffs, fields, precision=lax.Precision.HIGHEST)
        difference = exposure_image - model
        weight_now = coadd_weight[0, step] * intersection[0, step].astype(jnp.float32)
        pieces.append((weight_now * difference).reshape(rows, width))
        fitted.append(coeffs)
    weighted = jnp.stack(pieces)
    received_parts = lax.all_to_all(weighted[None], "expo", split_axis=3, concat_axis=0, tiled=True)
    coadd = jnp.sum(received_parts, axis=0)
    return (coadd, jnp.stack(fitted)[None])


def per_device(template, science, plan, orders, coadd_weight, intersection):
    expos = lax.axis_size("expo")
    rows, width = template.shape[1:]
    whole_lanes = width % (expos * LANES) == 0 and rows % 16 == 0
    few = (NU + 1) * expos <= LANES and NU + expos <= LANES
    body = tiled_device if whole_lanes and few else any_device
    return body(template, science, plan, orders, coadd_weight, intersection)


def solution(mesh):
    return jax.shard_map(
        per_device,
        mesh=mesh,
        in_specs=(
            P(("groups", "expo"), "tile", None),
            P(("groups", "expo"), None, "tile", None),
            P("groups"),
            P(),
            P(("groups", "expo"), None),
            P(("groups", "expo"), None),
        ),
        out_specs=(P("groups", "tile", "expo"), P(("groups", "expo"), None, None)),
        check_vma=False,
    )
```

```python
import functools

import jax
import jax.numpy as jnp
import numpy as np
from jax import lax
from jax.experimental import pallas as pl
from jax.experimental.pallas import tpu as pltpu
from jax.sharding import PartitionSpec as P

HALF = 15
NB = 6
NU = 13
LANES = 128
PAIRS = [(j, k) for j in range(NB) for k in range(j, NB)]

SIGMAS = (0.8, 1.4, 2.2, 3.0, 4.0, 5.5)
RIDGE = 0.05


def power_of(pos, order):
    return jnp.where(order == 0, 1.0, jnp.where(order == 1, pos, pos * pos))


def tap_values(pos, sigma, order):
    value = jnp.exp(-pos * pos / (2.0 * sigma * sigma)) * power_of(pos, order)
    return jnp.where(jnp.abs(pos) <= HALF, value, 0.0)


def tap_norm(sigma, order):
    pos = lax.broadcasted_iota(jnp.int32, (8, LANES), 1).astype(jnp.float32) - HALF
    value = tap_values(pos, sigma, order)
    return jnp.sqrt(jnp.sum(value * value, axis=1, keepdims=True))[:1]


def send_kernel(template_ref, science_ref, out_ref, rim_ref, sems):
    parts, rows, wide = out_ref.shape
    chunk = (wide - LANES) // 2
    rims = []
    copies = []
    for part in range(parts):
        start = part * chunk
        if part:
            rims.append(
                pltpu.make_async_copy(
                    template_ref.at[:, pl.ds(start - LANES, LANES)], rim_ref.at[0, part], sems.at[0, part]
                )
            )
        if part < parts - 1:
            rims.append(
                pltpu.make_async_copy(
                    template_ref.at[:, pl.ds(start + chunk, LANES)], rim_ref.at[1, part], sems.at[1, part]
                )
            )
        copies.append(
            pltpu.make_async_copy(
                template_ref.at[:, pl.ds(start, chunk)], out_ref.at[part, :, pl.ds(0, chunk)], sems.at[2, part]
            )
        )
        copies.append(
            pltpu.make_async_copy(
                science_ref.at[:, pl.ds(start, chunk)],
                out_ref.at[part, :, pl.ds(chunk + LANES, chunk)],
                sems.at[3, part],
            )
        )
    for copy in rims + copies:
        copy.start()
    for copy in rims:
        copy.wait()
    lane = lax.broadcasted_iota(jnp.int32, (rows, LANES), 1)
    for part in range(parts):
        before = rim_ref[0, part].astype(jnp.float32) if part else 0.0
        after = rim_ref[1, part].astype(jnp.float32) if part < parts - 1 else 0.0
        rim = jnp.where(lane < LANES // 2, after, before)
        out_ref[part, :, chunk : chunk + LANES] = rim.astype(out_ref.dtype)
    for copy in copies:
        copy.wait()


def pick_kernel(owner_ref, recv_ref, out_ref):
    ext = out_ref.shape[1]
    chunk = ext - LANES
    block = recv_ref[owner_ref[0], :, :ext]
    rim = block[:, chunk:]
    whole = jnp.concatenate([rim, block], axis=1)
    out_ref[...] = whole[:, LANES - HALF : LANES - HALF + ext]


def column_positions(first_col, block, width):
    col = lax.broadcasted_iota(jnp.int32, (8, LANES), 1) + (first_col + block * LANES)
    return 2.0 * (col.astype(jnp.float32) + 0.5) / width - 1.0


def band_kernel(where_ref, orders_ref, row_ref, col_ref):
    rows = row_ref.shape[0] // NB
    near = 1 - 2 * lax.rem(where_ref[0], 2)
    source = lax.broadcasted_iota(jnp.int32, (rows, 3 * rows), 1)
    moved = jnp.where(source < rows, 0, jnp.where(source < 2 * rows, near - 1, -near - 2))
    offset = (
        source + moved * rows - lax.broadcasted_iota(jnp.int32, (rows, 3 * rows), 0)
    ).astype(jnp.float32)
    shift = (
        lax.broadcasted_iota(jnp.int32, (2 * LANES, LANES), 0)
        - lax.broadcasted_iota(jnp.int32, (2 * LANES, LANES), 1)
        - HALF
    ).astype(jnp.float32)
    for k in range(NB):
        norm = tap_norm(SIGMAS[k], orders_ref[k, 0])
        row_ref[k * rows : (k + 1) * rows] = (
            tap_values(offset, SIGMAS[k], orders_ref[k, 0]) / norm
        ).astype(jnp.bfloat16)
        norm = tap_norm(SIGMAS[k], orders_ref[k, 1])
        col_ref[k] = (tap_values(shift, SIGMAS[k], orders_ref[k, 1]) / norm).astype(jnp.bfloat16)


def fit_kernel(where_ref, weight_ref, hits_ref, row_band_ref, col_band_ref, own_ref, near_ref, far_ref,
               recv_ref, conv_ref, sums_ref, row_ref, parts_ref, *, width):
    tile_at = where_ref[0]
    expo_at = where_ref[1]
    rows, ext = own_ref.shape
    expos = recv_ref.shape[0]
    chunk = ext - LANES
    blocks = chunk // LANES

    patch = jnp.concatenate([own_ref[...], near_ref[...], far_ref[...]], axis=0)
    row_ref[...] = jnp.dot(
        row_band_ref[...], patch, preferred_element_type=jnp.float32
    ).astype(jnp.bfloat16)
    for k in range(NB):
        window = jnp.concatenate(
            [
                row_ref[k * rows : (k + 1) * rows, b * LANES : (b + 2) * LANES]
                for b in range(blocks)
            ],
            axis=0,
        )
        out = jnp.dot(window, col_band_ref[k], preferred_element_type=jnp.float32)
        conv_ref[k] = out.reshape(blocks, rows, LANES)

    first_col = expo_at * chunk
    xs = [column_positions(first_col, b, width) for b in range(blocks)]

    def fold(x):
        total = x[:8]
        for i in range(8, rows, 8):
            total = total + x[i : i + 8]
        return total

    def moments(at, left, right, count):
        total = [None] * count
        for b in range(blocks):
            term = fold(left(b) * right(b)) if right is not None else fold(left(b))
            for i in range(count):
                total[i] = term if total[i] is None else total[i] + term
                if i < count - 1:
                    term = term * xs[b]
        for i in range(count):
            parts_ref[at + i] = total[i]

    def conv(k):
        return lambda b: conv_ref[k, b]

    def sci(e):
        return lambda b: recv_ref[e, :, ext + b * LANES : ext + (b + 1) * LANES].astype(jnp.float32)

    at = 0
    for j, k in PAIRS:
        moments(at, conv(j), conv(k), 3)
        at += 3
    for k in range(NB):
        moments(at, conv(k), None, 2)
        at += 2
    parts_ref[at:LANES] = jnp.zeros((LANES - at, 8, LANES), jnp.float32)
    at = LANES
    for e in range(expos):
        for k in range(NB):
            moments(at, conv(k), sci(e), 2)
            at += 2
        moments(at, sci(e), None, 1)
        at += 1
    weight = weight_ref[0, 0] * hits_ref[0, 0].astype(jnp.float32)
    weight = jnp.where(tile_at == 0, weight, 0.0)
    spot = (
        (lax.broadcasted_iota(jnp.int32, (8, LANES), 0) == 0)
        & (lax.broadcasted_iota(jnp.int32, (8, LANES), 1) == 0)
    )
    for e in range(expos):
        parts_ref[at + e] = jnp.where(spot & (expo_at == e), weight, 0.0)
    at += expos
    parts_ref[at : 2 * LANES] = jnp.zeros((2 * LANES - at, 8, LANES), jnp.float32)
    lanes = jnp.sum(parts_ref[...], axis=1)
    ones = jnp.ones((8, LANES), jnp.float32)
    rows_of = [
        lax.dot_general(
            ones,
            lanes[i * LANES : (i + 1) * LANES],
            (((1,), (1,)), ((), ())),
            precision=lax.Precision.HIGHEST,
            preferred_element_type=jnp.float32,
        )
        for i in range(2)
    ]
    both = jnp.where(lax.broadcasted_iota(jnp.int32, (8, LANES), 0) < 4, rows_of[0], rows_of[1])
    for i in range(sums_ref.shape[0]):
        sums_ref[i] = both


def table(expos):
    matrix = np.zeros((16, LANES), np.int32)
    for at, (j, k) in enumerate(PAIRS):
        for a, b in ((j, k), (k, j)):
            matrix[a, b] = 3 * at
            matrix[a, NB + b] = matrix[NB + a, b] = 3 * at + 1
            matrix[NB + a, NB + b] = 3 * at + 2
    for k in range(NB):
        for x in range(2):
            matrix[x * NB + k, NU - 1] = matrix[NU - 1, x * NB + k] = 3 * len(PAIRS) + 2 * k + x
    for e in range(expos):
        for k in range(NB):
            for x in range(2):
                matrix[x * NB + k, NU + e] = NU * e + 2 * k + x
        matrix[NU - 1, NU + e] = NU * e + NU - 1
        matrix[NU:, NU + e] = NU * expos + e
    return matrix


def solve_kernel(where_ref, table_ref, sums_ref, conv_ref, recv_ref, coadd_ref, coeffs_ref, *, width, pixels):
    expo_at = where_ref[1]
    expos, rows, wide = recv_ref.shape
    chunk = coadd_ref.shape[1]
    blocks = chunk // LANES
    ext = wide - chunk
    where = table_ref[...]
    sub = lax.broadcasted_iota(jnp.int32, (16, LANES), 0)
    lane = lax.broadcasted_iota(jnp.int32, (16, LANES), 1)
    sums = sums_ref[0]
    for i in range(1, sums_ref.shape[0]):
        sums = sums + sums_ref[i]
    first = jnp.broadcast_to(sums[0:1], (16, LANES))
    second = jnp.broadcast_to(sums[4:5], (16, LANES))
    picked = jnp.where(
        lane < NU,
        jnp.take_along_axis(first, where, axis=1),
        jnp.take_along_axis(second, where, axis=1),
    )
    weights = jnp.where((lane >= NU) & (lane < NU + expos), picked[15:16], 0.0)
    mine = (sub < NU) & (lane < NU + expos)
    system = jnp.where((sub == NU - 1) & (lane == NU - 1), float(pixels), picked)
    system = jnp.where(mine, system, 0.0)
    diagonal = (sub == lane) & (sub < NU)
    trace = jnp.sum(jnp.where(diagonal, system, 0.0), axis=0, keepdims=True)
    trace = jnp.sum(trace, axis=1, keepdims=True)
    system = system + jnp.where(diagonal, RIDGE * (trace / NU), 0.0)
    for i in range(NU):
        column = system[:, i : i + 1]
        row = system[i : i + 1] / column[i : i + 1]
        system = jnp.where(sub == i, row, system - column * row)
    own = jnp.sum(jnp.where(lane == NU + expo_at, system, 0.0), axis=1, keepdims=True)
    coeffs_ref[...] = jnp.sum(jnp.where(diagonal, own, 0.0), axis=0, keepdims=True)[:, :NU]
    mixed = jnp.broadcast_to(jnp.sum(system * weights, axis=1, keepdims=True), (16, LANES))
    scale = [jnp.broadcast_to(mixed[u : u + 1], (8, LANES)) for u in range(NU)]
    weight = [
        jnp.broadcast_to(
            jnp.sum(jnp.where(lane[:8] == NU + e, weights[:8], 0.0), axis=1, keepdims=True), (8, LANES)
        )
        for e in range(expos)
    ]
    first_col = expo_at * chunk
    for b in range(blocks):
        x = column_positions(first_col, b, width)
        gains = [scale[k] + scale[NB + k] * x for k in range(NB)]
        image = [
            recv_ref[e, :, ext + b * LANES : ext + (b + 1) * LANES].astype(jnp.float32) for e in range(expos)
        ]
        for r in range(0, rows, 8):
            total = weight[0] * image[0][r : r + 8]
            for e in range(1, expos):
                total = total + weight[e] * image[e][r : r + 8]
            model = scale[NU - 1]
            for k in range(NB):
                model = model + gains[k] * conv_ref[k, b, r : r + 8]
            coadd_ref[r : r + 8, b * LANES : (b + 1) * LANES] = total - model


def swaps(first, size):
    return [pair for i in range(first, size - 1, 2) for pair in ((i, i + 1), (i + 1, i))]


def tiled_device(template, science, plan, orders, coadd_weight, intersection):
    expos = lax.axis_size("expo")
    tiles = lax.axis_size("tile")
    _, rows, width = template.shape
    steps = science.shape[1]
    chunk = width // expos
    ext = chunk + LANES
    blocks = chunk // LANES
    where = jnp.stack([lax.axis_index("tile"), lax.axis_index("expo")]).astype(jnp.int32)
    smem = pl.BlockSpec(memory_space=pltpu.SMEM)
    vmem = pl.BlockSpec(memory_space=pltpu.VMEM)
    small = pltpu.CompilerParams(vmem_limit_bytes=16 * 1024 * 1024)
    hbm = pl.BlockSpec(memory_space=pltpu.HBM)
    row_band, col_band = pl.pallas_call(
        band_kernel,
        out_shape=(
            jax.ShapeDtypeStruct((NB * rows, 3 * rows), jnp.bfloat16),
            jax.ShapeDtypeStruct((NB, 2 * LANES, LANES), jnp.bfloat16),
        ),
        in_specs=[smem, smem],
        out_specs=(vmem, vmem),
        compiler_params=small,
        cost_estimate=pl.CostEstimate(flops=4_000_000, bytes_accessed=500_000, transcendentals=200_000),
    )(where, orders)
    coadds = []
    fitted = []
    for step in range(steps):
        send = pl.pallas_call(
            send_kernel,
            out_shape=pltpu.VMEM((expos, rows, ext + chunk), template.dtype),
            in_specs=[hbm, hbm],
            out_specs=vmem,
            scratch_shapes=[
                pltpu.VMEM((2, expos, rows, LANES), template.dtype),
                pltpu.SemaphoreType.DMA((4, expos)),
            ],
            compiler_params=small,
        )(
            pltpu.with_memory_space_constraint(template[0], pltpu.HBM),
            pltpu.with_memory_space_constraint(science[0, step], pltpu.HBM),
        )
        recv = lax.all_to_all(send, "expo", split_axis=0, concat_axis=0, tiled=True)
        own = pl.pallas_call(
            pick_kernel,
            out_shape=jax.ShapeDtypeStruct((rows, ext), template.dtype),
            in_specs=[smem, vmem],
            out_specs=vmem,
            compiler_params=small,
        )(plan[step : step + 1], recv)
        far = lax.ppermute(own, "tile", swaps(1, tiles))
        near = lax.ppermute(own, "tile", swaps(0, tiles))
        conv, sums = pl.pallas_call(
            functools.partial(fit_kernel, width=width),
            out_shape=(
                jax.ShapeDtypeStruct((NB, blocks, rows, LANES), jnp.float32),
                jax.ShapeDtypeStruct((tiles * expos, 8, LANES), jnp.float32),
            ),
            in_specs=[smem, smem, smem, vmem, vmem, vmem, vmem, vmem, vmem],
            out_specs=(vmem, vmem),
            scratch_shapes=[
                pltpu.VMEM((NB * rows, ext), jnp.bfloat16),
                pltpu.VMEM((2 * LANES, 8, LANES), jnp.float32),
            ],
            compiler_params=small,
        )(
            where,
            coadd_weight[:, step : step + 1],
            intersection[:, step : step + 1],
            row_band,
            col_band,
            own,
            near,
            far,
            recv,
        )
        sums = lax.all_to_all(sums, ("tile", "expo"), split_axis=0, concat_axis=0, tiled=True)
        coadd, coeffs = pl.pallas_call(
            functools.partial(solve_kernel, width=width, pixels=tiles * rows * width),
            out_shape=(
                jax.ShapeDtypeStruct((rows, chunk), jnp.float32),
                jax.ShapeDtypeStruct((1, NU), jnp.float32),
            ),
            in_specs=[smem, vmem, vmem, vmem, vmem],
            out_specs=(vmem, vmem),
            compiler_params=small,
        )(where, jnp.asarray(table(expos)), sums, conv, recv)
        coadds.append(coadd[None])
        fitted.append(coeffs)
    return (jnp.concatenate(coadds), jnp.stack(fitted, axis=1))


def broadcast(block, axis, holder):
    block = jnp.where(lax.axis_index(axis) == holder, block, jnp.zeros_like(block))
    return lax.psum(block, axis)


def extended(x, sides, width):
    for axis, dim in sides:
        size, length = (lax.axis_size(axis), x.shape[dim])
        up = [(i, (i + 1) % size) for i in range(size - 1)]
        down = [(j, i) for i, j in up]
        last = lax.slice_in_dim(x, length - width, length, axis=dim)
        first = lax.slice_in_dim(x, 0, width, axis=dim)
        before = lax.ppermute(last, axis, up)
        after = lax.ppermute(first, axis, down)
        x = jnp.concatenate([before, x, after], axis=dim)
    return x


def make_filters(orders):
    taps_pos = jnp.arange(2 * HALF + 1).astype(jnp.float32) - HALF
    row_list = []
    col_list = []
    for basis in range(NB):
        sigma = SIGMAS[basis]
        envelope = jnp.exp(-taps_pos * taps_pos / (2.0 * sigma * sigma))
        row_filter = envelope * power_of(taps_pos, orders[basis, 0])
        col_filter = envelope * power_of(taps_pos, orders[basis, 1])
        row_list.append(row_filter / jnp.sqrt(jnp.sum(row_filter * row_filter)))
        col_list.append(col_filter / jnp.sqrt(jnp.sum(col_filter * col_filter)))
    return (jnp.stack(row_list).astype(jnp.bfloat16), jnp.stack(col_list).astype(jnp.bfloat16))


def band_matrix(filters, out_len, in_len):
    offset = jnp.arange(in_len)[None, :] - jnp.arange(out_len)[:, None]
    taps_idx = jnp.arange(2 * HALF + 1)
    picks = (offset[:, :, None] == taps_idx[None, None, :]).astype(jnp.float32)
    band = jnp.einsum("ijt,kt->kij", picks, filters.astype(jnp.float32))
    return band.astype(jnp.bfloat16)


def any_device(template, science, plan, orders, coadd_weight, intersection):
    row_filters, col_filters = make_filters(orders)
    rows = template.shape[1]
    width = template.shape[2]
    blocks_count = width // 128
    steps_count = science.shape[1]
    row_band = band_matrix(row_filters, rows, rows + 2 * HALF)
    col_band = jnp.transpose(band_matrix(col_filters, 128, 128 + 2 * HALF), (0, 2, 1))
    column_pos = 2.0 * (jnp.arange(width).astype(jnp.float32) + 0.5) / width - 1.0
    pieces = []
    fitted = []
    for step in range(steps_count):
        received = broadcast(template[0], "expo", plan[step])
        padded = extended(received, (("tile", 0),), HALF)
        rowconv = jnp.einsum(
            "kij,jw->kiw", row_band, padded, preferred_element_type=jnp.float32
        ).astype(jnp.bfloat16)
        blocks = rowconv.reshape(NB, rows, blocks_count, 128)
        empty_rim = jnp.zeros((NB, rows, 1, HALF), jnp.bfloat16)
        previous = jnp.concatenate([empty_rim, blocks[:, :, :-1, 128 - HALF :]], axis=2)
        following = jnp.concatenate([blocks[:, :, 1:, :HALF], empty_rim], axis=2)
        window = jnp.concatenate([previous, blocks, following], axis=3)
        conv = jnp.einsum("krbj,kjc->krbc", window, col_band, preferred_element_type=jnp.float32)
        conv = conv.reshape(NB, rows, width)
        fields = jnp.concatenate(
            [conv, conv * column_pos, jnp.ones((1, rows, width), jnp.float32)], axis=0
        )
        fields = fields.reshape(NU, rows * width)
        exposure_image = science[0, step].astype(jnp.float32).reshape(rows * width)
        normal_local = jnp.dot(fields, fields.T, precision=lax.Precision.HIGHEST)
        project_local = jnp.dot(fields, exposure_image, precision=lax.Precision.HIGHEST)
        normal_matrix, projections = lax.psum((normal_local, project_local), "tile")
        normal_matrix = normal_matrix + RIDGE * (jnp.trace(normal_matrix) / NU) * jnp.eye(
            NU, dtype=jnp.float32
        )
        factor = jnp.linalg.cholesky(normal_matrix)
        coeffs = jax.scipy.linalg.cho_solve((factor, True), projections)
        model = jnp.dot(coeffs, fields, precision=lax.Precision.HIGHEST)
        difference = exposure_image - model
        weight_now = coadd_weight[0, step] * intersection[0, step].astype(jnp.float32)
        pieces.append((weight_now * difference).reshape(rows, width))
        fitted.append(coeffs)
    weighted = jnp.stack(pieces)
    received_parts = lax.all_to_all(weighted[None], "expo", split_axis=3, concat_axis=0, tiled=True)
    coadd = jnp.sum(received_parts, axis=0)
    return (coadd, jnp.stack(fitted)[None])


def per_device(template, science, plan, orders, coadd_weight, intersection):
    expos = lax.axis_size("expo")
    rows, width = template.shape[1:]
    whole_lanes = width % (expos * LANES) == 0 and rows % 16 == 0
    few = (NU + 1) * expos <= LANES and NU + expos <= LANES
    body = tiled_device if whole_lanes and few else any_device
    return body(template, science, plan, orders, coadd_weight, intersection)


def solution(mesh):
    return jax.shard_map(
        per_device,
        mesh=mesh,
        in_specs=(
            P(("groups", "expo"), "tile", None),
            P(("groups", "expo"), None, "tile", None),
            P("groups"),
            P(),
            P(("groups", "expo"), None),
            P(("groups", "expo"), None),
        ),
        out_specs=(P("groups", "tile", "expo"), P(("groups", "expo"), None, None)),
        check_vma=False,
    )
```

```python
import functools

import jax
import jax.numpy as jnp
import numpy as np
from jax import lax
from jax.experimental import pallas as pl
from jax.experimental.pallas import tpu as pltpu
from jax.sharding import PartitionSpec as P

HALF = 15
NB = 6
NU = 13
LANES = 128
PAIRS = [(j, k) for j in range(NB) for k in range(j, NB)]

SIGMAS = (0.8, 1.4, 2.2, 3.0, 4.0, 5.5)
RIDGE = 0.05


def power_of(pos, order):
    return jnp.where(order == 0, 1.0, jnp.where(order == 1, pos, pos * pos))


def tap_values(pos, sigma, order):
    value = jnp.exp(-pos * pos / (2.0 * sigma * sigma)) * power_of(pos, order)
    return jnp.where(jnp.abs(pos) <= HALF, value, 0.0)


def tap_norm(sigma, order):
    pos = lax.broadcasted_iota(jnp.int32, (8, LANES), 1).astype(jnp.float32) - HALF
    value = tap_values(pos, sigma, order)
    return jnp.sqrt(jnp.sum(value * value, axis=1, keepdims=True))[:1]


def send_kernel(template_ref, science_ref, out_ref, patch_ref, image_ref, sems):
    parts, rows, wide = out_ref.shape
    chunk = (wide - LANES) // 2
    half = parts * chunk // 2
    copies = [
        pltpu.make_async_copy(
            source.at[:, pl.ds(i * half, half)], target.at[:, pl.ds(i * half, half)], sems.at[at, i]
        )
        for at, (source, target) in enumerate(((template_ref, patch_ref), (science_ref, image_ref)))
        for i in range(2)
    ]
    for copy in copies:
        copy.start()
    for copy in copies[:2]:
        copy.wait()
    lane = lax.broadcasted_iota(jnp.int32, (rows, LANES), 1)
    for part in range(parts):
        start = part * chunk
        out_ref[part, :, :chunk] = patch_ref[:, start : start + chunk]
        before = patch_ref[:, start - LANES : start].astype(jnp.float32) if part else 0.0
        after = patch_ref[:, start + chunk : start + chunk + LANES].astype(jnp.float32) if part < parts - 1 else 0.0
        rim = jnp.where(lane < LANES // 2, after, before)
        out_ref[part, :, chunk : chunk + LANES] = rim.astype(out_ref.dtype)
    for copy in copies[2:]:
        copy.wait()
    for part in range(parts):
        out_ref[part, :, chunk + LANES :] = image_ref[:, part * chunk : (part + 1) * chunk]


def pick_kernel(owner_ref, recv_ref, row_band_ref, out_ref):
    del row_band_ref
    ext = out_ref.shape[1]
    chunk = ext - LANES
    block = recv_ref[owner_ref[0], :, :ext]
    rim = block[:, chunk:]
    whole = jnp.concatenate([rim, block], axis=1)
    out_ref[...] = whole[:, LANES - HALF : LANES - HALF + ext]


def column_positions(first_col, block, width):
    col = lax.broadcasted_iota(jnp.int32, (8, LANES), 1) + (first_col + block * LANES)
    return 2.0 * (col.astype(jnp.float32) + 0.5) / width - 1.0


def band_kernel(orders_ref, row_ref, col_ref):
    rows = row_ref.shape[0] // NB
    near = 1 - 2 * lax.rem(lax.axis_index("tile"), 2)
    source = lax.broadcasted_iota(jnp.int32, (rows, 3 * rows), 1)
    moved = jnp.where(source < rows, 0, jnp.where(source < 2 * rows, near - 1, -near - 2))
    offset = (
        source + moved * rows - lax.broadcasted_iota(jnp.int32, (rows, 3 * rows), 0)
    ).astype(jnp.float32)
    shift = (
        lax.broadcasted_iota(jnp.int32, (2 * LANES, LANES), 0)
        - lax.broadcasted_iota(jnp.int32, (2 * LANES, LANES), 1)
        - HALF
    ).astype(jnp.float32)
    for k in range(NB):
        norm = tap_norm(SIGMAS[k], orders_ref[k, 0])
        row_ref[k * rows : (k + 1) * rows] = (
            tap_values(offset, SIGMAS[k], orders_ref[k, 0]) / norm
        ).astype(jnp.bfloat16)
        norm = tap_norm(SIGMAS[k], orders_ref[k, 1])
        col_ref[k] = (tap_values(shift, SIGMAS[k], orders_ref[k, 1]) / norm).astype(jnp.bfloat16)


def fit_kernel(weight_ref, hits_ref, row_band_ref, col_band_ref, own_ref, near_ref, far_ref,
               recv_ref, conv_ref, sums_ref, row_ref, parts_ref, *, width):
    tile_at = lax.axis_index("tile")
    expo_at = lax.axis_index("expo")
    rows, ext = own_ref.shape
    expos = recv_ref.shape[0]
    chunk = ext - LANES
    blocks = chunk // LANES

    patch = jnp.concatenate([own_ref[...], near_ref[...], far_ref[...]], axis=0)
    row_ref[...] = jnp.dot(
        row_band_ref[...], patch, preferred_element_type=jnp.float32
    ).astype(jnp.bfloat16)
    for k in range(NB):
        window = jnp.concatenate(
            [
                row_ref[k * rows : (k + 1) * rows, b * LANES : (b + 2) * LANES]
                for b in range(blocks)
            ],
            axis=0,
        )
        out = jnp.dot(window, col_band_ref[k], preferred_element_type=jnp.float32)
        conv_ref[k] = out.reshape(blocks, rows, LANES)

    first_col = expo_at * chunk
    xs = [column_positions(first_col, b, width) for b in range(blocks)]

    def fold(x):
        total = x[:8]
        for i in range(8, rows, 8):
            total = total + x[i : i + 8]
        return total

    def moments(at, left, right, count):
        total = [None] * count
        for b in range(blocks):
            term = fold(left(b) * right(b)) if right is not None else fold(left(b))
            for i in range(count):
                total[i] = term if total[i] is None else total[i] + term
                if i < count - 1:
                    term = term * xs[b]
        for i in range(count):
            parts_ref[at + i] = total[i]

    def conv(k):
        return lambda b: conv_ref[k, b]

    def sci(e):
        return lambda b: recv_ref[e, :, ext + b * LANES : ext + (b + 1) * LANES].astype(jnp.float32)

    blank = jnp.zeros((8, LANES), jnp.float32)
    at = 0
    for j, k in PAIRS:
        moments(at, conv(j), conv(k), 3)
        at += 3
    for k in range(NB):
        moments(at, conv(k), None, 2)
        at += 2
    while at % 8:
        parts_ref[at] = blank
        at += 1
    begin = at
    for e in range(expos):
        for k in range(NB):
            moments(at, conv(k), sci(e), 2)
            at += 2
        moments(at, sci(e), None, 1)
        at += 1
    weight = weight_ref[0, 0] * hits_ref[0, 0].astype(jnp.float32)
    weight = jnp.where(tile_at == 0, weight, 0.0)
    spot = (
        (lax.broadcasted_iota(jnp.int32, (8, LANES), 0) == 0)
        & (lax.broadcasted_iota(jnp.int32, (8, LANES), 1) == 0)
    )
    for e in range(expos):
        parts_ref[at + e] = jnp.where(spot & (expo_at == e), weight, 0.0)
    at += expos
    while at % 8:
        parts_ref[at] = blank
        at += 1
    ones = jnp.ones((8, LANES), jnp.float32)
    rows_of = []
    for first, last in ((0, begin), (begin, at)):
        lanes = jnp.sum(parts_ref[first:last], axis=1)
        spare = LANES - (last - first)
        if spare:
            lanes = jnp.concatenate([lanes, jnp.zeros((spare, LANES), jnp.float32)], axis=0)
        rows_of.append(
            lax.dot_general(
                ones,
                lanes,
                (((1,), (1,)), ((), ())),
                precision=lax.Precision.HIGHEST,
                preferred_element_type=jnp.float32,
            )
        )
    both = jnp.where(lax.broadcasted_iota(jnp.int32, (8, LANES), 0) < 4, rows_of[0], rows_of[1])
    for i in range(sums_ref.shape[0]):
        sums_ref[i] = both


def table(expos):
    matrix = np.zeros((16, LANES), np.int32)
    for at, (j, k) in enumerate(PAIRS):
        for a, b in ((j, k), (k, j)):
            matrix[a, b] = 3 * at
            matrix[a, NB + b] = matrix[NB + a, b] = 3 * at + 1
            matrix[NB + a, NB + b] = 3 * at + 2
    for k in range(NB):
        for x in range(2):
            matrix[x * NB + k, NU - 1] = matrix[NU - 1, x * NB + k] = 3 * len(PAIRS) + 2 * k + x
    for e in range(expos):
        for k in range(NB):
            for x in range(2):
                matrix[x * NB + k, NU + e] = NU * e + 2 * k + x
        matrix[NU - 1, NU + e] = NU * e + NU - 1
        matrix[NU:, NU + e] = NU * expos + e
    return matrix


def solve_kernel(table_ref, sums_ref, conv_ref, recv_ref, coadd_ref, coeffs_ref, tile_ref, sems, *, width,
                 pixels):
    expo_at = lax.axis_index("expo")
    expos, rows, wide = recv_ref.shape
    chunk = coadd_ref.shape[1]
    blocks = chunk // LANES
    ext = wide - chunk
    where = table_ref[...]
    sub = lax.broadcasted_iota(jnp.int32, (16, LANES), 0)
    lane = lax.broadcasted_iota(jnp.int32, (16, LANES), 1)
    sums = sums_ref[0]
    for i in range(1, sums_ref.shape[0]):
        sums = sums + sums_ref[i]
    first = jnp.broadcast_to(sums[0:1], (16, LANES))
    second = jnp.broadcast_to(sums[4:5], (16, LANES))
    picked = jnp.where(
        lane < NU,
        jnp.take_along_axis(first, where, axis=1),
        jnp.take_along_axis(second, where, axis=1),
    )
    weights = jnp.where((lane >= NU) & (lane < NU + expos), picked[15:16], 0.0)
    mine = (sub < NU) & (lane < NU + expos)
    system = jnp.where((sub == NU - 1) & (lane == NU - 1), float(pixels), picked)
    system = jnp.where(mine, system, 0.0)

    diagonal = (sub == lane) & (sub < NU)
    trace = jnp.sum(jnp.where(diagonal, system, 0.0), axis=0, keepdims=True)
    trace = jnp.sum(trace, axis=1, keepdims=True)
    system = system / trace + jnp.where(diagonal, RIDGE / NU, 0.0)
    for i in range(0, NU - 1, 2):
        col0, col1 = system[:, i : i + 1], system[:, i + 1 : i + 2]
        row0, row1 = system[i : i + 1], system[i + 1 : i + 2]
        a, b = col0[i : i + 1], col1[i : i + 1]
        c, d = col0[i + 1 : i + 2], col1[i + 1 : i + 2]
        scale = 1.0 / (a * d - b * c)
        new0 = (d * row0 - b * row1) * scale
        new1 = (a * row1 - c * row0) * scale
        rest = system - col0 * new0 - col1 * new1
        system = jnp.where(sub == i, new0, jnp.where(sub == i + 1, new1, rest))
    last = NU - 1
    row = system[last : last + 1] / system[last : last + 1, last : last + 1]
    system = jnp.where(sub == last, row, system - system[:, last : last + 1] * row)

    own = jnp.sum(jnp.where(lane == NU + expo_at, system, 0.0), axis=1, keepdims=True)
    coeffs_ref[...] = jnp.sum(jnp.where(diagonal, own, 0.0), axis=0, keepdims=True)[:, :NU]
    mixed = jnp.broadcast_to(jnp.sum(system * weights, axis=1, keepdims=True), (16, LANES))
    scale = [jnp.broadcast_to(mixed[u : u + 1], (8, LANES)) for u in range(NU)]
    weight = [
        jnp.broadcast_to(
            jnp.sum(jnp.where(lane[:8] == NU + e, weights[:8], 0.0), axis=1, keepdims=True), (8, LANES)
        )
        for e in range(expos)
    ]
    first_col = expo_at * chunk
    copies = []
    for r in range(0, rows, 8):
        for b in range(blocks):
            columns = slice(ext + b * LANES, ext + (b + 1) * LANES)
            x = column_positions(first_col, b, width)
            total = -scale[NU - 1]
            for e in range(expos):
                total = total + weight[e] * recv_ref[e, :, columns].astype(jnp.float32)[r : r + 8]
            model = (scale[0] + scale[NB] * x) * conv_ref[0, b, r : r + 8]
            for k in range(1, NB):
                model = model + (scale[k] + scale[NB + k] * x) * conv_ref[k, b, r : r + 8]
            tile_ref[r : r + 8, b * LANES : (b + 1) * LANES] = total - model
        copies.append(
            pltpu.make_async_copy(tile_ref.at[pl.ds(r, 8)], coadd_ref.at[pl.ds(r, 8)], sems.at[r // 8])
        )
        copies[-1].start()
    for copy in copies:
        copy.wait()


def swaps(first, size):
    return [pair for i in range(first, size - 1, 2) for pair in ((i, i + 1), (i + 1, i))]


def tiled_device(template, science, plan, orders, coadd_weight, intersection):
    expos = lax.axis_size("expo")
    tiles = lax.axis_size("tile")
    _, rows, width = template.shape
    steps = science.shape[1]
    chunk = width // expos
    ext = chunk + LANES
    blocks = chunk // LANES
    smem = pl.BlockSpec(memory_space=pltpu.SMEM)
    vmem = pl.BlockSpec(memory_space=pltpu.VMEM)
    small = pltpu.CompilerParams(vmem_limit_bytes=16 * 1024 * 1024)
    hbm = pl.BlockSpec(memory_space=pltpu.HBM)
    row_band, col_band = pl.pallas_call(
        band_kernel,
        out_shape=(
            jax.ShapeDtypeStruct((NB * rows, 3 * rows), jnp.bfloat16),
            jax.ShapeDtypeStruct((NB, 2 * LANES, LANES), jnp.bfloat16),
        ),
        in_specs=[smem],
        out_specs=(vmem, vmem),
        compiler_params=small,
        cost_estimate=pl.CostEstimate(flops=4_000_000, bytes_accessed=500_000, transcendentals=200_000),
    )(orders)
    coadds = []
    fitted = []
    for step in range(steps):
        send = pl.pallas_call(
            send_kernel,
            out_shape=pltpu.VMEM((expos, rows, ext + chunk), template.dtype),
            in_specs=[hbm, hbm],
            out_specs=vmem,
            scratch_shapes=[
                pltpu.VMEM((rows, width), template.dtype),
                pltpu.VMEM((rows, width), science.dtype),
                pltpu.SemaphoreType.DMA((2, 2)),
            ],
            compiler_params=small,
        )(
            pltpu.with_memory_space_constraint(template[0], pltpu.HBM),
            pltpu.with_memory_space_constraint(science[0, step], pltpu.HBM),
        )
        recv = lax.all_to_all(send, "expo", split_axis=0, concat_axis=0, tiled=True)
        own = pl.pallas_call(
            pick_kernel,
            out_shape=jax.ShapeDtypeStruct((rows, ext), template.dtype),
            in_specs=[smem, vmem, pl.BlockSpec(memory_space=pl.ANY)],
            out_specs=vmem,
            compiler_params=small,
        )(plan[step : step + 1], recv, row_band)
        far = lax.ppermute(own, "tile", swaps(1, tiles))
        near = lax.ppermute(own, "tile", swaps(0, tiles))
        conv, sums = pl.pallas_call(
            functools.partial(fit_kernel, width=width),
            out_shape=(
                jax.ShapeDtypeStruct((NB, blocks, rows, LANES), jnp.float32),
                jax.ShapeDtypeStruct((tiles * expos, 8, LANES), jnp.float32),
            ),
            in_specs=[smem, smem, vmem, vmem, vmem, vmem, vmem, vmem],
            out_specs=(vmem, vmem),
            scratch_shapes=[
                pltpu.VMEM((NB * rows, ext), jnp.bfloat16),
                pltpu.VMEM((80 + 14 * expos + 8, 8, LANES), jnp.float32),
            ],
            compiler_params=small,
        )(
            coadd_weight[:, step : step + 1],
            intersection[:, step : step + 1],
            row_band,
            col_band,
            own,
            near,
            far,
            recv,
        )
        sums = lax.all_to_all(sums, ("tile", "expo"), split_axis=0, concat_axis=0, tiled=True)
        coadd, coeffs = pl.pallas_call(
            functools.partial(solve_kernel, width=width, pixels=tiles * rows * width),
            out_shape=(
                jax.ShapeDtypeStruct((rows, chunk), jnp.float32),
                jax.ShapeDtypeStruct((1, NU), jnp.float32),
            ),
            in_specs=[vmem, vmem, vmem, vmem],
            out_specs=(pl.BlockSpec(memory_space=pl.ANY), vmem),
            scratch_shapes=[
                pltpu.VMEM((rows, chunk), jnp.float32),
                pltpu.SemaphoreType.DMA((rows // 8,)),
            ],
            compiler_params=small,
        )(jnp.asarray(table(expos)), sums, conv, recv)
        coadds.append(coadd[None])
        fitted.append(coeffs)
    return (jnp.concatenate(coadds), jnp.stack(fitted, axis=1))


def broadcast(block, axis, holder):
    block = jnp.where(lax.axis_index(axis) == holder, block, jnp.zeros_like(block))
    return lax.psum(block, axis)


def extended(x, sides, width):
    for axis, dim in sides:
        size, length = (lax.axis_size(axis), x.shape[dim])
        up = [(i, (i + 1) % size) for i in range(size - 1)]
        down = [(j, i) for i, j in up]
        last = lax.slice_in_dim(x, length - width, length, axis=dim)
        first = lax.slice_in_dim(x, 0, width, axis=dim)
        before = lax.ppermute(last, axis, up)
        after = lax.ppermute(first, axis, down)
        x = jnp.concatenate([before, x, after], axis=dim)
    return x


def make_filters(orders):
    taps_pos = jnp.arange(2 * HALF + 1).astype(jnp.float32) - HALF
    row_list = []
    col_list = []
    for basis in range(NB):
        sigma = SIGMAS[basis]
        envelope = jnp.exp(-taps_pos * taps_pos / (2.0 * sigma * sigma))
        row_filter = envelope * power_of(taps_pos, orders[basis, 0])
        col_filter = envelope * power_of(taps_pos, orders[basis, 1])
        row_list.append(row_filter / jnp.sqrt(jnp.sum(row_filter * row_filter)))
        col_list.append(col_filter / jnp.sqrt(jnp.sum(col_filter * col_filter)))
    return (jnp.stack(row_list).astype(jnp.bfloat16), jnp.stack(col_list).astype(jnp.bfloat16))


def band_matrix(filters, out_len, in_len):
    offset = jnp.arange(in_len)[None, :] - jnp.arange(out_len)[:, None]
    taps_idx = jnp.arange(2 * HALF + 1)
    picks = (offset[:, :, None] == taps_idx[None, None, :]).astype(jnp.float32)
    band = jnp.einsum("ijt,kt->kij", picks, filters.astype(jnp.float32))
    return band.astype(jnp.bfloat16)


def any_device(template, science, plan, orders, coadd_weight, intersection):
    row_filters, col_filters = make_filters(orders)
    rows = template.shape[1]
    width = template.shape[2]
    blocks_count = width // 128
    steps_count = science.shape[1]
    row_band = band_matrix(row_filters, rows, rows + 2 * HALF)
    col_band = jnp.transpose(band_matrix(col_filters, 128, 128 + 2 * HALF), (0, 2, 1))
    column_pos = 2.0 * (jnp.arange(width).astype(jnp.float32) + 0.5) / width - 1.0
    pieces = []
    fitted = []
    for step in range(steps_count):
        received = broadcast(template[0], "expo", plan[step])
        padded = extended(received, (("tile", 0),), HALF)
        rowconv = jnp.einsum(
            "kij,jw->kiw", row_band, padded, preferred_element_type=jnp.float32
        ).astype(jnp.bfloat16)
        blocks = rowconv.reshape(NB, rows, blocks_count, 128)
        empty_rim = jnp.zeros((NB, rows, 1, HALF), jnp.bfloat16)
        previous = jnp.concatenate([empty_rim, blocks[:, :, :-1, 128 - HALF :]], axis=2)
        following = jnp.concatenate([blocks[:, :, 1:, :HALF], empty_rim], axis=2)
        window = jnp.concatenate([previous, blocks, following], axis=3)
        conv = jnp.einsum("krbj,kjc->krbc", window, col_band, preferred_element_type=jnp.float32)
        conv = conv.reshape(NB, rows, width)
        fields = jnp.concatenate(
            [conv, conv * column_pos, jnp.ones((1, rows, width), jnp.float32)], axis=0
        )
        fields = fields.reshape(NU, rows * width)
        exposure_image = science[0, step].astype(jnp.float32).reshape(rows * width)
        normal_local = jnp.dot(fields, fields.T, precision=lax.Precision.HIGHEST)
        project_local = jnp.dot(fields, exposure_image, precision=lax.Precision.HIGHEST)
        normal_matrix, projections = lax.psum((normal_local, project_local), "tile")
        normal_matrix = normal_matrix + RIDGE * (jnp.trace(normal_matrix) / NU) * jnp.eye(
            NU, dtype=jnp.float32
        )
        factor = jnp.linalg.cholesky(normal_matrix)
        coeffs = jax.scipy.linalg.cho_solve((factor, True), projections)
        model = jnp.dot(coeffs, fields, precision=lax.Precision.HIGHEST)
        difference = exposure_image - model
        weight_now = coadd_weight[0, step] * intersection[0, step].astype(jnp.float32)
        pieces.append((weight_now * difference).reshape(rows, width))
        fitted.append(coeffs)
    weighted = jnp.stack(pieces)
    received_parts = lax.all_to_all(weighted[None], "expo", split_axis=3, concat_axis=0, tiled=True)
    coadd = jnp.sum(received_parts, axis=0)
    return (coadd, jnp.stack(fitted)[None])


def per_device(template, science, plan, orders, coadd_weight, intersection):
    expos = lax.axis_size("expo")
    rows, width = template.shape[1:]
    whole_lanes = width % (expos * LANES) == 0 and rows % 16 == 0
    few = (NU + 1) * expos <= LANES and NU + expos <= LANES
    body = tiled_device if whole_lanes and few else any_device
    return body(template, science, plan, orders, coadd_weight, intersection)


def solution(mesh):
    return jax.shard_map(
        per_device,
        mesh=mesh,
        in_specs=(
            P(("groups", "expo"), "tile", None),
            P(("groups", "expo"), None, "tile", None),
            P("groups"),
            P(),
            P(("groups", "expo"), None),
            P(("groups", "expo"), None),
        ),
        out_specs=(P("groups", "tile", "expo"), P(("groups", "expo"), None, None)),
        check_vma=False,
    )
```

```python
import functools

import jax
import jax.numpy as jnp
import numpy as np
from jax import lax
from jax.experimental import pallas as pl
from jax.experimental.pallas import tpu as pltpu
from jax.sharding import PartitionSpec as P

HALF = 15
NB = 6
NU = 13
LANES = 128
PAIRS = [(j, k) for j in range(NB) for k in range(j, NB)]

SIGMAS = (0.8, 1.4, 2.2, 3.0, 4.0, 5.5)
RIDGE = 0.05


def power_of(pos, order):
    return jnp.where(order == 0, 1.0, jnp.where(order == 1, pos, pos * pos))


def tap_values(pos, sigma, order):
    value = jnp.exp(-pos * pos / (2.0 * sigma * sigma)) * power_of(pos, order)
    return jnp.where(jnp.abs(pos) <= HALF, value, 0.0)


def tap_norm(sigma, order):
    pos = lax.broadcasted_iota(jnp.int32, (8, LANES), 1).astype(jnp.float32) - HALF
    value = tap_values(pos, sigma, order)
    return jnp.sqrt(jnp.sum(value * value, axis=1, keepdims=True))[:1]


def send_kernel(template_ref, science_ref, out_ref, patch_ref, image_ref, sems):
    parts, rows, wide = out_ref.shape
    chunk = (wide - LANES) // 2
    half = parts * chunk // 2
    copies = [
        pltpu.make_async_copy(
            source.at[:, pl.ds(i * half, half)], target.at[:, pl.ds(i * half, half)], sems.at[at, i]
        )
        for at, (source, target) in enumerate(((template_ref, patch_ref), (science_ref, image_ref)))
        for i in range(2)
    ]
    for copy in copies:
        copy.start()
    for copy in copies[:2]:
        copy.wait()
    lane = lax.broadcasted_iota(jnp.int32, (rows, LANES), 1)
    for part in range(parts):
        start = part * chunk
        out_ref[part, :, :chunk] = patch_ref[:, start : start + chunk]
        before = patch_ref[:, start - LANES : start].astype(jnp.float32) if part else 0.0
        after = patch_ref[:, start + chunk : start + chunk + LANES].astype(jnp.float32) if part < parts - 1 else 0.0
        rim = jnp.where(lane < LANES // 2, after, before)
        out_ref[part, :, chunk : chunk + LANES] = rim.astype(out_ref.dtype)
    for copy in copies[2:]:
        copy.wait()
    for part in range(parts):
        out_ref[part, :, chunk + LANES :] = image_ref[:, part * chunk : (part + 1) * chunk]


def pick_kernel(owner_ref, recv_ref, out_ref):
    rows, ext = out_ref.shape
    chunk = ext - LANES
    blocks = []
    for b in range(ext // LANES):
        columns = slice(b * LANES, (b + 1) * LANES)
        block = recv_ref[0, :, columns].astype(jnp.float32)
        for e in range(1, recv_ref.shape[0]):
            block = jnp.where(owner_ref[...] == e, recv_ref[e, :, columns].astype(jnp.float32), block)
        blocks.append(block.astype(out_ref.dtype))
    whole = jnp.concatenate(blocks[-1:] + blocks, axis=1)
    out_ref[...] = whole[:, LANES - HALF : LANES - HALF + ext]


def column_positions(first_col, block, width):
    col = lax.broadcasted_iota(jnp.int32, (8, LANES), 1) + (first_col + block * LANES)
    return 2.0 * (col.astype(jnp.float32) + 0.5) / width - 1.0


def band_kernel(orders_ref, plan_ref, weight_ref, hits_ref, row_ref, col_ref, owner_ref, own_weight_ref):
    for step in range(owner_ref.shape[0]):
        owner_ref[step] = jnp.full(owner_ref.shape[1:], plan_ref[step], jnp.int32)
        weight = weight_ref[0, step] * hits_ref[0, step].astype(jnp.float32)
        own_weight_ref[step] = jnp.full(own_weight_ref.shape[1:], weight, jnp.float32)
    rows = row_ref.shape[0] // NB
    near = 1 - 2 * lax.rem(lax.axis_index("tile"), 2)
    source = lax.broadcasted_iota(jnp.int32, (rows, 3 * rows), 1)
    moved = jnp.where(source < rows, 0, jnp.where(source < 2 * rows, near - 1, -near - 2))
    offset = (
        source + moved * rows - lax.broadcasted_iota(jnp.int32, (rows, 3 * rows), 0)
    ).astype(jnp.float32)
    shift = (
        lax.broadcasted_iota(jnp.int32, (2 * LANES, LANES), 0)
        - lax.broadcasted_iota(jnp.int32, (2 * LANES, LANES), 1)
        - HALF
    ).astype(jnp.float32)
    for k in range(NB):
        norm = tap_norm(SIGMAS[k], orders_ref[k, 0])
        row_ref[k * rows : (k + 1) * rows] = (
            tap_values(offset, SIGMAS[k], orders_ref[k, 0]) / norm
        ).astype(jnp.bfloat16)
        norm = tap_norm(SIGMAS[k], orders_ref[k, 1])
        col_ref[k] = (tap_values(shift, SIGMAS[k], orders_ref[k, 1]) / norm).astype(jnp.bfloat16)


def fit_kernel(weight_ref, row_band_ref, col_band_ref, own_ref, near_ref, far_ref,
               recv_ref, conv_ref, sums_ref, row_ref, parts_ref, *, width):
    tile_at = lax.axis_index("tile")
    expo_at = lax.axis_index("expo")
    rows, ext = own_ref.shape
    expos = recv_ref.shape[0]
    chunk = ext - LANES
    blocks = chunk // LANES

    patch = jnp.concatenate([own_ref[...], near_ref[...], far_ref[...]], axis=0)
    row_ref[...] = jnp.dot(
        row_band_ref[...], patch, preferred_element_type=jnp.float32
    ).astype(jnp.bfloat16)
    for k in range(NB):
        window = jnp.concatenate(
            [
                row_ref[k * rows : (k + 1) * rows, b * LANES : (b + 2) * LANES]
                for b in range(blocks)
            ],
            axis=0,
        )
        out = jnp.dot(window, col_band_ref[k], preferred_element_type=jnp.float32)
        conv_ref[k] = out.reshape(blocks, rows, LANES)

    first_col = expo_at * chunk
    xs = [column_positions(first_col, b, width) for b in range(blocks)]

    def fold(x):
        total = x[:8]
        for i in range(8, rows, 8):
            total = total + x[i : i + 8]
        return total

    def moments(at, left, right, count):
        total = [None] * count
        for b in range(blocks):
            term = fold(left(b) * right(b)) if right is not None else fold(left(b))
            for i in range(count):
                total[i] = term if total[i] is None else total[i] + term
                if i < count - 1:
                    term = term * xs[b]
        for i in range(count):
            parts_ref[at + i] = total[i]

    def conv(k):
        return lambda b: conv_ref[k, b]

    def sci(e):
        return lambda b: recv_ref[e, :, ext + b * LANES : ext + (b + 1) * LANES].astype(jnp.float32)

    blank = jnp.zeros((8, LANES), jnp.float32)
    at = 0
    for j, k in PAIRS:
        moments(at, conv(j), conv(k), 3)
        at += 3
    for k in range(NB):
        moments(at, conv(k), None, 2)
        at += 2
    while at % 8:
        parts_ref[at] = blank
        at += 1
    begin = at
    for e in range(expos):
        for k in range(NB):
            moments(at, conv(k), sci(e), 2)
            at += 2
        moments(at, sci(e), None, 1)
        at += 1
    weight = jnp.where(tile_at == 0, weight_ref[...], 0.0)
    spot = (
        (lax.broadcasted_iota(jnp.int32, (8, LANES), 0) == 0)
        & (lax.broadcasted_iota(jnp.int32, (8, LANES), 1) == 0)
    )
    for e in range(expos):
        parts_ref[at + e] = jnp.where(spot & (expo_at == e), weight, 0.0)
    at += expos
    while at % 8:
        parts_ref[at] = blank
        at += 1
    ones = jnp.ones((8, LANES), jnp.float32)
    rows_of = []
    for first, last in ((0, begin), (begin, at)):
        lanes = jnp.sum(parts_ref[first:last], axis=1)
        spare = LANES - (last - first)
        if spare:
            lanes = jnp.concatenate([lanes, jnp.zeros((spare, LANES), jnp.float32)], axis=0)
        rows_of.append(
            lax.dot_general(
                ones,
                lanes,
                (((1,), (1,)), ((), ())),
                precision=lax.Precision.HIGHEST,
                preferred_element_type=jnp.float32,
            )
        )
    both = jnp.where(lax.broadcasted_iota(jnp.int32, (8, LANES), 0) < 4, rows_of[0], rows_of[1])
    for i in range(sums_ref.shape[0]):
        sums_ref[i] = both


def table(expos):
    columns = np.zeros((NU + expos + 1, 16), np.int32)
    for at, (j, k) in enumerate(PAIRS):
        for a, b in ((j, k), (k, j)):
            columns[b, a] = 3 * at
            columns[NB + b, a] = columns[b, NB + a] = 3 * at + 1
            columns[NB + b, NB + a] = 3 * at + 2
    for k in range(NB):
        for x in range(2):
            columns[NU - 1, x * NB + k] = columns[x * NB + k, NU - 1] = 3 * len(PAIRS) + 2 * k + x
    for e in range(expos):
        columns[NU + e, :NU] = [NU * e + 2 * k + x for x in range(2) for k in range(NB)] + [NU * e + NU - 1]
        columns[NU + expos, e] = NU * expos + e
    return np.ascontiguousarray(np.broadcast_to(columns[:, :, None], columns.shape + (LANES,)))


def solve_kernel(table_ref, sums_ref, conv_ref, recv_ref, coadd_ref, coeffs_ref, tile_ref, sems, *, width,
                 pixels):
    expo_at = lax.axis_index("expo")
    expos, rows, wide = recv_ref.shape
    chunk = coadd_ref.shape[1]
    blocks = chunk // LANES
    ext = wide - chunk
    sub = lax.broadcasted_iota(jnp.int32, (16, LANES), 0)
    lane = lax.broadcasted_iota(jnp.int32, (16, LANES), 1)
    sums = sums_ref[0]
    for i in range(1, sums_ref.shape[0]):
        sums = sums + sums_ref[i]
    first = jnp.broadcast_to(sums[0:1], (16, LANES))
    second = jnp.broadcast_to(sums[4:5], (16, LANES))

    columns = [
        jnp.take_along_axis(first if j < NU else second, table_ref[j], axis=1) for j in range(NU + expos)
    ]
    spread = jnp.take_along_axis(second, table_ref[NU + expos], axis=1)
    weight = [jnp.broadcast_to(spread[e : e + 1], (16, LANES)) for e in range(expos)]
    columns[NU - 1] = jnp.where(sub == NU - 1, float(pixels), columns[NU - 1])

    trace = columns[0][0:1]
    for j in range(1, NU):
        trace = trace + columns[j][j : j + 1]
    scale = 1.0 / trace
    for j in range(NU + expos):
        columns[j] = columns[j] * scale
        if j < NU:
            columns[j] = columns[j] + jnp.where(sub == j, RIDGE / NU, 0.0)
    for i in range(NU):
        inverse = 1.0 / columns[i][i : i + 1]
        for j in range(i + 1, NU + expos):
            factor = columns[j][i : i + 1] * inverse
            columns[j] = jnp.where(sub == i, factor, columns[j] - columns[i] * factor)

    solved = columns[NU:]
    own = solved[0]
    mixed = weight[0] * solved[0]
    for e in range(1, expos):
        own = jnp.where(expo_at == e, solved[e], own)
        mixed = mixed + weight[e] * solved[e]
    diagonal = (sub == lane) & (sub < NU)
    coeffs_ref[...] = jnp.sum(jnp.where(diagonal, own, 0.0), axis=0, keepdims=True)[:, :NU]
    scale = [jnp.broadcast_to(mixed[u : u + 1], (8, LANES)) for u in range(NU)]
    weight = [value[:8] for value in weight]
    first_col = expo_at * chunk
    copies = []
    for r in range(0, rows, 8):
        for b in range(blocks):
            at = slice(ext + b * LANES, ext + (b + 1) * LANES)
            x = column_positions(first_col, b, width)
            total = -scale[NU - 1]
            for e in range(expos):
                total = total + weight[e] * recv_ref[e, :, at].astype(jnp.float32)[r : r + 8]
            model = (scale[0] + scale[NB] * x) * conv_ref[0, b, r : r + 8]
            for k in range(1, NB):
                model = model + (scale[k] + scale[NB + k] * x) * conv_ref[k, b, r : r + 8]
            tile_ref[r : r + 8, b * LANES : (b + 1) * LANES] = total - model
        copies.append(
            pltpu.make_async_copy(tile_ref.at[pl.ds(r, 8)], coadd_ref.at[pl.ds(r, 8)], sems.at[r // 8])
        )
        copies[-1].start()
    for copy in copies:
        copy.wait()


def swaps(first, size):
    return [pair for i in range(first, size - 1, 2) for pair in ((i, i + 1), (i + 1, i))]


def tiled_device(template, science, plan, orders, coadd_weight, intersection):
    expos = lax.axis_size("expo")
    tiles = lax.axis_size("tile")
    _, rows, width = template.shape
    steps = science.shape[1]
    chunk = width // expos
    ext = chunk + LANES
    blocks = chunk // LANES
    smem = pl.BlockSpec(memory_space=pltpu.SMEM)
    vmem = pl.BlockSpec(memory_space=pltpu.VMEM)
    small = pltpu.CompilerParams(vmem_limit_bytes=16 * 1024 * 1024)
    hbm = pl.BlockSpec(memory_space=pltpu.HBM)
    row_band, col_band, owner, own_weight = pl.pallas_call(
        band_kernel,
        out_shape=(
            jax.ShapeDtypeStruct((NB * rows, 3 * rows), jnp.bfloat16),
            jax.ShapeDtypeStruct((NB, 2 * LANES, LANES), jnp.bfloat16),
            jax.ShapeDtypeStruct((steps, rows, LANES), jnp.int32),
            jax.ShapeDtypeStruct((steps, 8, LANES), jnp.float32),
        ),
        in_specs=[smem] * 4,
        out_specs=(vmem,) * 4,
        compiler_params=small,
        cost_estimate=pl.CostEstimate(flops=4_000_000, bytes_accessed=500_000, transcendentals=200_000),
    )(orders, plan, coadd_weight, intersection)
    coadds = []
    fitted = []
    for step in range(steps):
        send = pl.pallas_call(
            send_kernel,
            out_shape=pltpu.VMEM((expos, rows, ext + chunk), template.dtype),
            in_specs=[hbm, hbm],
            out_specs=vmem,
            scratch_shapes=[
                pltpu.VMEM((rows, width), template.dtype),
                pltpu.VMEM((rows, width), science.dtype),
                pltpu.SemaphoreType.DMA((2, 2)),
            ],
            compiler_params=small,
        )(
            pltpu.with_memory_space_constraint(template[0], pltpu.HBM),
            pltpu.with_memory_space_constraint(science[0, step], pltpu.HBM),
        )
        recv = lax.all_to_all(send, "expo", split_axis=0, concat_axis=0, tiled=True)
        own = pl.pallas_call(
            pick_kernel,
            out_shape=jax.ShapeDtypeStruct((rows, ext), template.dtype),
            in_specs=[vmem, vmem],
            out_specs=vmem,
            compiler_params=small,
        )(owner[step], recv)
        far = lax.ppermute(own, "tile", swaps(1, tiles))
        near = lax.ppermute(own, "tile", swaps(0, tiles))
        conv, sums = pl.pallas_call(
            functools.partial(fit_kernel, width=width),
            out_shape=(
                jax.ShapeDtypeStruct((NB, blocks, rows, LANES), jnp.float32),
                jax.ShapeDtypeStruct((tiles * expos, 8, LANES), jnp.float32),
            ),
            in_specs=[vmem] * 7,
            out_specs=(vmem, vmem),
            scratch_shapes=[
                pltpu.VMEM((NB * rows, ext), jnp.bfloat16),
                pltpu.VMEM((80 + 14 * expos + 8, 8, LANES), jnp.float32),
            ],
            compiler_params=small,
        )(
            own_weight[step],
            row_band,
            col_band,
            own,
            near,
            far,
            recv,
        )
        sums = lax.all_to_all(sums, ("tile", "expo"), split_axis=0, concat_axis=0, tiled=True)
        coadd, coeffs = pl.pallas_call(
            functools.partial(solve_kernel, width=width, pixels=tiles * rows * width),
            out_shape=(
                jax.ShapeDtypeStruct((rows, chunk), jnp.float32),
                jax.ShapeDtypeStruct((1, NU), jnp.float32),
            ),
            in_specs=[vmem, vmem, vmem, vmem],
            out_specs=(pl.BlockSpec(memory_space=pl.ANY), vmem),
            scratch_shapes=[
                pltpu.VMEM((rows, chunk), jnp.float32),
                pltpu.SemaphoreType.DMA((rows // 8,)),
            ],
            compiler_params=small,
        )(jnp.asarray(table(expos)), sums, conv, recv)
        coadds.append(coadd[None])
        fitted.append(coeffs)
    return (jnp.concatenate(coadds), jnp.stack(fitted, axis=1))


def broadcast(block, axis, holder):
    block = jnp.where(lax.axis_index(axis) == holder, block, jnp.zeros_like(block))
    return lax.psum(block, axis)


def extended(x, sides, width):
    for axis, dim in sides:
        size, length = (lax.axis_size(axis), x.shape[dim])
        up = [(i, (i + 1) % size) for i in range(size - 1)]
        down = [(j, i) for i, j in up]
        last = lax.slice_in_dim(x, length - width, length, axis=dim)
        first = lax.slice_in_dim(x, 0, width, axis=dim)
        before = lax.ppermute(last, axis, up)
        after = lax.ppermute(first, axis, down)
        x = jnp.concatenate([before, x, after], axis=dim)
    return x


def make_filters(orders):
    taps_pos = jnp.arange(2 * HALF + 1).astype(jnp.float32) - HALF
    row_list = []
    col_list = []
    for basis in range(NB):
        sigma = SIGMAS[basis]
        envelope = jnp.exp(-taps_pos * taps_pos / (2.0 * sigma * sigma))
        row_filter = envelope * power_of(taps_pos, orders[basis, 0])
        col_filter = envelope * power_of(taps_pos, orders[basis, 1])
        row_list.append(row_filter / jnp.sqrt(jnp.sum(row_filter * row_filter)))
        col_list.append(col_filter / jnp.sqrt(jnp.sum(col_filter * col_filter)))
    return (jnp.stack(row_list).astype(jnp.bfloat16), jnp.stack(col_list).astype(jnp.bfloat16))


def band_matrix(filters, out_len, in_len):
    offset = jnp.arange(in_len)[None, :] - jnp.arange(out_len)[:, None]
    taps_idx = jnp.arange(2 * HALF + 1)
    picks = (offset[:, :, None] == taps_idx[None, None, :]).astype(jnp.float32)
    band = jnp.einsum("ijt,kt->kij", picks, filters.astype(jnp.float32))
    return band.astype(jnp.bfloat16)


def any_device(template, science, plan, orders, coadd_weight, intersection):
    row_filters, col_filters = make_filters(orders)
    rows = template.shape[1]
    width = template.shape[2]
    blocks_count = width // 128
    steps_count = science.shape[1]
    row_band = band_matrix(row_filters, rows, rows + 2 * HALF)
    col_band = jnp.transpose(band_matrix(col_filters, 128, 128 + 2 * HALF), (0, 2, 1))
    column_pos = 2.0 * (jnp.arange(width).astype(jnp.float32) + 0.5) / width - 1.0
    pieces = []
    fitted = []
    for step in range(steps_count):
        received = broadcast(template[0], "expo", plan[step])
        padded = extended(received, (("tile", 0),), HALF)
        rowconv = jnp.einsum(
            "kij,jw->kiw", row_band, padded, preferred_element_type=jnp.float32
        ).astype(jnp.bfloat16)
        blocks = rowconv.reshape(NB, rows, blocks_count, 128)
        empty_rim = jnp.zeros((NB, rows, 1, HALF), jnp.bfloat16)
        previous = jnp.concatenate([empty_rim, blocks[:, :, :-1, 128 - HALF :]], axis=2)
        following = jnp.concatenate([blocks[:, :, 1:, :HALF], empty_rim], axis=2)
        window = jnp.concatenate([previous, blocks, following], axis=3)
        conv = jnp.einsum("krbj,kjc->krbc", window, col_band, preferred_element_type=jnp.float32)
        conv = conv.reshape(NB, rows, width)
        fields = jnp.concatenate(
            [conv, conv * column_pos, jnp.ones((1, rows, width), jnp.float32)], axis=0
        )
        fields = fields.reshape(NU, rows * width)
        exposure_image = science[0, step].astype(jnp.float32).reshape(rows * width)
        normal_local = jnp.dot(fields, fields.T, precision=lax.Precision.HIGHEST)
        project_local = jnp.dot(fields, exposure_image, precision=lax.Precision.HIGHEST)
        normal_matrix, projections = lax.psum((normal_local, project_local), "tile")
        normal_matrix = normal_matrix + RIDGE * (jnp.trace(normal_matrix) / NU) * jnp.eye(
            NU, dtype=jnp.float32
        )
        factor = jnp.linalg.cholesky(normal_matrix)
        coeffs = jax.scipy.linalg.cho_solve((factor, True), projections)
        model = jnp.dot(coeffs, fields, precision=lax.Precision.HIGHEST)
        difference = exposure_image - model
        weight_now = coadd_weight[0, step] * intersection[0, step].astype(jnp.float32)
        pieces.append((weight_now * difference).reshape(rows, width))
        fitted.append(coeffs)
    weighted = jnp.stack(pieces)
    received_parts = lax.all_to_all(weighted[None], "expo", split_axis=3, concat_axis=0, tiled=True)
    coadd = jnp.sum(received_parts, axis=0)
    return (coadd, jnp.stack(fitted)[None])


def per_device(template, science, plan, orders, coadd_weight, intersection):
    expos = lax.axis_size("expo")
    rows, width = template.shape[1:]
    whole_lanes = width % (expos * LANES) == 0 and rows % 16 == 0
    few = (NU + 1) * expos <= LANES and NU + expos <= LANES
    body = tiled_device if whole_lanes and few else any_device
    return body(template, science, plan, orders, coadd_weight, intersection)


def solution(mesh):
    return jax.shard_map(
        per_device,
        mesh=mesh,
        in_specs=(
            P(("groups", "expo"), "tile", None),
            P(("groups", "expo"), None, "tile", None),
            P("groups"),
            P(),
            P(("groups", "expo"), None),
            P(("groups", "expo"), None),
        ),
        out_specs=(P("groups", "tile", "expo"), P(("groups", "expo"), None, None)),
        check_vma=False,
    )
```

```python
import functools

import jax
import jax.numpy as jnp
import numpy as np
from jax import lax
from jax.experimental import pallas as pl
from jax.experimental.pallas import tpu as pltpu
from jax.sharding import PartitionSpec as P

HALF = 15
NB = 6
NU = 13
LANES = 128
PAIRS = [(j, k) for j in range(NB) for k in range(j, NB)]

SIGMAS = (0.8, 1.4, 2.2, 3.0, 4.0, 5.5)
RIDGE = 0.05


def power_of(pos, order):
    return jnp.where(order == 0, 1.0, jnp.where(order == 1, pos, pos * pos))


def tap_values(pos, sigma, order):
    value = jnp.exp(-pos * pos / (2.0 * sigma * sigma)) * power_of(pos, order)
    return jnp.where(jnp.abs(pos) <= HALF, value, 0.0)


def tap_norm(sigma, order):
    pos = lax.broadcasted_iota(jnp.int32, (8, LANES), 1).astype(jnp.float32) - HALF
    value = tap_values(pos, sigma, order)
    return jnp.sqrt(jnp.sum(value * value, axis=1, keepdims=True))[:1]


def target(me, shift, size):
    return me ^ shift if size & (size - 1) == 0 else (me + shift) % size


def source(me, shift, size):
    return me ^ shift if size & (size - 1) == 0 else (me - shift + size) % size


def send_kernel(template_ref, out_ref, patch_ref, sems):
    parts, rows, ext = out_ref.shape
    chunk = ext - LANES
    half = parts * chunk // 2
    copies = [
        pltpu.make_async_copy(
            template_ref.at[:, pl.ds(i * half, half)], patch_ref.at[:, pl.ds(i * half, half)], sems.at[i]
        )
        for i in range(2)
    ]
    for copy in copies:
        copy.start()
    for copy in copies:
        copy.wait()
    lane = lax.broadcasted_iota(jnp.int32, (rows, LANES), 1)
    for part in range(parts):
        start = part * chunk
        out_ref[part, :, :chunk] = patch_ref[:, start : start + chunk]
        before = patch_ref[:, start - LANES : start].astype(jnp.float32) if part else 0.0
        after = patch_ref[:, start + chunk : start + chunk + LANES].astype(jnp.float32) if part < parts - 1 else 0.0
        rim = jnp.where(lane < LANES // 2, after, before)
        out_ref[part, :, chunk:] = rim.astype(out_ref.dtype)


def cut_kernel(science_ref, *refs):
    out_refs, sems = refs[:-1], refs[-1]
    size = len(out_refs)
    chunk = out_refs[0].shape[1]
    me = lax.axis_index("expo")
    copies = []
    for shift in range(size):
        start = pl.multiple_of(target(me, shift, size) * chunk, chunk)
        copies.append(
            pltpu.make_async_copy(science_ref.at[:, pl.ds(start, chunk)], out_refs[shift], sems.at[shift])
        )
    for copy in copies:
        copy.start()
    for copy in copies:
        copy.wait()


def pick_kernel(owner_ref, recv_ref, image_ref, out_ref, image_out_ref):
    image_out_ref[...] = image_ref[...]
    rows, ext = out_ref.shape
    chunk = ext - LANES
    blocks = []
    for b in range(ext // LANES):
        columns = slice(b * LANES, (b + 1) * LANES)
        block = recv_ref[0, :, columns].astype(jnp.float32)
        for e in range(1, recv_ref.shape[0]):
            block = jnp.where(owner_ref[...] == e, recv_ref[e, :, columns].astype(jnp.float32), block)
        blocks.append(block.astype(out_ref.dtype))
    whole = jnp.concatenate(blocks[-1:] + blocks, axis=1)
    out_ref[...] = whole[:, LANES - HALF : LANES - HALF + ext]


def column_positions(first_col, block, width):
    col = lax.broadcasted_iota(jnp.int32, (8, LANES), 1) + (first_col + block * LANES)
    return 2.0 * (col.astype(jnp.float32) + 0.5) / width - 1.0


def band_kernel(orders_ref, plan_ref, weight_ref, hits_ref, row_ref, col_ref, owner_ref, own_weight_ref):
    for step in range(owner_ref.shape[0]):
        owner_ref[step] = jnp.full(owner_ref.shape[1:], plan_ref[step], jnp.int32)
        weight = weight_ref[0, step] * hits_ref[0, step].astype(jnp.float32)
        own_weight_ref[step] = jnp.full(own_weight_ref.shape[1:], weight, jnp.float32)
    rows = row_ref.shape[0] // NB
    near = 1 - 2 * lax.rem(lax.axis_index("tile"), 2)
    source = lax.broadcasted_iota(jnp.int32, (rows, 3 * rows), 1)
    moved = jnp.where(source < rows, 0, jnp.where(source < 2 * rows, near - 1, -near - 2))
    offset = (
        source + moved * rows - lax.broadcasted_iota(jnp.int32, (rows, 3 * rows), 0)
    ).astype(jnp.float32)
    shift = (
        lax.broadcasted_iota(jnp.int32, (2 * LANES, LANES), 0)
        - lax.broadcasted_iota(jnp.int32, (2 * LANES, LANES), 1)
        - HALF
    ).astype(jnp.float32)
    for k in range(NB):
        norm = tap_norm(SIGMAS[k], orders_ref[k, 0])
        row_ref[k * rows : (k + 1) * rows] = (
            tap_values(offset, SIGMAS[k], orders_ref[k, 0]) / norm
        ).astype(jnp.bfloat16)
        norm = tap_norm(SIGMAS[k], orders_ref[k, 1])
        col_ref[k] = (tap_values(shift, SIGMAS[k], orders_ref[k, 1]) / norm).astype(jnp.bfloat16)


def fit_kernel(weight_ref, row_band_ref, col_band_ref, own_ref, near_ref, far_ref, *refs, width):
    *image_refs, conv_ref, sums_ref, row_ref, parts_ref = refs
    tile_at = lax.axis_index("tile")
    expo_at = lax.axis_index("expo")
    rows, ext = own_ref.shape
    expos = len(image_refs)
    chunk = ext - LANES
    blocks = chunk // LANES

    patch = jnp.concatenate([own_ref[...], near_ref[...], far_ref[...]], axis=0)
    row_ref[...] = jnp.dot(
        row_band_ref[...], patch, preferred_element_type=jnp.float32
    ).astype(jnp.bfloat16)
    for k in range(NB):
        window = jnp.concatenate(
            [
                row_ref[k * rows : (k + 1) * rows, b * LANES : (b + 2) * LANES]
                for b in range(blocks)
            ],
            axis=0,
        )
        out = jnp.dot(window, col_band_ref[k], preferred_element_type=jnp.float32)
        conv_ref[k] = out.reshape(blocks, rows, LANES)

    first_col = expo_at * chunk
    xs = [column_positions(first_col, b, width) for b in range(blocks)]

    def fold(x):
        total = x[:8]
        for i in range(8, rows, 8):
            total = total + x[i : i + 8]
        return total

    def moments(at, left, right, count):
        total = [None] * count
        for b in range(blocks):
            term = fold(left(b) * right(b)) if right is not None else fold(left(b))
            for i in range(count):
                total[i] = term if total[i] is None else total[i] + term
                if i < count - 1:
                    term = term * xs[b]
        for i in range(count):
            parts_ref[at + i] = total[i]

    def conv(k):
        return lambda b: conv_ref[k, b]

    def sci(shift):
        return lambda b: image_refs[shift][:, b * LANES : (b + 1) * LANES].astype(jnp.float32)

    blank = jnp.zeros((8, LANES), jnp.float32)
    at = 0
    for j, k in PAIRS:
        moments(at, conv(j), conv(k), 3)
        at += 3
    for k in range(NB):
        moments(at, conv(k), None, 2)
        at += 2
    while at % 8:
        parts_ref[at] = blank
        at += 1
    begin = at
    for shift in range(expos):
        row = at + NU * source(expo_at, shift, expos)
        for k in range(NB):
            moments(row + 2 * k, conv(k), sci(shift), 2)
        moments(row + NU - 1, sci(shift), None, 1)
    at += NU * expos
    weight = jnp.where(tile_at == 0, weight_ref[...], 0.0)
    spot = (
        (lax.broadcasted_iota(jnp.int32, (8, LANES), 0) == 0)
        & (lax.broadcasted_iota(jnp.int32, (8, LANES), 1) == 0)
    )
    for e in range(expos):
        parts_ref[at + e] = jnp.where(spot & (expo_at == e), weight, 0.0)
    at += expos
    while at % 8:
        parts_ref[at] = blank
        at += 1
    ones = jnp.ones((8, LANES), jnp.float32)
    rows_of = []
    for first, last in ((0, begin), (begin, at)):
        lanes = jnp.sum(parts_ref[first:last], axis=1)
        spare = LANES - (last - first)
        if spare:
            lanes = jnp.concatenate([lanes, jnp.zeros((spare, LANES), jnp.float32)], axis=0)
        rows_of.append(
            lax.dot_general(
                ones,
                lanes,
                (((1,), (1,)), ((), ())),
                precision=lax.Precision.HIGHEST,
                preferred_element_type=jnp.float32,
            )
        )
    both = jnp.where(lax.broadcasted_iota(jnp.int32, (8, LANES), 0) < 4, rows_of[0], rows_of[1])
    for i in range(sums_ref.shape[0]):
        sums_ref[i] = both


def table(expos):
    columns = np.zeros((NU + expos + 1, 16), np.int32)
    for at, (j, k) in enumerate(PAIRS):
        for a, b in ((j, k), (k, j)):
            columns[b, a] = 3 * at
            columns[NB + b, a] = columns[b, NB + a] = 3 * at + 1
            columns[NB + b, NB + a] = 3 * at + 2
    for k in range(NB):
        for x in range(2):
            columns[NU - 1, x * NB + k] = columns[x * NB + k, NU - 1] = 3 * len(PAIRS) + 2 * k + x
    for e in range(expos):
        columns[NU + e, :NU] = [NU * e + 2 * k + x for x in range(2) for k in range(NB)] + [NU * e + NU - 1]
        columns[NU + expos, e] = NU * expos + e
    return np.ascontiguousarray(np.broadcast_to(columns[:, :, None], columns.shape + (LANES,)))


def solve_kernel(table_ref, sums_ref, conv_ref, *refs, width, pixels):
    *image_refs, coadd_ref, coeffs_ref, tile_ref, sems = refs
    expo_at = lax.axis_index("expo")
    expos = len(image_refs)
    rows, chunk = coadd_ref.shape
    blocks = chunk // LANES
    sub = lax.broadcasted_iota(jnp.int32, (16, LANES), 0)
    lane = lax.broadcasted_iota(jnp.int32, (16, LANES), 1)
    sums = sums_ref[0]
    for i in range(1, sums_ref.shape[0]):
        sums = sums + sums_ref[i]
    first = jnp.broadcast_to(sums[0:1], (16, LANES))
    second = jnp.broadcast_to(sums[4:5], (16, LANES))

    columns = [
        jnp.take_along_axis(first if j < NU else second, table_ref[j], axis=1) for j in range(NU + expos)
    ]
    spread = jnp.take_along_axis(second, table_ref[NU + expos], axis=1)
    weight = [jnp.broadcast_to(spread[e : e + 1], (16, LANES)) for e in range(expos)]
    columns[NU - 1] = jnp.where(sub == NU - 1, float(pixels), columns[NU - 1])

    trace = columns[0][0:1]
    for j in range(1, NU):
        trace = trace + columns[j][j : j + 1]
    scale = 1.0 / trace
    for j in range(NU + expos):
        columns[j] = columns[j] * scale
        if j < NU:
            columns[j] = columns[j] + jnp.where(sub == j, RIDGE / NU, 0.0)
    for i in range(NU):
        inverse = 1.0 / columns[i][i : i + 1]
        for j in range(i + 1, NU + expos):
            factor = columns[j][i : i + 1] * inverse
            columns[j] = jnp.where(sub == i, factor, columns[j] - columns[i] * factor)

    solved = columns[NU:]
    own = solved[0]
    mixed = weight[0] * solved[0]
    for e in range(1, expos):
        own = jnp.where(expo_at == e, solved[e], own)
        mixed = mixed + weight[e] * solved[e]
    diagonal = (sub == lane) & (sub < NU)
    coeffs_ref[...] = jnp.sum(jnp.where(diagonal, own, 0.0), axis=0, keepdims=True)[:, :NU]
    scale = [jnp.broadcast_to(mixed[u : u + 1], (8, LANES)) for u in range(NU)]
    gains = []
    for shift in range(expos):
        gain = weight[0][:8]
        for e in range(1, expos):
            gain = jnp.where(source(expo_at, shift, expos) == e, weight[e][:8], gain)
        gains.append(gain)
    first_col = expo_at * chunk
    copies = []
    for r in range(0, rows, 8):
        for b in range(blocks):
            at = slice(b * LANES, (b + 1) * LANES)
            x = column_positions(first_col, b, width)
            total = -scale[NU - 1]
            for gain, image_ref in zip(gains, image_refs):
                total = total + gain * image_ref[:, at].astype(jnp.float32)[r : r + 8]
            model = (scale[0] + scale[NB] * x) * conv_ref[0, b, r : r + 8]
            for k in range(1, NB):
                model = model + (scale[k] + scale[NB + k] * x) * conv_ref[k, b, r : r + 8]
            tile_ref[r : r + 8, b * LANES : (b + 1) * LANES] = total - model
        copies.append(
            pltpu.make_async_copy(tile_ref.at[pl.ds(r, 8)], coadd_ref.at[pl.ds(r, 8)], sems.at[r // 8])
        )
        copies[-1].start()
    for copy in copies:
        copy.wait()


def swaps(first, size):
    return [pair for i in range(first, size - 1, 2) for pair in ((i, i + 1), (i + 1, i))]


def tiled_device(template, science, plan, orders, coadd_weight, intersection):
    expos = lax.axis_size("expo")
    tiles = lax.axis_size("tile")
    _, rows, width = template.shape
    steps = science.shape[1]
    chunk = width // expos
    ext = chunk + LANES
    blocks = chunk // LANES
    smem = pl.BlockSpec(memory_space=pltpu.SMEM)
    vmem = pl.BlockSpec(memory_space=pltpu.VMEM)
    small = pltpu.CompilerParams(vmem_limit_bytes=16 * 1024 * 1024)
    hbm = pl.BlockSpec(memory_space=pltpu.HBM)
    row_band, col_band, owner, own_weight = pl.pallas_call(
        band_kernel,
        out_shape=(
            jax.ShapeDtypeStruct((NB * rows, 3 * rows), jnp.bfloat16),
            jax.ShapeDtypeStruct((NB, 2 * LANES, LANES), jnp.bfloat16),
            jax.ShapeDtypeStruct((steps, rows, LANES), jnp.int32),
            jax.ShapeDtypeStruct((steps, 8, LANES), jnp.float32),
        ),
        in_specs=[smem] * 4,
        out_specs=(vmem,) * 4,
        compiler_params=small,
        cost_estimate=pl.CostEstimate(flops=4_000_000, bytes_accessed=500_000, transcendentals=200_000),
    )(orders, plan, coadd_weight, intersection)
    coadds = []
    fitted = []
    for step in range(steps):
        send = pl.pallas_call(
            send_kernel,
            out_shape=pltpu.VMEM((expos, rows, ext), template.dtype),
            in_specs=[hbm],
            out_specs=vmem,
            scratch_shapes=[
                pltpu.VMEM((rows, width), template.dtype),
                pltpu.SemaphoreType.DMA((2,)),
            ],
            compiler_params=small,
        )(pltpu.with_memory_space_constraint(template[0], pltpu.HBM))
        recv = lax.all_to_all(send, "expo", split_axis=0, concat_axis=0, tiled=True)
        images = pl.pallas_call(
            cut_kernel,
            out_shape=(pltpu.VMEM((rows, chunk), science.dtype),) * expos,
            in_specs=[hbm],
            out_specs=(vmem,) * expos,
            scratch_shapes=[pltpu.SemaphoreType.DMA((expos,))],
            compiler_params=small,
        )(pltpu.with_memory_space_constraint(science[0, step], pltpu.HBM))
        images = list(images)

        def exchange(shift):
            pairs = [(e, int(target(e, shift, expos))) for e in range(expos)]
            images[shift] = lax.ppermute(images[shift], "expo", pairs)

        for shift in range(expos - 1, 1, -1):
            exchange(shift)
        own, images[1 % expos] = pl.pallas_call(
            pick_kernel,
            out_shape=(
                jax.ShapeDtypeStruct((rows, ext), template.dtype),
                jax.ShapeDtypeStruct((rows, chunk), science.dtype),
            ),
            in_specs=[vmem, vmem, vmem],
            out_specs=(vmem, vmem),
            compiler_params=small,
        )(owner[step], recv, images[1 % expos])
        far = lax.ppermute(own, "tile", swaps(1, tiles))
        near = lax.ppermute(own, "tile", swaps(0, tiles))
        if expos > 1:
            exchange(1)
        conv, sums = pl.pallas_call(
            functools.partial(fit_kernel, width=width),
            out_shape=(
                jax.ShapeDtypeStruct((NB, blocks, rows, LANES), jnp.float32),
                jax.ShapeDtypeStruct((tiles * expos, 8, LANES), jnp.float32),
            ),
            in_specs=[vmem] * (6 + expos),
            out_specs=(vmem, vmem),
            scratch_shapes=[
                pltpu.VMEM((NB * rows, ext), jnp.bfloat16),
                pltpu.VMEM((80 + 14 * expos + 8, 8, LANES), jnp.float32),
            ],
            compiler_params=small,
        )(
            own_weight[step],
            row_band,
            col_band,
            own,
            near,
            far,
            *images,
        )
        sums = lax.all_to_all(sums, ("tile", "expo"), split_axis=0, concat_axis=0, tiled=True)
        coadd, coeffs = pl.pallas_call(
            functools.partial(solve_kernel, width=width, pixels=tiles * rows * width),
            out_shape=(
                jax.ShapeDtypeStruct((rows, chunk), jnp.float32),
                jax.ShapeDtypeStruct((1, NU), jnp.float32),
            ),
            in_specs=[vmem] * (3 + expos),
            out_specs=(pl.BlockSpec(memory_space=pl.ANY), vmem),
            scratch_shapes=[
                pltpu.VMEM((rows, chunk), jnp.float32),
                pltpu.SemaphoreType.DMA((rows // 8,)),
            ],
            compiler_params=small,
        )(jnp.asarray(table(expos)), sums, conv, *images)
        coadds.append(coadd[None])
        fitted.append(coeffs)
    return (jnp.concatenate(coadds), jnp.stack(fitted, axis=1))


def broadcast(block, axis, holder):
    block = jnp.where(lax.axis_index(axis) == holder, block, jnp.zeros_like(block))
    return lax.psum(block, axis)


def extended(x, sides, width):
    for axis, dim in sides:
        size, length = (lax.axis_size(axis), x.shape[dim])
        up = [(i, (i + 1) % size) for i in range(size - 1)]
        down = [(j, i) for i, j in up]
        last = lax.slice_in_dim(x, length - width, length, axis=dim)
        first = lax.slice_in_dim(x, 0, width, axis=dim)
        before = lax.ppermute(last, axis, up)
        after = lax.ppermute(first, axis, down)
        x = jnp.concatenate([before, x, after], axis=dim)
    return x


def make_filters(orders):
    taps_pos = jnp.arange(2 * HALF + 1).astype(jnp.float32) - HALF
    row_list = []
    col_list = []
    for basis in range(NB):
        sigma = SIGMAS[basis]
        envelope = jnp.exp(-taps_pos * taps_pos / (2.0 * sigma * sigma))
        row_filter = envelope * power_of(taps_pos, orders[basis, 0])
        col_filter = envelope * power_of(taps_pos, orders[basis, 1])
        row_list.append(row_filter / jnp.sqrt(jnp.sum(row_filter * row_filter)))
        col_list.append(col_filter / jnp.sqrt(jnp.sum(col_filter * col_filter)))
    return (jnp.stack(row_list).astype(jnp.bfloat16), jnp.stack(col_list).astype(jnp.bfloat16))


def band_matrix(filters, out_len, in_len):
    offset = jnp.arange(in_len)[None, :] - jnp.arange(out_len)[:, None]
    taps_idx = jnp.arange(2 * HALF + 1)
    picks = (offset[:, :, None] == taps_idx[None, None, :]).astype(jnp.float32)
    band = jnp.einsum("ijt,kt->kij", picks, filters.astype(jnp.float32))
    return band.astype(jnp.bfloat16)


def any_device(template, science, plan, orders, coadd_weight, intersection):
    row_filters, col_filters = make_filters(orders)
    rows = template.shape[1]
    width = template.shape[2]
    blocks_count = width // 128
    steps_count = science.shape[1]
    row_band = band_matrix(row_filters, rows, rows + 2 * HALF)
    col_band = jnp.transpose(band_matrix(col_filters, 128, 128 + 2 * HALF), (0, 2, 1))
    column_pos = 2.0 * (jnp.arange(width).astype(jnp.float32) + 0.5) / width - 1.0
    pieces = []
    fitted = []
    for step in range(steps_count):
        received = broadcast(template[0], "expo", plan[step])
        padded = extended(received, (("tile", 0),), HALF)
        rowconv = jnp.einsum(
            "kij,jw->kiw", row_band, padded, preferred_element_type=jnp.float32
        ).astype(jnp.bfloat16)
        blocks = rowconv.reshape(NB, rows, blocks_count, 128)
        empty_rim = jnp.zeros((NB, rows, 1, HALF), jnp.bfloat16)
        previous = jnp.concatenate([empty_rim, blocks[:, :, :-1, 128 - HALF :]], axis=2)
        following = jnp.concatenate([blocks[:, :, 1:, :HALF], empty_rim], axis=2)
        window = jnp.concatenate([previous, blocks, following], axis=3)
        conv = jnp.einsum("krbj,kjc->krbc", window, col_band, preferred_element_type=jnp.float32)
        conv = conv.reshape(NB, rows, width)
        fields = jnp.concatenate(
            [conv, conv * column_pos, jnp.ones((1, rows, width), jnp.float32)], axis=0
        )
        fields = fields.reshape(NU, rows * width)
        exposure_image = science[0, step].astype(jnp.float32).reshape(rows * width)
        normal_local = jnp.dot(fields, fields.T, precision=lax.Precision.HIGHEST)
        project_local = jnp.dot(fields, exposure_image, precision=lax.Precision.HIGHEST)
        normal_matrix, projections = lax.psum((normal_local, project_local), "tile")
        normal_matrix = normal_matrix + RIDGE * (jnp.trace(normal_matrix) / NU) * jnp.eye(
            NU, dtype=jnp.float32
        )
        factor = jnp.linalg.cholesky(normal_matrix)
        coeffs = jax.scipy.linalg.cho_solve((factor, True), projections)
        model = jnp.dot(coeffs, fields, precision=lax.Precision.HIGHEST)
        difference = exposure_image - model
        weight_now = coadd_weight[0, step] * intersection[0, step].astype(jnp.float32)
        pieces.append((weight_now * difference).reshape(rows, width))
        fitted.append(coeffs)
    weighted = jnp.stack(pieces)
    received_parts = lax.all_to_all(weighted[None], "expo", split_axis=3, concat_axis=0, tiled=True)
    coadd = jnp.sum(received_parts, axis=0)
    return (coadd, jnp.stack(fitted)[None])


def per_device(template, science, plan, orders, coadd_weight, intersection):
    expos = lax.axis_size("expo")
    rows, width = template.shape[1:]
    whole_lanes = width % (expos * LANES) == 0 and rows % 16 == 0
    few = (NU + 1) * expos <= LANES and NU + expos <= LANES
    body = tiled_device if whole_lanes and few else any_device
    return body(template, science, plan, orders, coadd_weight, intersection)


def solution(mesh):
    return jax.shard_map(
        per_device,
        mesh=mesh,
        in_specs=(
            P(("groups", "expo"), "tile", None),
            P(("groups", "expo"), None, "tile", None),
            P("groups"),
            P(),
            P(("groups", "expo"), None),
            P(("groups", "expo"), None),
        ),
        out_specs=(P("groups", "tile", "expo"), P(("groups", "expo"), None, None)),
        check_vma=False,
    )
```

```python
import functools

import jax
import jax.numpy as jnp
import numpy as np
from jax import lax
from jax.experimental import pallas as pl
from jax.experimental.pallas import tpu as pltpu
from jax.sharding import PartitionSpec as P

HALF = 15
NB = 6
NU = 13
LANES = 128
PAIRS = [(j, k) for j in range(NB) for k in range(j, NB)]

SIGMAS = (0.8, 1.4, 2.2, 3.0, 4.0, 5.5)
RIDGE = 0.05


def power_of(pos, order):
    return jnp.where(order == 0, 1.0, jnp.where(order == 1, pos, pos * pos))


def tap_values(pos, sigma, order):
    value = jnp.exp(-pos * pos / (2.0 * sigma * sigma)) * power_of(pos, order)
    return jnp.where(jnp.abs(pos) <= HALF, value, 0.0)


def tap_norm(sigma, order):
    pos = lax.broadcasted_iota(jnp.int32, (8, LANES), 1).astype(jnp.float32) - HALF
    value = tap_values(pos, sigma, order)
    return jnp.sqrt(jnp.sum(value * value, axis=1, keepdims=True))[:1]


def target(me, shift, size):
    return me ^ shift if size & (size - 1) == 0 else (me + shift) % size


def source(me, shift, size):
    return me ^ shift if size & (size - 1) == 0 else (me - shift + size) % size


def send_kernel(template_ref, out_ref, patch_ref, sems):
    parts, rows, ext = out_ref.shape
    chunk = ext - LANES
    half = parts * chunk // 2
    copies = [
        pltpu.make_async_copy(
            template_ref.at[:, pl.ds(i * half, half)], patch_ref.at[:, pl.ds(i * half, half)], sems.at[i]
        )
        for i in range(2)
    ]
    for copy in copies:
        copy.start()
    for copy in copies:
        copy.wait()
    lane = lax.broadcasted_iota(jnp.int32, (rows, LANES), 1)
    for part in range(parts):
        start = part * chunk
        out_ref[part, :, :chunk] = patch_ref[:, start : start + chunk]
        before = patch_ref[:, start - LANES : start].astype(jnp.float32) if part else 0.0
        after = patch_ref[:, start + chunk : start + chunk + LANES].astype(jnp.float32) if part < parts - 1 else 0.0
        rim = jnp.where(lane < LANES // 2, after, before)
        out_ref[part, :, chunk:] = rim.astype(out_ref.dtype)


def cut_kernel(science_ref, plan_ref, _, *refs, step):
    *out_refs, owner_ref, plan_now, sems = refs
    size = len(out_refs)
    chunk = out_refs[0].shape[1]
    me = lax.axis_index("expo")
    copies = [pltpu.make_async_copy(plan_ref, plan_now, sems.at[size])]
    for shift in range(size):
        start = pl.multiple_of(target(me, shift, size) * chunk, chunk)
        copies.append(
            pltpu.make_async_copy(science_ref.at[:, pl.ds(start, chunk)], out_refs[shift], sems.at[shift])
        )
    for copy in copies:
        copy.start()
    for copy in copies:
        copy.wait()
    owner_ref[...] = jnp.full(owner_ref.shape, plan_now[step], jnp.int32)


def pick_kernel(owner_ref, recv_ref, image_ref, *refs):
    *_, out_ref, image_out_ref = refs
    image_out_ref[...] = image_ref[...]
    rows, ext = out_ref.shape
    chunk = ext - LANES
    blocks = []
    for b in range(ext // LANES):
        columns = slice(b * LANES, (b + 1) * LANES)
        block = recv_ref[0, :, columns].astype(jnp.float32)
        for e in range(1, recv_ref.shape[0]):
            block = jnp.where(owner_ref[...] == e, recv_ref[e, :, columns].astype(jnp.float32), block)
        blocks.append(block.astype(out_ref.dtype))
    whole = jnp.concatenate(blocks[-1:] + blocks, axis=1)
    out_ref[...] = whole[:, LANES - HALF : LANES - HALF + ext]


def column_positions(first_col, block, width):
    col = lax.broadcasted_iota(jnp.int32, (8, LANES), 1) + (first_col + block * LANES)
    return 2.0 * (col.astype(jnp.float32) + 0.5) / width - 1.0


def band_kernel(orders_ref, row_ref, col_ref):
    rows = row_ref.shape[0] // NB
    near = 1 - 2 * lax.rem(lax.axis_index("tile"), 2)
    source = lax.broadcasted_iota(jnp.int32, (rows, 3 * rows), 1)
    moved = jnp.where(source < rows, 0, jnp.where(source < 2 * rows, near - 1, -near - 2))
    offset = (
        source + moved * rows - lax.broadcasted_iota(jnp.int32, (rows, 3 * rows), 0)
    ).astype(jnp.float32)
    shift = (
        lax.broadcasted_iota(jnp.int32, (2 * LANES, LANES), 0)
        - lax.broadcasted_iota(jnp.int32, (2 * LANES, LANES), 1)
        - HALF
    ).astype(jnp.float32)
    for k in range(NB):
        norm = tap_norm(SIGMAS[k], orders_ref[k, 0])
        row_ref[k * rows : (k + 1) * rows] = (
            tap_values(offset, SIGMAS[k], orders_ref[k, 0]) / norm
        ).astype(jnp.bfloat16)
        norm = tap_norm(SIGMAS[k], orders_ref[k, 1])
        col_ref[k] = (tap_values(shift, SIGMAS[k], orders_ref[k, 1]) / norm).astype(jnp.bfloat16)


def fit_kernel(weight_ref, hits_ref, row_band_ref, col_band_ref, own_ref, near_ref, far_ref, *refs, width):
    *image_refs, conv_ref, sums_ref, row_ref, parts_ref = refs
    tile_at = lax.axis_index("tile")
    expo_at = lax.axis_index("expo")
    rows, ext = own_ref.shape
    expos = len(image_refs)
    chunk = ext - LANES
    blocks = chunk // LANES

    patch = jnp.concatenate([own_ref[...], near_ref[...], far_ref[...]], axis=0)
    row_ref[...] = jnp.dot(
        row_band_ref[...], patch, preferred_element_type=jnp.float32
    ).astype(jnp.bfloat16)
    for k in range(NB):
        window = jnp.concatenate(
            [
                row_ref[k * rows : (k + 1) * rows, b * LANES : (b + 2) * LANES]
                for b in range(blocks)
            ],
            axis=0,
        )
        out = jnp.dot(window, col_band_ref[k], preferred_element_type=jnp.float32)
        conv_ref[k] = out.reshape(blocks, rows, LANES)

    first_col = expo_at * chunk
    xs = [column_positions(first_col, b, width) for b in range(blocks)]

    def fold(x):
        total = x[:8]
        for i in range(8, rows, 8):
            total = total + x[i : i + 8]
        return total

    def moments(at, left, right, count):
        total = [None] * count
        for b in range(blocks):
            term = fold(left(b) * right(b)) if right is not None else fold(left(b))
            for i in range(count):
                total[i] = term if total[i] is None else total[i] + term
                if i < count - 1:
                    term = term * xs[b]
        for i in range(count):
            parts_ref[at + i] = total[i]

    def conv(k):
        return lambda b: conv_ref[k, b]

    def sci(shift):
        return lambda b: image_refs[shift][:, b * LANES : (b + 1) * LANES].astype(jnp.float32)

    blank = jnp.zeros((8, LANES), jnp.float32)
    at = 0
    for j, k in PAIRS:
        moments(at, conv(j), conv(k), 3)
        at += 3
    for k in range(NB):
        moments(at, conv(k), None, 2)
        at += 2
    while at % 8:
        parts_ref[at] = blank
        at += 1
    begin = at
    for shift in range(expos):
        row = at + NU * source(expo_at, shift, expos)
        for k in range(NB):
            moments(row + 2 * k, conv(k), sci(shift), 2)
        moments(row + NU - 1, sci(shift), None, 1)
    at += NU * expos
    weight = jnp.broadcast_to(weight_ref[...] * hits_ref[...].astype(jnp.float32), (8, LANES))
    weight = jnp.where(tile_at == 0, weight, 0.0)
    spot = (
        (lax.broadcasted_iota(jnp.int32, (8, LANES), 0) == 0)
        & (lax.broadcasted_iota(jnp.int32, (8, LANES), 1) == 0)
    )
    for e in range(expos):
        parts_ref[at + e] = jnp.where(spot & (expo_at == e), weight, 0.0)
    at += expos
    while at % 8:
        parts_ref[at] = blank
        at += 1
    ones = jnp.ones((8, LANES), jnp.float32)
    rows_of = []
    for first, last in ((0, begin), (begin, at)):
        lanes = jnp.sum(parts_ref[first:last], axis=1)
        spare = LANES - (last - first)
        if spare:
            lanes = jnp.concatenate([lanes, jnp.zeros((spare, LANES), jnp.float32)], axis=0)
        rows_of.append(
            lax.dot_general(
                ones,
                lanes,
                (((1,), (1,)), ((), ())),
                precision=lax.Precision.HIGHEST,
                preferred_element_type=jnp.float32,
            )
        )
    both = jnp.where(lax.broadcasted_iota(jnp.int32, (8, LANES), 0) < 4, rows_of[0], rows_of[1])
    for i in range(sums_ref.shape[0]):
        sums_ref[i] = both


def table(expos):
    columns = np.zeros((NU + expos + 1, 16), np.int32)
    for at, (j, k) in enumerate(PAIRS):
        for a, b in ((j, k), (k, j)):
            columns[b, a] = 3 * at
            columns[NB + b, a] = columns[b, NB + a] = 3 * at + 1
            columns[NB + b, NB + a] = 3 * at + 2
    for k in range(NB):
        for x in range(2):
            columns[NU - 1, x * NB + k] = columns[x * NB + k, NU - 1] = 3 * len(PAIRS) + 2 * k + x
    for e in range(expos):
        columns[NU + e, :NU] = [NU * e + 2 * k + x for x in range(2) for k in range(NB)] + [NU * e + NU - 1]
        columns[NU + expos, e] = NU * expos + e
    return np.ascontiguousarray(np.broadcast_to(columns[:, :, None], columns.shape + (LANES,)))


def solve_kernel(table_ref, sums_ref, conv_ref, *refs, width, pixels):
    *image_refs, coadd_ref, coeffs_ref, tile_ref, sems = refs
    expo_at = lax.axis_index("expo")
    expos = len(image_refs)
    rows, chunk = coadd_ref.shape
    blocks = chunk // LANES
    sub = lax.broadcasted_iota(jnp.int32, (16, LANES), 0)
    lane = lax.broadcasted_iota(jnp.int32, (16, LANES), 1)
    sums = sums_ref[0]
    for i in range(1, sums_ref.shape[0]):
        sums = sums + sums_ref[i]
    first = jnp.broadcast_to(sums[0:1], (16, LANES))
    second = jnp.broadcast_to(sums[4:5], (16, LANES))

    columns = [
        jnp.take_along_axis(first if j < NU else second, table_ref[j], axis=1) for j in range(NU + expos)
    ]
    spread = jnp.take_along_axis(second, table_ref[NU + expos], axis=1)
    weight = [jnp.broadcast_to(spread[e : e + 1], (16, LANES)) for e in range(expos)]
    columns[NU - 1] = jnp.where(sub == NU - 1, float(pixels), columns[NU - 1])

    trace = columns[0][0:1]
    for j in range(1, NU):
        trace = trace + columns[j][j : j + 1]
    scale = 1.0 / trace
    for j in range(NU + expos):
        columns[j] = columns[j] * scale
        if j < NU:
            columns[j] = columns[j] + jnp.where(sub == j, RIDGE / NU, 0.0)
    for i in range(NU):
        inverse = 1.0 / columns[i][i : i + 1]
        for j in range(i + 1, NU + expos):
            factor = columns[j][i : i + 1] * inverse
            columns[j] = jnp.where(sub == i, factor, columns[j] - columns[i] * factor)

    solved = columns[NU:]
    own = solved[0]
    mixed = weight[0] * solved[0]
    for e in range(1, expos):
        own = jnp.where(expo_at == e, solved[e], own)
        mixed = mixed + weight[e] * solved[e]
    diagonal = (sub == lane) & (sub < NU)
    coeffs_ref[...] = jnp.sum(jnp.where(diagonal, own, 0.0), axis=0, keepdims=True)[:, :NU]
    scale = [jnp.broadcast_to(mixed[u : u + 1], (8, LANES)) for u in range(NU)]
    gains = []
    for shift in range(expos):
        gain = weight[0][:8]
        for e in range(1, expos):
            gain = jnp.where(source(expo_at, shift, expos) == e, weight[e][:8], gain)
        gains.append(gain)
    first_col = expo_at * chunk
    copies = []
    for r in range(0, rows, 8):
        for b in range(blocks):
            at = slice(b * LANES, (b + 1) * LANES)
            x = column_positions(first_col, b, width)
            total = -scale[NU - 1]
            for gain, image_ref in zip(gains, image_refs):
                total = total + gain * image_ref[:, at].astype(jnp.float32)[r : r + 8]
            model = (scale[0] + scale[NB] * x) * conv_ref[0, b, r : r + 8]
            for k in range(1, NB):
                model = model + (scale[k] + scale[NB + k] * x) * conv_ref[k, b, r : r + 8]
            tile_ref[r : r + 8, b * LANES : (b + 1) * LANES] = total - model
        copies.append(
            pltpu.make_async_copy(tile_ref.at[pl.ds(r, 8)], coadd_ref.at[pl.ds(r, 8)], sems.at[r // 8])
        )
        copies[-1].start()
    for copy in copies:
        copy.wait()


def swaps(first, size):
    return [pair for i in range(first, size - 1, 2) for pair in ((i, i + 1), (i + 1, i))]


def tiled_device(template, science, plan, orders, coadd_weight, intersection):
    expos = lax.axis_size("expo")
    tiles = lax.axis_size("tile")
    _, rows, width = template.shape
    steps = science.shape[1]
    chunk = width // expos
    ext = chunk + LANES
    blocks = chunk // LANES
    smem = pl.BlockSpec(memory_space=pltpu.SMEM)
    vmem = pl.BlockSpec(memory_space=pltpu.VMEM)
    small = pltpu.CompilerParams(vmem_limit_bytes=16 * 1024 * 1024)
    hbm = pl.BlockSpec(memory_space=pltpu.HBM)
    row_band, col_band = pl.pallas_call(
        band_kernel,
        out_shape=(
            jax.ShapeDtypeStruct((NB * rows, 3 * rows), jnp.bfloat16),
            jax.ShapeDtypeStruct((NB, 2 * LANES, LANES), jnp.bfloat16),
        ),
        in_specs=[smem],
        out_specs=(vmem, vmem),
        compiler_params=small,
        cost_estimate=pl.CostEstimate(flops=4_000_000, bytes_accessed=500_000, transcendentals=200_000),
    )(orders)
    coadds = []
    fitted = []
    for step in range(steps):
        send = pl.pallas_call(
            send_kernel,
            out_shape=pltpu.VMEM((expos, rows, ext), template.dtype),
            in_specs=[hbm],
            out_specs=vmem,
            scratch_shapes=[
                pltpu.VMEM((rows, width), template.dtype),
                pltpu.SemaphoreType.DMA((2,)),
            ],
            compiler_params=small,
        )(pltpu.with_memory_space_constraint(template[0], pltpu.HBM))
        recv = lax.all_to_all(send, "expo", split_axis=0, concat_axis=0, tiled=True)
        *images, owner = pl.pallas_call(
            functools.partial(cut_kernel, step=step),
            out_shape=(pltpu.VMEM((rows, chunk), science.dtype),) * expos
            + (jax.ShapeDtypeStruct((rows, LANES), jnp.int32),),
            in_specs=[hbm, hbm, pl.BlockSpec(memory_space=pl.ANY)],
            out_specs=(vmem,) * (expos + 1),
            scratch_shapes=[pltpu.SMEM(plan.shape, jnp.int32), pltpu.SemaphoreType.DMA((expos + 1,))],
            compiler_params=small,
        )(
            pltpu.with_memory_space_constraint(science[0, step], pltpu.HBM),
            pltpu.with_memory_space_constraint(plan, pltpu.HBM),
            send,
        )

        def exchange(shift):
            pairs = [(e, int(target(e, shift, expos))) for e in range(expos)]
            images[shift] = lax.ppermute(images[shift], "expo", pairs)

        for shift in range(expos - 1, 1, -1):
            exchange(shift)
        own, images[1 % expos] = pl.pallas_call(
            pick_kernel,
            out_shape=(
                jax.ShapeDtypeStruct((rows, ext), template.dtype),
                jax.ShapeDtypeStruct((rows, chunk), science.dtype),
            ),
            in_specs=[vmem, vmem, vmem] + [pl.BlockSpec(memory_space=pl.ANY)] * len(images[2:]),
            out_specs=(vmem, vmem),
            compiler_params=small,
        )(owner, recv, images[1 % expos], *images[2:])
        far = lax.ppermute(own, "tile", swaps(1, tiles))
        near = lax.ppermute(own, "tile", swaps(0, tiles))
        if expos > 1:
            exchange(1)
        conv, sums = pl.pallas_call(
            functools.partial(fit_kernel, width=width),
            out_shape=(
                jax.ShapeDtypeStruct((NB, blocks, rows, LANES), jnp.float32),
                jax.ShapeDtypeStruct((tiles * expos, 8, LANES), jnp.float32),
            ),
            in_specs=[vmem] * (7 + expos),
            out_specs=(vmem, vmem),
            scratch_shapes=[
                pltpu.VMEM((NB * rows, ext), jnp.bfloat16),
                pltpu.VMEM((80 + 14 * expos + 8, 8, LANES), jnp.float32),
            ],
            compiler_params=small,
        )(
            coadd_weight[:, step : step + 1],
            intersection[:, step : step + 1],
            row_band,
            col_band,
            own,
            near,
            far,
            *images,
        )
        sums = lax.all_to_all(sums, ("tile", "expo"), split_axis=0, concat_axis=0, tiled=True)
        coadd, coeffs = pl.pallas_call(
            functools.partial(solve_kernel, width=width, pixels=tiles * rows * width),
            out_shape=(
                jax.ShapeDtypeStruct((rows, chunk), jnp.float32),
                jax.ShapeDtypeStruct((1, NU), jnp.float32),
            ),
            in_specs=[vmem] * (3 + expos),
            out_specs=(pl.BlockSpec(memory_space=pl.ANY), vmem),
            scratch_shapes=[
                pltpu.VMEM((rows, chunk), jnp.float32),
                pltpu.SemaphoreType.DMA((rows // 8,)),
            ],
            compiler_params=small,
        )(jnp.asarray(table(expos)), sums, conv, *images)
        coadds.append(coadd[None])
        fitted.append(coeffs)
    return (jnp.concatenate(coadds), jnp.stack(fitted, axis=1))


def broadcast(block, axis, holder):
    block = jnp.where(lax.axis_index(axis) == holder, block, jnp.zeros_like(block))
    return lax.psum(block, axis)


def extended(x, sides, width):
    for axis, dim in sides:
        size, length = (lax.axis_size(axis), x.shape[dim])
        up = [(i, (i + 1) % size) for i in range(size - 1)]
        down = [(j, i) for i, j in up]
        last = lax.slice_in_dim(x, length - width, length, axis=dim)
        first = lax.slice_in_dim(x, 0, width, axis=dim)
        before = lax.ppermute(last, axis, up)
        after = lax.ppermute(first, axis, down)
        x = jnp.concatenate([before, x, after], axis=dim)
    return x


def make_filters(orders):
    taps_pos = jnp.arange(2 * HALF + 1).astype(jnp.float32) - HALF
    row_list = []
    col_list = []
    for basis in range(NB):
        sigma = SIGMAS[basis]
        envelope = jnp.exp(-taps_pos * taps_pos / (2.0 * sigma * sigma))
        row_filter = envelope * power_of(taps_pos, orders[basis, 0])
        col_filter = envelope * power_of(taps_pos, orders[basis, 1])
        row_list.append(row_filter / jnp.sqrt(jnp.sum(row_filter * row_filter)))
        col_list.append(col_filter / jnp.sqrt(jnp.sum(col_filter * col_filter)))
    return (jnp.stack(row_list).astype(jnp.bfloat16), jnp.stack(col_list).astype(jnp.bfloat16))


def band_matrix(filters, out_len, in_len):
    offset = jnp.arange(in_len)[None, :] - jnp.arange(out_len)[:, None]
    taps_idx = jnp.arange(2 * HALF + 1)
    picks = (offset[:, :, None] == taps_idx[None, None, :]).astype(jnp.float32)
    band = jnp.einsum("ijt,kt->kij", picks, filters.astype(jnp.float32))
    return band.astype(jnp.bfloat16)


def any_device(template, science, plan, orders, coadd_weight, intersection):
    row_filters, col_filters = make_filters(orders)
    rows = template.shape[1]
    width = template.shape[2]
    blocks_count = width // 128
    steps_count = science.shape[1]
    row_band = band_matrix(row_filters, rows, rows + 2 * HALF)
    col_band = jnp.transpose(band_matrix(col_filters, 128, 128 + 2 * HALF), (0, 2, 1))
    column_pos = 2.0 * (jnp.arange(width).astype(jnp.float32) + 0.5) / width - 1.0
    pieces = []
    fitted = []
    for step in range(steps_count):
        received = broadcast(template[0], "expo", plan[step])
        padded = extended(received, (("tile", 0),), HALF)
        rowconv = jnp.einsum(
            "kij,jw->kiw", row_band, padded, preferred_element_type=jnp.float32
        ).astype(jnp.bfloat16)
        blocks = rowconv.reshape(NB, rows, blocks_count, 128)
        empty_rim = jnp.zeros((NB, rows, 1, HALF), jnp.bfloat16)
        previous = jnp.concatenate([empty_rim, blocks[:, :, :-1, 128 - HALF :]], axis=2)
        following = jnp.concatenate([blocks[:, :, 1:, :HALF], empty_rim], axis=2)
        window = jnp.concatenate([previous, blocks, following], axis=3)
        conv = jnp.einsum("krbj,kjc->krbc", window, col_band, preferred_element_type=jnp.float32)
        conv = conv.reshape(NB, rows, width)
        fields = jnp.concatenate(
            [conv, conv * column_pos, jnp.ones((1, rows, width), jnp.float32)], axis=0
        )
        fields = fields.reshape(NU, rows * width)
        exposure_image = science[0, step].astype(jnp.float32).reshape(rows * width)
        normal_local = jnp.dot(fields, fields.T, precision=lax.Precision.HIGHEST)
        project_local = jnp.dot(fields, exposure_image, precision=lax.Precision.HIGHEST)
        normal_matrix, projections = lax.psum((normal_local, project_local), "tile")
        normal_matrix = normal_matrix + RIDGE * (jnp.trace(normal_matrix) / NU) * jnp.eye(
            NU, dtype=jnp.float32
        )
        factor = jnp.linalg.cholesky(normal_matrix)
        coeffs = jax.scipy.linalg.cho_solve((factor, True), projections)
        model = jnp.dot(coeffs, fields, precision=lax.Precision.HIGHEST)
        difference = exposure_image - model
        weight_now = coadd_weight[0, step] * intersection[0, step].astype(jnp.float32)
        pieces.append((weight_now * difference).reshape(rows, width))
        fitted.append(coeffs)
    weighted = jnp.stack(pieces)
    received_parts = lax.all_to_all(weighted[None], "expo", split_axis=3, concat_axis=0, tiled=True)
    coadd = jnp.sum(received_parts, axis=0)
    return (coadd, jnp.stack(fitted)[None])


def per_device(template, science, plan, orders, coadd_weight, intersection):
    expos = lax.axis_size("expo")
    rows, width = template.shape[1:]
    whole_lanes = width % (expos * LANES) == 0 and rows % 16 == 0
    few = (NU + 1) * expos <= LANES and NU + expos <= LANES
    body = tiled_device if whole_lanes and few else any_device
    return body(template, science, plan, orders, coadd_weight, intersection)


def solution(mesh):
    return jax.shard_map(
        per_device,
        mesh=mesh,
        in_specs=(
            P(("groups", "expo"), "tile", None),
            P(("groups", "expo"), None, "tile", None),
            P("groups"),
            P(),
            P(("groups", "expo"), None),
            P(("groups", "expo"), None),
        ),
        out_specs=(P("groups", "tile", "expo"), P(("groups", "expo"), None, None)),
        check_vma=False,
    )
```

```python
import functools

import jax
import jax.numpy as jnp
import numpy as np
from jax import lax
from jax.experimental import pallas as pl
from jax.experimental.pallas import tpu as pltpu
from jax.sharding import PartitionSpec as P

HALF = 15
NB = 6
NU = 13
LANES = 128
PAIRS = [(j, k) for j in range(NB) for k in range(j, NB)]

SIGMAS = (0.8, 1.4, 2.2, 3.0, 4.0, 5.5)
RIDGE = 0.05


def power_of(pos, order):
    return jnp.where(order == 0, 1.0, jnp.where(order == 1, pos, pos * pos))


def tap_values(pos, sigma, order):
    value = jnp.exp(-pos * pos / (2.0 * sigma * sigma)) * power_of(pos, order)
    return jnp.where(jnp.abs(pos) <= HALF, value, 0.0)


def tap_norm(sigma, order):
    pos = lax.broadcasted_iota(jnp.int32, (8, LANES), 1).astype(jnp.float32) - HALF
    value = tap_values(pos, sigma, order)
    return jnp.sqrt(jnp.sum(value * value, axis=1, keepdims=True))[:1]


def target(me, shift, size):
    return me ^ shift if size & (size - 1) == 0 else (me + shift) % size


def source(me, shift, size):
    return me ^ shift if size & (size - 1) == 0 else (me - shift + size) % size


def send_kernel(template_ref, science_ref, plan_ref, *refs, step):
    *out_refs, owner_ref, patch_ref, plan_now, sems = refs
    size = len(out_refs)
    rows, wide = out_refs[0].shape
    chunk = (wide - LANES) // 2
    half = size * chunk // 2
    me = lax.axis_index("expo")
    starts = [pl.multiple_of(target(me, shift, size) * chunk, chunk) for shift in range(size)]
    loads = [
        pltpu.make_async_copy(
            template_ref.at[:, pl.ds(i * half, half)], patch_ref.at[:, pl.ds((i * half + LANES), half)], sems.at[i]
        )
        for i in range(2)
    ]
    copies = [
        pltpu.make_async_copy(
            science_ref.at[:, pl.ds(starts[shift], chunk)],
            out_refs[shift].at[:, pl.ds(chunk + LANES, chunk)],
            sems.at[3 + shift],
        )
        for shift in range(size)
    ]
    copies.append(pltpu.make_async_copy(plan_ref, plan_now, sems.at[2]))
    for copy in loads + copies:
        copy.start()
    blank = jnp.zeros((rows, LANES), patch_ref.dtype)
    patch_ref[:, :LANES] = blank
    patch_ref[:, size * chunk + LANES :] = blank
    for copy in loads:
        copy.wait()
    lane = lax.broadcasted_iota(jnp.int32, (rows, LANES), 1)
    for shift in range(size):
        start = starts[shift]
        out_refs[shift][:, :chunk] = patch_ref[:, pl.ds(start + LANES, chunk)]
        before = patch_ref[:, pl.ds(start, LANES)].astype(jnp.float32)
        after = patch_ref[:, pl.ds(start + chunk + LANES, LANES)].astype(jnp.float32)
        rim = jnp.where(lane < LANES // 2, after, before)
        out_refs[shift][:, chunk : chunk + LANES] = rim.astype(patch_ref.dtype)
    for copy in copies:
        copy.wait()
    owner_ref[...] = jnp.full(owner_ref.shape, plan_now[step], jnp.int32)


def pick_kernel(owner_ref, *refs):
    *recv_refs, out_ref = refs
    rows, ext = out_ref.shape
    size = len(recv_refs)
    me = lax.axis_index("expo")
    blocks = []
    for b in range(ext // LANES):
        columns = slice(b * LANES, (b + 1) * LANES)
        block = recv_refs[0][:, columns].astype(jnp.float32)
        for shift in range(1, size):
            block = jnp.where(
                owner_ref[...] == source(me, shift, size), recv_refs[shift][:, columns].astype(jnp.float32), block
            )
        blocks.append(block.astype(out_ref.dtype))
    whole = jnp.concatenate(blocks[-1:] + blocks, axis=1)
    out_ref[...] = whole[:, LANES - HALF : LANES - HALF + ext]


def column_positions(first_col, block, width):
    col = lax.broadcasted_iota(jnp.int32, (8, LANES), 1) + (first_col + block * LANES)
    return 2.0 * (col.astype(jnp.float32) + 0.5) / width - 1.0


def band_kernel(orders_ref, row_ref, col_ref):
    rows = row_ref.shape[0] // NB
    near = 1 - 2 * lax.rem(lax.axis_index("tile"), 2)
    source = lax.broadcasted_iota(jnp.int32, (rows, 3 * rows), 1)
    moved = jnp.where(source < rows, 0, jnp.where(source < 2 * rows, near - 1, -near - 2))
    offset = (
        source + moved * rows - lax.broadcasted_iota(jnp.int32, (rows, 3 * rows), 0)
    ).astype(jnp.float32)
    shift = (
        lax.broadcasted_iota(jnp.int32, (2 * LANES, LANES), 0)
        - lax.broadcasted_iota(jnp.int32, (2 * LANES, LANES), 1)
        - HALF
    ).astype(jnp.float32)
    for k in range(NB):
        norm = tap_norm(SIGMAS[k], orders_ref[k, 0])
        row_ref[k * rows : (k + 1) * rows] = (
            tap_values(offset, SIGMAS[k], orders_ref[k, 0]) / norm
        ).astype(jnp.bfloat16)
        norm = tap_norm(SIGMAS[k], orders_ref[k, 1])
        col_ref[k] = (tap_values(shift, SIGMAS[k], orders_ref[k, 1]) / norm).astype(jnp.bfloat16)


def fit_kernel(weight_ref, hits_ref, row_band_ref, col_band_ref, own_ref, near_ref, far_ref, *refs, width):
    *image_refs, conv_ref, sums_ref, row_ref, parts_ref = refs
    tile_at = lax.axis_index("tile")
    expo_at = lax.axis_index("expo")
    rows, ext = own_ref.shape
    expos = len(image_refs)
    chunk = ext - LANES
    blocks = chunk // LANES

    patch = jnp.concatenate([own_ref[...], near_ref[...], far_ref[...]], axis=0)
    row_ref[...] = jnp.dot(
        row_band_ref[...], patch, preferred_element_type=jnp.float32
    ).astype(jnp.bfloat16)
    for k in range(NB):
        window = jnp.concatenate(
            [
                row_ref[k * rows : (k + 1) * rows, b * LANES : (b + 2) * LANES]
                for b in range(blocks)
            ],
            axis=0,
        )
        out = jnp.dot(window, col_band_ref[k], preferred_element_type=jnp.float32)
        conv_ref[k] = out.reshape(blocks, rows, LANES)

    first_col = expo_at * chunk
    xs = [column_positions(first_col, b, width) for b in range(blocks)]

    def fold(x):
        total = x[:8]
        for i in range(8, rows, 8):
            total = total + x[i : i + 8]
        return total

    def moments(at, left, right, count):
        total = [None] * count
        for b in range(blocks):
            term = fold(left(b) * right(b)) if right is not None else fold(left(b))
            for i in range(count):
                total[i] = term if total[i] is None else total[i] + term
                if i < count - 1:
                    term = term * xs[b]
        for i in range(count):
            parts_ref[at + i] = total[i]

    def conv(k):
        return lambda b: conv_ref[k, b]

    def sci(shift):
        return lambda b: image_refs[shift][:, ext + b * LANES : ext + (b + 1) * LANES].astype(jnp.float32)

    blank = jnp.zeros((8, LANES), jnp.float32)
    at = 0
    for j, k in PAIRS:
        moments(at, conv(j), conv(k), 3)
        at += 3
    for k in range(NB):
        moments(at, conv(k), None, 2)
        at += 2
    while at % 8:
        parts_ref[at] = blank
        at += 1
    begin = at
    for shift in range(expos):
        row = at + NU * source(expo_at, shift, expos)
        for k in range(NB):
            moments(row + 2 * k, conv(k), sci(shift), 2)
        moments(row + NU - 1, sci(shift), None, 1)
    at += NU * expos
    weight = jnp.broadcast_to(weight_ref[...] * hits_ref[...].astype(jnp.float32), (8, LANES))
    weight = jnp.where(tile_at == 0, weight, 0.0)
    spot = (
        (lax.broadcasted_iota(jnp.int32, (8, LANES), 0) == 0)
        & (lax.broadcasted_iota(jnp.int32, (8, LANES), 1) == 0)
    )
    for e in range(expos):
        parts_ref[at + e] = jnp.where(spot & (expo_at == e), weight, 0.0)
    at += expos
    while at % 8:
        parts_ref[at] = blank
        at += 1
    ones = jnp.ones((8, LANES), jnp.float32)
    rows_of = []
    for first, last in ((0, begin), (begin, at)):
        lanes = jnp.sum(parts_ref[first:last], axis=1)
        spare = LANES - (last - first)
        if spare:
            lanes = jnp.concatenate([lanes, jnp.zeros((spare, LANES), jnp.float32)], axis=0)
        rows_of.append(
            lax.dot_general(
                ones,
                lanes,
                (((1,), (1,)), ((), ())),
                precision=lax.Precision.HIGHEST,
                preferred_element_type=jnp.float32,
            )
        )
    both = jnp.where(lax.broadcasted_iota(jnp.int32, (8, LANES), 0) < 4, rows_of[0], rows_of[1])
    for i in range(sums_ref.shape[0]):
        sums_ref[i] = both


def table(expos):
    columns = np.zeros((NU + expos + 1, 16), np.int32)
    for at, (j, k) in enumerate(PAIRS):
        for a, b in ((j, k), (k, j)):
            columns[b, a] = 3 * at
            columns[NB + b, a] = columns[b, NB + a] = 3 * at + 1
            columns[NB + b, NB + a] = 3 * at + 2
    for k in range(NB):
        for x in range(2):
            columns[NU - 1, x * NB + k] = columns[x * NB + k, NU - 1] = 3 * len(PAIRS) + 2 * k + x
    for e in range(expos):
        columns[NU + e, :NU] = [NU * e + 2 * k + x for x in range(2) for k in range(NB)] + [NU * e + NU - 1]
        columns[NU + expos, e] = NU * expos + e
    return np.ascontiguousarray(np.broadcast_to(columns[:, :, None], columns.shape + (LANES,)))


def solve_kernel(table_ref, sums_ref, conv_ref, *refs, width, pixels):
    *image_refs, coadd_ref, coeffs_ref, tile_ref, sems = refs
    expo_at = lax.axis_index("expo")
    expos = len(image_refs)
    rows, chunk = coadd_ref.shape
    blocks = chunk // LANES
    ext = image_refs[0].shape[1] - chunk
    sub = lax.broadcasted_iota(jnp.int32, (16, LANES), 0)
    lane = lax.broadcasted_iota(jnp.int32, (16, LANES), 1)
    sums = sums_ref[0]
    for i in range(1, sums_ref.shape[0]):
        sums = sums + sums_ref[i]
    first = jnp.broadcast_to(sums[0:1], (16, LANES))
    second = jnp.broadcast_to(sums[4:5], (16, LANES))

    columns = [
        jnp.take_along_axis(first if j < NU else second, table_ref[j], axis=1) for j in range(NU + expos)
    ]
    spread = jnp.take_along_axis(second, table_ref[NU + expos], axis=1)
    weight = [jnp.broadcast_to(spread[e : e + 1], (16, LANES)) for e in range(expos)]
    columns[NU - 1] = jnp.where(sub == NU - 1, float(pixels), columns[NU - 1])

    trace = columns[0][0:1]
    for j in range(1, NU):
        trace = trace + columns[j][j : j + 1]
    scale = 1.0 / trace
    for j in range(NU + expos):
        columns[j] = columns[j] * scale
        if j < NU:
            columns[j] = columns[j] + jnp.where(sub == j, RIDGE / NU, 0.0)
    for i in range(NU):
        inverse = 1.0 / columns[i][i : i + 1]
        for j in range(i + 1, NU + expos):
            factor = columns[j][i : i + 1] * inverse
            columns[j] = jnp.where(sub == i, factor, columns[j] - columns[i] * factor)

    solved = columns[NU:]
    own = solved[0]
    mixed = weight[0] * solved[0]
    for e in range(1, expos):
        own = jnp.where(expo_at == e, solved[e], own)
        mixed = mixed + weight[e] * solved[e]
    diagonal = (sub == lane) & (sub < NU)
    coeffs_ref[...] = jnp.sum(jnp.where(diagonal, own, 0.0), axis=0, keepdims=True)[:, :NU]
    scale = [jnp.broadcast_to(mixed[u : u + 1], (8, LANES)) for u in range(NU)]
    gains = []
    for shift in range(expos):
        gain = weight[0][:8]
        for e in range(1, expos):
            gain = jnp.where(source(expo_at, shift, expos) == e, weight[e][:8], gain)
        gains.append(gain)
    first_col = expo_at * chunk
    copies = []
    for r in range(0, rows, 8):
        for b in range(blocks):
            at = slice(ext + b * LANES, ext + (b + 1) * LANES)
            x = column_positions(first_col, b, width)
            total = -scale[NU - 1]
            for gain, image_ref in zip(gains, image_refs):
                total = total + gain * image_ref[:, at].astype(jnp.float32)[r : r + 8]
            model = (scale[0] + scale[NB] * x) * conv_ref[0, b, r : r + 8]
            for k in range(1, NB):
                model = model + (scale[k] + scale[NB + k] * x) * conv_ref[k, b, r : r + 8]
            tile_ref[r : r + 8, b * LANES : (b + 1) * LANES] = total - model
        copies.append(
            pltpu.make_async_copy(tile_ref.at[pl.ds(r, 8)], coadd_ref.at[pl.ds(r, 8)], sems.at[r // 8])
        )
        copies[-1].start()
    for copy in copies:
        copy.wait()


def swaps(first, size):
    return [pair for i in range(first, size - 1, 2) for pair in ((i, i + 1), (i + 1, i))]


def tiled_device(template, science, plan, orders, coadd_weight, intersection):
    expos = lax.axis_size("expo")
    tiles = lax.axis_size("tile")
    _, rows, width = template.shape
    steps = science.shape[1]
    chunk = width // expos
    ext = chunk + LANES
    blocks = chunk // LANES
    smem = pl.BlockSpec(memory_space=pltpu.SMEM)
    vmem = pl.BlockSpec(memory_space=pltpu.VMEM)
    small = pltpu.CompilerParams(vmem_limit_bytes=16 * 1024 * 1024)
    hbm = pl.BlockSpec(memory_space=pltpu.HBM)
    row_band, col_band = pl.pallas_call(
        band_kernel,
        out_shape=(
            jax.ShapeDtypeStruct((NB * rows, 3 * rows), jnp.bfloat16),
            jax.ShapeDtypeStruct((NB, 2 * LANES, LANES), jnp.bfloat16),
        ),
        in_specs=[smem],
        out_specs=(vmem, vmem),
        compiler_params=small,
        cost_estimate=pl.CostEstimate(flops=4_000_000, bytes_accessed=500_000, transcendentals=200_000),
    )(orders)
    coadds = []
    fitted = []
    for step in range(steps):
        *images, owner = pl.pallas_call(
            functools.partial(send_kernel, step=step),
            out_shape=(pltpu.VMEM((rows, ext + chunk), template.dtype),) * expos
            + (jax.ShapeDtypeStruct((rows, LANES), jnp.int32),),
            in_specs=[hbm] * 3,
            out_specs=(vmem,) * (expos + 1),
            scratch_shapes=[
                pltpu.VMEM((rows, width + 2 * LANES), template.dtype),
                pltpu.SMEM(plan.shape, jnp.int32),
                pltpu.SemaphoreType.DMA((expos + 3,)),
            ],
            compiler_params=small,
        )(
            pltpu.with_memory_space_constraint(template[0], pltpu.HBM),
            pltpu.with_memory_space_constraint(science[0, step], pltpu.HBM),
            pltpu.with_memory_space_constraint(plan, pltpu.HBM),
        )
        for shift in range(expos - 1, 0, -1):
            pairs = [(e, int(target(e, shift, expos))) for e in range(expos)]
            images[shift] = lax.ppermute(images[shift], "expo", pairs)
        own = pl.pallas_call(
            pick_kernel,
            out_shape=jax.ShapeDtypeStruct((rows, ext), template.dtype),
            in_specs=[vmem] * (1 + expos),
            out_specs=vmem,
            compiler_params=small,
        )(owner, *images)
        far = lax.ppermute(own, "tile", swaps(1, tiles))
        near = lax.ppermute(own, "tile", swaps(0, tiles))
        conv, sums = pl.pallas_call(
            functools.partial(fit_kernel, width=width),
            out_shape=(
                jax.ShapeDtypeStruct((NB, blocks, rows, LANES), jnp.float32),
                jax.ShapeDtypeStruct((tiles * expos, 8, LANES), jnp.float32),
            ),
            in_specs=[vmem] * (7 + expos),
            out_specs=(vmem, vmem),
            scratch_shapes=[
                pltpu.VMEM((NB * rows, ext), jnp.bfloat16),
                pltpu.VMEM((80 + 14 * expos + 8, 8, LANES), jnp.float32),
            ],
            compiler_params=small,
        )(
            coadd_weight[:, step : step + 1],
            intersection[:, step : step + 1],
            row_band,
            col_band,
            own,
            near,
            far,
            *images,
        )
        sums = lax.all_to_all(sums, ("tile", "expo"), split_axis=0, concat_axis=0, tiled=True)
        coadd, coeffs = pl.pallas_call(
            functools.partial(solve_kernel, width=width, pixels=tiles * rows * width),
            out_shape=(
                jax.ShapeDtypeStruct((rows, chunk), jnp.float32),
                jax.ShapeDtypeStruct((1, NU), jnp.float32),
            ),
            in_specs=[vmem] * (3 + expos),
            out_specs=(pl.BlockSpec(memory_space=pl.ANY), vmem),
            scratch_shapes=[
                pltpu.VMEM((rows, chunk), jnp.float32),
                pltpu.SemaphoreType.DMA((rows // 8,)),
            ],
            compiler_params=small,
        )(jnp.asarray(table(expos)), sums, conv, *images)
        coadds.append(coadd[None])
        fitted.append(coeffs)
    return (jnp.concatenate(coadds), jnp.stack(fitted, axis=1))


def broadcast(block, axis, holder):
    block = jnp.where(lax.axis_index(axis) == holder, block, jnp.zeros_like(block))
    return lax.psum(block, axis)


def extended(x, sides, width):
    for axis, dim in sides:
        size, length = (lax.axis_size(axis), x.shape[dim])
        up = [(i, (i + 1) % size) for i in range(size - 1)]
        down = [(j, i) for i, j in up]
        last = lax.slice_in_dim(x, length - width, length, axis=dim)
        first = lax.slice_in_dim(x, 0, width, axis=dim)
        before = lax.ppermute(last, axis, up)
        after = lax.ppermute(first, axis, down)
        x = jnp.concatenate([before, x, after], axis=dim)
    return x


def make_filters(orders):
    taps_pos = jnp.arange(2 * HALF + 1).astype(jnp.float32) - HALF
    row_list = []
    col_list = []
    for basis in range(NB):
        sigma = SIGMAS[basis]
        envelope = jnp.exp(-taps_pos * taps_pos / (2.0 * sigma * sigma))
        row_filter = envelope * power_of(taps_pos, orders[basis, 0])
        col_filter = envelope * power_of(taps_pos, orders[basis, 1])
        row_list.append(row_filter / jnp.sqrt(jnp.sum(row_filter * row_filter)))
        col_list.append(col_filter / jnp.sqrt(jnp.sum(col_filter * col_filter)))
    return (jnp.stack(row_list).astype(jnp.bfloat16), jnp.stack(col_list).astype(jnp.bfloat16))


def band_matrix(filters, out_len, in_len):
    offset = jnp.arange(in_len)[None, :] - jnp.arange(out_len)[:, None]
    taps_idx = jnp.arange(2 * HALF + 1)
    picks = (offset[:, :, None] == taps_idx[None, None, :]).astype(jnp.float32)
    band = jnp.einsum("ijt,kt->kij", picks, filters.astype(jnp.float32))
    return band.astype(jnp.bfloat16)


def any_device(template, science, plan, orders, coadd_weight, intersection):
    row_filters, col_filters = make_filters(orders)
    rows = template.shape[1]
    width = template.shape[2]
    blocks_count = width // 128
    steps_count = science.shape[1]
    row_band = band_matrix(row_filters, rows, rows + 2 * HALF)
    col_band = jnp.transpose(band_matrix(col_filters, 128, 128 + 2 * HALF), (0, 2, 1))
    column_pos = 2.0 * (jnp.arange(width).astype(jnp.float32) + 0.5) / width - 1.0
    pieces = []
    fitted = []
    for step in range(steps_count):
        received = broadcast(template[0], "expo", plan[step])
        padded = extended(received, (("tile", 0),), HALF)
        rowconv = jnp.einsum(
            "kij,jw->kiw", row_band, padded, preferred_element_type=jnp.float32
        ).astype(jnp.bfloat16)
        blocks = rowconv.reshape(NB, rows, blocks_count, 128)
        empty_rim = jnp.zeros((NB, rows, 1, HALF), jnp.bfloat16)
        previous = jnp.concatenate([empty_rim, blocks[:, :, :-1, 128 - HALF :]], axis=2)
        following = jnp.concatenate([blocks[:, :, 1:, :HALF], empty_rim], axis=2)
        window = jnp.concatenate([previous, blocks, following], axis=3)
        conv = jnp.einsum("krbj,kjc->krbc", window, col_band, preferred_element_type=jnp.float32)
        conv = conv.reshape(NB, rows, width)
        fields = jnp.concatenate(
            [conv, conv * column_pos, jnp.ones((1, rows, width), jnp.float32)], axis=0
        )
        fields = fields.reshape(NU, rows * width)
        exposure_image = science[0, step].astype(jnp.float32).reshape(rows * width)
        normal_local = jnp.dot(fields, fields.T, precision=lax.Precision.HIGHEST)
        project_local = jnp.dot(fields, exposure_image, precision=lax.Precision.HIGHEST)
        normal_matrix, projections = lax.psum((normal_local, project_local), "tile")
        normal_matrix = normal_matrix + RIDGE * (jnp.trace(normal_matrix) / NU) * jnp.eye(
            NU, dtype=jnp.float32
        )
        factor = jnp.linalg.cholesky(normal_matrix)
        coeffs = jax.scipy.linalg.cho_solve((factor, True), projections)
        model = jnp.dot(coeffs, fields, precision=lax.Precision.HIGHEST)
        difference = exposure_image - model
        weight_now = coadd_weight[0, step] * intersection[0, step].astype(jnp.float32)
        pieces.append((weight_now * difference).reshape(rows, width))
        fitted.append(coeffs)
    weighted = jnp.stack(pieces)
    received_parts = lax.all_to_all(weighted[None], "expo", split_axis=3, concat_axis=0, tiled=True)
    coadd = jnp.sum(received_parts, axis=0)
    return (coadd, jnp.stack(fitted)[None])


def per_device(template, science, plan, orders, coadd_weight, intersection):
    expos = lax.axis_size("expo")
    rows, width = template.shape[1:]
    whole_lanes = width % (expos * LANES) == 0 and rows % 16 == 0
    few = (NU + 1) * expos <= LANES and NU + expos <= LANES
    body = tiled_device if whole_lanes and few else any_device
    return body(template, science, plan, orders, coadd_weight, intersection)


def solution(mesh):
    return jax.shard_map(
        per_device,
        mesh=mesh,
        in_specs=(
            P(("groups", "expo"), "tile", None),
            P(("groups", "expo"), None, "tile", None),
            P("groups"),
            P(),
            P(("groups", "expo"), None),
            P(("groups", "expo"), None),
        ),
        out_specs=(P("groups", "tile", "expo"), P(("groups", "expo"), None, None)),
        check_vma=False,
    )
```

```python
import functools

import jax
import jax.numpy as jnp
import numpy as np
from jax import lax
from jax.experimental import pallas as pl
from jax.experimental.pallas import tpu as pltpu
from jax.sharding import PartitionSpec as P

HALF = 15
NB = 6
NU = 13
LANES = 128
PAIRS = [(j, k) for j in range(NB) for k in range(j, NB)]

SIGMAS = (0.8, 1.4, 2.2, 3.0, 4.0, 5.5)
RIDGE = 0.05


def power_of(pos, order):
    return jnp.where(order == 0, 1.0, jnp.where(order == 1, pos, pos * pos))


def tap_values(pos, sigma, order):
    value = jnp.exp(-pos * pos / (2.0 * sigma * sigma)) * power_of(pos, order)
    return jnp.where(jnp.abs(pos) <= HALF, value, 0.0)


def tap_norm(sigma, order):
    pos = lax.broadcasted_iota(jnp.int32, (8, LANES), 1).astype(jnp.float32) - HALF
    value = tap_values(pos, sigma, order)
    return jnp.sqrt(jnp.sum(value * value, axis=1, keepdims=True))[:1]


def target(me, shift, size):
    return me ^ shift if size & (size - 1) == 0 else (me + shift) % size


def source(me, shift, size):
    return me ^ shift if size & (size - 1) == 0 else (me - shift + size) % size


def send_kernel(template_ref, science_ref, plan_ref, *refs, step):
    *out_refs, owner_ref, patch_ref, plan_now, sems = refs
    size = len(out_refs) // 2
    image_refs = out_refs[size:]
    rows, ext = image_refs[0].shape
    chunk = ext - LANES
    half = size * chunk // 2
    me = lax.axis_index("expo")
    starts = [pl.multiple_of(target(me, shift, size) * chunk, chunk) for shift in range(size)]
    loads = [
        pltpu.make_async_copy(
            template_ref.at[:, pl.ds(i * half, half)], patch_ref.at[:, pl.ds((i * half + LANES), half)], sems.at[i]
        )
        for i in range(2)
    ]
    copies = [
        pltpu.make_async_copy(
            science_ref.at[:, pl.ds(starts[shift], chunk)],
            image_refs[shift].at[:, pl.ds(0, chunk)],
            sems.at[3 + shift],
        )
        for shift in range(size)
    ]
    copies.append(pltpu.make_async_copy(plan_ref, plan_now, sems.at[2]))
    for copy in loads + copies:
        copy.start()
    blank = jnp.zeros((rows, LANES), patch_ref.dtype)
    patch_ref[:, :LANES] = blank
    patch_ref[:, size * chunk + LANES :] = blank
    for image_ref in image_refs:
        image_ref[:, chunk:] = blank
    for copy in loads:
        copy.wait()
    lane = lax.broadcasted_iota(jnp.int32, (rows, LANES), 1)
    for shift in range(size):
        start = starts[shift]
        out_refs[shift][:, :chunk] = patch_ref[:, pl.ds(start + LANES, chunk)]
        before = patch_ref[:, pl.ds(start, LANES)].astype(jnp.float32)
        after = patch_ref[:, pl.ds(start + chunk + LANES, LANES)].astype(jnp.float32)
        rim = jnp.where(lane < LANES // 2, after, before)
        out_refs[shift][:, chunk:] = rim.astype(patch_ref.dtype)
    for copy in copies:
        copy.wait()
    owner_ref[...] = jnp.full(owner_ref.shape, plan_now[step], jnp.int32)


def pick_kernel(owner_ref, _, *refs):
    *recv_refs, out_ref = refs
    rows, ext = out_ref.shape
    size = len(recv_refs)
    me = lax.axis_index("expo")
    blocks = []
    for b in range(ext // LANES):
        columns = slice(b * LANES, (b + 1) * LANES)
        block = recv_refs[0][:, columns].astype(jnp.float32)
        for shift in range(1, size):
            block = jnp.where(
                owner_ref[...] == source(me, shift, size), recv_refs[shift][:, columns].astype(jnp.float32), block
            )
        blocks.append(block.astype(out_ref.dtype))
    whole = jnp.concatenate(blocks[-1:] + blocks, axis=1)
    out_ref[...] = whole[:, LANES - HALF : LANES - HALF + ext]


def column_positions(first_col, block, width):
    col = lax.broadcasted_iota(jnp.int32, (8, LANES), 1) + (first_col + block * LANES)
    return 2.0 * (col.astype(jnp.float32) + 0.5) / width - 1.0


def band_kernel(orders_ref, row_ref, col_ref):
    rows = row_ref.shape[0] // NB
    near = 1 - 2 * lax.rem(lax.axis_index("tile"), 2)
    source = lax.broadcasted_iota(jnp.int32, (rows, 3 * rows), 1)
    moved = jnp.where(source < rows, 0, jnp.where(source < 2 * rows, near - 1, -near - 2))
    offset = (
        source + moved * rows - lax.broadcasted_iota(jnp.int32, (rows, 3 * rows), 0)
    ).astype(jnp.float32)
    shift = (
        lax.broadcasted_iota(jnp.int32, (2 * LANES, LANES), 0)
        - lax.broadcasted_iota(jnp.int32, (2 * LANES, LANES), 1)
        - HALF
    ).astype(jnp.float32)
    for k in range(NB):
        norm = tap_norm(SIGMAS[k], orders_ref[k, 0])
        row_ref[k * rows : (k + 1) * rows] = (
            tap_values(offset, SIGMAS[k], orders_ref[k, 0]) / norm
        ).astype(jnp.bfloat16)
        norm = tap_norm(SIGMAS[k], orders_ref[k, 1])
        col_ref[k] = (tap_values(shift, SIGMAS[k], orders_ref[k, 1]) / norm).astype(jnp.bfloat16)


def fit_kernel(weight_ref, hits_ref, row_band_ref, col_band_ref, own_ref, near_ref, far_ref, *refs, width):
    *image_refs, conv_ref, sums_ref, row_ref, parts_ref = refs
    tile_at = lax.axis_index("tile")
    expo_at = lax.axis_index("expo")
    rows, ext = own_ref.shape
    expos = len(image_refs)
    chunk = ext - LANES
    blocks = chunk // LANES

    patch = jnp.concatenate([own_ref[...], near_ref[...], far_ref[...]], axis=0)
    row_ref[...] = jnp.dot(
        row_band_ref[...], patch, preferred_element_type=jnp.float32
    ).astype(jnp.bfloat16)
    for k in range(NB):
        window = jnp.concatenate(
            [
                row_ref[k * rows : (k + 1) * rows, b * LANES : (b + 2) * LANES]
                for b in range(blocks)
            ],
            axis=0,
        )
        out = jnp.dot(window, col_band_ref[k], preferred_element_type=jnp.float32)
        conv_ref[k] = out.reshape(blocks, rows, LANES)

    first_col = expo_at * chunk
    xs = [column_positions(first_col, b, width) for b in range(blocks)]

    def fold(x):
        total = x[:8]
        for i in range(8, rows, 8):
            total = total + x[i : i + 8]
        return total

    def moments(at, left, right, count):
        total = [None] * count
        for b in range(blocks):
            term = fold(left(b) * right(b)) if right is not None else fold(left(b))
            for i in range(count):
                total[i] = term if total[i] is None else total[i] + term
                if i < count - 1:
                    term = term * xs[b]
        for i in range(count):
            parts_ref[at + i] = total[i]

    def conv(k):
        return lambda b: conv_ref[k, b]

    def sci(shift):
        return lambda b: image_refs[shift][:, b * LANES : (b + 1) * LANES].astype(jnp.float32)

    blank = jnp.zeros((8, LANES), jnp.float32)
    at = 0
    for j, k in PAIRS:
        moments(at, conv(j), conv(k), 3)
        at += 3
    for k in range(NB):
        moments(at, conv(k), None, 2)
        at += 2
    while at % 8:
        parts_ref[at] = blank
        at += 1
    begin = at
    for shift in range(expos):
        row = at + NU * source(expo_at, shift, expos)
        for k in range(NB):
            moments(row + 2 * k, conv(k), sci(shift), 2)
        moments(row + NU - 1, sci(shift), None, 1)
    at += NU * expos
    weight = jnp.broadcast_to(weight_ref[...] * hits_ref[...].astype(jnp.float32), (8, LANES))
    weight = jnp.where(tile_at == 0, weight, 0.0)
    spot = (
        (lax.broadcasted_iota(jnp.int32, (8, LANES), 0) == 0)
        & (lax.broadcasted_iota(jnp.int32, (8, LANES), 1) == 0)
    )
    for e in range(expos):
        parts_ref[at + e] = jnp.where(spot & (expo_at == e), weight, 0.0)
    at += expos
    while at % 8:
        parts_ref[at] = blank
        at += 1
    ones = jnp.ones((8, LANES), jnp.float32)
    rows_of = []
    for first, last in ((0, begin), (begin, at)):
        lanes = jnp.sum(parts_ref[first:last], axis=1)
        spare = LANES - (last - first)
        if spare:
            lanes = jnp.concatenate([lanes, jnp.zeros((spare, LANES), jnp.float32)], axis=0)
        rows_of.append(
            lax.dot_general(
                ones,
                lanes,
                (((1,), (1,)), ((), ())),
                precision=lax.Precision.HIGHEST,
                preferred_element_type=jnp.float32,
            )
        )
    both = jnp.where(lax.broadcasted_iota(jnp.int32, (8, LANES), 0) < 4, rows_of[0], rows_of[1])
    for i in range(sums_ref.shape[0]):
        sums_ref[i] = both


def table(expos):
    columns = np.zeros((NU + expos + 1, 16), np.int32)
    for at, (j, k) in enumerate(PAIRS):
        for a, b in ((j, k), (k, j)):
            columns[b, a] = 3 * at
            columns[NB + b, a] = columns[b, NB + a] = 3 * at + 1
            columns[NB + b, NB + a] = 3 * at + 2
    for k in range(NB):
        for x in range(2):
            columns[NU - 1, x * NB + k] = columns[x * NB + k, NU - 1] = 3 * len(PAIRS) + 2 * k + x
    for e in range(expos):
        columns[NU + e, :NU] = [NU * e + 2 * k + x for x in range(2) for k in range(NB)] + [NU * e + NU - 1]
        columns[NU + expos, e] = NU * expos + e
    return np.ascontiguousarray(np.broadcast_to(columns[:, :, None], columns.shape + (LANES,)))


def solve_kernel(table_ref, sums_ref, conv_ref, *refs, width, pixels):
    *image_refs, coadd_ref, coeffs_ref, tile_ref, sems = refs
    expo_at = lax.axis_index("expo")
    expos = len(image_refs)
    rows, chunk = coadd_ref.shape
    blocks = chunk // LANES
    sub = lax.broadcasted_iota(jnp.int32, (16, LANES), 0)
    lane = lax.broadcasted_iota(jnp.int32, (16, LANES), 1)
    sums = sums_ref[0]
    for i in range(1, sums_ref.shape[0]):
        sums = sums + sums_ref[i]
    first = jnp.broadcast_to(sums[0:1], (16, LANES))
    second = jnp.broadcast_to(sums[4:5], (16, LANES))

    columns = [
        jnp.take_along_axis(first if j < NU else second, table_ref[j], axis=1) for j in range(NU + expos)
    ]
    spread = jnp.take_along_axis(second, table_ref[NU + expos], axis=1)
    weight = [jnp.broadcast_to(spread[e : e + 1], (16, LANES)) for e in range(expos)]
    columns[NU - 1] = jnp.where(sub == NU - 1, float(pixels), columns[NU - 1])

    trace = columns[0][0:1]
    for j in range(1, NU):
        trace = trace + columns[j][j : j + 1]
    scale = 1.0 / trace
    for j in range(NU + expos):
        columns[j] = columns[j] * scale
        if j < NU:
            columns[j] = columns[j] + jnp.where(sub == j, RIDGE / NU, 0.0)
    for i in range(NU):
        inverse = 1.0 / columns[i][i : i + 1]
        for j in range(i + 1, NU + expos):
            factor = columns[j][i : i + 1] * inverse
            columns[j] = jnp.where(sub == i, factor, columns[j] - columns[i] * factor)

    solved = columns[NU:]
    own = solved[0]
    mixed = weight[0] * solved[0]
    for e in range(1, expos):
        own = jnp.where(expo_at == e, solved[e], own)
        mixed = mixed + weight[e] * solved[e]
    diagonal = (sub == lane) & (sub < NU)
    coeffs_ref[...] = jnp.sum(jnp.where(diagonal, own, 0.0), axis=0, keepdims=True)[:, :NU]
    scale = [jnp.broadcast_to(mixed[u : u + 1], (8, LANES)) for u in range(NU)]
    gains = []
    for shift in range(expos):
        gain = weight[0][:8]
        for e in range(1, expos):
            gain = jnp.where(source(expo_at, shift, expos) == e, weight[e][:8], gain)
        gains.append(gain)
    first_col = expo_at * chunk
    copies = []
    for r in range(0, rows, 8):
        for b in range(blocks):
            at = slice(b * LANES, (b + 1) * LANES)
            x = column_positions(first_col, b, width)
            total = -scale[NU - 1]
            for gain, image_ref in zip(gains, image_refs):
                total = total + gain * image_ref[:, at].astype(jnp.float32)[r : r + 8]
            model = (scale[0] + scale[NB] * x) * conv_ref[0, b, r : r + 8]
            for k in range(1, NB):
                model = model + (scale[k] + scale[NB + k] * x) * conv_ref[k, b, r : r + 8]
            tile_ref[r : r + 8, b * LANES : (b + 1) * LANES] = total - model
        copies.append(
            pltpu.make_async_copy(tile_ref.at[pl.ds(r, 8)], coadd_ref.at[pl.ds(r, 8)], sems.at[r // 8])
        )
        copies[-1].start()
    for copy in copies:
        copy.wait()


def swaps(first, size):
    return [pair for i in range(first, size - 1, 2) for pair in ((i, i + 1), (i + 1, i))]


def tiled_device(template, science, plan, orders, coadd_weight, intersection):
    expos = lax.axis_size("expo")
    tiles = lax.axis_size("tile")
    _, rows, width = template.shape
    steps = science.shape[1]
    chunk = width // expos
    ext = chunk + LANES
    blocks = chunk // LANES
    smem = pl.BlockSpec(memory_space=pltpu.SMEM)
    vmem = pl.BlockSpec(memory_space=pltpu.VMEM)
    small = pltpu.CompilerParams(vmem_limit_bytes=16 * 1024 * 1024)
    hbm = pl.BlockSpec(memory_space=pltpu.HBM)
    row_band, col_band = pl.pallas_call(
        band_kernel,
        out_shape=(
            jax.ShapeDtypeStruct((NB * rows, 3 * rows), jnp.bfloat16),
            jax.ShapeDtypeStruct((NB, 2 * LANES, LANES), jnp.bfloat16),
        ),
        in_specs=[smem],
        out_specs=(vmem, vmem),
        compiler_params=small,
        cost_estimate=pl.CostEstimate(flops=4_000_000, bytes_accessed=500_000, transcendentals=200_000),
    )(orders)
    coadds = []
    fitted = []
    for step in range(steps):
        *blocks_out, owner = pl.pallas_call(
            functools.partial(send_kernel, step=step),
            out_shape=(pltpu.VMEM((rows, ext), template.dtype),) * expos
            + (pltpu.VMEM((rows, ext), science.dtype),) * expos
            + (jax.ShapeDtypeStruct((rows, LANES), jnp.int32),),
            in_specs=[hbm] * 3,
            out_specs=(vmem,) * (2 * expos + 1),
            scratch_shapes=[
                pltpu.VMEM((rows, width + 2 * LANES), template.dtype),
                pltpu.SMEM(plan.shape, jnp.int32),
                pltpu.SemaphoreType.DMA((expos + 3,)),
            ],
            compiler_params=small,
        )(
            pltpu.with_memory_space_constraint(template[0], pltpu.HBM),
            pltpu.with_memory_space_constraint(science[0, step], pltpu.HBM),
            pltpu.with_memory_space_constraint(plan, pltpu.HBM),
        )
        patches, images = blocks_out[:expos], blocks_out[expos:]
        for group in (patches, images):
            for shift in range(expos - 1, 0, -1):
                pairs = [(e, int(target(e, shift, expos))) for e in range(expos)]
                group[shift] = lax.ppermute(group[shift], "expo", pairs)
        own = pl.pallas_call(
            pick_kernel,
            out_shape=jax.ShapeDtypeStruct((rows, ext), template.dtype),
            in_specs=[vmem, pl.BlockSpec(memory_space=pl.ANY)] + [vmem] * expos,
            out_specs=vmem,
            compiler_params=small,
        )(owner, row_band, *patches)
        far = lax.ppermute(own, "tile", swaps(1, tiles))
        near = lax.ppermute(own, "tile", swaps(0, tiles))
        conv, sums = pl.pallas_call(
            functools.partial(fit_kernel, width=width),
            out_shape=(
                jax.ShapeDtypeStruct((NB, blocks, rows, LANES), jnp.float32),
                jax.ShapeDtypeStruct((tiles * expos, 8, LANES), jnp.float32),
            ),
            in_specs=[vmem] * (7 + expos),
            out_specs=(vmem, vmem),
            scratch_shapes=[
                pltpu.VMEM((NB * rows, ext), jnp.bfloat16),
                pltpu.VMEM((80 + 14 * expos + 8, 8, LANES), jnp.float32),
            ],
            compiler_params=small,
        )(
            coadd_weight[:, step : step + 1],
            intersection[:, step : step + 1],
            row_band,
            col_band,
            own,
            near,
            far,
            *images,
        )
        sums = lax.all_to_all(sums, ("tile", "expo"), split_axis=0, concat_axis=0, tiled=True)
        coadd, coeffs = pl.pallas_call(
            functools.partial(solve_kernel, width=width, pixels=tiles * rows * width),
            out_shape=(
                jax.ShapeDtypeStruct((rows, chunk), jnp.float32),
                jax.ShapeDtypeStruct((1, NU), jnp.float32),
            ),
            in_specs=[vmem] * (3 + expos),
            out_specs=(pl.BlockSpec(memory_space=pl.ANY), vmem),
            scratch_shapes=[
                pltpu.VMEM((rows, chunk), jnp.float32),
                pltpu.SemaphoreType.DMA((rows // 8,)),
            ],
            compiler_params=small,
        )(jnp.asarray(table(expos)), sums, conv, *images)
        coadds.append(coadd[None])
        fitted.append(coeffs)
    return (jnp.concatenate(coadds), jnp.stack(fitted, axis=1))


def broadcast(block, axis, holder):
    block = jnp.where(lax.axis_index(axis) == holder, block, jnp.zeros_like(block))
    return lax.psum(block, axis)


def extended(x, sides, width):
    for axis, dim in sides:
        size, length = (lax.axis_size(axis), x.shape[dim])
        up = [(i, (i + 1) % size) for i in range(size - 1)]
        down = [(j, i) for i, j in up]
        last = lax.slice_in_dim(x, length - width, length, axis=dim)
        first = lax.slice_in_dim(x, 0, width, axis=dim)
        before = lax.ppermute(last, axis, up)
        after = lax.ppermute(first, axis, down)
        x = jnp.concatenate([before, x, after], axis=dim)
    return x


def make_filters(orders):
    taps_pos = jnp.arange(2 * HALF + 1).astype(jnp.float32) - HALF
    row_list = []
    col_list = []
    for basis in range(NB):
        sigma = SIGMAS[basis]
        envelope = jnp.exp(-taps_pos * taps_pos / (2.0 * sigma * sigma))
        row_filter = envelope * power_of(taps_pos, orders[basis, 0])
        col_filter = envelope * power_of(taps_pos, orders[basis, 1])
        row_list.append(row_filter / jnp.sqrt(jnp.sum(row_filter * row_filter)))
        col_list.append(col_filter / jnp.sqrt(jnp.sum(col_filter * col_filter)))
    return (jnp.stack(row_list).astype(jnp.bfloat16), jnp.stack(col_list).astype(jnp.bfloat16))


def band_matrix(filters, out_len, in_len):
    offset = jnp.arange(in_len)[None, :] - jnp.arange(out_len)[:, None]
    taps_idx = jnp.arange(2 * HALF + 1)
    picks = (offset[:, :, None] == taps_idx[None, None, :]).astype(jnp.float32)
    band = jnp.einsum("ijt,kt->kij", picks, filters.astype(jnp.float32))
    return band.astype(jnp.bfloat16)


def any_device(template, science, plan, orders, coadd_weight, intersection):
    row_filters, col_filters = make_filters(orders)
    rows = template.shape[1]
    width = template.shape[2]
    blocks_count = width // 128
    steps_count = science.shape[1]
    row_band = band_matrix(row_filters, rows, rows + 2 * HALF)
    col_band = jnp.transpose(band_matrix(col_filters, 128, 128 + 2 * HALF), (0, 2, 1))
    column_pos = 2.0 * (jnp.arange(width).astype(jnp.float32) + 0.5) / width - 1.0
    pieces = []
    fitted = []
    for step in range(steps_count):
        received = broadcast(template[0], "expo", plan[step])
        padded = extended(received, (("tile", 0),), HALF)
        rowconv = jnp.einsum(
            "kij,jw->kiw", row_band, padded, preferred_element_type=jnp.float32
        ).astype(jnp.bfloat16)
        blocks = rowconv.reshape(NB, rows, blocks_count, 128)
        empty_rim = jnp.zeros((NB, rows, 1, HALF), jnp.bfloat16)
        previous = jnp.concatenate([empty_rim, blocks[:, :, :-1, 128 - HALF :]], axis=2)
        following = jnp.concatenate([blocks[:, :, 1:, :HALF], empty_rim], axis=2)
        window = jnp.concatenate([previous, blocks, following], axis=3)
        conv = jnp.einsum("krbj,kjc->krbc", window, col_band, preferred_element_type=jnp.float32)
        conv = conv.reshape(NB, rows, width)
        fields = jnp.concatenate(
            [conv, conv * column_pos, jnp.ones((1, rows, width), jnp.float32)], axis=0
        )
        fields = fields.reshape(NU, rows * width)
        exposure_image = science[0, step].astype(jnp.float32).reshape(rows * width)
        normal_local = jnp.dot(fields, fields.T, precision=lax.Precision.HIGHEST)
        project_local = jnp.dot(fields, exposure_image, precision=lax.Precision.HIGHEST)
        normal_matrix, projections = lax.psum((normal_local, project_local), "tile")
        normal_matrix = normal_matrix + RIDGE * (jnp.trace(normal_matrix) / NU) * jnp.eye(
            NU, dtype=jnp.float32
        )
        factor = jnp.linalg.cholesky(normal_matrix)
        coeffs = jax.scipy.linalg.cho_solve((factor, True), projections)
        model = jnp.dot(coeffs, fields, precision=lax.Precision.HIGHEST)
        difference = exposure_image - model
        weight_now = coadd_weight[0, step] * intersection[0, step].astype(jnp.float32)
        pieces.append((weight_now * difference).reshape(rows, width))
        fitted.append(coeffs)
    weighted = jnp.stack(pieces)
    received_parts = lax.all_to_all(weighted[None], "expo", split_axis=3, concat_axis=0, tiled=True)
    coadd = jnp.sum(received_parts, axis=0)
    return (coadd, jnp.stack(fitted)[None])


def per_device(template, science, plan, orders, coadd_weight, intersection):
    expos = lax.axis_size("expo")
    rows, width = template.shape[1:]
    whole_lanes = width % (expos * LANES) == 0 and rows % 16 == 0
    few = (NU + 1) * expos <= LANES and NU + expos <= LANES
    body = tiled_device if whole_lanes and few else any_device
    return body(template, science, plan, orders, coadd_weight, intersection)


def solution(mesh):
    return jax.shard_map(
        per_device,
        mesh=mesh,
        in_specs=(
            P(("groups", "expo"), "tile", None),
            P(("groups", "expo"), None, "tile", None),
            P("groups"),
            P(),
            P(("groups", "expo"), None),
            P(("groups", "expo"), None),
        ),
        out_specs=(P("groups", "tile", "expo"), P(("groups", "expo"), None, None)),
        check_vma=False,
    )
```

```python
import functools

import jax
import jax.numpy as jnp
import numpy as np
from jax import lax
from jax.experimental import pallas as pl
from jax.experimental.pallas import tpu as pltpu
from jax.sharding import PartitionSpec as P

HALF = 15
NB = 6
NU = 13
LANES = 128
BEYOND = 1000
PAIRS = [(j, k) for j in range(NB) for k in range(j, NB)]

SIGMAS = (0.8, 1.4, 2.2, 3.0, 4.0, 5.5)
RIDGE = 0.05


def power_of(pos, order):
    return jnp.where(order == 0, 1.0, jnp.where(order == 1, pos, pos * pos))


def tap_values(pos, sigma, order):
    value = jnp.exp(-pos * pos / (2.0 * sigma * sigma)) * power_of(pos, order)
    return jnp.where(jnp.abs(pos) <= HALF, value, 0.0)


def tap_norm(sigma, order):
    pos = lax.broadcasted_iota(jnp.int32, (8, LANES), 1).astype(jnp.float32) - HALF
    value = tap_values(pos, sigma, order)
    return jnp.sqrt(jnp.sum(value * value, axis=1, keepdims=True))[:1]


def target(me, shift, size):
    return me ^ shift if size & (size - 1) == 0 else (me + shift) % size


def source(me, shift, size):
    return me ^ shift if size & (size - 1) == 0 else (me - shift + size) % size


def far_first(size):
    return [*range(size // 2, size), *range(1, size // 2), 0] if size > 1 else [0]


def send_kernel(template_ref, science_ref, plan_ref, *refs, step):
    *out_refs, owner_ref, patch_ref, plan_now, sems = refs
    size = len(out_refs)
    rows, wide = out_refs[0].shape
    chunk = (wide - LANES) // 2
    half = size * chunk // 2
    me = lax.axis_index("expo")
    starts = [pl.multiple_of(target(me, shift, size) * chunk, chunk) for shift in range(size)]
    loads = [
        pltpu.make_async_copy(
            template_ref.at[:, pl.ds(i * half, half)], patch_ref.at[:, pl.ds((i * half + LANES), half)], sems.at[i]
        )
        for i in range(2)
    ]
    copies = [
        pltpu.make_async_copy(
            science_ref.at[:, pl.ds(starts[shift], chunk)],
            out_refs[shift].at[:, pl.ds(chunk + LANES, chunk)],
            sems.at[3 + shift],
        )
        for shift in range(size)
    ]
    copies.append(pltpu.make_async_copy(plan_ref, plan_now, sems.at[2]))
    for copy in loads + copies:
        copy.start()
    blank = jnp.zeros((rows, LANES), patch_ref.dtype)
    patch_ref[:, :LANES] = blank
    patch_ref[:, size * chunk + LANES :] = blank
    for copy in loads:
        copy.wait()
    lane = lax.broadcasted_iota(jnp.int32, (rows, LANES), 1)
    for shift in range(size):
        start = starts[shift]
        out_refs[shift][:, :chunk] = patch_ref[:, pl.ds(start + LANES, chunk)]
        before = patch_ref[:, pl.ds(start, LANES)].astype(jnp.float32)
        after = patch_ref[:, pl.ds(start + chunk + LANES, LANES)].astype(jnp.float32)
        rim = jnp.where(lane < LANES // 2, after, before)
        out_refs[shift][:, chunk : chunk + LANES] = rim.astype(patch_ref.dtype)
    for copy in copies:
        copy.wait()
    owner_ref[...] = jnp.full(owner_ref.shape, plan_now[step], jnp.int32)


def pick_kernel(owner_ref, _, *refs):
    *recv_refs, out_ref = refs
    rows, ext = out_ref.shape
    size = len(recv_refs)
    recv_refs = dict(zip(far_first(size), recv_refs))
    me = lax.axis_index("expo")
    blocks = []
    for b in range(ext // LANES):
        columns = slice(b * LANES, (b + 1) * LANES)
        block = recv_refs[0][:, columns].astype(jnp.float32)
        for shift in range(1, size):
            block = jnp.where(
                owner_ref[...] == source(me, shift, size), recv_refs[shift][:, columns].astype(jnp.float32), block
            )
        blocks.append(block.astype(out_ref.dtype))
    whole = jnp.concatenate(blocks[-1:] + blocks, axis=1)
    out_ref[...] = whole[:, LANES - HALF : LANES - HALF + ext]


def column_positions(first_col, block, width):
    col = lax.broadcasted_iota(jnp.int32, (8, LANES), 1) + (first_col + block * LANES)
    return 2.0 * (col.astype(jnp.float32) + 0.5) / width - 1.0


def band_kernel(orders_ref, row_ref, col_ref, *, tiles):
    rows = row_ref.shape[0] // NB
    tile_at = lax.axis_index("tile")
    near = 1 - 2 * lax.rem(tile_at, 2)
    near_move = jnp.where(tile_at + near < tiles, near - 1, BEYOND)
    far_move = jnp.where((tile_at >= near) & (tile_at - near < tiles), -near - 2, BEYOND)
    source = lax.broadcasted_iota(jnp.int32, (rows, 3 * rows), 1)
    moved = jnp.where(source < rows, 0, jnp.where(source < 2 * rows, near_move, far_move))
    offset = (
        source + moved * rows - lax.broadcasted_iota(jnp.int32, (rows, 3 * rows), 0)
    ).astype(jnp.float32)
    shift = (
        lax.broadcasted_iota(jnp.int32, (2 * LANES, LANES), 0)
        - lax.broadcasted_iota(jnp.int32, (2 * LANES, LANES), 1)
        - HALF
    ).astype(jnp.float32)
    for k in range(NB):
        norm = tap_norm(SIGMAS[k], orders_ref[k, 0])
        row_ref[k * rows : (k + 1) * rows] = (
            tap_values(offset, SIGMAS[k], orders_ref[k, 0]) / norm
        ).astype(jnp.bfloat16)
        norm = tap_norm(SIGMAS[k], orders_ref[k, 1])
        col_ref[k] = (tap_values(shift, SIGMAS[k], orders_ref[k, 1]) / norm).astype(jnp.bfloat16)


def fit_kernel(weight_ref, hits_ref, row_band_ref, col_band_ref, own_ref, near_ref, far_ref, *refs, width):
    *image_refs, conv_ref, sums_ref, row_ref, parts_ref = refs
    tile_at = lax.axis_index("tile")
    expo_at = lax.axis_index("expo")
    rows, ext = own_ref.shape
    expos = len(image_refs)
    chunk = ext - LANES
    blocks = chunk // LANES

    patch = jnp.concatenate([own_ref[...], near_ref[...], far_ref[...]], axis=0)
    row_ref[...] = jnp.dot(
        row_band_ref[...], patch, preferred_element_type=jnp.float32
    ).astype(jnp.bfloat16)
    for k in range(NB):
        window = jnp.concatenate(
            [
                row_ref[k * rows : (k + 1) * rows, b * LANES : (b + 2) * LANES]
                for b in range(blocks)
            ],
            axis=0,
        )
        out = jnp.dot(window, col_band_ref[k], preferred_element_type=jnp.float32)
        conv_ref[k] = out.reshape(blocks, rows, LANES)

    first_col = expo_at * chunk
    xs = [column_positions(first_col, b, width) for b in range(blocks)]

    def fold(x):
        total = x[:8]
        for i in range(8, rows, 8):
            total = total + x[i : i + 8]
        return total

    def moments(at, left, right, count):
        total = [None] * count
        for b in range(blocks):
            term = fold(left(b) * right(b)) if right is not None else fold(left(b))
            for i in range(count):
                total[i] = term if total[i] is None else total[i] + term
                if i < count - 1:
                    term = term * xs[b]
        for i in range(count):
            parts_ref[at + i] = total[i]

    def conv(k):
        return lambda b: conv_ref[k, b]

    def sci(shift):
        return lambda b: image_refs[shift][:, ext + b * LANES : ext + (b + 1) * LANES].astype(jnp.float32)

    blank = jnp.zeros((8, LANES), jnp.float32)
    at = 0
    for j, k in PAIRS:
        moments(at, conv(j), conv(k), 3)
        at += 3
    for k in range(NB):
        moments(at, conv(k), None, 2)
        at += 2
    while at % 8:
        parts_ref[at] = blank
        at += 1
    begin = at
    for shift in range(expos):
        row = at + NU * source(expo_at, shift, expos)
        for k in range(NB):
            moments(row + 2 * k, conv(k), sci(shift), 2)
        moments(row + NU - 1, sci(shift), None, 1)
    at += NU * expos
    weight = jnp.broadcast_to(weight_ref[...] * hits_ref[...].astype(jnp.float32), (8, LANES))
    weight = jnp.where(tile_at == 0, weight, 0.0)
    spot = (
        (lax.broadcasted_iota(jnp.int32, (8, LANES), 0) == 0)
        & (lax.broadcasted_iota(jnp.int32, (8, LANES), 1) == 0)
    )
    for e in range(expos):
        parts_ref[at + e] = jnp.where(spot & (expo_at == e), weight, 0.0)
    at += expos
    while at % 8:
        parts_ref[at] = blank
        at += 1
    ones = jnp.ones((8, LANES), jnp.float32)
    rows_of = []
    for first, last in ((0, begin), (begin, at)):
        lanes = jnp.sum(parts_ref[first:last], axis=1)
        spare = LANES - (last - first)
        if spare:
            lanes = jnp.concatenate([lanes, jnp.zeros((spare, LANES), jnp.float32)], axis=0)
        rows_of.append(
            lax.dot_general(
                ones,
                lanes,
                (((1,), (1,)), ((), ())),
                precision=lax.Precision.HIGHEST,
                preferred_element_type=jnp.float32,
            )
        )
    both = jnp.where(lax.broadcasted_iota(jnp.int32, (8, LANES), 0) < 4, rows_of[0], rows_of[1])
    for i in range(sums_ref.shape[0]):
        sums_ref[i] = both


def table(expos):
    columns = np.zeros((NU + expos + 1, 16), np.int32)
    for at, (j, k) in enumerate(PAIRS):
        for a, b in ((j, k), (k, j)):
            columns[b, a] = 3 * at
            columns[NB + b, a] = columns[b, NB + a] = 3 * at + 1
            columns[NB + b, NB + a] = 3 * at + 2
    for k in range(NB):
        for x in range(2):
            columns[NU - 1, x * NB + k] = columns[x * NB + k, NU - 1] = 3 * len(PAIRS) + 2 * k + x
    for e in range(expos):
        columns[NU + e, :NU] = [NU * e + 2 * k + x for x in range(2) for k in range(NB)] + [NU * e + NU - 1]
        columns[NU + expos, e] = NU * expos + e
    return np.ascontiguousarray(np.broadcast_to(columns[:, :, None], columns.shape + (LANES,)))


def solve_kernel(table_ref, sums_ref, conv_ref, *refs, width, pixels):
    *image_refs, coadd_ref, coeffs_ref, tile_ref, sems = refs
    expo_at = lax.axis_index("expo")
    expos = len(image_refs)
    rows, chunk = coadd_ref.shape
    blocks = chunk // LANES
    ext = image_refs[0].shape[1] - chunk
    sub = lax.broadcasted_iota(jnp.int32, (16, LANES), 0)
    lane = lax.broadcasted_iota(jnp.int32, (16, LANES), 1)
    sums = sums_ref[0]
    for i in range(1, sums_ref.shape[0]):
        sums = sums + sums_ref[i]
    first = jnp.broadcast_to(sums[0:1], (16, LANES))
    second = jnp.broadcast_to(sums[4:5], (16, LANES))

    columns = [
        jnp.take_along_axis(first if j < NU else second, table_ref[j], axis=1) for j in range(NU + expos)
    ]
    spread = jnp.take_along_axis(second, table_ref[NU + expos], axis=1)
    weight = [jnp.broadcast_to(spread[e : e + 1], (16, LANES)) for e in range(expos)]
    columns[NU - 1] = jnp.where(sub == NU - 1, float(pixels), columns[NU - 1])

    trace = columns[0][0:1]
    for j in range(1, NU):
        trace = trace + columns[j][j : j + 1]
    scale = 1.0 / trace
    for j in range(NU + expos):
        columns[j] = columns[j] * scale
        if j < NU:
            columns[j] = columns[j] + jnp.where(sub == j, RIDGE / NU, 0.0)
    for i in range(NU):
        inverse = 1.0 / columns[i][i : i + 1]
        for j in range(i + 1, NU + expos):
            factor = columns[j][i : i + 1] * inverse
            columns[j] = jnp.where(sub == i, factor, columns[j] - columns[i] * factor)

    solved = columns[NU:]
    own = solved[0]
    mixed = weight[0] * solved[0]
    for e in range(1, expos):
        own = jnp.where(expo_at == e, solved[e], own)
        mixed = mixed + weight[e] * solved[e]
    diagonal = (sub == lane) & (sub < NU)
    coeffs_ref[...] = jnp.sum(jnp.where(diagonal, own, 0.0), axis=0, keepdims=True)[:, :NU]
    scale = [jnp.broadcast_to(mixed[u : u + 1], (8, LANES)) for u in range(NU)]
    gains = []
    for shift in range(expos):
        gain = weight[0][:8]
        for e in range(1, expos):
            gain = jnp.where(source(expo_at, shift, expos) == e, weight[e][:8], gain)
        gains.append(gain)
    first_col = expo_at * chunk
    copies = []
    for r in range(0, rows, 8):
        for b in range(blocks):
            at = slice(ext + b * LANES, ext + (b + 1) * LANES)
            x = column_positions(first_col, b, width)
            total = -scale[NU - 1]
            for gain, image_ref in zip(gains, image_refs):
                total = total + gain * image_ref[:, at].astype(jnp.float32)[r : r + 8]
            model = (scale[0] + scale[NB] * x) * conv_ref[0, b, r : r + 8]
            for k in range(1, NB):
                model = model + (scale[k] + scale[NB + k] * x) * conv_ref[k, b, r : r + 8]
            tile_ref[r : r + 8, b * LANES : (b + 1) * LANES] = total - model
        copies.append(
            pltpu.make_async_copy(tile_ref.at[pl.ds(r, 8)], coadd_ref.at[pl.ds(r, 8)], sems.at[r // 8])
        )
        copies[-1].start()
    for copy in copies:
        copy.wait()


def swaps(first, size):
    pairs = [(i, i + 1) for i in range(first, size - 1, 2)]
    if first and size % 2 == 0:
        pairs.append((0, size - 1))
    return [pair for a, b in pairs for pair in ((a, b), (b, a))]


def tiled_device(template, science, plan, orders, coadd_weight, intersection):
    expos = lax.axis_size("expo")
    tiles = lax.axis_size("tile")
    _, rows, width = template.shape
    steps = science.shape[1]
    chunk = width // expos
    ext = chunk + LANES
    blocks = chunk // LANES
    smem = pl.BlockSpec(memory_space=pltpu.SMEM)
    vmem = pl.BlockSpec(memory_space=pltpu.VMEM)
    small = pltpu.CompilerParams(vmem_limit_bytes=16 * 1024 * 1024)
    hbm = pl.BlockSpec(memory_space=pltpu.HBM)
    row_band, col_band = pl.pallas_call(
        functools.partial(band_kernel, tiles=tiles),
        out_shape=(
            jax.ShapeDtypeStruct((NB * rows, 3 * rows), jnp.bfloat16),
            jax.ShapeDtypeStruct((NB, 2 * LANES, LANES), jnp.bfloat16),
        ),
        in_specs=[smem],
        out_specs=(vmem, vmem),
        compiler_params=small,
        cost_estimate=pl.CostEstimate(flops=4_000_000, bytes_accessed=500_000, transcendentals=200_000),
    )(orders)
    coadds = []
    fitted = []
    for step in range(steps):
        *images, owner = pl.pallas_call(
            functools.partial(send_kernel, step=step),
            out_shape=(pltpu.VMEM((rows, ext + chunk), template.dtype),) * expos
            + (jax.ShapeDtypeStruct((rows, LANES), jnp.int32),),
            in_specs=[hbm] * 3,
            out_specs=(vmem,) * (expos + 1),
            scratch_shapes=[
                pltpu.VMEM((rows, width + 2 * LANES), template.dtype),
                pltpu.SMEM(plan.shape, jnp.int32),
                pltpu.SemaphoreType.DMA((expos + 3,)),
            ],
            compiler_params=small,
        )(
            pltpu.with_memory_space_constraint(template[0], pltpu.HBM),
            pltpu.with_memory_space_constraint(science[0, step], pltpu.HBM),
            pltpu.with_memory_space_constraint(plan, pltpu.HBM),
        )
        for shift in range(1, expos):
            pairs = [(e, int(target(e, shift, expos))) for e in range(expos)]
            images[shift] = lax.ppermute(images[shift], "expo", pairs)
        own = pl.pallas_call(
            pick_kernel,
            out_shape=jax.ShapeDtypeStruct((rows, ext), template.dtype),
            in_specs=[vmem, pl.BlockSpec(memory_space=pl.ANY)] + [vmem] * expos,
            out_specs=vmem,
            compiler_params=small,
        )(owner, row_band, *(images[shift] for shift in far_first(expos)))
        far = lax.ppermute(own, "tile", swaps(1, tiles))
        near = lax.ppermute(own, "tile", swaps(0, tiles))
        conv, sums = pl.pallas_call(
            functools.partial(fit_kernel, width=width),
            out_shape=(
                jax.ShapeDtypeStruct((NB, blocks, rows, LANES), jnp.float32),
                jax.ShapeDtypeStruct((tiles * expos, 8, LANES), jnp.float32),
            ),
            in_specs=[vmem] * (7 + expos),
            out_specs=(vmem, vmem),
            scratch_shapes=[
                pltpu.VMEM((NB * rows, ext), jnp.bfloat16),
                pltpu.VMEM((80 + 14 * expos + 8, 8, LANES), jnp.float32),
            ],
            compiler_params=small,
        )(
            coadd_weight[:, step : step + 1],
            intersection[:, step : step + 1],
            row_band,
            col_band,
            own,
            near,
            far,
            *images,
        )
        sums = lax.all_to_all(sums, ("tile", "expo"), split_axis=0, concat_axis=0, tiled=True)
        coadd, coeffs = pl.pallas_call(
            functools.partial(solve_kernel, width=width, pixels=tiles * rows * width),
            out_shape=(
                jax.ShapeDtypeStruct((rows, chunk), jnp.float32),
                jax.ShapeDtypeStruct((1, NU), jnp.float32),
            ),
            in_specs=[vmem] * (3 + expos),
            out_specs=(pl.BlockSpec(memory_space=pl.ANY), vmem),
            scratch_shapes=[
                pltpu.VMEM((rows, chunk), jnp.float32),
                pltpu.SemaphoreType.DMA((rows // 8,)),
            ],
            compiler_params=small,
        )(jnp.asarray(table(expos)), sums, conv, *images)
        coadds.append(coadd[None])
        fitted.append(coeffs)
    return (jnp.concatenate(coadds), jnp.stack(fitted, axis=1))


def broadcast(block, axis, holder):
    block = jnp.where(lax.axis_index(axis) == holder, block, jnp.zeros_like(block))
    return lax.psum(block, axis)


def extended(x, sides, width):
    for axis, dim in sides:
        size, length = (lax.axis_size(axis), x.shape[dim])
        up = [(i, (i + 1) % size) for i in range(size - 1)]
        down = [(j, i) for i, j in up]
        last = lax.slice_in_dim(x, length - width, length, axis=dim)
        first = lax.slice_in_dim(x, 0, width, axis=dim)
        before = lax.ppermute(last, axis, up)
        after = lax.ppermute(first, axis, down)
        x = jnp.concatenate([before, x, after], axis=dim)
    return x


def make_filters(orders):
    taps_pos = jnp.arange(2 * HALF + 1).astype(jnp.float32) - HALF
    row_list = []
    col_list = []
    for basis in range(NB):
        sigma = SIGMAS[basis]
        envelope = jnp.exp(-taps_pos * taps_pos / (2.0 * sigma * sigma))
        row_filter = envelope * power_of(taps_pos, orders[basis, 0])
        col_filter = envelope * power_of(taps_pos, orders[basis, 1])
        row_list.append(row_filter / jnp.sqrt(jnp.sum(row_filter * row_filter)))
        col_list.append(col_filter / jnp.sqrt(jnp.sum(col_filter * col_filter)))
    return (jnp.stack(row_list).astype(jnp.bfloat16), jnp.stack(col_list).astype(jnp.bfloat16))


def band_matrix(filters, out_len, in_len):
    offset = jnp.arange(in_len)[None, :] - jnp.arange(out_len)[:, None]
    taps_idx = jnp.arange(2 * HALF + 1)
    picks = (offset[:, :, None] == taps_idx[None, None, :]).astype(jnp.float32)
    band = jnp.einsum("ijt,kt->kij", picks, filters.astype(jnp.float32))
    return band.astype(jnp.bfloat16)


def any_device(template, science, plan, orders, coadd_weight, intersection):
    row_filters, col_filters = make_filters(orders)
    rows = template.shape[1]
    width = template.shape[2]
    blocks_count = width // 128
    steps_count = science.shape[1]
    row_band = band_matrix(row_filters, rows, rows + 2 * HALF)
    col_band = jnp.transpose(band_matrix(col_filters, 128, 128 + 2 * HALF), (0, 2, 1))
    column_pos = 2.0 * (jnp.arange(width).astype(jnp.float32) + 0.5) / width - 1.0
    pieces = []
    fitted = []
    for step in range(steps_count):
        received = broadcast(template[0], "expo", plan[step])
        padded = extended(received, (("tile", 0),), HALF)
        rowconv = jnp.einsum(
            "kij,jw->kiw", row_band, padded, preferred_element_type=jnp.float32
        ).astype(jnp.bfloat16)
        blocks = rowconv.reshape(NB, rows, blocks_count, 128)
        empty_rim = jnp.zeros((NB, rows, 1, HALF), jnp.bfloat16)
        previous = jnp.concatenate([empty_rim, blocks[:, :, :-1, 128 - HALF :]], axis=2)
        following = jnp.concatenate([blocks[:, :, 1:, :HALF], empty_rim], axis=2)
        window = jnp.concatenate([previous, blocks, following], axis=3)
        conv = jnp.einsum("krbj,kjc->krbc", window, col_band, preferred_element_type=jnp.float32)
        conv = conv.reshape(NB, rows, width)
        fields = jnp.concatenate(
            [conv, conv * column_pos, jnp.ones((1, rows, width), jnp.float32)], axis=0
        )
        fields = fields.reshape(NU, rows * width)
        exposure_image = science[0, step].astype(jnp.float32).reshape(rows * width)
        normal_local = jnp.dot(fields, fields.T, precision=lax.Precision.HIGHEST)
        project_local = jnp.dot(fields, exposure_image, precision=lax.Precision.HIGHEST)
        normal_matrix, projections = lax.psum((normal_local, project_local), "tile")
        normal_matrix = normal_matrix + RIDGE * (jnp.trace(normal_matrix) / NU) * jnp.eye(
            NU, dtype=jnp.float32
        )
        factor = jnp.linalg.cholesky(normal_matrix)
        coeffs = jax.scipy.linalg.cho_solve((factor, True), projections)
        model = jnp.dot(coeffs, fields, precision=lax.Precision.HIGHEST)
        difference = exposure_image - model
        weight_now = coadd_weight[0, step] * intersection[0, step].astype(jnp.float32)
        pieces.append((weight_now * difference).reshape(rows, width))
        fitted.append(coeffs)
    weighted = jnp.stack(pieces)
    received_parts = lax.all_to_all(weighted[None], "expo", split_axis=3, concat_axis=0, tiled=True)
    coadd = jnp.sum(received_parts, axis=0)
    return (coadd, jnp.stack(fitted)[None])


def per_device(template, science, plan, orders, coadd_weight, intersection):
    expos = lax.axis_size("expo")
    rows, width = template.shape[1:]
    whole_lanes = width % (expos * LANES) == 0 and rows % 16 == 0
    few = (NU + 1) * expos <= LANES and NU + expos <= LANES
    body = tiled_device if whole_lanes and few else any_device
    return body(template, science, plan, orders, coadd_weight, intersection)


def solution(mesh):
    return jax.shard_map(
        per_device,
        mesh=mesh,
        in_specs=(
            P(("groups", "expo"), "tile", None),
            P(("groups", "expo"), None, "tile", None),
            P("groups"),
            P(),
            P(("groups", "expo"), None),
            P(("groups", "expo"), None),
        ),
        out_specs=(P("groups", "tile", "expo"), P(("groups", "expo"), None, None)),
        check_vma=False,
    )
```

```python
import functools

import jax
import jax.numpy as jnp
import numpy as np
from jax import lax
from jax.experimental import pallas as pl
from jax.experimental.pallas import tpu as pltpu
from jax.sharding import PartitionSpec as P

HALF = 15
NB = 6
NU = 13
LANES = 128
BEYOND = 1000
PAIRS = [(j, k) for j in range(NB) for k in range(j, NB)]

SIGMAS = (0.8, 1.4, 2.2, 3.0, 4.0, 5.5)
RIDGE = 0.05


def power_of(pos, order):
    return jnp.where(order == 0, 1.0, jnp.where(order == 1, pos, pos * pos))


def tap_values(pos, sigma, order):
    value = jnp.exp(-pos * pos / (2.0 * sigma * sigma)) * power_of(pos, order)
    return jnp.where(jnp.abs(pos) <= HALF, value, 0.0)


def tap_norm(sigma, order):
    pos = lax.broadcasted_iota(jnp.int32, (8, LANES), 1).astype(jnp.float32) - HALF
    value = tap_values(pos, sigma, order)
    return jnp.sqrt(jnp.sum(value * value, axis=1, keepdims=True))[:1]


def target(me, shift, size):
    return me ^ shift if size & (size - 1) == 0 else (me + shift) % size


def source(me, shift, size):
    return me ^ shift if size & (size - 1) == 0 else (me - shift + size) % size


def far_first(size):
    return [*range(size // 2, size), *range(1, size // 2), 0] if size > 1 else [0]


def joint(shift, size):
    return shift < size // 2


def send_kernel(template_ref, science_ref, plan_ref, *refs, step):
    *out_refs, owner_ref, patch_ref, plan_now, sems = refs
    rows, width = science_ref.shape
    me = lax.axis_index("expo")
    size = sems.shape[0] - 3
    chunk = width // size
    half = width // 2
    starts = [pl.multiple_of(target(me, shift, size) * chunk, chunk) for shift in range(size)]
    patch_refs, image_refs = [], []
    for shift in range(size):
        patch_refs.append(out_refs.pop(0))
        if joint(shift, size):
            image_refs.append(patch_refs[shift].at[:, pl.ds(chunk + LANES, chunk)])
        else:
            image_refs.append(out_refs.pop(0))
    loads = [
        pltpu.make_async_copy(
            template_ref.at[:, pl.ds(i * half, half)], patch_ref.at[:, pl.ds((i * half + LANES), half)], sems.at[i]
        )
        for i in range(2)
    ]
    copies = [
        pltpu.make_async_copy(
            science_ref.at[:, pl.ds(starts[shift], chunk)], image_refs[shift], sems.at[3 + shift]
        )
        for shift in range(size)
    ]
    copies.append(pltpu.make_async_copy(plan_ref, plan_now, sems.at[2]))
    for copy in loads + copies:
        copy.start()
    blank = jnp.zeros((rows, LANES), patch_ref.dtype)
    patch_ref[:, :LANES] = blank
    patch_ref[:, width + LANES :] = blank
    for copy in loads:
        copy.wait()
    lane = lax.broadcasted_iota(jnp.int32, (rows, LANES), 1)
    for shift in range(size):
        start = starts[shift]
        patch_refs[shift][:, :chunk] = patch_ref[:, pl.ds(start + LANES, chunk)]
        before = patch_ref[:, pl.ds(start, LANES)].astype(jnp.float32)
        after = patch_ref[:, pl.ds(start + chunk + LANES, LANES)].astype(jnp.float32)
        rim = jnp.where(lane < LANES // 2, after, before)
        patch_refs[shift][:, chunk : chunk + LANES] = rim.astype(patch_ref.dtype)
    for copy in copies:
        copy.wait()
    owner_ref[...] = jnp.full(owner_ref.shape, plan_now[step], jnp.int32)


def pick_kernel(owner_ref, _, *refs):
    *recv_refs, out_ref = refs
    rows, ext = out_ref.shape
    size = len(recv_refs)
    recv_refs = dict(zip(far_first(size), recv_refs))
    me = lax.axis_index("expo")
    blocks = []
    for b in range(ext // LANES):
        columns = slice(b * LANES, (b + 1) * LANES)
        block = recv_refs[0][:, columns].astype(jnp.float32)
        for shift in range(1, size):
            block = jnp.where(
                owner_ref[...] == source(me, shift, size), recv_refs[shift][:, columns].astype(jnp.float32), block
            )
        blocks.append(block.astype(out_ref.dtype))
    whole = jnp.concatenate(blocks[-1:] + blocks, axis=1)
    out_ref[...] = whole[:, LANES - HALF : LANES - HALF + ext]


def column_positions(first_col, block, width):
    col = lax.broadcasted_iota(jnp.int32, (8, LANES), 1) + (first_col + block * LANES)
    return 2.0 * (col.astype(jnp.float32) + 0.5) / width - 1.0


def band_kernel(orders_ref, row_ref, col_ref, *, tiles):
    rows = row_ref.shape[0] // NB
    tile_at = lax.axis_index("tile")
    near = 1 - 2 * lax.rem(tile_at, 2)
    near_move = jnp.where(tile_at + near < tiles, near - 1, BEYOND)
    far_move = jnp.where((tile_at >= near) & (tile_at - near < tiles), -near - 2, BEYOND)
    source = lax.broadcasted_iota(jnp.int32, (rows, 3 * rows), 1)
    moved = jnp.where(source < rows, 0, jnp.where(source < 2 * rows, near_move, far_move))
    offset = (
        source + moved * rows - lax.broadcasted_iota(jnp.int32, (rows, 3 * rows), 0)
    ).astype(jnp.float32)
    shift = (
        lax.broadcasted_iota(jnp.int32, (2 * LANES, LANES), 0)
        - lax.broadcasted_iota(jnp.int32, (2 * LANES, LANES), 1)
        - HALF
    ).astype(jnp.float32)
    for k in range(NB):
        norm = tap_norm(SIGMAS[k], orders_ref[k, 0])
        row_ref[k * rows : (k + 1) * rows] = (
            tap_values(offset, SIGMAS[k], orders_ref[k, 0]) / norm
        ).astype(jnp.bfloat16)
        norm = tap_norm(SIGMAS[k], orders_ref[k, 1])
        col_ref[k] = (tap_values(shift, SIGMAS[k], orders_ref[k, 1]) / norm).astype(jnp.bfloat16)


def image_blocks(image_refs, chunk):
    def reader(ref):
        first = ref.shape[1] - chunk
        return lambda b: ref[:, first + b * LANES : first + (b + 1) * LANES].astype(jnp.float32)

    return [reader(ref) for ref in image_refs]


def fold(x):
    total = x[:8]
    for i in range(8, x.shape[0], 8):
        total = total + x[i : i + 8]
    return total


def moments(parts_ref, at, left, right, xs, count):
    total = [None] * count
    for b in range(len(xs)):
        term = fold(left(b) * right(b)) if right is not None else fold(left(b))
        for i in range(count):
            total[i] = term if total[i] is None else total[i] + term
            if i < count - 1:
                term = term * xs[b]
    for i in range(count):
        parts_ref[at + i] = total[i]


def row_of_sums(parts_ref, count):
    blank = jnp.zeros((8, LANES), jnp.float32)
    while count % 8:
        parts_ref[count] = blank
        count += 1
    lanes = jnp.sum(parts_ref[:count], axis=1)
    if count < LANES:
        lanes = jnp.concatenate([lanes, jnp.zeros((LANES - count, LANES), jnp.float32)], axis=0)
    return lax.dot_general(
        jnp.ones((8, LANES), jnp.float32),
        lanes,
        (((1,), (1,)), ((), ())),
        precision=lax.Precision.HIGHEST,
        preferred_element_type=jnp.float32,
    )


def fields_kernel(row_band_ref, col_band_ref, own_ref, far_ref, near_ref, conv_ref, sums_ref, row_ref,
                  parts_ref, *, width):
    rows, ext = own_ref.shape
    chunk = ext - LANES
    blocks = chunk // LANES
    patch = jnp.concatenate([own_ref[...], near_ref[...], far_ref[...]], axis=0)
    row_ref[...] = jnp.dot(
        row_band_ref[...], patch, preferred_element_type=jnp.float32
    ).astype(jnp.bfloat16)
    for k in range(NB):
        window = jnp.concatenate(
            [
                row_ref[k * rows : (k + 1) * rows, b * LANES : (b + 2) * LANES]
                for b in range(blocks)
            ],
            axis=0,
        )
        out = jnp.dot(window, col_band_ref[k], preferred_element_type=jnp.float32)
        conv_ref[k] = out.reshape(blocks, rows, LANES)

    first_col = lax.axis_index("expo") * chunk
    xs = [column_positions(first_col, b, width) for b in range(blocks)]

    def conv(k):
        return lambda b: conv_ref[k, b]

    at = 0
    for j, k in PAIRS:
        moments(parts_ref, at, conv(j), conv(k), xs, 3)
        at += 3
    for k in range(NB):
        moments(parts_ref, at, conv(k), None, xs, 2)
        at += 2
    sums_ref[...] = row_of_sums(parts_ref, at)


def project_kernel(weight_ref, hits_ref, normal_ref, conv_ref, *refs, width):
    *image_refs, sums_ref, parts_ref = refs
    tile_at = lax.axis_index("tile")
    expo_at = lax.axis_index("expo")
    expos = len(image_refs)
    blocks = conv_ref.shape[1]
    chunk = blocks * LANES
    xs = [column_positions(expo_at * chunk, b, width) for b in range(blocks)]
    images = image_blocks(image_refs, chunk)

    def conv(k):
        return lambda b: conv_ref[k, b]

    for shift in range(expos):
        row = NU * source(expo_at, shift, expos)
        for k in range(NB):
            moments(parts_ref, row + 2 * k, conv(k), images[shift], xs, 2)
        moments(parts_ref, row + NU - 1, images[shift], None, xs, 1)
    weight = jnp.broadcast_to(weight_ref[...] * hits_ref[...].astype(jnp.float32), (8, LANES))
    weight = jnp.where(tile_at == 0, weight, 0.0)
    sub = lax.broadcasted_iota(jnp.int32, (8, LANES), 0)
    spot = (sub == 0) & (lax.broadcasted_iota(jnp.int32, (8, LANES), 1) == 0)
    for e in range(expos):
        parts_ref[NU * expos + e] = jnp.where(spot & (expo_at == e), weight, 0.0)
    both = jnp.where(sub < 4, normal_ref[...], row_of_sums(parts_ref, (NU + 1) * expos))
    for i in range(sums_ref.shape[0]):
        sums_ref[i] = both


def table(expos):
    columns = np.zeros((NU + expos + 1, 16), np.int32)
    for at, (j, k) in enumerate(PAIRS):
        for a, b in ((j, k), (k, j)):
            columns[b, a] = 3 * at
            columns[NB + b, a] = columns[b, NB + a] = 3 * at + 1
            columns[NB + b, NB + a] = 3 * at + 2
    for k in range(NB):
        for x in range(2):
            columns[NU - 1, x * NB + k] = columns[x * NB + k, NU - 1] = 3 * len(PAIRS) + 2 * k + x
    for e in range(expos):
        columns[NU + e, :NU] = [NU * e + 2 * k + x for x in range(2) for k in range(NB)] + [NU * e + NU - 1]
        columns[NU + expos, e] = NU * expos + e
    return np.ascontiguousarray(np.broadcast_to(columns[:, :, None], columns.shape + (LANES,)))


def solve_kernel(table_ref, sums_ref, conv_ref, *refs, width, pixels):
    *image_refs, coadd_ref, coeffs_ref, tile_ref, sems = refs
    expo_at = lax.axis_index("expo")
    expos = len(image_refs)
    rows, chunk = coadd_ref.shape
    blocks = chunk // LANES
    images = image_blocks(image_refs, chunk)
    sub = lax.broadcasted_iota(jnp.int32, (16, LANES), 0)
    lane = lax.broadcasted_iota(jnp.int32, (16, LANES), 1)
    sums = sums_ref[0]
    for i in range(1, sums_ref.shape[0]):
        sums = sums + sums_ref[i]
    first = jnp.broadcast_to(sums[0:1], (16, LANES))
    second = jnp.broadcast_to(sums[4:5], (16, LANES))

    columns = [
        jnp.take_along_axis(first if j < NU else second, table_ref[j], axis=1) for j in range(NU + expos)
    ]
    spread = jnp.take_along_axis(second, table_ref[NU + expos], axis=1)
    weight = [jnp.broadcast_to(spread[e : e + 1], (16, LANES)) for e in range(expos)]
    columns[NU - 1] = jnp.where(sub == NU - 1, float(pixels), columns[NU - 1])

    trace = columns[0][0:1]
    for j in range(1, NU):
        trace = trace + columns[j][j : j + 1]
    scale = 1.0 / trace
    for j in range(NU + expos):
        columns[j] = columns[j] * scale
        if j < NU:
            columns[j] = columns[j] + jnp.where(sub == j, RIDGE / NU, 0.0)
    for i in range(NU):
        inverse = 1.0 / columns[i][i : i + 1]
        for j in range(i + 1, NU + expos):
            factor = columns[j][i : i + 1] * inverse
            columns[j] = jnp.where(sub == i, factor, columns[j] - columns[i] * factor)

    solved = columns[NU:]
    own = solved[0]
    mixed = weight[0] * solved[0]
    for e in range(1, expos):
        own = jnp.where(expo_at == e, solved[e], own)
        mixed = mixed + weight[e] * solved[e]
    diagonal = (sub == lane) & (sub < NU)
    coeffs_ref[...] = jnp.sum(jnp.where(diagonal, own, 0.0), axis=0, keepdims=True)[:, :NU]
    scale = [jnp.broadcast_to(mixed[u : u + 1], (8, LANES)) for u in range(NU)]
    gains = []
    for shift in range(expos):
        gain = weight[0][:8]
        for e in range(1, expos):
            gain = jnp.where(source(expo_at, shift, expos) == e, weight[e][:8], gain)
        gains.append(gain)
    first_col = expo_at * chunk
    copies = []
    for r in range(0, rows, 8):
        for b in range(blocks):
            x = column_positions(first_col, b, width)
            total = -scale[NU - 1]
            for gain, image in zip(gains, images):
                total = total + gain * image(b)[r : r + 8]
            model = (scale[0] + scale[NB] * x) * conv_ref[0, b, r : r + 8]
            for k in range(1, NB):
                model = model + (scale[k] + scale[NB + k] * x) * conv_ref[k, b, r : r + 8]
            tile_ref[r : r + 8, b * LANES : (b + 1) * LANES] = total - model
        copies.append(
            pltpu.make_async_copy(tile_ref.at[pl.ds(r, 8)], coadd_ref.at[pl.ds(r, 8)], sems.at[r // 8])
        )
        copies[-1].start()
    for copy in copies:
        copy.wait()


def swaps(first, size):
    pairs = [(i, i + 1) for i in range(first, size - 1, 2)]
    if first and size % 2 == 0:
        pairs.append((0, size - 1))
    return [pair for a, b in pairs for pair in ((a, b), (b, a))]


def tiled_device(template, science, plan, orders, coadd_weight, intersection):
    expos = lax.axis_size("expo")
    tiles = lax.axis_size("tile")
    _, rows, width = template.shape
    steps = science.shape[1]
    chunk = width // expos
    ext = chunk + LANES
    blocks = chunk // LANES
    smem = pl.BlockSpec(memory_space=pltpu.SMEM)
    vmem = pl.BlockSpec(memory_space=pltpu.VMEM)
    small = pltpu.CompilerParams(vmem_limit_bytes=16 * 1024 * 1024)
    hbm = pl.BlockSpec(memory_space=pltpu.HBM)
    row_band, col_band = pl.pallas_call(
        functools.partial(band_kernel, tiles=tiles),
        out_shape=(
            jax.ShapeDtypeStruct((NB * rows, 3 * rows), jnp.bfloat16),
            jax.ShapeDtypeStruct((NB, 2 * LANES, LANES), jnp.bfloat16),
        ),
        in_specs=[smem],
        out_specs=(vmem, vmem),
        compiler_params=small,
        cost_estimate=pl.CostEstimate(flops=4_000_000, bytes_accessed=500_000, transcendentals=200_000),
    )(orders)
    coadds = []
    fitted = []
    for step in range(steps):
        wides = []
        for shift in range(expos):
            wides += [ext + chunk] if joint(shift, expos) else [ext, chunk]
        *blocks_out, owner = pl.pallas_call(
            functools.partial(send_kernel, step=step),
            out_shape=tuple(pltpu.VMEM((rows, wide), template.dtype) for wide in wides)
            + (jax.ShapeDtypeStruct((rows, LANES), jnp.int32),),
            in_specs=[hbm] * 3,
            out_specs=(vmem,) * (len(wides) + 1),
            scratch_shapes=[
                pltpu.VMEM((rows, width + 2 * LANES), template.dtype),
                pltpu.SMEM(plan.shape, jnp.int32),
                pltpu.SemaphoreType.DMA((expos + 3,)),
            ],
            compiler_params=small,
        )(
            pltpu.with_memory_space_constraint(template[0], pltpu.HBM),
            pltpu.with_memory_space_constraint(science[0, step], pltpu.HBM),
            pltpu.with_memory_space_constraint(plan, pltpu.HBM),
        )
        patches, images = [], []
        for shift in range(expos):
            pairs = [(e, int(target(e, shift, expos))) for e in range(expos)]
            for group in (patches,) if joint(shift, expos) else (patches, images):
                block = blocks_out.pop(0)
                group.append(lax.ppermute(block, "expo", pairs) if shift else block)
            if joint(shift, expos):
                images.append(patches[-1])
        own = pl.pallas_call(
            pick_kernel,
            out_shape=jax.ShapeDtypeStruct((rows, ext), template.dtype),
            in_specs=[vmem, pl.BlockSpec(memory_space=pl.ANY)] + [vmem] * expos,
            out_specs=vmem,
            compiler_params=small,
        )(owner, row_band, *(patches[shift] for shift in far_first(expos)))
        far = lax.ppermute(own, "tile", swaps(1, tiles))
        near = lax.ppermute(own, "tile", swaps(0, tiles))
        conv, normal = pl.pallas_call(
            functools.partial(fields_kernel, width=width),
            out_shape=(
                jax.ShapeDtypeStruct((NB, blocks, rows, LANES), jnp.float32),
                jax.ShapeDtypeStruct((8, LANES), jnp.float32),
            ),
            in_specs=[vmem] * 5,
            out_specs=(vmem, vmem),
            scratch_shapes=[
                pltpu.VMEM((NB * rows, ext), jnp.bfloat16),
                pltpu.VMEM((LANES, 8, LANES), jnp.float32),
            ],
            compiler_params=small,
        )(row_band, col_band, own, far, near)
        sums = pl.pallas_call(
            functools.partial(project_kernel, width=width),
            out_shape=jax.ShapeDtypeStruct((tiles * expos, 8, LANES), jnp.float32),
            in_specs=[vmem] * (4 + expos),
            out_specs=vmem,
            scratch_shapes=[pltpu.VMEM((LANES, 8, LANES), jnp.float32)],
            compiler_params=small,
        )(
            coadd_weight[:, step : step + 1],
            intersection[:, step : step + 1],
            normal,
            conv,
            *images,
        )
        sums = lax.all_to_all(sums, ("tile", "expo"), split_axis=0, concat_axis=0, tiled=True)
        coadd, coeffs = pl.pallas_call(
            functools.partial(solve_kernel, width=width, pixels=tiles * rows * width),
            out_shape=(
                jax.ShapeDtypeStruct((rows, chunk), jnp.float32),
                jax.ShapeDtypeStruct((1, NU), jnp.float32),
            ),
            in_specs=[vmem] * (3 + expos),
            out_specs=(pl.BlockSpec(memory_space=pl.ANY), vmem),
            scratch_shapes=[
                pltpu.VMEM((rows, chunk), jnp.float32),
                pltpu.SemaphoreType.DMA((rows // 8,)),
            ],
            compiler_params=small,
        )(jnp.asarray(table(expos)), sums, conv, *images)
        coadds.append(coadd[None])
        fitted.append(coeffs)
    return (jnp.concatenate(coadds), jnp.stack(fitted, axis=1))


def broadcast(block, axis, holder):
    block = jnp.where(lax.axis_index(axis) == holder, block, jnp.zeros_like(block))
    return lax.psum(block, axis)


def extended(x, sides, width):
    for axis, dim in sides:
        size, length = (lax.axis_size(axis), x.shape[dim])
        up = [(i, (i + 1) % size) for i in range(size - 1)]
        down = [(j, i) for i, j in up]
        last = lax.slice_in_dim(x, length - width, length, axis=dim)
        first = lax.slice_in_dim(x, 0, width, axis=dim)
        before = lax.ppermute(last, axis, up)
        after = lax.ppermute(first, axis, down)
        x = jnp.concatenate([before, x, after], axis=dim)
    return x


def make_filters(orders):
    taps_pos = jnp.arange(2 * HALF + 1).astype(jnp.float32) - HALF
    row_list = []
    col_list = []
    for basis in range(NB):
        sigma = SIGMAS[basis]
        envelope = jnp.exp(-taps_pos * taps_pos / (2.0 * sigma * sigma))
        row_filter = envelope * power_of(taps_pos, orders[basis, 0])
        col_filter = envelope * power_of(taps_pos, orders[basis, 1])
        row_list.append(row_filter / jnp.sqrt(jnp.sum(row_filter * row_filter)))
        col_list.append(col_filter / jnp.sqrt(jnp.sum(col_filter * col_filter)))
    return (jnp.stack(row_list).astype(jnp.bfloat16), jnp.stack(col_list).astype(jnp.bfloat16))


def band_matrix(filters, out_len, in_len):
    offset = jnp.arange(in_len)[None, :] - jnp.arange(out_len)[:, None]
    taps_idx = jnp.arange(2 * HALF + 1)
    picks = (offset[:, :, None] == taps_idx[None, None, :]).astype(jnp.float32)
    band = jnp.einsum("ijt,kt->kij", picks, filters.astype(jnp.float32))
    return band.astype(jnp.bfloat16)


def any_device(template, science, plan, orders, coadd_weight, intersection):
    row_filters, col_filters = make_filters(orders)
    rows = template.shape[1]
    width = template.shape[2]
    blocks_count = width // 128
    steps_count = science.shape[1]
    row_band = band_matrix(row_filters, rows, rows + 2 * HALF)
    col_band = jnp.transpose(band_matrix(col_filters, 128, 128 + 2 * HALF), (0, 2, 1))
    column_pos = 2.0 * (jnp.arange(width).astype(jnp.float32) + 0.5) / width - 1.0
    pieces = []
    fitted = []
    for step in range(steps_count):
        received = broadcast(template[0], "expo", plan[step])
        padded = extended(received, (("tile", 0),), HALF)
        rowconv = jnp.einsum(
            "kij,jw->kiw", row_band, padded, preferred_element_type=jnp.float32
        ).astype(jnp.bfloat16)
        blocks = rowconv.reshape(NB, rows, blocks_count, 128)
        empty_rim = jnp.zeros((NB, rows, 1, HALF), jnp.bfloat16)
        previous = jnp.concatenate([empty_rim, blocks[:, :, :-1, 128 - HALF :]], axis=2)
        following = jnp.concatenate([blocks[:, :, 1:, :HALF], empty_rim], axis=2)
        window = jnp.concatenate([previous, blocks, following], axis=3)
        conv = jnp.einsum("krbj,kjc->krbc", window, col_band, preferred_element_type=jnp.float32)
        conv = conv.reshape(NB, rows, width)
        fields = jnp.concatenate(
            [conv, conv * column_pos, jnp.ones((1, rows, width), jnp.float32)], axis=0
        )
        fields = fields.reshape(NU, rows * width)
        exposure_image = science[0, step].astype(jnp.float32).reshape(rows * width)
        normal_local = jnp.dot(fields, fields.T, precision=lax.Precision.HIGHEST)
        project_local = jnp.dot(fields, exposure_image, precision=lax.Precision.HIGHEST)
        normal_matrix, projections = lax.psum((normal_local, project_local), "tile")
        normal_matrix = normal_matrix + RIDGE * (jnp.trace(normal_matrix) / NU) * jnp.eye(
            NU, dtype=jnp.float32
        )
        factor = jnp.linalg.cholesky(normal_matrix)
        coeffs = jax.scipy.linalg.cho_solve((factor, True), projections)
        model = jnp.dot(coeffs, fields, precision=lax.Precision.HIGHEST)
        difference = exposure_image - model
        weight_now = coadd_weight[0, step] * intersection[0, step].astype(jnp.float32)
        pieces.append((weight_now * difference).reshape(rows, width))
        fitted.append(coeffs)
    weighted = jnp.stack(pieces)
    received_parts = lax.all_to_all(weighted[None], "expo", split_axis=3, concat_axis=0, tiled=True)
    coadd = jnp.sum(received_parts, axis=0)
    return (coadd, jnp.stack(fitted)[None])


def per_device(template, science, plan, orders, coadd_weight, intersection):
    expos = lax.axis_size("expo")
    rows, width = template.shape[1:]
    whole_lanes = width % (expos * LANES) == 0 and rows % 16 == 0
    few = (NU + 1) * expos <= LANES and NU + expos <= LANES
    body = tiled_device if whole_lanes and few else any_device
    return body(template, science, plan, orders, coadd_weight, intersection)


def solution(mesh):
    return jax.shard_map(
        per_device,
        mesh=mesh,
        in_specs=(
            P(("groups", "expo"), "tile", None),
            P(("groups", "expo"), None, "tile", None),
            P("groups"),
            P(),
            P(("groups", "expo"), None),
            P(("groups", "expo"), None),
        ),
        out_specs=(P("groups", "tile", "expo"), P(("groups", "expo"), None, None)),
        check_vma=False,
    )
```

```python
import functools

import jax
import jax.numpy as jnp
import numpy as np
from jax import lax
from jax.experimental import pallas as pl
from jax.experimental.pallas import tpu as pltpu
from jax.sharding import PartitionSpec as P

HALF = 15
NB = 6
NU = 13
LANES = 128
BEYOND = 1000
PAIRS = [(j, k) for j in range(NB) for k in range(j, NB)]

SIGMAS = (0.8, 1.4, 2.2, 3.0, 4.0, 5.5)
RIDGE = 0.05


def power_of(pos, order):
    return jnp.where(order == 0, 1.0, jnp.where(order == 1, pos, pos * pos))


def tap_values(pos, sigma, order):
    value = jnp.exp(-pos * pos / (2.0 * sigma * sigma)) * power_of(pos, order)
    return jnp.where(jnp.abs(pos) <= HALF, value, 0.0)


def tap_norm(sigma, order):
    pos = lax.broadcasted_iota(jnp.int32, (8, LANES), 1).astype(jnp.float32) - HALF
    value = tap_values(pos, sigma, order)
    return jnp.sqrt(jnp.sum(value * value, axis=1, keepdims=True))[:1]


def target(me, shift, size):
    return me ^ shift if size & (size - 1) == 0 else (me + shift) % size


def source(me, shift, size):
    return me ^ shift if size & (size - 1) == 0 else (me - shift + size) % size


def far_first(size):
    return [*range(size // 2, size), *range(1, size // 2), 0] if size > 1 else [0]


def send_kernel(template_ref, science_ref, plan_ref, *refs, step):
    *out_refs, owner_ref, patch_ref, plan_now, sems = refs
    size = len(out_refs)
    rows, wide = out_refs[0].shape
    chunk = (wide - LANES) // 2
    half = size * chunk // 2
    me = lax.axis_index("expo")
    starts = [pl.multiple_of(target(me, shift, size) * chunk, chunk) for shift in range(size)]
    loads = [
        pltpu.make_async_copy(
            template_ref.at[:, pl.ds(i * half, half)], patch_ref.at[:, pl.ds((i * half + LANES), half)], sems.at[i]
        )
        for i in range(2)
    ]
    copies = [
        pltpu.make_async_copy(
            science_ref.at[:, pl.ds(starts[shift], chunk)],
            out_refs[shift].at[:, pl.ds(chunk + LANES, chunk)],
            sems.at[3 + shift],
        )
        for shift in range(size)
    ]
    copies.append(pltpu.make_async_copy(plan_ref, plan_now, sems.at[2]))
    for copy in loads + copies:
        copy.start()
    blank = jnp.zeros((rows, LANES), patch_ref.dtype)
    patch_ref[:, :LANES] = blank
    patch_ref[:, size * chunk + LANES :] = blank
    for copy in loads:
        copy.wait()
    lane = lax.broadcasted_iota(jnp.int32, (rows, LANES), 1)
    for shift in range(size):
        start = starts[shift]
        out_refs[shift][:, :chunk] = patch_ref[:, pl.ds(start + LANES, chunk)]
        before = patch_ref[:, pl.ds(start, LANES)].astype(jnp.float32)
        after = patch_ref[:, pl.ds(start + chunk + LANES, LANES)].astype(jnp.float32)
        rim = jnp.where(lane < LANES // 2, after, before)
        out_refs[shift][:, chunk : chunk + LANES] = rim.astype(patch_ref.dtype)
    for copy in copies:
        copy.wait()
    owner_ref[...] = jnp.full(owner_ref.shape, plan_now[step], jnp.int32)


def pick_kernel(owner_ref, _, *refs):
    *recv_refs, out_ref = refs
    rows, ext = out_ref.shape
    size = len(recv_refs)
    recv_refs = dict(zip(far_first(size), recv_refs))
    me = lax.axis_index("expo")
    blocks = []
    for b in range(ext // LANES):
        columns = slice(b * LANES, (b + 1) * LANES)
        block = recv_refs[0][:, columns].astype(jnp.float32)
        for shift in range(1, size):
            block = jnp.where(
                owner_ref[...] == source(me, shift, size), recv_refs[shift][:, columns].astype(jnp.float32), block
            )
        blocks.append(block.astype(out_ref.dtype))
    whole = jnp.concatenate(blocks[-1:] + blocks, axis=1)
    out_ref[...] = whole[:, LANES - HALF : LANES - HALF + ext]


def column_positions(first_col, block, width):
    col = lax.broadcasted_iota(jnp.int32, (8, LANES), 1) + (first_col + block * LANES)
    return 2.0 * (col.astype(jnp.float32) + 0.5) / width - 1.0


def band_kernel(orders_ref, row_ref, col_ref, *, tiles):
    rows = row_ref.shape[0] // NB
    tile_at = lax.axis_index("tile")
    near = 1 - 2 * lax.rem(tile_at, 2)
    near_move = jnp.where(tile_at + near < tiles, near - 1, BEYOND)
    far_move = jnp.where((tile_at >= near) & (tile_at - near < tiles), -near - 2, BEYOND)
    source = lax.broadcasted_iota(jnp.int32, (rows, 3 * rows), 1)
    moved = jnp.where(source < rows, 0, jnp.where(source < 2 * rows, near_move, far_move))
    offset = (
        source + moved * rows - lax.broadcasted_iota(jnp.int32, (rows, 3 * rows), 0)
    ).astype(jnp.float32)
    shift = (
        lax.broadcasted_iota(jnp.int32, (2 * LANES, LANES), 0)
        - lax.broadcasted_iota(jnp.int32, (2 * LANES, LANES), 1)
        - HALF
    ).astype(jnp.float32)
    for k in range(NB):
        norm = tap_norm(SIGMAS[k], orders_ref[k, 0])
        row_ref[k * rows : (k + 1) * rows] = (
            tap_values(offset, SIGMAS[k], orders_ref[k, 0]) / norm
        ).astype(jnp.bfloat16)
        norm = tap_norm(SIGMAS[k], orders_ref[k, 1])
        col_ref[k] = (tap_values(shift, SIGMAS[k], orders_ref[k, 1]) / norm).astype(jnp.bfloat16)


def fit_kernel(weight_ref, hits_ref, row_band_ref, col_band_ref, own_ref, near_ref, far_ref, *refs, width):
    *image_refs, conv_ref, sums_ref, row_ref, parts_ref = refs
    tile_at = lax.axis_index("tile")
    expo_at = lax.axis_index("expo")
    rows, ext = own_ref.shape
    expos = len(image_refs)
    chunk = ext - LANES
    blocks = chunk // LANES

    patch = jnp.concatenate([own_ref[...], near_ref[...], far_ref[...]], axis=0)
    row_ref[...] = jnp.dot(
        row_band_ref[...], patch, preferred_element_type=jnp.float32
    ).astype(jnp.bfloat16)
    for k in range(NB):
        window = jnp.concatenate(
            [
                row_ref[k * rows : (k + 1) * rows, b * LANES : (b + 2) * LANES]
                for b in range(blocks)
            ],
            axis=0,
        )
        out = jnp.dot(window, col_band_ref[k], preferred_element_type=jnp.float32)
        conv_ref[k] = out.reshape(blocks, rows, LANES)

    first_col = expo_at * chunk
    xs = [column_positions(first_col, b, width) for b in range(blocks)]

    def fold(x):
        total = x[:8]
        for i in range(8, rows, 8):
            total = total + x[i : i + 8]
        return total

    def moments(at, left, right, count):
        total = [None] * count
        for b in range(blocks):
            term = fold(left(b) * right(b)) if right is not None else fold(left(b))
            for i in range(count):
                total[i] = term if total[i] is None else total[i] + term
                if i < count - 1:
                    term = term * xs[b]
        for i in range(count):
            parts_ref[at + i] = total[i]

    def conv(k):
        return lambda b: conv_ref[k, b]

    def sci(shift):
        return lambda b: image_refs[shift][:, ext + b * LANES : ext + (b + 1) * LANES].astype(jnp.float32)

    blank = jnp.zeros((8, LANES), jnp.float32)
    at = 0
    for j, k in PAIRS:
        moments(at, conv(j), conv(k), 3)
        at += 3
    for k in range(NB):
        moments(at, conv(k), None, 2)
        at += 2
    while at % 8:
        parts_ref[at] = blank
        at += 1
    begin = at
    for shift in range(expos):
        row = at + NU * source(expo_at, shift, expos)
        for k in range(NB):
            moments(row + 2 * k, conv(k), sci(shift), 2)
        moments(row + NU - 1, sci(shift), None, 1)
    at += NU * expos
    weight = jnp.broadcast_to(weight_ref[...] * hits_ref[...].astype(jnp.float32), (8, LANES))
    weight = jnp.where(tile_at == 0, weight, 0.0)
    spot = (
        (lax.broadcasted_iota(jnp.int32, (8, LANES), 0) == 0)
        & (lax.broadcasted_iota(jnp.int32, (8, LANES), 1) == 0)
    )
    for e in range(expos):
        parts_ref[at + e] = jnp.where(spot & (expo_at == e), weight, 0.0)
    at += expos
    while at % 8:
        parts_ref[at] = blank
        at += 1
    ones = jnp.ones((8, LANES), jnp.float32)
    rows_of = []
    for first, last in ((0, begin), (begin, at)):
        lanes = jnp.sum(parts_ref[first:last], axis=1)
        spare = LANES - (last - first)
        if spare:
            lanes = jnp.concatenate([lanes, jnp.zeros((spare, LANES), jnp.float32)], axis=0)
        rows_of.append(
            lax.dot_general(
                ones,
                lanes,
                (((1,), (1,)), ((), ())),
                precision=lax.Precision.HIGHEST,
                preferred_element_type=jnp.float32,
            )
        )
    both = jnp.where(lax.broadcasted_iota(jnp.int32, (8, LANES), 0) < 4, rows_of[0], rows_of[1])
    sums_ref[...] = both


def spread_kernel(*refs):
    *sums_refs, out_ref = refs
    total = sums_refs[0][...]
    for ref in sums_refs[1:]:
        total = total + ref[...]
    for i in range(out_ref.shape[0]):
        out_ref[i] = total


def table(expos):
    columns = np.zeros((NU + expos + 1, 16), np.int32)
    for at, (j, k) in enumerate(PAIRS):
        for a, b in ((j, k), (k, j)):
            columns[b, a] = 3 * at
            columns[NB + b, a] = columns[b, NB + a] = 3 * at + 1
            columns[NB + b, NB + a] = 3 * at + 2
    for k in range(NB):
        for x in range(2):
            columns[NU - 1, x * NB + k] = columns[x * NB + k, NU - 1] = 3 * len(PAIRS) + 2 * k + x
    for e in range(expos):
        columns[NU + e, :NU] = [NU * e + 2 * k + x for x in range(2) for k in range(NB)] + [NU * e + NU - 1]
        columns[NU + expos, e] = NU * expos + e
    return np.ascontiguousarray(np.broadcast_to(columns[:, :, None], columns.shape + (LANES,)))


def solve_kernel(table_ref, sums_ref, conv_ref, *refs, width, pixels):
    *image_refs, coadd_ref, coeffs_ref, tile_ref, sems = refs
    expo_at = lax.axis_index("expo")
    expos = len(image_refs)
    rows, chunk = coadd_ref.shape
    blocks = chunk // LANES
    ext = image_refs[0].shape[1] - chunk
    sub = lax.broadcasted_iota(jnp.int32, (16, LANES), 0)
    lane = lax.broadcasted_iota(jnp.int32, (16, LANES), 1)
    sums = sums_ref[0]
    for i in range(1, sums_ref.shape[0]):
        sums = sums + sums_ref[i]
    first = jnp.broadcast_to(sums[0:1], (16, LANES))
    second = jnp.broadcast_to(sums[4:5], (16, LANES))

    columns = [
        jnp.take_along_axis(first if j < NU else second, table_ref[j], axis=1) for j in range(NU + expos)
    ]
    spread = jnp.take_along_axis(second, table_ref[NU + expos], axis=1)
    weight = [jnp.broadcast_to(spread[e : e + 1], (16, LANES)) for e in range(expos)]
    columns[NU - 1] = jnp.where(sub == NU - 1, float(pixels), columns[NU - 1])

    trace = columns[0][0:1]
    for j in range(1, NU):
        trace = trace + columns[j][j : j + 1]
    scale = 1.0 / trace
    for j in range(NU + expos):
        columns[j] = columns[j] * scale
        if j < NU:
            columns[j] = columns[j] + jnp.where(sub == j, RIDGE / NU, 0.0)
    for i in range(NU):
        inverse = 1.0 / columns[i][i : i + 1]
        for j in range(i + 1, NU + expos):
            factor = columns[j][i : i + 1] * inverse
            columns[j] = jnp.where(sub == i, factor, columns[j] - columns[i] * factor)

    solved = columns[NU:]
    own = solved[0]
    mixed = weight[0] * solved[0]
    for e in range(1, expos):
        own = jnp.where(expo_at == e, solved[e], own)
        mixed = mixed + weight[e] * solved[e]
    diagonal = (sub == lane) & (sub < NU)
    coeffs_ref[...] = jnp.sum(jnp.where(diagonal, own, 0.0), axis=0, keepdims=True)[:, :NU]
    scale = [jnp.broadcast_to(mixed[u : u + 1], (8, LANES)) for u in range(NU)]
    gains = []
    for shift in range(expos):
        gain = weight[0][:8]
        for e in range(1, expos):
            gain = jnp.where(source(expo_at, shift, expos) == e, weight[e][:8], gain)
        gains.append(gain)
    first_col = expo_at * chunk
    copies = []
    for r in range(0, rows, 8):
        for b in range(blocks):
            at = slice(ext + b * LANES, ext + (b + 1) * LANES)
            x = column_positions(first_col, b, width)
            total = -scale[NU - 1]
            for gain, image_ref in zip(gains, image_refs):
                total = total + gain * image_ref[:, at].astype(jnp.float32)[r : r + 8]
            model = (scale[0] + scale[NB] * x) * conv_ref[0, b, r : r + 8]
            for k in range(1, NB):
                model = model + (scale[k] + scale[NB + k] * x) * conv_ref[k, b, r : r + 8]
            tile_ref[r : r + 8, b * LANES : (b + 1) * LANES] = total - model
        copies.append(
            pltpu.make_async_copy(tile_ref.at[pl.ds(r, 8)], coadd_ref.at[pl.ds(r, 8)], sems.at[r // 8])
        )
        copies[-1].start()
    for copy in copies:
        copy.wait()


def swaps(first, size):
    pairs = [(i, i + 1) for i in range(first, size - 1, 2)]
    if first and size % 2 == 0:
        pairs.append((0, size - 1))
    return [pair for a, b in pairs for pair in ((a, b), (b, a))]


def tiled_device(template, science, plan, orders, coadd_weight, intersection):
    expos = lax.axis_size("expo")
    tiles = lax.axis_size("tile")
    _, rows, width = template.shape
    steps = science.shape[1]
    chunk = width // expos
    ext = chunk + LANES
    blocks = chunk // LANES
    smem = pl.BlockSpec(memory_space=pltpu.SMEM)
    vmem = pl.BlockSpec(memory_space=pltpu.VMEM)
    small = pltpu.CompilerParams(vmem_limit_bytes=16 * 1024 * 1024)
    hbm = pl.BlockSpec(memory_space=pltpu.HBM)
    row_band, col_band = pl.pallas_call(
        functools.partial(band_kernel, tiles=tiles),
        out_shape=(
            jax.ShapeDtypeStruct((NB * rows, 3 * rows), jnp.bfloat16),
            jax.ShapeDtypeStruct((NB, 2 * LANES, LANES), jnp.bfloat16),
        ),
        in_specs=[smem],
        out_specs=(vmem, vmem),
        compiler_params=small,
        cost_estimate=pl.CostEstimate(flops=4_000_000, bytes_accessed=500_000, transcendentals=200_000),
    )(orders)
    coadds = []
    fitted = []
    for step in range(steps):
        *images, owner = pl.pallas_call(
            functools.partial(send_kernel, step=step),
            out_shape=(pltpu.VMEM((rows, ext + chunk), template.dtype),) * expos
            + (jax.ShapeDtypeStruct((rows, LANES), jnp.int32),),
            in_specs=[hbm] * 3,
            out_specs=(vmem,) * (expos + 1),
            scratch_shapes=[
                pltpu.VMEM((rows, width + 2 * LANES), template.dtype),
                pltpu.SMEM(plan.shape, jnp.int32),
                pltpu.SemaphoreType.DMA((expos + 3,)),
            ],
            compiler_params=small,
        )(
            pltpu.with_memory_space_constraint(template[0], pltpu.HBM),
            pltpu.with_memory_space_constraint(science[0, step], pltpu.HBM),
            pltpu.with_memory_space_constraint(plan, pltpu.HBM),
        )
        for shift in range(1, expos):
            pairs = [(e, int(target(e, shift, expos))) for e in range(expos)]
            images[shift] = lax.ppermute(images[shift], "expo", pairs)
        own = pl.pallas_call(
            pick_kernel,
            out_shape=jax.ShapeDtypeStruct((rows, ext), template.dtype),
            in_specs=[vmem, pl.BlockSpec(memory_space=pl.ANY)] + [vmem] * expos,
            out_specs=vmem,
            compiler_params=small,
        )(owner, row_band, *(images[shift] for shift in far_first(expos)))
        far = lax.ppermute(own, "tile", swaps(1, tiles))
        near = lax.ppermute(own, "tile", swaps(0, tiles))
        conv, sums = pl.pallas_call(
            functools.partial(fit_kernel, width=width),
            out_shape=(
                jax.ShapeDtypeStruct((NB, blocks, rows, LANES), jnp.float32),
                jax.ShapeDtypeStruct((8, LANES), jnp.float32),
            ),
            in_specs=[vmem] * (7 + expos),
            out_specs=(vmem, vmem),
            scratch_shapes=[
                pltpu.VMEM((NB * rows, ext), jnp.bfloat16),
                pltpu.VMEM((80 + 14 * expos + 8, 8, LANES), jnp.float32),
            ],
            compiler_params=small,
        )(
            coadd_weight[:, step : step + 1],
            intersection[:, step : step + 1],
            row_band,
            col_band,
            own,
            near,
            far,
            *images,
        )
        pairs = tiles // 2 if tiles % 2 == 0 else tiles
        partner = lax.ppermute(sums, "tile", swaps(0, tiles)) if tiles % 2 == 0 else None
        sums = pl.pallas_call(
            spread_kernel,
            out_shape=jax.ShapeDtypeStruct((pairs * expos, 8, LANES), jnp.float32),
            in_specs=[vmem] * (1 if partner is None else 2),
            out_specs=vmem,
            compiler_params=small,
        )(sums, *([] if partner is None else [partner]))
        step_by = tiles // pairs
        groups = [
            [tile * expos + e for tile in range(first, tiles, step_by) for e in range(expos)]
            for first in range(step_by)
        ]
        sums = lax.all_to_all(
            sums, ("tile", "expo"), split_axis=0, concat_axis=0, tiled=True, axis_index_groups=groups
        )
        coadd, coeffs = pl.pallas_call(
            functools.partial(solve_kernel, width=width, pixels=tiles * rows * width),
            out_shape=(
                jax.ShapeDtypeStruct((rows, chunk), jnp.float32),
                jax.ShapeDtypeStruct((1, NU), jnp.float32),
            ),
            in_specs=[vmem] * (3 + expos),
            out_specs=(pl.BlockSpec(memory_space=pl.ANY), vmem),
            scratch_shapes=[
                pltpu.VMEM((rows, chunk), jnp.float32),
                pltpu.SemaphoreType.DMA((rows // 8,)),
            ],
            compiler_params=small,
        )(jnp.asarray(table(expos)), sums, conv, *images)
        coadds.append(coadd[None])
        fitted.append(coeffs)
    return (jnp.concatenate(coadds), jnp.stack(fitted, axis=1))


def broadcast(block, axis, holder):
    block = jnp.where(lax.axis_index(axis) == holder, block, jnp.zeros_like(block))
    return lax.psum(block, axis)


def extended(x, sides, width):
    for axis, dim in sides:
        size, length = (lax.axis_size(axis), x.shape[dim])
        up = [(i, (i + 1) % size) for i in range(size - 1)]
        down = [(j, i) for i, j in up]
        last = lax.slice_in_dim(x, length - width, length, axis=dim)
        first = lax.slice_in_dim(x, 0, width, axis=dim)
        before = lax.ppermute(last, axis, up)
        after = lax.ppermute(first, axis, down)
        x = jnp.concatenate([before, x, after], axis=dim)
    return x


def make_filters(orders):
    taps_pos = jnp.arange(2 * HALF + 1).astype(jnp.float32) - HALF
    row_list = []
    col_list = []
    for basis in range(NB):
        sigma = SIGMAS[basis]
        envelope = jnp.exp(-taps_pos * taps_pos / (2.0 * sigma * sigma))
        row_filter = envelope * power_of(taps_pos, orders[basis, 0])
        col_filter = envelope * power_of(taps_pos, orders[basis, 1])
        row_list.append(row_filter / jnp.sqrt(jnp.sum(row_filter * row_filter)))
        col_list.append(col_filter / jnp.sqrt(jnp.sum(col_filter * col_filter)))
    return (jnp.stack(row_list).astype(jnp.bfloat16), jnp.stack(col_list).astype(jnp.bfloat16))


def band_matrix(filters, out_len, in_len):
    offset = jnp.arange(in_len)[None, :] - jnp.arange(out_len)[:, None]
    taps_idx = jnp.arange(2 * HALF + 1)
    picks = (offset[:, :, None] == taps_idx[None, None, :]).astype(jnp.float32)
    band = jnp.einsum("ijt,kt->kij", picks, filters.astype(jnp.float32))
    return band.astype(jnp.bfloat16)


def any_device(template, science, plan, orders, coadd_weight, intersection):
    row_filters, col_filters = make_filters(orders)
    rows = template.shape[1]
    width = template.shape[2]
    blocks_count = width // 128
    steps_count = science.shape[1]
    row_band = band_matrix(row_filters, rows, rows + 2 * HALF)
    col_band = jnp.transpose(band_matrix(col_filters, 128, 128 + 2 * HALF), (0, 2, 1))
    column_pos = 2.0 * (jnp.arange(width).astype(jnp.float32) + 0.5) / width - 1.0
    pieces = []
    fitted = []
    for step in range(steps_count):
        received = broadcast(template[0], "expo", plan[step])
        padded = extended(received, (("tile", 0),), HALF)
        rowconv = jnp.einsum(
            "kij,jw->kiw", row_band, padded, preferred_element_type=jnp.float32
        ).astype(jnp.bfloat16)
        blocks = rowconv.reshape(NB, rows, blocks_count, 128)
        empty_rim = jnp.zeros((NB, rows, 1, HALF), jnp.bfloat16)
        previous = jnp.concatenate([empty_rim, blocks[:, :, :-1, 128 - HALF :]], axis=2)
        following = jnp.concatenate([blocks[:, :, 1:, :HALF], empty_rim], axis=2)
        window = jnp.concatenate([previous, blocks, following], axis=3)
        conv = jnp.einsum("krbj,kjc->krbc", window, col_band, preferred_element_type=jnp.float32)
        conv = conv.reshape(NB, rows, width)
        fields = jnp.concatenate(
            [conv, conv * column_pos, jnp.ones((1, rows, width), jnp.float32)], axis=0
        )
        fields = fields.reshape(NU, rows * width)
        exposure_image = science[0, step].astype(jnp.float32).reshape(rows * width)
        normal_local = jnp.dot(fields, fields.T, precision=lax.Precision.HIGHEST)
        project_local = jnp.dot(fields, exposure_image, precision=lax.Precision.HIGHEST)
        normal_matrix, projections = lax.psum((normal_local, project_local), "tile")
        normal_matrix = normal_matrix + RIDGE * (jnp.trace(normal_matrix) / NU) * jnp.eye(
            NU, dtype=jnp.float32
        )
        factor = jnp.linalg.cholesky(normal_matrix)
        coeffs = jax.scipy.linalg.cho_solve((factor, True), projections)
        model = jnp.dot(coeffs, fields, precision=lax.Precision.HIGHEST)
        difference = exposure_image - model
        weight_now = coadd_weight[0, step] * intersection[0, step].astype(jnp.float32)
        pieces.append((weight_now * difference).reshape(rows, width))
        fitted.append(coeffs)
    weighted = jnp.stack(pieces)
    received_parts = lax.all_to_all(weighted[None], "expo", split_axis=3, concat_axis=0, tiled=True)
    coadd = jnp.sum(received_parts, axis=0)
    return (coadd, jnp.stack(fitted)[None])


def per_device(template, science, plan, orders, coadd_weight, intersection):
    expos = lax.axis_size("expo")
    rows, width = template.shape[1:]
    whole_lanes = width % (expos * LANES) == 0 and rows % 16 == 0
    few = (NU + 1) * expos <= LANES and NU + expos <= LANES
    body = tiled_device if whole_lanes and few else any_device
    return body(template, science, plan, orders, coadd_weight, intersection)


def solution(mesh):
    return jax.shard_map(
        per_device,
        mesh=mesh,
        in_specs=(
            P(("groups", "expo"), "tile", None),
            P(("groups", "expo"), None, "tile", None),
            P("groups"),
            P(),
            P(("groups", "expo"), None),
            P(("groups", "expo"), None),
        ),
        out_specs=(P("groups", "tile", "expo"), P(("groups", "expo"), None, None)),
        check_vma=False,
    )
```

```python
import functools

import jax
import jax.numpy as jnp
import numpy as np
from jax import lax
from jax.experimental import pallas as pl
from jax.experimental.pallas import tpu as pltpu
from jax.sharding import PartitionSpec as P

HALF = 15
NB = 6
NU = 13
LANES = 128
BEYOND = 1000
PAIRS = [(j, k) for j in range(NB) for k in range(j, NB)]

SIGMAS = (0.8, 1.4, 2.2, 3.0, 4.0, 5.5)
RIDGE = 0.05


def power_of(pos, order):
    return jnp.where(order == 0, 1.0, jnp.where(order == 1, pos, pos * pos))


def tap_values(pos, sigma, order):
    value = jnp.exp(-pos * pos / (2.0 * sigma * sigma)) * power_of(pos, order)
    return jnp.where(jnp.abs(pos) <= HALF, value, 0.0)


def tap_norm(sigma, order):
    pos = lax.broadcasted_iota(jnp.int32, (8, LANES), 1).astype(jnp.float32) - HALF
    value = tap_values(pos, sigma, order)
    return jnp.sqrt(jnp.sum(value * value, axis=1, keepdims=True))[:1]


def target(me, shift, size):
    return me ^ shift if size & (size - 1) == 0 else (me + shift) % size


def source(me, shift, size):
    return me ^ shift if size & (size - 1) == 0 else (me - shift + size) % size


def far_first(size):
    return [*range(size // 2, size), *range(1, size // 2), 0] if size > 1 else [0]


def send_kernel(template_ref, science_ref, plan_ref, *refs, step):
    *out_refs, owner_ref, patch_ref, plan_now, sems = refs
    size = len(out_refs)
    rows, wide = out_refs[0].shape
    chunk = (wide - LANES) // 2
    half = size * chunk // 2
    me = lax.axis_index("expo")
    starts = [pl.multiple_of(target(me, shift, size) * chunk, chunk) for shift in range(size)]
    loads = [
        pltpu.make_async_copy(
            template_ref.at[:, pl.ds(i * half, half)], patch_ref.at[:, pl.ds((i * half + LANES), half)], sems.at[i]
        )
        for i in range(2)
    ]
    copies = [
        pltpu.make_async_copy(
            science_ref.at[:, pl.ds(starts[shift], chunk)],
            out_refs[shift].at[:, pl.ds(chunk + LANES, chunk)],
            sems.at[3 + shift],
        )
        for shift in range(size)
    ]
    copies.append(pltpu.make_async_copy(plan_ref, plan_now, sems.at[2]))
    for copy in loads + copies:
        copy.start()
    blank = jnp.zeros((rows, LANES), patch_ref.dtype)
    patch_ref[:, :LANES] = blank
    patch_ref[:, size * chunk + LANES :] = blank
    for copy in loads:
        copy.wait()
    lane = lax.broadcasted_iota(jnp.int32, (rows, LANES), 1)
    for shift in range(size):
        start = starts[shift]
        out_refs[shift][:, :chunk] = patch_ref[:, pl.ds(start + LANES, chunk)]
        before = patch_ref[:, pl.ds(start, LANES)].astype(jnp.float32)
        after = patch_ref[:, pl.ds(start + chunk + LANES, LANES)].astype(jnp.float32)
        rim = jnp.where(lane < LANES // 2, after, before)
        out_refs[shift][:, chunk : chunk + LANES] = rim.astype(patch_ref.dtype)
    for copy in copies:
        copy.wait()
    owner_ref[...] = jnp.full(owner_ref.shape, plan_now[step], jnp.int32)


def pick_kernel(owner_ref, _, *refs):
    *recv_refs, out_ref = refs
    rows, ext = out_ref.shape
    size = len(recv_refs)
    recv_refs = dict(zip(far_first(size), recv_refs))
    me = lax.axis_index("expo")
    blocks = []
    for b in range(ext // LANES):
        columns = slice(b * LANES, (b + 1) * LANES)
        block = recv_refs[0][:, columns].astype(jnp.float32)
        for shift in range(1, size):
            block = jnp.where(
                owner_ref[...] == source(me, shift, size), recv_refs[shift][:, columns].astype(jnp.float32), block
            )
        blocks.append(block.astype(out_ref.dtype))
    whole = jnp.concatenate(blocks[-1:] + blocks, axis=1)
    out_ref[...] = whole[:, LANES - HALF : LANES - HALF + ext]


def column_positions(first_col, block, width):
    col = lax.broadcasted_iota(jnp.int32, (8, LANES), 1) + (first_col + block * LANES)
    return 2.0 * (col.astype(jnp.float32) + 0.5) / width - 1.0


def band_kernel(orders_ref, row_ref, col_ref, *, tiles):
    rows = row_ref.shape[0] // NB
    tile_at = lax.axis_index("tile")
    near = 1 - 2 * lax.rem(tile_at, 2)
    near_move = jnp.where(tile_at + near < tiles, near - 1, BEYOND)
    far_move = jnp.where((tile_at >= near) & (tile_at - near < tiles), -near - 2, BEYOND)
    source = lax.broadcasted_iota(jnp.int32, (rows, 3 * rows), 1)
    moved = jnp.where(source < rows, 0, jnp.where(source < 2 * rows, near_move, far_move))
    offset = (
        source + moved * rows - lax.broadcasted_iota(jnp.int32, (rows, 3 * rows), 0)
    ).astype(jnp.float32)
    shift = (
        lax.broadcasted_iota(jnp.int32, (2 * LANES, LANES), 0)
        - lax.broadcasted_iota(jnp.int32, (2 * LANES, LANES), 1)
        - HALF
    ).astype(jnp.float32)
    for k in range(NB):
        norm = tap_norm(SIGMAS[k], orders_ref[k, 0])
        row_ref[k * rows : (k + 1) * rows] = (
            tap_values(offset, SIGMAS[k], orders_ref[k, 0]) / norm
        ).astype(jnp.bfloat16)
        norm = tap_norm(SIGMAS[k], orders_ref[k, 1])
        col_ref[k] = (tap_values(shift, SIGMAS[k], orders_ref[k, 1]) / norm).astype(jnp.bfloat16)


def fit_kernel(weight_ref, hits_ref, row_band_ref, col_band_ref, own_ref, near_ref, far_ref, *refs, width):
    *image_refs, conv_ref, sums_ref, row_ref, parts_ref = refs
    tile_at = lax.axis_index("tile")
    expo_at = lax.axis_index("expo")
    rows, ext = own_ref.shape
    expos = len(image_refs)
    chunk = ext - LANES
    blocks = chunk // LANES

    patch = jnp.concatenate([own_ref[...], near_ref[...], far_ref[...]], axis=0)
    row_ref[...] = jnp.dot(
        row_band_ref[...], patch, preferred_element_type=jnp.float32
    ).astype(jnp.bfloat16)
    for k in range(NB):
        window = jnp.concatenate(
            [
                row_ref[k * rows : (k + 1) * rows, b * LANES : (b + 2) * LANES]
                for b in range(blocks)
            ],
            axis=0,
        )
        out = jnp.dot(window, col_band_ref[k], preferred_element_type=jnp.float32)
        conv_ref[k] = out.reshape(blocks, rows, LANES)

    first_col = expo_at * chunk
    xs = [column_positions(first_col, b, width) for b in range(blocks)]

    def fold(x):
        total = x[:8]
        for i in range(8, rows, 8):
            total = total + x[i : i + 8]
        return total

    def moments(at, left, right, count):
        total = [None] * count
        for b in range(blocks):
            term = fold(left(b) * right(b)) if right is not None else fold(left(b))
            for i in range(count):
                total[i] = term if total[i] is None else total[i] + term
                if i < count - 1:
                    term = term * xs[b]
        for i in range(count):
            parts_ref[at + i] = total[i]

    def conv(k):
        return lambda b: conv_ref[k, b]

    def sci(shift):
        return lambda b: image_refs[shift][:, ext + b * LANES : ext + (b + 1) * LANES].astype(jnp.float32)

    blank = jnp.zeros((8, LANES), jnp.float32)
    at = 0
    for j, k in PAIRS:
        moments(at, conv(j), conv(k), 3)
        at += 3
    for k in range(NB):
        moments(at, conv(k), None, 2)
        at += 2
    while at % 8:
        parts_ref[at] = blank
        at += 1
    begin = at
    for shift in range(expos):
        row = at + NU * source(expo_at, shift, expos)
        for k in range(NB):
            moments(row + 2 * k, conv(k), sci(shift), 2)
        moments(row + NU - 1, sci(shift), None, 1)
    at += NU * expos
    weight = jnp.broadcast_to(weight_ref[...] * hits_ref[...].astype(jnp.float32), (8, LANES))
    weight = jnp.where(tile_at == 0, weight, 0.0)
    spot = (
        (lax.broadcasted_iota(jnp.int32, (8, LANES), 0) == 0)
        & (lax.broadcasted_iota(jnp.int32, (8, LANES), 1) == 0)
    )
    for e in range(expos):
        parts_ref[at + e] = jnp.where(spot & (expo_at == e), weight, 0.0)
    at += expos
    while at % 8:
        parts_ref[at] = blank
        at += 1
    ones = jnp.ones((8, LANES), jnp.float32)
    rows_of = []
    for first, last in ((0, begin), (begin, at)):
        lanes = jnp.sum(parts_ref[first:last], axis=1)
        spare = LANES - (last - first)
        if spare:
            lanes = jnp.concatenate([lanes, jnp.zeros((spare, LANES), jnp.float32)], axis=0)
        rows_of.append(
            lax.dot_general(
                ones,
                lanes,
                (((1,), (1,)), ((), ())),
                precision=lax.Precision.HIGHEST,
                preferred_element_type=jnp.float32,
            )
        )
    both = jnp.where(lax.broadcasted_iota(jnp.int32, (8, LANES), 0) < 4, rows_of[0], rows_of[1])
    sums_ref[...] = both


def table(expos):
    columns = np.zeros((NU + expos + 1, 16), np.int32)
    for at, (j, k) in enumerate(PAIRS):
        for a, b in ((j, k), (k, j)):
            columns[b, a] = 3 * at
            columns[NB + b, a] = columns[b, NB + a] = 3 * at + 1
            columns[NB + b, NB + a] = 3 * at + 2
    for k in range(NB):
        for x in range(2):
            columns[NU - 1, x * NB + k] = columns[x * NB + k, NU - 1] = 3 * len(PAIRS) + 2 * k + x
    for e in range(expos):
        columns[NU + e, :NU] = [NU * e + 2 * k + x for x in range(2) for k in range(NB)] + [NU * e + NU - 1]
        columns[NU + expos, e] = NU * expos + e
    return np.ascontiguousarray(np.broadcast_to(columns[:, :, None], columns.shape + (LANES,)))


def solve_kernel(table_ref, sums_ref, conv_ref, *refs, width, pixels):
    *image_refs, coadd_ref, coeffs_ref, tile_ref, sems = refs
    expo_at = lax.axis_index("expo")
    expos = len(image_refs)
    rows, chunk = coadd_ref.shape
    blocks = chunk // LANES
    ext = image_refs[0].shape[1] - chunk
    sub = lax.broadcasted_iota(jnp.int32, (16, LANES), 0)
    lane = lax.broadcasted_iota(jnp.int32, (16, LANES), 1)
    sums = sums_ref[0]
    for i in range(1, sums_ref.shape[0]):
        sums = sums + sums_ref[i]
    first = jnp.broadcast_to(sums[0:1], (16, LANES))
    second = jnp.broadcast_to(sums[4:5], (16, LANES))

    columns = [
        jnp.take_along_axis(first if j < NU else second, table_ref[j], axis=1) for j in range(NU + expos)
    ]
    spread = jnp.take_along_axis(second, table_ref[NU + expos], axis=1)
    weight = [jnp.broadcast_to(spread[e : e + 1], (16, LANES)) for e in range(expos)]
    columns[NU - 1] = jnp.where(sub == NU - 1, float(pixels), columns[NU - 1])

    trace = columns[0][0:1]
    for j in range(1, NU):
        trace = trace + columns[j][j : j + 1]
    scale = 1.0 / trace
    for j in range(NU + expos):
        columns[j] = columns[j] * scale
        if j < NU:
            columns[j] = columns[j] + jnp.where(sub == j, RIDGE / NU, 0.0)
    for i in range(NU):
        inverse = 1.0 / columns[i][i : i + 1]
        for j in range(i + 1, NU + expos):
            factor = columns[j][i : i + 1] * inverse
            columns[j] = jnp.where(sub == i, factor, columns[j] - columns[i] * factor)

    solved = columns[NU:]
    own = solved[0]
    mixed = weight[0] * solved[0]
    for e in range(1, expos):
        own = jnp.where(expo_at == e, solved[e], own)
        mixed = mixed + weight[e] * solved[e]
    diagonal = (sub == lane) & (sub < NU)
    coeffs_ref[...] = jnp.sum(jnp.where(diagonal, own, 0.0), axis=0, keepdims=True)[:, :NU]
    scale = [jnp.broadcast_to(mixed[u : u + 1], (8, LANES)) for u in range(NU)]
    gains = []
    for shift in range(expos):
        gain = weight[0][:8]
        for e in range(1, expos):
            gain = jnp.where(source(expo_at, shift, expos) == e, weight[e][:8], gain)
        gains.append(gain)
    first_col = expo_at * chunk
    copies = []
    for r in range(0, rows, 8):
        for b in range(blocks):
            at = slice(ext + b * LANES, ext + (b + 1) * LANES)
            x = column_positions(first_col, b, width)
            total = -scale[NU - 1]
            for gain, image_ref in zip(gains, image_refs):
                total = total + gain * image_ref[:, at].astype(jnp.float32)[r : r + 8]
            model = (scale[0] + scale[NB] * x) * conv_ref[0, b, r : r + 8]
            for k in range(1, NB):
                model = model + (scale[k] + scale[NB + k] * x) * conv_ref[k, b, r : r + 8]
            tile_ref[r : r + 8, b * LANES : (b + 1) * LANES] = total - model
        copies.append(
            pltpu.make_async_copy(tile_ref.at[pl.ds(r, 8)], coadd_ref.at[pl.ds(r, 8)], sems.at[r // 8])
        )
        copies[-1].start()
    for copy in copies:
        copy.wait()


def swaps(first, size):
    pairs = [(i, i + 1) for i in range(first, size - 1, 2)]
    if first and size % 2 == 0:
        pairs.append((0, size - 1))
    return [pair for a, b in pairs for pair in ((a, b), (b, a))]


def tiled_device(template, science, plan, orders, coadd_weight, intersection):
    expos = lax.axis_size("expo")
    tiles = lax.axis_size("tile")
    _, rows, width = template.shape
    steps = science.shape[1]
    chunk = width // expos
    ext = chunk + LANES
    blocks = chunk // LANES
    smem = pl.BlockSpec(memory_space=pltpu.SMEM)
    vmem = pl.BlockSpec(memory_space=pltpu.VMEM)
    small = pltpu.CompilerParams(vmem_limit_bytes=16 * 1024 * 1024)
    hbm = pl.BlockSpec(memory_space=pltpu.HBM)
    row_band, col_band = pl.pallas_call(
        functools.partial(band_kernel, tiles=tiles),
        out_shape=(
            jax.ShapeDtypeStruct((NB * rows, 3 * rows), jnp.bfloat16),
            jax.ShapeDtypeStruct((NB, 2 * LANES, LANES), jnp.bfloat16),
        ),
        in_specs=[smem],
        out_specs=(vmem, vmem),
        compiler_params=small,
        cost_estimate=pl.CostEstimate(flops=4_000_000, bytes_accessed=500_000, transcendentals=200_000),
    )(orders)
    coadds = []
    fitted = []
    for step in range(steps):
        *images, owner = pl.pallas_call(
            functools.partial(send_kernel, step=step),
            out_shape=(pltpu.VMEM((rows, ext + chunk), template.dtype),) * expos
            + (jax.ShapeDtypeStruct((rows, LANES), jnp.int32),),
            in_specs=[hbm] * 3,
            out_specs=(vmem,) * (expos + 1),
            scratch_shapes=[
                pltpu.VMEM((rows, width + 2 * LANES), template.dtype),
                pltpu.SMEM(plan.shape, jnp.int32),
                pltpu.SemaphoreType.DMA((expos + 3,)),
            ],
            compiler_params=small,
        )(
            pltpu.with_memory_space_constraint(template[0], pltpu.HBM),
            pltpu.with_memory_space_constraint(science[0, step], pltpu.HBM),
            pltpu.with_memory_space_constraint(plan, pltpu.HBM),
        )
        for shift in range(1, expos):
            pairs = [(e, int(target(e, shift, expos))) for e in range(expos)]
            images[shift] = lax.ppermute(images[shift], "expo", pairs)
        own = pl.pallas_call(
            pick_kernel,
            out_shape=jax.ShapeDtypeStruct((rows, ext), template.dtype),
            in_specs=[vmem, pl.BlockSpec(memory_space=pl.ANY)] + [vmem] * expos,
            out_specs=vmem,
            compiler_params=small,
        )(owner, row_band, *(images[shift] for shift in far_first(expos)))
        far = lax.ppermute(own, "tile", swaps(1, tiles))
        near = lax.ppermute(own, "tile", swaps(0, tiles))
        conv, sums = pl.pallas_call(
            functools.partial(fit_kernel, width=width),
            out_shape=(
                jax.ShapeDtypeStruct((NB, blocks, rows, LANES), jnp.float32),
                jax.ShapeDtypeStruct((8, LANES), jnp.float32),
            ),
            in_specs=[vmem] * (7 + expos),
            out_specs=(vmem, vmem),
            scratch_shapes=[
                pltpu.VMEM((NB * rows, ext), jnp.bfloat16),
                pltpu.VMEM((80 + 14 * expos + 8, 8, LANES), jnp.float32),
            ],
            compiler_params=small,
        )(
            coadd_weight[:, step : step + 1],
            intersection[:, step : step + 1],
            row_band,
            col_band,
            own,
            near,
            far,
            *images,
        )
        sums = lax.all_gather(sums, ("tile", "expo"))
        coadd, coeffs = pl.pallas_call(
            functools.partial(solve_kernel, width=width, pixels=tiles * rows * width),
            out_shape=(
                jax.ShapeDtypeStruct((rows, chunk), jnp.float32),
                jax.ShapeDtypeStruct((1, NU), jnp.float32),
            ),
            in_specs=[vmem] * (3 + expos),
            out_specs=(pl.BlockSpec(memory_space=pl.ANY), vmem),
            scratch_shapes=[
                pltpu.VMEM((rows, chunk), jnp.float32),
                pltpu.SemaphoreType.DMA((rows // 8,)),
            ],
            compiler_params=small,
        )(jnp.asarray(table(expos)), sums, conv, *images)
        coadds.append(coadd[None])
        fitted.append(coeffs)
    return (jnp.concatenate(coadds), jnp.stack(fitted, axis=1))


def broadcast(block, axis, holder):
    block = jnp.where(lax.axis_index(axis) == holder, block, jnp.zeros_like(block))
    return lax.psum(block, axis)


def extended(x, sides, width):
    for axis, dim in sides:
        size, length = (lax.axis_size(axis), x.shape[dim])
        up = [(i, (i + 1) % size) for i in range(size - 1)]
        down = [(j, i) for i, j in up]
        last = lax.slice_in_dim(x, length - width, length, axis=dim)
        first = lax.slice_in_dim(x, 0, width, axis=dim)
        before = lax.ppermute(last, axis, up)
        after = lax.ppermute(first, axis, down)
        x = jnp.concatenate([before, x, after], axis=dim)
    return x


def make_filters(orders):
    taps_pos = jnp.arange(2 * HALF + 1).astype(jnp.float32) - HALF
    row_list = []
    col_list = []
    for basis in range(NB):
        sigma = SIGMAS[basis]
        envelope = jnp.exp(-taps_pos * taps_pos / (2.0 * sigma * sigma))
        row_filter = envelope * power_of(taps_pos, orders[basis, 0])
        col_filter = envelope * power_of(taps_pos, orders[basis, 1])
        row_list.append(row_filter / jnp.sqrt(jnp.sum(row_filter * row_filter)))
        col_list.append(col_filter / jnp.sqrt(jnp.sum(col_filter * col_filter)))
    return (jnp.stack(row_list).astype(jnp.bfloat16), jnp.stack(col_list).astype(jnp.bfloat16))


def band_matrix(filters, out_len, in_len):
    offset = jnp.arange(in_len)[None, :] - jnp.arange(out_len)[:, None]
    taps_idx = jnp.arange(2 * HALF + 1)
    picks = (offset[:, :, None] == taps_idx[None, None, :]).astype(jnp.float32)
    band = jnp.einsum("ijt,kt->kij", picks, filters.astype(jnp.float32))
    return band.astype(jnp.bfloat16)


def any_device(template, science, plan, orders, coadd_weight, intersection):
    row_filters, col_filters = make_filters(orders)
    rows = template.shape[1]
    width = template.shape[2]
    blocks_count = width // 128
    steps_count = science.shape[1]
    row_band = band_matrix(row_filters, rows, rows + 2 * HALF)
    col_band = jnp.transpose(band_matrix(col_filters, 128, 128 + 2 * HALF), (0, 2, 1))
    column_pos = 2.0 * (jnp.arange(width).astype(jnp.float32) + 0.5) / width - 1.0
    pieces = []
    fitted = []
    for step in range(steps_count):
        received = broadcast(template[0], "expo", plan[step])
        padded = extended(received, (("tile", 0),), HALF)
        rowconv = jnp.einsum(
            "kij,jw->kiw", row_band, padded, preferred_element_type=jnp.float32
        ).astype(jnp.bfloat16)
        blocks = rowconv.reshape(NB, rows, blocks_count, 128)
        empty_rim = jnp.zeros((NB, rows, 1, HALF), jnp.bfloat16)
        previous = jnp.concatenate([empty_rim, blocks[:, :, :-1, 128 - HALF :]], axis=2)
        following = jnp.concatenate([blocks[:, :, 1:, :HALF], empty_rim], axis=2)
        window = jnp.concatenate([previous, blocks, following], axis=3)
        conv = jnp.einsum("krbj,kjc->krbc", window, col_band, preferred_element_type=jnp.float32)
        conv = conv.reshape(NB, rows, width)
        fields = jnp.concatenate(
            [conv, conv * column_pos, jnp.ones((1, rows, width), jnp.float32)], axis=0
        )
        fields = fields.reshape(NU, rows * width)
        exposure_image = science[0, step].astype(jnp.float32).reshape(rows * width)
        normal_local = jnp.dot(fields, fields.T, precision=lax.Precision.HIGHEST)
        project_local = jnp.dot(fields, exposure_image, precision=lax.Precision.HIGHEST)
        normal_matrix, projections = lax.psum((normal_local, project_local), "tile")
        normal_matrix = normal_matrix + RIDGE * (jnp.trace(normal_matrix) / NU) * jnp.eye(
            NU, dtype=jnp.float32
        )
        factor = jnp.linalg.cholesky(normal_matrix)
        coeffs = jax.scipy.linalg.cho_solve((factor, True), projections)
        model = jnp.dot(coeffs, fields, precision=lax.Precision.HIGHEST)
        difference = exposure_image - model
        weight_now = coadd_weight[0, step] * intersection[0, step].astype(jnp.float32)
        pieces.append((weight_now * difference).reshape(rows, width))
        fitted.append(coeffs)
    weighted = jnp.stack(pieces)
    received_parts = lax.all_to_all(weighted[None], "expo", split_axis=3, concat_axis=0, tiled=True)
    coadd = jnp.sum(received_parts, axis=0)
    return (coadd, jnp.stack(fitted)[None])


def per_device(template, science, plan, orders, coadd_weight, intersection):
    expos = lax.axis_size("expo")
    rows, width = template.shape[1:]
    whole_lanes = width % (expos * LANES) == 0 and rows % 16 == 0
    few = (NU + 1) * expos <= LANES and NU + expos <= LANES
    body = tiled_device if whole_lanes and few else any_device
    return body(template, science, plan, orders, coadd_weight, intersection)


def solution(mesh):
    return jax.shard_map(
        per_device,
        mesh=mesh,
        in_specs=(
            P(("groups", "expo"), "tile", None),
            P(("groups", "expo"), None, "tile", None),
            P("groups"),
            P(),
            P(("groups", "expo"), None),
            P(("groups", "expo"), None),
        ),
        out_specs=(P("groups", "tile", "expo"), P(("groups", "expo"), None, None)),
        check_vma=False,
    )
```

```python
import functools

import jax
import jax.numpy as jnp
import numpy as np
from jax import lax
from jax.experimental import pallas as pl
from jax.experimental.pallas import tpu as pltpu
from jax.sharding import PartitionSpec as P

HALF = 15
NB = 6
NU = 13
LANES = 128
BEYOND = 1000
PAIRS = [(j, k) for j in range(NB) for k in range(j, NB)]

SIGMAS = (0.8, 1.4, 2.2, 3.0, 4.0, 5.5)
RIDGE = 0.05


def power_of(pos, order):
    return jnp.where(order == 0, 1.0, jnp.where(order == 1, pos, pos * pos))


def tap_values(pos, sigma, order):
    value = jnp.exp(-pos * pos / (2.0 * sigma * sigma)) * power_of(pos, order)
    return jnp.where(jnp.abs(pos) <= HALF, value, 0.0)


def tap_norm(sigma, order):
    pos = lax.broadcasted_iota(jnp.int32, (8, LANES), 1).astype(jnp.float32) - HALF
    value = tap_values(pos, sigma, order)
    return jnp.sqrt(jnp.sum(value * value, axis=1, keepdims=True))[:1]


def target(me, shift, size):
    return me ^ shift if size & (size - 1) == 0 else (me + shift) % size


def source(me, shift, size):
    return me ^ shift if size & (size - 1) == 0 else (me - shift + size) % size


def far_first(size):
    return [*range(size // 2, size), *range(1, size // 2), 0] if size > 1 else [0]


def send_kernel(template_ref, science_ref, plan_ref, *refs, step):
    *out_refs, owner_ref, patch_ref, plan_now, sems = refs
    size = len(out_refs) // 2
    image_refs = out_refs[size:]
    rows, ext = image_refs[0].shape
    chunk = ext - LANES
    half = size * chunk // 2
    me = lax.axis_index("expo")
    starts = [pl.multiple_of(target(me, shift, size) * chunk, chunk) for shift in range(size)]
    loads = [
        pltpu.make_async_copy(
            template_ref.at[:, pl.ds(i * half, half)], patch_ref.at[:, pl.ds((i * half + LANES), half)], sems.at[i]
        )
        for i in range(2)
    ]
    copies = [
        pltpu.make_async_copy(
            science_ref.at[:, pl.ds(starts[shift], chunk)],
            image_refs[shift].at[:, pl.ds(0, chunk)],
            sems.at[3 + shift],
        )
        for shift in range(size)
    ]
    copies.append(pltpu.make_async_copy(plan_ref, plan_now, sems.at[2]))
    for copy in loads + copies:
        copy.start()
    blank = jnp.zeros((rows, LANES), patch_ref.dtype)
    patch_ref[:, :LANES] = blank
    patch_ref[:, size * chunk + LANES :] = blank
    for image_ref in image_refs:
        image_ref[:, chunk:] = blank
    for copy in loads:
        copy.wait()
    lane = lax.broadcasted_iota(jnp.int32, (rows, LANES), 1)
    for shift in range(size):
        start = starts[shift]
        out_refs[shift][:, :chunk] = patch_ref[:, pl.ds(start + LANES, chunk)]
        before = patch_ref[:, pl.ds(start, LANES)].astype(jnp.float32)
        after = patch_ref[:, pl.ds(start + chunk + LANES, LANES)].astype(jnp.float32)
        rim = jnp.where(lane < LANES // 2, after, before)
        out_refs[shift][:, chunk:] = rim.astype(patch_ref.dtype)
    for copy in copies:
        copy.wait()
    owner_ref[...] = jnp.full(owner_ref.shape, plan_now[step], jnp.int32)


def pick_kernel(owner_ref, *refs):
    *recv_refs, out_ref = refs
    rows, ext = out_ref.shape
    size = len(recv_refs)
    recv_refs = dict(zip(far_first(size), recv_refs))
    me = lax.axis_index("expo")
    blocks = []
    for b in range(ext // LANES):
        columns = slice(b * LANES, (b + 1) * LANES)
        block = recv_refs[0][:, columns].astype(jnp.float32)
        for shift in range(1, size):
            block = jnp.where(
                owner_ref[...] == source(me, shift, size), recv_refs[shift][:, columns].astype(jnp.float32), block
            )
        blocks.append(block.astype(out_ref.dtype))
    whole = jnp.concatenate(blocks[-1:] + blocks, axis=1)
    out_ref[...] = whole[:, LANES - HALF : LANES - HALF + ext]


def column_positions(first_col, block, width):
    col = lax.broadcasted_iota(jnp.int32, (8, LANES), 1) + (first_col + block * LANES)
    return 2.0 * (col.astype(jnp.float32) + 0.5) / width - 1.0


def band_kernel(orders_ref, row_ref, col_ref, *, tiles):
    rows = row_ref.shape[0] // NB
    tile_at = lax.axis_index("tile")
    near = 1 - 2 * lax.rem(tile_at, 2)
    near_move = jnp.where(tile_at + near < tiles, near - 1, BEYOND)
    far_move = jnp.where((tile_at >= near) & (tile_at - near < tiles), -near - 2, BEYOND)
    source = lax.broadcasted_iota(jnp.int32, (rows, 3 * rows), 1)
    moved = jnp.where(source < rows, 0, jnp.where(source < 2 * rows, near_move, far_move))
    offset = (
        source + moved * rows - lax.broadcasted_iota(jnp.int32, (rows, 3 * rows), 0)
    ).astype(jnp.float32)
    shift = (
        lax.broadcasted_iota(jnp.int32, (2 * LANES, LANES), 0)
        - lax.broadcasted_iota(jnp.int32, (2 * LANES, LANES), 1)
        - HALF
    ).astype(jnp.float32)
    for k in range(NB):
        norm = tap_norm(SIGMAS[k], orders_ref[k, 0])
        row_ref[k * rows : (k + 1) * rows] = (
            tap_values(offset, SIGMAS[k], orders_ref[k, 0]) / norm
        ).astype(jnp.bfloat16)
        norm = tap_norm(SIGMAS[k], orders_ref[k, 1])
        col_ref[k] = (tap_values(shift, SIGMAS[k], orders_ref[k, 1]) / norm).astype(jnp.bfloat16)


def fit_kernel(weight_ref, hits_ref, row_band_ref, col_band_ref, own_ref, near_ref, far_ref, *refs, width):
    *image_refs, conv_ref, sums_ref, row_ref, parts_ref = refs
    image_refs = dict(zip(far_first(len(image_refs)), image_refs))
    tile_at = lax.axis_index("tile")
    expo_at = lax.axis_index("expo")
    rows, ext = own_ref.shape
    expos = len(image_refs)
    chunk = ext - LANES
    blocks = chunk // LANES

    patch = jnp.concatenate([own_ref[...], near_ref[...], far_ref[...]], axis=0)
    row_ref[...] = jnp.dot(
        row_band_ref[...], patch, preferred_element_type=jnp.float32
    ).astype(jnp.bfloat16)
    for k in range(NB):
        window = jnp.concatenate(
            [
                row_ref[k * rows : (k + 1) * rows, b * LANES : (b + 2) * LANES]
                for b in range(blocks)
            ],
            axis=0,
        )
        out = jnp.dot(window, col_band_ref[k], preferred_element_type=jnp.float32)
        conv_ref[k] = out.reshape(blocks, rows, LANES)

    first_col = expo_at * chunk
    xs = [column_positions(first_col, b, width) for b in range(blocks)]

    def fold(x):
        total = x[:8]
        for i in range(8, rows, 8):
            total = total + x[i : i + 8]
        return total

    def moments(at, left, right, count):
        total = [None] * count
        for b in range(blocks):
            term = fold(left(b) * right(b)) if right is not None else fold(left(b))
            for i in range(count):
                total[i] = term if total[i] is None else total[i] + term
                if i < count - 1:
                    term = term * xs[b]
        for i in range(count):
            parts_ref[at + i] = total[i]

    def conv(k):
        return lambda b: conv_ref[k, b]

    def sci(shift):
        return lambda b: image_refs[shift][:, b * LANES : (b + 1) * LANES].astype(jnp.float32)

    blank = jnp.zeros((8, LANES), jnp.float32)
    at = 0
    for j, k in PAIRS:
        moments(at, conv(j), conv(k), 3)
        at += 3
    for k in range(NB):
        moments(at, conv(k), None, 2)
        at += 2
    while at % 8:
        parts_ref[at] = blank
        at += 1
    begin = at
    for shift in range(expos):
        row = at + NU * source(expo_at, shift, expos)
        for k in range(NB):
            moments(row + 2 * k, conv(k), sci(shift), 2)
        moments(row + NU - 1, sci(shift), None, 1)
    at += NU * expos
    weight = jnp.broadcast_to(weight_ref[...] * hits_ref[...].astype(jnp.float32), (8, LANES))
    weight = jnp.where(tile_at == 0, weight, 0.0)
    spot = (
        (lax.broadcasted_iota(jnp.int32, (8, LANES), 0) == 0)
        & (lax.broadcasted_iota(jnp.int32, (8, LANES), 1) == 0)
    )
    for e in range(expos):
        parts_ref[at + e] = jnp.where(spot & (expo_at == e), weight, 0.0)
    at += expos
    while at % 8:
        parts_ref[at] = blank
        at += 1
    ones = jnp.ones((8, LANES), jnp.float32)
    rows_of = []
    for first, last in ((0, begin), (begin, at)):
        lanes = jnp.sum(parts_ref[first:last], axis=1)
        spare = LANES - (last - first)
        if spare:
            lanes = jnp.concatenate([lanes, jnp.zeros((spare, LANES), jnp.float32)], axis=0)
        rows_of.append(
            lax.dot_general(
                ones,
                lanes,
                (((1,), (1,)), ((), ())),
                precision=lax.Precision.HIGHEST,
                preferred_element_type=jnp.float32,
            )
        )
    both = jnp.where(lax.broadcasted_iota(jnp.int32, (8, LANES), 0) < 4, rows_of[0], rows_of[1])
    for i in range(sums_ref.shape[0]):
        sums_ref[i] = both


def table(expos):
    columns = np.zeros((NU + expos + 1, 16), np.int32)
    for at, (j, k) in enumerate(PAIRS):
        for a, b in ((j, k), (k, j)):
            columns[b, a] = 3 * at
            columns[NB + b, a] = columns[b, NB + a] = 3 * at + 1
            columns[NB + b, NB + a] = 3 * at + 2
    for k in range(NB):
        for x in range(2):
            columns[NU - 1, x * NB + k] = columns[x * NB + k, NU - 1] = 3 * len(PAIRS) + 2 * k + x
    for e in range(expos):
        columns[NU + e, :NU] = [NU * e + 2 * k + x for x in range(2) for k in range(NB)] + [NU * e + NU - 1]
        columns[NU + expos, e] = NU * expos + e
    return np.ascontiguousarray(np.broadcast_to(columns[:, :, None], columns.shape + (LANES,)))


def solve_kernel(table_ref, sums_ref, conv_ref, *refs, width, pixels):
    *image_refs, coadd_ref, coeffs_ref, tile_ref, sems = refs
    expo_at = lax.axis_index("expo")
    expos = len(image_refs)
    rows, chunk = coadd_ref.shape
    blocks = chunk // LANES
    sub = lax.broadcasted_iota(jnp.int32, (16, LANES), 0)
    lane = lax.broadcasted_iota(jnp.int32, (16, LANES), 1)
    sums = sums_ref[0]
    for i in range(1, sums_ref.shape[0]):
        sums = sums + sums_ref[i]
    first = jnp.broadcast_to(sums[0:1], (16, LANES))
    second = jnp.broadcast_to(sums[4:5], (16, LANES))

    columns = [
        jnp.take_along_axis(first if j < NU else second, table_ref[j], axis=1) for j in range(NU + expos)
    ]
    spread = jnp.take_along_axis(second, table_ref[NU + expos], axis=1)
    weight = [jnp.broadcast_to(spread[e : e + 1], (16, LANES)) for e in range(expos)]
    columns[NU - 1] = jnp.where(sub == NU - 1, float(pixels), columns[NU - 1])

    trace = columns[0][0:1]
    for j in range(1, NU):
        trace = trace + columns[j][j : j + 1]
    scale = 1.0 / trace
    for j in range(NU + expos):
        columns[j] = columns[j] * scale
        if j < NU:
            columns[j] = columns[j] + jnp.where(sub == j, RIDGE / NU, 0.0)
    for i in range(NU):
        inverse = 1.0 / columns[i][i : i + 1]
        for j in range(i + 1, NU + expos):
            factor = columns[j][i : i + 1] * inverse
            columns[j] = jnp.where(sub == i, factor, columns[j] - columns[i] * factor)

    solved = columns[NU:]
    own = solved[0]
    mixed = weight[0] * solved[0]
    for e in range(1, expos):
        own = jnp.where(expo_at == e, solved[e], own)
        mixed = mixed + weight[e] * solved[e]
    diagonal = (sub == lane) & (sub < NU)
    coeffs_ref[...] = jnp.sum(jnp.where(diagonal, own, 0.0), axis=0, keepdims=True)[:, :NU]
    scale = [jnp.broadcast_to(mixed[u : u + 1], (8, LANES)) for u in range(NU)]
    gains = []
    for shift in range(expos):
        gain = weight[0][:8]
        for e in range(1, expos):
            gain = jnp.where(source(expo_at, shift, expos) == e, weight[e][:8], gain)
        gains.append(gain)
    first_col = expo_at * chunk
    copies = []
    for r in range(0, rows, 8):
        for b in range(blocks):
            at = slice(b * LANES, (b + 1) * LANES)
            x = column_positions(first_col, b, width)
            total = -scale[NU - 1]
            for gain, image_ref in zip(gains, image_refs):
                total = total + gain * image_ref[:, at].astype(jnp.float32)[r : r + 8]
            model = (scale[0] + scale[NB] * x) * conv_ref[0, b, r : r + 8]
            for k in range(1, NB):
                model = model + (scale[k] + scale[NB + k] * x) * conv_ref[k, b, r : r + 8]
            tile_ref[r : r + 8, b * LANES : (b + 1) * LANES] = total - model
        copies.append(
            pltpu.make_async_copy(tile_ref.at[pl.ds(r, 8)], coadd_ref.at[pl.ds(r, 8)], sems.at[r // 8])
        )
        copies[-1].start()
    for copy in copies:
        copy.wait()


def swaps(first, size):
    pairs = [(i, i + 1) for i in range(first, size - 1, 2)]
    if first and size % 2 == 0:
        pairs.append((0, size - 1))
    return [pair for a, b in pairs for pair in ((a, b), (b, a))]


def tiled_device(template, science, plan, orders, coadd_weight, intersection):
    expos = lax.axis_size("expo")
    tiles = lax.axis_size("tile")
    _, rows, width = template.shape
    steps = science.shape[1]
    chunk = width // expos
    ext = chunk + LANES
    blocks = chunk // LANES
    smem = pl.BlockSpec(memory_space=pltpu.SMEM)
    vmem = pl.BlockSpec(memory_space=pltpu.VMEM)
    small = pltpu.CompilerParams(vmem_limit_bytes=16 * 1024 * 1024)
    hbm = pl.BlockSpec(memory_space=pltpu.HBM)
    row_band, col_band = pl.pallas_call(
        functools.partial(band_kernel, tiles=tiles),
        out_shape=(
            jax.ShapeDtypeStruct((NB * rows, 3 * rows), jnp.bfloat16),
            jax.ShapeDtypeStruct((NB, 2 * LANES, LANES), jnp.bfloat16),
        ),
        in_specs=[smem],
        out_specs=(vmem, vmem),
        compiler_params=small,
        cost_estimate=pl.CostEstimate(flops=4_000_000, bytes_accessed=500_000, transcendentals=200_000),
    )(orders)
    coadds = []
    fitted = []
    for step in range(steps):
        *blocks_out, owner = pl.pallas_call(
            functools.partial(send_kernel, step=step),
            out_shape=(pltpu.VMEM((rows, ext), template.dtype),) * (2 * expos)
            + (jax.ShapeDtypeStruct((rows, LANES), jnp.int32),),
            in_specs=[hbm] * 3,
            out_specs=(vmem,) * (2 * expos + 1),
            scratch_shapes=[
                pltpu.VMEM((rows, width + 2 * LANES), template.dtype),
                pltpu.SMEM(plan.shape, jnp.int32),
                pltpu.SemaphoreType.DMA((expos + 3,)),
            ],
            compiler_params=small,
        )(
            pltpu.with_memory_space_constraint(template[0], pltpu.HBM),
            pltpu.with_memory_space_constraint(science[0, step], pltpu.HBM),
            pltpu.with_memory_space_constraint(plan, pltpu.HBM),
        )
        patches, images = blocks_out[:expos], blocks_out[expos:]
        for group in (patches, images):
            for shift in range(1, expos):
                pairs = [(e, int(target(e, shift, expos))) for e in range(expos)]
                group[shift] = lax.ppermute(group[shift], "expo", pairs)
        own = pl.pallas_call(
            pick_kernel,
            out_shape=jax.ShapeDtypeStruct((rows, ext), template.dtype),
            in_specs=[vmem] * (1 + expos),
            out_specs=vmem,
            compiler_params=small,
        )(owner, *(patches[shift] for shift in far_first(expos)))
        far = lax.ppermute(own, "tile", swaps(1, tiles))
        near = lax.ppermute(own, "tile", swaps(0, tiles))
        conv, sums = pl.pallas_call(
            functools.partial(fit_kernel, width=width),
            out_shape=(
                jax.ShapeDtypeStruct((NB, blocks, rows, LANES), jnp.float32),
                jax.ShapeDtypeStruct((tiles * expos, 8, LANES), jnp.float32),
            ),
            in_specs=[vmem] * (7 + expos),
            out_specs=(vmem, vmem),
            scratch_shapes=[
                pltpu.VMEM((NB * rows, ext), jnp.bfloat16),
                pltpu.VMEM((80 + 14 * expos + 8, 8, LANES), jnp.float32),
            ],
            compiler_params=small,
        )(
            coadd_weight[:, step : step + 1],
            intersection[:, step : step + 1],
            row_band,
            col_band,
            own,
            near,
            far,
            *(images[shift] for shift in far_first(expos)),
        )
        sums = lax.all_to_all(sums, ("tile", "expo"), split_axis=0, concat_axis=0, tiled=True)
        coadd, coeffs = pl.pallas_call(
            functools.partial(solve_kernel, width=width, pixels=tiles * rows * width),
            out_shape=(
                jax.ShapeDtypeStruct((rows, chunk), jnp.float32),
                jax.ShapeDtypeStruct((1, NU), jnp.float32),
            ),
            in_specs=[vmem] * (3 + expos),
            out_specs=(pl.BlockSpec(memory_space=pl.ANY), vmem),
            scratch_shapes=[
                pltpu.VMEM((rows, chunk), jnp.float32),
                pltpu.SemaphoreType.DMA((rows // 8,)),
            ],
            compiler_params=small,
        )(jnp.asarray(table(expos)), sums, conv, *images)
        coadds.append(coadd[None])
        fitted.append(coeffs)
    return (jnp.concatenate(coadds), jnp.stack(fitted, axis=1))


def broadcast(block, axis, holder):
    block = jnp.where(lax.axis_index(axis) == holder, block, jnp.zeros_like(block))
    return lax.psum(block, axis)


def extended(x, sides, width):
    for axis, dim in sides:
        size, length = (lax.axis_size(axis), x.shape[dim])
        up = [(i, (i + 1) % size) for i in range(size - 1)]
        down = [(j, i) for i, j in up]
        last = lax.slice_in_dim(x, length - width, length, axis=dim)
        first = lax.slice_in_dim(x, 0, width, axis=dim)
        before = lax.ppermute(last, axis, up)
        after = lax.ppermute(first, axis, down)
        x = jnp.concatenate([before, x, after], axis=dim)
    return x


def make_filters(orders):
    taps_pos = jnp.arange(2 * HALF + 1).astype(jnp.float32) - HALF
    row_list = []
    col_list = []
    for basis in range(NB):
        sigma = SIGMAS[basis]
        envelope = jnp.exp(-taps_pos * taps_pos / (2.0 * sigma * sigma))
        row_filter = envelope * power_of(taps_pos, orders[basis, 0])
        col_filter = envelope * power_of(taps_pos, orders[basis, 1])
        row_list.append(row_filter / jnp.sqrt(jnp.sum(row_filter * row_filter)))
        col_list.append(col_filter / jnp.sqrt(jnp.sum(col_filter * col_filter)))
    return (jnp.stack(row_list).astype(jnp.bfloat16), jnp.stack(col_list).astype(jnp.bfloat16))


def band_matrix(filters, out_len, in_len):
    offset = jnp.arange(in_len)[None, :] - jnp.arange(out_len)[:, None]
    taps_idx = jnp.arange(2 * HALF + 1)
    picks = (offset[:, :, None] == taps_idx[None, None, :]).astype(jnp.float32)
    band = jnp.einsum("ijt,kt->kij", picks, filters.astype(jnp.float32))
    return band.astype(jnp.bfloat16)


def any_device(template, science, plan, orders, coadd_weight, intersection):
    row_filters, col_filters = make_filters(orders)
    rows = template.shape[1]
    width = template.shape[2]
    blocks_count = width // 128
    steps_count = science.shape[1]
    row_band = band_matrix(row_filters, rows, rows + 2 * HALF)
    col_band = jnp.transpose(band_matrix(col_filters, 128, 128 + 2 * HALF), (0, 2, 1))
    column_pos = 2.0 * (jnp.arange(width).astype(jnp.float32) + 0.5) / width - 1.0
    pieces = []
    fitted = []
    for step in range(steps_count):
        received = broadcast(template[0], "expo", plan[step])
        padded = extended(received, (("tile", 0),), HALF)
        rowconv = jnp.einsum(
            "kij,jw->kiw", row_band, padded, preferred_element_type=jnp.float32
        ).astype(jnp.bfloat16)
        blocks = rowconv.reshape(NB, rows, blocks_count, 128)
        empty_rim = jnp.zeros((NB, rows, 1, HALF), jnp.bfloat16)
        previous = jnp.concatenate([empty_rim, blocks[:, :, :-1, 128 - HALF :]], axis=2)
        following = jnp.concatenate([blocks[:, :, 1:, :HALF], empty_rim], axis=2)
        window = jnp.concatenate([previous, blocks, following], axis=3)
        conv = jnp.einsum("krbj,kjc->krbc", window, col_band, preferred_element_type=jnp.float32)
        conv = conv.reshape(NB, rows, width)
        fields = jnp.concatenate(
            [conv, conv * column_pos, jnp.ones((1, rows, width), jnp.float32)], axis=0
        )
        fields = fields.reshape(NU, rows * width)
        exposure_image = science[0, step].astype(jnp.float32).reshape(rows * width)
        normal_local = jnp.dot(fields, fields.T, precision=lax.Precision.HIGHEST)
        project_local = jnp.dot(fields, exposure_image, precision=lax.Precision.HIGHEST)
        normal_matrix, projections = lax.psum((normal_local, project_local), "tile")
        normal_matrix = normal_matrix + RIDGE * (jnp.trace(normal_matrix) / NU) * jnp.eye(
            NU, dtype=jnp.float32
        )
        factor = jnp.linalg.cholesky(normal_matrix)
        coeffs = jax.scipy.linalg.cho_solve((factor, True), projections)
        model = jnp.dot(coeffs, fields, precision=lax.Precision.HIGHEST)
        difference = exposure_image - model
        weight_now = coadd_weight[0, step] * intersection[0, step].astype(jnp.float32)
        pieces.append((weight_now * difference).reshape(rows, width))
        fitted.append(coeffs)
    weighted = jnp.stack(pieces)
    received_parts = lax.all_to_all(weighted[None], "expo", split_axis=3, concat_axis=0, tiled=True)
    coadd = jnp.sum(received_parts, axis=0)
    return (coadd, jnp.stack(fitted)[None])


def per_device(template, science, plan, orders, coadd_weight, intersection):
    expos = lax.axis_size("expo")
    rows, width = template.shape[1:]
    whole_lanes = width % (expos * LANES) == 0 and rows % 16 == 0
    few = (NU + 1) * expos <= LANES and NU + expos <= LANES
    body = tiled_device if whole_lanes and few else any_device
    return body(template, science, plan, orders, coadd_weight, intersection)


def solution(mesh):
    return jax.shard_map(
        per_device,
        mesh=mesh,
        in_specs=(
            P(("groups", "expo"), "tile", None),
            P(("groups", "expo"), None, "tile", None),
            P("groups"),
            P(),
            P(("groups", "expo"), None),
            P(("groups", "expo"), None),
        ),
        out_specs=(P("groups", "tile", "expo"), P(("groups", "expo"), None, None)),
        check_vma=False,
    )
```

```python
import functools

import jax
import jax.numpy as jnp
import numpy as np
from jax import lax
from jax.experimental import pallas as pl
from jax.experimental.pallas import tpu as pltpu
from jax.sharding import PartitionSpec as P

HALF = 15
NB = 6
NU = 13
LANES = 128
BEYOND = 1000
PAIRS = [(j, k) for j in range(NB) for k in range(j, NB)]

SIGMAS = (0.8, 1.4, 2.2, 3.0, 4.0, 5.5)
RIDGE = 0.05


def power_of(pos, order):
    return jnp.where(order == 0, 1.0, jnp.where(order == 1, pos, pos * pos))


def tap_values(pos, sigma, order):
    value = jnp.exp(-pos * pos / (2.0 * sigma * sigma)) * power_of(pos, order)
    return jnp.where(jnp.abs(pos) <= HALF, value, 0.0)


def tap_norm(sigma, order):
    pos = lax.broadcasted_iota(jnp.int32, (8, LANES), 1).astype(jnp.float32) - HALF
    value = tap_values(pos, sigma, order)
    return jnp.sqrt(jnp.sum(value * value, axis=1, keepdims=True))


def target(me, shift, size):
    return me ^ shift if size & (size - 1) == 0 else (me + shift) % size


def source(me, shift, size):
    return me ^ shift if size & (size - 1) == 0 else (me - shift + size) % size


def far_first(size):
    return [*range(size // 2, size), *range(1, size // 2), 0] if size > 1 else [0]


def send_kernel(template_ref, science_ref, plan_ref, orders_ref, *refs, step):
    *out_refs, owner_ref, order_ref, patch_ref, plan_now, orders_now, sems = refs
    size = len(out_refs) // 2
    image_refs = out_refs[size:]
    rows, ext = image_refs[0].shape
    chunk = ext - LANES
    half = size * chunk // 2
    me = lax.axis_index("expo")
    starts = [pl.multiple_of(target(me, shift, size) * chunk, chunk) for shift in range(size)]
    loads = [
        pltpu.make_async_copy(
            template_ref.at[:, pl.ds(i * half, half)], patch_ref.at[:, pl.ds((i * half + LANES), half)], sems.at[i]
        )
        for i in range(2)
    ]
    copies = [
        pltpu.make_async_copy(
            science_ref.at[:, pl.ds(starts[shift], chunk)],
            image_refs[shift].at[:, pl.ds(0, chunk)],
            sems.at[3 + shift],
        )
        for shift in range(size)
    ]
    copies.append(pltpu.make_async_copy(plan_ref, plan_now, sems.at[2]))
    copies.append(pltpu.make_async_copy(orders_ref, orders_now, sems.at[3 + size]))
    for copy in loads + copies:
        copy.start()
    blank = jnp.zeros((rows, LANES), patch_ref.dtype)
    patch_ref[:, :LANES] = blank
    patch_ref[:, size * chunk + LANES :] = blank
    for image_ref in image_refs:
        image_ref[:, chunk:] = blank
    for copy in loads:
        copy.wait()
    lane = lax.broadcasted_iota(jnp.int32, (rows, LANES), 1)
    for shift in range(size):
        start = starts[shift]
        out_refs[shift][:, :chunk] = patch_ref[:, pl.ds(start + LANES, chunk)]
        before = patch_ref[:, pl.ds(start, LANES)].astype(jnp.float32)
        after = patch_ref[:, pl.ds(start + chunk + LANES, LANES)].astype(jnp.float32)
        rim = jnp.where(lane < LANES // 2, after, before)
        out_refs[shift][:, chunk:] = rim.astype(patch_ref.dtype)
    for copy in copies:
        copy.wait()
    owner_ref[...] = jnp.full(owner_ref.shape, plan_now[step], jnp.int32)
    for way in range(2):
        for k in range(NB):
            order_ref[way, k] = jnp.full((8, LANES), orders_now[way, k], jnp.int32)


def pick_kernel(owner_ref, *refs):
    *recv_refs, out_ref = refs
    rows, ext = out_ref.shape
    size = len(recv_refs)
    recv_refs = dict(zip(far_first(size), recv_refs))
    me = lax.axis_index("expo")
    blocks = []
    for b in range(ext // LANES):
        columns = slice(b * LANES, (b + 1) * LANES)
        block = recv_refs[0][:, columns].astype(jnp.float32)
        for shift in range(1, size):
            block = jnp.where(
                owner_ref[...] == source(me, shift, size), recv_refs[shift][:, columns].astype(jnp.float32), block
            )
        blocks.append(block.astype(out_ref.dtype))
    whole = jnp.concatenate(blocks[-1:] + blocks, axis=1)
    out_ref[...] = whole[:, LANES - HALF : LANES - HALF + ext]


def column_positions(first_col, block, width):
    col = lax.broadcasted_iota(jnp.int32, (8, LANES), 1) + (first_col + block * LANES)
    return 2.0 * (col.astype(jnp.float32) + 0.5) / width - 1.0


def band_kernel(order_ref, _, row_ref, col_ref, *, tiles):
    rows = row_ref.shape[0] // NB
    tile_at = lax.axis_index("tile")
    near = 1 - 2 * lax.rem(tile_at, 2)
    near_move = jnp.where(tile_at + near < tiles, near - 1, BEYOND)
    far_move = jnp.where((tile_at >= near) & (tile_at - near < tiles), -near - 2, BEYOND)
    row_from = lax.broadcasted_iota(jnp.int32, (8, LANES), 1)
    moved = jnp.where(row_from < rows, 0, jnp.where(row_from < 2 * rows, near_move, far_move))
    sub = lax.broadcasted_iota(jnp.int32, (8, LANES), 0)
    lane = lax.broadcasted_iota(jnp.int32, (8, LANES), 1)
    shift = (sub - jnp.where(lane < LANES // 2, lane, lane - LANES) - HALF).astype(jnp.float32)
    for k in range(NB):
        norm = tap_norm(SIGMAS[k], order_ref[0, k])
        for r in range(0, rows, 16):
            parts = []
            for half in (r, r + 8):
                offset = (row_from + moved * rows - sub - half).astype(jnp.float32)
                parts.append(tap_values(offset, SIGMAS[k], order_ref[0, k]) / norm)
            both = jnp.concatenate(parts, axis=0).astype(jnp.bfloat16)
            row_ref[k * rows + r : k * rows + r + 16] = both[:, : 3 * rows]
        norm = tap_norm(SIGMAS[k], order_ref[1, k])
        pattern = tap_values(shift, SIGMAS[k], order_ref[1, k]) / norm
        for r in range(0, 2 * LANES, 16):
            parts = []
            for half in (r, r + 8):
                moved_on = pltpu.roll(pattern, half % LANES, 1) if half % LANES else pattern
                inside = lane <= half + 7 if half < LANES else lane >= half - LANES + LANES // 2
                parts.append(jnp.where(inside, moved_on, 0.0))
            col_ref[k, r : r + 16] = jnp.concatenate(parts, axis=0).astype(jnp.bfloat16)


def fit_kernel(weight_ref, hits_ref, row_band_ref, col_band_ref, own_ref, near_ref, far_ref, *refs, width):
    *image_refs, conv_ref, sums_ref, row_ref, parts_ref = refs
    image_refs = dict(zip(far_first(len(image_refs)), image_refs))
    tile_at = lax.axis_index("tile")
    expo_at = lax.axis_index("expo")
    rows, ext = own_ref.shape
    expos = len(image_refs)
    chunk = ext - LANES
    blocks = chunk // LANES

    patch = jnp.concatenate([own_ref[...], near_ref[...], far_ref[...]], axis=0)
    row_ref[...] = jnp.dot(
        row_band_ref[...], patch, preferred_element_type=jnp.float32
    ).astype(jnp.bfloat16)
    for k in range(NB):
        window = jnp.concatenate(
            [
                row_ref[k * rows : (k + 1) * rows, b * LANES : (b + 2) * LANES]
                for b in range(blocks)
            ],
            axis=0,
        )
        out = jnp.dot(window, col_band_ref[k], preferred_element_type=jnp.float32)
        conv_ref[k] = out.reshape(blocks, rows, LANES)

    first_col = expo_at * chunk
    xs = [column_positions(first_col, b, width) for b in range(blocks)]

    def fold(x):
        total = x[:8]
        for i in range(8, rows, 8):
            total = total + x[i : i + 8]
        return total

    def moments(at, left, right, count):
        total = [None] * count
        for b in range(blocks):
            term = fold(left(b) * right(b)) if right is not None else fold(left(b))
            for i in range(count):
                total[i] = term if total[i] is None else total[i] + term
                if i < count - 1:
                    term = term * xs[b]
        for i in range(count):
            parts_ref[at + i] = total[i]

    def conv(k):
        return lambda b: conv_ref[k, b]

    def sci(shift):
        return lambda b: image_refs[shift][:, b * LANES : (b + 1) * LANES].astype(jnp.float32)

    blank = jnp.zeros((8, LANES), jnp.float32)
    at = 0
    for j, k in PAIRS:
        moments(at, conv(j), conv(k), 3)
        at += 3
    for k in range(NB):
        moments(at, conv(k), None, 2)
        at += 2
    while at % 8:
        parts_ref[at] = blank
        at += 1
    begin = at
    for shift in range(expos):
        row = at + NU * source(expo_at, shift, expos)
        for k in range(NB):
            moments(row + 2 * k, conv(k), sci(shift), 2)
        moments(row + NU - 1, sci(shift), None, 1)
    at += NU * expos
    weight = jnp.broadcast_to(weight_ref[...] * hits_ref[...].astype(jnp.float32), (8, LANES))
    weight = jnp.where(tile_at == 0, weight, 0.0)
    spot = (
        (lax.broadcasted_iota(jnp.int32, (8, LANES), 0) == 0)
        & (lax.broadcasted_iota(jnp.int32, (8, LANES), 1) == 0)
    )
    for e in range(expos):
        parts_ref[at + e] = jnp.where(spot & (expo_at == e), weight, 0.0)
    at += expos
    while at % 8:
        parts_ref[at] = blank
        at += 1
    ones = jnp.ones((8, LANES), jnp.float32)
    rows_of = []
    for first, last in ((0, begin), (begin, at)):
        lanes = jnp.sum(parts_ref[first:last], axis=1)
        spare = LANES - (last - first)
        if spare:
            lanes = jnp.concatenate([lanes, jnp.zeros((spare, LANES), jnp.float32)], axis=0)
        rows_of.append(
            lax.dot_general(
                ones,
                lanes,
                (((1,), (1,)), ((), ())),
                precision=lax.Precision.HIGHEST,
                preferred_element_type=jnp.float32,
            )
        )
    both = jnp.where(lax.broadcasted_iota(jnp.int32, (8, LANES), 0) < 4, rows_of[0], rows_of[1])
    for i in range(sums_ref.shape[0]):
        sums_ref[i] = both


def table(expos):
    columns = np.zeros((NU + expos + 1, 16), np.int32)
    for at, (j, k) in enumerate(PAIRS):
        for a, b in ((j, k), (k, j)):
            columns[b, a] = 3 * at
            columns[NB + b, a] = columns[b, NB + a] = 3 * at + 1
            columns[NB + b, NB + a] = 3 * at + 2
    for k in range(NB):
        for x in range(2):
            columns[NU - 1, x * NB + k] = columns[x * NB + k, NU - 1] = 3 * len(PAIRS) + 2 * k + x
    for e in range(expos):
        columns[NU + e, :NU] = [NU * e + 2 * k + x for x in range(2) for k in range(NB)] + [NU * e + NU - 1]
        columns[NU + expos, e] = NU * expos + e
    return np.ascontiguousarray(np.broadcast_to(columns[:, :, None], columns.shape + (LANES,)))


def solve_kernel(table_ref, sums_ref, conv_ref, *refs, width, pixels):
    *image_refs, coadd_ref, coeffs_ref, tile_ref, sems = refs
    expo_at = lax.axis_index("expo")
    expos = len(image_refs)
    rows, chunk = coadd_ref.shape
    blocks = chunk // LANES
    sub = lax.broadcasted_iota(jnp.int32, (16, LANES), 0)
    lane = lax.broadcasted_iota(jnp.int32, (16, LANES), 1)
    sums = sums_ref[0]
    for i in range(1, sums_ref.shape[0]):
        sums = sums + sums_ref[i]
    first = jnp.broadcast_to(sums[0:1], (16, LANES))
    second = jnp.broadcast_to(sums[4:5], (16, LANES))

    columns = [
        jnp.take_along_axis(first if j < NU else second, table_ref[j], axis=1) for j in range(NU + expos)
    ]
    spread = jnp.take_along_axis(second, table_ref[NU + expos], axis=1)
    weight = [jnp.broadcast_to(spread[e : e + 1], (16, LANES)) for e in range(expos)]
    columns[NU - 1] = jnp.where(sub == NU - 1, float(pixels), columns[NU - 1])

    trace = columns[0][0:1]
    for j in range(1, NU):
        trace = trace + columns[j][j : j + 1]
    scale = 1.0 / trace
    for j in range(NU + expos):
        columns[j] = columns[j] * scale
        if j < NU:
            columns[j] = columns[j] + jnp.where(sub == j, RIDGE / NU, 0.0)
    for i in range(NU):
        inverse = 1.0 / columns[i][i : i + 1]
        for j in range(i + 1, NU + expos):
            factor = columns[j][i : i + 1] * inverse
            columns[j] = jnp.where(sub == i, factor, columns[j] - columns[i] * factor)

    solved = columns[NU:]
    own = solved[0]
    mixed = weight[0] * solved[0]
    for e in range(1, expos):
        own = jnp.where(expo_at == e, solved[e], own)
        mixed = mixed + weight[e] * solved[e]
    diagonal = (sub == lane) & (sub < NU)
    coeffs_ref[...] = jnp.sum(jnp.where(diagonal, own, 0.0), axis=0, keepdims=True)[:, :NU]
    scale = [jnp.broadcast_to(mixed[u : u + 1], (8, LANES)) for u in range(NU)]
    gains = []
    for shift in range(expos):
        gain = weight[0][:8]
        for e in range(1, expos):
            gain = jnp.where(source(expo_at, shift, expos) == e, weight[e][:8], gain)
        gains.append(gain)
    first_col = expo_at * chunk
    copies = []
    for r in range(0, rows, 8):
        for b in range(blocks):
            at = slice(b * LANES, (b + 1) * LANES)
            x = column_positions(first_col, b, width)
            total = -scale[NU - 1]
            for gain, image_ref in zip(gains, image_refs):
                total = total + gain * image_ref[:, at].astype(jnp.float32)[r : r + 8]
            model = (scale[0] + scale[NB] * x) * conv_ref[0, b, r : r + 8]
            for k in range(1, NB):
                model = model + (scale[k] + scale[NB + k] * x) * conv_ref[k, b, r : r + 8]
            tile_ref[r : r + 8, b * LANES : (b + 1) * LANES] = total - model
        copies.append(
            pltpu.make_async_copy(tile_ref.at[pl.ds(r, 8)], coadd_ref.at[pl.ds(r, 8)], sems.at[r // 8])
        )
        copies[-1].start()
    for copy in copies:
        copy.wait()


def swaps(first, size):
    pairs = [(i, i + 1) for i in range(first, size - 1, 2)]
    if first and size % 2 == 0:
        pairs.append((0, size - 1))
    return [pair for a, b in pairs for pair in ((a, b), (b, a))]


def tiled_device(template, science, plan, orders, coadd_weight, intersection):
    expos = lax.axis_size("expo")
    tiles = lax.axis_size("tile")
    _, rows, width = template.shape
    steps = science.shape[1]
    chunk = width // expos
    ext = chunk + LANES
    blocks = chunk // LANES
    vmem = pl.BlockSpec(memory_space=pltpu.VMEM)
    small = pltpu.CompilerParams(vmem_limit_bytes=16 * 1024 * 1024)
    hbm = pl.BlockSpec(memory_space=pltpu.HBM)
    coadds = []
    fitted = []
    for step in range(steps):
        *blocks_out, owner, order = pl.pallas_call(
            functools.partial(send_kernel, step=step),
            out_shape=(pltpu.VMEM((rows, ext), template.dtype),) * (2 * expos)
            + (
                jax.ShapeDtypeStruct((rows, LANES), jnp.int32),
                jax.ShapeDtypeStruct((2, NB, 8, LANES), jnp.int32),
            ),
            in_specs=[hbm] * 4,
            out_specs=(vmem,) * (2 * expos + 2),
            scratch_shapes=[
                pltpu.VMEM((rows, width + 2 * LANES), template.dtype),
                pltpu.SMEM(plan.shape, jnp.int32),
                pltpu.SMEM((2, NB), jnp.int32),
                pltpu.SemaphoreType.DMA((expos + 4,)),
            ],
            compiler_params=small,
        )(
            pltpu.with_memory_space_constraint(template[0], pltpu.HBM),
            pltpu.with_memory_space_constraint(science[0, step], pltpu.HBM),
            pltpu.with_memory_space_constraint(plan, pltpu.HBM),
            pltpu.with_memory_space_constraint(orders.T, pltpu.HBM),
        )
        patches, images = blocks_out[:expos], blocks_out[expos:]
        for group in (patches, images):
            for shift in range(1, expos):
                pairs = [(e, int(target(e, shift, expos))) for e in range(expos)]
                group[shift] = lax.ppermute(group[shift], "expo", pairs)
        own = pl.pallas_call(
            pick_kernel,
            out_shape=jax.ShapeDtypeStruct((rows, ext), template.dtype),
            in_specs=[vmem] * (1 + expos),
            out_specs=vmem,
            compiler_params=small,
        )(owner, *(patches[shift] for shift in far_first(expos)))
        row_band, col_band = pl.pallas_call(
            functools.partial(band_kernel, tiles=tiles),
            out_shape=(
                jax.ShapeDtypeStruct((NB * rows, 3 * rows), jnp.bfloat16),
                jax.ShapeDtypeStruct((NB, 2 * LANES, LANES), jnp.bfloat16),
            ),
            in_specs=[vmem, pl.BlockSpec(memory_space=pl.ANY)],
            out_specs=(vmem, vmem),
            compiler_params=small,
            cost_estimate=pl.CostEstimate(flops=4_000_000, bytes_accessed=500_000, transcendentals=200_000),
        )(order, own)
        far = lax.ppermute(own, "tile", swaps(1, tiles))
        near = lax.ppermute(own, "tile", swaps(0, tiles))
        conv, sums = pl.pallas_call(
            functools.partial(fit_kernel, width=width),
            out_shape=(
                jax.ShapeDtypeStruct((NB, blocks, rows, LANES), jnp.float32),
                jax.ShapeDtypeStruct((tiles * expos, 8, LANES), jnp.float32),
            ),
            in_specs=[vmem] * (7 + expos),
            out_specs=(vmem, vmem),
            scratch_shapes=[
                pltpu.VMEM((NB * rows, ext), jnp.bfloat16),
                pltpu.VMEM((80 + 14 * expos + 8, 8, LANES), jnp.float32),
            ],
            compiler_params=small,
        )(
            coadd_weight[:, step : step + 1],
            intersection[:, step : step + 1],
            row_band,
            col_band,
            own,
            near,
            far,
            *(images[shift] for shift in far_first(expos)),
        )
        sums = lax.all_to_all(sums, ("tile", "expo"), split_axis=0, concat_axis=0, tiled=True)
        coadd, coeffs = pl.pallas_call(
            functools.partial(solve_kernel, width=width, pixels=tiles * rows * width),
            out_shape=(
                jax.ShapeDtypeStruct((rows, chunk), jnp.float32),
                jax.ShapeDtypeStruct((1, NU), jnp.float32),
            ),
            in_specs=[vmem] * (3 + expos),
            out_specs=(pl.BlockSpec(memory_space=pl.ANY), vmem),
            scratch_shapes=[
                pltpu.VMEM((rows, chunk), jnp.float32),
                pltpu.SemaphoreType.DMA((rows // 8,)),
            ],
            compiler_params=small,
        )(jnp.asarray(table(expos)), sums, conv, *images)
        coadds.append(coadd[None])
        fitted.append(coeffs)
    return (jnp.concatenate(coadds), jnp.stack(fitted, axis=1))


def broadcast(block, axis, holder):
    block = jnp.where(lax.axis_index(axis) == holder, block, jnp.zeros_like(block))
    return lax.psum(block, axis)


def extended(x, sides, width):
    for axis, dim in sides:
        size, length = (lax.axis_size(axis), x.shape[dim])
        up = [(i, (i + 1) % size) for i in range(size - 1)]
        down = [(j, i) for i, j in up]
        last = lax.slice_in_dim(x, length - width, length, axis=dim)
        first = lax.slice_in_dim(x, 0, width, axis=dim)
        before = lax.ppermute(last, axis, up)
        after = lax.ppermute(first, axis, down)
        x = jnp.concatenate([before, x, after], axis=dim)
    return x


def make_filters(orders):
    taps_pos = jnp.arange(2 * HALF + 1).astype(jnp.float32) - HALF
    row_list = []
    col_list = []
    for basis in range(NB):
        sigma = SIGMAS[basis]
        envelope = jnp.exp(-taps_pos * taps_pos / (2.0 * sigma * sigma))
        row_filter = envelope * power_of(taps_pos, orders[basis, 0])
        col_filter = envelope * power_of(taps_pos, orders[basis, 1])
        row_list.append(row_filter / jnp.sqrt(jnp.sum(row_filter * row_filter)))
        col_list.append(col_filter / jnp.sqrt(jnp.sum(col_filter * col_filter)))
    return (jnp.stack(row_list).astype(jnp.bfloat16), jnp.stack(col_list).astype(jnp.bfloat16))


def band_matrix(filters, out_len, in_len):
    offset = jnp.arange(in_len)[None, :] - jnp.arange(out_len)[:, None]
    taps_idx = jnp.arange(2 * HALF + 1)
    picks = (offset[:, :, None] == taps_idx[None, None, :]).astype(jnp.float32)
    band = jnp.einsum("ijt,kt->kij", picks, filters.astype(jnp.float32))
    return band.astype(jnp.bfloat16)


def any_device(template, science, plan, orders, coadd_weight, intersection):
    row_filters, col_filters = make_filters(orders)
    rows = template.shape[1]
    width = template.shape[2]
    blocks_count = width // 128
    steps_count = science.shape[1]
    row_band = band_matrix(row_filters, rows, rows + 2 * HALF)
    col_band = jnp.transpose(band_matrix(col_filters, 128, 128 + 2 * HALF), (0, 2, 1))
    column_pos = 2.0 * (jnp.arange(width).astype(jnp.float32) + 0.5) / width - 1.0
    pieces = []
    fitted = []
    for step in range(steps_count):
        received = broadcast(template[0], "expo", plan[step])
        padded = extended(received, (("tile", 0),), HALF)
        rowconv = jnp.einsum(
            "kij,jw->kiw", row_band, padded, preferred_element_type=jnp.float32
        ).astype(jnp.bfloat16)
        blocks = rowconv.reshape(NB, rows, blocks_count, 128)
        empty_rim = jnp.zeros((NB, rows, 1, HALF), jnp.bfloat16)
        previous = jnp.concatenate([empty_rim, blocks[:, :, :-1, 128 - HALF :]], axis=2)
        following = jnp.concatenate([blocks[:, :, 1:, :HALF], empty_rim], axis=2)
        window = jnp.concatenate([previous, blocks, following], axis=3)
        conv = jnp.einsum("krbj,kjc->krbc", window, col_band, preferred_element_type=jnp.float32)
        conv = conv.reshape(NB, rows, width)
        fields = jnp.concatenate(
            [conv, conv * column_pos, jnp.ones((1, rows, width), jnp.float32)], axis=0
        )
        fields = fields.reshape(NU, rows * width)
        exposure_image = science[0, step].astype(jnp.float32).reshape(rows * width)
        normal_local = jnp.dot(fields, fields.T, precision=lax.Precision.HIGHEST)
        project_local = jnp.dot(fields, exposure_image, precision=lax.Precision.HIGHEST)
        normal_matrix, projections = lax.psum((normal_local, project_local), "tile")
        normal_matrix = normal_matrix + RIDGE * (jnp.trace(normal_matrix) / NU) * jnp.eye(
            NU, dtype=jnp.float32
        )
        factor = jnp.linalg.cholesky(normal_matrix)
        coeffs = jax.scipy.linalg.cho_solve((factor, True), projections)
        model = jnp.dot(coeffs, fields, precision=lax.Precision.HIGHEST)
        difference = exposure_image - model
        weight_now = coadd_weight[0, step] * intersection[0, step].astype(jnp.float32)
        pieces.append((weight_now * difference).reshape(rows, width))
        fitted.append(coeffs)
    weighted = jnp.stack(pieces)
    received_parts = lax.all_to_all(weighted[None], "expo", split_axis=3, concat_axis=0, tiled=True)
    coadd = jnp.sum(received_parts, axis=0)
    return (coadd, jnp.stack(fitted)[None])


def per_device(template, science, plan, orders, coadd_weight, intersection):
    expos = lax.axis_size("expo")
    rows, width = template.shape[1:]
    whole_lanes = width % (expos * LANES) == 0 and rows % 16 == 0 and 3 * rows <= LANES
    few = (NU + 1) * expos <= LANES and NU + expos <= LANES
    body = tiled_device if whole_lanes and few else any_device
    return body(template, science, plan, orders, coadd_weight, intersection)


def solution(mesh):
    return jax.shard_map(
        per_device,
        mesh=mesh,
        in_specs=(
            P(("groups", "expo"), "tile", None),
            P(("groups", "expo"), None, "tile", None),
            P("groups"),
            P(),
            P(("groups", "expo"), None),
            P(("groups", "expo"), None),
        ),
        out_specs=(P("groups", "tile", "expo"), P(("groups", "expo"), None, None)),
        check_vma=False,
    )
```

```python
import functools

import jax
import jax.numpy as jnp
import numpy as np
from jax import lax
from jax.experimental import pallas as pl
from jax.experimental.pallas import tpu as pltpu
from jax.sharding import PartitionSpec as P

HALF = 15
NB = 6
NU = 13
LANES = 128
BEYOND = 1000
PAIRS = [(j, k) for j in range(NB) for k in range(j, NB)]

SIGMAS = (0.8, 1.4, 2.2, 3.0, 4.0, 5.5)
RIDGE = 0.05


def power_of(pos, order):
    return jnp.where(order == 0, 1.0, jnp.where(order == 1, pos, pos * pos))


def tap_values(pos, sigma, order):
    value = jnp.exp(-pos * pos / (2.0 * sigma * sigma)) * power_of(pos, order)
    return jnp.where(jnp.abs(pos) <= HALF, value, 0.0)


def tap_norm(sigma, order):
    pos = lax.broadcasted_iota(jnp.int32, (8, LANES), 1).astype(jnp.float32) - HALF
    value = tap_values(pos, sigma, order)
    return jnp.sqrt(jnp.sum(value * value, axis=1, keepdims=True))


def target(me, shift, size):
    return me ^ shift if size & (size - 1) == 0 else (me + shift) % size


def source(me, shift, size):
    return me ^ shift if size & (size - 1) == 0 else (me - shift + size) % size


def far_first(size):
    return [*range(size // 2, size), *range(1, size // 2), 0] if size > 1 else [0]


def send_kernel(template_ref, science_ref, plan_ref, orders_ref, *refs, step):
    *out_refs, owner_ref, order_ref, patch_ref, plan_now, orders_now, sems = refs
    size = len(out_refs) // 2
    image_refs = out_refs[size:]
    rows, ext = out_refs[0].shape
    chunk = ext - LANES
    half = size * chunk // 2
    me = lax.axis_index("expo")
    starts = [pl.multiple_of(target(me, shift, size) * chunk, chunk) for shift in range(size)]
    loads = [
        pltpu.make_async_copy(
            template_ref.at[:, pl.ds(i * half, half)], patch_ref.at[:, pl.ds((i * half + LANES), half)], sems.at[i]
        )
        for i in range(2)
    ]
    copies = [
        pltpu.make_async_copy(
            science_ref.at[:, pl.ds(starts[shift], chunk)],
            image_refs[shift].at[:, pl.ds(0, chunk)],
            sems.at[3 + shift],
        )
        for shift in range(size)
    ]
    copies.append(pltpu.make_async_copy(plan_ref, plan_now, sems.at[2]))
    copies.append(pltpu.make_async_copy(orders_ref, orders_now, sems.at[3 + size]))
    for copy in loads + copies:
        copy.start()
    blank = jnp.zeros((rows, LANES), patch_ref.dtype)
    patch_ref[:, :LANES] = blank
    patch_ref[:, size * chunk + LANES :] = blank
    for image_ref in image_refs:
        if image_ref.shape[1] > chunk:
            image_ref[:, chunk:] = blank
    for copy in loads:
        copy.wait()
    lane = lax.broadcasted_iota(jnp.int32, (rows, LANES), 1)
    for shift in range(size):
        start = starts[shift]
        out_refs[shift][:, :chunk] = patch_ref[:, pl.ds(start + LANES, chunk)]
        before = patch_ref[:, pl.ds(start, LANES)].astype(jnp.float32)
        after = patch_ref[:, pl.ds(start + chunk + LANES, LANES)].astype(jnp.float32)
        rim = jnp.where(lane < LANES // 2, after, before)
        out_refs[shift][:, chunk:] = rim.astype(patch_ref.dtype)
    for copy in copies:
        copy.wait()
    owner_ref[...] = jnp.full(owner_ref.shape, plan_now[step], jnp.int32)
    for way in range(2):
        for k in range(NB):
            order_ref[way, k] = jnp.full((8, LANES), orders_now[way, k], jnp.int32)


def pick_kernel(owner_ref, *refs):
    *recv_refs, out_ref = refs
    rows, ext = out_ref.shape
    size = len(recv_refs)
    recv_refs = dict(zip(far_first(size), recv_refs))
    me = lax.axis_index("expo")
    blocks = []
    for b in range(ext // LANES):
        columns = slice(b * LANES, (b + 1) * LANES)
        block = recv_refs[0][:, columns].astype(jnp.float32)
        for shift in range(1, size):
            block = jnp.where(
                owner_ref[...] == source(me, shift, size), recv_refs[shift][:, columns].astype(jnp.float32), block
            )
        blocks.append(block.astype(out_ref.dtype))
    whole = jnp.concatenate(blocks[-1:] + blocks, axis=1)
    out_ref[...] = whole[:, LANES - HALF : LANES - HALF + ext]


def column_positions(first_col, block, width):
    col = lax.broadcasted_iota(jnp.int32, (8, LANES), 1) + (first_col + block * LANES)
    return 2.0 * (col.astype(jnp.float32) + 0.5) / width - 1.0


def band_kernel(order_ref, _, row_ref, col_ref, *, tiles):
    rows = row_ref.shape[0] // NB
    tile_at = lax.axis_index("tile")
    near = 1 - 2 * lax.rem(tile_at, 2)
    near_move = jnp.where(tile_at + near < tiles, near - 1, BEYOND)
    far_move = jnp.where((tile_at >= near) & (tile_at - near < tiles), -near - 2, BEYOND)
    row_from = lax.broadcasted_iota(jnp.int32, (8, LANES), 1)
    moved = jnp.where(row_from < rows, 0, jnp.where(row_from < 2 * rows, near_move, far_move))
    sub = lax.broadcasted_iota(jnp.int32, (8, LANES), 0)
    lane = lax.broadcasted_iota(jnp.int32, (8, LANES), 1)
    shift = (sub - jnp.where(lane < LANES // 2, lane, lane - LANES) - HALF).astype(jnp.float32)
    for k in range(NB):
        norm = tap_norm(SIGMAS[k], order_ref[0, k])
        for r in range(0, rows, 16):
            parts = []
            for half in (r, r + 8):
                offset = (row_from + moved * rows - sub - half).astype(jnp.float32)
                parts.append(tap_values(offset, SIGMAS[k], order_ref[0, k]) / norm)
            both = jnp.concatenate(parts, axis=0).astype(jnp.bfloat16)
            row_ref[k * rows + r : k * rows + r + 16] = both[:, : 3 * rows]
        norm = tap_norm(SIGMAS[k], order_ref[1, k])
        pattern = tap_values(shift, SIGMAS[k], order_ref[1, k]) / norm
        for r in range(0, 2 * LANES, 16):
            parts = []
            for half in (r, r + 8):
                moved_on = pltpu.roll(pattern, half % LANES, 1) if half % LANES else pattern
                inside = lane <= half + 7 if half < LANES else lane >= half - LANES + LANES // 2
                parts.append(jnp.where(inside, moved_on, 0.0))
            col_ref[k, r : r + 16] = jnp.concatenate(parts, axis=0).astype(jnp.bfloat16)


def fit_kernel(weight_ref, row_band_ref, col_band_ref, own_ref, near_ref, far_ref, *refs, width):
    *image_refs, conv_ref, sums_ref, row_ref, parts_ref = refs
    image_refs = dict(zip(far_first(len(image_refs)), image_refs))
    tile_at = lax.axis_index("tile")
    expo_at = lax.axis_index("expo")
    rows, ext = own_ref.shape
    expos = len(image_refs)
    chunk = ext - LANES
    blocks = chunk // LANES

    patch = jnp.concatenate([own_ref[...], near_ref[...], far_ref[...]], axis=0)
    row_ref[...] = jnp.dot(
        row_band_ref[...], patch, preferred_element_type=jnp.float32
    ).astype(jnp.bfloat16)
    for k in range(NB):
        window = jnp.concatenate(
            [
                row_ref[k * rows : (k + 1) * rows, b * LANES : (b + 2) * LANES]
                for b in range(blocks)
            ],
            axis=0,
        )
        out = jnp.dot(window, col_band_ref[k], preferred_element_type=jnp.float32)
        conv_ref[k] = out.reshape(blocks, rows, LANES)

    first_col = expo_at * chunk
    xs = [column_positions(first_col, b, width) for b in range(blocks)]

    def fold(x):
        total = x[:8]
        for i in range(8, rows, 8):
            total = total + x[i : i + 8]
        return total

    def moments(at, left, right, count):
        total = [None] * count
        for b in range(blocks):
            term = fold(left(b) * right(b)) if right is not None else fold(left(b))
            for i in range(count):
                total[i] = term if total[i] is None else total[i] + term
                if i < count - 1:
                    term = term * xs[b]
        for i in range(count):
            parts_ref[at + i] = total[i]

    def conv(k):
        return lambda b: conv_ref[k, b]

    def sci(shift):
        return lambda b: image_refs[shift][:, b * LANES : (b + 1) * LANES].astype(jnp.float32)

    blank = jnp.zeros((8, LANES), jnp.float32)
    at = 0
    for j, k in PAIRS:
        moments(at, conv(j), conv(k), 3)
        at += 3
    for k in range(NB):
        moments(at, conv(k), None, 2)
        at += 2
    while at % 8:
        parts_ref[at] = blank
        at += 1
    begin = at
    for shift in range(expos):
        row = at + NU * source(expo_at, shift, expos)
        for k in range(NB):
            moments(row + 2 * k, conv(k), sci(shift), 2)
        moments(row + NU - 1, sci(shift), None, 1)
    at += NU * expos
    weight = jnp.where(tile_at == 0, jnp.broadcast_to(weight_ref[...], (8, LANES)), 0.0)
    spot = (
        (lax.broadcasted_iota(jnp.int32, (8, LANES), 0) == 0)
        & (lax.broadcasted_iota(jnp.int32, (8, LANES), 1) == 0)
    )
    for e in range(expos):
        parts_ref[at + e] = jnp.where(spot & (expo_at == e), weight, 0.0)
    at += expos
    while at % 8:
        parts_ref[at] = blank
        at += 1
    ones = jnp.ones((8, LANES), jnp.float32)
    rows_of = []
    for first, last in ((0, begin), (begin, at)):
        lanes = jnp.sum(parts_ref[first:last], axis=1)
        spare = LANES - (last - first)
        if spare:
            lanes = jnp.concatenate([lanes, jnp.zeros((spare, LANES), jnp.float32)], axis=0)
        rows_of.append(
            lax.dot_general(
                ones,
                lanes,
                (((1,), (1,)), ((), ())),
                precision=lax.Precision.HIGHEST,
                preferred_element_type=jnp.float32,
            )
        )
    both = jnp.where(lax.broadcasted_iota(jnp.int32, (8, LANES), 0) < 4, rows_of[0], rows_of[1])
    for i in range(sums_ref.shape[0]):
        sums_ref[i] = both


def table(expos):
    columns = np.zeros((NU + expos + 1, 16), np.int32)
    for at, (j, k) in enumerate(PAIRS):
        for a, b in ((j, k), (k, j)):
            columns[b, a] = 3 * at
            columns[NB + b, a] = columns[b, NB + a] = 3 * at + 1
            columns[NB + b, NB + a] = 3 * at + 2
    for k in range(NB):
        for x in range(2):
            columns[NU - 1, x * NB + k] = columns[x * NB + k, NU - 1] = 3 * len(PAIRS) + 2 * k + x
    for e in range(expos):
        columns[NU + e, :NU] = [NU * e + 2 * k + x for x in range(2) for k in range(NB)] + [NU * e + NU - 1]
        columns[NU + expos, e] = NU * expos + e
    return np.ascontiguousarray(np.broadcast_to(columns[:, :, None], columns.shape + (LANES,)))


def solve_kernel(table_ref, sums_ref, conv_ref, *refs, width, pixels):
    *image_refs, coadd_ref, coeffs_ref, tile_ref, sems = refs
    expo_at = lax.axis_index("expo")
    expos = len(image_refs)
    rows, chunk = coadd_ref.shape
    blocks = chunk // LANES
    sub = lax.broadcasted_iota(jnp.int32, (16, LANES), 0)
    lane = lax.broadcasted_iota(jnp.int32, (16, LANES), 1)
    sums = sums_ref[0]
    for i in range(1, sums_ref.shape[0]):
        sums = sums + sums_ref[i]
    first = jnp.broadcast_to(sums[0:1], (16, LANES))
    second = jnp.broadcast_to(sums[4:5], (16, LANES))

    columns = [
        jnp.take_along_axis(first if j < NU else second, table_ref[j], axis=1) for j in range(NU + expos)
    ]
    spread = jnp.take_along_axis(second, table_ref[NU + expos], axis=1)
    weight = [jnp.broadcast_to(spread[e : e + 1], (16, LANES)) for e in range(expos)]
    columns[NU - 1] = jnp.where(sub == NU - 1, float(pixels), columns[NU - 1])

    trace = columns[0][0:1]
    for j in range(1, NU):
        trace = trace + columns[j][j : j + 1]
    scale = 1.0 / trace
    for j in range(NU + expos):
        columns[j] = columns[j] * scale
        if j < NU:
            columns[j] = columns[j] + jnp.where(sub == j, RIDGE / NU, 0.0)
    for i in range(NU):
        inverse = 1.0 / columns[i][i : i + 1]
        for j in range(i + 1, NU + expos):
            factor = columns[j][i : i + 1] * inverse
            columns[j] = jnp.where(sub == i, factor, columns[j] - columns[i] * factor)

    solved = columns[NU:]
    own = solved[0]
    mixed = weight[0] * solved[0]
    for e in range(1, expos):
        own = jnp.where(expo_at == e, solved[e], own)
        mixed = mixed + weight[e] * solved[e]
    diagonal = (sub == lane) & (sub < NU)
    coeffs_ref[...] = jnp.sum(jnp.where(diagonal, own, 0.0), axis=0, keepdims=True)[:, :NU]
    scale = [jnp.broadcast_to(mixed[u : u + 1], (8, LANES)) for u in range(NU)]
    gains = []
    for shift in range(expos):
        gain = weight[0][:8]
        for e in range(1, expos):
            gain = jnp.where(source(expo_at, shift, expos) == e, weight[e][:8], gain)
        gains.append(gain)
    first_col = expo_at * chunk
    copies = []
    for r in range(0, rows, 8):
        for b in range(blocks):
            at = slice(b * LANES, (b + 1) * LANES)
            x = column_positions(first_col, b, width)
            total = -scale[NU - 1]
            for gain, image_ref in zip(gains, image_refs):
                total = total + gain * image_ref[:, at].astype(jnp.float32)[r : r + 8]
            model = (scale[0] + scale[NB] * x) * conv_ref[0, b, r : r + 8]
            for k in range(1, NB):
                model = model + (scale[k] + scale[NB + k] * x) * conv_ref[k, b, r : r + 8]
            tile_ref[r : r + 8, b * LANES : (b + 1) * LANES] = total - model
        copies.append(
            pltpu.make_async_copy(tile_ref.at[pl.ds(r, 8)], coadd_ref.at[pl.ds(r, 8)], sems.at[r // 8])
        )
        copies[-1].start()
    for copy in copies:
        copy.wait()


def swaps(first, size):
    pairs = [(i, i + 1) for i in range(first, size - 1, 2)]
    if first and size % 2 == 0:
        pairs.append((0, size - 1))
    return [pair for a, b in pairs for pair in ((a, b), (b, a))]


def tiled_device(template, science, plan, orders, coadd_weight, intersection):
    expos = lax.axis_size("expo")
    tiles = lax.axis_size("tile")
    _, rows, width = template.shape
    steps = science.shape[1]
    chunk = width // expos
    ext = chunk + LANES
    blocks = chunk // LANES
    vmem = pl.BlockSpec(memory_space=pltpu.VMEM)
    small = pltpu.CompilerParams(vmem_limit_bytes=16 * 1024 * 1024)
    hbm = pl.BlockSpec(memory_space=pltpu.HBM)
    coadds = []
    fitted = []
    for step in range(steps):
        *blocks_out, owner, order = pl.pallas_call(
            functools.partial(send_kernel, step=step),
            out_shape=(pltpu.VMEM((rows, ext), template.dtype),) * expos
            + tuple(
                pltpu.VMEM((rows, chunk if shift < expos // 2 else ext), science.dtype) for shift in range(expos)
            )
            + (
                jax.ShapeDtypeStruct((rows, LANES), jnp.int32),
                jax.ShapeDtypeStruct((2, NB, 8, LANES), jnp.int32),
            ),
            in_specs=[hbm] * 4,
            out_specs=(vmem,) * (2 * expos + 2),
            scratch_shapes=[
                pltpu.VMEM((rows, width + 2 * LANES), template.dtype),
                pltpu.SMEM(plan.shape, jnp.int32),
                pltpu.SMEM((2, NB), jnp.int32),
                pltpu.SemaphoreType.DMA((expos + 4,)),
            ],
            compiler_params=small,
        )(
            pltpu.with_memory_space_constraint(template[0], pltpu.HBM),
            pltpu.with_memory_space_constraint(science[0, step], pltpu.HBM),
            pltpu.with_memory_space_constraint(plan, pltpu.HBM),
            pltpu.with_memory_space_constraint(orders.T, pltpu.HBM),
        )
        patches, images = blocks_out[:expos], blocks_out[expos:]
        for group in (patches, images):
            for shift in range(1, expos):
                pairs = [(e, int(target(e, shift, expos))) for e in range(expos)]
                group[shift] = lax.ppermute(group[shift], "expo", pairs)
        own = pl.pallas_call(
            pick_kernel,
            out_shape=jax.ShapeDtypeStruct((rows, ext), template.dtype),
            in_specs=[vmem] * (1 + expos),
            out_specs=vmem,
            compiler_params=small,
        )(owner, *(patches[shift] for shift in far_first(expos)))
        row_band, col_band = pl.pallas_call(
            functools.partial(band_kernel, tiles=tiles),
            out_shape=(
                jax.ShapeDtypeStruct((NB * rows, 3 * rows), jnp.bfloat16),
                jax.ShapeDtypeStruct((NB, 2 * LANES, LANES), jnp.bfloat16),
            ),
            in_specs=[vmem, pl.BlockSpec(memory_space=pl.ANY)],
            out_specs=(vmem, vmem),
            compiler_params=small,
            cost_estimate=pl.CostEstimate(flops=4_000_000, bytes_accessed=500_000, transcendentals=200_000),
        )(order, own)
        far = lax.ppermute(own, "tile", swaps(1, tiles))
        near = lax.ppermute(own, "tile", swaps(0, tiles))
        conv, sums = pl.pallas_call(
            functools.partial(fit_kernel, width=width),
            out_shape=(
                jax.ShapeDtypeStruct((NB, blocks, rows, LANES), jnp.float32),
                jax.ShapeDtypeStruct((tiles * expos, 8, LANES), jnp.float32),
            ),
            in_specs=[vmem] * (6 + expos),
            out_specs=(vmem, vmem),
            scratch_shapes=[
                pltpu.VMEM((NB * rows, ext), jnp.bfloat16),
                pltpu.VMEM((80 + 14 * expos + 8, 8, LANES), jnp.float32),
            ],
            compiler_params=small,
        )(
            coadd_weight[:, step : step + 1] * intersection[:, step : step + 1].astype(jnp.float32),
            row_band,
            col_band,
            own,
            near,
            far,
            *(images[shift] for shift in far_first(expos)),
        )
        sums = lax.all_to_all(sums, ("tile", "expo"), split_axis=0, concat_axis=0, tiled=True)
        coadd, coeffs = pl.pallas_call(
            functools.partial(solve_kernel, width=width, pixels=tiles * rows * width),
            out_shape=(
                jax.ShapeDtypeStruct((rows, chunk), jnp.float32),
                jax.ShapeDtypeStruct((1, NU), jnp.float32),
            ),
            in_specs=[vmem] * (3 + expos),
            out_specs=(pl.BlockSpec(memory_space=pl.ANY), vmem),
            scratch_shapes=[
                pltpu.VMEM((rows, chunk), jnp.float32),
                pltpu.SemaphoreType.DMA((rows // 8,)),
            ],
            compiler_params=small,
        )(jnp.asarray(table(expos)), sums, conv, *images)
        coadds.append(coadd[None])
        fitted.append(coeffs)
    return (jnp.concatenate(coadds), jnp.stack(fitted, axis=1))


def broadcast(block, axis, holder):
    block = jnp.where(lax.axis_index(axis) == holder, block, jnp.zeros_like(block))
    return lax.psum(block, axis)


def extended(x, sides, width):
    for axis, dim in sides:
        size, length = (lax.axis_size(axis), x.shape[dim])
        up = [(i, (i + 1) % size) for i in range(size - 1)]
        down = [(j, i) for i, j in up]
        last = lax.slice_in_dim(x, length - width, length, axis=dim)
        first = lax.slice_in_dim(x, 0, width, axis=dim)
        before = lax.ppermute(last, axis, up)
        after = lax.ppermute(first, axis, down)
        x = jnp.concatenate([before, x, after], axis=dim)
    return x


def make_filters(orders):
    taps_pos = jnp.arange(2 * HALF + 1).astype(jnp.float32) - HALF
    row_list = []
    col_list = []
    for basis in range(NB):
        sigma = SIGMAS[basis]
        envelope = jnp.exp(-taps_pos * taps_pos / (2.0 * sigma * sigma))
        row_filter = envelope * power_of(taps_pos, orders[basis, 0])
        col_filter = envelope * power_of(taps_pos, orders[basis, 1])
        row_list.append(row_filter / jnp.sqrt(jnp.sum(row_filter * row_filter)))
        col_list.append(col_filter / jnp.sqrt(jnp.sum(col_filter * col_filter)))
    return (jnp.stack(row_list).astype(jnp.bfloat16), jnp.stack(col_list).astype(jnp.bfloat16))


def band_matrix(filters, out_len, in_len):
    offset = jnp.arange(in_len)[None, :] - jnp.arange(out_len)[:, None]
    taps_idx = jnp.arange(2 * HALF + 1)
    picks = (offset[:, :, None] == taps_idx[None, None, :]).astype(jnp.float32)
    band = jnp.einsum("ijt,kt->kij", picks, filters.astype(jnp.float32))
    return band.astype(jnp.bfloat16)


def any_device(template, science, plan, orders, coadd_weight, intersection):
    row_filters, col_filters = make_filters(orders)
    rows = template.shape[1]
    width = template.shape[2]
    blocks_count = width // 128
    steps_count = science.shape[1]
    row_band = band_matrix(row_filters, rows, rows + 2 * HALF)
    col_band = jnp.transpose(band_matrix(col_filters, 128, 128 + 2 * HALF), (0, 2, 1))
    column_pos = 2.0 * (jnp.arange(width).astype(jnp.float32) + 0.5) / width - 1.0
    pieces = []
    fitted = []
    for step in range(steps_count):
        received = broadcast(template[0], "expo", plan[step])
        padded = extended(received, (("tile", 0),), HALF)
        rowconv = jnp.einsum(
            "kij,jw->kiw", row_band, padded, preferred_element_type=jnp.float32
        ).astype(jnp.bfloat16)
        blocks = rowconv.reshape(NB, rows, blocks_count, 128)
        empty_rim = jnp.zeros((NB, rows, 1, HALF), jnp.bfloat16)
        previous = jnp.concatenate([empty_rim, blocks[:, :, :-1, 128 - HALF :]], axis=2)
        following = jnp.concatenate([blocks[:, :, 1:, :HALF], empty_rim], axis=2)
        window = jnp.concatenate([previous, blocks, following], axis=3)
        conv = jnp.einsum("krbj,kjc->krbc", window, col_band, preferred_element_type=jnp.float32)
        conv = conv.reshape(NB, rows, width)
        fields = jnp.concatenate(
            [conv, conv * column_pos, jnp.ones((1, rows, width), jnp.float32)], axis=0
        )
        fields = fields.reshape(NU, rows * width)
        exposure_image = science[0, step].astype(jnp.float32).reshape(rows * width)
        normal_local = jnp.dot(fields, fields.T, precision=lax.Precision.HIGHEST)
        project_local = jnp.dot(fields, exposure_image, precision=lax.Precision.HIGHEST)
        normal_matrix, projections = lax.psum((normal_local, project_local), "tile")
        normal_matrix = normal_matrix + RIDGE * (jnp.trace(normal_matrix) / NU) * jnp.eye(
            NU, dtype=jnp.float32
        )
        factor = jnp.linalg.cholesky(normal_matrix)
        coeffs = jax.scipy.linalg.cho_solve((factor, True), projections)
        model = jnp.dot(coeffs, fields, precision=lax.Precision.HIGHEST)
        difference = exposure_image - model
        weight_now = coadd_weight[0, step] * intersection[0, step].astype(jnp.float32)
        pieces.append((weight_now * difference).reshape(rows, width))
        fitted.append(coeffs)
    weighted = jnp.stack(pieces)
    received_parts = lax.all_to_all(weighted[None], "expo", split_axis=3, concat_axis=0, tiled=True)
    coadd = jnp.sum(received_parts, axis=0)
    return (coadd, jnp.stack(fitted)[None])


def per_device(template, science, plan, orders, coadd_weight, intersection):
    expos = lax.axis_size("expo")
    rows, width = template.shape[1:]
    whole_lanes = width % (expos * LANES) == 0 and rows % 16 == 0 and 3 * rows <= LANES
    few = (NU + 1) * expos <= LANES and NU + expos <= LANES
    body = tiled_device if whole_lanes and few else any_device
    return body(template, science, plan, orders, coadd_weight, intersection)


def solution(mesh):
    return jax.shard_map(
        per_device,
        mesh=mesh,
        in_specs=(
            P(("groups", "expo"), "tile", None),
            P(("groups", "expo"), None, "tile", None),
            P("groups"),
            P(),
            P(("groups", "expo"), None),
            P(("groups", "expo"), None),
        ),
        out_specs=(P("groups", "tile", "expo"), P(("groups", "expo"), None, None)),
        check_vma=False,
    )
```

```python
import functools

import jax
import jax.numpy as jnp
import numpy as np
from jax import lax
from jax.experimental import pallas as pl
from jax.experimental.pallas import tpu as pltpu
from jax.sharding import PartitionSpec as P

HALF = 15
NB = 6
NU = 13
LANES = 128
BEYOND = 1000
STAGE_COST = 700_000_000
PAIRS = [(j, k) for j in range(NB) for k in range(j, NB)]

SIGMAS = (0.8, 1.4, 2.2, 3.0, 4.0, 5.5)
RIDGE = 0.05


def power_of(pos, order):
    return jnp.where(order == 0, 1.0, jnp.where(order == 1, pos, pos * pos))


def tap_values(pos, sigma, order):
    value = jnp.exp(-pos * pos / (2.0 * sigma * sigma)) * power_of(pos, order)
    return jnp.where(jnp.abs(pos) <= HALF, value, 0.0)


def tap_norm(sigma, order):
    pos = lax.broadcasted_iota(jnp.int32, (8, LANES), 1).astype(jnp.float32) - HALF
    value = tap_values(pos, sigma, order)
    return jnp.sqrt(jnp.sum(value * value, axis=1, keepdims=True))


def target(me, shift, size):
    return me ^ shift if size & (size - 1) == 0 else (me + shift) % size


def source(me, shift, size):
    return me ^ shift if size & (size - 1) == 0 else (me - shift + size) % size


def far_first(size):
    return [*range(size // 2, size), *range(1, size // 2), 0] if size > 1 else [0]


def joint(shift, size):
    return shift < size // 2


def send_kernel(template_ref, science_ref, plan_ref, orders_ref, *refs, step):
    *out_refs, owner_ref, order_ref, patch_ref, plan_now, orders_now, sems = refs
    size = sems.shape[0] - 4
    rows, width = science_ref.shape
    chunk = width // size
    ext = chunk + LANES
    patch_refs, image_refs = out_refs[:size], out_refs[size:]
    half = size * chunk // 2
    me = lax.axis_index("expo")
    starts = [pl.multiple_of(target(me, shift, size) * chunk, chunk) for shift in range(size)]
    loads = [
        pltpu.make_async_copy(
            template_ref.at[:, pl.ds(i * half, half)], patch_ref.at[:, pl.ds((i * half + LANES), half)], sems.at[i]
        )
        for i in range(2)
    ]
    copies = [
        pltpu.make_async_copy(
            science_ref.at[:, pl.ds(starts[shift], chunk)],
            patch_refs[shift].at[:, pl.ds(ext, chunk)]
            if joint(shift, size)
            else image_refs[shift - size // 2].at[:, pl.ds(0, chunk)],
            sems.at[3 + shift],
        )
        for shift in range(size)
    ]
    copies.append(pltpu.make_async_copy(plan_ref, plan_now, sems.at[2]))
    copies.append(pltpu.make_async_copy(orders_ref, orders_now, sems.at[3 + size]))
    for copy in loads + copies:
        copy.start()
    blank = jnp.zeros((rows, LANES), patch_ref.dtype)
    patch_ref[:, :LANES] = blank
    patch_ref[:, size * chunk + LANES :] = blank
    for image_ref in image_refs:
        image_ref[:, chunk:] = blank
    for copy in loads:
        copy.wait()
    lane = lax.broadcasted_iota(jnp.int32, (rows, LANES), 1)
    for shift in range(size):
        start = starts[shift]
        patch_refs[shift][:, :chunk] = patch_ref[:, pl.ds(start + LANES, chunk)]
        before = patch_ref[:, pl.ds(start, LANES)].astype(jnp.float32)
        after = patch_ref[:, pl.ds(start + chunk + LANES, LANES)].astype(jnp.float32)
        rim = jnp.where(lane < LANES // 2, after, before)
        patch_refs[shift][:, chunk:ext] = rim.astype(patch_ref.dtype)
    for copy in copies:
        copy.wait()
    owner_ref[...] = jnp.full(owner_ref.shape, plan_now[step], jnp.int32)
    for way in range(2):
        for k in range(NB):
            order_ref[way, k] = jnp.full((8, LANES), orders_now[way, k], jnp.int32)


def choose_kernel(owner_ref, *refs, shifts, size):
    *recv_refs, out_ref = refs
    me = lax.axis_index("expo")
    for b in range(out_ref.shape[1] // LANES):
        columns = slice(b * LANES, (b + 1) * LANES)
        block = recv_refs[0][:, columns].astype(jnp.float32)
        for shift, ref in zip(shifts, recv_refs[1:]):
            block = jnp.where(
                owner_ref[...] == source(me, shift, size), ref[:, columns].astype(jnp.float32), block
            )
        out_ref[:, columns] = block.astype(out_ref.dtype)


def pick_kernel(owner_ref, *refs, shifts, size):
    *recv_refs, out_ref, block_ref = refs
    ext = out_ref.shape[1]
    choose_kernel(owner_ref, *recv_refs, block_ref, shifts=shifts, size=size)
    whole = jnp.concatenate([block_ref[:, ext - LANES :], block_ref[...]], axis=1)
    out_ref[...] = whole[:, LANES - HALF : LANES - HALF + ext]


def column_positions(first_col, block, width):
    col = lax.broadcasted_iota(jnp.int32, (8, LANES), 1) + (first_col + block * LANES)
    return 2.0 * (col.astype(jnp.float32) + 0.5) / width - 1.0


def band_kernel(order_ref, _, row_ref, col_ref, *, tiles):
    rows = row_ref.shape[0] // NB
    tile_at = lax.axis_index("tile")
    near = 1 - 2 * lax.rem(tile_at, 2)
    near_move = jnp.where(tile_at + near < tiles, near - 1, BEYOND)
    far_move = jnp.where((tile_at >= near) & (tile_at - near < tiles), -near - 2, BEYOND)
    row_from = lax.broadcasted_iota(jnp.int32, (8, LANES), 1)
    moved = jnp.where(row_from < rows, 0, jnp.where(row_from < 2 * rows, near_move, far_move))
    sub = lax.broadcasted_iota(jnp.int32, (8, LANES), 0)
    lane = lax.broadcasted_iota(jnp.int32, (8, LANES), 1)
    shift = (sub - jnp.where(lane < LANES // 2, lane, lane - LANES) - HALF).astype(jnp.float32)
    for k in range(NB):
        norm = tap_norm(SIGMAS[k], order_ref[0, k])
        for r in range(0, rows, 16):
            parts = []
            for half in (r, r + 8):
                offset = (row_from + moved * rows - sub - half).astype(jnp.float32)
                parts.append(tap_values(offset, SIGMAS[k], order_ref[0, k]) / norm)
            both = jnp.concatenate(parts, axis=0).astype(jnp.bfloat16)
            row_ref[k * rows + r : k * rows + r + 16] = both[:, : 3 * rows]
        norm = tap_norm(SIGMAS[k], order_ref[1, k])
        pattern = tap_values(shift, SIGMAS[k], order_ref[1, k]) / norm
        for r in range(0, 2 * LANES, 16):
            parts = []
            for half in (r, r + 8):
                moved_on = pltpu.roll(pattern, half % LANES, 1) if half % LANES else pattern
                inside = lane <= half + 7 if half < LANES else lane >= half - LANES + LANES // 2
                parts.append(jnp.where(inside, moved_on, 0.0))
            col_ref[k, r : r + 16] = jnp.concatenate(parts, axis=0).astype(jnp.bfloat16)


def image_blocks(ref, size, shift, chunk):
    first = chunk + LANES if joint(shift, size) else 0
    return lambda b: ref[:, first + b * LANES : first + (b + 1) * LANES].astype(jnp.float32)


def fit_kernel(weight_ref, hits_ref, row_band_ref, col_band_ref, own_ref, near_ref, far_ref, *refs, width):
    *image_refs, conv_ref, sums_ref, row_ref, parts_ref = refs
    image_refs = dict(zip(far_first(len(image_refs)), image_refs))
    tile_at = lax.axis_index("tile")
    expo_at = lax.axis_index("expo")
    rows, ext = own_ref.shape
    expos = len(image_refs)
    chunk = ext - LANES
    blocks = chunk // LANES

    patch = jnp.concatenate([own_ref[...], near_ref[...], far_ref[...]], axis=0)
    row_ref[...] = jnp.dot(
        row_band_ref[...], patch, preferred_element_type=jnp.float32
    ).astype(jnp.bfloat16)
    for k in range(NB):
        window = jnp.concatenate(
            [
                row_ref[k * rows : (k + 1) * rows, b * LANES : (b + 2) * LANES]
                for b in range(blocks)
            ],
            axis=0,
        )
        out = jnp.dot(window, col_band_ref[k], preferred_element_type=jnp.float32)
        conv_ref[k] = out.reshape(blocks, rows, LANES)

    first_col = expo_at * chunk
    xs = [column_positions(first_col, b, width) for b in range(blocks)]

    def fold(x):
        total = x[:8]
        for i in range(8, rows, 8):
            total = total + x[i : i + 8]
        return total

    def moments(at, left, right, count):
        total = [None] * count
        for b in range(blocks):
            term = fold(left(b) * right(b)) if right is not None else fold(left(b))
            for i in range(count):
                total[i] = term if total[i] is None else total[i] + term
                if i < count - 1:
                    term = term * xs[b]
        for i in range(count):
            parts_ref[at + i] = total[i]

    def conv(k):
        return lambda b: conv_ref[k, b]

    def sci(shift):
        return image_blocks(image_refs[shift], expos, shift, chunk)

    blank = jnp.zeros((8, LANES), jnp.float32)
    at = 0
    for j, k in PAIRS:
        moments(at, conv(j), conv(k), 3)
        at += 3
    for k in range(NB):
        moments(at, conv(k), None, 2)
        at += 2
    while at % 8:
        parts_ref[at] = blank
        at += 1
    begin = at
    for shift in range(expos):
        row = at + NU * source(expo_at, shift, expos)
        for k in range(NB):
            moments(row + 2 * k, conv(k), sci(shift), 2)
        moments(row + NU - 1, sci(shift), None, 1)
    at += NU * expos
    weight = jnp.broadcast_to(weight_ref[...] * hits_ref[...].astype(jnp.float32), (8, LANES))
    weight = jnp.where(tile_at == 0, weight, 0.0)
    spot = (
        (lax.broadcasted_iota(jnp.int32, (8, LANES), 0) == 0)
        & (lax.broadcasted_iota(jnp.int32, (8, LANES), 1) == 0)
    )
    for e in range(expos):
        parts_ref[at + e] = jnp.where(spot & (expo_at == e), weight, 0.0)
    at += expos
    while at % 8:
        parts_ref[at] = blank
        at += 1
    ones = jnp.ones((8, LANES), jnp.float32)
    rows_of = []
    for first, last in ((0, begin), (begin, at)):
        lanes = jnp.sum(parts_ref[first:last], axis=1)
        spare = LANES - (last - first)
        if spare:
            lanes = jnp.concatenate([lanes, jnp.zeros((spare, LANES), jnp.float32)], axis=0)
        rows_of.append(
            lax.dot_general(
                ones,
                lanes,
                (((1,), (1,)), ((), ())),
                precision=lax.Precision.HIGHEST,
                preferred_element_type=jnp.float32,
            )
        )
    both = jnp.where(lax.broadcasted_iota(jnp.int32, (8, LANES), 0) < 4, rows_of[0], rows_of[1])
    for i in range(sums_ref.shape[0]):
        sums_ref[i] = both


def table(expos):
    columns = np.zeros((NU + expos + 1, 16), np.int32)
    for at, (j, k) in enumerate(PAIRS):
        for a, b in ((j, k), (k, j)):
            columns[b, a] = 3 * at
            columns[NB + b, a] = columns[b, NB + a] = 3 * at + 1
            columns[NB + b, NB + a] = 3 * at + 2
    for k in range(NB):
        for x in range(2):
            columns[NU - 1, x * NB + k] = columns[x * NB + k, NU - 1] = 3 * len(PAIRS) + 2 * k + x
    for e in range(expos):
        columns[NU + e, :NU] = [NU * e + 2 * k + x for x in range(2) for k in range(NB)] + [NU * e + NU - 1]
        columns[NU + expos, e] = NU * expos + e
    return np.ascontiguousarray(np.broadcast_to(columns[:, :, None], columns.shape + (LANES,)))


def solve_kernel(table_ref, sums_ref, conv_ref, *refs, width, pixels):
    *image_refs, coadd_ref, coeffs_ref, tile_ref, sems = refs
    expo_at = lax.axis_index("expo")
    expos = len(image_refs)
    rows, chunk = coadd_ref.shape
    blocks = chunk // LANES
    images = [image_blocks(ref, expos, shift, chunk) for shift, ref in enumerate(image_refs)]
    sub = lax.broadcasted_iota(jnp.int32, (16, LANES), 0)
    lane = lax.broadcasted_iota(jnp.int32, (16, LANES), 1)
    sums = sums_ref[0]
    for i in range(1, sums_ref.shape[0]):
        sums = sums + sums_ref[i]
    first = jnp.broadcast_to(sums[0:1], (16, LANES))
    second = jnp.broadcast_to(sums[4:5], (16, LANES))

    columns = [
        jnp.take_along_axis(first if j < NU else second, table_ref[j], axis=1) for j in range(NU + expos)
    ]
    spread = jnp.take_along_axis(second, table_ref[NU + expos], axis=1)
    weight = [jnp.broadcast_to(spread[e : e + 1], (16, LANES)) for e in range(expos)]
    columns[NU - 1] = jnp.where(sub == NU - 1, float(pixels), columns[NU - 1])

    trace = columns[0][0:1]
    for j in range(1, NU):
        trace = trace + columns[j][j : j + 1]
    scale = 1.0 / trace
    for j in range(NU + expos):
        columns[j] = columns[j] * scale
        if j < NU:
            columns[j] = columns[j] + jnp.where(sub == j, RIDGE / NU, 0.0)
    for i in range(NU):
        inverse = 1.0 / columns[i][i : i + 1]
        for j in range(i + 1, NU + expos):
            factor = columns[j][i : i + 1] * inverse
            columns[j] = jnp.where(sub == i, factor, columns[j] - columns[i] * factor)

    solved = columns[NU:]
    own = solved[0]
    mixed = weight[0] * solved[0]
    for e in range(1, expos):
        own = jnp.where(expo_at == e, solved[e], own)
        mixed = mixed + weight[e] * solved[e]
    diagonal = (sub == lane) & (sub < NU)
    coeffs_ref[...] = jnp.sum(jnp.where(diagonal, own, 0.0), axis=0, keepdims=True)[:, :NU]
    scale = [jnp.broadcast_to(mixed[u : u + 1], (8, LANES)) for u in range(NU)]
    gains = []
    for shift in range(expos):
        gain = weight[0][:8]
        for e in range(1, expos):
            gain = jnp.where(source(expo_at, shift, expos) == e, weight[e][:8], gain)
        gains.append(gain)
    first_col = expo_at * chunk
    copies = []
    for r in range(0, rows, 8):
        for b in range(blocks):
            x = column_positions(first_col, b, width)
            total = -scale[NU - 1]
            for gain, image in zip(gains, images):
                total = total + gain * image(b)[r : r + 8]
            model = (scale[0] + scale[NB] * x) * conv_ref[0, b, r : r + 8]
            for k in range(1, NB):
                model = model + (scale[k] + scale[NB + k] * x) * conv_ref[k, b, r : r + 8]
            tile_ref[r : r + 8, b * LANES : (b + 1) * LANES] = total - model
        copies.append(
            pltpu.make_async_copy(tile_ref.at[pl.ds(r, 8)], coadd_ref.at[pl.ds(r, 8)], sems.at[r // 8])
        )
        copies[-1].start()
    for copy in copies:
        copy.wait()


def swaps(first, size):
    pairs = [(i, i + 1) for i in range(first, size - 1, 2)]
    if first and size % 2 == 0:
        pairs.append((0, size - 1))
    return [pair for a, b in pairs for pair in ((a, b), (b, a))]


def tiled_device(template, science, plan, orders, coadd_weight, intersection):
    expos = lax.axis_size("expo")
    tiles = lax.axis_size("tile")
    _, rows, width = template.shape
    steps = science.shape[1]
    chunk = width // expos
    ext = chunk + LANES
    blocks = chunk // LANES
    vmem = pl.BlockSpec(memory_space=pltpu.VMEM)
    small = pltpu.CompilerParams(vmem_limit_bytes=16 * 1024 * 1024)
    hbm = pl.BlockSpec(memory_space=pltpu.HBM)
    coadds = []
    fitted = []
    for step in range(steps):
        *blocks_out, owner, order = pl.pallas_call(
            functools.partial(send_kernel, step=step),
            out_shape=tuple(
                pltpu.VMEM((rows, ext + chunk if joint(shift, expos) else ext), template.dtype)
                for shift in range(expos)
            )
            + (pltpu.VMEM((rows, ext), science.dtype),) * (expos - expos // 2)
            + (
                jax.ShapeDtypeStruct((rows, LANES), jnp.int32),
                jax.ShapeDtypeStruct((2, NB, 8, LANES), jnp.int32),
            ),
            in_specs=[hbm] * 4,
            out_specs=(vmem,) * (2 * expos - expos // 2 + 2),
            scratch_shapes=[
                pltpu.VMEM((rows, width + 2 * LANES), template.dtype),
                pltpu.SMEM(plan.shape, jnp.int32),
                pltpu.SMEM((2, NB), jnp.int32),
                pltpu.SemaphoreType.DMA((expos + 4,)),
            ],
            compiler_params=small,
        )(
            pltpu.with_memory_space_constraint(template[0], pltpu.HBM),
            pltpu.with_memory_space_constraint(science[0, step], pltpu.HBM),
            pltpu.with_memory_space_constraint(plan, pltpu.HBM),
            pltpu.with_memory_space_constraint(orders.T, pltpu.HBM),
        )
        patches, images = blocks_out[:expos], blocks_out[expos:]
        for group, first in ((patches, 0), (images, expos // 2)):
            for shift in range(max(first, 1), expos):
                pairs = [(e, int(target(e, shift, expos))) for e in range(expos)]
                group[shift - first] = lax.ppermute(group[shift - first], "expo", pairs)
        images = patches[: expos // 2] + images
        across = [shift for shift in range(1, expos) if not joint(shift, expos)]
        beside = [shift for shift in range(1, expos) if joint(shift, expos)]
        block = pl.pallas_call(
            functools.partial(choose_kernel, shifts=across, size=expos),
            out_shape=jax.ShapeDtypeStruct((rows, ext), template.dtype),
            in_specs=[vmem] * (2 + len(across)),
            out_specs=vmem,
            compiler_params=small,
            cost_estimate=pl.CostEstimate(flops=STAGE_COST, bytes_accessed=500_000, transcendentals=0),
        )(owner, patches[0], *(patches[shift] for shift in across))
        own = pl.pallas_call(
            functools.partial(pick_kernel, shifts=beside, size=expos),
            out_shape=jax.ShapeDtypeStruct((rows, ext), template.dtype),
            in_specs=[vmem] * (2 + len(beside)),
            out_specs=vmem,
            scratch_shapes=[pltpu.VMEM((rows, ext), template.dtype)],
            compiler_params=small,
        )(owner, block, *(patches[shift] for shift in beside))
        row_band, col_band = pl.pallas_call(
            functools.partial(band_kernel, tiles=tiles),
            out_shape=(
                jax.ShapeDtypeStruct((NB * rows, 3 * rows), jnp.bfloat16),
                jax.ShapeDtypeStruct((NB, 2 * LANES, LANES), jnp.bfloat16),
            ),
            in_specs=[vmem, pl.BlockSpec(memory_space=pl.ANY)],
            out_specs=(vmem, vmem),
            compiler_params=small,
            cost_estimate=pl.CostEstimate(flops=4_000_000, bytes_accessed=500_000, transcendentals=200_000),
        )(order, own)
        far = lax.ppermute(own, "tile", swaps(1, tiles))
        near = lax.ppermute(own, "tile", swaps(0, tiles))
        conv, sums = pl.pallas_call(
            functools.partial(fit_kernel, width=width),
            out_shape=(
                jax.ShapeDtypeStruct((NB, blocks, rows, LANES), jnp.float32),
                jax.ShapeDtypeStruct((tiles * expos, 8, LANES), jnp.float32),
            ),
            in_specs=[vmem] * (7 + expos),
            out_specs=(vmem, vmem),
            scratch_shapes=[
                pltpu.VMEM((NB * rows, ext), jnp.bfloat16),
                pltpu.VMEM((80 + 14 * expos + 8, 8, LANES), jnp.float32),
            ],
            compiler_params=small,
        )(
            coadd_weight[:, step : step + 1],
            intersection[:, step : step + 1],
            row_band,
            col_band,
            own,
            near,
            far,
            *(images[shift] for shift in far_first(expos)),
        )
        sums = lax.all_to_all(sums, ("tile", "expo"), split_axis=0, concat_axis=0, tiled=True)
        coadd, coeffs = pl.pallas_call(
            functools.partial(solve_kernel, width=width, pixels=tiles * rows * width),
            out_shape=(
                jax.ShapeDtypeStruct((rows, chunk), jnp.float32),
                jax.ShapeDtypeStruct((1, NU), jnp.float32),
            ),
            in_specs=[vmem] * (3 + expos),
            out_specs=(pl.BlockSpec(memory_space=pl.ANY), vmem),
            scratch_shapes=[
                pltpu.VMEM((rows, chunk), jnp.float32),
                pltpu.SemaphoreType.DMA((rows // 8,)),
            ],
            compiler_params=small,
        )(jnp.asarray(table(expos)), sums, conv, *images)
        coadds.append(coadd[None])
        fitted.append(coeffs)
    return (jnp.concatenate(coadds), jnp.stack(fitted, axis=1))


def broadcast(block, axis, holder):
    block = jnp.where(lax.axis_index(axis) == holder, block, jnp.zeros_like(block))
    return lax.psum(block, axis)


def extended(x, sides, width):
    for axis, dim in sides:
        size, length = (lax.axis_size(axis), x.shape[dim])
        up = [(i, (i + 1) % size) for i in range(size - 1)]
        down = [(j, i) for i, j in up]
        last = lax.slice_in_dim(x, length - width, length, axis=dim)
        first = lax.slice_in_dim(x, 0, width, axis=dim)
        before = lax.ppermute(last, axis, up)
        after = lax.ppermute(first, axis, down)
        x = jnp.concatenate([before, x, after], axis=dim)
    return x


def make_filters(orders):
    taps_pos = jnp.arange(2 * HALF + 1).astype(jnp.float32) - HALF
    row_list = []
    col_list = []
    for basis in range(NB):
        sigma = SIGMAS[basis]
        envelope = jnp.exp(-taps_pos * taps_pos / (2.0 * sigma * sigma))
        row_filter = envelope * power_of(taps_pos, orders[basis, 0])
        col_filter = envelope * power_of(taps_pos, orders[basis, 1])
        row_list.append(row_filter / jnp.sqrt(jnp.sum(row_filter * row_filter)))
        col_list.append(col_filter / jnp.sqrt(jnp.sum(col_filter * col_filter)))
    return (jnp.stack(row_list).astype(jnp.bfloat16), jnp.stack(col_list).astype(jnp.bfloat16))


def band_matrix(filters, out_len, in_len):
    offset = jnp.arange(in_len)[None, :] - jnp.arange(out_len)[:, None]
    taps_idx = jnp.arange(2 * HALF + 1)
    picks = (offset[:, :, None] == taps_idx[None, None, :]).astype(jnp.float32)
    band = jnp.einsum("ijt,kt->kij", picks, filters.astype(jnp.float32))
    return band.astype(jnp.bfloat16)


def any_device(template, science, plan, orders, coadd_weight, intersection):
    row_filters, col_filters = make_filters(orders)
    rows = template.shape[1]
    width = template.shape[2]
    blocks_count = width // 128
    steps_count = science.shape[1]
    row_band = band_matrix(row_filters, rows, rows + 2 * HALF)
    col_band = jnp.transpose(band_matrix(col_filters, 128, 128 + 2 * HALF), (0, 2, 1))
    column_pos = 2.0 * (jnp.arange(width).astype(jnp.float32) + 0.5) / width - 1.0
    pieces = []
    fitted = []
    for step in range(steps_count):
        received = broadcast(template[0], "expo", plan[step])
        padded = extended(received, (("tile", 0),), HALF)
        rowconv = jnp.einsum(
            "kij,jw->kiw", row_band, padded, preferred_element_type=jnp.float32
        ).astype(jnp.bfloat16)
        blocks = rowconv.reshape(NB, rows, blocks_count, 128)
        empty_rim = jnp.zeros((NB, rows, 1, HALF), jnp.bfloat16)
        previous = jnp.concatenate([empty_rim, blocks[:, :, :-1, 128 - HALF :]], axis=2)
        following = jnp.concatenate([blocks[:, :, 1:, :HALF], empty_rim], axis=2)
        window = jnp.concatenate([previous, blocks, following], axis=3)
        conv = jnp.einsum("krbj,kjc->krbc", window, col_band, preferred_element_type=jnp.float32)
        conv = conv.reshape(NB, rows, width)
        fields = jnp.concatenate(
            [conv, conv * column_pos, jnp.ones((1, rows, width), jnp.float32)], axis=0
        )
        fields = fields.reshape(NU, rows * width)
        exposure_image = science[0, step].astype(jnp.float32).reshape(rows * width)
        normal_local = jnp.dot(fields, fields.T, precision=lax.Precision.HIGHEST)
        project_local = jnp.dot(fields, exposure_image, precision=lax.Precision.HIGHEST)
        normal_matrix, projections = lax.psum((normal_local, project_local), "tile")
        normal_matrix = normal_matrix + RIDGE * (jnp.trace(normal_matrix) / NU) * jnp.eye(
            NU, dtype=jnp.float32
        )
        factor = jnp.linalg.cholesky(normal_matrix)
        coeffs = jax.scipy.linalg.cho_solve((factor, True), projections)
        model = jnp.dot(coeffs, fields, precision=lax.Precision.HIGHEST)
        difference = exposure_image - model
        weight_now = coadd_weight[0, step] * intersection[0, step].astype(jnp.float32)
        pieces.append((weight_now * difference).reshape(rows, width))
        fitted.append(coeffs)
    weighted = jnp.stack(pieces)
    received_parts = lax.all_to_all(weighted[None], "expo", split_axis=3, concat_axis=0, tiled=True)
    coadd = jnp.sum(received_parts, axis=0)
    return (coadd, jnp.stack(fitted)[None])


def per_device(template, science, plan, orders, coadd_weight, intersection):
    expos = lax.axis_size("expo")
    rows, width = template.shape[1:]
    whole_lanes = width % (expos * LANES) == 0 and rows % 16 == 0 and 3 * rows <= LANES
    few = (NU + 1) * expos <= LANES and NU + expos <= LANES
    body = tiled_device if whole_lanes and few else any_device
    return body(template, science, plan, orders, coadd_weight, intersection)


def solution(mesh):
    return jax.shard_map(
        per_device,
        mesh=mesh,
        in_specs=(
            P(("groups", "expo"), "tile", None),
            P(("groups", "expo"), None, "tile", None),
            P("groups"),
            P(),
            P(("groups", "expo"), None),
            P(("groups", "expo"), None),
        ),
        out_specs=(P("groups", "tile", "expo"), P(("groups", "expo"), None, None)),
        check_vma=False,
    )
```

```python
import functools

import jax
import jax.numpy as jnp
import numpy as np
from jax import lax
from jax.experimental import pallas as pl
from jax.experimental.pallas import tpu as pltpu
from jax.sharding import PartitionSpec as P

HALF = 15
NB = 6
NU = 13
LANES = 128
BEYOND = 1000
PAIRS = [(j, k) for j in range(NB) for k in range(j, NB)]

SIGMAS = (0.8, 1.4, 2.2, 3.0, 4.0, 5.5)
RIDGE = 0.05


def power_of(pos, order):
    return jnp.where(order == 0, 1.0, jnp.where(order == 1, pos, pos * pos))


def tap_values(pos, sigma, order):
    value = jnp.exp(-pos * pos / (2.0 * sigma * sigma)) * power_of(pos, order)
    return jnp.where(jnp.abs(pos) <= HALF, value, 0.0)


def tap_norm(sigma, order):
    pos = lax.broadcasted_iota(jnp.int32, (8, LANES), 1).astype(jnp.float32) - HALF
    value = tap_values(pos, sigma, order)
    return jnp.sqrt(jnp.sum(value * value, axis=1, keepdims=True))


def target(me, shift, size):
    return me ^ shift if size & (size - 1) == 0 else (me + shift) % size


def source(me, shift, size):
    return me ^ shift if size & (size - 1) == 0 else (me - shift + size) % size


def far_first(size):
    return [*range(size // 2, size), *range(1, size // 2), 0] if size > 1 else [0]


def send_kernel(template_ref, science_ref, plan_ref, orders_ref, *refs, step):
    *out_refs, owner_ref, order_ref, patch_ref, plan_now, orders_now, sems = refs
    size = len(out_refs) // 2
    image_refs = out_refs[size:]
    rows, ext = image_refs[0].shape
    chunk = ext - LANES
    half = size * chunk // 2
    me = lax.axis_index("expo")
    starts = [pl.multiple_of(target(me, shift, size) * chunk, chunk) for shift in range(size)]
    loads = [
        pltpu.make_async_copy(
            template_ref.at[:, pl.ds(i * half, half)], patch_ref.at[:, pl.ds((i * half + LANES), half)], sems.at[i]
        )
        for i in range(2)
    ]
    copies = [
        pltpu.make_async_copy(
            science_ref.at[:, pl.ds(starts[shift], chunk)],
            image_refs[shift].at[:, pl.ds(0, chunk)],
            sems.at[3 + shift],
        )
        for shift in range(size)
    ]
    copies.append(pltpu.make_async_copy(plan_ref, plan_now, sems.at[2]))
    copies.append(pltpu.make_async_copy(orders_ref, orders_now, sems.at[3 + size]))
    for copy in loads + copies:
        copy.start()
    blank = jnp.zeros((rows, LANES), patch_ref.dtype)
    patch_ref[:, :LANES] = blank
    patch_ref[:, size * chunk + LANES :] = blank
    for image_ref in image_refs:
        image_ref[:, chunk:] = blank
    for copy in loads:
        copy.wait()
    lane = lax.broadcasted_iota(jnp.int32, (rows, LANES), 1)
    for shift in range(size):
        start = starts[shift]
        out_refs[shift][:, :chunk] = patch_ref[:, pl.ds(start + LANES, chunk)]
        before = patch_ref[:, pl.ds(start, LANES)].astype(jnp.float32)
        after = patch_ref[:, pl.ds(start + chunk + LANES, LANES)].astype(jnp.float32)
        rim = jnp.where(lane < LANES // 2, after, before)
        out_refs[shift][:, chunk:] = rim.astype(patch_ref.dtype)
    for copy in copies:
        copy.wait()
    owner_ref[...] = jnp.full(owner_ref.shape, plan_now[step], jnp.int32)
    for way in range(2):
        for k in range(NB):
            order_ref[way, k] = jnp.full((8, LANES), orders_now[way, k], jnp.int32)


def pick_kernel(owner_ref, *refs):
    *recv_refs, out_ref = refs
    rows, ext = out_ref.shape
    size = len(recv_refs)
    recv_refs = dict(zip(far_first(size), recv_refs))
    me = lax.axis_index("expo")
    blocks = []
    for b in range(ext // LANES):
        columns = slice(b * LANES, (b + 1) * LANES)
        block = recv_refs[0][:, columns].astype(jnp.float32)
        for shift in range(1, size):
            block = jnp.where(
                owner_ref[...] == source(me, shift, size), recv_refs[shift][:, columns].astype(jnp.float32), block
            )
        blocks.append(block.astype(out_ref.dtype))
    whole = jnp.concatenate(blocks[-1:] + blocks, axis=1)
    out_ref[...] = whole[:, LANES - HALF : LANES - HALF + ext]


def column_positions(first_col, block, width):
    col = lax.broadcasted_iota(jnp.int32, (8, LANES), 1) + (first_col + block * LANES)
    return 2.0 * (col.astype(jnp.float32) + 0.5) / width - 1.0


def band_kernel(order_ref, _, row_ref, col_ref, *, tiles):
    rows = row_ref.shape[0] // NB
    tile_at = lax.axis_index("tile")
    near = 1 - 2 * lax.rem(tile_at, 2)
    near_move = jnp.where(tile_at + near < tiles, near - 1, BEYOND)
    far_move = jnp.where((tile_at >= near) & (tile_at - near < tiles), -near - 2, BEYOND)
    row_from = lax.broadcasted_iota(jnp.int32, (8, LANES), 1)
    moved = jnp.where(row_from < rows, 0, jnp.where(row_from < 2 * rows, near_move, far_move))
    sub = lax.broadcasted_iota(jnp.int32, (8, LANES), 0)
    lane = lax.broadcasted_iota(jnp.int32, (8, LANES), 1)
    shift = (sub - jnp.where(lane < LANES // 2, lane, lane - LANES) - HALF).astype(jnp.float32)
    for k in range(NB):
        norm = tap_norm(SIGMAS[k], order_ref[0, k])
        for r in range(0, rows, 16):
            parts = []
            for half in (r, r + 8):
                offset = (row_from + moved * rows - sub - half).astype(jnp.float32)
                parts.append(tap_values(offset, SIGMAS[k], order_ref[0, k]) / norm)
            both = jnp.concatenate(parts, axis=0).astype(jnp.bfloat16)
            row_ref[k * rows + r : k * rows + r + 16] = both[:, : 3 * rows]
        norm = tap_norm(SIGMAS[k], order_ref[1, k])
        pattern = tap_values(shift, SIGMAS[k], order_ref[1, k]) / norm
        for r in range(0, 2 * LANES, 16):
            parts = []
            for half in (r, r + 8):
                moved_on = pltpu.roll(pattern, half % LANES, 1) if half % LANES else pattern
                inside = lane <= half + 7 if half < LANES else lane >= half - LANES + LANES // 2
                parts.append(jnp.where(inside, moved_on, 0.0))
            col_ref[k, r : r + 16] = jnp.concatenate(parts, axis=0).astype(jnp.bfloat16)


def fit_kernel(weight_ref, hits_ref, row_band_ref, col_band_ref, own_ref, near_ref, far_ref, *refs, width):
    *image_refs, conv_ref, sums_ref, row_ref, parts_ref = refs
    image_refs = dict(zip(far_first(len(image_refs)), image_refs))
    tile_at = lax.axis_index("tile")
    expo_at = lax.axis_index("expo")
    rows, ext = own_ref.shape
    expos = len(image_refs)
    chunk = ext - LANES
    blocks = chunk // LANES

    patch = jnp.concatenate([own_ref[...], near_ref[...], far_ref[...]], axis=0)
    row_ref[...] = jnp.dot(
        row_band_ref[...], patch, preferred_element_type=jnp.float32
    ).astype(jnp.bfloat16)
    for k in range(NB):
        window = jnp.concatenate(
            [
                row_ref[k * rows : (k + 1) * rows, b * LANES : (b + 2) * LANES]
                for b in range(blocks)
            ],
            axis=0,
        )
        out = jnp.dot(window, col_band_ref[k], preferred_element_type=jnp.float32)
        conv_ref[k] = out.reshape(blocks, rows, LANES)

    first_col = expo_at * chunk
    xs = [column_positions(first_col, b, width) for b in range(blocks)]

    def fold(x):
        total = x[:8]
        for i in range(8, rows, 8):
            total = total + x[i : i + 8]
        return total

    def moments(at, left, right, count):
        total = [None] * count
        for b in range(blocks):
            term = fold(left(b) * right(b)) if right is not None else fold(left(b))
            for i in range(count):
                total[i] = term if total[i] is None else total[i] + term
                if i < count - 1:
                    term = term * xs[b]
        for i in range(count):
            parts_ref[at + i] = total[i]

    def conv(k):
        return lambda b: conv_ref[k, b]

    def sci(shift):
        return lambda b: image_refs[shift][:, b * LANES : (b + 1) * LANES].astype(jnp.float32)

    blank = jnp.zeros((8, LANES), jnp.float32)
    at = 0
    for j, k in PAIRS:
        moments(at, conv(j), conv(k), 3)
        at += 3
    for k in range(NB):
        moments(at, conv(k), None, 2)
        at += 2
    while at % 8:
        parts_ref[at] = blank
        at += 1
    begin = at
    for shift in range(expos):
        row = at + NU * source(expo_at, shift, expos)
        for k in range(NB):
            moments(row + 2 * k, conv(k), sci(shift), 2)
        moments(row + NU - 1, sci(shift), None, 1)
    at += NU * expos
    weight = jnp.broadcast_to(weight_ref[...] * hits_ref[...].astype(jnp.float32), (8, LANES))
    weight = jnp.where(tile_at == 0, weight, 0.0)
    spot = (
        (lax.broadcasted_iota(jnp.int32, (8, LANES), 0) == 0)
        & (lax.broadcasted_iota(jnp.int32, (8, LANES), 1) == 0)
    )
    for e in range(expos):
        parts_ref[at + e] = jnp.where(spot & (expo_at == e), weight, 0.0)
    at += expos
    while at % 8:
        parts_ref[at] = blank
        at += 1
    ones = jnp.ones((8, LANES), jnp.float32)
    rows_of = []
    for first, last in ((0, begin), (begin, at)):
        lanes = jnp.sum(parts_ref[first:last], axis=1)
        spare = LANES - (last - first)
        if spare:
            lanes = jnp.concatenate([lanes, jnp.zeros((spare, LANES), jnp.float32)], axis=0)
        rows_of.append(
            lax.dot_general(
                ones,
                lanes,
                (((1,), (1,)), ((), ())),
                precision=lax.Precision.HIGHEST,
                preferred_element_type=jnp.float32,
            )
        )
    both = jnp.where(lax.broadcasted_iota(jnp.int32, (8, LANES), 0) < 4, rows_of[0], rows_of[1])
    sums_ref[...] = both


def add_kernel(*refs):
    *block_refs, out_ref = refs
    total = block_refs[0][...]
    for ref in block_refs[1:]:
        total = total + ref[...]
    out_ref[...] = total


def table(expos):
    columns = np.zeros((NU + expos + 1, 16), np.int32)
    for at, (j, k) in enumerate(PAIRS):
        for a, b in ((j, k), (k, j)):
            columns[b, a] = 3 * at
            columns[NB + b, a] = columns[b, NB + a] = 3 * at + 1
            columns[NB + b, NB + a] = 3 * at + 2
    for k in range(NB):
        for x in range(2):
            columns[NU - 1, x * NB + k] = columns[x * NB + k, NU - 1] = 3 * len(PAIRS) + 2 * k + x
    for e in range(expos):
        columns[NU + e, :NU] = [NU * e + 2 * k + x for x in range(2) for k in range(NB)] + [NU * e + NU - 1]
        columns[NU + expos, e] = NU * expos + e
    return np.ascontiguousarray(np.broadcast_to(columns[:, :, None], columns.shape + (LANES,)))


def solve_kernel(table_ref, conv_ref, *refs, width, pixels, tiles):
    sums_refs, refs = refs[:tiles], refs[tiles:]
    *image_refs, coadd_ref, coeffs_ref, tile_ref, sems = refs
    expo_at = lax.axis_index("expo")
    expos = len(image_refs)
    rows, chunk = coadd_ref.shape
    blocks = chunk // LANES
    sub = lax.broadcasted_iota(jnp.int32, (16, LANES), 0)
    lane = lax.broadcasted_iota(jnp.int32, (16, LANES), 1)
    sums = sums_refs[0][...]
    for ref in sums_refs[1:]:
        sums = sums + ref[...]
    first = jnp.broadcast_to(sums[0:1], (16, LANES))
    second = jnp.broadcast_to(sums[4:5], (16, LANES))

    columns = [
        jnp.take_along_axis(first if j < NU else second, table_ref[j], axis=1) for j in range(NU + expos)
    ]
    spread = jnp.take_along_axis(second, table_ref[NU + expos], axis=1)
    weight = [jnp.broadcast_to(spread[e : e + 1], (16, LANES)) for e in range(expos)]
    columns[NU - 1] = jnp.where(sub == NU - 1, float(pixels), columns[NU - 1])

    trace = columns[0][0:1]
    for j in range(1, NU):
        trace = trace + columns[j][j : j + 1]
    scale = 1.0 / trace
    for j in range(NU + expos):
        columns[j] = columns[j] * scale
        if j < NU:
            columns[j] = columns[j] + jnp.where(sub == j, RIDGE / NU, 0.0)
    for i in range(NU):
        inverse = 1.0 / columns[i][i : i + 1]
        for j in range(i + 1, NU + expos):
            factor = columns[j][i : i + 1] * inverse
            columns[j] = jnp.where(sub == i, factor, columns[j] - columns[i] * factor)

    solved = columns[NU:]
    own = solved[0]
    mixed = weight[0] * solved[0]
    for e in range(1, expos):
        own = jnp.where(expo_at == e, solved[e], own)
        mixed = mixed + weight[e] * solved[e]
    diagonal = (sub == lane) & (sub < NU)
    coeffs_ref[...] = jnp.sum(jnp.where(diagonal, own, 0.0), axis=0, keepdims=True)[:, :NU]
    scale = [jnp.broadcast_to(mixed[u : u + 1], (8, LANES)) for u in range(NU)]
    gains = []
    for shift in range(expos):
        gain = weight[0][:8]
        for e in range(1, expos):
            gain = jnp.where(source(expo_at, shift, expos) == e, weight[e][:8], gain)
        gains.append(gain)
    first_col = expo_at * chunk
    copies = []
    for r in range(0, rows, 8):
        for b in range(blocks):
            at = slice(b * LANES, (b + 1) * LANES)
            x = column_positions(first_col, b, width)
            total = -scale[NU - 1]
            for gain, image_ref in zip(gains, image_refs):
                total = total + gain * image_ref[:, at].astype(jnp.float32)[r : r + 8]
            model = (scale[0] + scale[NB] * x) * conv_ref[0, b, r : r + 8]
            for k in range(1, NB):
                model = model + (scale[k] + scale[NB + k] * x) * conv_ref[k, b, r : r + 8]
            tile_ref[r : r + 8, b * LANES : (b + 1) * LANES] = total - model
        copies.append(
            pltpu.make_async_copy(tile_ref.at[pl.ds(r, 8)], coadd_ref.at[pl.ds(r, 8)], sems.at[r // 8])
        )
        copies[-1].start()
    for copy in copies:
        copy.wait()


def swaps(first, size):
    pairs = [(i, i + 1) for i in range(first, size - 1, 2)]
    if first and size % 2 == 0:
        pairs.append((0, size - 1))
    return [pair for a, b in pairs for pair in ((a, b), (b, a))]


def copies_of(block, axis):
    size = lax.axis_size(axis)
    blocks = []
    for shift in far_first(size):
        pairs = [(i, int(target(i, shift, size))) for i in range(size)]
        blocks.append(lax.ppermute(block, axis, pairs) if shift else block)
    return blocks


def tiled_device(template, science, plan, orders, coadd_weight, intersection):
    expos = lax.axis_size("expo")
    tiles = lax.axis_size("tile")
    _, rows, width = template.shape
    steps = science.shape[1]
    chunk = width // expos
    ext = chunk + LANES
    blocks = chunk // LANES
    vmem = pl.BlockSpec(memory_space=pltpu.VMEM)
    small = pltpu.CompilerParams(vmem_limit_bytes=16 * 1024 * 1024)
    hbm = pl.BlockSpec(memory_space=pltpu.HBM)
    coadds = []
    fitted = []
    for step in range(steps):
        *blocks_out, owner, order = pl.pallas_call(
            functools.partial(send_kernel, step=step),
            out_shape=(pltpu.VMEM((rows, ext), template.dtype),) * (2 * expos)
            + (
                jax.ShapeDtypeStruct((rows, LANES), jnp.int32),
                jax.ShapeDtypeStruct((2, NB, 8, LANES), jnp.int32),
            ),
            in_specs=[hbm] * 4,
            out_specs=(vmem,) * (2 * expos + 2),
            scratch_shapes=[
                pltpu.VMEM((rows, width + 2 * LANES), template.dtype),
                pltpu.SMEM(plan.shape, jnp.int32),
                pltpu.SMEM((2, NB), jnp.int32),
                pltpu.SemaphoreType.DMA((expos + 4,)),
            ],
            compiler_params=small,
        )(
            pltpu.with_memory_space_constraint(template[0], pltpu.HBM),
            pltpu.with_memory_space_constraint(science[0, step], pltpu.HBM),
            pltpu.with_memory_space_constraint(plan, pltpu.HBM),
            pltpu.with_memory_space_constraint(orders.T, pltpu.HBM),
        )
        patches, images = blocks_out[:expos], blocks_out[expos:]
        for group in (patches, images):
            for shift in range(1, expos):
                pairs = [(e, int(target(e, shift, expos))) for e in range(expos)]
                group[shift] = lax.ppermute(group[shift], "expo", pairs)
        own = pl.pallas_call(
            pick_kernel,
            out_shape=jax.ShapeDtypeStruct((rows, ext), template.dtype),
            in_specs=[vmem] * (1 + expos),
            out_specs=vmem,
            compiler_params=small,
        )(owner, *(patches[shift] for shift in far_first(expos)))
        row_band, col_band = pl.pallas_call(
            functools.partial(band_kernel, tiles=tiles),
            out_shape=(
                jax.ShapeDtypeStruct((NB * rows, 3 * rows), jnp.bfloat16),
                jax.ShapeDtypeStruct((NB, 2 * LANES, LANES), jnp.bfloat16),
            ),
            in_specs=[vmem, pl.BlockSpec(memory_space=pl.ANY)],
            out_specs=(vmem, vmem),
            compiler_params=small,
            cost_estimate=pl.CostEstimate(flops=4_000_000, bytes_accessed=500_000, transcendentals=200_000),
        )(order, own)
        far = lax.ppermute(own, "tile", swaps(1, tiles))
        near = lax.ppermute(own, "tile", swaps(0, tiles))
        conv, sums = pl.pallas_call(
            functools.partial(fit_kernel, width=width),
            out_shape=(
                jax.ShapeDtypeStruct((NB, blocks, rows, LANES), jnp.float32),
                jax.ShapeDtypeStruct((8, LANES), jnp.float32),
            ),
            in_specs=[vmem] * (7 + expos),
            out_specs=(vmem, vmem),
            scratch_shapes=[
                pltpu.VMEM((NB * rows, ext), jnp.bfloat16),
                pltpu.VMEM((80 + 14 * expos + 8, 8, LANES), jnp.float32),
            ],
            compiler_params=small,
        )(
            coadd_weight[:, step : step + 1],
            intersection[:, step : step + 1],
            row_band,
            col_band,
            own,
            near,
            far,
            *(images[shift] for shift in far_first(expos)),
        )
        sums = pl.pallas_call(
            add_kernel,
            out_shape=jax.ShapeDtypeStruct((8, LANES), jnp.float32),
            in_specs=[vmem] * expos,
            out_specs=vmem,
            compiler_params=small,
        )(*copies_of(sums, "expo"))
        sums = copies_of(sums, "tile")
        coadd, coeffs = pl.pallas_call(
            functools.partial(solve_kernel, width=width, pixels=tiles * rows * width, tiles=tiles),
            out_shape=(
                jax.ShapeDtypeStruct((rows, chunk), jnp.float32),
                jax.ShapeDtypeStruct((1, NU), jnp.float32),
            ),
            in_specs=[vmem] * (2 + tiles + expos),
            out_specs=(pl.BlockSpec(memory_space=pl.ANY), vmem),
            scratch_shapes=[
                pltpu.VMEM((rows, chunk), jnp.float32),
                pltpu.SemaphoreType.DMA((rows // 8,)),
            ],
            compiler_params=small,
        )(jnp.asarray(table(expos)), conv, *sums, *images)
        coadds.append(coadd[None])
        fitted.append(coeffs)
    return (jnp.concatenate(coadds), jnp.stack(fitted, axis=1))


def broadcast(block, axis, holder):
    block = jnp.where(lax.axis_index(axis) == holder, block, jnp.zeros_like(block))
    return lax.psum(block, axis)


def extended(x, sides, width):
    for axis, dim in sides:
        size, length = (lax.axis_size(axis), x.shape[dim])
        up = [(i, (i + 1) % size) for i in range(size - 1)]
        down = [(j, i) for i, j in up]
        last = lax.slice_in_dim(x, length - width, length, axis=dim)
        first = lax.slice_in_dim(x, 0, width, axis=dim)
        before = lax.ppermute(last, axis, up)
        after = lax.ppermute(first, axis, down)
        x = jnp.concatenate([before, x, after], axis=dim)
    return x


def make_filters(orders):
    taps_pos = jnp.arange(2 * HALF + 1).astype(jnp.float32) - HALF
    row_list = []
    col_list = []
    for basis in range(NB):
        sigma = SIGMAS[basis]
        envelope = jnp.exp(-taps_pos * taps_pos / (2.0 * sigma * sigma))
        row_filter = envelope * power_of(taps_pos, orders[basis, 0])
        col_filter = envelope * power_of(taps_pos, orders[basis, 1])
        row_list.append(row_filter / jnp.sqrt(jnp.sum(row_filter * row_filter)))
        col_list.append(col_filter / jnp.sqrt(jnp.sum(col_filter * col_filter)))
    return (jnp.stack(row_list).astype(jnp.bfloat16), jnp.stack(col_list).astype(jnp.bfloat16))


def band_matrix(filters, out_len, in_len):
    offset = jnp.arange(in_len)[None, :] - jnp.arange(out_len)[:, None]
    taps_idx = jnp.arange(2 * HALF + 1)
    picks = (offset[:, :, None] == taps_idx[None, None, :]).astype(jnp.float32)
    band = jnp.einsum("ijt,kt->kij", picks, filters.astype(jnp.float32))
    return band.astype(jnp.bfloat16)


def any_device(template, science, plan, orders, coadd_weight, intersection):
    row_filters, col_filters = make_filters(orders)
    rows = template.shape[1]
    width = template.shape[2]
    blocks_count = width // 128
    steps_count = science.shape[1]
    row_band = band_matrix(row_filters, rows, rows + 2 * HALF)
    col_band = jnp.transpose(band_matrix(col_filters, 128, 128 + 2 * HALF), (0, 2, 1))
    column_pos = 2.0 * (jnp.arange(width).astype(jnp.float32) + 0.5) / width - 1.0
    pieces = []
    fitted = []
    for step in range(steps_count):
        received = broadcast(template[0], "expo", plan[step])
        padded = extended(received, (("tile", 0),), HALF)
        rowconv = jnp.einsum(
            "kij,jw->kiw", row_band, padded, preferred_element_type=jnp.float32
        ).astype(jnp.bfloat16)
        blocks = rowconv.reshape(NB, rows, blocks_count, 128)
        empty_rim = jnp.zeros((NB, rows, 1, HALF), jnp.bfloat16)
        previous = jnp.concatenate([empty_rim, blocks[:, :, :-1, 128 - HALF :]], axis=2)
        following = jnp.concatenate([blocks[:, :, 1:, :HALF], empty_rim], axis=2)
        window = jnp.concatenate([previous, blocks, following], axis=3)
        conv = jnp.einsum("krbj,kjc->krbc", window, col_band, preferred_element_type=jnp.float32)
        conv = conv.reshape(NB, rows, width)
        fields = jnp.concatenate(
            [conv, conv * column_pos, jnp.ones((1, rows, width), jnp.float32)], axis=0
        )
        fields = fields.reshape(NU, rows * width)
        exposure_image = science[0, step].astype(jnp.float32).reshape(rows * width)
        normal_local = jnp.dot(fields, fields.T, precision=lax.Precision.HIGHEST)
        project_local = jnp.dot(fields, exposure_image, precision=lax.Precision.HIGHEST)
        normal_matrix, projections = lax.psum((normal_local, project_local), "tile")
        normal_matrix = normal_matrix + RIDGE * (jnp.trace(normal_matrix) / NU) * jnp.eye(
            NU, dtype=jnp.float32
        )
        factor = jnp.linalg.cholesky(normal_matrix)
        coeffs = jax.scipy.linalg.cho_solve((factor, True), projections)
        model = jnp.dot(coeffs, fields, precision=lax.Precision.HIGHEST)
        difference = exposure_image - model
        weight_now = coadd_weight[0, step] * intersection[0, step].astype(jnp.float32)
        pieces.append((weight_now * difference).reshape(rows, width))
        fitted.append(coeffs)
    weighted = jnp.stack(pieces)
    received_parts = lax.all_to_all(weighted[None], "expo", split_axis=3, concat_axis=0, tiled=True)
    coadd = jnp.sum(received_parts, axis=0)
    return (coadd, jnp.stack(fitted)[None])


def per_device(template, science, plan, orders, coadd_weight, intersection):
    expos = lax.axis_size("expo")
    rows, width = template.shape[1:]
    whole_lanes = width % (expos * LANES) == 0 and rows % 16 == 0 and 3 * rows <= LANES
    few = (NU + 1) * expos <= LANES and NU + expos <= LANES
    body = tiled_device if whole_lanes and few else any_device
    return body(template, science, plan, orders, coadd_weight, intersection)


def solution(mesh):
    return jax.shard_map(
        per_device,
        mesh=mesh,
        in_specs=(
            P(("groups", "expo"), "tile", None),
            P(("groups", "expo"), None, "tile", None),
            P("groups"),
            P(),
            P(("groups", "expo"), None),
            P(("groups", "expo"), None),
        ),
        out_specs=(P("groups", "tile", "expo"), P(("groups", "expo"), None, None)),
        check_vma=False,
    )
```

```python
import functools

import jax
import jax.numpy as jnp
import numpy as np
from jax import lax
from jax.experimental import pallas as pl
from jax.experimental.pallas import tpu as pltpu
from jax.sharding import PartitionSpec as P

HALF = 15
NB = 6
NU = 13
LANES = 128
BEYOND = 1000
STAGE_COST = 700_000_000
PAIRS = [(j, k) for j in range(NB) for k in range(j, NB)]

SIGMAS = (0.8, 1.4, 2.2, 3.0, 4.0, 5.5)
RIDGE = 0.05


def power_of(pos, order):
    return jnp.where(order == 0, 1.0, jnp.where(order == 1, pos, pos * pos))


def tap_values(pos, sigma, order):
    value = jnp.exp(-pos * pos / (2.0 * sigma * sigma)) * power_of(pos, order)
    return jnp.where(jnp.abs(pos) <= HALF, value, 0.0)


def tap_norm(sigma, order):
    pos = lax.broadcasted_iota(jnp.int32, (8, LANES), 1).astype(jnp.float32) - HALF
    value = tap_values(pos, sigma, order)
    return jnp.sqrt(jnp.sum(value * value, axis=1, keepdims=True))


def target(me, shift, size):
    return me ^ shift if size & (size - 1) == 0 else (me + shift) % size


def source(me, shift, size):
    return me ^ shift if size & (size - 1) == 0 else (me - shift + size) % size


def far_first(size):
    return [*range(size // 2, size), *range(1, size // 2), 0] if size > 1 else [0]


def joint(shift, size):
    return shift < size // 2


def send_kernel(template_ref, science_ref, plan_ref, orders_ref, *refs, step):
    *out_refs, owner_ref, order_ref, patch_ref, plan_now, orders_now, sems = refs
    size = sems.shape[0] - 4
    rows, width = science_ref.shape
    chunk = width // size
    ext = chunk + LANES
    patch_refs, image_refs = out_refs[:size], out_refs[size:]
    half = size * chunk // 2
    me = lax.axis_index("expo")
    starts = [pl.multiple_of(target(me, shift, size) * chunk, chunk) for shift in range(size)]
    loads = [
        pltpu.make_async_copy(
            template_ref.at[:, pl.ds(i * half, half)], patch_ref.at[:, pl.ds((i * half + LANES), half)], sems.at[i]
        )
        for i in range(2)
    ]
    copies = [
        pltpu.make_async_copy(
            science_ref.at[:, pl.ds(starts[shift], chunk)],
            patch_refs[shift].at[:, pl.ds(ext, chunk)]
            if joint(shift, size)
            else image_refs[shift - size // 2].at[:, pl.ds(0, chunk)],
            sems.at[3 + shift],
        )
        for shift in range(size)
    ]
    copies.append(pltpu.make_async_copy(plan_ref, plan_now, sems.at[2]))
    copies.append(pltpu.make_async_copy(orders_ref, orders_now, sems.at[3 + size]))
    for copy in loads + copies:
        copy.start()
    blank = jnp.zeros((rows, LANES), patch_ref.dtype)
    patch_ref[:, :LANES] = blank
    patch_ref[:, size * chunk + LANES :] = blank
    for image_ref in image_refs:
        image_ref[:, chunk:] = blank
    for copy in loads:
        copy.wait()
    lane = lax.broadcasted_iota(jnp.int32, (rows, LANES), 1)
    for shift in range(size):
        start = starts[shift]
        patch_refs[shift][:, :chunk] = patch_ref[:, pl.ds(start + LANES, chunk)]
        before = patch_ref[:, pl.ds(start, LANES)].astype(jnp.float32)
        after = patch_ref[:, pl.ds(start + chunk + LANES, LANES)].astype(jnp.float32)
        rim = jnp.where(lane < LANES // 2, after, before)
        patch_refs[shift][:, chunk:ext] = rim.astype(patch_ref.dtype)
    for copy in copies:
        copy.wait()
    owner_ref[...] = jnp.full(owner_ref.shape, plan_now[step], jnp.int32)
    for way in range(2):
        for k in range(NB):
            order_ref[way, k] = jnp.full((8, LANES), orders_now[way, k], jnp.int32)


def choose_kernel(owner_ref, *refs, shifts, size):
    *recv_refs, out_ref = refs
    me = lax.axis_index("expo")
    for b in range(out_ref.shape[1] // LANES):
        columns = slice(b * LANES, (b + 1) * LANES)
        block = recv_refs[0][:, columns].astype(jnp.float32)
        for shift, ref in zip(shifts, recv_refs[1:]):
            block = jnp.where(
                owner_ref[...] == source(me, shift, size), ref[:, columns].astype(jnp.float32), block
            )
        out_ref[:, columns] = block.astype(out_ref.dtype)


def pick_kernel(owner_ref, *refs, shifts, size):
    *recv_refs, out_ref, block_ref = refs
    ext = out_ref.shape[1]
    choose_kernel(owner_ref, *recv_refs, block_ref, shifts=shifts, size=size)
    whole = jnp.concatenate([block_ref[:, ext - LANES :], block_ref[...]], axis=1)
    out_ref[...] = whole[:, LANES - HALF : LANES - HALF + ext]


def column_positions(first_col, block, width):
    col = lax.broadcasted_iota(jnp.int32, (8, LANES), 1) + (first_col + block * LANES)
    return 2.0 * (col.astype(jnp.float32) + 0.5) / width - 1.0


def band_kernel(order_ref, _, row_ref, col_ref, *, tiles):
    rows = row_ref.shape[0] // NB
    tile_at = lax.axis_index("tile")
    near = 1 - 2 * lax.rem(tile_at, 2)
    near_move = jnp.where(tile_at + near < tiles, near - 1, BEYOND)
    far_move = jnp.where((tile_at >= near) & (tile_at - near < tiles), -near - 2, BEYOND)
    row_from = lax.broadcasted_iota(jnp.int32, (8, LANES), 1)
    moved = jnp.where(row_from < rows, 0, jnp.where(row_from < 2 * rows, near_move, far_move))
    sub = lax.broadcasted_iota(jnp.int32, (8, LANES), 0)
    lane = lax.broadcasted_iota(jnp.int32, (8, LANES), 1)
    shift = (sub - jnp.where(lane < LANES // 2, lane, lane - LANES) - HALF).astype(jnp.float32)
    for k in range(NB):
        norm = tap_norm(SIGMAS[k], order_ref[0, k])
        for r in range(0, rows, 16):
            parts = []
            for half in (r, r + 8):
                offset = (row_from + moved * rows - sub - half).astype(jnp.float32)
                parts.append(tap_values(offset, SIGMAS[k], order_ref[0, k]) / norm)
            both = jnp.concatenate(parts, axis=0).astype(jnp.bfloat16)
            row_ref[k * rows + r : k * rows + r + 16] = both[:, : 3 * rows]
        norm = tap_norm(SIGMAS[k], order_ref[1, k])
        pattern = tap_values(shift, SIGMAS[k], order_ref[1, k]) / norm
        for r in range(0, 2 * LANES, 16):
            parts = []
            for half in (r, r + 8):
                moved_on = pltpu.roll(pattern, half % LANES, 1) if half % LANES else pattern
                inside = lane <= half + 7 if half < LANES else lane >= half - LANES + LANES // 2
                parts.append(jnp.where(inside, moved_on, 0.0))
            col_ref[k, r : r + 16] = jnp.concatenate(parts, axis=0).astype(jnp.bfloat16)


def image_blocks(ref, size, shift, chunk):
    first = chunk + LANES if joint(shift, size) else 0
    return lambda b: ref[:, first + b * LANES : first + (b + 1) * LANES].astype(jnp.float32)


def fit_kernel(weight_ref, hits_ref, row_band_ref, col_band_ref, own_ref, near_ref, far_ref, *refs, width):
    *image_refs, conv_ref, sums_ref, row_ref, parts_ref = refs
    image_refs = dict(zip(far_first(len(image_refs)), image_refs))
    tile_at = lax.axis_index("tile")
    expo_at = lax.axis_index("expo")
    rows, ext = own_ref.shape
    expos = len(image_refs)
    chunk = ext - LANES
    blocks = chunk // LANES

    patch = jnp.concatenate([own_ref[...], near_ref[...], far_ref[...]], axis=0)
    row_ref[...] = jnp.dot(
        row_band_ref[...], patch, preferred_element_type=jnp.float32
    ).astype(jnp.bfloat16)
    for k in range(NB):
        window = jnp.concatenate(
            [
                row_ref[k * rows : (k + 1) * rows, b * LANES : (b + 2) * LANES]
                for b in range(blocks)
            ],
            axis=0,
        )
        out = jnp.dot(window, col_band_ref[k], preferred_element_type=jnp.float32)
        conv_ref[k] = out.reshape(blocks, rows, LANES)

    first_col = expo_at * chunk
    xs = [column_positions(first_col, b, width) for b in range(blocks)]

    def fold(x):
        total = x[:8]
        for i in range(8, rows, 8):
            total = total + x[i : i + 8]
        return total

    def moments(at, left, right, count):
        total = [None] * count
        for b in range(blocks):
            term = fold(left(b) * right(b)) if right is not None else fold(left(b))
            for i in range(count):
                total[i] = term if total[i] is None else total[i] + term
                if i < count - 1:
                    term = term * xs[b]
        for i in range(count):
            parts_ref[at + i] = total[i]

    def conv(k):
        return lambda b: conv_ref[k, b]

    def sci(shift):
        return image_blocks(image_refs[shift], expos, shift, chunk)

    blank = jnp.zeros((8, LANES), jnp.float32)
    at = 0
    for j, k in PAIRS:
        moments(at, conv(j), conv(k), 3)
        at += 3
    for k in range(NB):
        moments(at, conv(k), None, 2)
        at += 2
    while at % 8:
        parts_ref[at] = blank
        at += 1
    begin = at
    for shift in range(expos):
        row = at + NU * source(expo_at, shift, expos)
        for k in range(NB):
            moments(row + 2 * k, conv(k), sci(shift), 2)
        moments(row + NU - 1, sci(shift), None, 1)
    at += NU * expos
    weight = jnp.broadcast_to(weight_ref[...] * hits_ref[...].astype(jnp.float32), (8, LANES))
    weight = jnp.where(tile_at == 0, weight, 0.0)
    spot = (
        (lax.broadcasted_iota(jnp.int32, (8, LANES), 0) == 0)
        & (lax.broadcasted_iota(jnp.int32, (8, LANES), 1) == 0)
    )
    for e in range(expos):
        parts_ref[at + e] = jnp.where(spot & (expo_at == e), weight, 0.0)
    at += expos
    while at % 8:
        parts_ref[at] = blank
        at += 1
    lanes = []
    for first, last in ((0, begin), (begin, at)):
        lanes.append(jnp.sum(parts_ref[first:last], axis=1))
        if last - first < LANES:
            lanes.append(jnp.zeros((LANES - (last - first), LANES), jnp.float32))
    rest = jnp.concatenate(lanes, axis=0)
    thirds = []
    for _ in range(3):
        thirds.append(rest.astype(jnp.bfloat16))
        rest = rest - thirds[-1].astype(jnp.float32)
    line = lax.dot_general(
        jnp.ones((16, 3 * LANES), jnp.bfloat16),
        jnp.concatenate(thirds, axis=1),
        (((1,), (1,)), ((), ())),
        preferred_element_type=jnp.float32,
    )[:8]
    both = jnp.where(lax.broadcasted_iota(jnp.int32, (8, LANES), 0) < 4, line[:, :LANES], line[:, LANES:])
    for i in range(sums_ref.shape[0]):
        sums_ref[i] = both


def table(expos):
    columns = np.zeros((NU + expos + 1, 16), np.int32)
    for at, (j, k) in enumerate(PAIRS):
        for a, b in ((j, k), (k, j)):
            columns[b, a] = 3 * at
            columns[NB + b, a] = columns[b, NB + a] = 3 * at + 1
            columns[NB + b, NB + a] = 3 * at + 2
    for k in range(NB):
        for x in range(2):
            columns[NU - 1, x * NB + k] = columns[x * NB + k, NU - 1] = 3 * len(PAIRS) + 2 * k + x
    for e in range(expos):
        columns[NU + e, :NU] = [NU * e + 2 * k + x for x in range(2) for k in range(NB)] + [NU * e + NU - 1]
        columns[NU + expos, e] = NU * expos + e
    return np.ascontiguousarray(np.broadcast_to(columns[:, :, None], columns.shape + (LANES,)))


def solve_kernel(table_ref, sums_ref, conv_ref, *refs, width, pixels):
    *image_refs, coadd_ref, coeffs_ref, tile_ref, sems = refs
    expo_at = lax.axis_index("expo")
    expos = len(image_refs)
    rows, chunk = coadd_ref.shape
    blocks = chunk // LANES
    images = [image_blocks(ref, expos, shift, chunk) for shift, ref in enumerate(image_refs)]
    sub = lax.broadcasted_iota(jnp.int32, (16, LANES), 0)
    lane = lax.broadcasted_iota(jnp.int32, (16, LANES), 1)
    blocks_left = [sums_ref[i] for i in range(sums_ref.shape[0])]
    while len(blocks_left) > 1:
        odd = blocks_left[len(blocks_left) // 2 * 2 :]
        blocks_left = [x + y for x, y in zip(blocks_left[::2], blocks_left[1::2])] + odd
    sums = blocks_left[0]
    first = jnp.broadcast_to(sums[0:1], (16, LANES))
    second = jnp.broadcast_to(sums[4:5], (16, LANES))

    columns = [
        jnp.take_along_axis(first if j < NU else second, table_ref[j], axis=1) for j in range(NU + expos)
    ]
    spread = jnp.take_along_axis(second, table_ref[NU + expos], axis=1)
    weight = [jnp.broadcast_to(spread[e : e + 1], (16, LANES)) for e in range(expos)]
    columns[NU - 1] = jnp.where(sub == NU - 1, float(pixels), columns[NU - 1])

    trace = columns[0][0:1]
    for j in range(1, NU):
        trace = trace + columns[j][j : j + 1]
    scale = 1.0 / trace
    for j in range(NU + expos):
        columns[j] = columns[j] * scale
        if j < NU:
            columns[j] = columns[j] + jnp.where(sub == j, RIDGE / NU, 0.0)
    for i in range(0, NU - 1, 2):
        one, two = columns[i], columns[i + 1]
        a, b = one[i : i + 1], two[i : i + 1]
        c, d = one[i + 1 : i + 2], two[i + 1 : i + 2]
        inverse = 1.0 / (a * d - b * c)
        a, b, c, d = a * inverse, b * inverse, c * inverse, d * inverse
        for j in range(i + 2, NU + expos):
            upper, lower = columns[j][i : i + 1], columns[j][i + 1 : i + 2]
            first, second = d * upper - b * lower, a * lower - c * upper
            rest = columns[j] - one * first - two * second
            columns[j] = jnp.where(sub == i, first, jnp.where(sub == i + 1, second, rest))
    end = NU - 1
    inverse = 1.0 / columns[end][end:NU]
    for j in range(NU, NU + expos):
        factor = columns[j][end:NU] * inverse
        columns[j] = jnp.where(sub == end, factor, columns[j] - columns[end] * factor)

    solved = columns[NU:]
    own = solved[0]
    mixed = weight[0] * solved[0]
    for e in range(1, expos):
        own = jnp.where(expo_at == e, solved[e], own)
        mixed = mixed + weight[e] * solved[e]
    diagonal = (sub == lane) & (sub < NU)
    coeffs_ref[...] = jnp.sum(jnp.where(diagonal, own, 0.0), axis=0, keepdims=True)[:, :NU]
    scale = [jnp.broadcast_to(mixed[u : u + 1], (8, LANES)) for u in range(NU)]
    gains = []
    for shift in range(expos):
        gain = weight[0][:8]
        for e in range(1, expos):
            gain = jnp.where(source(expo_at, shift, expos) == e, weight[e][:8], gain)
        gains.append(gain)
    first_col = expo_at * chunk
    copies = []
    for r in range(0, rows, 8):
        for b in range(blocks):
            x = column_positions(first_col, b, width)
            total = -scale[NU - 1]
            for gain, image in zip(gains, images):
                total = total + gain * image(b)[r : r + 8]
            model = (scale[0] + scale[NB] * x) * conv_ref[0, b, r : r + 8]
            for k in range(1, NB):
                model = model + (scale[k] + scale[NB + k] * x) * conv_ref[k, b, r : r + 8]
            tile_ref[r : r + 8, b * LANES : (b + 1) * LANES] = total - model
        copies.append(
            pltpu.make_async_copy(tile_ref.at[pl.ds(r, 8)], coadd_ref.at[pl.ds(r, 8)], sems.at[r // 8])
        )
        copies[-1].start()
    for copy in copies:
        copy.wait()


def swaps(first, size):
    pairs = [(i, i + 1) for i in range(first, size - 1, 2)]
    if first and size % 2 == 0:
        pairs.append((0, size - 1))
    return [pair for a, b in pairs for pair in ((a, b), (b, a))]


def tiled_device(template, science, plan, orders, coadd_weight, intersection):
    expos = lax.axis_size("expo")
    tiles = lax.axis_size("tile")
    _, rows, width = template.shape
    steps = science.shape[1]
    chunk = width // expos
    ext = chunk + LANES
    blocks = chunk // LANES
    vmem = pl.BlockSpec(memory_space=pltpu.VMEM)
    small = pltpu.CompilerParams(vmem_limit_bytes=16 * 1024 * 1024)
    hbm = pl.BlockSpec(memory_space=pltpu.HBM)
    coadds = []
    fitted = []
    for step in range(steps):
        *blocks_out, owner, order = pl.pallas_call(
            functools.partial(send_kernel, step=step),
            out_shape=tuple(
                pltpu.VMEM((rows, ext + chunk if joint(shift, expos) else ext), template.dtype)
                for shift in range(expos)
            )
            + (pltpu.VMEM((rows, ext), science.dtype),) * (expos - expos // 2)
            + (
                jax.ShapeDtypeStruct((rows, LANES), jnp.int32),
                jax.ShapeDtypeStruct((2, NB, 8, LANES), jnp.int32),
            ),
            in_specs=[hbm] * 4,
            out_specs=(vmem,) * (2 * expos - expos // 2 + 2),
            scratch_shapes=[
                pltpu.VMEM((rows, width + 2 * LANES), template.dtype),
                pltpu.SMEM(plan.shape, jnp.int32),
                pltpu.SMEM((2, NB), jnp.int32),
                pltpu.SemaphoreType.DMA((expos + 4,)),
            ],
            compiler_params=small,
        )(
            pltpu.with_memory_space_constraint(template[0], pltpu.HBM),
            pltpu.with_memory_space_constraint(science[0, step], pltpu.HBM),
            pltpu.with_memory_space_constraint(plan, pltpu.HBM),
            pltpu.with_memory_space_constraint(orders.T, pltpu.HBM),
        )
        patches, images = blocks_out[:expos], blocks_out[expos:]
        for group, first in ((patches, 0), (images, expos // 2)):
            for shift in range(max(first, 1), expos):
                pairs = [(e, int(target(e, shift, expos))) for e in range(expos)]
                group[shift - first] = lax.ppermute(group[shift - first], "expo", pairs)
        images = patches[: expos // 2] + images
        across = [shift for shift in range(1, expos) if not joint(shift, expos)]
        beside = [shift for shift in range(1, expos) if joint(shift, expos)]
        block = pl.pallas_call(
            functools.partial(choose_kernel, shifts=across, size=expos),
            out_shape=jax.ShapeDtypeStruct((rows, ext), template.dtype),
            in_specs=[vmem] * (2 + len(across)),
            out_specs=vmem,
            compiler_params=small,
            cost_estimate=pl.CostEstimate(flops=STAGE_COST, bytes_accessed=500_000, transcendentals=0),
        )(owner, patches[0], *(patches[shift] for shift in across))
        own = pl.pallas_call(
            functools.partial(pick_kernel, shifts=beside, size=expos),
            out_shape=jax.ShapeDtypeStruct((rows, ext), template.dtype),
            in_specs=[vmem] * (2 + len(beside)),
            out_specs=vmem,
            scratch_shapes=[pltpu.VMEM((rows, ext), template.dtype)],
            compiler_params=small,
        )(owner, block, *(patches[shift] for shift in beside))
        row_band, col_band = pl.pallas_call(
            functools.partial(band_kernel, tiles=tiles),
            out_shape=(
                jax.ShapeDtypeStruct((NB * rows, 3 * rows), jnp.bfloat16),
                jax.ShapeDtypeStruct((NB, 2 * LANES, LANES), jnp.bfloat16),
            ),
            in_specs=[vmem, pl.BlockSpec(memory_space=pl.ANY)],
            out_specs=(vmem, vmem),
            compiler_params=small,
            cost_estimate=pl.CostEstimate(flops=4_000_000, bytes_accessed=500_000, transcendentals=200_000),
        )(order, own)
        far = lax.ppermute(own, "tile", swaps(1, tiles))
        near = lax.ppermute(own, "tile", swaps(0, tiles))
        conv, sums = pl.pallas_call(
            functools.partial(fit_kernel, width=width),
            out_shape=(
                jax.ShapeDtypeStruct((NB, blocks, rows, LANES), jnp.float32),
                jax.ShapeDtypeStruct((tiles * expos, 8, LANES), jnp.float32),
            ),
            in_specs=[vmem] * (7 + expos),
            out_specs=(vmem, vmem),
            scratch_shapes=[
                pltpu.VMEM((NB * rows, ext), jnp.bfloat16),
                pltpu.VMEM((80 + 14 * expos + 8, 8, LANES), jnp.float32),
            ],
            compiler_params=small,
        )(
            coadd_weight[:, step : step + 1],
            intersection[:, step : step + 1],
            row_band,
            col_band,
            own,
            near,
            far,
            *(images[shift] for shift in far_first(expos)),
        )
        sums = lax.all_to_all(sums, ("tile", "expo"), split_axis=0, concat_axis=0, tiled=True)
        coadd, coeffs = pl.pallas_call(
            functools.partial(solve_kernel, width=width, pixels=tiles * rows * width),
            out_shape=(
                jax.ShapeDtypeStruct((rows, chunk), jnp.float32),
                jax.ShapeDtypeStruct((1, NU), jnp.float32),
            ),
            in_specs=[vmem] * (3 + expos),
            out_specs=(pl.BlockSpec(memory_space=pl.ANY), vmem),
            scratch_shapes=[
                pltpu.VMEM((rows, chunk), jnp.float32),
                pltpu.SemaphoreType.DMA((rows // 8,)),
            ],
            compiler_params=small,
        )(jnp.asarray(table(expos)), sums, conv, *images)
        coadds.append(coadd[None])
        fitted.append(coeffs)
    return (jnp.concatenate(coadds), jnp.stack(fitted, axis=1))


def broadcast(block, axis, holder):
    block = jnp.where(lax.axis_index(axis) == holder, block, jnp.zeros_like(block))
    return lax.psum(block, axis)


def extended(x, sides, width):
    for axis, dim in sides:
        size, length = (lax.axis_size(axis), x.shape[dim])
        up = [(i, (i + 1) % size) for i in range(size - 1)]
        down = [(j, i) for i, j in up]
        last = lax.slice_in_dim(x, length - width, length, axis=dim)
        first = lax.slice_in_dim(x, 0, width, axis=dim)
        before = lax.ppermute(last, axis, up)
        after = lax.ppermute(first, axis, down)
        x = jnp.concatenate([before, x, after], axis=dim)
    return x


def make_filters(orders):
    taps_pos = jnp.arange(2 * HALF + 1).astype(jnp.float32) - HALF
    row_list = []
    col_list = []
    for basis in range(NB):
        sigma = SIGMAS[basis]
        envelope = jnp.exp(-taps_pos * taps_pos / (2.0 * sigma * sigma))
        row_filter = envelope * power_of(taps_pos, orders[basis, 0])
        col_filter = envelope * power_of(taps_pos, orders[basis, 1])
        row_list.append(row_filter / jnp.sqrt(jnp.sum(row_filter * row_filter)))
        col_list.append(col_filter / jnp.sqrt(jnp.sum(col_filter * col_filter)))
    return (jnp.stack(row_list).astype(jnp.bfloat16), jnp.stack(col_list).astype(jnp.bfloat16))


def band_matrix(filters, out_len, in_len):
    offset = jnp.arange(in_len)[None, :] - jnp.arange(out_len)[:, None]
    taps_idx = jnp.arange(2 * HALF + 1)
    picks = (offset[:, :, None] == taps_idx[None, None, :]).astype(jnp.float32)
    band = jnp.einsum("ijt,kt->kij", picks, filters.astype(jnp.float32))
    return band.astype(jnp.bfloat16)


def any_device(template, science, plan, orders, coadd_weight, intersection):
    row_filters, col_filters = make_filters(orders)
    rows = template.shape[1]
    width = template.shape[2]
    blocks_count = width // 128
    steps_count = science.shape[1]
    row_band = band_matrix(row_filters, rows, rows + 2 * HALF)
    col_band = jnp.transpose(band_matrix(col_filters, 128, 128 + 2 * HALF), (0, 2, 1))
    column_pos = 2.0 * (jnp.arange(width).astype(jnp.float32) + 0.5) / width - 1.0
    pieces = []
    fitted = []
    for step in range(steps_count):
        received = broadcast(template[0], "expo", plan[step])
        padded = extended(received, (("tile", 0),), HALF)
        rowconv = jnp.einsum(
            "kij,jw->kiw", row_band, padded, preferred_element_type=jnp.float32
        ).astype(jnp.bfloat16)
        blocks = rowconv.reshape(NB, rows, blocks_count, 128)
        empty_rim = jnp.zeros((NB, rows, 1, HALF), jnp.bfloat16)
        previous = jnp.concatenate([empty_rim, blocks[:, :, :-1, 128 - HALF :]], axis=2)
        following = jnp.concatenate([blocks[:, :, 1:, :HALF], empty_rim], axis=2)
        window = jnp.concatenate([previous, blocks, following], axis=3)
        conv = jnp.einsum("krbj,kjc->krbc", window, col_band, preferred_element_type=jnp.float32)
        conv = conv.reshape(NB, rows, width)
        fields = jnp.concatenate(
            [conv, conv * column_pos, jnp.ones((1, rows, width), jnp.float32)], axis=0
        )
        fields = fields.reshape(NU, rows * width)
        exposure_image = science[0, step].astype(jnp.float32).reshape(rows * width)
        normal_local = jnp.dot(fields, fields.T, precision=lax.Precision.HIGHEST)
        project_local = jnp.dot(fields, exposure_image, precision=lax.Precision.HIGHEST)
        normal_matrix, projections = lax.psum((normal_local, project_local), "tile")
        normal_matrix = normal_matrix + RIDGE * (jnp.trace(normal_matrix) / NU) * jnp.eye(
            NU, dtype=jnp.float32
        )
        factor = jnp.linalg.cholesky(normal_matrix)
        coeffs = jax.scipy.linalg.cho_solve((factor, True), projections)
        model = jnp.dot(coeffs, fields, precision=lax.Precision.HIGHEST)
        difference = exposure_image - model
        weight_now = coadd_weight[0, step] * intersection[0, step].astype(jnp.float32)
        pieces.append((weight_now * difference).reshape(rows, width))
        fitted.append(coeffs)
    weighted = jnp.stack(pieces)
    received_parts = lax.all_to_all(weighted[None], "expo", split_axis=3, concat_axis=0, tiled=True)
    coadd = jnp.sum(received_parts, axis=0)
    return (coadd, jnp.stack(fitted)[None])


def per_device(template, science, plan, orders, coadd_weight, intersection):
    expos = lax.axis_size("expo")
    rows, width = template.shape[1:]
    whole_lanes = width % (expos * LANES) == 0 and rows % 16 == 0 and 3 * rows <= LANES
    few = (NU + 1) * expos <= LANES and NU + expos <= LANES
    body = tiled_device if whole_lanes and few else any_device
    return body(template, science, plan, orders, coadd_weight, intersection)


def solution(mesh):
    return jax.shard_map(
        per_device,
        mesh=mesh,
        in_specs=(
            P(("groups", "expo"), "tile", None),
            P(("groups", "expo"), None, "tile", None),
            P("groups"),
            P(),
            P(("groups", "expo"), None),
            P(("groups", "expo"), None),
        ),
        out_specs=(P("groups", "tile", "expo"), P(("groups", "expo"), None, None)),
        check_vma=False,
    )
```

```python
import functools

import jax
import jax.numpy as jnp
import numpy as np
from jax import lax
from jax.experimental import pallas as pl
from jax.experimental.pallas import tpu as pltpu
from jax.sharding import PartitionSpec as P

HALF = 15
NB = 6
NU = 13
LANES = 128
BEYOND = 1000
STAGE_COST = 700_000_000
PAIRS = [(j, k) for j in range(NB) for k in range(j, NB)]

SIGMAS = (0.8, 1.4, 2.2, 3.0, 4.0, 5.5)
RIDGE = 0.05


def power_of(pos, order):
    return jnp.where(order == 0, 1.0, jnp.where(order == 1, pos, pos * pos))


def tap_values(pos, sigma, order):
    value = jnp.exp(-pos * pos / (2.0 * sigma * sigma)) * power_of(pos, order)
    return jnp.where(jnp.abs(pos) <= HALF, value, 0.0)


def tap_norm(sigma, order):
    pos = lax.broadcasted_iota(jnp.int32, (8, LANES), 1).astype(jnp.float32) - HALF
    value = tap_values(pos, sigma, order)
    return jnp.sqrt(jnp.sum(value * value, axis=1, keepdims=True))


def target(me, shift, size):
    return me ^ shift if size & (size - 1) == 0 else (me + shift) % size


def source(me, shift, size):
    return me ^ shift if size & (size - 1) == 0 else (me - shift + size) % size


def far_first(size):
    return [*range(size - 1, 0, -1), 0]


def joint(shift, size):
    return shift < size // 2


def send_kernel(template_ref, science_ref, plan_ref, orders_ref, *refs, step):
    *out_refs, owner_ref, order_ref, patch_ref, plan_now, orders_now, sems = refs
    size = sems.shape[0] - 4
    rows, width = science_ref.shape
    chunk = width // size
    ext = chunk + LANES
    patch_refs, image_refs = out_refs[:size], out_refs[size:]
    half = size * chunk // 2
    me = lax.axis_index("expo")
    starts = [pl.multiple_of(target(me, shift, size) * chunk, chunk) for shift in range(size)]
    loads = [
        pltpu.make_async_copy(
            template_ref.at[:, pl.ds(i * half, half)], patch_ref.at[:, pl.ds((i * half + LANES), half)], sems.at[i]
        )
        for i in range(2)
    ]
    copies = [
        pltpu.make_async_copy(
            science_ref.at[:, pl.ds(starts[shift], chunk)],
            patch_refs[shift].at[:, pl.ds(ext, chunk)]
            if joint(shift, size)
            else image_refs[shift - size // 2].at[:, pl.ds(0, chunk)],
            sems.at[3 + shift],
        )
        for shift in range(size)
    ]
    copies.append(pltpu.make_async_copy(plan_ref, plan_now, sems.at[2]))
    copies.append(pltpu.make_async_copy(orders_ref, orders_now, sems.at[3 + size]))
    for copy in loads + copies:
        copy.start()
    blank = jnp.zeros((rows, LANES), patch_ref.dtype)
    patch_ref[:, :LANES] = blank
    patch_ref[:, size * chunk + LANES :] = blank
    for image_ref in image_refs:
        image_ref[:, chunk:] = blank
    for copy in loads:
        copy.wait()
    lane = lax.broadcasted_iota(jnp.int32, (rows, LANES), 1)
    for shift in range(size):
        start = starts[shift]
        patch_refs[shift][:, :chunk] = patch_ref[:, pl.ds(start + LANES, chunk)]
        before = patch_ref[:, pl.ds(start, LANES)].astype(jnp.float32)
        after = patch_ref[:, pl.ds(start + chunk + LANES, LANES)].astype(jnp.float32)
        rim = jnp.where(lane < LANES // 2, after, before)
        patch_refs[shift][:, chunk:ext] = rim.astype(patch_ref.dtype)
    for copy in copies:
        copy.wait()
    owner_ref[...] = jnp.full(owner_ref.shape, plan_now[step], jnp.int32)
    for way in range(2):
        for k in range(NB):
            order_ref[way, k] = jnp.full((8, LANES), orders_now[way, k], jnp.int32)


def choose_kernel(owner_ref, *refs, shifts, size):
    *recv_refs, out_ref = refs
    me = lax.axis_index("expo")
    for b in range(out_ref.shape[1] // LANES):
        columns = slice(b * LANES, (b + 1) * LANES)
        block = recv_refs[0][:, columns].astype(jnp.float32)
        for shift, ref in zip(shifts, recv_refs[1:]):
            block = jnp.where(
                owner_ref[...] == source(me, shift, size), ref[:, columns].astype(jnp.float32), block
            )
        out_ref[:, columns] = block.astype(out_ref.dtype)


def pick_kernel(owner_ref, *refs, shifts, size):
    *recv_refs, out_ref, block_ref = refs
    ext = out_ref.shape[1]
    choose_kernel(owner_ref, *recv_refs, block_ref, shifts=shifts, size=size)
    whole = jnp.concatenate([block_ref[:, ext - LANES :], block_ref[...]], axis=1)
    out_ref[...] = whole[:, LANES - HALF : LANES - HALF + ext]


def column_positions(first_col, block, width):
    col = lax.broadcasted_iota(jnp.int32, (8, LANES), 1) + (first_col + block * LANES)
    return 2.0 * (col.astype(jnp.float32) + 0.5) / width - 1.0


def band_kernel(order_ref, _, row_ref, col_ref, *, tiles):
    rows = row_ref.shape[0] // NB
    tile_at = lax.axis_index("tile")
    near = 1 - 2 * lax.rem(tile_at, 2)
    near_move = jnp.where(tile_at + near < tiles, near - 1, BEYOND)
    far_move = jnp.where((tile_at >= near) & (tile_at - near < tiles), -near - 2, BEYOND)
    row_from = lax.broadcasted_iota(jnp.int32, (8, LANES), 1)
    moved = jnp.where(row_from < rows, 0, jnp.where(row_from < 2 * rows, near_move, far_move))
    sub = lax.broadcasted_iota(jnp.int32, (8, LANES), 0)
    lane = lax.broadcasted_iota(jnp.int32, (8, LANES), 1)
    shift = (sub - jnp.where(lane < LANES // 2, lane, lane - LANES) - HALF).astype(jnp.float32)
    for k in range(NB):
        norm = tap_norm(SIGMAS[k], order_ref[0, k])
        for r in range(0, rows, 16):
            parts = []
            for half in (r, r + 8):
                offset = (row_from + moved * rows - sub - half).astype(jnp.float32)
                parts.append(tap_values(offset, SIGMAS[k], order_ref[0, k]) / norm)
            both = jnp.concatenate(parts, axis=0).astype(jnp.bfloat16)
            row_ref[k * rows + r : k * rows + r + 16] = both[:, : 3 * rows]
        norm = tap_norm(SIGMAS[k], order_ref[1, k])
        pattern = tap_values(shift, SIGMAS[k], order_ref[1, k]) / norm
        for r in range(0, 2 * LANES, 16):
            parts = []
            for half in (r, r + 8):
                moved_on = pltpu.roll(pattern, half % LANES, 1) if half % LANES else pattern
                inside = lane <= half + 7 if half < LANES else lane >= half - LANES + LANES // 2
                parts.append(jnp.where(inside, moved_on, 0.0))
            col_ref[k, r : r + 16] = jnp.concatenate(parts, axis=0).astype(jnp.bfloat16)


def image_blocks(ref, size, shift, chunk):
    first = chunk + LANES if joint(shift, size) else 0
    return lambda b: ref[:, first + b * LANES : first + (b + 1) * LANES].astype(jnp.float32)


def fit_kernel(weight_ref, hits_ref, row_band_ref, col_band_ref, own_ref, near_ref, far_ref, *refs, width):
    *image_refs, conv_ref, sums_ref, row_ref, parts_ref = refs
    image_refs = dict(zip(far_first(len(image_refs)), image_refs))
    tile_at = lax.axis_index("tile")
    expo_at = lax.axis_index("expo")
    rows, ext = own_ref.shape
    expos = len(image_refs)
    chunk = ext - LANES
    blocks = chunk // LANES

    patch = jnp.concatenate([own_ref[...], near_ref[...], far_ref[...]], axis=0)
    row_ref[...] = jnp.dot(
        row_band_ref[...], patch, preferred_element_type=jnp.float32
    ).astype(jnp.bfloat16)
    for k in range(NB):
        window = jnp.concatenate(
            [
                row_ref[k * rows : (k + 1) * rows, b * LANES : (b + 2) * LANES]
                for b in range(blocks)
            ],
            axis=0,
        )
        out = jnp.dot(window, col_band_ref[k], preferred_element_type=jnp.float32)
        conv_ref[k] = out.reshape(blocks, rows, LANES)

    first_col = expo_at * chunk
    xs = [column_positions(first_col, b, width) for b in range(blocks)]

    def fold(x):
        total = x[:8]
        for i in range(8, rows, 8):
            total = total + x[i : i + 8]
        return total

    def moments(at, left, right, count):
        total = [None] * count
        for b in range(blocks):
            term = fold(left(b) * right(b)) if right is not None else fold(left(b))
            for i in range(count):
                total[i] = term if total[i] is None else total[i] + term
                if i < count - 1:
                    term = term * xs[b]
        for i in range(count):
            parts_ref[at + i] = total[i]

    def conv(k):
        return lambda b: conv_ref[k, b]

    def sci(shift):
        return image_blocks(image_refs[shift], expos, shift, chunk)

    blank = jnp.zeros((8, LANES), jnp.float32)
    at = 0
    for j, k in PAIRS:
        moments(at, conv(j), conv(k), 3)
        at += 3
    for k in range(NB):
        moments(at, conv(k), None, 2)
        at += 2
    while at % 8:
        parts_ref[at] = blank
        at += 1
    begin = at
    for shift in range(expos):
        row = at + NU * source(expo_at, shift, expos)
        for k in range(NB):
            moments(row + 2 * k, conv(k), sci(shift), 2)
        moments(row + NU - 1, sci(shift), None, 1)
    at += NU * expos
    weight = jnp.broadcast_to(weight_ref[...] * hits_ref[...].astype(jnp.float32), (8, LANES))
    weight = jnp.where(tile_at == 0, weight, 0.0)
    spot = (
        (lax.broadcasted_iota(jnp.int32, (8, LANES), 0) == 0)
        & (lax.broadcasted_iota(jnp.int32, (8, LANES), 1) == 0)
    )
    for e in range(expos):
        parts_ref[at + e] = jnp.where(spot & (expo_at == e), weight, 0.0)
    at += expos
    while at % 8:
        parts_ref[at] = blank
        at += 1
    ones = jnp.ones((8, LANES), jnp.float32)
    rows_of = []
    for first, last in ((0, begin), (begin, at)):
        lanes = jnp.sum(parts_ref[first:last], axis=1)
        spare = LANES - (last - first)
        if spare:
            lanes = jnp.concatenate([lanes, jnp.zeros((spare, LANES), jnp.float32)], axis=0)
        rows_of.append(
            lax.dot_general(
                ones,
                lanes,
                (((1,), (1,)), ((), ())),
                precision=lax.Precision.HIGHEST,
                preferred_element_type=jnp.float32,
            )
        )
    both = jnp.where(lax.broadcasted_iota(jnp.int32, (8, LANES), 0) < 4, rows_of[0], rows_of[1])
    for i in range(sums_ref.shape[0]):
        sums_ref[i] = both


def table(expos):
    columns = np.zeros((NU + expos + 1, 16), np.int32)
    for at, (j, k) in enumerate(PAIRS):
        for a, b in ((j, k), (k, j)):
            columns[b, a] = 3 * at
            columns[NB + b, a] = columns[b, NB + a] = 3 * at + 1
            columns[NB + b, NB + a] = 3 * at + 2
    for k in range(NB):
        for x in range(2):
            columns[NU - 1, x * NB + k] = columns[x * NB + k, NU - 1] = 3 * len(PAIRS) + 2 * k + x
    for e in range(expos):
        columns[NU + e, :NU] = [NU * e + 2 * k + x for x in range(2) for k in range(NB)] + [NU * e + NU - 1]
        columns[NU + expos, e] = NU * expos + e
    return np.ascontiguousarray(np.broadcast_to(columns[:, :, None], columns.shape + (LANES,)))


def solve_kernel(table_ref, sums_ref, conv_ref, *refs, width, pixels):
    *image_refs, coadd_ref, coeffs_ref, tile_ref, sems = refs
    expo_at = lax.axis_index("expo")
    expos = len(image_refs)
    rows, chunk = coadd_ref.shape
    blocks = chunk // LANES
    images = [image_blocks(ref, expos, shift, chunk) for shift, ref in enumerate(image_refs)]
    sub = lax.broadcasted_iota(jnp.int32, (16, LANES), 0)
    lane = lax.broadcasted_iota(jnp.int32, (16, LANES), 1)
    sums = sums_ref[0]
    for i in range(1, sums_ref.shape[0]):
        sums = sums + sums_ref[i]
    first = jnp.broadcast_to(sums[0:1], (16, LANES))
    second = jnp.broadcast_to(sums[4:5], (16, LANES))

    columns = [
        jnp.take_along_axis(first if j < NU else second, table_ref[j], axis=1) for j in range(NU + expos)
    ]
    spread = jnp.take_along_axis(second, table_ref[NU + expos], axis=1)
    weight = [jnp.broadcast_to(spread[e : e + 1], (16, LANES)) for e in range(expos)]
    columns[NU - 1] = jnp.where(sub == NU - 1, float(pixels), columns[NU - 1])

    trace = columns[0][0:1]
    for j in range(1, NU):
        trace = trace + columns[j][j : j + 1]
    scale = 1.0 / trace
    for j in range(NU + expos):
        columns[j] = columns[j] * scale
        if j < NU:
            columns[j] = columns[j] + jnp.where(sub == j, RIDGE / NU, 0.0)
    for i in range(NU):
        inverse = 1.0 / columns[i][i : i + 1]
        for j in range(i + 1, NU + expos):
            factor = columns[j][i : i + 1] * inverse
            columns[j] = jnp.where(sub == i, factor, columns[j] - columns[i] * factor)

    solved = columns[NU:]
    own = solved[0]
    mixed = weight[0] * solved[0]
    for e in range(1, expos):
        own = jnp.where(expo_at == e, solved[e], own)
        mixed = mixed + weight[e] * solved[e]
    diagonal = (sub == lane) & (sub < NU)
    coeffs_ref[...] = jnp.sum(jnp.where(diagonal, own, 0.0), axis=0, keepdims=True)[:, :NU]
    scale = [jnp.broadcast_to(mixed[u : u + 1], (8, LANES)) for u in range(NU)]
    gains = []
    for shift in range(expos):
        gain = weight[0][:8]
        for e in range(1, expos):
            gain = jnp.where(source(expo_at, shift, expos) == e, weight[e][:8], gain)
        gains.append(gain)
    first_col = expo_at * chunk
    copies = []
    for r in range(0, rows, 8):
        for b in range(blocks):
            x = column_positions(first_col, b, width)
            total = -scale[NU - 1]
            for gain, image in zip(gains, images):
                total = total + gain * image(b)[r : r + 8]
            model = (scale[0] + scale[NB] * x) * conv_ref[0, b, r : r + 8]
            for k in range(1, NB):
                model = model + (scale[k] + scale[NB + k] * x) * conv_ref[k, b, r : r + 8]
            tile_ref[r : r + 8, b * LANES : (b + 1) * LANES] = total - model
        copies.append(
            pltpu.make_async_copy(tile_ref.at[pl.ds(r, 8)], coadd_ref.at[pl.ds(r, 8)], sems.at[r // 8])
        )
        copies[-1].start()
    for copy in copies:
        copy.wait()


def swaps(first, size):
    pairs = [(i, i + 1) for i in range(first, size - 1, 2)]
    if first and size % 2 == 0:
        pairs.append((0, size - 1))
    return [pair for a, b in pairs for pair in ((a, b), (b, a))]


def tiled_device(template, science, plan, orders, coadd_weight, intersection):
    expos = lax.axis_size("expo")
    tiles = lax.axis_size("tile")
    _, rows, width = template.shape
    steps = science.shape[1]
    chunk = width // expos
    ext = chunk + LANES
    blocks = chunk // LANES
    vmem = pl.BlockSpec(memory_space=pltpu.VMEM)
    small = pltpu.CompilerParams(vmem_limit_bytes=16 * 1024 * 1024)
    hbm = pl.BlockSpec(memory_space=pltpu.HBM)
    coadds = []
    fitted = []
    for step in range(steps):
        *blocks_out, owner, order = pl.pallas_call(
            functools.partial(send_kernel, step=step),
            out_shape=tuple(
                pltpu.VMEM((rows, ext + chunk if joint(shift, expos) else ext), template.dtype)
                for shift in range(expos)
            )
            + (pltpu.VMEM((rows, ext), science.dtype),) * (expos - expos // 2)
            + (
                jax.ShapeDtypeStruct((rows, LANES), jnp.int32),
                jax.ShapeDtypeStruct((2, NB, 8, LANES), jnp.int32),
            ),
            in_specs=[hbm] * 4,
            out_specs=(vmem,) * (2 * expos - expos // 2 + 2),
            scratch_shapes=[
                pltpu.VMEM((rows, width + 2 * LANES), template.dtype),
                pltpu.SMEM(plan.shape, jnp.int32),
                pltpu.SMEM((2, NB), jnp.int32),
                pltpu.SemaphoreType.DMA((expos + 4,)),
            ],
            compiler_params=small,
        )(
            pltpu.with_memory_space_constraint(template[0], pltpu.HBM),
            pltpu.with_memory_space_constraint(science[0, step], pltpu.HBM),
            pltpu.with_memory_space_constraint(plan, pltpu.HBM),
            pltpu.with_memory_space_constraint(orders.T, pltpu.HBM),
        )
        patches, images = blocks_out[:expos], blocks_out[expos:]
        for group, first in ((patches, 0), (images, expos // 2)):
            for shift in range(max(first, 1), expos):
                pairs = [(e, int(target(e, shift, expos))) for e in range(expos)]
                group[shift - first] = lax.ppermute(group[shift - first], "expo", pairs)
        images = patches[: expos // 2] + images
        across = [shift for shift in far_first(expos)[:-1] if not joint(shift, expos)]
        beside = [shift for shift in far_first(expos)[:-1] if joint(shift, expos)]
        block = pl.pallas_call(
            functools.partial(choose_kernel, shifts=across, size=expos),
            out_shape=jax.ShapeDtypeStruct((rows, ext), template.dtype),
            in_specs=[vmem] * (2 + len(across)),
            out_specs=vmem,
            compiler_params=small,
            cost_estimate=pl.CostEstimate(flops=STAGE_COST, bytes_accessed=500_000, transcendentals=0),
        )(owner, patches[0], *(patches[shift] for shift in across))
        own = pl.pallas_call(
            functools.partial(pick_kernel, shifts=beside, size=expos),
            out_shape=jax.ShapeDtypeStruct((rows, ext), template.dtype),
            in_specs=[vmem] * (2 + len(beside)),
            out_specs=vmem,
            scratch_shapes=[pltpu.VMEM((rows, ext), template.dtype)],
            compiler_params=small,
        )(owner, block, *(patches[shift] for shift in beside))
        row_band, col_band = pl.pallas_call(
            functools.partial(band_kernel, tiles=tiles),
            out_shape=(
                jax.ShapeDtypeStruct((NB * rows, 3 * rows), jnp.bfloat16),
                jax.ShapeDtypeStruct((NB, 2 * LANES, LANES), jnp.bfloat16),
            ),
            in_specs=[vmem, pl.BlockSpec(memory_space=pl.ANY)],
            out_specs=(vmem, vmem),
            compiler_params=small,
            cost_estimate=pl.CostEstimate(flops=4_000_000, bytes_accessed=500_000, transcendentals=200_000),
        )(order, own)
        far = lax.ppermute(own, "tile", swaps(1, tiles))
        near = lax.ppermute(own, "tile", swaps(0, tiles))
        conv, sums = pl.pallas_call(
            functools.partial(fit_kernel, width=width),
            out_shape=(
                jax.ShapeDtypeStruct((NB, blocks, rows, LANES), jnp.float32),
                jax.ShapeDtypeStruct((tiles * expos, 8, LANES), jnp.float32),
            ),
            in_specs=[vmem] * (7 + expos),
            out_specs=(vmem, vmem),
            scratch_shapes=[
                pltpu.VMEM((NB * rows, ext), jnp.bfloat16),
                pltpu.VMEM((80 + 14 * expos + 8, 8, LANES), jnp.float32),
            ],
            compiler_params=small,
        )(
            coadd_weight[:, step : step + 1],
            intersection[:, step : step + 1],
            row_band,
            col_band,
            own,
            near,
            far,
            *(images[shift] for shift in far_first(expos)),
        )
        sums = lax.all_to_all(sums, ("tile", "expo"), split_axis=0, concat_axis=0, tiled=True)
        coadd, coeffs = pl.pallas_call(
            functools.partial(solve_kernel, width=width, pixels=tiles * rows * width),
            out_shape=(
                jax.ShapeDtypeStruct((rows, chunk), jnp.float32),
                jax.ShapeDtypeStruct((1, NU), jnp.float32),
            ),
            in_specs=[vmem] * (3 + expos),
            out_specs=(pl.BlockSpec(memory_space=pl.ANY), vmem),
            scratch_shapes=[
                pltpu.VMEM((rows, chunk), jnp.float32),
                pltpu.SemaphoreType.DMA((rows // 8,)),
            ],
            compiler_params=small,
        )(jnp.asarray(table(expos)), sums, conv, *images)
        coadds.append(coadd[None])
        fitted.append(coeffs)
    return (jnp.concatenate(coadds), jnp.stack(fitted, axis=1))


def broadcast(block, axis, holder):
    block = jnp.where(lax.axis_index(axis) == holder, block, jnp.zeros_like(block))
    return lax.psum(block, axis)


def extended(x, sides, width):
    for axis, dim in sides:
        size, length = (lax.axis_size(axis), x.shape[dim])
        up = [(i, (i + 1) % size) for i in range(size - 1)]
        down = [(j, i) for i, j in up]
        last = lax.slice_in_dim(x, length - width, length, axis=dim)
        first = lax.slice_in_dim(x, 0, width, axis=dim)
        before = lax.ppermute(last, axis, up)
        after = lax.ppermute(first, axis, down)
        x = jnp.concatenate([before, x, after], axis=dim)
    return x


def make_filters(orders):
    taps_pos = jnp.arange(2 * HALF + 1).astype(jnp.float32) - HALF
    row_list = []
    col_list = []
    for basis in range(NB):
        sigma = SIGMAS[basis]
        envelope = jnp.exp(-taps_pos * taps_pos / (2.0 * sigma * sigma))
        row_filter = envelope * power_of(taps_pos, orders[basis, 0])
        col_filter = envelope * power_of(taps_pos, orders[basis, 1])
        row_list.append(row_filter / jnp.sqrt(jnp.sum(row_filter * row_filter)))
        col_list.append(col_filter / jnp.sqrt(jnp.sum(col_filter * col_filter)))
    return (jnp.stack(row_list).astype(jnp.bfloat16), jnp.stack(col_list).astype(jnp.bfloat16))


def band_matrix(filters, out_len, in_len):
    offset = jnp.arange(in_len)[None, :] - jnp.arange(out_len)[:, None]
    taps_idx = jnp.arange(2 * HALF + 1)
    picks = (offset[:, :, None] == taps_idx[None, None, :]).astype(jnp.float32)
    band = jnp.einsum("ijt,kt->kij", picks, filters.astype(jnp.float32))
    return band.astype(jnp.bfloat16)


def any_device(template, science, plan, orders, coadd_weight, intersection):
    row_filters, col_filters = make_filters(orders)
    rows = template.shape[1]
    width = template.shape[2]
    blocks_count = width // 128
    steps_count = science.shape[1]
    row_band = band_matrix(row_filters, rows, rows + 2 * HALF)
    col_band = jnp.transpose(band_matrix(col_filters, 128, 128 + 2 * HALF), (0, 2, 1))
    column_pos = 2.0 * (jnp.arange(width).astype(jnp.float32) + 0.5) / width - 1.0
    pieces = []
    fitted = []
    for step in range(steps_count):
        received = broadcast(template[0], "expo", plan[step])
        padded = extended(received, (("tile", 0),), HALF)
        rowconv = jnp.einsum(
            "kij,jw->kiw", row_band, padded, preferred_element_type=jnp.float32
        ).astype(jnp.bfloat16)
        blocks = rowconv.reshape(NB, rows, blocks_count, 128)
        empty_rim = jnp.zeros((NB, rows, 1, HALF), jnp.bfloat16)
        previous = jnp.concatenate([empty_rim, blocks[:, :, :-1, 128 - HALF :]], axis=2)
        following = jnp.concatenate([blocks[:, :, 1:, :HALF], empty_rim], axis=2)
        window = jnp.concatenate([previous, blocks, following], axis=3)
        conv = jnp.einsum("krbj,kjc->krbc", window, col_band, preferred_element_type=jnp.float32)
        conv = conv.reshape(NB, rows, width)
        fields = jnp.concatenate(
            [conv, conv * column_pos, jnp.ones((1, rows, width), jnp.float32)], axis=0
        )
        fields = fields.reshape(NU, rows * width)
        exposure_image = science[0, step].astype(jnp.float32).reshape(rows * width)
        normal_local = jnp.dot(fields, fields.T, precision=lax.Precision.HIGHEST)
        project_local = jnp.dot(fields, exposure_image, precision=lax.Precision.HIGHEST)
        normal_matrix, projections = lax.psum((normal_local, project_local), "tile")
        normal_matrix = normal_matrix + RIDGE * (jnp.trace(normal_matrix) / NU) * jnp.eye(
            NU, dtype=jnp.float32
        )
        factor = jnp.linalg.cholesky(normal_matrix)
        coeffs = jax.scipy.linalg.cho_solve((factor, True), projections)
        model = jnp.dot(coeffs, fields, precision=lax.Precision.HIGHEST)
        difference = exposure_image - model
        weight_now = coadd_weight[0, step] * intersection[0, step].astype(jnp.float32)
        pieces.append((weight_now * difference).reshape(rows, width))
        fitted.append(coeffs)
    weighted = jnp.stack(pieces)
    received_parts = lax.all_to_all(weighted[None], "expo", split_axis=3, concat_axis=0, tiled=True)
    coadd = jnp.sum(received_parts, axis=0)
    return (coadd, jnp.stack(fitted)[None])


def per_device(template, science, plan, orders, coadd_weight, intersection):
    expos = lax.axis_size("expo")
    rows, width = template.shape[1:]
    whole_lanes = width % (expos * LANES) == 0 and rows % 16 == 0 and 3 * rows <= LANES
    few = (NU + 1) * expos <= LANES and NU + expos <= LANES
    body = tiled_device if whole_lanes and few else any_device
    return body(template, science, plan, orders, coadd_weight, intersection)


def solution(mesh):
    return jax.shard_map(
        per_device,
        mesh=mesh,
        in_specs=(
            P(("groups", "expo"), "tile", None),
            P(("groups", "expo"), None, "tile", None),
            P("groups"),
            P(),
            P(("groups", "expo"), None),
            P(("groups", "expo"), None),
        ),
        out_specs=(P("groups", "tile", "expo"), P(("groups", "expo"), None, None)),
        check_vma=False,
    )
```

```python
import functools

import jax
import jax.numpy as jnp
import numpy as np
from jax import lax
from jax.experimental import pallas as pl
from jax.experimental.pallas import tpu as pltpu
from jax.sharding import PartitionSpec as P

HALF = 15
NB = 6
NU = 13
LANES = 128
BEYOND = 1000
STAGE_COST = 700_000_000
PAIRS = [(j, k) for j in range(NB) for k in range(j, NB)]

SIGMAS = (0.8, 1.4, 2.2, 3.0, 4.0, 5.5)
RIDGE = 0.05


def power_of(pos, order):
    return jnp.where(order == 0, 1.0, jnp.where(order == 1, pos, pos * pos))


def tap_values(pos, sigma, order):
    value = jnp.exp(-pos * pos / (2.0 * sigma * sigma)) * power_of(pos, order)
    return jnp.where(jnp.abs(pos) <= HALF, value, 0.0)


def tap_norm(sigma, order):
    pos = lax.broadcasted_iota(jnp.int32, (8, LANES), 1).astype(jnp.float32) - HALF
    value = tap_values(pos, sigma, order)
    return jnp.sqrt(jnp.sum(value * value, axis=1, keepdims=True))


def target(me, shift, size):
    return me ^ shift if size & (size - 1) == 0 else (me + shift) % size


def source(me, shift, size):
    return me ^ shift if size & (size - 1) == 0 else (me - shift + size) % size


def far_first(size):
    return [*range(size - 1, 0, -1), 0]


def middle_first(size):
    return [*range(size // 2, size), *range(1, size // 2), 0] if size > 1 else [0]


def joint(shift, size):
    return shift < size // 2


def send_kernel(template_ref, science_ref, plan_ref, orders_ref, *refs, step):
    *out_refs, owner_ref, order_ref, patch_ref, plan_now, orders_now, sems = refs
    size = sems.shape[0] - 4
    rows, width = science_ref.shape
    chunk = width // size
    ext = chunk + LANES
    patch_refs, image_refs = out_refs[:size], out_refs[size:]
    half = size * chunk // 2
    me = lax.axis_index("expo")
    starts = [pl.multiple_of(target(me, shift, size) * chunk, chunk) for shift in range(size)]
    loads = [
        pltpu.make_async_copy(
            template_ref.at[:, pl.ds(i * half, half)], patch_ref.at[:, pl.ds((i * half + LANES), half)], sems.at[i]
        )
        for i in range(2)
    ]
    copies = [
        pltpu.make_async_copy(
            science_ref.at[:, pl.ds(starts[shift], chunk)],
            patch_refs[shift].at[:, pl.ds(ext, chunk)]
            if joint(shift, size)
            else image_refs[shift - size // 2].at[:, pl.ds(0, chunk)],
            sems.at[3 + shift],
        )
        for shift in range(size)
    ]
    copies.append(pltpu.make_async_copy(plan_ref, plan_now, sems.at[2]))
    copies.append(pltpu.make_async_copy(orders_ref, orders_now, sems.at[3 + size]))
    for copy in loads + copies:
        copy.start()
    blank = jnp.zeros((rows, LANES), patch_ref.dtype)
    patch_ref[:, :LANES] = blank
    patch_ref[:, size * chunk + LANES :] = blank
    for image_ref in image_refs:
        image_ref[:, chunk:] = blank
    for copy in loads:
        copy.wait()
    lane = lax.broadcasted_iota(jnp.int32, (rows, LANES), 1)
    for shift in range(size):
        start = starts[shift]
        patch_refs[shift][:, :chunk] = patch_ref[:, pl.ds(start + LANES, chunk)]
        before = patch_ref[:, pl.ds(start, LANES)].astype(jnp.float32)
        after = patch_ref[:, pl.ds(start + chunk + LANES, LANES)].astype(jnp.float32)
        rim = jnp.where(lane < LANES // 2, after, before)
        patch_refs[shift][:, chunk:ext] = rim.astype(patch_ref.dtype)
    for copy in copies:
        copy.wait()
    owner_ref[...] = jnp.full(owner_ref.shape, plan_now[step], jnp.int32)
    for way in range(2):
        for k in range(NB):
            order_ref[way, k] = jnp.full((8, LANES), orders_now[way, k], jnp.int32)


def choose_kernel(owner_ref, *refs, shifts, size):
    *recv_refs, out_ref = refs
    me = lax.axis_index("expo")
    for b in range(out_ref.shape[1] // LANES):
        columns = slice(b * LANES, (b + 1) * LANES)
        block = recv_refs[0][:, columns].astype(jnp.float32)
        for shift, ref in zip(shifts, recv_refs[1:]):
            block = jnp.where(
                owner_ref[...] == source(me, shift, size), ref[:, columns].astype(jnp.float32), block
            )
        out_ref[:, columns] = block.astype(out_ref.dtype)


def pick_kernel(owner_ref, *refs, shifts, size):
    *recv_refs, out_ref, block_ref = refs
    ext = out_ref.shape[1]
    choose_kernel(owner_ref, *recv_refs, block_ref, shifts=shifts, size=size)
    whole = jnp.concatenate([block_ref[:, ext - LANES :], block_ref[...]], axis=1)
    out_ref[...] = whole[:, LANES - HALF : LANES - HALF + ext]


def column_positions(first_col, block, width):
    col = lax.broadcasted_iota(jnp.int32, (8, LANES), 1) + (first_col + block * LANES)
    return 2.0 * (col.astype(jnp.float32) + 0.5) / width - 1.0


def band_kernel(order_ref, _, row_ref, col_ref, *, tiles):
    rows = row_ref.shape[0] // NB
    tile_at = lax.axis_index("tile")
    near = 1 - 2 * lax.rem(tile_at, 2)
    near_move = jnp.where(tile_at + near < tiles, near - 1, BEYOND)
    far_move = jnp.where((tile_at >= near) & (tile_at - near < tiles), -near - 2, BEYOND)
    row_from = lax.broadcasted_iota(jnp.int32, (8, LANES), 1)
    moved = jnp.where(row_from < rows, 0, jnp.where(row_from < 2 * rows, near_move, far_move))
    sub = lax.broadcasted_iota(jnp.int32, (8, LANES), 0)
    lane = lax.broadcasted_iota(jnp.int32, (8, LANES), 1)
    shift = (sub - jnp.where(lane < LANES // 2, lane, lane - LANES) - HALF).astype(jnp.float32)
    for k in range(NB):
        norm = tap_norm(SIGMAS[k], order_ref[0, k])
        for r in range(0, rows, 16):
            parts = []
            for half in (r, r + 8):
                offset = (row_from + moved * rows - sub - half).astype(jnp.float32)
                parts.append(tap_values(offset, SIGMAS[k], order_ref[0, k]) / norm)
            both = jnp.concatenate(parts, axis=0).astype(jnp.bfloat16)
            row_ref[k * rows + r : k * rows + r + 16] = both[:, : 3 * rows]
        norm = tap_norm(SIGMAS[k], order_ref[1, k])
        pattern = tap_values(shift, SIGMAS[k], order_ref[1, k]) / norm
        for r in range(0, 2 * LANES, 16):
            parts = []
            for half in (r, r + 8):
                moved_on = pltpu.roll(pattern, half % LANES, 1) if half % LANES else pattern
                inside = lane <= half + 7 if half < LANES else lane >= half - LANES + LANES // 2
                parts.append(jnp.where(inside, moved_on, 0.0))
            col_ref[k, r : r + 16] = jnp.concatenate(parts, axis=0).astype(jnp.bfloat16)


def image_blocks(ref, size, shift, chunk):
    first = chunk + LANES if joint(shift, size) else 0
    return lambda b: ref[:, first + b * LANES : first + (b + 1) * LANES].astype(jnp.float32)


def fit_kernel(weight_ref, hits_ref, row_band_ref, col_band_ref, own_ref, near_ref, far_ref, *refs, width):
    *image_refs, conv_ref, sums_ref, row_ref, parts_ref = refs
    image_refs = dict(zip(middle_first(len(image_refs)), image_refs))
    tile_at = lax.axis_index("tile")
    expo_at = lax.axis_index("expo")
    rows, ext = own_ref.shape
    expos = len(image_refs)
    chunk = ext - LANES
    blocks = chunk // LANES

    patch = jnp.concatenate([own_ref[...], near_ref[...], far_ref[...]], axis=0)
    row_ref[...] = jnp.dot(
        row_band_ref[...], patch, preferred_element_type=jnp.float32
    ).astype(jnp.bfloat16)
    for k in range(NB):
        window = jnp.concatenate(
            [
                row_ref[k * rows : (k + 1) * rows, b * LANES : (b + 2) * LANES]
                for b in range(blocks)
            ],
            axis=0,
        )
        out = jnp.dot(window, col_band_ref[k], preferred_element_type=jnp.float32)
        conv_ref[k] = out.reshape(blocks, rows, LANES)

    first_col = expo_at * chunk
    xs = [column_positions(first_col, b, width) for b in range(blocks)]

    def fold(x):
        total = x[:8]
        for i in range(8, rows, 8):
            total = total + x[i : i + 8]
        return total

    def moments(at, left, right, count):
        total = [None] * count
        for b in range(blocks):
            term = fold(left(b) * right(b)) if right is not None else fold(left(b))
            for i in range(count):
                total[i] = term if total[i] is None else total[i] + term
                if i < count - 1:
                    term = term * xs[b]
        for i in range(count):
            parts_ref[at + i] = total[i]

    def conv(k):
        return lambda b: conv_ref[k, b]

    def sci(shift):
        return image_blocks(image_refs[shift], expos, shift, chunk)

    blank = jnp.zeros((8, LANES), jnp.float32)
    at = 0
    for j, k in PAIRS:
        moments(at, conv(j), conv(k), 3)
        at += 3
    for k in range(NB):
        moments(at, conv(k), None, 2)
        at += 2
    while at % 8:
        parts_ref[at] = blank
        at += 1
    begin = at
    for shift in range(expos):
        row = at + NU * source(expo_at, shift, expos)
        for k in range(NB):
            moments(row + 2 * k, conv(k), sci(shift), 2)
        moments(row + NU - 1, sci(shift), None, 1)
    at += NU * expos
    weight = jnp.broadcast_to(weight_ref[...] * hits_ref[...].astype(jnp.float32), (8, LANES))
    weight = jnp.where(tile_at == 0, weight, 0.0)
    spot = (
        (lax.broadcasted_iota(jnp.int32, (8, LANES), 0) == 0)
        & (lax.broadcasted_iota(jnp.int32, (8, LANES), 1) == 0)
    )
    for e in range(expos):
        parts_ref[at + e] = jnp.where(spot & (expo_at == e), weight, 0.0)
    at += expos
    while at % 8:
        parts_ref[at] = blank
        at += 1
    ones = jnp.ones((8, LANES), jnp.float32)
    rows_of = []
    for first, last in ((0, begin), (begin, at)):
        lanes = jnp.sum(parts_ref[first:last], axis=1)
        spare = LANES - (last - first)
        if spare:
            lanes = jnp.concatenate([lanes, jnp.zeros((spare, LANES), jnp.float32)], axis=0)
        rows_of.append(
            lax.dot_general(
                ones,
                lanes,
                (((1,), (1,)), ((), ())),
                precision=lax.Precision.HIGHEST,
                preferred_element_type=jnp.float32,
            )
        )
    both = jnp.where(lax.broadcasted_iota(jnp.int32, (8, LANES), 0) < 4, rows_of[0], rows_of[1])
    for i in range(sums_ref.shape[0]):
        sums_ref[i] = both


def table(expos):
    columns = np.zeros((NU + expos + 1, 16), np.int32)
    for at, (j, k) in enumerate(PAIRS):
        for a, b in ((j, k), (k, j)):
            columns[b, a] = 3 * at
            columns[NB + b, a] = columns[b, NB + a] = 3 * at + 1
            columns[NB + b, NB + a] = 3 * at + 2
    for k in range(NB):
        for x in range(2):
            columns[NU - 1, x * NB + k] = columns[x * NB + k, NU - 1] = 3 * len(PAIRS) + 2 * k + x
    for e in range(expos):
        columns[NU + e, :NU] = [NU * e + 2 * k + x for x in range(2) for k in range(NB)] + [NU * e + NU - 1]
        columns[NU + expos, e] = NU * expos + e
    return np.ascontiguousarray(np.broadcast_to(columns[:, :, None], columns.shape + (LANES,)))


def solve_kernel(table_ref, sums_ref, conv_ref, *refs, width, pixels):
    *image_refs, coadd_ref, coeffs_ref, tile_ref, sems = refs
    expo_at = lax.axis_index("expo")
    expos = len(image_refs)
    rows, chunk = coadd_ref.shape
    blocks = chunk // LANES
    images = [image_blocks(ref, expos, shift, chunk) for shift, ref in enumerate(image_refs)]
    sub = lax.broadcasted_iota(jnp.int32, (16, LANES), 0)
    lane = lax.broadcasted_iota(jnp.int32, (16, LANES), 1)
    sums = sums_ref[0]
    for i in range(1, sums_ref.shape[0]):
        sums = sums + sums_ref[i]
    first = jnp.broadcast_to(sums[0:1], (16, LANES))
    second = jnp.broadcast_to(sums[4:5], (16, LANES))

    columns = [
        jnp.take_along_axis(first if j < NU else second, table_ref[j], axis=1) for j in range(NU + expos)
    ]
    spread = jnp.take_along_axis(second, table_ref[NU + expos], axis=1)
    weight = [jnp.broadcast_to(spread[e : e + 1], (16, LANES)) for e in range(expos)]
    columns[NU - 1] = jnp.where(sub == NU - 1, float(pixels), columns[NU - 1])

    trace = columns[0][0:1]
    for j in range(1, NU):
        trace = trace + columns[j][j : j + 1]
    scale = 1.0 / trace
    for j in range(NU + expos):
        columns[j] = columns[j] * scale
        if j < NU:
            columns[j] = columns[j] + jnp.where(sub == j, RIDGE / NU, 0.0)
    for i in range(NU):
        inverse = 1.0 / columns[i][i : i + 1]
        for j in range(i + 1, NU + expos):
            factor = columns[j][i : i + 1] * inverse
            columns[j] = jnp.where(sub == i, factor, columns[j] - columns[i] * factor)

    solved = columns[NU:]
    own = solved[0]
    mixed = weight[0] * solved[0]
    for e in range(1, expos):
        own = jnp.where(expo_at == e, solved[e], own)
        mixed = mixed + weight[e] * solved[e]
    diagonal = (sub == lane) & (sub < NU)
    coeffs_ref[...] = jnp.sum(jnp.where(diagonal, own, 0.0), axis=0, keepdims=True)[:, :NU]
    scale = [jnp.broadcast_to(mixed[u : u + 1], (8, LANES)) for u in range(NU)]
    gains = []
    for shift in range(expos):
        gain = weight[0][:8]
        for e in range(1, expos):
            gain = jnp.where(source(expo_at, shift, expos) == e, weight[e][:8], gain)
        gains.append(gain)
    first_col = expo_at * chunk
    copies = []
    for r in range(0, rows, 8):
        for b in range(blocks):
            x = column_positions(first_col, b, width)
            total = -scale[NU - 1]
            for gain, image in zip(gains, images):
                total = total + gain * image(b)[r : r + 8]
            model = (scale[0] + scale[NB] * x) * conv_ref[0, b, r : r + 8]
            for k in range(1, NB):
                model = model + (scale[k] + scale[NB + k] * x) * conv_ref[k, b, r : r + 8]
            tile_ref[r : r + 8, b * LANES : (b + 1) * LANES] = total - model
        copies.append(
            pltpu.make_async_copy(tile_ref.at[pl.ds(r, 8)], coadd_ref.at[pl.ds(r, 8)], sems.at[r // 8])
        )
        copies[-1].start()
    for copy in copies:
        copy.wait()


def swaps(first, size):
    pairs = [(i, i + 1) for i in range(first, size - 1, 2)]
    if first and size % 2 == 0:
        pairs.append((0, size - 1))
    return [pair for a, b in pairs for pair in ((a, b), (b, a))]


def tiled_device(template, science, plan, orders, coadd_weight, intersection):
    expos = lax.axis_size("expo")
    tiles = lax.axis_size("tile")
    _, rows, width = template.shape
    steps = science.shape[1]
    chunk = width // expos
    ext = chunk + LANES
    blocks = chunk // LANES
    vmem = pl.BlockSpec(memory_space=pltpu.VMEM)
    small = pltpu.CompilerParams(vmem_limit_bytes=16 * 1024 * 1024)
    hbm = pl.BlockSpec(memory_space=pltpu.HBM)
    coadds = []
    fitted = []
    for step in range(steps):
        *blocks_out, owner, order = pl.pallas_call(
            functools.partial(send_kernel, step=step),
            out_shape=tuple(
                pltpu.VMEM((rows, ext + chunk if joint(shift, expos) else ext), template.dtype)
                for shift in range(expos)
            )
            + (pltpu.VMEM((rows, ext), science.dtype),) * (expos - expos // 2)
            + (
                jax.ShapeDtypeStruct((rows, LANES), jnp.int32),
                jax.ShapeDtypeStruct((2, NB, 8, LANES), jnp.int32),
            ),
            in_specs=[hbm] * 4,
            out_specs=(vmem,) * (2 * expos - expos // 2 + 2),
            scratch_shapes=[
                pltpu.VMEM((rows, width + 2 * LANES), template.dtype),
                pltpu.SMEM(plan.shape, jnp.int32),
                pltpu.SMEM((2, NB), jnp.int32),
                pltpu.SemaphoreType.DMA((expos + 4,)),
            ],
            compiler_params=small,
        )(
            pltpu.with_memory_space_constraint(template[0], pltpu.HBM),
            pltpu.with_memory_space_constraint(science[0, step], pltpu.HBM),
            pltpu.with_memory_space_constraint(plan, pltpu.HBM),
            pltpu.with_memory_space_constraint(orders.T, pltpu.HBM),
        )
        patches, images = blocks_out[:expos], blocks_out[expos:]
        for group, first in ((patches, 0), (images, expos // 2)):
            for shift in range(max(first, 1), expos):
                pairs = [(e, int(target(e, shift, expos))) for e in range(expos)]
                group[shift - first] = lax.ppermute(group[shift - first], "expo", pairs)
        images = patches[: expos // 2] + images
        across = [shift for shift in far_first(expos)[:-1] if not joint(shift, expos)]
        beside = [shift for shift in far_first(expos)[:-1] if joint(shift, expos)]
        block = pl.pallas_call(
            functools.partial(choose_kernel, shifts=across, size=expos),
            out_shape=jax.ShapeDtypeStruct((rows, ext), template.dtype),
            in_specs=[vmem] * (2 + len(across)),
            out_specs=vmem,
            compiler_params=small,
            cost_estimate=pl.CostEstimate(flops=STAGE_COST, bytes_accessed=500_000, transcendentals=0),
        )(owner, patches[0], *(patches[shift] for shift in across))
        own = pl.pallas_call(
            functools.partial(pick_kernel, shifts=beside, size=expos),
            out_shape=jax.ShapeDtypeStruct((rows, ext), template.dtype),
            in_specs=[vmem] * (2 + len(beside)),
            out_specs=vmem,
            scratch_shapes=[pltpu.VMEM((rows, ext), template.dtype)],
            compiler_params=small,
        )(owner, block, *(patches[shift] for shift in beside))
        row_band, col_band = pl.pallas_call(
            functools.partial(band_kernel, tiles=tiles),
            out_shape=(
                jax.ShapeDtypeStruct((NB * rows, 3 * rows), jnp.bfloat16),
                jax.ShapeDtypeStruct((NB, 2 * LANES, LANES), jnp.bfloat16),
            ),
            in_specs=[vmem, pl.BlockSpec(memory_space=pl.ANY)],
            out_specs=(vmem, vmem),
            compiler_params=small,
            cost_estimate=pl.CostEstimate(flops=4_000_000, bytes_accessed=500_000, transcendentals=200_000),
        )(order, own)
        far = lax.ppermute(own, "tile", swaps(1, tiles))
        near = lax.ppermute(own, "tile", swaps(0, tiles))
        conv, sums = pl.pallas_call(
            functools.partial(fit_kernel, width=width),
            out_shape=(
                jax.ShapeDtypeStruct((NB, blocks, rows, LANES), jnp.float32),
                jax.ShapeDtypeStruct((tiles * expos, 8, LANES), jnp.float32),
            ),
            in_specs=[vmem] * (7 + expos),
            out_specs=(vmem, vmem),
            scratch_shapes=[
                pltpu.VMEM((NB * rows, ext), jnp.bfloat16),
                pltpu.VMEM((80 + 14 * expos + 8, 8, LANES), jnp.float32),
            ],
            compiler_params=small,
        )(
            coadd_weight[:, step : step + 1],
            intersection[:, step : step + 1],
            row_band,
            col_band,
            own,
            near,
            far,
            *(images[shift] for shift in middle_first(expos)),
        )
        sums = lax.all_to_all(sums, ("tile", "expo"), split_axis=0, concat_axis=0, tiled=True)
        coadd, coeffs = pl.pallas_call(
            functools.partial(solve_kernel, width=width, pixels=tiles * rows * width),
            out_shape=(
                jax.ShapeDtypeStruct((rows, chunk), jnp.float32),
                jax.ShapeDtypeStruct((1, NU), jnp.float32),
            ),
            in_specs=[vmem] * (3 + expos),
            out_specs=(pl.BlockSpec(memory_space=pl.ANY), vmem),
            scratch_shapes=[
                pltpu.VMEM((rows, chunk), jnp.float32),
                pltpu.SemaphoreType.DMA((rows // 8,)),
            ],
            compiler_params=small,
        )(jnp.asarray(table(expos)), sums, conv, *images)
        coadds.append(coadd[None])
        fitted.append(coeffs)
    return (jnp.concatenate(coadds), jnp.stack(fitted, axis=1))


def broadcast(block, axis, holder):
    block = jnp.where(lax.axis_index(axis) == holder, block, jnp.zeros_like(block))
    return lax.psum(block, axis)


def extended(x, sides, width):
    for axis, dim in sides:
        size, length = (lax.axis_size(axis), x.shape[dim])
        up = [(i, (i + 1) % size) for i in range(size - 1)]
        down = [(j, i) for i, j in up]
        last = lax.slice_in_dim(x, length - width, length, axis=dim)
        first = lax.slice_in_dim(x, 0, width, axis=dim)
        before = lax.ppermute(last, axis, up)
        after = lax.ppermute(first, axis, down)
        x = jnp.concatenate([before, x, after], axis=dim)
    return x


def make_filters(orders):
    taps_pos = jnp.arange(2 * HALF + 1).astype(jnp.float32) - HALF
    row_list = []
    col_list = []
    for basis in range(NB):
        sigma = SIGMAS[basis]
        envelope = jnp.exp(-taps_pos * taps_pos / (2.0 * sigma * sigma))
        row_filter = envelope * power_of(taps_pos, orders[basis, 0])
        col_filter = envelope * power_of(taps_pos, orders[basis, 1])
        row_list.append(row_filter / jnp.sqrt(jnp.sum(row_filter * row_filter)))
        col_list.append(col_filter / jnp.sqrt(jnp.sum(col_filter * col_filter)))
    return (jnp.stack(row_list).astype(jnp.bfloat16), jnp.stack(col_list).astype(jnp.bfloat16))


def band_matrix(filters, out_len, in_len):
    offset = jnp.arange(in_len)[None, :] - jnp.arange(out_len)[:, None]
    taps_idx = jnp.arange(2 * HALF + 1)
    picks = (offset[:, :, None] == taps_idx[None, None, :]).astype(jnp.float32)
    band = jnp.einsum("ijt,kt->kij", picks, filters.astype(jnp.float32))
    return band.astype(jnp.bfloat16)


def any_device(template, science, plan, orders, coadd_weight, intersection):
    row_filters, col_filters = make_filters(orders)
    rows = template.shape[1]
    width = template.shape[2]
    blocks_count = width // 128
    steps_count = science.shape[1]
    row_band = band_matrix(row_filters, rows, rows + 2 * HALF)
    col_band = jnp.transpose(band_matrix(col_filters, 128, 128 + 2 * HALF), (0, 2, 1))
    column_pos = 2.0 * (jnp.arange(width).astype(jnp.float32) + 0.5) / width - 1.0
    pieces = []
    fitted = []
    for step in range(steps_count):
        received = broadcast(template[0], "expo", plan[step])
        padded = extended(received, (("tile", 0),), HALF)
        rowconv = jnp.einsum(
            "kij,jw->kiw", row_band, padded, preferred_element_type=jnp.float32
        ).astype(jnp.bfloat16)
        blocks = rowconv.reshape(NB, rows, blocks_count, 128)
        empty_rim = jnp.zeros((NB, rows, 1, HALF), jnp.bfloat16)
        previous = jnp.concatenate([empty_rim, blocks[:, :, :-1, 128 - HALF :]], axis=2)
        following = jnp.concatenate([blocks[:, :, 1:, :HALF], empty_rim], axis=2)
        window = jnp.concatenate([previous, blocks, following], axis=3)
        conv = jnp.einsum("krbj,kjc->krbc", window, col_band, preferred_element_type=jnp.float32)
        conv = conv.reshape(NB, rows, width)
        fields = jnp.concatenate(
            [conv, conv * column_pos, jnp.ones((1, rows, width), jnp.float32)], axis=0
        )
        fields = fields.reshape(NU, rows * width)
        exposure_image = science[0, step].astype(jnp.float32).reshape(rows * width)
        normal_local = jnp.dot(fields, fields.T, precision=lax.Precision.HIGHEST)
        project_local = jnp.dot(fields, exposure_image, precision=lax.Precision.HIGHEST)
        normal_matrix, projections = lax.psum((normal_local, project_local), "tile")
        normal_matrix = normal_matrix + RIDGE * (jnp.trace(normal_matrix) / NU) * jnp.eye(
            NU, dtype=jnp.float32
        )
        factor = jnp.linalg.cholesky(normal_matrix)
        coeffs = jax.scipy.linalg.cho_solve((factor, True), projections)
        model = jnp.dot(coeffs, fields, precision=lax.Precision.HIGHEST)
        difference = exposure_image - model
        weight_now = coadd_weight[0, step] * intersection[0, step].astype(jnp.float32)
        pieces.append((weight_now * difference).reshape(rows, width))
        fitted.append(coeffs)
    weighted = jnp.stack(pieces)
    received_parts = lax.all_to_all(weighted[None], "expo", split_axis=3, concat_axis=0, tiled=True)
    coadd = jnp.sum(received_parts, axis=0)
    return (coadd, jnp.stack(fitted)[None])


def per_device(template, science, plan, orders, coadd_weight, intersection):
    expos = lax.axis_size("expo")
    rows, width = template.shape[1:]
    whole_lanes = width % (expos * LANES) == 0 and rows % 16 == 0 and 3 * rows <= LANES
    few = (NU + 1) * expos <= LANES and NU + expos <= LANES
    body = tiled_device if whole_lanes and few else any_device
    return body(template, science, plan, orders, coadd_weight, intersection)


def solution(mesh):
    return jax.shard_map(
        per_device,
        mesh=mesh,
        in_specs=(
            P(("groups", "expo"), "tile", None),
            P(("groups", "expo"), None, "tile", None),
            P("groups"),
            P(),
            P(("groups", "expo"), None),
            P(("groups", "expo"), None),
        ),
        out_specs=(P("groups", "tile", "expo"), P(("groups", "expo"), None, None)),
        check_vma=False,
    )
```

```python
import functools

import jax
import jax.numpy as jnp
import numpy as np
from jax import lax
from jax.experimental import pallas as pl
from jax.experimental.pallas import tpu as pltpu
from jax.sharding import PartitionSpec as P

HALF = 15
NB = 6
NU = 13
LANES = 128
BEYOND = 1000
PAIRS = [(j, k) for j in range(NB) for k in range(j, NB)]

SIGMAS = (0.8, 1.4, 2.2, 3.0, 4.0, 5.5)
RIDGE = 0.05


def power_of(pos, order):
    return jnp.where(order == 0, 1.0, jnp.where(order == 1, pos, pos * pos))


def tap_values(pos, sigma, order):
    value = jnp.exp(-pos * pos / (2.0 * sigma * sigma)) * power_of(pos, order)
    return jnp.where(jnp.abs(pos) <= HALF, value, 0.0)


def tap_norm(sigma, order):
    pos = lax.broadcasted_iota(jnp.int32, (8, LANES), 1).astype(jnp.float32) - HALF
    value = tap_values(pos, sigma, order)
    return jnp.sqrt(jnp.sum(value * value, axis=1, keepdims=True))


def target(me, shift, size):
    return (me + shift) % size


def source(me, shift, size):
    return (me - shift + size) % size


def joint(shift, size):
    return shift in (0, size // 2)


def template_order(size):
    first = [shift for shift in range(1, size) if joint(shift, size)]
    return first + [shift for shift in range(size - 1, 0, -1) if shift not in first] + [0]


def send_kernel(template_ref, science_ref, plan_ref, orders_ref, *refs, step):
    *out_refs, owner_ref, order_ref, patch_ref, plan_now, orders_now, sems = refs
    size = sems.shape[0] - 4
    rows, width = science_ref.shape
    chunk = width // size
    ext = chunk + LANES
    patch_refs, apart = out_refs[:size], out_refs[size:]
    image_refs = [
        patch_refs[shift].at[:, pl.ds(ext, chunk)] if joint(shift, size) else apart.pop(0).at[:, pl.ds(0, chunk)]
        for shift in range(size)
    ]
    half = size * chunk // 2
    me = lax.axis_index("expo")
    starts = [pl.multiple_of(target(me, shift, size) * chunk, chunk) for shift in range(size)]
    loads = [
        pltpu.make_async_copy(
            template_ref.at[:, pl.ds(i * half, half)], patch_ref.at[:, pl.ds((i * half + LANES), half)], sems.at[i]
        )
        for i in range(2)
    ]
    copies = [
        pltpu.make_async_copy(
            science_ref.at[:, pl.ds(starts[shift], chunk)],
            image_refs[shift],
            sems.at[3 + shift],
        )
        for shift in range(size)
    ]
    copies.append(pltpu.make_async_copy(plan_ref, plan_now, sems.at[2]))
    copies.append(pltpu.make_async_copy(orders_ref, orders_now, sems.at[3 + size]))
    for copy in loads + copies:
        copy.start()
    blank = jnp.zeros((rows, LANES), patch_ref.dtype)
    patch_ref[:, :LANES] = blank
    patch_ref[:, size * chunk + LANES :] = blank
    for ref in out_refs[size:]:
        ref[:, chunk:] = blank
    for copy in loads:
        copy.wait()
    lane = lax.broadcasted_iota(jnp.int32, (rows, LANES), 1)
    for shift in range(size):
        start = starts[shift]
        patch_refs[shift][:, :chunk] = patch_ref[:, pl.ds(start + LANES, chunk)]
        before = patch_ref[:, pl.ds(start, LANES)].astype(jnp.float32)
        after = patch_ref[:, pl.ds(start + chunk + LANES, LANES)].astype(jnp.float32)
        rim = jnp.where(lane < LANES // 2, after, before)
        patch_refs[shift][:, chunk:ext] = rim.astype(patch_ref.dtype)
    for copy in copies:
        copy.wait()
    owner_ref[...] = jnp.full(owner_ref.shape, plan_now[step], jnp.int32)
    for way in range(2):
        for k in range(NB):
            order_ref[way, k] = jnp.full((8, LANES), orders_now[way, k], jnp.int32)


def pick_kernel(owner_ref, *refs):
    *recv_refs, out_ref, block_ref = refs
    ext = out_ref.shape[1]
    size = len(recv_refs)
    me = lax.axis_index("expo")
    order = template_order(size)
    for b in range(ext // LANES):
        columns = slice(b * LANES, (b + 1) * LANES)
        block = recv_refs[-1][:, columns].astype(jnp.float32)
        for shift, ref in zip(order[:-1], recv_refs):
            block = jnp.where(
                owner_ref[...] == source(me, shift, size), ref[:, columns].astype(jnp.float32), block
            )
        block_ref[:, columns] = block.astype(out_ref.dtype)
    whole = jnp.concatenate([block_ref[:, ext - LANES :], block_ref[...]], axis=1)
    out_ref[...] = whole[:, LANES - HALF : LANES - HALF + ext]


def column_positions(first_col, block, width):
    col = lax.broadcasted_iota(jnp.int32, (8, LANES), 1) + (first_col + block * LANES)
    return 2.0 * (col.astype(jnp.float32) + 0.5) / width - 1.0


def band_kernel(order_ref, _, row_ref, col_ref, *, tiles):
    rows = row_ref.shape[0] // NB
    tile_at = lax.axis_index("tile")
    near = 1 - 2 * lax.rem(tile_at, 2)
    near_move = jnp.where(tile_at + near < tiles, near - 1, BEYOND)
    far_move = jnp.where((tile_at >= near) & (tile_at - near < tiles), -near - 2, BEYOND)
    row_from = lax.broadcasted_iota(jnp.int32, (8, LANES), 1)
    moved = jnp.where(row_from < rows, 0, jnp.where(row_from < 2 * rows, near_move, far_move))
    sub = lax.broadcasted_iota(jnp.int32, (8, LANES), 0)
    lane = lax.broadcasted_iota(jnp.int32, (8, LANES), 1)
    shift = (sub - jnp.where(lane < LANES // 2, lane, lane - LANES) - HALF).astype(jnp.float32)
    for k in range(NB):
        norm = tap_norm(SIGMAS[k], order_ref[0, k])
        for r in range(0, rows, 16):
            parts = []
            for half in (r, r + 8):
                offset = (row_from + moved * rows - sub - half).astype(jnp.float32)
                parts.append(tap_values(offset, SIGMAS[k], order_ref[0, k]) / norm)
            both = jnp.concatenate(parts, axis=0).astype(jnp.bfloat16)
            row_ref[k * rows + r : k * rows + r + 16] = both[:, : 3 * rows]
        norm = tap_norm(SIGMAS[k], order_ref[1, k])
        pattern = tap_values(shift, SIGMAS[k], order_ref[1, k]) / norm
        for r in range(0, 2 * LANES, 16):
            parts = []
            for half in (r, r + 8):
                moved_on = pltpu.roll(pattern, half % LANES, 1) if half % LANES else pattern
                inside = lane <= half + 7 if half < LANES else lane >= half - LANES + LANES // 2
                parts.append(jnp.where(inside, moved_on, 0.0))
            col_ref[k, r : r + 16] = jnp.concatenate(parts, axis=0).astype(jnp.bfloat16)


def image_blocks(ref, size, shift, chunk):
    first = chunk + LANES if joint(shift, size) else 0
    return lambda b: ref[:, first + b * LANES : first + (b + 1) * LANES].astype(jnp.float32)


def fit_kernel(weight_ref, hits_ref, row_band_ref, col_band_ref, own_ref, near_ref, far_ref, *refs, width):
    *image_refs, conv_ref, sums_ref, row_ref, parts_ref = refs
    tile_at = lax.axis_index("tile")
    expo_at = lax.axis_index("expo")
    rows, ext = own_ref.shape
    expos = len(image_refs)
    chunk = ext - LANES
    blocks = chunk // LANES

    patch = jnp.concatenate([own_ref[...], near_ref[...], far_ref[...]], axis=0)
    row_ref[...] = jnp.dot(
        row_band_ref[...], patch, preferred_element_type=jnp.float32
    ).astype(jnp.bfloat16)
    for k in range(NB):
        window = jnp.concatenate(
            [
                row_ref[k * rows : (k + 1) * rows, b * LANES : (b + 2) * LANES]
                for b in range(blocks)
            ],
            axis=0,
        )
        out = jnp.dot(window, col_band_ref[k], preferred_element_type=jnp.float32)
        conv_ref[k] = out.reshape(blocks, rows, LANES)

    first_col = expo_at * chunk
    xs = [column_positions(first_col, b, width) for b in range(blocks)]

    def fold(x):
        total = x[:8]
        for i in range(8, rows, 8):
            total = total + x[i : i + 8]
        return total

    def moments(at, left, right, count):
        total = [None] * count
        for b in range(blocks):
            term = fold(left(b) * right(b)) if right is not None else fold(left(b))
            for i in range(count):
                total[i] = term if total[i] is None else total[i] + term
                if i < count - 1:
                    term = term * xs[b]
        for i in range(count):
            parts_ref[at + i] = total[i]

    def conv(k):
        return lambda b: conv_ref[k, b]

    def sci(shift):
        return image_blocks(image_refs[shift], expos, shift, chunk)

    blank = jnp.zeros((8, LANES), jnp.float32)
    at = 0
    for j, k in PAIRS:
        moments(at, conv(j), conv(k), 3)
        at += 3
    for k in range(NB):
        moments(at, conv(k), None, 2)
        at += 2
    while at % 8:
        parts_ref[at] = blank
        at += 1
    begin = at
    for shift in range(expos):
        row = at + NU * source(expo_at, shift, expos)
        for k in range(NB):
            moments(row + 2 * k, conv(k), sci(shift), 2)
        moments(row + NU - 1, sci(shift), None, 1)
    at += NU * expos
    weight = jnp.broadcast_to(weight_ref[...] * hits_ref[...].astype(jnp.float32), (8, LANES))
    weight = jnp.where(tile_at == 0, weight, 0.0)
    spot = (
        (lax.broadcasted_iota(jnp.int32, (8, LANES), 0) == 0)
        & (lax.broadcasted_iota(jnp.int32, (8, LANES), 1) == 0)
    )
    for e in range(expos):
        parts_ref[at + e] = jnp.where(spot & (expo_at == e), weight, 0.0)
    at += expos
    while at % 8:
        parts_ref[at] = blank
        at += 1
    ones = jnp.ones((8, LANES), jnp.float32)
    rows_of = []
    for first, last in ((0, begin), (begin, at)):
        lanes = jnp.sum(parts_ref[first:last], axis=1)
        spare = LANES - (last - first)
        if spare:
            lanes = jnp.concatenate([lanes, jnp.zeros((spare, LANES), jnp.float32)], axis=0)
        rows_of.append(
            lax.dot_general(
                ones,
                lanes,
                (((1,), (1,)), ((), ())),
                precision=lax.Precision.HIGHEST,
                preferred_element_type=jnp.float32,
            )
        )
    both = jnp.where(lax.broadcasted_iota(jnp.int32, (8, LANES), 0) < 4, rows_of[0], rows_of[1])
    for i in range(sums_ref.shape[0]):
        sums_ref[i] = both


def table(expos):
    columns = np.zeros((NU + expos + 1, 16), np.int32)
    for at, (j, k) in enumerate(PAIRS):
        for a, b in ((j, k), (k, j)):
            columns[b, a] = 3 * at
            columns[NB + b, a] = columns[b, NB + a] = 3 * at + 1
            columns[NB + b, NB + a] = 3 * at + 2
    for k in range(NB):
        for x in range(2):
            columns[NU - 1, x * NB + k] = columns[x * NB + k, NU - 1] = 3 * len(PAIRS) + 2 * k + x
    for e in range(expos):
        columns[NU + e, :NU] = [NU * e + 2 * k + x for x in range(2) for k in range(NB)] + [NU * e + NU - 1]
        columns[NU + expos, e] = NU * expos + e
    return np.ascontiguousarray(np.broadcast_to(columns[:, :, None], columns.shape + (LANES,)))


def solve_kernel(table_ref, sums_ref, conv_ref, *refs, width, pixels):
    *image_refs, coadd_ref, coeffs_ref, tile_ref, sems = refs
    expo_at = lax.axis_index("expo")
    expos = len(image_refs)
    rows, chunk = coadd_ref.shape
    blocks = chunk // LANES
    images = [image_blocks(ref, expos, shift, chunk) for shift, ref in enumerate(image_refs)]
    sub = lax.broadcasted_iota(jnp.int32, (16, LANES), 0)
    lane = lax.broadcasted_iota(jnp.int32, (16, LANES), 1)
    sums = sums_ref[0]
    for i in range(1, sums_ref.shape[0]):
        sums = sums + sums_ref[i]
    first = jnp.broadcast_to(sums[0:1], (16, LANES))
    second = jnp.broadcast_to(sums[4:5], (16, LANES))

    columns = [
        jnp.take_along_axis(first if j < NU else second, table_ref[j], axis=1) for j in range(NU + expos)
    ]
    spread = jnp.take_along_axis(second, table_ref[NU + expos], axis=1)
    weight = [jnp.broadcast_to(spread[e : e + 1], (16, LANES)) for e in range(expos)]
    columns[NU - 1] = jnp.where(sub == NU - 1, float(pixels), columns[NU - 1])

    trace = columns[0][0:1]
    for j in range(1, NU):
        trace = trace + columns[j][j : j + 1]
    scale = 1.0 / trace
    for j in range(NU + expos):
        columns[j] = columns[j] * scale
        if j < NU:
            columns[j] = columns[j] + jnp.where(sub == j, RIDGE / NU, 0.0)
    for i in range(NU):
        inverse = 1.0 / columns[i][i : i + 1]
        for j in range(i + 1, NU + expos):
            factor = columns[j][i : i + 1] * inverse
            columns[j] = jnp.where(sub == i, factor, columns[j] - columns[i] * factor)

    solved = columns[NU:]
    own = solved[0]
    mixed = weight[0] * solved[0]
    for e in range(1, expos):
        own = jnp.where(expo_at == e, solved[e], own)
        mixed = mixed + weight[e] * solved[e]
    diagonal = (sub == lane) & (sub < NU)
    coeffs_ref[...] = jnp.sum(jnp.where(diagonal, own, 0.0), axis=0, keepdims=True)[:, :NU]
    scale = [jnp.broadcast_to(mixed[u : u + 1], (8, LANES)) for u in range(NU)]
    gains = []
    for shift in range(expos):
        gain = weight[0][:8]
        for e in range(1, expos):
            gain = jnp.where(source(expo_at, shift, expos) == e, weight[e][:8], gain)
        gains.append(gain)
    first_col = expo_at * chunk
    copies = []
    for r in range(0, rows, 8):
        for b in range(blocks):
            x = column_positions(first_col, b, width)
            total = -scale[NU - 1]
            for gain, image in zip(gains, images):
                total = total + gain * image(b)[r : r + 8]
            model = (scale[0] + scale[NB] * x) * conv_ref[0, b, r : r + 8]
            for k in range(1, NB):
                model = model + (scale[k] + scale[NB + k] * x) * conv_ref[k, b, r : r + 8]
            tile_ref[r : r + 8, b * LANES : (b + 1) * LANES] = total - model
        copies.append(
            pltpu.make_async_copy(tile_ref.at[pl.ds(r, 8)], coadd_ref.at[pl.ds(r, 8)], sems.at[r // 8])
        )
        copies[-1].start()
    for copy in copies:
        copy.wait()


def swaps(first, size):
    pairs = [(i, i + 1) for i in range(first, size - 1, 2)]
    if first and size % 2 == 0:
        pairs.append((0, size - 1))
    return [pair for a, b in pairs for pair in ((a, b), (b, a))]


def tiled_device(template, science, plan, orders, coadd_weight, intersection):
    expos = lax.axis_size("expo")
    tiles = lax.axis_size("tile")
    _, rows, width = template.shape
    steps = science.shape[1]
    chunk = width // expos
    ext = chunk + LANES
    blocks = chunk // LANES
    vmem = pl.BlockSpec(memory_space=pltpu.VMEM)
    small = pltpu.CompilerParams(vmem_limit_bytes=16 * 1024 * 1024)
    hbm = pl.BlockSpec(memory_space=pltpu.HBM)
    coadds = []
    fitted = []
    for step in range(steps):
        apart = sum(not joint(shift, expos) for shift in range(expos))
        *blocks_out, owner, order = pl.pallas_call(
            functools.partial(send_kernel, step=step),
            out_shape=tuple(
                pltpu.VMEM((rows, ext + chunk if joint(shift, expos) else ext), template.dtype)
                for shift in range(expos)
            )
            + (pltpu.VMEM((rows, ext), science.dtype),) * apart
            + (
                jax.ShapeDtypeStruct((rows, LANES), jnp.int32),
                jax.ShapeDtypeStruct((2, NB, 8, LANES), jnp.int32),
            ),
            in_specs=[hbm] * 4,
            out_specs=(vmem,) * (expos + apart + 2),
            scratch_shapes=[
                pltpu.VMEM((rows, width + 2 * LANES), template.dtype),
                pltpu.SMEM(plan.shape, jnp.int32),
                pltpu.SMEM((2, NB), jnp.int32),
                pltpu.SemaphoreType.DMA((expos + 4,)),
            ],
            compiler_params=small,
        )(
            pltpu.with_memory_space_constraint(template[0], pltpu.HBM),
            pltpu.with_memory_space_constraint(science[0, step], pltpu.HBM),
            pltpu.with_memory_space_constraint(plan, pltpu.HBM),
            pltpu.with_memory_space_constraint(orders.T, pltpu.HBM),
        )
        patches, images = [], []
        for shift in range(expos):
            pairs = [(e, target(e, shift, expos)) for e in range(expos)]
            patches.append(lax.ppermute(blocks_out[shift], "expo", pairs) if shift else blocks_out[shift])
        blocks_out = blocks_out[expos:]
        for shift in range(expos):
            pairs = [(e, target(e, shift, expos)) for e in range(expos)]
            images.append(
                patches[shift] if joint(shift, expos) else lax.ppermute(blocks_out.pop(0), "expo", pairs)
            )
        own = pl.pallas_call(
            pick_kernel,
            out_shape=jax.ShapeDtypeStruct((rows, ext), template.dtype),
            in_specs=[vmem] * (1 + expos),
            out_specs=vmem,
            scratch_shapes=[pltpu.VMEM((rows, ext), template.dtype)],
            compiler_params=small,
        )(owner, *(patches[shift] for shift in template_order(expos)))
        row_band, col_band = pl.pallas_call(
            functools.partial(band_kernel, tiles=tiles),
            out_shape=(
                jax.ShapeDtypeStruct((NB * rows, 3 * rows), jnp.bfloat16),
                jax.ShapeDtypeStruct((NB, 2 * LANES, LANES), jnp.bfloat16),
            ),
            in_specs=[vmem, pl.BlockSpec(memory_space=pl.ANY)],
            out_specs=(vmem, vmem),
            compiler_params=small,
            cost_estimate=pl.CostEstimate(flops=4_000_000, bytes_accessed=500_000, transcendentals=200_000),
        )(order, own)
        far = lax.ppermute(own, "tile", swaps(1, tiles))
        near = lax.ppermute(own, "tile", swaps(0, tiles))
        conv, sums = pl.pallas_call(
            functools.partial(fit_kernel, width=width),
            out_shape=(
                jax.ShapeDtypeStruct((NB, blocks, rows, LANES), jnp.float32),
                jax.ShapeDtypeStruct((tiles * expos, 8, LANES), jnp.float32),
            ),
            in_specs=[vmem] * (7 + expos),
            out_specs=(vmem, vmem),
            scratch_shapes=[
                pltpu.VMEM((NB * rows, ext), jnp.bfloat16),
                pltpu.VMEM((80 + 14 * expos + 8, 8, LANES), jnp.float32),
            ],
            compiler_params=small,
        )(
            coadd_weight[:, step : step + 1],
            intersection[:, step : step + 1],
            row_band,
            col_band,
            own,
            near,
            far,
            *images,
        )
        sums = lax.all_to_all(sums, ("tile", "expo"), split_axis=0, concat_axis=0, tiled=True)
        coadd, coeffs = pl.pallas_call(
            functools.partial(solve_kernel, width=width, pixels=tiles * rows * width),
            out_shape=(
                jax.ShapeDtypeStruct((rows, chunk), jnp.float32),
                jax.ShapeDtypeStruct((1, NU), jnp.float32),
            ),
            in_specs=[vmem] * (3 + expos),
            out_specs=(pl.BlockSpec(memory_space=pl.ANY), vmem),
            scratch_shapes=[
                pltpu.VMEM((rows, chunk), jnp.float32),
                pltpu.SemaphoreType.DMA((rows // 8,)),
            ],
            compiler_params=small,
        )(jnp.asarray(table(expos)), sums, conv, *images)
        coadds.append(coadd[None])
        fitted.append(coeffs)
    return (jnp.concatenate(coadds), jnp.stack(fitted, axis=1))


def broadcast(block, axis, holder):
    block = jnp.where(lax.axis_index(axis) == holder, block, jnp.zeros_like(block))
    return lax.psum(block, axis)


def extended(x, sides, width):
    for axis, dim in sides:
        size, length = (lax.axis_size(axis), x.shape[dim])
        up = [(i, (i + 1) % size) for i in range(size - 1)]
        down = [(j, i) for i, j in up]
        last = lax.slice_in_dim(x, length - width, length, axis=dim)
        first = lax.slice_in_dim(x, 0, width, axis=dim)
        before = lax.ppermute(last, axis, up)
        after = lax.ppermute(first, axis, down)
        x = jnp.concatenate([before, x, after], axis=dim)
    return x


def make_filters(orders):
    taps_pos = jnp.arange(2 * HALF + 1).astype(jnp.float32) - HALF
    row_list = []
    col_list = []
    for basis in range(NB):
        sigma = SIGMAS[basis]
        envelope = jnp.exp(-taps_pos * taps_pos / (2.0 * sigma * sigma))
        row_filter = envelope * power_of(taps_pos, orders[basis, 0])
        col_filter = envelope * power_of(taps_pos, orders[basis, 1])
        row_list.append(row_filter / jnp.sqrt(jnp.sum(row_filter * row_filter)))
        col_list.append(col_filter / jnp.sqrt(jnp.sum(col_filter * col_filter)))
    return (jnp.stack(row_list).astype(jnp.bfloat16), jnp.stack(col_list).astype(jnp.bfloat16))


def band_matrix(filters, out_len, in_len):
    offset = jnp.arange(in_len)[None, :] - jnp.arange(out_len)[:, None]
    taps_idx = jnp.arange(2 * HALF + 1)
    picks = (offset[:, :, None] == taps_idx[None, None, :]).astype(jnp.float32)
    band = jnp.einsum("ijt,kt->kij", picks, filters.astype(jnp.float32))
    return band.astype(jnp.bfloat16)


def any_device(template, science, plan, orders, coadd_weight, intersection):
    row_filters, col_filters = make_filters(orders)
    rows = template.shape[1]
    width = template.shape[2]
    blocks_count = width // 128
    steps_count = science.shape[1]
    row_band = band_matrix(row_filters, rows, rows + 2 * HALF)
    col_band = jnp.transpose(band_matrix(col_filters, 128, 128 + 2 * HALF), (0, 2, 1))
    column_pos = 2.0 * (jnp.arange(width).astype(jnp.float32) + 0.5) / width - 1.0
    pieces = []
    fitted = []
    for step in range(steps_count):
        received = broadcast(template[0], "expo", plan[step])
        padded = extended(received, (("tile", 0),), HALF)
        rowconv = jnp.einsum(
            "kij,jw->kiw", row_band, padded, preferred_element_type=jnp.float32
        ).astype(jnp.bfloat16)
        blocks = rowconv.reshape(NB, rows, blocks_count, 128)
        empty_rim = jnp.zeros((NB, rows, 1, HALF), jnp.bfloat16)
        previous = jnp.concatenate([empty_rim, blocks[:, :, :-1, 128 - HALF :]], axis=2)
        following = jnp.concatenate([blocks[:, :, 1:, :HALF], empty_rim], axis=2)
        window = jnp.concatenate([previous, blocks, following], axis=3)
        conv = jnp.einsum("krbj,kjc->krbc", window, col_band, preferred_element_type=jnp.float32)
        conv = conv.reshape(NB, rows, width)
        fields = jnp.concatenate(
            [conv, conv * column_pos, jnp.ones((1, rows, width), jnp.float32)], axis=0
        )
        fields = fields.reshape(NU, rows * width)
        exposure_image = science[0, step].astype(jnp.float32).reshape(rows * width)
        normal_local = jnp.dot(fields, fields.T, precision=lax.Precision.HIGHEST)
        project_local = jnp.dot(fields, exposure_image, precision=lax.Precision.HIGHEST)
        normal_matrix, projections = lax.psum((normal_local, project_local), "tile")
        normal_matrix = normal_matrix + RIDGE * (jnp.trace(normal_matrix) / NU) * jnp.eye(
            NU, dtype=jnp.float32
        )
        factor = jnp.linalg.cholesky(normal_matrix)
        coeffs = jax.scipy.linalg.cho_solve((factor, True), projections)
        model = jnp.dot(coeffs, fields, precision=lax.Precision.HIGHEST)
        difference = exposure_image - model
        weight_now = coadd_weight[0, step] * intersection[0, step].astype(jnp.float32)
        pieces.append((weight_now * difference).reshape(rows, width))
        fitted.append(coeffs)
    weighted = jnp.stack(pieces)
    received_parts = lax.all_to_all(weighted[None], "expo", split_axis=3, concat_axis=0, tiled=True)
    coadd = jnp.sum(received_parts, axis=0)
    return (coadd, jnp.stack(fitted)[None])


def per_device(template, science, plan, orders, coadd_weight, intersection):
    expos = lax.axis_size("expo")
    rows, width = template.shape[1:]
    whole_lanes = width % (expos * LANES) == 0 and rows % 16 == 0 and 3 * rows <= LANES
    few = (NU + 1) * expos <= LANES and NU + expos <= LANES
    body = tiled_device if whole_lanes and few else any_device
    return body(template, science, plan, orders, coadd_weight, intersection)


def solution(mesh):
    return jax.shard_map(
        per_device,
        mesh=mesh,
        in_specs=(
            P(("groups", "expo"), "tile", None),
            P(("groups", "expo"), None, "tile", None),
            P("groups"),
            P(),
            P(("groups", "expo"), None),
            P(("groups", "expo"), None),
        ),
        out_specs=(P("groups", "tile", "expo"), P(("groups", "expo"), None, None)),
        check_vma=False,
    )
```

```python
import functools

import jax
import jax.numpy as jnp
import numpy as np
from jax import lax
from jax.experimental import pallas as pl
from jax.experimental.pallas import tpu as pltpu
from jax.sharding import PartitionSpec as P

HALF = 15
NB = 6
NU = 13
LANES = 128
BEYOND = 1000
PAIRS = [(j, k) for j in range(NB) for k in range(j, NB)]

SIGMAS = (0.8, 1.4, 2.2, 3.0, 4.0, 5.5)
RIDGE = 0.05


def power_of(pos, order):
    return jnp.where(order == 0, 1.0, jnp.where(order == 1, pos, pos * pos))


def tap_values(pos, sigma, order):
    value = jnp.exp(-pos * pos / (2.0 * sigma * sigma)) * power_of(pos, order)
    return jnp.where(jnp.abs(pos) <= HALF, value, 0.0)


def tap_norm(sigma, order):
    pos = lax.broadcasted_iota(jnp.int32, (8, LANES), 1).astype(jnp.float32) - HALF
    value = tap_values(pos, sigma, order)
    return jnp.sqrt(jnp.sum(value * value, axis=1, keepdims=True))


def target(me, shift, size):
    return (me + shift) % size


def source(me, shift, size):
    return (me - shift + size) % size


def joint(shift, size):
    return shift < min(2, size)


def template_order(size):
    return [*range(1, size), 0]


def send_kernel(template_ref, science_ref, plan_ref, orders_ref, *refs, step):
    *out_refs, owner_ref, order_ref, patch_ref, plan_now, orders_now, sems = refs
    size = sems.shape[0] - 4
    rows, width = science_ref.shape
    chunk = width // size
    ext = chunk + LANES
    patch_refs, apart = out_refs[:size], out_refs[size:]
    image_refs = [
        patch_refs[shift].at[:, pl.ds(ext, chunk)] if joint(shift, size) else apart.pop(0).at[:, pl.ds(0, chunk)]
        for shift in range(size)
    ]
    half = size * chunk // 2
    me = lax.axis_index("expo")
    starts = [pl.multiple_of(target(me, shift, size) * chunk, chunk) for shift in range(size)]
    loads = [
        pltpu.make_async_copy(
            template_ref.at[:, pl.ds(i * half, half)], patch_ref.at[:, pl.ds((i * half + LANES), half)], sems.at[i]
        )
        for i in range(2)
    ]
    copies = [
        pltpu.make_async_copy(
            science_ref.at[:, pl.ds(starts[shift], chunk)],
            image_refs[shift],
            sems.at[3 + shift],
        )
        for shift in range(size)
    ]
    copies.append(pltpu.make_async_copy(plan_ref, plan_now, sems.at[2]))
    copies.append(pltpu.make_async_copy(orders_ref, orders_now, sems.at[3 + size]))
    for copy in loads + copies:
        copy.start()
    blank = jnp.zeros((rows, LANES), patch_ref.dtype)
    patch_ref[:, :LANES] = blank
    patch_ref[:, size * chunk + LANES :] = blank
    for ref in out_refs[size:]:
        ref[:, chunk:] = blank
    for copy in loads:
        copy.wait()
    lane = lax.broadcasted_iota(jnp.int32, (rows, LANES), 1)
    for shift in range(size):
        start = starts[shift]
        patch_refs[shift][:, :chunk] = patch_ref[:, pl.ds(start + LANES, chunk)]
        before = patch_ref[:, pl.ds(start, LANES)].astype(jnp.float32)
        after = patch_ref[:, pl.ds(start + chunk + LANES, LANES)].astype(jnp.float32)
        rim = jnp.where(lane < LANES // 2, after, before)
        patch_refs[shift][:, chunk:ext] = rim.astype(patch_ref.dtype)
    for copy in copies:
        copy.wait()
    owner_ref[...] = jnp.full(owner_ref.shape, plan_now[step], jnp.int32)
    for way in range(2):
        for k in range(NB):
            order_ref[way, k] = jnp.full((8, LANES), orders_now[way, k], jnp.int32)


def pick_kernel(owner_ref, *refs):
    *recv_refs, out_ref, block_ref = refs
    ext = out_ref.shape[1]
    size = len(recv_refs)
    me = lax.axis_index("expo")
    order = template_order(size)
    for b in range(ext // LANES):
        columns = slice(b * LANES, (b + 1) * LANES)
        block = recv_refs[-1][:, columns].astype(jnp.float32)
        for shift, ref in zip(order[:-1], recv_refs):
            block = jnp.where(
                owner_ref[...] == source(me, shift, size), ref[:, columns].astype(jnp.float32), block
            )
        block_ref[:, columns] = block.astype(out_ref.dtype)
    whole = jnp.concatenate([block_ref[:, ext - LANES :], block_ref[...]], axis=1)
    out_ref[...] = whole[:, LANES - HALF : LANES - HALF + ext]


def column_positions(first_col, block, width):
    col = lax.broadcasted_iota(jnp.int32, (8, LANES), 1) + (first_col + block * LANES)
    return 2.0 * (col.astype(jnp.float32) + 0.5) / width - 1.0


def band_kernel(order_ref, _, row_ref, col_ref, *, tiles):
    rows = row_ref.shape[0] // NB
    tile_at = lax.axis_index("tile")
    near = 1 - 2 * lax.rem(tile_at, 2)
    near_move = jnp.where(tile_at + near < tiles, near - 1, BEYOND)
    far_move = jnp.where((tile_at >= near) & (tile_at - near < tiles), -near - 2, BEYOND)
    row_from = lax.broadcasted_iota(jnp.int32, (8, LANES), 1)
    moved = jnp.where(row_from < rows, 0, jnp.where(row_from < 2 * rows, near_move, far_move))
    sub = lax.broadcasted_iota(jnp.int32, (8, LANES), 0)
    lane = lax.broadcasted_iota(jnp.int32, (8, LANES), 1)
    shift = (sub - jnp.where(lane < LANES // 2, lane, lane - LANES) - HALF).astype(jnp.float32)
    for k in range(NB):
        norm = tap_norm(SIGMAS[k], order_ref[0, k])
        for r in range(0, rows, 16):
            parts = []
            for half in (r, r + 8):
                offset = (row_from + moved * rows - sub - half).astype(jnp.float32)
                parts.append(tap_values(offset, SIGMAS[k], order_ref[0, k]) / norm)
            both = jnp.concatenate(parts, axis=0).astype(jnp.bfloat16)
            row_ref[k * rows + r : k * rows + r + 16] = both[:, : 3 * rows]
        norm = tap_norm(SIGMAS[k], order_ref[1, k])
        pattern = tap_values(shift, SIGMAS[k], order_ref[1, k]) / norm
        for r in range(0, 2 * LANES, 16):
            parts = []
            for half in (r, r + 8):
                moved_on = pltpu.roll(pattern, half % LANES, 1) if half % LANES else pattern
                inside = lane <= half + 7 if half < LANES else lane >= half - LANES + LANES // 2
                parts.append(jnp.where(inside, moved_on, 0.0))
            col_ref[k, r : r + 16] = jnp.concatenate(parts, axis=0).astype(jnp.bfloat16)


def image_blocks(ref, size, shift, chunk):
    first = chunk + LANES if joint(shift, size) else 0
    return lambda b: ref[:, first + b * LANES : first + (b + 1) * LANES].astype(jnp.float32)


def fit_kernel(weight_ref, hits_ref, row_band_ref, col_band_ref, own_ref, near_ref, far_ref, *refs, width):
    *image_refs, conv_ref, sums_ref, row_ref, parts_ref = refs
    tile_at = lax.axis_index("tile")
    expo_at = lax.axis_index("expo")
    rows, ext = own_ref.shape
    expos = len(image_refs)
    chunk = ext - LANES
    blocks = chunk // LANES

    patch = jnp.concatenate([own_ref[...], near_ref[...], far_ref[...]], axis=0)
    row_ref[...] = jnp.dot(
        row_band_ref[...], patch, preferred_element_type=jnp.float32
    ).astype(jnp.bfloat16)
    for k in range(NB):
        window = jnp.concatenate(
            [
                row_ref[k * rows : (k + 1) * rows, b * LANES : (b + 2) * LANES]
                for b in range(blocks)
            ],
            axis=0,
        )
        out = jnp.dot(window, col_band_ref[k], preferred_element_type=jnp.float32)
        conv_ref[k] = out.reshape(blocks, rows, LANES)

    first_col = expo_at * chunk
    xs = [column_positions(first_col, b, width) for b in range(blocks)]

    def fold(x):
        total = x[:8]
        for i in range(8, rows, 8):
            total = total + x[i : i + 8]
        return total

    def moments(at, left, right, count):
        total = [None] * count
        for b in range(blocks):
            term = fold(left(b) * right(b)) if right is not None else fold(left(b))
            for i in range(count):
                total[i] = term if total[i] is None else total[i] + term
                if i < count - 1:
                    term = term * xs[b]
        for i in range(count):
            parts_ref[at + i] = total[i]

    def conv(k):
        return lambda b: conv_ref[k, b]

    def sci(shift):
        return image_blocks(image_refs[shift], expos, shift, chunk)

    blank = jnp.zeros((8, LANES), jnp.float32)
    at = 0
    for j, k in PAIRS:
        moments(at, conv(j), conv(k), 3)
        at += 3
    for k in range(NB):
        moments(at, conv(k), None, 2)
        at += 2
    while at % 8:
        parts_ref[at] = blank
        at += 1
    begin = at
    for shift in range(expos):
        row = at + NU * source(expo_at, shift, expos)
        for k in range(NB):
            moments(row + 2 * k, conv(k), sci(shift), 2)
        moments(row + NU - 1, sci(shift), None, 1)
    at += NU * expos
    weight = jnp.broadcast_to(weight_ref[...] * hits_ref[...].astype(jnp.float32), (8, LANES))
    weight = jnp.where(tile_at == 0, weight, 0.0)
    spot = (
        (lax.broadcasted_iota(jnp.int32, (8, LANES), 0) == 0)
        & (lax.broadcasted_iota(jnp.int32, (8, LANES), 1) == 0)
    )
    for e in range(expos):
        parts_ref[at + e] = jnp.where(spot & (expo_at == e), weight, 0.0)
    at += expos
    while at % 8:
        parts_ref[at] = blank
        at += 1
    ones = jnp.ones((8, LANES), jnp.float32)
    rows_of = []
    for first, last in ((0, begin), (begin, at)):
        lanes = jnp.sum(parts_ref[first:last], axis=1)
        spare = LANES - (last - first)
        if spare:
            lanes = jnp.concatenate([lanes, jnp.zeros((spare, LANES), jnp.float32)], axis=0)
        rows_of.append(
            lax.dot_general(
                ones,
                lanes,
                (((1,), (1,)), ((), ())),
                precision=lax.Precision.HIGHEST,
                preferred_element_type=jnp.float32,
            )
        )
    both = jnp.where(lax.broadcasted_iota(jnp.int32, (8, LANES), 0) < 4, rows_of[0], rows_of[1])
    for i in range(sums_ref.shape[0]):
        sums_ref[i] = both


def table(expos):
    columns = np.zeros((NU + expos + 1, 16), np.int32)
    for at, (j, k) in enumerate(PAIRS):
        for a, b in ((j, k), (k, j)):
            columns[b, a] = 3 * at
            columns[NB + b, a] = columns[b, NB + a] = 3 * at + 1
            columns[NB + b, NB + a] = 3 * at + 2
    for k in range(NB):
        for x in range(2):
            columns[NU - 1, x * NB + k] = columns[x * NB + k, NU - 1] = 3 * len(PAIRS) + 2 * k + x
    for e in range(expos):
        columns[NU + e, :NU] = [NU * e + 2 * k + x for x in range(2) for k in range(NB)] + [NU * e + NU - 1]
        columns[NU + expos, e] = NU * expos + e
    return np.ascontiguousarray(np.broadcast_to(columns[:, :, None], columns.shape + (LANES,)))


def solve_kernel(table_ref, sums_ref, conv_ref, *refs, width, pixels):
    *image_refs, coadd_ref, coeffs_ref, tile_ref, sems = refs
    expo_at = lax.axis_index("expo")
    expos = len(image_refs)
    rows, chunk = coadd_ref.shape
    blocks = chunk // LANES
    images = [image_blocks(ref, expos, shift, chunk) for shift, ref in enumerate(image_refs)]
    sub = lax.broadcasted_iota(jnp.int32, (16, LANES), 0)
    lane = lax.broadcasted_iota(jnp.int32, (16, LANES), 1)
    sums = sums_ref[0]
    for i in range(1, sums_ref.shape[0]):
        sums = sums + sums_ref[i]
    first = jnp.broadcast_to(sums[0:1], (16, LANES))
    second = jnp.broadcast_to(sums[4:5], (16, LANES))

    columns = [
        jnp.take_along_axis(first if j < NU else second, table_ref[j], axis=1) for j in range(NU + expos)
    ]
    spread = jnp.take_along_axis(second, table_ref[NU + expos], axis=1)
    weight = [jnp.broadcast_to(spread[e : e + 1], (16, LANES)) for e in range(expos)]
    columns[NU - 1] = jnp.where(sub == NU - 1, float(pixels), columns[NU - 1])

    trace = columns[0][0:1]
    for j in range(1, NU):
        trace = trace + columns[j][j : j + 1]
    scale = 1.0 / trace
    for j in range(NU + expos):
        columns[j] = columns[j] * scale
        if j < NU:
            columns[j] = columns[j] + jnp.where(sub == j, RIDGE / NU, 0.0)
    for i in range(NU):
        inverse = 1.0 / columns[i][i : i + 1]
        for j in range(i + 1, NU + expos):
            factor = columns[j][i : i + 1] * inverse
            columns[j] = jnp.where(sub == i, factor, columns[j] - columns[i] * factor)

    solved = columns[NU:]
    own = solved[0]
    mixed = weight[0] * solved[0]
    for e in range(1, expos):
        own = jnp.where(expo_at == e, solved[e], own)
        mixed = mixed + weight[e] * solved[e]
    diagonal = (sub == lane) & (sub < NU)
    coeffs_ref[...] = jnp.sum(jnp.where(diagonal, own, 0.0), axis=0, keepdims=True)[:, :NU]
    scale = [jnp.broadcast_to(mixed[u : u + 1], (8, LANES)) for u in range(NU)]
    gains = []
    for shift in range(expos):
        gain = weight[0][:8]
        for e in range(1, expos):
            gain = jnp.where(source(expo_at, shift, expos) == e, weight[e][:8], gain)
        gains.append(gain)
    first_col = expo_at * chunk
    copies = []
    for r in range(0, rows, 8):
        for b in range(blocks):
            x = column_positions(first_col, b, width)
            total = -scale[NU - 1]
            for gain, image in zip(gains, images):
                total = total + gain * image(b)[r : r + 8]
            model = (scale[0] + scale[NB] * x) * conv_ref[0, b, r : r + 8]
            for k in range(1, NB):
                model = model + (scale[k] + scale[NB + k] * x) * conv_ref[k, b, r : r + 8]
            tile_ref[r : r + 8, b * LANES : (b + 1) * LANES] = total - model
        copies.append(
            pltpu.make_async_copy(tile_ref.at[pl.ds(r, 8)], coadd_ref.at[pl.ds(r, 8)], sems.at[r // 8])
        )
        copies[-1].start()
    for copy in copies:
        copy.wait()


def swaps(first, size):
    pairs = [(i, i + 1) for i in range(first, size - 1, 2)]
    if first and size % 2 == 0:
        pairs.append((0, size - 1))
    return [pair for a, b in pairs for pair in ((a, b), (b, a))]


def tiled_device(template, science, plan, orders, coadd_weight, intersection):
    expos = lax.axis_size("expo")
    tiles = lax.axis_size("tile")
    _, rows, width = template.shape
    steps = science.shape[1]
    chunk = width // expos
    ext = chunk + LANES
    blocks = chunk // LANES
    vmem = pl.BlockSpec(memory_space=pltpu.VMEM)
    small = pltpu.CompilerParams(vmem_limit_bytes=16 * 1024 * 1024)
    hbm = pl.BlockSpec(memory_space=pltpu.HBM)
    coadds = []
    fitted = []
    for step in range(steps):
        apart = sum(not joint(shift, expos) for shift in range(expos))
        *blocks_out, owner, order = pl.pallas_call(
            functools.partial(send_kernel, step=step),
            out_shape=tuple(
                pltpu.VMEM((rows, ext + chunk if joint(shift, expos) else ext), template.dtype)
                for shift in range(expos)
            )
            + (pltpu.VMEM((rows, ext), science.dtype),) * apart
            + (
                jax.ShapeDtypeStruct((rows, LANES), jnp.int32),
                jax.ShapeDtypeStruct((2, NB, 8, LANES), jnp.int32),
            ),
            in_specs=[hbm] * 4,
            out_specs=(vmem,) * (expos + apart + 2),
            scratch_shapes=[
                pltpu.VMEM((rows, width + 2 * LANES), template.dtype),
                pltpu.SMEM(plan.shape, jnp.int32),
                pltpu.SMEM((2, NB), jnp.int32),
                pltpu.SemaphoreType.DMA((expos + 4,)),
            ],
            compiler_params=small,
        )(
            pltpu.with_memory_space_constraint(template[0], pltpu.HBM),
            pltpu.with_memory_space_constraint(science[0, step], pltpu.HBM),
            pltpu.with_memory_space_constraint(plan, pltpu.HBM),
            pltpu.with_memory_space_constraint(orders.T, pltpu.HBM),
        )
        patches, images = [], []
        for shift in range(expos):
            pairs = [(e, target(e, shift, expos)) for e in range(expos)]
            patches.append(lax.ppermute(blocks_out[shift], "expo", pairs) if shift else blocks_out[shift])
        blocks_out = blocks_out[expos:]
        for shift in range(expos):
            pairs = [(e, target(e, shift, expos)) for e in range(expos)]
            images.append(
                patches[shift] if joint(shift, expos) else lax.ppermute(blocks_out.pop(0), "expo", pairs)
            )
        own = pl.pallas_call(
            pick_kernel,
            out_shape=jax.ShapeDtypeStruct((rows, ext), template.dtype),
            in_specs=[vmem] * (1 + expos),
            out_specs=vmem,
            scratch_shapes=[pltpu.VMEM((rows, ext), template.dtype)],
            compiler_params=small,
        )(owner, *(patches[shift] for shift in template_order(expos)))
        row_band, col_band = pl.pallas_call(
            functools.partial(band_kernel, tiles=tiles),
            out_shape=(
                jax.ShapeDtypeStruct((NB * rows, 3 * rows), jnp.bfloat16),
                jax.ShapeDtypeStruct((NB, 2 * LANES, LANES), jnp.bfloat16),
            ),
            in_specs=[vmem, pl.BlockSpec(memory_space=pl.ANY)],
            out_specs=(vmem, vmem),
            compiler_params=small,
            cost_estimate=pl.CostEstimate(flops=4_000_000, bytes_accessed=500_000, transcendentals=200_000),
        )(order, own)
        far = lax.ppermute(own, "tile", swaps(1, tiles))
        near = lax.ppermute(own, "tile", swaps(0, tiles))
        conv, sums = pl.pallas_call(
            functools.partial(fit_kernel, width=width),
            out_shape=(
                jax.ShapeDtypeStruct((NB, blocks, rows, LANES), jnp.float32),
                jax.ShapeDtypeStruct((tiles * expos, 8, LANES), jnp.float32),
            ),
            in_specs=[vmem] * (7 + expos),
            out_specs=(vmem, vmem),
            scratch_shapes=[
                pltpu.VMEM((NB * rows, ext), jnp.bfloat16),
                pltpu.VMEM((80 + 14 * expos + 8, 8, LANES), jnp.float32),
            ],
            compiler_params=small,
        )(
            coadd_weight[:, step : step + 1],
            intersection[:, step : step + 1],
            row_band,
            col_band,
            own,
            near,
            far,
            *images,
        )
        sums = lax.all_to_all(sums, ("tile", "expo"), split_axis=0, concat_axis=0, tiled=True)
        coadd, coeffs = pl.pallas_call(
            functools.partial(solve_kernel, width=width, pixels=tiles * rows * width),
            out_shape=(
                jax.ShapeDtypeStruct((rows, chunk), jnp.float32),
                jax.ShapeDtypeStruct((1, NU), jnp.float32),
            ),
            in_specs=[vmem] * (3 + expos),
            out_specs=(pl.BlockSpec(memory_space=pl.ANY), vmem),
            scratch_shapes=[
                pltpu.VMEM((rows, chunk), jnp.float32),
                pltpu.SemaphoreType.DMA((rows // 8,)),
            ],
            compiler_params=small,
        )(jnp.asarray(table(expos)), sums, conv, *images)
        coadds.append(coadd[None])
        fitted.append(coeffs)
    return (jnp.concatenate(coadds), jnp.stack(fitted, axis=1))


def broadcast(block, axis, holder):
    block = jnp.where(lax.axis_index(axis) == holder, block, jnp.zeros_like(block))
    return lax.psum(block, axis)


def extended(x, sides, width):
    for axis, dim in sides:
        size, length = (lax.axis_size(axis), x.shape[dim])
        up = [(i, (i + 1) % size) for i in range(size - 1)]
        down = [(j, i) for i, j in up]
        last = lax.slice_in_dim(x, length - width, length, axis=dim)
        first = lax.slice_in_dim(x, 0, width, axis=dim)
        before = lax.ppermute(last, axis, up)
        after = lax.ppermute(first, axis, down)
        x = jnp.concatenate([before, x, after], axis=dim)
    return x


def make_filters(orders):
    taps_pos = jnp.arange(2 * HALF + 1).astype(jnp.float32) - HALF
    row_list = []
    col_list = []
    for basis in range(NB):
        sigma = SIGMAS[basis]
        envelope = jnp.exp(-taps_pos * taps_pos / (2.0 * sigma * sigma))
        row_filter = envelope * power_of(taps_pos, orders[basis, 0])
        col_filter = envelope * power_of(taps_pos, orders[basis, 1])
        row_list.append(row_filter / jnp.sqrt(jnp.sum(row_filter * row_filter)))
        col_list.append(col_filter / jnp.sqrt(jnp.sum(col_filter * col_filter)))
    return (jnp.stack(row_list).astype(jnp.bfloat16), jnp.stack(col_list).astype(jnp.bfloat16))


def band_matrix(filters, out_len, in_len):
    offset = jnp.arange(in_len)[None, :] - jnp.arange(out_len)[:, None]
    taps_idx = jnp.arange(2 * HALF + 1)
    picks = (offset[:, :, None] == taps_idx[None, None, :]).astype(jnp.float32)
    band = jnp.einsum("ijt,kt->kij", picks, filters.astype(jnp.float32))
    return band.astype(jnp.bfloat16)


def any_device(template, science, plan, orders, coadd_weight, intersection):
    row_filters, col_filters = make_filters(orders)
    rows = template.shape[1]
    width = template.shape[2]
    blocks_count = width // 128
    steps_count = science.shape[1]
    row_band = band_matrix(row_filters, rows, rows + 2 * HALF)
    col_band = jnp.transpose(band_matrix(col_filters, 128, 128 + 2 * HALF), (0, 2, 1))
    column_pos = 2.0 * (jnp.arange(width).astype(jnp.float32) + 0.5) / width - 1.0
    pieces = []
    fitted = []
    for step in range(steps_count):
        received = broadcast(template[0], "expo", plan[step])
        padded = extended(received, (("tile", 0),), HALF)
        rowconv = jnp.einsum(
            "kij,jw->kiw", row_band, padded, preferred_element_type=jnp.float32
        ).astype(jnp.bfloat16)
        blocks = rowconv.reshape(NB, rows, blocks_count, 128)
        empty_rim = jnp.zeros((NB, rows, 1, HALF), jnp.bfloat16)
        previous = jnp.concatenate([empty_rim, blocks[:, :, :-1, 128 - HALF :]], axis=2)
        following = jnp.concatenate([blocks[:, :, 1:, :HALF], empty_rim], axis=2)
        window = jnp.concatenate([previous, blocks, following], axis=3)
        conv = jnp.einsum("krbj,kjc->krbc", window, col_band, preferred_element_type=jnp.float32)
        conv = conv.reshape(NB, rows, width)
        fields = jnp.concatenate(
            [conv, conv * column_pos, jnp.ones((1, rows, width), jnp.float32)], axis=0
        )
        fields = fields.reshape(NU, rows * width)
        exposure_image = science[0, step].astype(jnp.float32).reshape(rows * width)
        normal_local = jnp.dot(fields, fields.T, precision=lax.Precision.HIGHEST)
        project_local = jnp.dot(fields, exposure_image, precision=lax.Precision.HIGHEST)
        normal_matrix, projections = lax.psum((normal_local, project_local), "tile")
        normal_matrix = normal_matrix + RIDGE * (jnp.trace(normal_matrix) / NU) * jnp.eye(
            NU, dtype=jnp.float32
        )
        factor = jnp.linalg.cholesky(normal_matrix)
        coeffs = jax.scipy.linalg.cho_solve((factor, True), projections)
        model = jnp.dot(coeffs, fields, precision=lax.Precision.HIGHEST)
        difference = exposure_image - model
        weight_now = coadd_weight[0, step] * intersection[0, step].astype(jnp.float32)
        pieces.append((weight_now * difference).reshape(rows, width))
        fitted.append(coeffs)
    weighted = jnp.stack(pieces)
    received_parts = lax.all_to_all(weighted[None], "expo", split_axis=3, concat_axis=0, tiled=True)
    coadd = jnp.sum(received_parts, axis=0)
    return (coadd, jnp.stack(fitted)[None])


def per_device(template, science, plan, orders, coadd_weight, intersection):
    expos = lax.axis_size("expo")
    rows, width = template.shape[1:]
    whole_lanes = width % (expos * LANES) == 0 and rows % 16 == 0 and 3 * rows <= LANES
    few = (NU + 1) * expos <= LANES and NU + expos <= LANES
    body = tiled_device if whole_lanes and few else any_device
    return body(template, science, plan, orders, coadd_weight, intersection)


def solution(mesh):
    return jax.shard_map(
        per_device,
        mesh=mesh,
        in_specs=(
            P(("groups", "expo"), "tile", None),
            P(("groups", "expo"), None, "tile", None),
            P("groups"),
            P(),
            P(("groups", "expo"), None),
            P(("groups", "expo"), None),
        ),
        out_specs=(P("groups", "tile", "expo"), P(("groups", "expo"), None, None)),
        check_vma=False,
    )
```

```python
import functools

import jax
import jax.numpy as jnp
import numpy as np
from jax import lax
from jax.experimental import pallas as pl
from jax.experimental.pallas import tpu as pltpu
from jax.sharding import PartitionSpec as P

HALF = 15
NB = 6
NU = 13
LANES = 128
BEYOND = 1000
PAIRS = [(j, k) for j in range(NB) for k in range(j, NB)]

SIGMAS = (0.8, 1.4, 2.2, 3.0, 4.0, 5.5)
RIDGE = 0.05


def power_of(pos, order):
    return jnp.where(order == 0, 1.0, jnp.where(order == 1, pos, pos * pos))


def tap_values(pos, sigma, order):
    value = jnp.exp(-pos * pos / (2.0 * sigma * sigma)) * power_of(pos, order)
    return jnp.where(jnp.abs(pos) <= HALF, value, 0.0)


def tap_norm(sigma, order):
    pos = lax.broadcasted_iota(jnp.int32, (8, LANES), 1).astype(jnp.float32) - HALF
    value = tap_values(pos, sigma, order)
    return jnp.sqrt(jnp.sum(value * value, axis=1, keepdims=True))


def target(me, shift, size):
    return (me + shift) % size


def source(me, shift, size):
    return (me - shift + size) % size


def joint(shift, size):
    return shift in (0, size // 2)


def template_order(size):
    first = [shift for shift in range(1, size) if joint(shift, size)]
    return first + [shift for shift in range(size - 1, 0, -1) if shift not in first] + [0]


def send_kernel(template_ref, science_ref, plan_ref, orders_ref, *refs, step):
    *out_refs, owner_ref, order_ref, patch_ref, plan_now, orders_now, sems = refs
    size = sems.shape[0] - 4
    rows, width = science_ref.shape
    chunk = width // size
    ext = chunk + LANES
    patch_refs, apart = out_refs[:size], out_refs[size:]
    image_refs = [
        patch_refs[shift].at[:, pl.ds(ext, chunk)] if joint(shift, size) else apart.pop(0).at[:, pl.ds(0, chunk)]
        for shift in range(size)
    ]
    half = size * chunk // 2
    me = lax.axis_index("expo")
    starts = [pl.multiple_of(target(me, shift, size) * chunk, chunk) for shift in range(size)]
    loads = [
        pltpu.make_async_copy(
            template_ref.at[:, pl.ds(i * half, half)], patch_ref.at[:, pl.ds((i * half + LANES), half)], sems.at[i]
        )
        for i in range(2)
    ]
    copies = [
        pltpu.make_async_copy(
            science_ref.at[:, pl.ds(starts[shift], chunk)],
            image_refs[shift],
            sems.at[3 + shift],
        )
        for shift in range(size)
    ]
    copies.append(pltpu.make_async_copy(plan_ref, plan_now, sems.at[2]))
    copies.append(pltpu.make_async_copy(orders_ref, orders_now, sems.at[3 + size]))
    for copy in loads + copies:
        copy.start()
    blank = jnp.zeros((rows, LANES), patch_ref.dtype)
    patch_ref[:, :LANES] = blank
    patch_ref[:, size * chunk + LANES :] = blank
    for ref in out_refs[size:]:
        ref[:, chunk:] = blank
    for copy in loads:
        copy.wait()
    lane = lax.broadcasted_iota(jnp.int32, (rows, LANES), 1)
    for shift in range(size):
        start = starts[shift]
        patch_refs[shift][:, :chunk] = patch_ref[:, pl.ds(start + LANES, chunk)]
        before = patch_ref[:, pl.ds(start, LANES)].astype(jnp.float32)
        after = patch_ref[:, pl.ds(start + chunk + LANES, LANES)].astype(jnp.float32)
        rim = jnp.where(lane < LANES // 2, after, before)
        patch_refs[shift][:, chunk:ext] = rim.astype(patch_ref.dtype)
    for copy in copies:
        copy.wait()
    owner_ref[...] = jnp.full(owner_ref.shape, plan_now[step], jnp.int32)
    for way in range(2):
        for k in range(NB):
            order_ref[way, k] = jnp.full((8, LANES), orders_now[way, k], jnp.int32)


def pick_kernel(owner_ref, *refs):
    *recv_refs, out_ref, block_ref = refs
    ext = out_ref.shape[1]
    size = len(recv_refs)
    me = lax.axis_index("expo")
    order = template_order(size)
    for b in range(ext // LANES):
        columns = slice(b * LANES, (b + 1) * LANES)
        block = recv_refs[-1][:, columns].astype(jnp.float32)
        for shift, ref in zip(order[:-1], recv_refs):
            block = jnp.where(
                owner_ref[...] == source(me, shift, size), ref[:, columns].astype(jnp.float32), block
            )
        block_ref[:, columns] = block.astype(out_ref.dtype)
    whole = jnp.concatenate([block_ref[:, ext - LANES :], block_ref[...]], axis=1)
    out_ref[...] = whole[:, LANES - HALF : LANES - HALF + ext]


def column_positions(first_col, block, width):
    col = lax.broadcasted_iota(jnp.int32, (8, LANES), 1) + (first_col + block * LANES)
    return 2.0 * (col.astype(jnp.float32) + 0.5) / width - 1.0


def band_kernel(order_ref, _, row_ref, col_ref, *, tiles):
    rows = row_ref.shape[0] // NB
    tile_at = lax.axis_index("tile")
    near = 1 - 2 * lax.rem(tile_at, 2)
    near_move = jnp.where(tile_at + near < tiles, near - 1, BEYOND)
    far_move = jnp.where((tile_at >= near) & (tile_at - near < tiles), -near - 2, BEYOND)
    row_from = lax.broadcasted_iota(jnp.int32, (8, LANES), 1)
    moved = jnp.where(row_from < rows, 0, jnp.where(row_from < 2 * rows, near_move, far_move))
    sub = lax.broadcasted_iota(jnp.int32, (8, LANES), 0)
    lane = lax.broadcasted_iota(jnp.int32, (8, LANES), 1)
    shift = (sub - jnp.where(lane < LANES // 2, lane, lane - LANES) - HALF).astype(jnp.float32)
    for k in range(NB):
        norm = tap_norm(SIGMAS[k], order_ref[0, k])
        for r in range(0, rows, 16):
            parts = []
            for half in (r, r + 8):
                offset = (row_from + moved * rows - sub - half).astype(jnp.float32)
                parts.append(tap_values(offset, SIGMAS[k], order_ref[0, k]) / norm)
            both = jnp.concatenate(parts, axis=0).astype(jnp.bfloat16)
            row_ref[k * rows + r : k * rows + r + 16] = both[:, : 3 * rows]
        norm = tap_norm(SIGMAS[k], order_ref[1, k])
        pattern = tap_values(shift, SIGMAS[k], order_ref[1, k]) / norm
        for r in range(0, 2 * LANES, 16):
            parts = []
            for half in (r, r + 8):
                moved_on = pltpu.roll(pattern, half % LANES, 1) if half % LANES else pattern
                inside = lane <= half + 7 if half < LANES else lane >= half - LANES + LANES // 2
                parts.append(jnp.where(inside, moved_on, 0.0))
            col_ref[k, r : r + 16] = jnp.concatenate(parts, axis=0).astype(jnp.bfloat16)


def image_blocks(ref, size, shift, chunk):
    first = chunk + LANES if joint(shift, size) else 0
    return lambda b: ref[:, first + b * LANES : first + (b + 1) * LANES].astype(jnp.float32)


def fit_kernel(weight_ref, hits_ref, row_band_ref, col_band_ref, own_ref, near_ref, far_ref, *refs, width):
    *image_refs, conv_ref, sums_ref, row_ref, parts_ref = refs
    tile_at = lax.axis_index("tile")
    expo_at = lax.axis_index("expo")
    rows, ext = own_ref.shape
    expos = len(image_refs)
    chunk = ext - LANES
    blocks = chunk // LANES

    patch = jnp.concatenate([own_ref[...], near_ref[...], far_ref[...]], axis=0)
    row_ref[...] = jnp.dot(
        row_band_ref[...], patch, preferred_element_type=jnp.float32
    ).astype(jnp.bfloat16)
    for k in range(NB):
        window = jnp.concatenate(
            [
                row_ref[k * rows : (k + 1) * rows, b * LANES : (b + 2) * LANES]
                for b in range(blocks)
            ],
            axis=0,
        )
        out = jnp.dot(window, col_band_ref[k], preferred_element_type=jnp.float32)
        conv_ref[k] = out.reshape(blocks, rows, LANES)

    first_col = expo_at * chunk
    xs = [column_positions(first_col, b, width) for b in range(blocks)]

    def fold(x):
        total = x[:8]
        for i in range(8, rows, 8):
            total = total + x[i : i + 8]
        return total

    def moments(at, left, right, count):
        total = [None] * count
        for b in range(blocks):
            term = fold(left(b) * right(b)) if right is not None else fold(left(b))
            for i in range(count):
                total[i] = term if total[i] is None else total[i] + term
                if i < count - 1:
                    term = term * xs[b]
        for i in range(count):
            parts_ref[at + i] = total[i]

    def conv(k):
        return lambda b: conv_ref[k, b]

    def sci(shift):
        return image_blocks(image_refs[shift], expos, shift, chunk)

    blank = jnp.zeros((8, LANES), jnp.float32)
    at = 0
    for j, k in PAIRS:
        moments(at, conv(j), conv(k), 3)
        at += 3
    for k in range(NB):
        moments(at, conv(k), None, 2)
        at += 2
    while at % 8:
        parts_ref[at] = blank
        at += 1
    begin = at
    for shift in range(expos):
        row = at + NU * source(expo_at, shift, expos)
        for k in range(NB):
            moments(row + 2 * k, conv(k), sci(shift), 2)
        moments(row + NU - 1, sci(shift), None, 1)
    at += NU * expos
    weight = jnp.broadcast_to(weight_ref[...] * hits_ref[...].astype(jnp.float32), (8, LANES))
    weight = jnp.where(tile_at == 0, weight, 0.0)
    spot = (
        (lax.broadcasted_iota(jnp.int32, (8, LANES), 0) == 0)
        & (lax.broadcasted_iota(jnp.int32, (8, LANES), 1) == 0)
    )
    for e in range(expos):
        parts_ref[at + e] = jnp.where(spot & (expo_at == e), weight, 0.0)
    at += expos
    while at % 8:
        parts_ref[at] = blank
        at += 1
    ones = jnp.ones((8, LANES), jnp.float32)
    rows_of = []
    for first, last in ((0, begin), (begin, at)):
        lanes = jnp.sum(parts_ref[first:last], axis=1)
        spare = LANES - (last - first)
        if spare:
            lanes = jnp.concatenate([lanes, jnp.zeros((spare, LANES), jnp.float32)], axis=0)
        rows_of.append(
            lax.dot_general(
                ones,
                lanes,
                (((1,), (1,)), ((), ())),
                precision=lax.Precision.HIGHEST,
                preferred_element_type=jnp.float32,
            )
        )
    both = jnp.where(lax.broadcasted_iota(jnp.int32, (8, LANES), 0) < 4, rows_of[0], rows_of[1])
    for i in range(sums_ref.shape[0]):
        sums_ref[i] = both


def table(expos):
    columns = np.zeros((NU + expos + 1, 16), np.int32)
    for at, (j, k) in enumerate(PAIRS):
        for a, b in ((j, k), (k, j)):
            columns[b, a] = 3 * at
            columns[NB + b, a] = columns[b, NB + a] = 3 * at + 1
            columns[NB + b, NB + a] = 3 * at + 2
    for k in range(NB):
        for x in range(2):
            columns[NU - 1, x * NB + k] = columns[x * NB + k, NU - 1] = 3 * len(PAIRS) + 2 * k + x
    for e in range(expos):
        columns[NU + e, :NU] = [NU * e + 2 * k + x for x in range(2) for k in range(NB)] + [NU * e + NU - 1]
        columns[NU + expos, e] = NU * expos + e
    return np.ascontiguousarray(np.broadcast_to(columns[:, :, None], columns.shape + (LANES,)))


def solve_kernel(table_ref, sums_ref, conv_ref, *refs, width, pixels):
    *image_refs, coadd_ref, coeffs_ref, tile_ref, sems = refs
    expo_at = lax.axis_index("expo")
    expos = len(image_refs)
    rows, chunk = coadd_ref.shape
    blocks = chunk // LANES
    images = [image_blocks(ref, expos, shift, chunk) for shift, ref in enumerate(image_refs)]
    sub = lax.broadcasted_iota(jnp.int32, (16, LANES), 0)
    lane = lax.broadcasted_iota(jnp.int32, (16, LANES), 1)
    sums = sums_ref[0]
    for i in range(1, sums_ref.shape[0]):
        sums = sums + sums_ref[i]
    first = jnp.broadcast_to(sums[0:1], (16, LANES))
    second = jnp.broadcast_to(sums[4:5], (16, LANES))

    columns = [
        jnp.take_along_axis(first if j < NU else second, table_ref[j], axis=1) for j in range(NU + expos)
    ]
    spread = jnp.take_along_axis(second, table_ref[NU + expos], axis=1)
    weight = [jnp.broadcast_to(spread[e : e + 1], (16, LANES)) for e in range(expos)]
    columns[NU - 1] = jnp.where(sub == NU - 1, float(pixels), columns[NU - 1])

    trace = columns[0][0:1]
    for j in range(1, NU):
        trace = trace + columns[j][j : j + 1]
    scale = 1.0 / trace
    for j in range(NU + expos):
        columns[j] = columns[j] * scale
        if j < NU:
            columns[j] = columns[j] + jnp.where(sub == j, RIDGE / NU, 0.0)
    for i in range(NU):
        inverse = 1.0 / columns[i][i : i + 1]
        for j in range(i + 1, NU + expos):
            factor = columns[j][i : i + 1] * inverse
            columns[j] = jnp.where(sub == i, factor, columns[j] - columns[i] * factor)

    solved = columns[NU:]
    own = solved[0]
    mixed = weight[0] * solved[0]
    for e in range(1, expos):
        own = jnp.where(expo_at == e, solved[e], own)
        mixed = mixed + weight[e] * solved[e]
    diagonal = (sub == lane) & (sub < NU)
    coeffs_ref[...] = jnp.sum(jnp.where(diagonal, own, 0.0), axis=0, keepdims=True)[:, :NU]
    scale = [jnp.broadcast_to(mixed[u : u + 1], (8, LANES)) for u in range(NU)]
    gains = []
    for shift in range(expos):
        gain = weight[0][:8]
        for e in range(1, expos):
            gain = jnp.where(source(expo_at, shift, expos) == e, weight[e][:8], gain)
        gains.append(gain)
    first_col = expo_at * chunk
    copies = []
    for r in range(0, rows, 8):
        for b in range(blocks):
            x = column_positions(first_col, b, width)
            total = -scale[NU - 1]
            for gain, image in zip(gains, images):
                total = total + gain * image(b)[r : r + 8]
            model = (scale[0] + scale[NB] * x) * conv_ref[0, b, r : r + 8]
            for k in range(1, NB):
                model = model + (scale[k] + scale[NB + k] * x) * conv_ref[k, b, r : r + 8]
            tile_ref[r : r + 8, b * LANES : (b + 1) * LANES] = total - model
        copies.append(
            pltpu.make_async_copy(tile_ref.at[pl.ds(r, 8)], coadd_ref.at[pl.ds(r, 8)], sems.at[r // 8])
        )
        copies[-1].start()
    for copy in copies:
        copy.wait()


def swaps(first, size):
    pairs = [(i, i + 1) for i in range(first, size - 1, 2)]
    if first and size % 2 == 0:
        pairs.append((0, size - 1))
    return [pair for a, b in pairs for pair in ((a, b), (b, a))]


def tiled_device(template, science, plan, orders, coadd_weight, intersection):
    expos = lax.axis_size("expo")
    tiles = lax.axis_size("tile")
    _, rows, width = template.shape
    steps = science.shape[1]
    chunk = width // expos
    ext = chunk + LANES
    blocks = chunk // LANES
    vmem = pl.BlockSpec(memory_space=pltpu.VMEM)
    small = pltpu.CompilerParams(vmem_limit_bytes=16 * 1024 * 1024)
    hbm = pl.BlockSpec(memory_space=pltpu.HBM)
    coadds = []
    fitted = []
    for step in range(steps):
        apart = sum(not joint(shift, expos) for shift in range(expos))
        *blocks_out, owner, order = pl.pallas_call(
            functools.partial(send_kernel, step=step),
            out_shape=tuple(
                pltpu.VMEM((rows, ext + chunk if joint(shift, expos) else ext), template.dtype)
                for shift in range(expos)
            )
            + (pltpu.VMEM((rows, ext), science.dtype),) * apart
            + (
                jax.ShapeDtypeStruct((rows, LANES), jnp.int32),
                jax.ShapeDtypeStruct((2, NB, 8, LANES), jnp.int32),
            ),
            in_specs=[hbm] * 4,
            out_specs=(vmem,) * (expos + apart + 2),
            scratch_shapes=[
                pltpu.VMEM((rows, width + 2 * LANES), template.dtype),
                pltpu.SMEM(plan.shape, jnp.int32),
                pltpu.SMEM((2, NB), jnp.int32),
                pltpu.SemaphoreType.DMA((expos + 4,)),
            ],
            compiler_params=small,
        )(
            pltpu.with_memory_space_constraint(template[0], pltpu.HBM),
            pltpu.with_memory_space_constraint(science[0, step], pltpu.HBM),
            pltpu.with_memory_space_constraint(plan, pltpu.HBM),
            pltpu.with_memory_space_constraint(orders.T, pltpu.HBM),
        )
        patches, images = [], []
        for shift in range(expos):
            pairs = [(e, target(e, shift, expos)) for e in range(expos)]
            patches.append(lax.ppermute(blocks_out[shift], "expo", pairs) if shift else blocks_out[shift])
        blocks_out = blocks_out[expos:]
        for shift in range(expos):
            pairs = [(e, target(e, shift, expos)) for e in range(expos)]
            images.append(
                patches[shift] if joint(shift, expos) else lax.ppermute(blocks_out.pop(0), "expo", pairs)
            )
        own = pl.pallas_call(
            pick_kernel,
            out_shape=jax.ShapeDtypeStruct((rows, ext), template.dtype),
            in_specs=[vmem] * (1 + expos),
            out_specs=vmem,
            scratch_shapes=[pltpu.VMEM((rows, ext), template.dtype)],
            compiler_params=small,
        )(owner, *(patches[shift] for shift in template_order(expos)))
        row_band, col_band = pl.pallas_call(
            functools.partial(band_kernel, tiles=tiles),
            out_shape=(
                jax.ShapeDtypeStruct((NB * rows, 3 * rows), jnp.bfloat16),
                jax.ShapeDtypeStruct((NB, 2 * LANES, LANES), jnp.bfloat16),
            ),
            in_specs=[vmem, pl.BlockSpec(memory_space=pl.ANY)],
            out_specs=(vmem, vmem),
            compiler_params=small,
            cost_estimate=pl.CostEstimate(flops=4_000_000, bytes_accessed=500_000, transcendentals=200_000),
        )(order, own)
        far = lax.ppermute(own, "tile", swaps(1, tiles))
        near = lax.ppermute(own, "tile", swaps(0, tiles))
        conv, sums = pl.pallas_call(
            functools.partial(fit_kernel, width=width),
            out_shape=(
                jax.ShapeDtypeStruct((NB, blocks, rows, LANES), jnp.float32),
                jax.ShapeDtypeStruct((tiles * expos, 8, LANES), jnp.float32),
            ),
            in_specs=[vmem] * (7 + expos),
            out_specs=(vmem, vmem),
            scratch_shapes=[
                pltpu.VMEM((NB * rows, ext), jnp.bfloat16),
                pltpu.VMEM((80 + 14 * expos + 8, 8, LANES), jnp.float32),
            ],
            compiler_params=small,
        )(
            coadd_weight[:, step : step + 1],
            intersection[:, step : step + 1],
            row_band,
            col_band,
            own,
            near,
            far,
            *images,
        )
        sums = lax.all_to_all(sums, ("expo", "tile"), split_axis=0, concat_axis=0, tiled=True)
        coadd, coeffs = pl.pallas_call(
            functools.partial(solve_kernel, width=width, pixels=tiles * rows * width),
            out_shape=(
                jax.ShapeDtypeStruct((rows, chunk), jnp.float32),
                jax.ShapeDtypeStruct((1, NU), jnp.float32),
            ),
            in_specs=[vmem] * (3 + expos),
            out_specs=(pl.BlockSpec(memory_space=pl.ANY), vmem),
            scratch_shapes=[
                pltpu.VMEM((rows, chunk), jnp.float32),
                pltpu.SemaphoreType.DMA((rows // 8,)),
            ],
            compiler_params=small,
        )(jnp.asarray(table(expos)), sums, conv, *images)
        coadds.append(coadd[None])
        fitted.append(coeffs)
    return (jnp.concatenate(coadds), jnp.stack(fitted, axis=1))


def broadcast(block, axis, holder):
    block = jnp.where(lax.axis_index(axis) == holder, block, jnp.zeros_like(block))
    return lax.psum(block, axis)


def extended(x, sides, width):
    for axis, dim in sides:
        size, length = (lax.axis_size(axis), x.shape[dim])
        up = [(i, (i + 1) % size) for i in range(size - 1)]
        down = [(j, i) for i, j in up]
        last = lax.slice_in_dim(x, length - width, length, axis=dim)
        first = lax.slice_in_dim(x, 0, width, axis=dim)
        before = lax.ppermute(last, axis, up)
        after = lax.ppermute(first, axis, down)
        x = jnp.concatenate([before, x, after], axis=dim)
    return x


def make_filters(orders):
    taps_pos = jnp.arange(2 * HALF + 1).astype(jnp.float32) - HALF
    row_list = []
    col_list = []
    for basis in range(NB):
        sigma = SIGMAS[basis]
        envelope = jnp.exp(-taps_pos * taps_pos / (2.0 * sigma * sigma))
        row_filter = envelope * power_of(taps_pos, orders[basis, 0])
        col_filter = envelope * power_of(taps_pos, orders[basis, 1])
        row_list.append(row_filter / jnp.sqrt(jnp.sum(row_filter * row_filter)))
        col_list.append(col_filter / jnp.sqrt(jnp.sum(col_filter * col_filter)))
    return (jnp.stack(row_list).astype(jnp.bfloat16), jnp.stack(col_list).astype(jnp.bfloat16))


def band_matrix(filters, out_len, in_len):
    offset = jnp.arange(in_len)[None, :] - jnp.arange(out_len)[:, None]
    taps_idx = jnp.arange(2 * HALF + 1)
    picks = (offset[:, :, None] == taps_idx[None, None, :]).astype(jnp.float32)
    band = jnp.einsum("ijt,kt->kij", picks, filters.astype(jnp.float32))
    return band.astype(jnp.bfloat16)


def any_device(template, science, plan, orders, coadd_weight, intersection):
    row_filters, col_filters = make_filters(orders)
    rows = template.shape[1]
    width = template.shape[2]
    blocks_count = width // 128
    steps_count = science.shape[1]
    row_band = band_matrix(row_filters, rows, rows + 2 * HALF)
    col_band = jnp.transpose(band_matrix(col_filters, 128, 128 + 2 * HALF), (0, 2, 1))
    column_pos = 2.0 * (jnp.arange(width).astype(jnp.float32) + 0.5) / width - 1.0
    pieces = []
    fitted = []
    for step in range(steps_count):
        received = broadcast(template[0], "expo", plan[step])
        padded = extended(received, (("tile", 0),), HALF)
        rowconv = jnp.einsum(
            "kij,jw->kiw", row_band, padded, preferred_element_type=jnp.float32
        ).astype(jnp.bfloat16)
        blocks = rowconv.reshape(NB, rows, blocks_count, 128)
        empty_rim = jnp.zeros((NB, rows, 1, HALF), jnp.bfloat16)
        previous = jnp.concatenate([empty_rim, blocks[:, :, :-1, 128 - HALF :]], axis=2)
        following = jnp.concatenate([blocks[:, :, 1:, :HALF], empty_rim], axis=2)
        window = jnp.concatenate([previous, blocks, following], axis=3)
        conv = jnp.einsum("krbj,kjc->krbc", window, col_band, preferred_element_type=jnp.float32)
        conv = conv.reshape(NB, rows, width)
        fields = jnp.concatenate(
            [conv, conv * column_pos, jnp.ones((1, rows, width), jnp.float32)], axis=0
        )
        fields = fields.reshape(NU, rows * width)
        exposure_image = science[0, step].astype(jnp.float32).reshape(rows * width)
        normal_local = jnp.dot(fields, fields.T, precision=lax.Precision.HIGHEST)
        project_local = jnp.dot(fields, exposure_image, precision=lax.Precision.HIGHEST)
        normal_matrix, projections = lax.psum((normal_local, project_local), "tile")
        normal_matrix = normal_matrix + RIDGE * (jnp.trace(normal_matrix) / NU) * jnp.eye(
            NU, dtype=jnp.float32
        )
        factor = jnp.linalg.cholesky(normal_matrix)
        coeffs = jax.scipy.linalg.cho_solve((factor, True), projections)
        model = jnp.dot(coeffs, fields, precision=lax.Precision.HIGHEST)
        difference = exposure_image - model
        weight_now = coadd_weight[0, step] * intersection[0, step].astype(jnp.float32)
        pieces.append((weight_now * difference).reshape(rows, width))
        fitted.append(coeffs)
    weighted = jnp.stack(pieces)
    received_parts = lax.all_to_all(weighted[None], "expo", split_axis=3, concat_axis=0, tiled=True)
    coadd = jnp.sum(received_parts, axis=0)
    return (coadd, jnp.stack(fitted)[None])


def per_device(template, science, plan, orders, coadd_weight, intersection):
    expos = lax.axis_size("expo")
    rows, width = template.shape[1:]
    whole_lanes = width % (expos * LANES) == 0 and rows % 16 == 0 and 3 * rows <= LANES
    few = (NU + 1) * expos <= LANES and NU + expos <= LANES
    body = tiled_device if whole_lanes and few else any_device
    return body(template, science, plan, orders, coadd_weight, intersection)


def solution(mesh):
    return jax.shard_map(
        per_device,
        mesh=mesh,
        in_specs=(
            P(("groups", "expo"), "tile", None),
            P(("groups", "expo"), None, "tile", None),
            P("groups"),
            P(),
            P(("groups", "expo"), None),
            P(("groups", "expo"), None),
        ),
        out_specs=(P("groups", "tile", "expo"), P(("groups", "expo"), None, None)),
        check_vma=False,
    )
```

```python
import functools

import jax
import jax.numpy as jnp
import numpy as np
from jax import lax
from jax.experimental import pallas as pl
from jax.experimental.pallas import tpu as pltpu
from jax.sharding import PartitionSpec as P

HALF = 15
NB = 6
NU = 13
LANES = 128
BEYOND = 1000
STAGE_COST = 700_000_000
PAIRS = [(j, k) for j in range(NB) for k in range(j, NB)]

SIGMAS = (0.8, 1.4, 2.2, 3.0, 4.0, 5.5)
RIDGE = 0.05


def power_of(pos, order):
    return jnp.where(order == 0, 1.0, jnp.where(order == 1, pos, pos * pos))


def tap_values(pos, sigma, order):
    value = jnp.exp(-pos * pos / (2.0 * sigma * sigma)) * power_of(pos, order)
    return jnp.where(jnp.abs(pos) <= HALF, value, 0.0)


def tap_norm(sigma, order):
    pos = lax.broadcasted_iota(jnp.int32, (8, LANES), 1).astype(jnp.float32) - HALF
    value = tap_values(pos, sigma, order)
    return jnp.sqrt(jnp.sum(value * value, axis=1, keepdims=True))


def target(me, shift, size):
    return me ^ shift if size & (size - 1) == 0 else (me + shift) % size


def source(me, shift, size):
    return me ^ shift if size & (size - 1) == 0 else (me - shift + size) % size


def far_first(size):
    return [*range(size - 1, 0, -1), 0]


def joint(shift, size):
    return shift < size // 2


def send_kernel(template_ref, science_ref, plan_ref, orders_ref, *refs, step):
    *out_refs, owner_ref, order_ref, patch_ref, plan_now, orders_now, sems = refs
    size = sems.shape[0] - 4
    rows, width = science_ref.shape
    chunk = width // size
    ext = chunk + LANES
    patch_refs, image_refs = out_refs[:size], out_refs[size:]
    half = size * chunk // 2
    me = lax.axis_index("expo")
    starts = [pl.multiple_of(target(me, shift, size) * chunk, chunk) for shift in range(size)]
    loads = [
        pltpu.make_async_copy(
            template_ref.at[:, pl.ds(i * half, half)], patch_ref.at[:, pl.ds((i * half + LANES), half)], sems.at[i]
        )
        for i in range(2)
    ]
    copies = [
        pltpu.make_async_copy(
            science_ref.at[:, pl.ds(starts[shift], chunk)],
            patch_refs[shift].at[:, pl.ds(ext, chunk)]
            if joint(shift, size)
            else image_refs[shift - size // 2].at[:, pl.ds(0, chunk)],
            sems.at[3 + shift],
        )
        for shift in range(size)
    ]
    copies.append(pltpu.make_async_copy(plan_ref, plan_now, sems.at[2]))
    copies.append(pltpu.make_async_copy(orders_ref, orders_now, sems.at[3 + size]))
    for copy in loads + copies:
        copy.start()
    blank = jnp.zeros((rows, LANES), patch_ref.dtype)
    patch_ref[:, :LANES] = blank
    patch_ref[:, size * chunk + LANES :] = blank
    for image_ref in image_refs:
        image_ref[:, chunk:] = blank
    for copy in loads:
        copy.wait()
    lane = lax.broadcasted_iota(jnp.int32, (rows, LANES), 1)
    for shift in range(size):
        start = starts[shift]
        patch_refs[shift][:, :chunk] = patch_ref[:, pl.ds(start + LANES, chunk)]
        before = patch_ref[:, pl.ds(start, LANES)].astype(jnp.float32)
        after = patch_ref[:, pl.ds(start + chunk + LANES, LANES)].astype(jnp.float32)
        rim = jnp.where(lane < LANES // 2, after, before)
        patch_refs[shift][:, chunk:ext] = rim.astype(patch_ref.dtype)
    for copy in copies:
        copy.wait()
    owner_ref[...] = jnp.full(owner_ref.shape, plan_now[step], jnp.int32)
    for way in range(2):
        for k in range(NB):
            order_ref[way, k] = jnp.full((8, LANES), orders_now[way, k], jnp.int32)


def choose_kernel(owner_ref, *refs, shifts, size):
    *recv_refs, out_ref = refs
    me = lax.axis_index("expo")
    for b in range(out_ref.shape[1] // LANES):
        columns = slice(b * LANES, (b + 1) * LANES)
        block = recv_refs[0][:, columns].astype(jnp.float32)
        for shift, ref in zip(shifts, recv_refs[1:]):
            block = jnp.where(
                owner_ref[...] == source(me, shift, size), ref[:, columns].astype(jnp.float32), block
            )
        out_ref[:, columns] = block.astype(out_ref.dtype)


def pick_kernel(owner_ref, *refs, shifts, size):
    *recv_refs, out_ref, block_ref = refs
    ext = out_ref.shape[1]
    choose_kernel(owner_ref, *recv_refs, block_ref, shifts=shifts, size=size)
    whole = jnp.concatenate([block_ref[:, ext - LANES :], block_ref[...]], axis=1)
    out_ref[...] = whole[:, LANES - HALF : LANES - HALF + ext]


def column_positions(first_col, block, width):
    col = lax.broadcasted_iota(jnp.int32, (8, LANES), 1) + (first_col + block * LANES)
    return 2.0 * (col.astype(jnp.float32) + 0.5) / width - 1.0


def band_kernel(order_ref, _, row_ref, col_ref, *, tiles):
    rows = row_ref.shape[0] // NB
    tile_at = lax.axis_index("tile")
    near = 1 - 2 * lax.rem(tile_at, 2)
    near_move = jnp.where(tile_at + near < tiles, near - 1, BEYOND)
    far_move = jnp.where((tile_at >= near) & (tile_at - near < tiles), -near - 2, BEYOND)
    row_from = lax.broadcasted_iota(jnp.int32, (8, LANES), 1)
    moved = jnp.where(row_from < rows, 0, jnp.where(row_from < 2 * rows, near_move, far_move))
    sub = lax.broadcasted_iota(jnp.int32, (8, LANES), 0)
    lane = lax.broadcasted_iota(jnp.int32, (8, LANES), 1)
    shift = (sub - jnp.where(lane < LANES // 2, lane, lane - LANES) - HALF).astype(jnp.float32)
    for k in range(NB):
        norm = tap_norm(SIGMAS[k], order_ref[0, k])
        for r in range(0, rows, 16):
            parts = []
            for half in (r, r + 8):
                offset = (row_from + moved * rows - sub - half).astype(jnp.float32)
                parts.append(tap_values(offset, SIGMAS[k], order_ref[0, k]) / norm)
            both = jnp.concatenate(parts, axis=0).astype(jnp.bfloat16)
            row_ref[k * rows + r : k * rows + r + 16] = both[:, : 3 * rows]
        norm = tap_norm(SIGMAS[k], order_ref[1, k])
        pattern = tap_values(shift, SIGMAS[k], order_ref[1, k]) / norm
        for r in range(0, 2 * LANES, 16):
            parts = []
            for half in (r, r + 8):
                moved_on = pltpu.roll(pattern, half % LANES, 1) if half % LANES else pattern
                inside = lane <= half + 7 if half < LANES else lane >= half - LANES + LANES // 2
                parts.append(jnp.where(inside, moved_on, 0.0))
            col_ref[k, r : r + 16] = jnp.concatenate(parts, axis=0).astype(jnp.bfloat16)


def image_blocks(ref, size, shift, chunk):
    first = chunk + LANES if joint(shift, size) else 0
    return lambda b: ref[:, first + b * LANES : first + (b + 1) * LANES].astype(jnp.float32)


def fit_kernel(weight_ref, hits_ref, row_band_ref, col_band_ref, own_ref, near_ref, far_ref, *refs, width):
    *image_refs, conv_ref, sums_ref, row_ref, parts_ref = refs
    image_refs = dict(zip(far_first(len(image_refs)), image_refs))
    tile_at = lax.axis_index("tile")
    expo_at = lax.axis_index("expo")
    rows, ext = own_ref.shape
    expos = len(image_refs)
    chunk = ext - LANES
    blocks = chunk // LANES

    patch = jnp.concatenate([own_ref[...], near_ref[...], far_ref[...]], axis=0)
    row_ref[...] = jnp.dot(
        row_band_ref[...], patch, preferred_element_type=jnp.float32
    ).astype(jnp.bfloat16)
    for k in range(NB):
        window = jnp.concatenate(
            [
                row_ref[k * rows : (k + 1) * rows, b * LANES : (b + 2) * LANES]
                for b in range(blocks)
            ],
            axis=0,
        )
        out = jnp.dot(window, col_band_ref[k], preferred_element_type=jnp.float32)
        conv_ref[k] = out.reshape(blocks, rows, LANES)

    first_col = expo_at * chunk
    xs = [column_positions(first_col, b, width) for b in range(blocks)]

    def fold(x):
        total = x[:8]
        for i in range(8, rows, 8):
            total = total + x[i : i + 8]
        return total

    def moments(at, left, right, count):
        total = [None] * count
        for b in range(blocks):
            term = fold(left(b) * right(b)) if right is not None else fold(left(b))
            for i in range(count):
                total[i] = term if total[i] is None else total[i] + term
                if i < count - 1:
                    term = term * xs[b]
        for i in range(count):
            parts_ref[at + i] = total[i]

    def conv(k):
        return lambda b: conv_ref[k, b]

    def sci(shift):
        return image_blocks(image_refs[shift], expos, shift, chunk)

    blank = jnp.zeros((8, LANES), jnp.float32)
    at = 0
    for j, k in PAIRS:
        moments(at, conv(j), conv(k), 3)
        at += 3
    for k in range(NB):
        moments(at, conv(k), None, 2)
        at += 2
    while at % 8:
        parts_ref[at] = blank
        at += 1
    begin = at
    for shift in range(expos):
        row = at + NU * source(expo_at, shift, expos)
        for k in range(NB):
            moments(row + 2 * k, conv(k), sci(shift), 2)
        moments(row + NU - 1, sci(shift), None, 1)
    at += NU * expos
    weight = jnp.broadcast_to(weight_ref[...] * hits_ref[...].astype(jnp.float32), (8, LANES))
    weight = jnp.where(tile_at == 0, weight, 0.0)
    spot = (
        (lax.broadcasted_iota(jnp.int32, (8, LANES), 0) == 0)
        & (lax.broadcasted_iota(jnp.int32, (8, LANES), 1) == 0)
    )
    for e in range(expos):
        parts_ref[at + e] = jnp.where(spot & (expo_at == e), weight, 0.0)
    at += expos
    while at % 8:
        parts_ref[at] = blank
        at += 1
    ones = jnp.ones((8, LANES), jnp.float32)
    rows_of = []
    for first, last in ((0, begin), (begin, at)):
        lanes = jnp.sum(parts_ref[first:last], axis=1)
        spare = LANES - (last - first)
        if spare:
            lanes = jnp.concatenate([lanes, jnp.zeros((spare, LANES), jnp.float32)], axis=0)
        rows_of.append(
            lax.dot_general(
                ones,
                lanes,
                (((1,), (1,)), ((), ())),
                precision=lax.Precision.HIGHEST,
                preferred_element_type=jnp.float32,
            )
        )
    both = jnp.where(lax.broadcasted_iota(jnp.int32, (8, LANES), 0) < 4, rows_of[0], rows_of[1])
    for i in range(sums_ref.shape[0]):
        sums_ref[i] = both


def table(expos):
    columns = np.zeros((NU + expos + 1, 16), np.int32)
    for at, (j, k) in enumerate(PAIRS):
        for a, b in ((j, k), (k, j)):
            columns[b, a] = 3 * at
            columns[NB + b, a] = columns[b, NB + a] = 3 * at + 1
            columns[NB + b, NB + a] = 3 * at + 2
    for k in range(NB):
        for x in range(2):
            columns[NU - 1, x * NB + k] = columns[x * NB + k, NU - 1] = 3 * len(PAIRS) + 2 * k + x
    for e in range(expos):
        columns[NU + e, :NU] = [NU * e + 2 * k + x for x in range(2) for k in range(NB)] + [NU * e + NU - 1]
        columns[NU + expos, e] = NU * expos + e
    return np.ascontiguousarray(np.broadcast_to(columns[:, :, None], columns.shape + (LANES,)))


def solve_kernel(table_ref, sums_ref, conv_ref, *refs, width, pixels):
    *image_refs, coadd_ref, coeffs_ref, tile_ref, sems = refs
    expo_at = lax.axis_index("expo")
    expos = len(image_refs)
    rows, chunk = coadd_ref.shape
    blocks = chunk // LANES
    images = [image_blocks(ref, expos, shift, chunk) for shift, ref in enumerate(image_refs)]
    sub = lax.broadcasted_iota(jnp.int32, (16, LANES), 0)
    lane = lax.broadcasted_iota(jnp.int32, (16, LANES), 1)
    sums = sums_ref[0]
    for i in range(1, sums_ref.shape[0]):
        sums = sums + sums_ref[i]
    first = jnp.broadcast_to(sums[0:1], (16, LANES))
    second = jnp.broadcast_to(sums[4:5], (16, LANES))

    columns = [
        jnp.take_along_axis(first if j < NU else second, table_ref[j], axis=1) for j in range(NU + expos)
    ]
    spread = jnp.take_along_axis(second, table_ref[NU + expos], axis=1)
    weight = [jnp.broadcast_to(spread[e : e + 1], (16, LANES)) for e in range(expos)]
    columns[NU - 1] = jnp.where(sub == NU - 1, float(pixels), columns[NU - 1])

    trace = columns[0][0:1]
    for j in range(1, NU):
        trace = trace + columns[j][j : j + 1]
    scale = 1.0 / trace
    for j in range(NU + expos):
        columns[j] = columns[j] * scale
        if j < NU:
            columns[j] = columns[j] + jnp.where(sub == j, RIDGE / NU, 0.0)
    for i in range(NU):
        inverse = 1.0 / columns[i][i : i + 1]
        for j in range(i + 1, NU + expos):
            factor = columns[j][i : i + 1] * inverse
            columns[j] = jnp.where(sub == i, factor, columns[j] - columns[i] * factor)

    solved = columns[NU:]
    own = solved[0]
    mixed = weight[0] * solved[0]
    for e in range(1, expos):
        own = jnp.where(expo_at == e, solved[e], own)
        mixed = mixed + weight[e] * solved[e]
    diagonal = (sub == lane) & (sub < NU)
    coeffs_ref[...] = jnp.sum(jnp.where(diagonal, own, 0.0), axis=0, keepdims=True)[:, :NU]
    scale = [jnp.broadcast_to(mixed[u : u + 1], (8, LANES)) for u in range(NU)]
    gains = []
    for shift in range(expos):
        gain = weight[0][:8]
        for e in range(1, expos):
            gain = jnp.where(source(expo_at, shift, expos) == e, weight[e][:8], gain)
        gains.append(gain)
    first_col = expo_at * chunk
    copies = []
    for r in range(0, rows, 8):
        for b in range(blocks):
            x = column_positions(first_col, b, width)
            total = -scale[NU - 1]
            for gain, image in zip(gains, images):
                total = total + gain * image(b)[r : r + 8]
            model = (scale[0] + scale[NB] * x) * conv_ref[0, b, r : r + 8]
            for k in range(1, NB):
                model = model + (scale[k] + scale[NB + k] * x) * conv_ref[k, b, r : r + 8]
            tile_ref[r : r + 8, b * LANES : (b + 1) * LANES] = total - model
        copies.append(
            pltpu.make_async_copy(tile_ref.at[pl.ds(r, 8)], coadd_ref.at[pl.ds(r, 8)], sems.at[r // 8])
        )
        copies[-1].start()
    for copy in copies:
        copy.wait()


def swaps(first, size):
    pairs = [(i, i + 1) for i in range(first, size - 1, 2)]
    if first and size % 2 == 0:
        pairs.append((0, size - 1))
    return [pair for a, b in pairs for pair in ((a, b), (b, a))]


def tiled_device(template, science, plan, orders, coadd_weight, intersection):
    expos = lax.axis_size("expo")
    tiles = lax.axis_size("tile")
    _, rows, width = template.shape
    steps = science.shape[1]
    chunk = width // expos
    ext = chunk + LANES
    blocks = chunk // LANES
    vmem = pl.BlockSpec(memory_space=pltpu.VMEM)
    small = pltpu.CompilerParams(vmem_limit_bytes=16 * 1024 * 1024)
    hbm = pl.BlockSpec(memory_space=pltpu.HBM)
    coadds = []
    fitted = []
    for step in range(steps):
        *blocks_out, owner, order = pl.pallas_call(
            functools.partial(send_kernel, step=step),
            out_shape=tuple(
                pltpu.VMEM((rows, ext + chunk if joint(shift, expos) else ext), template.dtype)
                for shift in range(expos)
            )
            + (pltpu.VMEM((rows, ext), science.dtype),) * (expos - expos // 2)
            + (
                jax.ShapeDtypeStruct((rows, LANES), jnp.int32),
                jax.ShapeDtypeStruct((2, NB, 8, LANES), jnp.int32),
            ),
            in_specs=[hbm] * 4,
            out_specs=(vmem,) * (2 * expos - expos // 2 + 2),
            scratch_shapes=[
                pltpu.VMEM((rows, width + 2 * LANES), template.dtype),
                pltpu.SMEM(plan.shape, jnp.int32),
                pltpu.SMEM((2, NB), jnp.int32),
                pltpu.SemaphoreType.DMA((expos + 4,)),
            ],
            compiler_params=small,
        )(
            pltpu.with_memory_space_constraint(template[0], pltpu.HBM),
            pltpu.with_memory_space_constraint(science[0, step], pltpu.HBM),
            pltpu.with_memory_space_constraint(plan, pltpu.HBM),
            pltpu.with_memory_space_constraint(orders.T, pltpu.HBM),
        )
        patches, images = blocks_out[:expos], blocks_out[expos:]
        for group, first in ((patches, 0), (images, expos // 2)):
            for shift in range(max(first, 1), expos):
                pairs = [(e, int(target(e, shift, expos))) for e in range(expos)]
                group[shift - first] = lax.ppermute(group[shift - first], "expo", pairs)
        images = patches[: expos // 2] + images
        across = [shift for shift in far_first(expos)[:-1] if not joint(shift, expos)]
        beside = [shift for shift in far_first(expos)[:-1] if joint(shift, expos)]
        block = pl.pallas_call(
            functools.partial(choose_kernel, shifts=across, size=expos),
            out_shape=jax.ShapeDtypeStruct((rows, ext), template.dtype),
            in_specs=[vmem] * (2 + len(across)),
            out_specs=vmem,
            compiler_params=small,
            cost_estimate=pl.CostEstimate(flops=STAGE_COST, bytes_accessed=500_000, transcendentals=0),
        )(owner, patches[0], *(patches[shift] for shift in across))
        own = pl.pallas_call(
            functools.partial(pick_kernel, shifts=beside, size=expos),
            out_shape=jax.ShapeDtypeStruct((rows, ext), template.dtype),
            in_specs=[vmem] * (2 + len(beside)),
            out_specs=vmem,
            scratch_shapes=[pltpu.VMEM((rows, ext), template.dtype)],
            compiler_params=small,
        )(owner, block, *(patches[shift] for shift in beside))
        row_band, col_band = pl.pallas_call(
            functools.partial(band_kernel, tiles=tiles),
            out_shape=(
                jax.ShapeDtypeStruct((NB * rows, 3 * rows), jnp.bfloat16),
                jax.ShapeDtypeStruct((NB, 2 * LANES, LANES), jnp.bfloat16),
            ),
            in_specs=[vmem, pl.BlockSpec(memory_space=pl.ANY)],
            out_specs=(vmem, vmem),
            compiler_params=small,
            cost_estimate=pl.CostEstimate(flops=4_000_000, bytes_accessed=500_000, transcendentals=200_000),
        )(order, own)
        far = lax.ppermute(own, "tile", swaps(1, tiles))
        near = lax.ppermute(own, "tile", swaps(0, tiles))
        conv, sums = pl.pallas_call(
            functools.partial(fit_kernel, width=width),
            out_shape=(
                jax.ShapeDtypeStruct((NB, blocks, rows, LANES), jnp.float32),
                jax.ShapeDtypeStruct((tiles * expos, 8, LANES), jnp.float32),
            ),
            in_specs=[vmem] * (7 + expos),
            out_specs=(vmem, vmem),
            scratch_shapes=[
                pltpu.VMEM((NB * rows, ext), jnp.bfloat16),
                pltpu.VMEM((80 + 14 * expos + 8, 8, LANES), jnp.float32),
            ],
            compiler_params=small,
        )(
            coadd_weight[:, step : step + 1],
            intersection[:, step : step + 1],
            row_band,
            col_band,
            own,
            near,
            far,
            *(images[shift] for shift in far_first(expos)),
        )
        sums = lax.all_to_all(sums, ("expo", "tile"), split_axis=0, concat_axis=0, tiled=True)
        coadd, coeffs = pl.pallas_call(
            functools.partial(solve_kernel, width=width, pixels=tiles * rows * width),
            out_shape=(
                jax.ShapeDtypeStruct((rows, chunk), jnp.float32),
                jax.ShapeDtypeStruct((1, NU), jnp.float32),
            ),
            in_specs=[vmem] * (3 + expos),
            out_specs=(pl.BlockSpec(memory_space=pl.ANY), vmem),
            scratch_shapes=[
                pltpu.VMEM((rows, chunk), jnp.float32),
                pltpu.SemaphoreType.DMA((rows // 8,)),
            ],
            compiler_params=small,
        )(jnp.asarray(table(expos)), sums, conv, *images)
        coadds.append(coadd[None])
        fitted.append(coeffs)
    return (jnp.concatenate(coadds), jnp.stack(fitted, axis=1))


def broadcast(block, axis, holder):
    block = jnp.where(lax.axis_index(axis) == holder, block, jnp.zeros_like(block))
    return lax.psum(block, axis)


def extended(x, sides, width):
    for axis, dim in sides:
        size, length = (lax.axis_size(axis), x.shape[dim])
        up = [(i, (i + 1) % size) for i in range(size - 1)]
        down = [(j, i) for i, j in up]
        last = lax.slice_in_dim(x, length - width, length, axis=dim)
        first = lax.slice_in_dim(x, 0, width, axis=dim)
        before = lax.ppermute(last, axis, up)
        after = lax.ppermute(first, axis, down)
        x = jnp.concatenate([before, x, after], axis=dim)
    return x


def make_filters(orders):
    taps_pos = jnp.arange(2 * HALF + 1).astype(jnp.float32) - HALF
    row_list = []
    col_list = []
    for basis in range(NB):
        sigma = SIGMAS[basis]
        envelope = jnp.exp(-taps_pos * taps_pos / (2.0 * sigma * sigma))
        row_filter = envelope * power_of(taps_pos, orders[basis, 0])
        col_filter = envelope * power_of(taps_pos, orders[basis, 1])
        row_list.append(row_filter / jnp.sqrt(jnp.sum(row_filter * row_filter)))
        col_list.append(col_filter / jnp.sqrt(jnp.sum(col_filter * col_filter)))
    return (jnp.stack(row_list).astype(jnp.bfloat16), jnp.stack(col_list).astype(jnp.bfloat16))


def band_matrix(filters, out_len, in_len):
    offset = jnp.arange(in_len)[None, :] - jnp.arange(out_len)[:, None]
    taps_idx = jnp.arange(2 * HALF + 1)
    picks = (offset[:, :, None] == taps_idx[None, None, :]).astype(jnp.float32)
    band = jnp.einsum("ijt,kt->kij", picks, filters.astype(jnp.float32))
    return band.astype(jnp.bfloat16)


def any_device(template, science, plan, orders, coadd_weight, intersection):
    row_filters, col_filters = make_filters(orders)
    rows = template.shape[1]
    width = template.shape[2]
    blocks_count = width // 128
    steps_count = science.shape[1]
    row_band = band_matrix(row_filters, rows, rows + 2 * HALF)
    col_band = jnp.transpose(band_matrix(col_filters, 128, 128 + 2 * HALF), (0, 2, 1))
    column_pos = 2.0 * (jnp.arange(width).astype(jnp.float32) + 0.5) / width - 1.0
    pieces = []
    fitted = []
    for step in range(steps_count):
        received = broadcast(template[0], "expo", plan[step])
        padded = extended(received, (("tile", 0),), HALF)
        rowconv = jnp.einsum(
            "kij,jw->kiw", row_band, padded, preferred_element_type=jnp.float32
        ).astype(jnp.bfloat16)
        blocks = rowconv.reshape(NB, rows, blocks_count, 128)
        empty_rim = jnp.zeros((NB, rows, 1, HALF), jnp.bfloat16)
        previous = jnp.concatenate([empty_rim, blocks[:, :, :-1, 128 - HALF :]], axis=2)
        following = jnp.concatenate([blocks[:, :, 1:, :HALF], empty_rim], axis=2)
        window = jnp.concatenate([previous, blocks, following], axis=3)
        conv = jnp.einsum("krbj,kjc->krbc", window, col_band, preferred_element_type=jnp.float32)
        conv = conv.reshape(NB, rows, width)
        fields = jnp.concatenate(
            [conv, conv * column_pos, jnp.ones((1, rows, width), jnp.float32)], axis=0
        )
        fields = fields.reshape(NU, rows * width)
        exposure_image = science[0, step].astype(jnp.float32).reshape(rows * width)
        normal_local = jnp.dot(fields, fields.T, precision=lax.Precision.HIGHEST)
        project_local = jnp.dot(fields, exposure_image, precision=lax.Precision.HIGHEST)
        normal_matrix, projections = lax.psum((normal_local, project_local), "tile")
        normal_matrix = normal_matrix + RIDGE * (jnp.trace(normal_matrix) / NU) * jnp.eye(
            NU, dtype=jnp.float32
        )
        factor = jnp.linalg.cholesky(normal_matrix)
        coeffs = jax.scipy.linalg.cho_solve((factor, True), projections)
        model = jnp.dot(coeffs, fields, precision=lax.Precision.HIGHEST)
        difference = exposure_image - model
        weight_now = coadd_weight[0, step] * intersection[0, step].astype(jnp.float32)
        pieces.append((weight_now * difference).reshape(rows, width))
        fitted.append(coeffs)
    weighted = jnp.stack(pieces)
    received_parts = lax.all_to_all(weighted[None], "expo", split_axis=3, concat_axis=0, tiled=True)
    coadd = jnp.sum(received_parts, axis=0)
    return (coadd, jnp.stack(fitted)[None])


def per_device(template, science, plan, orders, coadd_weight, intersection):
    expos = lax.axis_size("expo")
    rows, width = template.shape[1:]
    whole_lanes = width % (expos * LANES) == 0 and rows % 16 == 0 and 3 * rows <= LANES
    few = (NU + 1) * expos <= LANES and NU + expos <= LANES
    body = tiled_device if whole_lanes and few else any_device
    return body(template, science, plan, orders, coadd_weight, intersection)


def solution(mesh):
    return jax.shard_map(
        per_device,
        mesh=mesh,
        in_specs=(
            P(("groups", "expo"), "tile", None),
            P(("groups", "expo"), None, "tile", None),
            P("groups"),
            P(),
            P(("groups", "expo"), None),
            P(("groups", "expo"), None),
        ),
        out_specs=(P("groups", "tile", "expo"), P(("groups", "expo"), None, None)),
        check_vma=False,
    )
```

```python
import functools

import jax
import jax.numpy as jnp
import numpy as np
from jax import lax
from jax.experimental import pallas as pl
from jax.experimental.pallas import tpu as pltpu
from jax.sharding import PartitionSpec as P

HALF = 15
NB = 6
NU = 13
LANES = 128
BEYOND = 1000
STAGE_COST = 700_000_000
PAIRS = [(j, k) for j in range(NB) for k in range(j, NB)]

SIGMAS = (0.8, 1.4, 2.2, 3.0, 4.0, 5.5)
RIDGE = 0.05


def power_of(pos, order):
    return jnp.where(order == 0, 1.0, jnp.where(order == 1, pos, pos * pos))


def tap_values(pos, sigma, order):
    value = jnp.exp(-pos * pos / (2.0 * sigma * sigma)) * power_of(pos, order)
    return jnp.where(jnp.abs(pos) <= HALF, value, 0.0)


def tap_norm(sigma, order):
    pos = lax.broadcasted_iota(jnp.int32, (8, LANES), 1).astype(jnp.float32) - HALF
    value = tap_values(pos, sigma, order)
    return jnp.sqrt(jnp.sum(value * value, axis=1, keepdims=True))


def target(me, shift, size):
    return me ^ shift if size & (size - 1) == 0 else (me + shift) % size


def source(me, shift, size):
    return me ^ shift if size & (size - 1) == 0 else (me - shift + size) % size


def far_first(size):
    return [*range(size - 1, 0, -1), 0]


def joint(shift, size):
    return shift < size // 2


def send_kernel(template_ref, science_ref, plan_ref, orders_ref, *refs, step):
    *out_refs, owner_ref, order_ref, patch_ref, plan_now, orders_now, sems = refs
    size = sems.shape[0] - 4
    rows, width = science_ref.shape
    chunk = width // size
    ext = chunk + LANES
    patch_refs, image_refs = out_refs[:size], out_refs[size:]
    half = size * chunk // 2
    me = lax.axis_index("expo")
    starts = [pl.multiple_of(target(me, shift, size) * chunk, chunk) for shift in range(size)]
    loads = [
        pltpu.make_async_copy(
            template_ref.at[:, pl.ds(i * half, half)], patch_ref.at[:, pl.ds((i * half + LANES), half)], sems.at[i]
        )
        for i in range(2)
    ]
    copies = [
        pltpu.make_async_copy(
            science_ref.at[:, pl.ds(starts[shift], chunk)],
            patch_refs[shift].at[:, pl.ds(ext, chunk)]
            if joint(shift, size)
            else image_refs[shift - size // 2].at[:, pl.ds(0, chunk)],
            sems.at[3 + shift],
        )
        for shift in range(size)
    ]
    copies.append(pltpu.make_async_copy(plan_ref, plan_now, sems.at[2]))
    copies.append(pltpu.make_async_copy(orders_ref, orders_now, sems.at[3 + size]))
    for copy in loads + copies:
        copy.start()
    blank = jnp.zeros((rows, LANES), patch_ref.dtype)
    patch_ref[:, :LANES] = blank
    patch_ref[:, size * chunk + LANES :] = blank
    for image_ref in image_refs:
        image_ref[:, chunk:] = blank
    for copy in loads:
        copy.wait()
    lane = lax.broadcasted_iota(jnp.int32, (rows, LANES), 1)
    for shift in range(size):
        start = starts[shift]
        patch_refs[shift][:, :chunk] = patch_ref[:, pl.ds(start + LANES, chunk)]
        before = patch_ref[:, pl.ds(start, LANES)].astype(jnp.float32)
        after = patch_ref[:, pl.ds(start + chunk + LANES, LANES)].astype(jnp.float32)
        rim = jnp.where(lane < LANES // 2, after, before)
        patch_refs[shift][:, chunk:ext] = rim.astype(patch_ref.dtype)
    for copy in copies:
        copy.wait()
    owner_ref[...] = jnp.full(owner_ref.shape, plan_now[step], jnp.int32)
    for way in range(2):
        for k in range(NB):
            order_ref[way, k] = jnp.full((8, LANES), orders_now[way, k], jnp.int32)


def choose_kernel(owner_ref, *refs, shifts, size):
    *recv_refs, out_ref = refs
    me = lax.axis_index("expo")
    for b in range(out_ref.shape[1] // LANES):
        columns = slice(b * LANES, (b + 1) * LANES)
        block = recv_refs[0][:, columns].astype(jnp.float32)
        for shift, ref in zip(shifts, recv_refs[1:]):
            block = jnp.where(
                owner_ref[...] == source(me, shift, size), ref[:, columns].astype(jnp.float32), block
            )
        out_ref[:, columns] = block.astype(out_ref.dtype)


def pick_kernel(owner_ref, *refs, shifts, size):
    *recv_refs, out_ref, block_ref = refs
    ext = out_ref.shape[1]
    choose_kernel(owner_ref, *recv_refs, block_ref, shifts=shifts, size=size)
    whole = jnp.concatenate([block_ref[:, ext - LANES :], block_ref[...]], axis=1)
    out_ref[...] = whole[:, LANES - HALF : LANES - HALF + ext]


def column_positions(first_col, block, width):
    col = lax.broadcasted_iota(jnp.int32, (8, LANES), 1) + (first_col + block * LANES)
    return 2.0 * (col.astype(jnp.float32) + 0.5) / width - 1.0


def band_kernel(order_ref, _, row_ref, col_ref, *, tiles):
    rows = row_ref.shape[0] // NB
    tile_at = lax.axis_index("tile")
    near = 1 - 2 * lax.rem(tile_at, 2)
    near_move = jnp.where(tile_at + near < tiles, near - 1, BEYOND)
    far_move = jnp.where((tile_at >= near) & (tile_at - near < tiles), -near - 2, BEYOND)
    row_from = lax.broadcasted_iota(jnp.int32, (8, LANES), 1)
    moved = jnp.where(row_from < rows, 0, jnp.where(row_from < 2 * rows, near_move, far_move))
    sub = lax.broadcasted_iota(jnp.int32, (8, LANES), 0)
    lane = lax.broadcasted_iota(jnp.int32, (8, LANES), 1)
    shift = (sub - jnp.where(lane < LANES // 2, lane, lane - LANES) - HALF).astype(jnp.float32)
    for k in range(NB):
        norm = tap_norm(SIGMAS[k], order_ref[0, k])
        for r in range(0, rows, 16):
            parts = []
            for half in (r, r + 8):
                offset = (row_from + moved * rows - sub - half).astype(jnp.float32)
                parts.append(tap_values(offset, SIGMAS[k], order_ref[0, k]) / norm)
            both = jnp.concatenate(parts, axis=0).astype(jnp.bfloat16)
            row_ref[k * rows + r : k * rows + r + 16] = both[:, : 3 * rows]
        norm = tap_norm(SIGMAS[k], order_ref[1, k])
        pattern = tap_values(shift, SIGMAS[k], order_ref[1, k]) / norm
        for r in range(0, 2 * LANES, 16):
            parts = []
            for half in (r, r + 8):
                moved_on = pltpu.roll(pattern, half % LANES, 1) if half % LANES else pattern
                inside = lane <= half + 7 if half < LANES else lane >= half - LANES + LANES // 2
                parts.append(jnp.where(inside, moved_on, 0.0))
            col_ref[k, r : r + 16] = jnp.concatenate(parts, axis=0).astype(jnp.bfloat16)


def image_blocks(ref, size, shift, chunk):
    first = chunk + LANES if joint(shift, size) else 0
    return lambda b: ref[:, first + b * LANES : first + (b + 1) * LANES].astype(jnp.float32)


def fit_kernel(weight_ref, hits_ref, row_band_ref, col_band_ref, own_ref, near_ref, far_ref, *refs, width):
    *image_refs, conv_ref, sums_ref, row_ref, parts_ref = refs
    image_refs = dict(zip(far_first(len(image_refs)), image_refs))
    tile_at = lax.axis_index("tile")
    expo_at = lax.axis_index("expo")
    rows, ext = own_ref.shape
    expos = len(image_refs)
    chunk = ext - LANES
    blocks = chunk // LANES

    patch = jnp.concatenate([own_ref[...], near_ref[...], far_ref[...]], axis=0)
    row_ref[...] = jnp.dot(
        row_band_ref[...], patch, preferred_element_type=jnp.float32
    ).astype(jnp.bfloat16)
    for k in range(NB):
        window = jnp.concatenate(
            [
                row_ref[k * rows : (k + 1) * rows, b * LANES : (b + 2) * LANES]
                for b in range(blocks)
            ],
            axis=0,
        )
        out = jnp.dot(window, col_band_ref[k], preferred_element_type=jnp.float32)
        conv_ref[k] = out.reshape(blocks, rows, LANES)

    first_col = expo_at * chunk
    xs = [column_positions(first_col, b, width) for b in range(blocks)]

    def fold(x):
        total = x[:8]
        for i in range(8, rows, 8):
            total = total + x[i : i + 8]
        return total

    def moments(at, left, right, count):
        total = [None] * count
        for b in range(blocks):
            term = fold(left(b) * right(b)) if right is not None else fold(left(b))
            for i in range(count):
                total[i] = term if total[i] is None else total[i] + term
                if i < count - 1:
                    term = term * xs[b]
        for i in range(count):
            parts_ref[at + i] = total[i]

    def conv(k):
        return lambda b: conv_ref[k, b]

    def sci(shift):
        return image_blocks(image_refs[shift], expos, shift, chunk)

    blank = jnp.zeros((8, LANES), jnp.float32)
    at = 0
    for j, k in PAIRS:
        moments(at, conv(j), conv(k), 3)
        at += 3
    for k in range(NB):
        moments(at, conv(k), None, 2)
        at += 2
    while at % 8:
        parts_ref[at] = blank
        at += 1
    begin = at
    for shift in range(expos):
        row = at + NU * source(expo_at, shift, expos)
        for k in range(NB):
            moments(row + 2 * k, conv(k), sci(shift), 2)
        moments(row + NU - 1, sci(shift), None, 1)
    at += NU * expos
    weight = jnp.broadcast_to(weight_ref[...] * hits_ref[...].astype(jnp.float32), (8, LANES))
    weight = jnp.where(tile_at == 0, weight, 0.0)
    spot = (
        (lax.broadcasted_iota(jnp.int32, (8, LANES), 0) == 0)
        & (lax.broadcasted_iota(jnp.int32, (8, LANES), 1) == 0)
    )
    for e in range(expos):
        parts_ref[at + e] = jnp.where(spot & (expo_at == e), weight, 0.0)
    at += expos
    while at % 8:
        parts_ref[at] = blank
        at += 1
    ones = jnp.ones((8, LANES), jnp.float32)
    rows_of = []
    for first, last in ((0, begin), (begin, at)):
        lanes = jnp.sum(parts_ref[first:last], axis=1)
        spare = LANES - (last - first)
        if spare:
            lanes = jnp.concatenate([lanes, jnp.zeros((spare, LANES), jnp.float32)], axis=0)
        rows_of.append(
            lax.dot_general(
                ones,
                lanes,
                (((1,), (1,)), ((), ())),
                precision=lax.Precision.HIGHEST,
                preferred_element_type=jnp.float32,
            )
        )
    both = jnp.where(lax.broadcasted_iota(jnp.int32, (8, LANES), 0) < 4, rows_of[0], rows_of[1])
    for i in range(sums_ref.shape[0]):
        sums_ref[i] = both


def table(expos):
    columns = np.zeros((NU + expos + 1, 16), np.int32)
    for at, (j, k) in enumerate(PAIRS):
        for a, b in ((j, k), (k, j)):
            columns[b, a] = 3 * at
            columns[NB + b, a] = columns[b, NB + a] = 3 * at + 1
            columns[NB + b, NB + a] = 3 * at + 2
    for k in range(NB):
        for x in range(2):
            columns[NU - 1, x * NB + k] = columns[x * NB + k, NU - 1] = 3 * len(PAIRS) + 2 * k + x
    for e in range(expos):
        columns[NU + e, :NU] = [NU * e + 2 * k + x for x in range(2) for k in range(NB)] + [NU * e + NU - 1]
        columns[NU + expos, e] = NU * expos + e
    return np.ascontiguousarray(np.broadcast_to(columns[:, :, None], columns.shape + (LANES,)))


def solve_kernel(table_ref, sums_ref, conv_ref, *refs, width, pixels):
    *image_refs, coadd_ref, coeffs_ref, tile_ref, sems = refs
    expo_at = lax.axis_index("expo")
    expos = len(image_refs)
    rows, chunk = coadd_ref.shape
    blocks = chunk // LANES
    images = [image_blocks(ref, expos, shift, chunk) for shift, ref in enumerate(image_refs)]
    sub = lax.broadcasted_iota(jnp.int32, (16, LANES), 0)
    lane = lax.broadcasted_iota(jnp.int32, (16, LANES), 1)
    sums = sums_ref[0]
    for i in range(1, sums_ref.shape[0]):
        sums = sums + sums_ref[i]
    first = jnp.broadcast_to(sums[0:1], (16, LANES))
    second = jnp.broadcast_to(sums[4:5], (16, LANES))

    columns = [
        jnp.take_along_axis(first if j < NU else second, table_ref[j], axis=1) for j in range(NU + expos)
    ]
    spread = jnp.take_along_axis(second, table_ref[NU + expos], axis=1)
    weight = [jnp.broadcast_to(spread[e : e + 1], (16, LANES)) for e in range(expos)]
    columns[NU - 1] = jnp.where(sub == NU - 1, float(pixels), columns[NU - 1])

    trace = columns[0][0:1]
    for j in range(1, NU):
        trace = trace + columns[j][j : j + 1]
    scale = 1.0 / trace
    for j in range(NU + expos):
        columns[j] = columns[j] * scale
        if j < NU:
            columns[j] = columns[j] + jnp.where(sub == j, RIDGE / NU, 0.0)
    for i in range(NU):
        inverse = 1.0 / columns[i][i : i + 1]
        for j in range(i + 1, NU + expos):
            factor = columns[j][i : i + 1] * inverse
            columns[j] = jnp.where(sub == i, factor, columns[j] - columns[i] * factor)

    solved = columns[NU:]
    own = solved[0]
    mixed = weight[0] * solved[0]
    for e in range(1, expos):
        own = jnp.where(expo_at == e, solved[e], own)
        mixed = mixed + weight[e] * solved[e]
    diagonal = (sub == lane) & (sub < NU)
    coeffs_ref[...] = jnp.sum(jnp.where(diagonal, own, 0.0), axis=0, keepdims=True)[:, :NU]
    scale = [jnp.broadcast_to(mixed[u : u + 1], (8, LANES)) for u in range(NU)]
    gains = []
    for shift in range(expos):
        gain = weight[0][:8]
        for e in range(1, expos):
            gain = jnp.where(source(expo_at, shift, expos) == e, weight[e][:8], gain)
        gains.append(gain)
    first_col = expo_at * chunk
    copies = []
    for r in range(0, rows, 8):
        for b in range(blocks):
            x = column_positions(first_col, b, width)
            total = -scale[NU - 1]
            for gain, image in zip(gains, images):
                total = total + gain * image(b)[r : r + 8]
            model = (scale[0] + scale[NB] * x) * conv_ref[0, b, r : r + 8]
            for k in range(1, NB):
                model = model + (scale[k] + scale[NB + k] * x) * conv_ref[k, b, r : r + 8]
            tile_ref[r : r + 8, b * LANES : (b + 1) * LANES] = total - model
        copies.append(
            pltpu.make_async_copy(tile_ref.at[pl.ds(r, 8)], coadd_ref.at[pl.ds(r, 8)], sems.at[r // 8])
        )
        copies[-1].start()
    for copy in copies:
        copy.wait()


def swaps(first, size):
    pairs = [(i, i + 1) for i in range(first, size - 1, 2)]
    if first and size % 2 == 0:
        pairs.append((0, size - 1))
    return [pair for a, b in pairs for pair in ((a, b), (b, a))]


def tiled_device(template, science, plan, orders, coadd_weight, intersection):
    expos = lax.axis_size("expo")
    tiles = lax.axis_size("tile")
    _, rows, width = template.shape
    steps = science.shape[1]
    chunk = width // expos
    ext = chunk + LANES
    blocks = chunk // LANES
    vmem = pl.BlockSpec(memory_space=pltpu.VMEM)
    small = pltpu.CompilerParams(vmem_limit_bytes=16 * 1024 * 1024)
    hbm = pl.BlockSpec(memory_space=pltpu.HBM)
    coadds = []
    fitted = []
    for step in range(steps):
        *blocks_out, owner, order = pl.pallas_call(
            functools.partial(send_kernel, step=step),
            out_shape=tuple(
                pltpu.VMEM((rows, ext + chunk if joint(shift, expos) else ext), template.dtype)
                for shift in range(expos)
            )
            + (pltpu.VMEM((rows, ext), science.dtype),) * (expos - expos // 2)
            + (
                jax.ShapeDtypeStruct((rows, LANES), jnp.int32),
                jax.ShapeDtypeStruct((2, NB, 8, LANES), jnp.int32),
            ),
            in_specs=[hbm] * 4,
            out_specs=(vmem,) * (2 * expos - expos // 2 + 2),
            scratch_shapes=[
                pltpu.VMEM((rows, width + 2 * LANES), template.dtype),
                pltpu.SMEM(plan.shape, jnp.int32),
                pltpu.SMEM((2, NB), jnp.int32),
                pltpu.SemaphoreType.DMA((expos + 4,)),
            ],
            compiler_params=small,
        )(
            pltpu.with_memory_space_constraint(template[0], pltpu.HBM),
            pltpu.with_memory_space_constraint(science[0, step], pltpu.HBM),
            pltpu.with_memory_space_constraint(plan, pltpu.HBM),
            pltpu.with_memory_space_constraint(orders.T, pltpu.HBM),
        )
        patches, images = blocks_out[:expos], blocks_out[expos:]
        for group, first in ((patches, 0), (images, expos // 2)):
            for shift in range(max(first, 1), expos):
                pairs = [(e, int(target(e, shift, expos))) for e in range(expos)]
                group[shift - first] = lax.ppermute(group[shift - first], "expo", pairs)
        images = patches[: expos // 2] + images
        across = [shift for shift in far_first(expos)[:-1] if not joint(shift, expos)]
        beside = [shift for shift in far_first(expos)[:-1] if joint(shift, expos)]
        block = pl.pallas_call(
            functools.partial(choose_kernel, shifts=across, size=expos),
            out_shape=jax.ShapeDtypeStruct((rows, ext), template.dtype),
            in_specs=[vmem] * (2 + len(across)),
            out_specs=vmem,
            compiler_params=small,
            cost_estimate=pl.CostEstimate(flops=STAGE_COST, bytes_accessed=500_000, transcendentals=0),
        )(owner, patches[0], *(patches[shift] for shift in across))
        own = pl.pallas_call(
            functools.partial(pick_kernel, shifts=beside, size=expos),
            out_shape=jax.ShapeDtypeStruct((rows, ext), template.dtype),
            in_specs=[vmem] * (2 + len(beside)),
            out_specs=vmem,
            scratch_shapes=[pltpu.VMEM((rows, ext), template.dtype)],
            compiler_params=small,
        )(owner, block, *(patches[shift] for shift in beside))
        row_band, col_band = pl.pallas_call(
            functools.partial(band_kernel, tiles=tiles),
            out_shape=(
                jax.ShapeDtypeStruct((NB * rows, 3 * rows), jnp.bfloat16),
                jax.ShapeDtypeStruct((NB, 2 * LANES, LANES), jnp.bfloat16),
            ),
            in_specs=[vmem, pl.BlockSpec(memory_space=pl.ANY)],
            out_specs=(vmem, vmem),
            compiler_params=small,
            cost_estimate=pl.CostEstimate(flops=4_000_000, bytes_accessed=500_000, transcendentals=200_000),
        )(order, own)
        far = lax.ppermute(own, "tile", swaps(1, tiles))
        near = lax.ppermute(own, "tile", swaps(0, tiles))
        conv, sums = pl.pallas_call(
            functools.partial(fit_kernel, width=width),
            out_shape=(
                jax.ShapeDtypeStruct((NB, blocks, rows, LANES), jnp.float32),
                jax.ShapeDtypeStruct((tiles * expos, 8, LANES), jnp.float32),
            ),
            in_specs=[vmem] * (7 + expos),
            out_specs=(vmem, vmem),
            scratch_shapes=[
                pltpu.VMEM((NB * rows, ext), jnp.bfloat16),
                pltpu.VMEM((80 + 14 * expos + 8, 8, LANES), jnp.float32),
            ],
            compiler_params=small,
        )(
            coadd_weight[:, step : step + 1],
            intersection[:, step : step + 1],
            row_band,
            col_band,
            own,
            near,
            far,
            *(images[shift] for shift in far_first(expos)),
        )
        group = [e * tiles + t for e in reversed(range(expos)) for t in range(tiles)]
        sums = lax.all_to_all(
            sums, ("expo", "tile"), split_axis=0, concat_axis=0, tiled=True, axis_index_groups=[group]
        )
        coadd, coeffs = pl.pallas_call(
            functools.partial(solve_kernel, width=width, pixels=tiles * rows * width),
            out_shape=(
                jax.ShapeDtypeStruct((rows, chunk), jnp.float32),
                jax.ShapeDtypeStruct((1, NU), jnp.float32),
            ),
            in_specs=[vmem] * (3 + expos),
            out_specs=(pl.BlockSpec(memory_space=pl.ANY), vmem),
            scratch_shapes=[
                pltpu.VMEM((rows, chunk), jnp.float32),
                pltpu.SemaphoreType.DMA((rows // 8,)),
            ],
            compiler_params=small,
        )(jnp.asarray(table(expos)), sums, conv, *images)
        coadds.append(coadd[None])
        fitted.append(coeffs)
    return (jnp.concatenate(coadds), jnp.stack(fitted, axis=1))


def broadcast(block, axis, holder):
    block = jnp.where(lax.axis_index(axis) == holder, block, jnp.zeros_like(block))
    return lax.psum(block, axis)


def extended(x, sides, width):
    for axis, dim in sides:
        size, length = (lax.axis_size(axis), x.shape[dim])
        up = [(i, (i + 1) % size) for i in range(size - 1)]
        down = [(j, i) for i, j in up]
        last = lax.slice_in_dim(x, length - width, length, axis=dim)
        first = lax.slice_in_dim(x, 0, width, axis=dim)
        before = lax.ppermute(last, axis, up)
        after = lax.ppermute(first, axis, down)
        x = jnp.concatenate([before, x, after], axis=dim)
    return x


def make_filters(orders):
    taps_pos = jnp.arange(2 * HALF + 1).astype(jnp.float32) - HALF
    row_list = []
    col_list = []
    for basis in range(NB):
        sigma = SIGMAS[basis]
        envelope = jnp.exp(-taps_pos * taps_pos / (2.0 * sigma * sigma))
        row_filter = envelope * power_of(taps_pos, orders[basis, 0])
        col_filter = envelope * power_of(taps_pos, orders[basis, 1])
        row_list.append(row_filter / jnp.sqrt(jnp.sum(row_filter * row_filter)))
        col_list.append(col_filter / jnp.sqrt(jnp.sum(col_filter * col_filter)))
    return (jnp.stack(row_list).astype(jnp.bfloat16), jnp.stack(col_list).astype(jnp.bfloat16))


def band_matrix(filters, out_len, in_len):
    offset = jnp.arange(in_len)[None, :] - jnp.arange(out_len)[:, None]
    taps_idx = jnp.arange(2 * HALF + 1)
    picks = (offset[:, :, None] == taps_idx[None, None, :]).astype(jnp.float32)
    band = jnp.einsum("ijt,kt->kij", picks, filters.astype(jnp.float32))
    return band.astype(jnp.bfloat16)


def any_device(template, science, plan, orders, coadd_weight, intersection):
    row_filters, col_filters = make_filters(orders)
    rows = template.shape[1]
    width = template.shape[2]
    blocks_count = width // 128
    steps_count = science.shape[1]
    row_band = band_matrix(row_filters, rows, rows + 2 * HALF)
    col_band = jnp.transpose(band_matrix(col_filters, 128, 128 + 2 * HALF), (0, 2, 1))
    column_pos = 2.0 * (jnp.arange(width).astype(jnp.float32) + 0.5) / width - 1.0
    pieces = []
    fitted = []
    for step in range(steps_count):
        received = broadcast(template[0], "expo", plan[step])
        padded = extended(received, (("tile", 0),), HALF)
        rowconv = jnp.einsum(
            "kij,jw->kiw", row_band, padded, preferred_element_type=jnp.float32
        ).astype(jnp.bfloat16)
        blocks = rowconv.reshape(NB, rows, blocks_count, 128)
        empty_rim = jnp.zeros((NB, rows, 1, HALF), jnp.bfloat16)
        previous = jnp.concatenate([empty_rim, blocks[:, :, :-1, 128 - HALF :]], axis=2)
        following = jnp.concatenate([blocks[:, :, 1:, :HALF], empty_rim], axis=2)
        window = jnp.concatenate([previous, blocks, following], axis=3)
        conv = jnp.einsum("krbj,kjc->krbc", window, col_band, preferred_element_type=jnp.float32)
        conv = conv.reshape(NB, rows, width)
        fields = jnp.concatenate(
            [conv, conv * column_pos, jnp.ones((1, rows, width), jnp.float32)], axis=0
        )
        fields = fields.reshape(NU, rows * width)
        exposure_image = science[0, step].astype(jnp.float32).reshape(rows * width)
        normal_local = jnp.dot(fields, fields.T, precision=lax.Precision.HIGHEST)
        project_local = jnp.dot(fields, exposure_image, precision=lax.Precision.HIGHEST)
        normal_matrix, projections = lax.psum((normal_local, project_local), "tile")
        normal_matrix = normal_matrix + RIDGE * (jnp.trace(normal_matrix) / NU) * jnp.eye(
            NU, dtype=jnp.float32
        )
        factor = jnp.linalg.cholesky(normal_matrix)
        coeffs = jax.scipy.linalg.cho_solve((factor, True), projections)
        model = jnp.dot(coeffs, fields, precision=lax.Precision.HIGHEST)
        difference = exposure_image - model
        weight_now = coadd_weight[0, step] * intersection[0, step].astype(jnp.float32)
        pieces.append((weight_now * difference).reshape(rows, width))
        fitted.append(coeffs)
    weighted = jnp.stack(pieces)
    received_parts = lax.all_to_all(weighted[None], "expo", split_axis=3, concat_axis=0, tiled=True)
    coadd = jnp.sum(received_parts, axis=0)
    return (coadd, jnp.stack(fitted)[None])


def per_device(template, science, plan, orders, coadd_weight, intersection):
    expos = lax.axis_size("expo")
    rows, width = template.shape[1:]
    whole_lanes = width % (expos * LANES) == 0 and rows % 16 == 0 and 3 * rows <= LANES
    few = (NU + 1) * expos <= LANES and NU + expos <= LANES
    body = tiled_device if whole_lanes and few else any_device
    return body(template, science, plan, orders, coadd_weight, intersection)


def solution(mesh):
    return jax.shard_map(
        per_device,
        mesh=mesh,
        in_specs=(
            P(("groups", "expo"), "tile", None),
            P(("groups", "expo"), None, "tile", None),
            P("groups"),
            P(),
            P(("groups", "expo"), None),
            P(("groups", "expo"), None),
        ),
        out_specs=(P("groups", "tile", "expo"), P(("groups", "expo"), None, None)),
        check_vma=False,
    )
```

```python
import functools

import jax
import jax.numpy as jnp
import numpy as np
from jax import lax
from jax.experimental import pallas as pl
from jax.experimental.pallas import tpu as pltpu
from jax.sharding import PartitionSpec as P

HALF = 15
NB = 6
NU = 13
LANES = 128
BEYOND = 1000
STAGE_COST = 700_000_000
PAIRS = [(j, k) for j in range(NB) for k in range(j, NB)]

SIGMAS = (0.8, 1.4, 2.2, 3.0, 4.0, 5.5)
RIDGE = 0.05


def power_of(pos, order):
    return jnp.where(order == 0, 1.0, jnp.where(order == 1, pos, pos * pos))


def tap_values(pos, sigma, order):
    value = jnp.exp(-pos * pos / (2.0 * sigma * sigma)) * power_of(pos, order)
    return jnp.where(jnp.abs(pos) <= HALF, value, 0.0)


def tap_norm(sigma, order):
    pos = lax.broadcasted_iota(jnp.int32, (8, LANES), 1).astype(jnp.float32) - HALF
    value = tap_values(pos, sigma, order)
    return jnp.sqrt(jnp.sum(value * value, axis=1, keepdims=True))


def target(me, shift, size):
    return me ^ shift if size & (size - 1) == 0 else (me + shift) % size


def source(me, shift, size):
    return me ^ shift if size & (size - 1) == 0 else (me - shift + size) % size


def far_first(size):
    return [*range(size - 1, 0, -1), 0]


def joint(shift, size):
    return shift < size // 2


def send_kernel(template_ref, science_ref, plan_ref, orders_ref, *refs, step):
    *out_refs, owner_ref, order_ref, patch_ref, plan_now, orders_now, sems = refs
    size = sems.shape[0] - 4
    rows, width = science_ref.shape
    chunk = width // size
    ext = chunk + LANES
    patch_refs, image_refs = out_refs[:size], out_refs[size:]
    half = size * chunk // 2
    me = lax.axis_index("expo")
    starts = [pl.multiple_of(target(me, shift, size) * chunk, chunk) for shift in range(size)]
    loads = [
        pltpu.make_async_copy(
            template_ref.at[:, pl.ds(i * half, half)], patch_ref.at[:, pl.ds((i * half + LANES), half)], sems.at[i]
        )
        for i in range(2)
    ]
    copies = [
        pltpu.make_async_copy(
            science_ref.at[:, pl.ds(starts[shift], chunk)],
            patch_refs[shift].at[:, pl.ds(ext, chunk)]
            if joint(shift, size)
            else image_refs[shift - size // 2].at[:, pl.ds(0, chunk)],
            sems.at[3 + shift],
        )
        for shift in range(size)
    ]
    copies.append(pltpu.make_async_copy(plan_ref, plan_now, sems.at[2]))
    copies.append(pltpu.make_async_copy(orders_ref, orders_now, sems.at[3 + size]))
    for copy in loads + copies:
        copy.start()
    blank = jnp.zeros((rows, LANES), patch_ref.dtype)
    patch_ref[:, :LANES] = blank
    patch_ref[:, size * chunk + LANES :] = blank
    for image_ref in image_refs:
        image_ref[:, chunk:] = blank
    for copy in loads:
        copy.wait()
    lane = lax.broadcasted_iota(jnp.int32, (rows, LANES), 1)
    for shift in range(size):
        start = starts[shift]
        patch_refs[shift][:, :chunk] = patch_ref[:, pl.ds(start + LANES, chunk)]
        before = patch_ref[:, pl.ds(start, LANES)].astype(jnp.float32)
        after = patch_ref[:, pl.ds(start + chunk + LANES, LANES)].astype(jnp.float32)
        rim = jnp.where(lane < LANES // 2, after, before)
        patch_refs[shift][:, chunk:ext] = rim.astype(patch_ref.dtype)
    for copy in copies:
        copy.wait()
    owner_ref[...] = jnp.full(owner_ref.shape, plan_now[step], jnp.int32)
    for way in range(2):
        for k in range(NB):
            order_ref[way, k] = jnp.full((8, LANES), orders_now[way, k], jnp.int32)


def choose_kernel(owner_ref, *refs, shifts, size):
    *recv_refs, out_ref = refs
    me = lax.axis_index("expo")
    for b in range(out_ref.shape[1] // LANES):
        columns = slice(b * LANES, (b + 1) * LANES)
        block = recv_refs[0][:, columns].astype(jnp.float32)
        for shift, ref in zip(shifts, recv_refs[1:]):
            block = jnp.where(
                owner_ref[...] == source(me, shift, size), ref[:, columns].astype(jnp.float32), block
            )
        out_ref[:, columns] = block.astype(out_ref.dtype)


def pick_kernel(owner_ref, *refs, shifts, size):
    *recv_refs, out_ref, block_ref = refs
    ext = out_ref.shape[1]
    choose_kernel(owner_ref, *recv_refs, block_ref, shifts=shifts, size=size)
    whole = jnp.concatenate([block_ref[:, ext - LANES :], block_ref[...]], axis=1)
    out_ref[...] = whole[:, LANES - HALF : LANES - HALF + ext]


def column_positions(first_col, block, width):
    col = lax.broadcasted_iota(jnp.int32, (8, LANES), 1) + (first_col + block * LANES)
    return 2.0 * (col.astype(jnp.float32) + 0.5) / width - 1.0


def band_kernel(order_ref, _, row_ref, col_ref, *, tiles):
    rows = row_ref.shape[0] // NB
    tile_at = lax.axis_index("tile")
    near = 1 - 2 * lax.rem(tile_at, 2)
    near_move = jnp.where(tile_at + near < tiles, near - 1, BEYOND)
    far_move = jnp.where((tile_at >= near) & (tile_at - near < tiles), -near - 2, BEYOND)
    row_from = lax.broadcasted_iota(jnp.int32, (8, LANES), 1)
    moved = jnp.where(row_from < rows, 0, jnp.where(row_from < 2 * rows, near_move, far_move))
    sub = lax.broadcasted_iota(jnp.int32, (8, LANES), 0)
    lane = lax.broadcasted_iota(jnp.int32, (8, LANES), 1)
    shift = (sub - jnp.where(lane < LANES // 2, lane, lane - LANES) - HALF).astype(jnp.float32)
    for k in range(NB):
        norm = tap_norm(SIGMAS[k], order_ref[0, k])
        for r in range(0, rows, 16):
            parts = []
            for half in (r, r + 8):
                offset = (row_from + moved * rows - sub - half).astype(jnp.float32)
                parts.append(tap_values(offset, SIGMAS[k], order_ref[0, k]) / norm)
            both = jnp.concatenate(parts, axis=0).astype(jnp.bfloat16)
            row_ref[k * rows + r : k * rows + r + 16] = both[:, : 3 * rows]
        norm = tap_norm(SIGMAS[k], order_ref[1, k])
        pattern = tap_values(shift, SIGMAS[k], order_ref[1, k]) / norm
        for r in range(0, 2 * LANES, 16):
            parts = []
            for half in (r, r + 8):
                moved_on = pltpu.roll(pattern, half % LANES, 1) if half % LANES else pattern
                inside = lane <= half + 7 if half < LANES else lane >= half - LANES + LANES // 2
                parts.append(jnp.where(inside, moved_on, 0.0))
            col_ref[k, r : r + 16] = jnp.concatenate(parts, axis=0).astype(jnp.bfloat16)


def image_blocks(ref, size, shift, chunk):
    first = chunk + LANES if joint(shift, size) else 0
    return lambda b: ref[:, first + b * LANES : first + (b + 1) * LANES].astype(jnp.float32)


def fit_kernel(weight_ref, hits_ref, row_band_ref, col_band_ref, own_ref, near_ref, far_ref, *refs, width):
    *image_refs, conv_ref, sums_ref, row_ref, parts_ref = refs
    image_refs = dict(zip(far_first(len(image_refs)), image_refs))
    tile_at = lax.axis_index("tile")
    expo_at = lax.axis_index("expo")
    rows, ext = own_ref.shape
    expos = len(image_refs)
    chunk = ext - LANES
    blocks = chunk // LANES

    patch = jnp.concatenate([own_ref[...], near_ref[...], far_ref[...]], axis=0)
    row_ref[...] = jnp.dot(
        row_band_ref[...], patch, preferred_element_type=jnp.float32
    ).astype(jnp.bfloat16)
    for k in range(NB):
        window = jnp.concatenate(
            [
                row_ref[k * rows : (k + 1) * rows, b * LANES : (b + 2) * LANES]
                for b in range(blocks)
            ],
            axis=0,
        )
        out = jnp.dot(window, col_band_ref[k], preferred_element_type=jnp.float32)
        conv_ref[k] = out.reshape(blocks, rows, LANES)

    first_col = expo_at * chunk
    xs = [column_positions(first_col, b, width) for b in range(blocks)]

    def fold(x):
        total = x[:8]
        for i in range(8, rows, 8):
            total = total + x[i : i + 8]
        return total

    def moments(at, left, right, count):
        total = [None] * count
        for b in range(blocks):
            term = fold(left(b) * right(b)) if right is not None else fold(left(b))
            for i in range(count):
                total[i] = term if total[i] is None else total[i] + term
                if i < count - 1:
                    term = term * xs[b]
        for i in range(count):
            parts_ref[at + i] = total[i]

    def conv(k):
        return lambda b: conv_ref[k, b]

    def sci(shift):
        return image_blocks(image_refs[shift], expos, shift, chunk)

    blank = jnp.zeros((8, LANES), jnp.float32)
    at = 0
    for j, k in PAIRS:
        moments(at, conv(j), conv(k), 3)
        at += 3
    for k in range(NB):
        moments(at, conv(k), None, 2)
        at += 2
    while at % 8:
        parts_ref[at] = blank
        at += 1
    begin = at
    for shift in range(expos):
        row = at + NU * source(expo_at, shift, expos)
        for k in range(NB):
            moments(row + 2 * k, conv(k), sci(shift), 2)
        moments(row + NU - 1, sci(shift), None, 1)
    at += NU * expos
    weight = jnp.broadcast_to(weight_ref[...] * hits_ref[...].astype(jnp.float32), (8, LANES))
    weight = jnp.where(tile_at == 0, weight, 0.0)
    spot = (
        (lax.broadcasted_iota(jnp.int32, (8, LANES), 0) == 0)
        & (lax.broadcasted_iota(jnp.int32, (8, LANES), 1) == 0)
    )
    for e in range(expos):
        parts_ref[at + e] = jnp.where(spot & (expo_at == e), weight, 0.0)
    at += expos
    while at % 8:
        parts_ref[at] = blank
        at += 1
    ones = jnp.ones((8, LANES), jnp.float32)
    rows_of = []
    for first, last in ((0, begin), (begin, at)):
        lanes = jnp.sum(parts_ref[first:last], axis=1)
        spare = LANES - (last - first)
        if spare:
            lanes = jnp.concatenate([lanes, jnp.zeros((spare, LANES), jnp.float32)], axis=0)
        rows_of.append(
            lax.dot_general(
                ones,
                lanes,
                (((1,), (1,)), ((), ())),
                precision=lax.Precision.HIGHEST,
                preferred_element_type=jnp.float32,
            )
        )
    both = jnp.where(lax.broadcasted_iota(jnp.int32, (8, LANES), 0) < 4, rows_of[0], rows_of[1])
    for i in range(sums_ref.shape[0]):
        sums_ref[i] = both


def table(expos):
    columns = np.zeros((NU + expos + 1, 16), np.int32)
    for at, (j, k) in enumerate(PAIRS):
        for a, b in ((j, k), (k, j)):
            columns[b, a] = 3 * at
            columns[NB + b, a] = columns[b, NB + a] = 3 * at + 1
            columns[NB + b, NB + a] = 3 * at + 2
    for k in range(NB):
        for x in range(2):
            columns[NU - 1, x * NB + k] = columns[x * NB + k, NU - 1] = 3 * len(PAIRS) + 2 * k + x
    for e in range(expos):
        columns[NU + e, :NU] = [NU * e + 2 * k + x for x in range(2) for k in range(NB)] + [NU * e + NU - 1]
        columns[NU + expos, e] = NU * expos + e
    return np.ascontiguousarray(np.broadcast_to(columns[:, :, None], columns.shape + (LANES,)))


def solve_kernel(table_ref, sums_ref, conv_ref, *refs, width, pixels):
    *image_refs, coadd_ref, coeffs_ref, tile_ref, sems = refs
    expo_at = lax.axis_index("expo")
    expos = len(image_refs)
    rows, chunk = coadd_ref.shape
    blocks = chunk // LANES
    images = [image_blocks(ref, expos, shift, chunk) for shift, ref in enumerate(image_refs)]
    sub = lax.broadcasted_iota(jnp.int32, (16, LANES), 0)
    lane = lax.broadcasted_iota(jnp.int32, (16, LANES), 1)
    sums = sums_ref[0]
    for i in range(1, sums_ref.shape[0]):
        sums = sums + sums_ref[i]
    first = jnp.broadcast_to(sums[0:1], (16, LANES))
    second = jnp.broadcast_to(sums[4:5], (16, LANES))

    columns = [
        jnp.take_along_axis(first if j < NU else second, table_ref[j], axis=1) for j in range(NU + expos)
    ]
    spread = jnp.take_along_axis(second, table_ref[NU + expos], axis=1)
    weight = [jnp.broadcast_to(spread[e : e + 1], (16, LANES)) for e in range(expos)]
    columns[NU - 1] = jnp.where(sub == NU - 1, float(pixels), columns[NU - 1])

    trace = columns[0][0:1]
    for j in range(1, NU):
        trace = trace + columns[j][j : j + 1]
    scale = 1.0 / trace
    for j in range(NU + expos):
        columns[j] = columns[j] * scale
        if j < NU:
            columns[j] = columns[j] + jnp.where(sub == j, RIDGE / NU, 0.0)
    for i in range(NU):
        inverse = 1.0 / columns[i][i : i + 1]
        for j in range(i + 1, NU + expos):
            factor = columns[j][i : i + 1] * inverse
            columns[j] = jnp.where(sub == i, factor, columns[j] - columns[i] * factor)

    solved = columns[NU:]
    own = solved[0]
    mixed = weight[0] * solved[0]
    for e in range(1, expos):
        own = jnp.where(expo_at == e, solved[e], own)
        mixed = mixed + weight[e] * solved[e]
    diagonal = (sub == lane) & (sub < NU)
    coeffs_ref[...] = jnp.sum(jnp.where(diagonal, own, 0.0), axis=0, keepdims=True)[:, :NU]
    scale = [jnp.broadcast_to(mixed[u : u + 1], (8, LANES)) for u in range(NU)]
    gains = []
    for shift in range(expos):
        gain = weight[0][:8]
        for e in range(1, expos):
            gain = jnp.where(source(expo_at, shift, expos) == e, weight[e][:8], gain)
        gains.append(gain)
    first_col = expo_at * chunk
    copies = []
    for r in range(0, rows, 8):
        for b in range(blocks):
            x = column_positions(first_col, b, width)
            total = -scale[NU - 1]
            for gain, image in zip(gains, images):
                total = total + gain * image(b)[r : r + 8]
            model = (scale[0] + scale[NB] * x) * conv_ref[0, b, r : r + 8]
            for k in range(1, NB):
                model = model + (scale[k] + scale[NB + k] * x) * conv_ref[k, b, r : r + 8]
            tile_ref[r : r + 8, b * LANES : (b + 1) * LANES] = total - model
        copies.append(
            pltpu.make_async_copy(tile_ref.at[pl.ds(r, 8)], coadd_ref.at[pl.ds(r, 8)], sems.at[r // 8])
        )
        copies[-1].start()
    for copy in copies:
        copy.wait()


def swaps(first, size):
    pairs = [(i, i + 1) for i in range(first, size - 1, 2)]
    if first and size % 2 == 0:
        pairs.append((0, size - 1))
    return [pair for a, b in pairs for pair in ((a, b), (b, a))]


def tiled_device(template, science, plan, orders, coadd_weight, intersection):
    expos = lax.axis_size("expo")
    tiles = lax.axis_size("tile")
    _, rows, width = template.shape
    steps = science.shape[1]
    chunk = width // expos
    ext = chunk + LANES
    blocks = chunk // LANES
    vmem = pl.BlockSpec(memory_space=pltpu.VMEM)
    small = pltpu.CompilerParams(vmem_limit_bytes=16 * 1024 * 1024)
    hbm = pl.BlockSpec(memory_space=pltpu.HBM)
    coadds = []
    fitted = []
    for step in range(steps):
        *blocks_out, owner, order = pl.pallas_call(
            functools.partial(send_kernel, step=step),
            out_shape=tuple(
                pltpu.VMEM((rows, ext + chunk if joint(shift, expos) else ext), template.dtype)
                for shift in range(expos)
            )
            + (pltpu.VMEM((rows, ext), science.dtype),) * (expos - expos // 2)
            + (
                jax.ShapeDtypeStruct((rows, LANES), jnp.int32),
                jax.ShapeDtypeStruct((2, NB, 8, LANES), jnp.int32),
            ),
            in_specs=[hbm] * 4,
            out_specs=(vmem,) * (2 * expos - expos // 2 + 2),
            scratch_shapes=[
                pltpu.VMEM((rows, width + 2 * LANES), template.dtype),
                pltpu.SMEM(plan.shape, jnp.int32),
                pltpu.SMEM((2, NB), jnp.int32),
                pltpu.SemaphoreType.DMA((expos + 4,)),
            ],
            compiler_params=small,
        )(
            pltpu.with_memory_space_constraint(template[0], pltpu.HBM),
            pltpu.with_memory_space_constraint(science[0, step], pltpu.HBM),
            pltpu.with_memory_space_constraint(plan, pltpu.HBM),
            pltpu.with_memory_space_constraint(orders.T, pltpu.HBM),
        )
        patches, images = blocks_out[:expos], blocks_out[expos:]
        for group, first in ((patches, 0), (images, expos // 2)):
            for shift in range(max(first, 1), expos):
                pairs = [(e, int(target(e, shift, expos))) for e in range(expos)]
                group[shift - first] = lax.ppermute(group[shift - first], "expo", pairs)
        images = patches[: expos // 2] + images
        across = [shift for shift in far_first(expos)[:-1] if not joint(shift, expos)]
        beside = [shift for shift in far_first(expos)[:-1] if joint(shift, expos)]
        block = pl.pallas_call(
            functools.partial(choose_kernel, shifts=across, size=expos),
            out_shape=jax.ShapeDtypeStruct((rows, ext), template.dtype),
            in_specs=[vmem] * (2 + len(across)),
            out_specs=vmem,
            compiler_params=small,
            cost_estimate=pl.CostEstimate(flops=STAGE_COST, bytes_accessed=500_000, transcendentals=0),
        )(owner, patches[0], *(patches[shift] for shift in across))
        own = pl.pallas_call(
            functools.partial(pick_kernel, shifts=beside, size=expos),
            out_shape=jax.ShapeDtypeStruct((rows, ext), template.dtype),
            in_specs=[vmem] * (2 + len(beside)),
            out_specs=vmem,
            scratch_shapes=[pltpu.VMEM((rows, ext), template.dtype)],
            compiler_params=small,
        )(owner, block, *(patches[shift] for shift in beside))
        row_band, col_band = pl.pallas_call(
            functools.partial(band_kernel, tiles=tiles),
            out_shape=(
                jax.ShapeDtypeStruct((NB * rows, 3 * rows), jnp.bfloat16),
                jax.ShapeDtypeStruct((NB, 2 * LANES, LANES), jnp.bfloat16),
            ),
            in_specs=[vmem, pl.BlockSpec(memory_space=pl.ANY)],
            out_specs=(vmem, vmem),
            compiler_params=small,
            cost_estimate=pl.CostEstimate(flops=4_000_000, bytes_accessed=500_000, transcendentals=200_000),
        )(order, own)
        far = lax.ppermute(own, "tile", swaps(1, tiles))
        near = lax.ppermute(own, "tile", swaps(0, tiles))
        conv, sums = pl.pallas_call(
            functools.partial(fit_kernel, width=width),
            out_shape=(
                jax.ShapeDtypeStruct((NB, blocks, rows, LANES), jnp.float32),
                jax.ShapeDtypeStruct((tiles * expos, 8, LANES), jnp.float32),
            ),
            in_specs=[vmem] * (7 + expos),
            out_specs=(vmem, vmem),
            scratch_shapes=[
                pltpu.VMEM((NB * rows, ext), jnp.bfloat16),
                pltpu.VMEM((80 + 14 * expos + 8, 8, LANES), jnp.float32),
            ],
            compiler_params=small,
        )(
            coadd_weight[:, step : step + 1],
            intersection[:, step : step + 1],
            row_band,
            col_band,
            own,
            near,
            far,
            *(images[shift] for shift in far_first(expos)),
        )
        group = list(reversed(range(expos * tiles)))
        sums = lax.all_to_all(
            sums, ("expo", "tile"), split_axis=0, concat_axis=0, tiled=True, axis_index_groups=[group]
        )
        coadd, coeffs = pl.pallas_call(
            functools.partial(solve_kernel, width=width, pixels=tiles * rows * width),
            out_shape=(
                jax.ShapeDtypeStruct((rows, chunk), jnp.float32),
                jax.ShapeDtypeStruct((1, NU), jnp.float32),
            ),
            in_specs=[vmem] * (3 + expos),
            out_specs=(pl.BlockSpec(memory_space=pl.ANY), vmem),
            scratch_shapes=[
                pltpu.VMEM((rows, chunk), jnp.float32),
                pltpu.SemaphoreType.DMA((rows // 8,)),
            ],
            compiler_params=small,
        )(jnp.asarray(table(expos)), sums, conv, *images)
        coadds.append(coadd[None])
        fitted.append(coeffs)
    return (jnp.concatenate(coadds), jnp.stack(fitted, axis=1))


def broadcast(block, axis, holder):
    block = jnp.where(lax.axis_index(axis) == holder, block, jnp.zeros_like(block))
    return lax.psum(block, axis)


def extended(x, sides, width):
    for axis, dim in sides:
        size, length = (lax.axis_size(axis), x.shape[dim])
        up = [(i, (i + 1) % size) for i in range(size - 1)]
        down = [(j, i) for i, j in up]
        last = lax.slice_in_dim(x, length - width, length, axis=dim)
        first = lax.slice_in_dim(x, 0, width, axis=dim)
        before = lax.ppermute(last, axis, up)
        after = lax.ppermute(first, axis, down)
        x = jnp.concatenate([before, x, after], axis=dim)
    return x


def make_filters(orders):
    taps_pos = jnp.arange(2 * HALF + 1).astype(jnp.float32) - HALF
    row_list = []
    col_list = []
    for basis in range(NB):
        sigma = SIGMAS[basis]
        envelope = jnp.exp(-taps_pos * taps_pos / (2.0 * sigma * sigma))
        row_filter = envelope * power_of(taps_pos, orders[basis, 0])
        col_filter = envelope * power_of(taps_pos, orders[basis, 1])
        row_list.append(row_filter / jnp.sqrt(jnp.sum(row_filter * row_filter)))
        col_list.append(col_filter / jnp.sqrt(jnp.sum(col_filter * col_filter)))
    return (jnp.stack(row_list).astype(jnp.bfloat16), jnp.stack(col_list).astype(jnp.bfloat16))


def band_matrix(filters, out_len, in_len):
    offset = jnp.arange(in_len)[None, :] - jnp.arange(out_len)[:, None]
    taps_idx = jnp.arange(2 * HALF + 1)
    picks = (offset[:, :, None] == taps_idx[None, None, :]).astype(jnp.float32)
    band = jnp.einsum("ijt,kt->kij", picks, filters.astype(jnp.float32))
    return band.astype(jnp.bfloat16)


def any_device(template, science, plan, orders, coadd_weight, intersection):
    row_filters, col_filters = make_filters(orders)
    rows = template.shape[1]
    width = template.shape[2]
    blocks_count = width // 128
    steps_count = science.shape[1]
    row_band = band_matrix(row_filters, rows, rows + 2 * HALF)
    col_band = jnp.transpose(band_matrix(col_filters, 128, 128 + 2 * HALF), (0, 2, 1))
    column_pos = 2.0 * (jnp.arange(width).astype(jnp.float32) + 0.5) / width - 1.0
    pieces = []
    fitted = []
    for step in range(steps_count):
        received = broadcast(template[0], "expo", plan[step])
        padded = extended(received, (("tile", 0),), HALF)
        rowconv = jnp.einsum(
            "kij,jw->kiw", row_band, padded, preferred_element_type=jnp.float32
        ).astype(jnp.bfloat16)
        blocks = rowconv.reshape(NB, rows, blocks_count, 128)
        empty_rim = jnp.zeros((NB, rows, 1, HALF), jnp.bfloat16)
        previous = jnp.concatenate([empty_rim, blocks[:, :, :-1, 128 - HALF :]], axis=2)
        following = jnp.concatenate([blocks[:, :, 1:, :HALF], empty_rim], axis=2)
        window = jnp.concatenate([previous, blocks, following], axis=3)
        conv = jnp.einsum("krbj,kjc->krbc", window, col_band, preferred_element_type=jnp.float32)
        conv = conv.reshape(NB, rows, width)
        fields = jnp.concatenate(
            [conv, conv * column_pos, jnp.ones((1, rows, width), jnp.float32)], axis=0
        )
        fields = fields.reshape(NU, rows * width)
        exposure_image = science[0, step].astype(jnp.float32).reshape(rows * width)
        normal_local = jnp.dot(fields, fields.T, precision=lax.Precision.HIGHEST)
        project_local = jnp.dot(fields, exposure_image, precision=lax.Precision.HIGHEST)
        normal_matrix, projections = lax.psum((normal_local, project_local), "tile")
        normal_matrix = normal_matrix + RIDGE * (jnp.trace(normal_matrix) / NU) * jnp.eye(
            NU, dtype=jnp.float32
        )
        factor = jnp.linalg.cholesky(normal_matrix)
        coeffs = jax.scipy.linalg.cho_solve((factor, True), projections)
        model = jnp.dot(coeffs, fields, precision=lax.Precision.HIGHEST)
        difference = exposure_image - model
        weight_now = coadd_weight[0, step] * intersection[0, step].astype(jnp.float32)
        pieces.append((weight_now * difference).reshape(rows, width))
        fitted.append(coeffs)
    weighted = jnp.stack(pieces)
    received_parts = lax.all_to_all(weighted[None], "expo", split_axis=3, concat_axis=0, tiled=True)
    coadd = jnp.sum(received_parts, axis=0)
    return (coadd, jnp.stack(fitted)[None])


def per_device(template, science, plan, orders, coadd_weight, intersection):
    expos = lax.axis_size("expo")
    rows, width = template.shape[1:]
    whole_lanes = width % (expos * LANES) == 0 and rows % 16 == 0 and 3 * rows <= LANES
    few = (NU + 1) * expos <= LANES and NU + expos <= LANES
    body = tiled_device if whole_lanes and few else any_device
    return body(template, science, plan, orders, coadd_weight, intersection)


def solution(mesh):
    return jax.shard_map(
        per_device,
        mesh=mesh,
        in_specs=(
            P(("groups", "expo"), "tile", None),
            P(("groups", "expo"), None, "tile", None),
            P("groups"),
            P(),
            P(("groups", "expo"), None),
            P(("groups", "expo"), None),
        ),
        out_specs=(P("groups", "tile", "expo"), P(("groups", "expo"), None, None)),
        check_vma=False,
    )
```

```python
import functools

import jax
import jax.numpy as jnp
import numpy as np
from jax import lax
from jax.experimental import pallas as pl
from jax.experimental.pallas import tpu as pltpu
from jax.sharding import PartitionSpec as P

HALF = 15
NB = 6
NU = 13
LANES = 128
BEYOND = 1000
STAGE_COST = 700_000_000
PAIRS = [(j, k) for j in range(NB) for k in range(j, NB)]

SIGMAS = (0.8, 1.4, 2.2, 3.0, 4.0, 5.5)
RIDGE = 0.05


def power_of(pos, order):
    return jnp.where(order == 0, 1.0, jnp.where(order == 1, pos, pos * pos))


def tap_values(pos, sigma, order):
    value = jnp.exp(-pos * pos / (2.0 * sigma * sigma)) * power_of(pos, order)
    return jnp.where(jnp.abs(pos) <= HALF, value, 0.0)


def tap_norm(sigma, order):
    pos = lax.broadcasted_iota(jnp.int32, (8, LANES), 1).astype(jnp.float32) - HALF
    value = tap_values(pos, sigma, order)
    return jnp.sqrt(jnp.sum(value * value, axis=1, keepdims=True))


def target(me, shift, size):
    return me ^ shift if size & (size - 1) == 0 else (me + shift) % size


def source(me, shift, size):
    return me ^ shift if size & (size - 1) == 0 else (me - shift + size) % size


def far_first(size):
    return [*range(size - 1, 0, -1), 0]


def joint(shift, size):
    return shift < size // 2


def send_kernel(template_ref, science_ref, plan_ref, orders_ref, *refs, step):
    *out_refs, owner_ref, order_ref, patch_ref, plan_now, orders_now, sems = refs
    size = sems.shape[0] - 4
    rows, width = science_ref.shape
    chunk = width // size
    ext = chunk + LANES
    patch_refs, image_refs = out_refs[:size], out_refs[size:]
    half = size * chunk // 2
    me = lax.axis_index("expo")
    starts = [pl.multiple_of(target(me, shift, size) * chunk, chunk) for shift in range(size)]
    loads = [
        pltpu.make_async_copy(
            template_ref.at[:, pl.ds(i * half, half)], patch_ref.at[:, pl.ds((i * half + LANES), half)], sems.at[i]
        )
        for i in range(2)
    ]
    copies = [
        pltpu.make_async_copy(
            science_ref.at[:, pl.ds(starts[shift], chunk)],
            patch_refs[shift].at[:, pl.ds(ext, chunk)]
            if joint(shift, size)
            else image_refs[shift - size // 2].at[:, pl.ds(0, chunk)],
            sems.at[3 + shift],
        )
        for shift in range(size)
    ]
    copies.append(pltpu.make_async_copy(plan_ref, plan_now, sems.at[2]))
    copies.append(pltpu.make_async_copy(orders_ref, orders_now, sems.at[3 + size]))
    for copy in loads + copies:
        copy.start()
    blank = jnp.zeros((rows, LANES), patch_ref.dtype)
    patch_ref[:, :LANES] = blank
    patch_ref[:, size * chunk + LANES :] = blank
    for image_ref in image_refs:
        image_ref[:, chunk:] = blank
    for copy in loads:
        copy.wait()
    lane = lax.broadcasted_iota(jnp.int32, (rows, LANES), 1)
    for shift in range(size):
        start = starts[shift]
        patch_refs[shift][:, :chunk] = patch_ref[:, pl.ds(start + LANES, chunk)]
        before = patch_ref[:, pl.ds(start, LANES)].astype(jnp.float32)
        after = patch_ref[:, pl.ds(start + chunk + LANES, LANES)].astype(jnp.float32)
        rim = jnp.where(lane < LANES // 2, after, before)
        patch_refs[shift][:, chunk:ext] = rim.astype(patch_ref.dtype)
    for copy in copies:
        copy.wait()
    owner_ref[...] = jnp.full(owner_ref.shape, plan_now[step], jnp.int32)
    for way in range(2):
        for k in range(NB):
            order_ref[way, k] = jnp.full((8, LANES), orders_now[way, k], jnp.int32)


def choose_kernel(owner_ref, *refs, shifts, size):
    *recv_refs, out_ref = refs
    me = lax.axis_index("expo")
    for b in range(out_ref.shape[1] // LANES):
        columns = slice(b * LANES, (b + 1) * LANES)
        block = recv_refs[0][:, columns].astype(jnp.float32)
        for shift, ref in zip(shifts, recv_refs[1:]):
            block = jnp.where(
                owner_ref[...] == source(me, shift, size), ref[:, columns].astype(jnp.float32), block
            )
        out_ref[:, columns] = block.astype(out_ref.dtype)


def pick_kernel(owner_ref, *refs, shifts, size):
    *recv_refs, out_ref, block_ref = refs
    ext = out_ref.shape[1]
    choose_kernel(owner_ref, *recv_refs, block_ref, shifts=shifts, size=size)
    whole = jnp.concatenate([block_ref[:, ext - LANES :], block_ref[...]], axis=1)
    out_ref[...] = whole[:, LANES - HALF : LANES - HALF + ext]


def column_positions(first_col, block, width):
    col = lax.broadcasted_iota(jnp.int32, (8, LANES), 1) + (first_col + block * LANES)
    return 2.0 * (col.astype(jnp.float32) + 0.5) / width - 1.0


def band_kernel(order_ref, _, row_ref, col_ref, *, tiles):
    rows = row_ref.shape[0] // NB
    tile_at = lax.axis_index("tile")
    near = 1 - 2 * lax.rem(tile_at, 2)
    near_move = jnp.where(tile_at + near < tiles, near - 1, BEYOND)
    far_move = jnp.where((tile_at >= near) & (tile_at - near < tiles), -near - 2, BEYOND)
    row_from = lax.broadcasted_iota(jnp.int32, (8, LANES), 1)
    moved = jnp.where(row_from < rows, 0, jnp.where(row_from < 2 * rows, near_move, far_move))
    sub = lax.broadcasted_iota(jnp.int32, (8, LANES), 0)
    lane = lax.broadcasted_iota(jnp.int32, (8, LANES), 1)
    shift = (sub - jnp.where(lane < LANES // 2, lane, lane - LANES) - HALF).astype(jnp.float32)
    for k in range(NB):
        norm = tap_norm(SIGMAS[k], order_ref[0, k])
        for r in range(0, rows, 16):
            parts = []
            for half in (r, r + 8):
                offset = (row_from + moved * rows - sub - half).astype(jnp.float32)
                parts.append(tap_values(offset, SIGMAS[k], order_ref[0, k]) / norm)
            both = jnp.concatenate(parts, axis=0).astype(jnp.bfloat16)
            row_ref[k * rows + r : k * rows + r + 16] = both[:, : 3 * rows]
        norm = tap_norm(SIGMAS[k], order_ref[1, k])
        pattern = tap_values(shift, SIGMAS[k], order_ref[1, k]) / norm
        for r in range(0, 2 * LANES, 16):
            parts = []
            for half in (r, r + 8):
                moved_on = pltpu.roll(pattern, half % LANES, 1) if half % LANES else pattern
                inside = lane <= half + 7 if half < LANES else lane >= half - LANES + LANES // 2
                parts.append(jnp.where(inside, moved_on, 0.0))
            col_ref[k, r : r + 16] = jnp.concatenate(parts, axis=0).astype(jnp.bfloat16)


def image_blocks(ref, size, shift, chunk):
    first = chunk + LANES if joint(shift, size) else 0
    return lambda b: ref[:, first + b * LANES : first + (b + 1) * LANES].astype(jnp.float32)


def fit_kernel(weight_ref, hits_ref, row_band_ref, col_band_ref, own_ref, near_ref, far_ref, *refs, width):
    *image_refs, conv_ref, sums_ref, row_ref, parts_ref = refs
    image_refs = dict(zip(far_first(len(image_refs)), image_refs))
    tile_at = lax.axis_index("tile")
    expo_at = lax.axis_index("expo")
    rows, ext = own_ref.shape
    expos = len(image_refs)
    chunk = ext - LANES
    blocks = chunk // LANES

    patch = jnp.concatenate([own_ref[...], near_ref[...], far_ref[...]], axis=0)
    row_ref[...] = jnp.dot(
        row_band_ref[...], patch, preferred_element_type=jnp.float32
    ).astype(jnp.bfloat16)
    for k in range(NB):
        window = jnp.concatenate(
            [
                row_ref[k * rows : (k + 1) * rows, b * LANES : (b + 2) * LANES]
                for b in range(blocks)
            ],
            axis=0,
        )
        out = jnp.dot(window, col_band_ref[k], preferred_element_type=jnp.float32)
        conv_ref[k] = out.reshape(blocks, rows, LANES)

    first_col = expo_at * chunk
    xs = [column_positions(first_col, b, width) for b in range(blocks)]

    def fold(x):
        total = x[:8]
        for i in range(8, rows, 8):
            total = total + x[i : i + 8]
        return total

    def moments(at, left, right, count):
        total = [None] * count
        for b in range(blocks):
            term = fold(left(b) * right(b)) if right is not None else fold(left(b))
            for i in range(count):
                total[i] = term if total[i] is None else total[i] + term
                if i < count - 1:
                    term = term * xs[b]
        for i in range(count):
            parts_ref[at + i] = total[i]

    def conv(k):
        return lambda b: conv_ref[k, b]

    def sci(shift):
        return image_blocks(image_refs[shift], expos, shift, chunk)

    blank = jnp.zeros((8, LANES), jnp.float32)
    at = 0
    for j, k in PAIRS:
        moments(at, conv(j), conv(k), 3)
        at += 3
    for k in range(NB):
        moments(at, conv(k), None, 2)
        at += 2
    while at % 8:
        parts_ref[at] = blank
        at += 1
    begin = at
    for shift in range(expos):
        row = at + NU * source(expo_at, shift, expos)
        for k in range(NB):
            moments(row + 2 * k, conv(k), sci(shift), 2)
        moments(row + NU - 1, sci(shift), None, 1)
    at += NU * expos
    weight = jnp.broadcast_to(weight_ref[...] * hits_ref[...].astype(jnp.float32), (8, LANES))
    weight = jnp.where(tile_at == 0, weight, 0.0)
    spot = (
        (lax.broadcasted_iota(jnp.int32, (8, LANES), 0) == 0)
        & (lax.broadcasted_iota(jnp.int32, (8, LANES), 1) == 0)
    )
    for e in range(expos):
        parts_ref[at + e] = jnp.where(spot & (expo_at == e), weight, 0.0)
    at += expos
    while at % 8:
        parts_ref[at] = blank
        at += 1
    ones = jnp.ones((8, LANES), jnp.float32)
    rows_of = []
    for first, last in ((0, begin), (begin, at)):
        lanes = jnp.sum(parts_ref[first:last], axis=1)
        spare = LANES - (last - first)
        if spare:
            lanes = jnp.concatenate([lanes, jnp.zeros((spare, LANES), jnp.float32)], axis=0)
        rows_of.append(
            lax.dot_general(
                ones,
                lanes,
                (((1,), (1,)), ((), ())),
                precision=lax.Precision.HIGHEST,
                preferred_element_type=jnp.float32,
            )
        )
    both = jnp.where(lax.broadcasted_iota(jnp.int32, (8, LANES), 0) < 4, rows_of[0], rows_of[1])
    for i in range(sums_ref.shape[0]):
        sums_ref[i] = both


def table(expos):
    columns = np.zeros((NU + expos + 1, 16), np.int32)
    for at, (j, k) in enumerate(PAIRS):
        for a, b in ((j, k), (k, j)):
            columns[b, a] = 3 * at
            columns[NB + b, a] = columns[b, NB + a] = 3 * at + 1
            columns[NB + b, NB + a] = 3 * at + 2
    for k in range(NB):
        for x in range(2):
            columns[NU - 1, x * NB + k] = columns[x * NB + k, NU - 1] = 3 * len(PAIRS) + 2 * k + x
    for e in range(expos):
        columns[NU + e, :NU] = [NU * e + 2 * k + x for x in range(2) for k in range(NB)] + [NU * e + NU - 1]
        columns[NU + expos, e] = NU * expos + e
    return np.ascontiguousarray(np.broadcast_to(columns[:, :, None], columns.shape + (LANES,)))


def solve_kernel(table_ref, sums_ref, conv_ref, *refs, width, pixels):
    *image_refs, coadd_ref, coeffs_ref, tile_ref, sems = refs
    expo_at = lax.axis_index("expo")
    expos = len(image_refs)
    rows, chunk = coadd_ref.shape
    blocks = chunk // LANES
    images = [image_blocks(ref, expos, shift, chunk) for shift, ref in enumerate(image_refs)]
    sub = lax.broadcasted_iota(jnp.int32, (16, LANES), 0)
    lane = lax.broadcasted_iota(jnp.int32, (16, LANES), 1)
    sums = sums_ref[0]
    for i in range(1, sums_ref.shape[0]):
        sums = sums + sums_ref[i]
    first = jnp.broadcast_to(sums[0:1], (16, LANES))
    second = jnp.broadcast_to(sums[4:5], (16, LANES))

    columns = [
        jnp.take_along_axis(first if j < NU else second, table_ref[j], axis=1) for j in range(NU + expos)
    ]
    spread = jnp.take_along_axis(second, table_ref[NU + expos], axis=1)
    weight = [jnp.broadcast_to(spread[e : e + 1], (16, LANES)) for e in range(expos)]
    columns[NU - 1] = jnp.where(sub == NU - 1, float(pixels), columns[NU - 1])

    trace = columns[0][0:1]
    for j in range(1, NU):
        trace = trace + columns[j][j : j + 1]
    scale = 1.0 / trace
    for j in range(NU + expos):
        columns[j] = columns[j] * scale
        if j < NU:
            columns[j] = columns[j] + jnp.where(sub == j, RIDGE / NU, 0.0)
    for i in range(NU):
        inverse = 1.0 / columns[i][i : i + 1]
        for j in range(i + 1, NU + expos):
            factor = columns[j][i : i + 1] * inverse
            columns[j] = jnp.where(sub == i, factor, columns[j] - columns[i] * factor)

    solved = columns[NU:]
    own = solved[0]
    mixed = weight[0] * solved[0]
    for e in range(1, expos):
        own = jnp.where(expo_at == e, solved[e], own)
        mixed = mixed + weight[e] * solved[e]
    diagonal = (sub == lane) & (sub < NU)
    coeffs_ref[...] = jnp.sum(jnp.where(diagonal, own, 0.0), axis=0, keepdims=True)[:, :NU]
    scale = [jnp.broadcast_to(mixed[u : u + 1], (8, LANES)) for u in range(NU)]
    gains = []
    for shift in range(expos):
        gain = weight[0][:8]
        for e in range(1, expos):
            gain = jnp.where(source(expo_at, shift, expos) == e, weight[e][:8], gain)
        gains.append(gain)
    first_col = expo_at * chunk
    copies = []
    for r in range(0, rows, 8):
        for b in range(blocks):
            x = column_positions(first_col, b, width)
            total = -scale[NU - 1]
            for gain, image in zip(gains, images):
                total = total + gain * image(b)[r : r + 8]
            model = (scale[0] + scale[NB] * x) * conv_ref[0, b, r : r + 8]
            for k in range(1, NB):
                model = model + (scale[k] + scale[NB + k] * x) * conv_ref[k, b, r : r + 8]
            tile_ref[r : r + 8, b * LANES : (b + 1) * LANES] = total - model
        copies.append(
            pltpu.make_async_copy(tile_ref.at[pl.ds(r, 8)], coadd_ref.at[pl.ds(r, 8)], sems.at[r // 8])
        )
        copies[-1].start()
    for copy in copies:
        copy.wait()


def swaps(first, size):
    pairs = [(i, i + 1) for i in range(first, size - 1, 2)]
    if first and size % 2 == 0:
        pairs.append((0, size - 1))
    return [pair for a, b in pairs for pair in ((a, b), (b, a))]


def service_order(expos, tiles):
    early = list(range(tiles // 2))
    late = list(reversed(range(expos // 2 * tiles, expos * tiles)))
    return early + [i for i in late if i not in early] + list(range(len(early), expos // 2 * tiles))


def tiled_device(template, science, plan, orders, coadd_weight, intersection):
    expos = lax.axis_size("expo")
    tiles = lax.axis_size("tile")
    _, rows, width = template.shape
    steps = science.shape[1]
    chunk = width // expos
    ext = chunk + LANES
    blocks = chunk // LANES
    vmem = pl.BlockSpec(memory_space=pltpu.VMEM)
    small = pltpu.CompilerParams(vmem_limit_bytes=16 * 1024 * 1024)
    hbm = pl.BlockSpec(memory_space=pltpu.HBM)
    coadds = []
    fitted = []
    for step in range(steps):
        *blocks_out, owner, order = pl.pallas_call(
            functools.partial(send_kernel, step=step),
            out_shape=tuple(
                pltpu.VMEM((rows, ext + chunk if joint(shift, expos) else ext), template.dtype)
                for shift in range(expos)
            )
            + (pltpu.VMEM((rows, ext), science.dtype),) * (expos - expos // 2)
            + (
                jax.ShapeDtypeStruct((rows, LANES), jnp.int32),
                jax.ShapeDtypeStruct((2, NB, 8, LANES), jnp.int32),
            ),
            in_specs=[hbm] * 4,
            out_specs=(vmem,) * (2 * expos - expos // 2 + 2),
            scratch_shapes=[
                pltpu.VMEM((rows, width + 2 * LANES), template.dtype),
                pltpu.SMEM(plan.shape, jnp.int32),
                pltpu.SMEM((2, NB), jnp.int32),
                pltpu.SemaphoreType.DMA((expos + 4,)),
            ],
            compiler_params=small,
        )(
            pltpu.with_memory_space_constraint(template[0], pltpu.HBM),
            pltpu.with_memory_space_constraint(science[0, step], pltpu.HBM),
            pltpu.with_memory_space_constraint(plan, pltpu.HBM),
            pltpu.with_memory_space_constraint(orders.T, pltpu.HBM),
        )
        patches, images = blocks_out[:expos], blocks_out[expos:]
        for group, first in ((patches, 0), (images, expos // 2)):
            for shift in range(max(first, 1), expos):
                pairs = [(e, int(target(e, shift, expos))) for e in range(expos)]
                group[shift - first] = lax.ppermute(group[shift - first], "expo", pairs)
        images = patches[: expos // 2] + images
        across = [shift for shift in far_first(expos)[:-1] if not joint(shift, expos)]
        beside = [shift for shift in far_first(expos)[:-1] if joint(shift, expos)]
        block = pl.pallas_call(
            functools.partial(choose_kernel, shifts=across, size=expos),
            out_shape=jax.ShapeDtypeStruct((rows, ext), template.dtype),
            in_specs=[vmem] * (2 + len(across)),
            out_specs=vmem,
            compiler_params=small,
            cost_estimate=pl.CostEstimate(flops=STAGE_COST, bytes_accessed=500_000, transcendentals=0),
        )(owner, patches[0], *(patches[shift] for shift in across))
        own = pl.pallas_call(
            functools.partial(pick_kernel, shifts=beside, size=expos),
            out_shape=jax.ShapeDtypeStruct((rows, ext), template.dtype),
            in_specs=[vmem] * (2 + len(beside)),
            out_specs=vmem,
            scratch_shapes=[pltpu.VMEM((rows, ext), template.dtype)],
            compiler_params=small,
        )(owner, block, *(patches[shift] for shift in beside))
        row_band, col_band = pl.pallas_call(
            functools.partial(band_kernel, tiles=tiles),
            out_shape=(
                jax.ShapeDtypeStruct((NB * rows, 3 * rows), jnp.bfloat16),
                jax.ShapeDtypeStruct((NB, 2 * LANES, LANES), jnp.bfloat16),
            ),
            in_specs=[vmem, pl.BlockSpec(memory_space=pl.ANY)],
            out_specs=(vmem, vmem),
            compiler_params=small,
            cost_estimate=pl.CostEstimate(flops=4_000_000, bytes_accessed=500_000, transcendentals=200_000),
        )(order, own)
        far = lax.ppermute(own, "tile", swaps(1, tiles))
        near = lax.ppermute(own, "tile", swaps(0, tiles))
        conv, sums = pl.pallas_call(
            functools.partial(fit_kernel, width=width),
            out_shape=(
                jax.ShapeDtypeStruct((NB, blocks, rows, LANES), jnp.float32),
                jax.ShapeDtypeStruct((tiles * expos, 8, LANES), jnp.float32),
            ),
            in_specs=[vmem] * (7 + expos),
            out_specs=(vmem, vmem),
            scratch_shapes=[
                pltpu.VMEM((NB * rows, ext), jnp.bfloat16),
                pltpu.VMEM((80 + 14 * expos + 8, 8, LANES), jnp.float32),
            ],
            compiler_params=small,
        )(
            coadd_weight[:, step : step + 1],
            intersection[:, step : step + 1],
            row_band,
            col_band,
            own,
            near,
            far,
            *(images[shift] for shift in far_first(expos)),
        )
        group = list(reversed(service_order(expos, tiles)))
        sums = lax.all_to_all(
            sums, ("expo", "tile"), split_axis=0, concat_axis=0, tiled=True, axis_index_groups=[group]
        )
        coadd, coeffs = pl.pallas_call(
            functools.partial(solve_kernel, width=width, pixels=tiles * rows * width),
            out_shape=(
                jax.ShapeDtypeStruct((rows, chunk), jnp.float32),
                jax.ShapeDtypeStruct((1, NU), jnp.float32),
            ),
            in_specs=[vmem] * (3 + expos),
            out_specs=(pl.BlockSpec(memory_space=pl.ANY), vmem),
            scratch_shapes=[
                pltpu.VMEM((rows, chunk), jnp.float32),
                pltpu.SemaphoreType.DMA((rows // 8,)),
            ],
            compiler_params=small,
        )(jnp.asarray(table(expos)), sums, conv, *images)
        coadds.append(coadd[None])
        fitted.append(coeffs)
    return (jnp.concatenate(coadds), jnp.stack(fitted, axis=1))


def broadcast(block, axis, holder):
    block = jnp.where(lax.axis_index(axis) == holder, block, jnp.zeros_like(block))
    return lax.psum(block, axis)


def extended(x, sides, width):
    for axis, dim in sides:
        size, length = (lax.axis_size(axis), x.shape[dim])
        up = [(i, (i + 1) % size) for i in range(size - 1)]
        down = [(j, i) for i, j in up]
        last = lax.slice_in_dim(x, length - width, length, axis=dim)
        first = lax.slice_in_dim(x, 0, width, axis=dim)
        before = lax.ppermute(last, axis, up)
        after = lax.ppermute(first, axis, down)
        x = jnp.concatenate([before, x, after], axis=dim)
    return x


def make_filters(orders):
    taps_pos = jnp.arange(2 * HALF + 1).astype(jnp.float32) - HALF
    row_list = []
    col_list = []
    for basis in range(NB):
        sigma = SIGMAS[basis]
        envelope = jnp.exp(-taps_pos * taps_pos / (2.0 * sigma * sigma))
        row_filter = envelope * power_of(taps_pos, orders[basis, 0])
        col_filter = envelope * power_of(taps_pos, orders[basis, 1])
        row_list.append(row_filter / jnp.sqrt(jnp.sum(row_filter * row_filter)))
        col_list.append(col_filter / jnp.sqrt(jnp.sum(col_filter * col_filter)))
    return (jnp.stack(row_list).astype(jnp.bfloat16), jnp.stack(col_list).astype(jnp.bfloat16))


def band_matrix(filters, out_len, in_len):
    offset = jnp.arange(in_len)[None, :] - jnp.arange(out_len)[:, None]
    taps_idx = jnp.arange(2 * HALF + 1)
    picks = (offset[:, :, None] == taps_idx[None, None, :]).astype(jnp.float32)
    band = jnp.einsum("ijt,kt->kij", picks, filters.astype(jnp.float32))
    return band.astype(jnp.bfloat16)


def any_device(template, science, plan, orders, coadd_weight, intersection):
    row_filters, col_filters = make_filters(orders)
    rows = template.shape[1]
    width = template.shape[2]
    blocks_count = width // 128
    steps_count = science.shape[1]
    row_band = band_matrix(row_filters, rows, rows + 2 * HALF)
    col_band = jnp.transpose(band_matrix(col_filters, 128, 128 + 2 * HALF), (0, 2, 1))
    column_pos = 2.0 * (jnp.arange(width).astype(jnp.float32) + 0.5) / width - 1.0
    pieces = []
    fitted = []
    for step in range(steps_count):
        received = broadcast(template[0], "expo", plan[step])
        padded = extended(received, (("tile", 0),), HALF)
        rowconv = jnp.einsum(
            "kij,jw->kiw", row_band, padded, preferred_element_type=jnp.float32
        ).astype(jnp.bfloat16)
        blocks = rowconv.reshape(NB, rows, blocks_count, 128)
        empty_rim = jnp.zeros((NB, rows, 1, HALF), jnp.bfloat16)
        previous = jnp.concatenate([empty_rim, blocks[:, :, :-1, 128 - HALF :]], axis=2)
        following = jnp.concatenate([blocks[:, :, 1:, :HALF], empty_rim], axis=2)
        window = jnp.concatenate([previous, blocks, following], axis=3)
        conv = jnp.einsum("krbj,kjc->krbc", window, col_band, preferred_element_type=jnp.float32)
        conv = conv.reshape(NB, rows, width)
        fields = jnp.concatenate(
            [conv, conv * column_pos, jnp.ones((1, rows, width), jnp.float32)], axis=0
        )
        fields = fields.reshape(NU, rows * width)
        exposure_image = science[0, step].astype(jnp.float32).reshape(rows * width)
        normal_local = jnp.dot(fields, fields.T, precision=lax.Precision.HIGHEST)
        project_local = jnp.dot(fields, exposure_image, precision=lax.Precision.HIGHEST)
        normal_matrix, projections = lax.psum((normal_local, project_local), "tile")
        normal_matrix = normal_matrix + RIDGE * (jnp.trace(normal_matrix) / NU) * jnp.eye(
            NU, dtype=jnp.float32
        )
        factor = jnp.linalg.cholesky(normal_matrix)
        coeffs = jax.scipy.linalg.cho_solve((factor, True), projections)
        model = jnp.dot(coeffs, fields, precision=lax.Precision.HIGHEST)
        difference = exposure_image - model
        weight_now = coadd_weight[0, step] * intersection[0, step].astype(jnp.float32)
        pieces.append((weight_now * difference).reshape(rows, width))
        fitted.append(coeffs)
    weighted = jnp.stack(pieces)
    received_parts = lax.all_to_all(weighted[None], "expo", split_axis=3, concat_axis=0, tiled=True)
    coadd = jnp.sum(received_parts, axis=0)
    return (coadd, jnp.stack(fitted)[None])


def per_device(template, science, plan, orders, coadd_weight, intersection):
    expos = lax.axis_size("expo")
    rows, width = template.shape[1:]
    whole_lanes = width % (expos * LANES) == 0 and rows % 16 == 0 and 3 * rows <= LANES
    few = (NU + 1) * expos <= LANES and NU + expos <= LANES
    body = tiled_device if whole_lanes and few else any_device
    return body(template, science, plan, orders, coadd_weight, intersection)


def solution(mesh):
    return jax.shard_map(
        per_device,
        mesh=mesh,
        in_specs=(
            P(("groups", "expo"), "tile", None),
            P(("groups", "expo"), None, "tile", None),
            P("groups"),
            P(),
            P(("groups", "expo"), None),
            P(("groups", "expo"), None),
        ),
        out_specs=(P("groups", "tile", "expo"), P(("groups", "expo"), None, None)),
        check_vma=False,
    )
```

```python
import functools

import jax
import jax.numpy as jnp
import numpy as np
from jax import lax
from jax.experimental import pallas as pl
from jax.experimental.pallas import tpu as pltpu
from jax.sharding import PartitionSpec as P

HALF = 15
NB = 6
NU = 13
LANES = 128
BEYOND = 1000
STAGE_COST = 700_000_000
PAIRS = [(j, k) for j in range(NB) for k in range(j, NB)]

SIGMAS = (0.8, 1.4, 2.2, 3.0, 4.0, 5.5)
RIDGE = 0.05


def power_of(pos, order):
    return jnp.where(order == 0, 1.0, jnp.where(order == 1, pos, pos * pos))


def tap_values(pos, sigma, order):
    value = jnp.exp(-pos * pos / (2.0 * sigma * sigma)) * power_of(pos, order)
    return jnp.where(jnp.abs(pos) <= HALF, value, 0.0)


def tap_norm(sigma, order):
    pos = lax.broadcasted_iota(jnp.int32, (8, LANES), 1).astype(jnp.float32) - HALF
    value = tap_values(pos, sigma, order)
    return jnp.sqrt(jnp.sum(value * value, axis=1, keepdims=True))


def target(me, shift, size):
    return me ^ shift if size & (size - 1) == 0 else (me + shift) % size


def source(me, shift, size):
    return me ^ shift if size & (size - 1) == 0 else (me - shift + size) % size


def far_first(size):
    return [*range(size // 2, size), *range(1, size // 2), 0] if size > 1 else [0]


def joint(shift, size):
    return shift < size // 2


def send_kernel(template_ref, science_ref, plan_ref, orders_ref, *refs, step):
    *out_refs, owner_ref, order_ref, patch_ref, plan_now, orders_now, sems = refs
    size = sems.shape[0] - 4
    rows, width = science_ref.shape
    chunk = width // size
    ext = chunk + LANES
    patch_refs, image_refs = out_refs[:size], out_refs[size:]
    half = size * chunk // 2
    me = lax.axis_index("expo")
    starts = [pl.multiple_of(target(me, shift, size) * chunk, chunk) for shift in range(size)]
    loads = [
        pltpu.make_async_copy(
            template_ref.at[:, pl.ds(i * half, half)], patch_ref.at[:, pl.ds((i * half + LANES), half)], sems.at[i]
        )
        for i in range(2)
    ]
    copies = [
        pltpu.make_async_copy(
            science_ref.at[:, pl.ds(starts[shift], chunk)],
            patch_refs[shift].at[:, pl.ds(ext, chunk)]
            if joint(shift, size)
            else image_refs[shift - size // 2].at[:, pl.ds(0, chunk)],
            sems.at[3 + shift],
        )
        for shift in range(size)
    ]
    copies.append(pltpu.make_async_copy(plan_ref, plan_now, sems.at[2]))
    copies.append(pltpu.make_async_copy(orders_ref, orders_now, sems.at[3 + size]))
    for copy in loads + copies:
        copy.start()
    blank = jnp.zeros((rows, LANES), patch_ref.dtype)
    patch_ref[:, :LANES] = blank
    patch_ref[:, size * chunk + LANES :] = blank
    for image_ref in image_refs:
        image_ref[:, chunk:] = blank
    for copy in loads:
        copy.wait()
    lane = lax.broadcasted_iota(jnp.int32, (rows, LANES), 1)
    for shift in range(size):
        start = starts[shift]
        patch_refs[shift][:, :chunk] = patch_ref[:, pl.ds(start + LANES, chunk)]
        before = patch_ref[:, pl.ds(start, LANES)].astype(jnp.float32)
        after = patch_ref[:, pl.ds(start + chunk + LANES, LANES)].astype(jnp.float32)
        rim = jnp.where(lane < LANES // 2, after, before)
        patch_refs[shift][:, chunk:ext] = rim.astype(patch_ref.dtype)
    for copy in copies:
        copy.wait()
    owner_ref[...] = jnp.full(owner_ref.shape, plan_now[step], jnp.int32)
    for way in range(2):
        for k in range(NB):
            order_ref[way, k] = jnp.full((8, LANES), orders_now[way, k], jnp.int32)


def choose_kernel(owner_ref, *refs, shifts, size):
    *recv_refs, out_ref = refs
    me = lax.axis_index("expo")
    for b in range(out_ref.shape[1] // LANES):
        columns = slice(b * LANES, (b + 1) * LANES)
        block = recv_refs[0][:, columns].astype(jnp.float32)
        for shift, ref in zip(shifts, recv_refs[1:]):
            block = jnp.where(
                owner_ref[...] == source(me, shift, size), ref[:, columns].astype(jnp.float32), block
            )
        out_ref[:, columns] = block.astype(out_ref.dtype)


def pick_kernel(owner_ref, *refs, shifts, size):
    *recv_refs, out_ref, block_ref = refs
    ext = out_ref.shape[1]
    choose_kernel(owner_ref, *recv_refs, block_ref, shifts=shifts, size=size)
    whole = jnp.concatenate([block_ref[:, ext - LANES :], block_ref[...]], axis=1)
    out_ref[...] = whole[:, LANES - HALF : LANES - HALF + ext]


def column_positions(first_col, block, width):
    col = lax.broadcasted_iota(jnp.int32, (8, LANES), 1) + (first_col + block * LANES)
    return 2.0 * (col.astype(jnp.float32) + 0.5) / width - 1.0


def band_kernel(order_ref, _, row_ref, col_ref, *, tiles):
    rows = row_ref.shape[0] // NB
    tile_at = lax.axis_index("tile")
    near = 1 - 2 * lax.rem(tile_at, 2)
    near_move = jnp.where(tile_at + near < tiles, near - 1, BEYOND)
    far_move = jnp.where((tile_at >= near) & (tile_at - near < tiles), -near - 2, BEYOND)
    row_from = lax.broadcasted_iota(jnp.int32, (8, LANES), 1)
    moved = jnp.where(row_from < rows, 0, jnp.where(row_from < 2 * rows, near_move, far_move))
    sub = lax.broadcasted_iota(jnp.int32, (8, LANES), 0)
    lane = lax.broadcasted_iota(jnp.int32, (8, LANES), 1)
    shift = (sub - jnp.where(lane < LANES // 2, lane, lane - LANES) - HALF).astype(jnp.float32)
    for k in range(NB):
        norm = tap_norm(SIGMAS[k], order_ref[0, k])
        for r in range(0, rows, 16):
            parts = []
            for half in (r, r + 8):
                offset = (row_from + moved * rows - sub - half).astype(jnp.float32)
                parts.append(tap_values(offset, SIGMAS[k], order_ref[0, k]) / norm)
            both = jnp.concatenate(parts, axis=0).astype(jnp.bfloat16)
            row_ref[k * rows + r : k * rows + r + 16] = both[:, : 3 * rows]
        norm = tap_norm(SIGMAS[k], order_ref[1, k])
        pattern = tap_values(shift, SIGMAS[k], order_ref[1, k]) / norm
        for r in range(0, 2 * LANES, 16):
            parts = []
            for half in (r, r + 8):
                moved_on = pltpu.roll(pattern, half % LANES, 1) if half % LANES else pattern
                inside = lane <= half + 7 if half < LANES else lane >= half - LANES + LANES // 2
                parts.append(jnp.where(inside, moved_on, 0.0))
            col_ref[k, r : r + 16] = jnp.concatenate(parts, axis=0).astype(jnp.bfloat16)


def image_blocks(ref, size, shift, chunk):
    first = chunk + LANES if joint(shift, size) else 0
    return lambda b: ref[:, first + b * LANES : first + (b + 1) * LANES].astype(jnp.float32)


def fit_kernel(weight_ref, hits_ref, row_band_ref, col_band_ref, own_ref, near_ref, far_ref, *refs, width):
    *image_refs, conv_ref, sums_ref, row_ref, parts_ref = refs
    image_refs = dict(zip(far_first(len(image_refs)), image_refs))
    tile_at = lax.axis_index("tile")
    expo_at = lax.axis_index("expo")
    rows, ext = own_ref.shape
    expos = len(image_refs)
    chunk = ext - LANES
    blocks = chunk // LANES

    patch = jnp.concatenate([own_ref[...], near_ref[...], far_ref[...]], axis=0)
    row_ref[...] = jnp.dot(
        row_band_ref[...], patch, preferred_element_type=jnp.float32
    ).astype(jnp.bfloat16)
    for k in range(NB):
        window = jnp.concatenate(
            [
                row_ref[k * rows : (k + 1) * rows, b * LANES : (b + 2) * LANES]
                for b in range(blocks)
            ],
            axis=0,
        )
        out = jnp.dot(window, col_band_ref[k], preferred_element_type=jnp.float32)
        conv_ref[k] = out.reshape(blocks, rows, LANES)

    first_col = expo_at * chunk
    xs = [column_positions(first_col, b, width) for b in range(blocks)]

    def fold(x):
        total = x[:8]
        for i in range(8, rows, 8):
            total = total + x[i : i + 8]
        return total

    def moments(at, left, right, count):
        total = [None] * count
        for b in range(blocks):
            term = fold(left(b) * right(b)) if right is not None else fold(left(b))
            for i in range(count):
                total[i] = term if total[i] is None else total[i] + term
                if i < count - 1:
                    term = term * xs[b]
        for i in range(count):
            parts_ref[at + i] = total[i]

    def conv(k):
        return lambda b: conv_ref[k, b]

    def sci(shift):
        return image_blocks(image_refs[shift], expos, shift, chunk)

    blank = jnp.zeros((8, LANES), jnp.float32)
    at = 0
    for j, k in PAIRS:
        moments(at, conv(j), conv(k), 3)
        at += 3
    for k in range(NB):
        moments(at, conv(k), None, 2)
        at += 2
    while at % 8:
        parts_ref[at] = blank
        at += 1
    begin = at
    for shift in range(expos):
        row = at + NU * source(expo_at, shift, expos)
        for k in range(NB):
            moments(row + 2 * k, conv(k), sci(shift), 2)
        moments(row + NU - 1, sci(shift), None, 1)
    at += NU * expos
    weight = jnp.broadcast_to(weight_ref[...] * hits_ref[...].astype(jnp.float32), (8, LANES))
    weight = jnp.where(tile_at == 0, weight, 0.0)
    spot = (
        (lax.broadcasted_iota(jnp.int32, (8, LANES), 0) == 0)
        & (lax.broadcasted_iota(jnp.int32, (8, LANES), 1) == 0)
    )
    for e in range(expos):
        parts_ref[at + e] = jnp.where(spot & (expo_at == e), weight, 0.0)
    at += expos
    while at % 8:
        parts_ref[at] = blank
        at += 1
    ones = jnp.ones((8, LANES), jnp.float32)
    rows_of = []
    for first, last in ((0, begin), (begin, at)):
        lanes = jnp.sum(parts_ref[first:last], axis=1)
        spare = LANES - (last - first)
        if spare:
            lanes = jnp.concatenate([lanes, jnp.zeros((spare, LANES), jnp.float32)], axis=0)
        rows_of.append(
            lax.dot_general(
                ones,
                lanes,
                (((1,), (1,)), ((), ())),
                precision=lax.Precision.HIGHEST,
                preferred_element_type=jnp.float32,
            )
        )
    both = jnp.where(lax.broadcasted_iota(jnp.int32, (8, LANES), 0) < 4, rows_of[0], rows_of[1])
    for i in range(sums_ref.shape[0]):
        sums_ref[i] = both


def table(expos):
    columns = np.zeros((NU + expos + 1, 16), np.int32)
    for at, (j, k) in enumerate(PAIRS):
        for a, b in ((j, k), (k, j)):
            columns[b, a] = 3 * at
            columns[NB + b, a] = columns[b, NB + a] = 3 * at + 1
            columns[NB + b, NB + a] = 3 * at + 2
    for k in range(NB):
        for x in range(2):
            columns[NU - 1, x * NB + k] = columns[x * NB + k, NU - 1] = 3 * len(PAIRS) + 2 * k + x
    for e in range(expos):
        columns[NU + e, :NU] = [NU * e + 2 * k + x for x in range(2) for k in range(NB)] + [NU * e + NU - 1]
        columns[NU + expos, e] = NU * expos + e
    return np.ascontiguousarray(np.broadcast_to(columns[:, :, None], columns.shape + (LANES,)))


def solve_kernel(table_ref, sums_ref, conv_ref, *refs, width, pixels):
    *image_refs, coadd_ref, coeffs_ref, tile_ref, sems = refs
    expo_at = lax.axis_index("expo")
    expos = len(image_refs)
    rows, chunk = coadd_ref.shape
    blocks = chunk // LANES
    images = [image_blocks(ref, expos, shift, chunk) for shift, ref in enumerate(image_refs)]
    sub = lax.broadcasted_iota(jnp.int32, (16, LANES), 0)
    lane = lax.broadcasted_iota(jnp.int32, (16, LANES), 1)
    sums = sums_ref[0]
    for i in range(1, sums_ref.shape[0]):
        sums = sums + sums_ref[i]
    first = jnp.broadcast_to(sums[0:1], (16, LANES))
    second = jnp.broadcast_to(sums[4:5], (16, LANES))

    columns = [
        jnp.take_along_axis(first if j < NU else second, table_ref[j], axis=1) for j in range(NU + expos)
    ]
    spread = jnp.take_along_axis(second, table_ref[NU + expos], axis=1)
    weight = [jnp.broadcast_to(spread[e : e + 1], (16, LANES)) for e in range(expos)]
    columns[NU - 1] = jnp.where(sub == NU - 1, float(pixels), columns[NU - 1])

    trace = columns[0][0:1]
    for j in range(1, NU):
        trace = trace + columns[j][j : j + 1]
    scale = 1.0 / trace
    for j in range(NU + expos):
        columns[j] = columns[j] * scale
        if j < NU:
            columns[j] = columns[j] + jnp.where(sub == j, RIDGE / NU, 0.0)
    for i in range(NU):
        inverse = 1.0 / columns[i][i : i + 1]
        for j in range(i + 1, NU + expos):
            factor = columns[j][i : i + 1] * inverse
            columns[j] = jnp.where(sub == i, factor, columns[j] - columns[i] * factor)

    solved = columns[NU:]
    own = solved[0]
    mixed = weight[0] * solved[0]
    for e in range(1, expos):
        own = jnp.where(expo_at == e, solved[e], own)
        mixed = mixed + weight[e] * solved[e]
    diagonal = (sub == lane) & (sub < NU)
    coeffs_ref[...] = jnp.sum(jnp.where(diagonal, own, 0.0), axis=0, keepdims=True)[:, :NU]
    scale = [jnp.broadcast_to(mixed[u : u + 1], (8, LANES)) for u in range(NU)]
    gains = []
    for shift in range(expos):
        gain = weight[0][:8]
        for e in range(1, expos):
            gain = jnp.where(source(expo_at, shift, expos) == e, weight[e][:8], gain)
        gains.append(gain)
    first_col = expo_at * chunk
    copies = []
    for r in range(0, rows, 8):
        for b in range(blocks):
            x = column_positions(first_col, b, width)
            total = -scale[NU - 1]
            for gain, image in zip(gains, images):
                total = total + gain * image(b)[r : r + 8]
            model = (scale[0] + scale[NB] * x) * conv_ref[0, b, r : r + 8]
            for k in range(1, NB):
                model = model + (scale[k] + scale[NB + k] * x) * conv_ref[k, b, r : r + 8]
            tile_ref[r : r + 8, b * LANES : (b + 1) * LANES] = total - model
        copies.append(
            pltpu.make_async_copy(tile_ref.at[pl.ds(r, 8)], coadd_ref.at[pl.ds(r, 8)], sems.at[r // 8])
        )
        copies[-1].start()
    for copy in copies:
        copy.wait()


def swaps(first, size):
    pairs = [(i, i + 1) for i in range(first, size - 1, 2)]
    if first and size % 2 == 0:
        pairs.append((0, size - 1))
    return [pair for a, b in pairs for pair in ((a, b), (b, a))]


def service_order(expos, tiles):
    early = list(range(tiles // 2))
    late = list(reversed(range(expos // 2 * tiles, expos * tiles)))
    return early + [i for i in late if i not in early] + list(range(len(early), expos // 2 * tiles))


def tiled_device(template, science, plan, orders, coadd_weight, intersection):
    expos = lax.axis_size("expo")
    tiles = lax.axis_size("tile")
    _, rows, width = template.shape
    steps = science.shape[1]
    chunk = width // expos
    ext = chunk + LANES
    blocks = chunk // LANES
    vmem = pl.BlockSpec(memory_space=pltpu.VMEM)
    small = pltpu.CompilerParams(vmem_limit_bytes=16 * 1024 * 1024)
    hbm = pl.BlockSpec(memory_space=pltpu.HBM)
    coadds = []
    fitted = []
    for step in range(steps):
        *blocks_out, owner, order = pl.pallas_call(
            functools.partial(send_kernel, step=step),
            out_shape=tuple(
                pltpu.VMEM((rows, ext + chunk if joint(shift, expos) else ext), template.dtype)
                for shift in range(expos)
            )
            + (pltpu.VMEM((rows, ext), science.dtype),) * (expos - expos // 2)
            + (
                jax.ShapeDtypeStruct((rows, LANES), jnp.int32),
                jax.ShapeDtypeStruct((2, NB, 8, LANES), jnp.int32),
            ),
            in_specs=[hbm] * 4,
            out_specs=(vmem,) * (2 * expos - expos // 2 + 2),
            scratch_shapes=[
                pltpu.VMEM((rows, width + 2 * LANES), template.dtype),
                pltpu.SMEM(plan.shape, jnp.int32),
                pltpu.SMEM((2, NB), jnp.int32),
                pltpu.SemaphoreType.DMA((expos + 4,)),
            ],
            compiler_params=small,
        )(
            pltpu.with_memory_space_constraint(template[0], pltpu.HBM),
            pltpu.with_memory_space_constraint(science[0, step], pltpu.HBM),
            pltpu.with_memory_space_constraint(plan, pltpu.HBM),
            pltpu.with_memory_space_constraint(orders.T, pltpu.HBM),
        )
        patches, images = blocks_out[:expos], blocks_out[expos:]
        for group, first in ((patches, 0), (images, expos // 2)):
            for shift in range(max(first, 1), expos):
                pairs = [(e, int(target(e, shift, expos))) for e in range(expos)]
                group[shift - first] = lax.ppermute(group[shift - first], "expo", pairs)
        images = patches[: expos // 2] + images
        across = [shift for shift in range(1, expos) if not joint(shift, expos)]
        beside = [shift for shift in range(1, expos) if joint(shift, expos)]
        block = pl.pallas_call(
            functools.partial(choose_kernel, shifts=across, size=expos),
            out_shape=jax.ShapeDtypeStruct((rows, ext), template.dtype),
            in_specs=[vmem] * (2 + len(across)),
            out_specs=vmem,
            compiler_params=small,
            cost_estimate=pl.CostEstimate(flops=STAGE_COST, bytes_accessed=500_000, transcendentals=0),
        )(owner, patches[0], *(patches[shift] for shift in across))
        own = pl.pallas_call(
            functools.partial(pick_kernel, shifts=beside, size=expos),
            out_shape=jax.ShapeDtypeStruct((rows, ext), template.dtype),
            in_specs=[vmem] * (2 + len(beside)),
            out_specs=vmem,
            scratch_shapes=[pltpu.VMEM((rows, ext), template.dtype)],
            compiler_params=small,
        )(owner, block, *(patches[shift] for shift in beside))
        row_band, col_band = pl.pallas_call(
            functools.partial(band_kernel, tiles=tiles),
            out_shape=(
                jax.ShapeDtypeStruct((NB * rows, 3 * rows), jnp.bfloat16),
                jax.ShapeDtypeStruct((NB, 2 * LANES, LANES), jnp.bfloat16),
            ),
            in_specs=[vmem, pl.BlockSpec(memory_space=pl.ANY)],
            out_specs=(vmem, vmem),
            compiler_params=small,
            cost_estimate=pl.CostEstimate(flops=4_000_000, bytes_accessed=500_000, transcendentals=200_000),
        )(order, own)
        far = lax.ppermute(own, "tile", swaps(1, tiles))
        near = lax.ppermute(own, "tile", swaps(0, tiles))
        conv, sums = pl.pallas_call(
            functools.partial(fit_kernel, width=width),
            out_shape=(
                jax.ShapeDtypeStruct((NB, blocks, rows, LANES), jnp.float32),
                jax.ShapeDtypeStruct((tiles * expos, 8, LANES), jnp.float32),
            ),
            in_specs=[vmem] * (7 + expos),
            out_specs=(vmem, vmem),
            scratch_shapes=[
                pltpu.VMEM((NB * rows, ext), jnp.bfloat16),
                pltpu.VMEM((80 + 14 * expos + 8, 8, LANES), jnp.float32),
            ],
            compiler_params=small,
        )(
            coadd_weight[:, step : step + 1],
            intersection[:, step : step + 1],
            row_band,
            col_band,
            own,
            near,
            far,
            *(images[shift] for shift in far_first(expos)),
        )
        group = list(reversed(service_order(expos, tiles)))
        sums = lax.all_to_all(
            sums, ("expo", "tile"), split_axis=0, concat_axis=0, tiled=True, axis_index_groups=[group]
        )
        coadd, coeffs = pl.pallas_call(
            functools.partial(solve_kernel, width=width, pixels=tiles * rows * width),
            out_shape=(
                jax.ShapeDtypeStruct((rows, chunk), jnp.float32),
                jax.ShapeDtypeStruct((1, NU), jnp.float32),
            ),
            in_specs=[vmem] * (3 + expos),
            out_specs=(pl.BlockSpec(memory_space=pl.ANY), vmem),
            scratch_shapes=[
                pltpu.VMEM((rows, chunk), jnp.float32),
                pltpu.SemaphoreType.DMA((rows // 8,)),
            ],
            compiler_params=small,
        )(jnp.asarray(table(expos)), sums, conv, *images)
        coadds.append(coadd[None])
        fitted.append(coeffs)
    return (jnp.concatenate(coadds), jnp.stack(fitted, axis=1))


def broadcast(block, axis, holder):
    block = jnp.where(lax.axis_index(axis) == holder, block, jnp.zeros_like(block))
    return lax.psum(block, axis)


def extended(x, sides, width):
    for axis, dim in sides:
        size, length = (lax.axis_size(axis), x.shape[dim])
        up = [(i, (i + 1) % size) for i in range(size - 1)]
        down = [(j, i) for i, j in up]
        last = lax.slice_in_dim(x, length - width, length, axis=dim)
        first = lax.slice_in_dim(x, 0, width, axis=dim)
        before = lax.ppermute(last, axis, up)
        after = lax.ppermute(first, axis, down)
        x = jnp.concatenate([before, x, after], axis=dim)
    return x


def make_filters(orders):
    taps_pos = jnp.arange(2 * HALF + 1).astype(jnp.float32) - HALF
    row_list = []
    col_list = []
    for basis in range(NB):
        sigma = SIGMAS[basis]
        envelope = jnp.exp(-taps_pos * taps_pos / (2.0 * sigma * sigma))
        row_filter = envelope * power_of(taps_pos, orders[basis, 0])
        col_filter = envelope * power_of(taps_pos, orders[basis, 1])
        row_list.append(row_filter / jnp.sqrt(jnp.sum(row_filter * row_filter)))
        col_list.append(col_filter / jnp.sqrt(jnp.sum(col_filter * col_filter)))
    return (jnp.stack(row_list).astype(jnp.bfloat16), jnp.stack(col_list).astype(jnp.bfloat16))


def band_matrix(filters, out_len, in_len):
    offset = jnp.arange(in_len)[None, :] - jnp.arange(out_len)[:, None]
    taps_idx = jnp.arange(2 * HALF + 1)
    picks = (offset[:, :, None] == taps_idx[None, None, :]).astype(jnp.float32)
    band = jnp.einsum("ijt,kt->kij", picks, filters.astype(jnp.float32))
    return band.astype(jnp.bfloat16)


def any_device(template, science, plan, orders, coadd_weight, intersection):
    row_filters, col_filters = make_filters(orders)
    rows = template.shape[1]
    width = template.shape[2]
    blocks_count = width // 128
    steps_count = science.shape[1]
    row_band = band_matrix(row_filters, rows, rows + 2 * HALF)
    col_band = jnp.transpose(band_matrix(col_filters, 128, 128 + 2 * HALF), (0, 2, 1))
    column_pos = 2.0 * (jnp.arange(width).astype(jnp.float32) + 0.5) / width - 1.0
    pieces = []
    fitted = []
    for step in range(steps_count):
        received = broadcast(template[0], "expo", plan[step])
        padded = extended(received, (("tile", 0),), HALF)
        rowconv = jnp.einsum(
            "kij,jw->kiw", row_band, padded, preferred_element_type=jnp.float32
        ).astype(jnp.bfloat16)
        blocks = rowconv.reshape(NB, rows, blocks_count, 128)
        empty_rim = jnp.zeros((NB, rows, 1, HALF), jnp.bfloat16)
        previous = jnp.concatenate([empty_rim, blocks[:, :, :-1, 128 - HALF :]], axis=2)
        following = jnp.concatenate([blocks[:, :, 1:, :HALF], empty_rim], axis=2)
        window = jnp.concatenate([previous, blocks, following], axis=3)
        conv = jnp.einsum("krbj,kjc->krbc", window, col_band, preferred_element_type=jnp.float32)
        conv = conv.reshape(NB, rows, width)
        fields = jnp.concatenate(
            [conv, conv * column_pos, jnp.ones((1, rows, width), jnp.float32)], axis=0
        )
        fields = fields.reshape(NU, rows * width)
        exposure_image = science[0, step].astype(jnp.float32).reshape(rows * width)
        normal_local = jnp.dot(fields, fields.T, precision=lax.Precision.HIGHEST)
        project_local = jnp.dot(fields, exposure_image, precision=lax.Precision.HIGHEST)
        normal_matrix, projections = lax.psum((normal_local, project_local), "tile")
        normal_matrix = normal_matrix + RIDGE * (jnp.trace(normal_matrix) / NU) * jnp.eye(
            NU, dtype=jnp.float32
        )
        factor = jnp.linalg.cholesky(normal_matrix)
        coeffs = jax.scipy.linalg.cho_solve((factor, True), projections)
        model = jnp.dot(coeffs, fields, precision=lax.Precision.HIGHEST)
        difference = exposure_image - model
        weight_now = coadd_weight[0, step] * intersection[0, step].astype(jnp.float32)
        pieces.append((weight_now * difference).reshape(rows, width))
        fitted.append(coeffs)
    weighted = jnp.stack(pieces)
    received_parts = lax.all_to_all(weighted[None], "expo", split_axis=3, concat_axis=0, tiled=True)
    coadd = jnp.sum(received_parts, axis=0)
    return (coadd, jnp.stack(fitted)[None])


def per_device(template, science, plan, orders, coadd_weight, intersection):
    expos = lax.axis_size("expo")
    rows, width = template.shape[1:]
    whole_lanes = width % (expos * LANES) == 0 and rows % 16 == 0 and 3 * rows <= LANES
    few = (NU + 1) * expos <= LANES and NU + expos <= LANES
    body = tiled_device if whole_lanes and few else any_device
    return body(template, science, plan, orders, coadd_weight, intersection)


def solution(mesh):
    return jax.shard_map(
        per_device,
        mesh=mesh,
        in_specs=(
            P(("groups", "expo"), "tile", None),
            P(("groups", "expo"), None, "tile", None),
            P("groups"),
            P(),
            P(("groups", "expo"), None),
            P(("groups", "expo"), None),
        ),
        out_specs=(P("groups", "tile", "expo"), P(("groups", "expo"), None, None)),
        check_vma=False,
    )
```

```python
import functools

import jax
import jax.numpy as jnp
import numpy as np
from jax import lax
from jax.experimental import pallas as pl
from jax.experimental.pallas import tpu as pltpu
from jax.sharding import PartitionSpec as P

HALF = 15
NB = 6
NU = 13
LANES = 128
BEYOND = 1000
STAGE_COST = 700_000_000
PAIRS = [(j, k) for j in range(NB) for k in range(j, NB)]

SIGMAS = (0.8, 1.4, 2.2, 3.0, 4.0, 5.5)
RIDGE = 0.05


def power_of(pos, order):
    return jnp.where(order == 0, 1.0, jnp.where(order == 1, pos, pos * pos))


def tap_values(pos, sigma, order):
    value = jnp.exp(-pos * pos / (2.0 * sigma * sigma)) * power_of(pos, order)
    return jnp.where(jnp.abs(pos) <= HALF, value, 0.0)


def tap_norm(sigma, order):
    pos = lax.broadcasted_iota(jnp.int32, (8, LANES), 1).astype(jnp.float32) - HALF
    value = tap_values(pos, sigma, order)
    return jnp.sqrt(jnp.sum(value * value, axis=1, keepdims=True))


def target(me, shift, size):
    return me ^ shift if size & (size - 1) == 0 else (me + shift) % size


def source(me, shift, size):
    return me ^ shift if size & (size - 1) == 0 else (me - shift + size) % size


def far_first(size):
    return [*range(size - 1, 0, -1), 0]


def joint(shift, size):
    return shift < size // 2


def send_kernel(template_ref, science_ref, plan_ref, orders_ref, *refs, step):
    *out_refs, owner_ref, order_ref, patch_ref, plan_now, orders_now, sems = refs
    size = sems.shape[0] - 4
    rows, width = science_ref.shape
    chunk = width // size
    ext = chunk + LANES
    patch_refs, image_refs = out_refs[:size], out_refs[size:]
    half = size * chunk // 2
    me = lax.axis_index("expo")
    starts = [pl.multiple_of(target(me, shift, size) * chunk, chunk) for shift in range(size)]
    loads = [
        pltpu.make_async_copy(
            template_ref.at[:, pl.ds(i * half, half)], patch_ref.at[:, pl.ds((i * half + LANES), half)], sems.at[i]
        )
        for i in range(2)
    ]
    copies = [
        pltpu.make_async_copy(
            science_ref.at[:, pl.ds(starts[shift], chunk)],
            patch_refs[shift].at[:, pl.ds(ext, chunk)]
            if joint(shift, size)
            else image_refs[shift - size // 2].at[:, pl.ds(0, chunk)],
            sems.at[3 + shift],
        )
        for shift in range(size)
    ]
    copies.append(pltpu.make_async_copy(plan_ref, plan_now, sems.at[2]))
    copies.append(pltpu.make_async_copy(orders_ref, orders_now, sems.at[3 + size]))
    for copy in loads + copies:
        copy.start()
    blank = jnp.zeros((rows, LANES), patch_ref.dtype)
    patch_ref[:, :LANES] = blank
    patch_ref[:, size * chunk + LANES :] = blank
    for image_ref in image_refs:
        image_ref[:, chunk:] = blank
    for copy in loads:
        copy.wait()
    lane = lax.broadcasted_iota(jnp.int32, (rows, LANES), 1)
    for shift in range(size):
        start = starts[shift]
        patch_refs[shift][:, :chunk] = patch_ref[:, pl.ds(start + LANES, chunk)]
        before = patch_ref[:, pl.ds(start, LANES)].astype(jnp.float32)
        after = patch_ref[:, pl.ds(start + chunk + LANES, LANES)].astype(jnp.float32)
        rim = jnp.where(lane < LANES // 2, after, before)
        patch_refs[shift][:, chunk:ext] = rim.astype(patch_ref.dtype)
    for copy in copies:
        copy.wait()
    owner_ref[...] = jnp.full(owner_ref.shape, plan_now[step], jnp.int32)
    for way in range(2):
        for k in range(NB):
            order_ref[way, k] = jnp.full((8, LANES), orders_now[way, k], jnp.int32)


def choose_kernel(owner_ref, *refs, shifts, size):
    *recv_refs, out_ref = refs
    me = lax.axis_index("expo")
    for b in range(out_ref.shape[1] // LANES):
        columns = slice(b * LANES, (b + 1) * LANES)
        block = recv_refs[0][:, columns].astype(jnp.float32)
        for shift, ref in zip(shifts, recv_refs[1:]):
            block = jnp.where(
                owner_ref[...] == source(me, shift, size), ref[:, columns].astype(jnp.float32), block
            )
        out_ref[:, columns] = block.astype(out_ref.dtype)


def pick_kernel(owner_ref, *refs, shifts, size):
    *recv_refs, out_ref, block_ref = refs
    ext = out_ref.shape[1]
    choose_kernel(owner_ref, *recv_refs, block_ref, shifts=shifts, size=size)
    whole = jnp.concatenate([block_ref[:, ext - LANES :], block_ref[...]], axis=1)
    out_ref[...] = whole[:, LANES - HALF : LANES - HALF + ext]


def column_positions(first_col, block, width):
    col = lax.broadcasted_iota(jnp.int32, (8, LANES), 1) + (first_col + block * LANES)
    return 2.0 * (col.astype(jnp.float32) + 0.5) / width - 1.0


def band_kernel(order_ref, _, row_ref, col_ref, *, tiles):
    rows = row_ref.shape[0] // NB
    tile_at = lax.axis_index("tile")
    near = 1 - 2 * lax.rem(tile_at, 2)
    near_move = jnp.where(tile_at + near < tiles, near - 1, BEYOND)
    far_move = jnp.where((tile_at >= near) & (tile_at - near < tiles), -near - 2, BEYOND)
    row_from = lax.broadcasted_iota(jnp.int32, (8, LANES), 1)
    moved = jnp.where(row_from < rows, 0, jnp.where(row_from < 2 * rows, near_move, far_move))
    sub = lax.broadcasted_iota(jnp.int32, (8, LANES), 0)
    lane = lax.broadcasted_iota(jnp.int32, (8, LANES), 1)
    shift = (sub - jnp.where(lane < LANES // 2, lane, lane - LANES) - HALF).astype(jnp.float32)
    for k in range(NB):
        norm = tap_norm(SIGMAS[k], order_ref[0, k])
        for r in range(0, rows, 16):
            parts = []
            for half in (r, r + 8):
                offset = (row_from + moved * rows - sub - half).astype(jnp.float32)
                parts.append(tap_values(offset, SIGMAS[k], order_ref[0, k]) / norm)
            both = jnp.concatenate(parts, axis=0).astype(jnp.bfloat16)
            row_ref[k * rows + r : k * rows + r + 16] = both[:, : 3 * rows]
        norm = tap_norm(SIGMAS[k], order_ref[1, k])
        pattern = tap_values(shift, SIGMAS[k], order_ref[1, k]) / norm
        for r in range(0, 2 * LANES, 16):
            parts = []
            for half in (r, r + 8):
                moved_on = pltpu.roll(pattern, half % LANES, 1) if half % LANES else pattern
                inside = lane <= half + 7 if half < LANES else lane >= half - LANES + LANES // 2
                parts.append(jnp.where(inside, moved_on, 0.0))
            col_ref[k, r : r + 16] = jnp.concatenate(parts, axis=0).astype(jnp.bfloat16)


def image_blocks(ref, size, shift, chunk):
    first = chunk + LANES if joint(shift, size) else 0
    return lambda b: ref[:, first + b * LANES : first + (b + 1) * LANES].astype(jnp.float32)


def fit_kernel(weight_ref, hits_ref, row_band_ref, col_band_ref, own_ref, near_ref, far_ref, *refs, width):
    *image_refs, conv_ref, sums_ref, row_ref, parts_ref = refs
    image_refs = dict(zip(far_first(len(image_refs)), image_refs))
    tile_at = lax.axis_index("tile")
    expo_at = lax.axis_index("expo")
    rows, ext = own_ref.shape
    expos = len(image_refs)
    chunk = ext - LANES
    blocks = chunk // LANES

    patch = jnp.concatenate([own_ref[...], near_ref[...], far_ref[...]], axis=0)
    row_ref[...] = jnp.dot(
        row_band_ref[...], patch, preferred_element_type=jnp.float32
    ).astype(jnp.bfloat16)
    for k in range(NB):
        window = jnp.concatenate(
            [
                row_ref[k * rows : (k + 1) * rows, b * LANES : (b + 2) * LANES]
                for b in range(blocks)
            ],
            axis=0,
        )
        out = jnp.dot(window, col_band_ref[k], preferred_element_type=jnp.float32)
        conv_ref[k] = out.reshape(blocks, rows, LANES)

    first_col = expo_at * chunk
    xs = [column_positions(first_col, b, width) for b in range(blocks)]

    def fold(x):
        total = x[:8]
        for i in range(8, rows, 8):
            total = total + x[i : i + 8]
        return total

    def moments(at, left, right, count):
        total = [None] * count
        for b in range(blocks):
            term = fold(left(b) * right(b)) if right is not None else fold(left(b))
            for i in range(count):
                total[i] = term if total[i] is None else total[i] + term
                if i < count - 1:
                    term = term * xs[b]
        for i in range(count):
            parts_ref[at + i] = total[i]

    def conv(k):
        return lambda b: conv_ref[k, b]

    def sci(shift):
        return image_blocks(image_refs[shift], expos, shift, chunk)

    blank = jnp.zeros((8, LANES), jnp.float32)
    at = 0
    for j, k in PAIRS:
        moments(at, conv(j), conv(k), 3)
        at += 3
    for k in range(NB):
        moments(at, conv(k), None, 2)
        at += 2
    while at % 8:
        parts_ref[at] = blank
        at += 1
    begin = at
    for shift in range(expos):
        row = at + NU * source(expo_at, shift, expos)
        for k in range(NB):
            moments(row + 2 * k, conv(k), sci(shift), 2)
        moments(row + NU - 1, sci(shift), None, 1)
    at += NU * expos
    weight = jnp.broadcast_to(weight_ref[...] * hits_ref[...].astype(jnp.float32), (8, LANES))
    weight = jnp.where(tile_at == 0, weight, 0.0)
    spot = (
        (lax.broadcasted_iota(jnp.int32, (8, LANES), 0) == 0)
        & (lax.broadcasted_iota(jnp.int32, (8, LANES), 1) == 0)
    )
    for e in range(expos):
        parts_ref[at + e] = jnp.where(spot & (expo_at == e), weight, 0.0)
    at += expos
    while at % 8:
        parts_ref[at] = blank
        at += 1
    ones = jnp.ones((8, LANES), jnp.float32)
    rows_of = []
    for first, last in ((0, begin), (begin, at)):
        lanes = jnp.sum(parts_ref[first:last], axis=1)
        spare = LANES - (last - first)
        if spare:
            lanes = jnp.concatenate([lanes, jnp.zeros((spare, LANES), jnp.float32)], axis=0)
        rows_of.append(
            lax.dot_general(
                ones,
                lanes,
                (((1,), (1,)), ((), ())),
                precision=lax.Precision.HIGHEST,
                preferred_element_type=jnp.float32,
            )
        )
    both = jnp.where(lax.broadcasted_iota(jnp.int32, (8, LANES), 0) < 4, rows_of[0], rows_of[1])
    for i in range(sums_ref.shape[0]):
        sums_ref[i] = both


def table(expos):
    columns = np.zeros((NU + expos + 1, 16), np.int32)
    for at, (j, k) in enumerate(PAIRS):
        for a, b in ((j, k), (k, j)):
            columns[b, a] = 3 * at
            columns[NB + b, a] = columns[b, NB + a] = 3 * at + 1
            columns[NB + b, NB + a] = 3 * at + 2
    for k in range(NB):
        for x in range(2):
            columns[NU - 1, x * NB + k] = columns[x * NB + k, NU - 1] = 3 * len(PAIRS) + 2 * k + x
    for e in range(expos):
        columns[NU + e, :NU] = [NU * e + 2 * k + x for x in range(2) for k in range(NB)] + [NU * e + NU - 1]
        columns[NU + expos, e] = NU * expos + e
    return np.ascontiguousarray(np.broadcast_to(columns[:, :, None], columns.shape + (LANES,)))


def solve_kernel(table_ref, sums_ref, conv_ref, *refs, width, pixels):
    *image_refs, coadd_ref, coeffs_ref, tile_ref, sems = refs
    expo_at = lax.axis_index("expo")
    expos = len(image_refs)
    rows, chunk = coadd_ref.shape
    blocks = chunk // LANES
    images = [image_blocks(ref, expos, shift, chunk) for shift, ref in enumerate(image_refs)]
    sub = lax.broadcasted_iota(jnp.int32, (16, LANES), 0)
    lane = lax.broadcasted_iota(jnp.int32, (16, LANES), 1)
    sums = sums_ref[0]
    for i in range(1, sums_ref.shape[0]):
        sums = sums + sums_ref[i]
    first = jnp.broadcast_to(sums[0:1], (16, LANES))
    second = jnp.broadcast_to(sums[4:5], (16, LANES))

    columns = [
        jnp.take_along_axis(first if j < NU else second, table_ref[j], axis=1) for j in range(NU + expos)
    ]
    spread = jnp.take_along_axis(second, table_ref[NU + expos], axis=1)
    weight = [jnp.broadcast_to(spread[e : e + 1], (16, LANES)) for e in range(expos)]
    columns[NU - 1] = jnp.where(sub == NU - 1, float(pixels), columns[NU - 1])

    trace = columns[0][0:1]
    for j in range(1, NU):
        trace = trace + columns[j][j : j + 1]
    scale = 1.0 / trace
    for j in range(NU + expos):
        columns[j] = columns[j] * scale
        if j < NU:
            columns[j] = columns[j] + jnp.where(sub == j, RIDGE / NU, 0.0)
    for i in range(NU):
        inverse = 1.0 / columns[i][i : i + 1]
        for j in range(i + 1, NU + expos):
            factor = columns[j][i : i + 1] * inverse
            columns[j] = jnp.where(sub == i, factor, columns[j] - columns[i] * factor)

    solved = columns[NU:]
    own = solved[0]
    mixed = weight[0] * solved[0]
    for e in range(1, expos):
        own = jnp.where(expo_at == e, solved[e], own)
        mixed = mixed + weight[e] * solved[e]
    diagonal = (sub == lane) & (sub < NU)
    coeffs_ref[...] = jnp.sum(jnp.where(diagonal, own, 0.0), axis=0, keepdims=True)[:, :NU]
    scale = [jnp.broadcast_to(mixed[u : u + 1], (8, LANES)) for u in range(NU)]
    gains = []
    for shift in range(expos):
        gain = weight[0][:8]
        for e in range(1, expos):
            gain = jnp.where(source(expo_at, shift, expos) == e, weight[e][:8], gain)
        gains.append(gain)
    first_col = expo_at * chunk
    copies = []
    for r in range(0, rows, 8):
        for b in range(blocks):
            x = column_positions(first_col, b, width)
            total = -scale[NU - 1]
            for gain, image in zip(gains, images):
                total = total + gain * image(b)[r : r + 8]
            model = (scale[0] + scale[NB] * x) * conv_ref[0, b, r : r + 8]
            for k in range(1, NB):
                model = model + (scale[k] + scale[NB + k] * x) * conv_ref[k, b, r : r + 8]
            tile_ref[r : r + 8, b * LANES : (b + 1) * LANES] = total - model
        copies.append(
            pltpu.make_async_copy(tile_ref.at[pl.ds(r, 8)], coadd_ref.at[pl.ds(r, 8)], sems.at[r // 8])
        )
        copies[-1].start()
    for copy in copies:
        copy.wait()


def swaps(first, size):
    pairs = [(i, i + 1) for i in range(first, size - 1, 2)]
    if first and size % 2 == 0:
        pairs.append((0, size - 1))
    return [pair for a, b in pairs for pair in ((a, b), (b, a))]


def service_order(expos, tiles):
    half = tiles // 2
    first = list(range(tiles))
    last = list(reversed(range((expos - 1) * tiles, expos * tiles)))
    middle = list(reversed(range(tiles, (expos - 1) * tiles)))
    return list(dict.fromkeys(first[:1] + last[:half] + first[1:half] + last[half:] + first[half:] + middle))


def tiled_device(template, science, plan, orders, coadd_weight, intersection):
    expos = lax.axis_size("expo")
    tiles = lax.axis_size("tile")
    _, rows, width = template.shape
    steps = science.shape[1]
    chunk = width // expos
    ext = chunk + LANES
    blocks = chunk // LANES
    vmem = pl.BlockSpec(memory_space=pltpu.VMEM)
    small = pltpu.CompilerParams(vmem_limit_bytes=16 * 1024 * 1024)
    hbm = pl.BlockSpec(memory_space=pltpu.HBM)
    coadds = []
    fitted = []
    for step in range(steps):
        *blocks_out, owner, order = pl.pallas_call(
            functools.partial(send_kernel, step=step),
            out_shape=tuple(
                pltpu.VMEM((rows, ext + chunk if joint(shift, expos) else ext), template.dtype)
                for shift in range(expos)
            )
            + (pltpu.VMEM((rows, ext), science.dtype),) * (expos - expos // 2)
            + (
                jax.ShapeDtypeStruct((rows, LANES), jnp.int32),
                jax.ShapeDtypeStruct((2, NB, 8, LANES), jnp.int32),
            ),
            in_specs=[hbm] * 4,
            out_specs=(vmem,) * (2 * expos - expos // 2 + 2),
            scratch_shapes=[
                pltpu.VMEM((rows, width + 2 * LANES), template.dtype),
                pltpu.SMEM(plan.shape, jnp.int32),
                pltpu.SMEM((2, NB), jnp.int32),
                pltpu.SemaphoreType.DMA((expos + 4,)),
            ],
            compiler_params=small,
        )(
            pltpu.with_memory_space_constraint(template[0], pltpu.HBM),
            pltpu.with_memory_space_constraint(science[0, step], pltpu.HBM),
            pltpu.with_memory_space_constraint(plan, pltpu.HBM),
            pltpu.with_memory_space_constraint(orders.T, pltpu.HBM),
        )
        patches, images = blocks_out[:expos], blocks_out[expos:]
        for group, first in ((patches, 0), (images, expos // 2)):
            for shift in range(max(first, 1), expos):
                pairs = [(e, int(target(e, shift, expos))) for e in range(expos)]
                group[shift - first] = lax.ppermute(group[shift - first], "expo", pairs)
        images = patches[: expos // 2] + images
        across = [shift for shift in far_first(expos)[:-1] if not joint(shift, expos)]
        beside = [shift for shift in far_first(expos)[:-1] if joint(shift, expos)]
        block = pl.pallas_call(
            functools.partial(choose_kernel, shifts=across, size=expos),
            out_shape=jax.ShapeDtypeStruct((rows, ext), template.dtype),
            in_specs=[vmem] * (2 + len(across)),
            out_specs=vmem,
            compiler_params=small,
            cost_estimate=pl.CostEstimate(flops=STAGE_COST, bytes_accessed=500_000, transcendentals=0),
        )(owner, patches[0], *(patches[shift] for shift in across))
        own = pl.pallas_call(
            functools.partial(pick_kernel, shifts=beside, size=expos),
            out_shape=jax.ShapeDtypeStruct((rows, ext), template.dtype),
            in_specs=[vmem] * (2 + len(beside)),
            out_specs=vmem,
            scratch_shapes=[pltpu.VMEM((rows, ext), template.dtype)],
            compiler_params=small,
        )(owner, block, *(patches[shift] for shift in beside))
        row_band, col_band = pl.pallas_call(
            functools.partial(band_kernel, tiles=tiles),
            out_shape=(
                jax.ShapeDtypeStruct((NB * rows, 3 * rows), jnp.bfloat16),
                jax.ShapeDtypeStruct((NB, 2 * LANES, LANES), jnp.bfloat16),
            ),
            in_specs=[vmem, pl.BlockSpec(memory_space=pl.ANY)],
            out_specs=(vmem, vmem),
            compiler_params=small,
            cost_estimate=pl.CostEstimate(flops=4_000_000, bytes_accessed=500_000, transcendentals=200_000),
        )(order, own)
        far = lax.ppermute(own, "tile", swaps(1, tiles))
        near = lax.ppermute(own, "tile", swaps(0, tiles))
        conv, sums = pl.pallas_call(
            functools.partial(fit_kernel, width=width),
            out_shape=(
                jax.ShapeDtypeStruct((NB, blocks, rows, LANES), jnp.float32),
                jax.ShapeDtypeStruct((tiles * expos, 8, LANES), jnp.float32),
            ),
            in_specs=[vmem] * (7 + expos),
            out_specs=(vmem, vmem),
            scratch_shapes=[
                pltpu.VMEM((NB * rows, ext), jnp.bfloat16),
                pltpu.VMEM((80 + 14 * expos + 8, 8, LANES), jnp.float32),
            ],
            compiler_params=small,
        )(
            coadd_weight[:, step : step + 1],
            intersection[:, step : step + 1],
            row_band,
            col_band,
            own,
            near,
            far,
            *(images[shift] for shift in far_first(expos)),
        )
        group = list(reversed(service_order(expos, tiles)))
        sums = lax.all_to_all(
            sums, ("expo", "tile"), split_axis=0, concat_axis=0, tiled=True, axis_index_groups=[group]
        )
        coadd, coeffs = pl.pallas_call(
            functools.partial(solve_kernel, width=width, pixels=tiles * rows * width),
            out_shape=(
                jax.ShapeDtypeStruct((rows, chunk), jnp.float32),
                jax.ShapeDtypeStruct((1, NU), jnp.float32),
            ),
            in_specs=[vmem] * (3 + expos),
            out_specs=(pl.BlockSpec(memory_space=pl.ANY), vmem),
            scratch_shapes=[
                pltpu.VMEM((rows, chunk), jnp.float32),
                pltpu.SemaphoreType.DMA((rows // 8,)),
            ],
            compiler_params=small,
        )(jnp.asarray(table(expos)), sums, conv, *images)
        coadds.append(coadd[None])
        fitted.append(coeffs)
    return (jnp.concatenate(coadds), jnp.stack(fitted, axis=1))


def broadcast(block, axis, holder):
    block = jnp.where(lax.axis_index(axis) == holder, block, jnp.zeros_like(block))
    return lax.psum(block, axis)


def extended(x, sides, width):
    for axis, dim in sides:
        size, length = (lax.axis_size(axis), x.shape[dim])
        up = [(i, (i + 1) % size) for i in range(size - 1)]
        down = [(j, i) for i, j in up]
        last = lax.slice_in_dim(x, length - width, length, axis=dim)
        first = lax.slice_in_dim(x, 0, width, axis=dim)
        before = lax.ppermute(last, axis, up)
        after = lax.ppermute(first, axis, down)
        x = jnp.concatenate([before, x, after], axis=dim)
    return x


def make_filters(orders):
    taps_pos = jnp.arange(2 * HALF + 1).astype(jnp.float32) - HALF
    row_list = []
    col_list = []
    for basis in range(NB):
        sigma = SIGMAS[basis]
        envelope = jnp.exp(-taps_pos * taps_pos / (2.0 * sigma * sigma))
        row_filter = envelope * power_of(taps_pos, orders[basis, 0])
        col_filter = envelope * power_of(taps_pos, orders[basis, 1])
        row_list.append(row_filter / jnp.sqrt(jnp.sum(row_filter * row_filter)))
        col_list.append(col_filter / jnp.sqrt(jnp.sum(col_filter * col_filter)))
    return (jnp.stack(row_list).astype(jnp.bfloat16), jnp.stack(col_list).astype(jnp.bfloat16))


def band_matrix(filters, out_len, in_len):
    offset = jnp.arange(in_len)[None, :] - jnp.arange(out_len)[:, None]
    taps_idx = jnp.arange(2 * HALF + 1)
    picks = (offset[:, :, None] == taps_idx[None, None, :]).astype(jnp.float32)
    band = jnp.einsum("ijt,kt->kij", picks, filters.astype(jnp.float32))
    return band.astype(jnp.bfloat16)


def any_device(template, science, plan, orders, coadd_weight, intersection):
    row_filters, col_filters = make_filters(orders)
    rows = template.shape[1]
    width = template.shape[2]
    blocks_count = width // 128
    steps_count = science.shape[1]
    row_band = band_matrix(row_filters, rows, rows + 2 * HALF)
    col_band = jnp.transpose(band_matrix(col_filters, 128, 128 + 2 * HALF), (0, 2, 1))
    column_pos = 2.0 * (jnp.arange(width).astype(jnp.float32) + 0.5) / width - 1.0
    pieces = []
    fitted = []
    for step in range(steps_count):
        received = broadcast(template[0], "expo", plan[step])
        padded = extended(received, (("tile", 0),), HALF)
        rowconv = jnp.einsum(
            "kij,jw->kiw", row_band, padded, preferred_element_type=jnp.float32
        ).astype(jnp.bfloat16)
        blocks = rowconv.reshape(NB, rows, blocks_count, 128)
        empty_rim = jnp.zeros((NB, rows, 1, HALF), jnp.bfloat16)
        previous = jnp.concatenate([empty_rim, blocks[:, :, :-1, 128 - HALF :]], axis=2)
        following = jnp.concatenate([blocks[:, :, 1:, :HALF], empty_rim], axis=2)
        window = jnp.concatenate([previous, blocks, following], axis=3)
        conv = jnp.einsum("krbj,kjc->krbc", window, col_band, preferred_element_type=jnp.float32)
        conv = conv.reshape(NB, rows, width)
        fields = jnp.concatenate(
            [conv, conv * column_pos, jnp.ones((1, rows, width), jnp.float32)], axis=0
        )
        fields = fields.reshape(NU, rows * width)
        exposure_image = science[0, step].astype(jnp.float32).reshape(rows * width)
        normal_local = jnp.dot(fields, fields.T, precision=lax.Precision.HIGHEST)
        project_local = jnp.dot(fields, exposure_image, precision=lax.Precision.HIGHEST)
        normal_matrix, projections = lax.psum((normal_local, project_local), "tile")
        normal_matrix = normal_matrix + RIDGE * (jnp.trace(normal_matrix) / NU) * jnp.eye(
            NU, dtype=jnp.float32
        )
        factor = jnp.linalg.cholesky(normal_matrix)
        coeffs = jax.scipy.linalg.cho_solve((factor, True), projections)
        model = jnp.dot(coeffs, fields, precision=lax.Precision.HIGHEST)
        difference = exposure_image - model
        weight_now = coadd_weight[0, step] * intersection[0, step].astype(jnp.float32)
        pieces.append((weight_now * difference).reshape(rows, width))
        fitted.append(coeffs)
    weighted = jnp.stack(pieces)
    received_parts = lax.all_to_all(weighted[None], "expo", split_axis=3, concat_axis=0, tiled=True)
    coadd = jnp.sum(received_parts, axis=0)
    return (coadd, jnp.stack(fitted)[None])


def per_device(template, science, plan, orders, coadd_weight, intersection):
    expos = lax.axis_size("expo")
    rows, width = template.shape[1:]
    whole_lanes = width % (expos * LANES) == 0 and rows % 16 == 0 and 3 * rows <= LANES
    few = (NU + 1) * expos <= LANES and NU + expos <= LANES
    body = tiled_device if whole_lanes and few else any_device
    return body(template, science, plan, orders, coadd_weight, intersection)


def solution(mesh):
    return jax.shard_map(
        per_device,
        mesh=mesh,
        in_specs=(
            P(("groups", "expo"), "tile", None),
            P(("groups", "expo"), None, "tile", None),
            P("groups"),
            P(),
            P(("groups", "expo"), None),
            P(("groups", "expo"), None),
        ),
        out_specs=(P("groups", "tile", "expo"), P(("groups", "expo"), None, None)),
        check_vma=False,
    )
```

```python
import functools

import jax
import jax.numpy as jnp
import numpy as np
from jax import lax
from jax.experimental import pallas as pl
from jax.experimental.pallas import tpu as pltpu
from jax.sharding import PartitionSpec as P

HALF = 15
NB = 6
NU = 13
LANES = 128
BEYOND = 1000
STAGE_COST = 700_000_000
PAIRS = [(j, k) for j in range(NB) for k in range(j, NB)]

SIGMAS = (0.8, 1.4, 2.2, 3.0, 4.0, 5.5)
RIDGE = 0.05


def power_of(pos, order):
    return jnp.where(order == 0, 1.0, jnp.where(order == 1, pos, pos * pos))


def tap_values(pos, sigma, order):
    value = jnp.exp(-pos * pos / (2.0 * sigma * sigma)) * power_of(pos, order)
    return jnp.where(jnp.abs(pos) <= HALF, value, 0.0)


def tap_norm(sigma, order):
    pos = lax.broadcasted_iota(jnp.int32, (8, LANES), 1).astype(jnp.float32) - HALF
    value = tap_values(pos, sigma, order)
    return jnp.sqrt(jnp.sum(value * value, axis=1, keepdims=True))


def target(me, shift, size):
    return me ^ shift if size & (size - 1) == 0 else (me + shift) % size


def source(me, shift, size):
    return me ^ shift if size & (size - 1) == 0 else (me - shift + size) % size


def far_first(size):
    return [*range(size - 1, 0, -1), 0]


def joint(shift, size):
    return shift < size // 2


def send_kernel(template_ref, science_ref, plan_ref, orders_ref, *refs, step):
    *out_refs, owner_ref, order_ref, patch_ref, plan_now, orders_now, sems = refs
    size = sems.shape[0] - 4
    rows, width = science_ref.shape
    chunk = width // size
    ext = chunk + LANES
    patch_refs, image_refs = out_refs[:size], out_refs[size:]
    half = size * chunk // 2
    me = lax.axis_index("expo")
    starts = [pl.multiple_of(target(me, shift, size) * chunk, chunk) for shift in range(size)]
    loads = [
        pltpu.make_async_copy(
            template_ref.at[:, pl.ds(i * half, half)], patch_ref.at[:, pl.ds((i * half + LANES), half)], sems.at[i]
        )
        for i in range(2)
    ]
    copies = [
        pltpu.make_async_copy(
            science_ref.at[:, pl.ds(starts[shift], chunk)],
            patch_refs[shift].at[:, pl.ds(ext, chunk)]
            if joint(shift, size)
            else image_refs[shift - size // 2].at[:, pl.ds(0, chunk)],
            sems.at[3 + shift],
        )
        for shift in range(size)
    ]
    copies.append(pltpu.make_async_copy(plan_ref, plan_now, sems.at[2]))
    copies.append(pltpu.make_async_copy(orders_ref, orders_now, sems.at[3 + size]))
    for copy in loads + copies:
        copy.start()
    blank = jnp.zeros((rows, LANES), patch_ref.dtype)
    patch_ref[:, :LANES] = blank
    patch_ref[:, size * chunk + LANES :] = blank
    for image_ref in image_refs:
        image_ref[:, chunk:] = blank
    for copy in loads:
        copy.wait()
    lane = lax.broadcasted_iota(jnp.int32, (rows, LANES), 1)
    for shift in range(size):
        start = starts[shift]
        patch_refs[shift][:, :chunk] = patch_ref[:, pl.ds(start + LANES, chunk)]
        before = patch_ref[:, pl.ds(start, LANES)].astype(jnp.float32)
        after = patch_ref[:, pl.ds(start + chunk + LANES, LANES)].astype(jnp.float32)
        rim = jnp.where(lane < LANES // 2, after, before)
        patch_refs[shift][:, chunk:ext] = rim.astype(patch_ref.dtype)
    for copy in copies:
        copy.wait()
    owner_ref[...] = jnp.full(owner_ref.shape, plan_now[step], jnp.int32)
    for way in range(2):
        for k in range(NB):
            order_ref[way, k] = jnp.full((8, LANES), orders_now[way, k], jnp.int32)


def choose_kernel(owner_ref, *refs, shifts, size):
    *recv_refs, out_ref = refs
    me = lax.axis_index("expo")
    for b in range(out_ref.shape[1] // LANES):
        columns = slice(b * LANES, (b + 1) * LANES)
        block = recv_refs[0][:, columns].astype(jnp.float32)
        for shift, ref in zip(shifts, recv_refs[1:]):
            block = jnp.where(
                owner_ref[...] == source(me, shift, size), ref[:, columns].astype(jnp.float32), block
            )
        out_ref[:, columns] = block.astype(out_ref.dtype)


def pick_kernel(owner_ref, *refs, shifts, size):
    *recv_refs, out_ref, block_ref = refs
    ext = out_ref.shape[1]
    choose_kernel(owner_ref, *recv_refs, block_ref, shifts=shifts, size=size)
    whole = jnp.concatenate([block_ref[:, ext - LANES :], block_ref[...]], axis=1)
    out_ref[...] = whole[:, LANES - HALF : LANES - HALF + ext]


def column_positions(first_col, block, width):
    col = lax.broadcasted_iota(jnp.int32, (8, LANES), 1) + (first_col + block * LANES)
    return 2.0 * (col.astype(jnp.float32) + 0.5) / width - 1.0


def band_kernel(order_ref, _, row_ref, col_ref, *, tiles):
    rows = row_ref.shape[0] // NB
    tile_at = lax.axis_index("tile")
    near = 1 - 2 * lax.rem(tile_at, 2)
    near_move = jnp.where(tile_at + near < tiles, near - 1, BEYOND)
    far_move = jnp.where((tile_at >= near) & (tile_at - near < tiles), -near - 2, BEYOND)
    row_from = lax.broadcasted_iota(jnp.int32, (8, LANES), 1)
    moved = jnp.where(row_from < rows, 0, jnp.where(row_from < 2 * rows, near_move, far_move))
    sub = lax.broadcasted_iota(jnp.int32, (8, LANES), 0)
    lane = lax.broadcasted_iota(jnp.int32, (8, LANES), 1)
    shift = (sub - jnp.where(lane < LANES // 2, lane, lane - LANES) - HALF).astype(jnp.float32)
    for k in range(NB):
        norm = tap_norm(SIGMAS[k], order_ref[0, k])
        for r in range(0, rows, 16):
            parts = []
            for half in (r, r + 8):
                offset = (row_from + moved * rows - sub - half).astype(jnp.float32)
                parts.append(tap_values(offset, SIGMAS[k], order_ref[0, k]) / norm)
            both = jnp.concatenate(parts, axis=0).astype(jnp.bfloat16)
            row_ref[k * rows + r : k * rows + r + 16] = both[:, : 3 * rows]
        norm = tap_norm(SIGMAS[k], order_ref[1, k])
        pattern = tap_values(shift, SIGMAS[k], order_ref[1, k]) / norm
        for r in range(0, 2 * LANES, 16):
            parts = []
            for half in (r, r + 8):
                moved_on = pltpu.roll(pattern, half % LANES, 1) if half % LANES else pattern
                inside = lane <= half + 7 if half < LANES else lane >= half - LANES + LANES // 2
                parts.append(jnp.where(inside, moved_on, 0.0))
            col_ref[k, r : r + 16] = jnp.concatenate(parts, axis=0).astype(jnp.bfloat16)


def image_blocks(ref, size, shift, chunk):
    first = chunk + LANES if joint(shift, size) else 0
    return lambda b: ref[:, first + b * LANES : first + (b + 1) * LANES].astype(jnp.float32)


def fit_kernel(weight_ref, hits_ref, row_band_ref, col_band_ref, own_ref, near_ref, far_ref, *refs, width):
    *image_refs, conv_ref, sums_ref, row_ref, parts_ref = refs
    image_refs = dict(zip(far_first(len(image_refs)), image_refs))
    tile_at = lax.axis_index("tile")
    expo_at = lax.axis_index("expo")
    rows, ext = own_ref.shape
    expos = len(image_refs)
    chunk = ext - LANES
    blocks = chunk // LANES

    patch = jnp.concatenate([own_ref[...], near_ref[...], far_ref[...]], axis=0)
    row_ref[...] = jnp.dot(
        row_band_ref[...], patch, preferred_element_type=jnp.float32
    ).astype(jnp.bfloat16)
    for k in range(NB):
        window = jnp.concatenate(
            [
                row_ref[k * rows : (k + 1) * rows, b * LANES : (b + 2) * LANES]
                for b in range(blocks)
            ],
            axis=0,
        )
        out = jnp.dot(window, col_band_ref[k], preferred_element_type=jnp.float32)
        conv_ref[k] = out.reshape(blocks, rows, LANES)

    first_col = expo_at * chunk
    xs = [column_positions(first_col, b, width) for b in range(blocks)]

    def fold(x):
        total = x[:8]
        for i in range(8, rows, 8):
            total = total + x[i : i + 8]
        return total

    def moments(at, left, right, count):
        total = [None] * count
        for b in range(blocks):
            term = fold(left(b) * right(b)) if right is not None else fold(left(b))
            for i in range(count):
                total[i] = term if total[i] is None else total[i] + term
                if i < count - 1:
                    term = term * xs[b]
        for i in range(count):
            parts_ref[at + i] = total[i]

    def conv(k):
        return lambda b: conv_ref[k, b]

    def sci(shift):
        return image_blocks(image_refs[shift], expos, shift, chunk)

    blank = jnp.zeros((8, LANES), jnp.float32)
    at = 0
    for j, k in PAIRS:
        moments(at, conv(j), conv(k), 3)
        at += 3
    for k in range(NB):
        moments(at, conv(k), None, 2)
        at += 2
    while at % 8:
        parts_ref[at] = blank
        at += 1
    begin = at
    for shift in range(expos):
        row = at + NU * source(expo_at, shift, expos)
        for k in range(NB):
            moments(row + 2 * k, conv(k), sci(shift), 2)
        moments(row + NU - 1, sci(shift), None, 1)
    at += NU * expos
    weight = jnp.broadcast_to(weight_ref[...] * hits_ref[...].astype(jnp.float32), (8, LANES))
    weight = jnp.where(tile_at == 0, weight, 0.0)
    spot = (
        (lax.broadcasted_iota(jnp.int32, (8, LANES), 0) == 0)
        & (lax.broadcasted_iota(jnp.int32, (8, LANES), 1) == 0)
    )
    for e in range(expos):
        parts_ref[at + e] = jnp.where(spot & (expo_at == e), weight, 0.0)
    at += expos
    while at % 8:
        parts_ref[at] = blank
        at += 1
    ones = jnp.ones((8, LANES), jnp.float32)
    rows_of = []
    for first, last in ((0, begin), (begin, at)):
        lanes = jnp.sum(parts_ref[first:last], axis=1)
        spare = LANES - (last - first)
        if spare:
            lanes = jnp.concatenate([lanes, jnp.zeros((spare, LANES), jnp.float32)], axis=0)
        rows_of.append(
            lax.dot_general(
                ones,
                lanes,
                (((1,), (1,)), ((), ())),
                precision=lax.Precision.HIGHEST,
                preferred_element_type=jnp.float32,
            )
        )
    both = jnp.where(lax.broadcasted_iota(jnp.int32, (8, LANES), 0) < 4, rows_of[0], rows_of[1])
    for i in range(sums_ref.shape[0]):
        sums_ref[i] = both


def table(expos):
    columns = np.zeros((NU + expos + 1, 16), np.int32)
    for at, (j, k) in enumerate(PAIRS):
        for a, b in ((j, k), (k, j)):
            columns[b, a] = 3 * at
            columns[NB + b, a] = columns[b, NB + a] = 3 * at + 1
            columns[NB + b, NB + a] = 3 * at + 2
    for k in range(NB):
        for x in range(2):
            columns[NU - 1, x * NB + k] = columns[x * NB + k, NU - 1] = 3 * len(PAIRS) + 2 * k + x
    for e in range(expos):
        columns[NU + e, :NU] = [NU * e + 2 * k + x for x in range(2) for k in range(NB)] + [NU * e + NU - 1]
        columns[NU + expos, e] = NU * expos + e
    return np.ascontiguousarray(np.broadcast_to(columns[:, :, None], columns.shape + (LANES,)))


def solve_kernel(table_ref, sums_ref, conv_ref, *refs, width, pixels):
    *image_refs, coadd_ref, coeffs_ref, tile_ref, sems = refs
    expo_at = lax.axis_index("expo")
    expos = len(image_refs)
    rows, chunk = coadd_ref.shape
    blocks = chunk // LANES
    images = [image_blocks(ref, expos, shift, chunk) for shift, ref in enumerate(image_refs)]
    sub = lax.broadcasted_iota(jnp.int32, (16, LANES), 0)
    lane = lax.broadcasted_iota(jnp.int32, (16, LANES), 1)
    sums = sums_ref[0]
    for i in range(1, sums_ref.shape[0]):
        sums = sums + sums_ref[i]
    first = jnp.broadcast_to(sums[0:1], (16, LANES))
    second = jnp.broadcast_to(sums[4:5], (16, LANES))

    columns = [
        jnp.take_along_axis(first if j < NU else second, table_ref[j], axis=1) for j in range(NU + expos)
    ]
    spread = jnp.take_along_axis(second, table_ref[NU + expos], axis=1)
    weight = [jnp.broadcast_to(spread[e : e + 1], (16, LANES)) for e in range(expos)]
    columns[NU - 1] = jnp.where(sub == NU - 1, float(pixels), columns[NU - 1])

    trace = columns[0][0:1]
    for j in range(1, NU):
        trace = trace + columns[j][j : j + 1]
    scale = 1.0 / trace
    for j in range(NU + expos):
        columns[j] = columns[j] * scale
        if j < NU:
            columns[j] = columns[j] + jnp.where(sub == j, RIDGE / NU, 0.0)
    for i in range(NU):
        inverse = 1.0 / columns[i][i : i + 1]
        for j in range(i + 1, NU + expos):
            factor = columns[j][i : i + 1] * inverse
            columns[j] = jnp.where(sub == i, factor, columns[j] - columns[i] * factor)

    solved = columns[NU:]
    own = solved[0]
    mixed = weight[0] * solved[0]
    for e in range(1, expos):
        own = jnp.where(expo_at == e, solved[e], own)
        mixed = mixed + weight[e] * solved[e]
    diagonal = (sub == lane) & (sub < NU)
    coeffs_ref[...] = jnp.sum(jnp.where(diagonal, own, 0.0), axis=0, keepdims=True)[:, :NU]
    scale = [jnp.broadcast_to(mixed[u : u + 1], (8, LANES)) for u in range(NU)]
    gains = []
    for shift in range(expos):
        gain = weight[0][:8]
        for e in range(1, expos):
            gain = jnp.where(source(expo_at, shift, expos) == e, weight[e][:8], gain)
        gains.append(gain)
    first_col = expo_at * chunk
    copies = []
    for r in range(0, rows, 8):
        for b in range(blocks):
            x = column_positions(first_col, b, width)
            total = -scale[NU - 1]
            for gain, image in zip(gains, images):
                total = total + gain * image(b)[r : r + 8]
            model = (scale[0] + scale[NB] * x) * conv_ref[0, b, r : r + 8]
            for k in range(1, NB):
                model = model + (scale[k] + scale[NB + k] * x) * conv_ref[k, b, r : r + 8]
            tile_ref[r : r + 8, b * LANES : (b + 1) * LANES] = total - model
        copies.append(
            pltpu.make_async_copy(tile_ref.at[pl.ds(r, 8)], coadd_ref.at[pl.ds(r, 8)], sems.at[r // 8])
        )
        copies[-1].start()
    for copy in copies:
        copy.wait()


def swaps(first, size):
    pairs = [(i, i + 1) for i in range(first, size - 1, 2)]
    if first and size % 2 == 0:
        pairs.append((0, size - 1))
    return [pair for a, b in pairs for pair in ((a, b), (b, a))]


def service_order(expos, tiles):
    early = list(range(tiles // 2))
    late = [e * tiles + t for e in range(expos // 2, expos) for t in reversed(range(tiles))]
    return early + [i for i in late if i not in early] + list(range(len(early), expos // 2 * tiles))


def tiled_device(template, science, plan, orders, coadd_weight, intersection):
    expos = lax.axis_size("expo")
    tiles = lax.axis_size("tile")
    _, rows, width = template.shape
    steps = science.shape[1]
    chunk = width // expos
    ext = chunk + LANES
    blocks = chunk // LANES
    vmem = pl.BlockSpec(memory_space=pltpu.VMEM)
    small = pltpu.CompilerParams(vmem_limit_bytes=16 * 1024 * 1024)
    hbm = pl.BlockSpec(memory_space=pltpu.HBM)
    coadds = []
    fitted = []
    for step in range(steps):
        *blocks_out, owner, order = pl.pallas_call(
            functools.partial(send_kernel, step=step),
            out_shape=tuple(
                pltpu.VMEM((rows, ext + chunk if joint(shift, expos) else ext), template.dtype)
                for shift in range(expos)
            )
            + (pltpu.VMEM((rows, ext), science.dtype),) * (expos - expos // 2)
            + (
                jax.ShapeDtypeStruct((rows, LANES), jnp.int32),
                jax.ShapeDtypeStruct((2, NB, 8, LANES), jnp.int32),
            ),
            in_specs=[hbm] * 4,
            out_specs=(vmem,) * (2 * expos - expos // 2 + 2),
            scratch_shapes=[
                pltpu.VMEM((rows, width + 2 * LANES), template.dtype),
                pltpu.SMEM(plan.shape, jnp.int32),
                pltpu.SMEM((2, NB), jnp.int32),
                pltpu.SemaphoreType.DMA((expos + 4,)),
            ],
            compiler_params=small,
        )(
            pltpu.with_memory_space_constraint(template[0], pltpu.HBM),
            pltpu.with_memory_space_constraint(science[0, step], pltpu.HBM),
            pltpu.with_memory_space_constraint(plan, pltpu.HBM),
            pltpu.with_memory_space_constraint(orders.T, pltpu.HBM),
        )
        patches, images = blocks_out[:expos], blocks_out[expos:]
        for group, first in ((patches, 0), (images, expos // 2)):
            for shift in range(max(first, 1), expos):
                pairs = [(e, int(target(e, shift, expos))) for e in range(expos)]
                group[shift - first] = lax.ppermute(group[shift - first], "expo", pairs)
        images = patches[: expos // 2] + images
        across = [shift for shift in far_first(expos)[:-1] if not joint(shift, expos)]
        beside = [shift for shift in far_first(expos)[:-1] if joint(shift, expos)]
        block = pl.pallas_call(
            functools.partial(choose_kernel, shifts=across, size=expos),
            out_shape=jax.ShapeDtypeStruct((rows, ext), template.dtype),
            in_specs=[vmem] * (2 + len(across)),
            out_specs=vmem,
            compiler_params=small,
            cost_estimate=pl.CostEstimate(flops=STAGE_COST, bytes_accessed=500_000, transcendentals=0),
        )(owner, patches[0], *(patches[shift] for shift in across))
        own = pl.pallas_call(
            functools.partial(pick_kernel, shifts=beside, size=expos),
            out_shape=jax.ShapeDtypeStruct((rows, ext), template.dtype),
            in_specs=[vmem] * (2 + len(beside)),
            out_specs=vmem,
            scratch_shapes=[pltpu.VMEM((rows, ext), template.dtype)],
            compiler_params=small,
        )(owner, block, *(patches[shift] for shift in beside))
        row_band, col_band = pl.pallas_call(
            functools.partial(band_kernel, tiles=tiles),
            out_shape=(
                jax.ShapeDtypeStruct((NB * rows, 3 * rows), jnp.bfloat16),
                jax.ShapeDtypeStruct((NB, 2 * LANES, LANES), jnp.bfloat16),
            ),
            in_specs=[vmem, pl.BlockSpec(memory_space=pl.ANY)],
            out_specs=(vmem, vmem),
            compiler_params=small,
            cost_estimate=pl.CostEstimate(flops=4_000_000, bytes_accessed=500_000, transcendentals=200_000),
        )(order, own)
        far = lax.ppermute(own, "tile", swaps(1, tiles))
        near = lax.ppermute(own, "tile", swaps(0, tiles))
        conv, sums = pl.pallas_call(
            functools.partial(fit_kernel, width=width),
            out_shape=(
                jax.ShapeDtypeStruct((NB, blocks, rows, LANES), jnp.float32),
                jax.ShapeDtypeStruct((tiles * expos, 8, LANES), jnp.float32),
            ),
            in_specs=[vmem] * (7 + expos),
            out_specs=(vmem, vmem),
            scratch_shapes=[
                pltpu.VMEM((NB * rows, ext), jnp.bfloat16),
                pltpu.VMEM((80 + 14 * expos + 8, 8, LANES), jnp.float32),
            ],
            compiler_params=small,
        )(
            coadd_weight[:, step : step + 1],
            intersection[:, step : step + 1],
            row_band,
            col_band,
            own,
            near,
            far,
            *(images[shift] for shift in far_first(expos)),
        )
        group = list(reversed(service_order(expos, tiles)))
        sums = lax.all_to_all(
            sums, ("expo", "tile"), split_axis=0, concat_axis=0, tiled=True, axis_index_groups=[group]
        )
        coadd, coeffs = pl.pallas_call(
            functools.partial(solve_kernel, width=width, pixels=tiles * rows * width),
            out_shape=(
                jax.ShapeDtypeStruct((rows, chunk), jnp.float32),
                jax.ShapeDtypeStruct((1, NU), jnp.float32),
            ),
            in_specs=[vmem] * (3 + expos),
            out_specs=(pl.BlockSpec(memory_space=pl.ANY), vmem),
            scratch_shapes=[
                pltpu.VMEM((rows, chunk), jnp.float32),
                pltpu.SemaphoreType.DMA((rows // 8,)),
            ],
            compiler_params=small,
        )(jnp.asarray(table(expos)), sums, conv, *images)
        coadds.append(coadd[None])
        fitted.append(coeffs)
    return (jnp.concatenate(coadds), jnp.stack(fitted, axis=1))


def broadcast(block, axis, holder):
    block = jnp.where(lax.axis_index(axis) == holder, block, jnp.zeros_like(block))
    return lax.psum(block, axis)


def extended(x, sides, width):
    for axis, dim in sides:
        size, length = (lax.axis_size(axis), x.shape[dim])
        up = [(i, (i + 1) % size) for i in range(size - 1)]
        down = [(j, i) for i, j in up]
        last = lax.slice_in_dim(x, length - width, length, axis=dim)
        first = lax.slice_in_dim(x, 0, width, axis=dim)
        before = lax.ppermute(last, axis, up)
        after = lax.ppermute(first, axis, down)
        x = jnp.concatenate([before, x, after], axis=dim)
    return x


def make_filters(orders):
    taps_pos = jnp.arange(2 * HALF + 1).astype(jnp.float32) - HALF
    row_list = []
    col_list = []
    for basis in range(NB):
        sigma = SIGMAS[basis]
        envelope = jnp.exp(-taps_pos * taps_pos / (2.0 * sigma * sigma))
        row_filter = envelope * power_of(taps_pos, orders[basis, 0])
        col_filter = envelope * power_of(taps_pos, orders[basis, 1])
        row_list.append(row_filter / jnp.sqrt(jnp.sum(row_filter * row_filter)))
        col_list.append(col_filter / jnp.sqrt(jnp.sum(col_filter * col_filter)))
    return (jnp.stack(row_list).astype(jnp.bfloat16), jnp.stack(col_list).astype(jnp.bfloat16))


def band_matrix(filters, out_len, in_len):
    offset = jnp.arange(in_len)[None, :] - jnp.arange(out_len)[:, None]
    taps_idx = jnp.arange(2 * HALF + 1)
    picks = (offset[:, :, None] == taps_idx[None, None, :]).astype(jnp.float32)
    band = jnp.einsum("ijt,kt->kij", picks, filters.astype(jnp.float32))
    return band.astype(jnp.bfloat16)


def any_device(template, science, plan, orders, coadd_weight, intersection):
    row_filters, col_filters = make_filters(orders)
    rows = template.shape[1]
    width = template.shape[2]
    blocks_count = width // 128
    steps_count = science.shape[1]
    row_band = band_matrix(row_filters, rows, rows + 2 * HALF)
    col_band = jnp.transpose(band_matrix(col_filters, 128, 128 + 2 * HALF), (0, 2, 1))
    column_pos = 2.0 * (jnp.arange(width).astype(jnp.float32) + 0.5) / width - 1.0
    pieces = []
    fitted = []
    for step in range(steps_count):
        received = broadcast(template[0], "expo", plan[step])
        padded = extended(received, (("tile", 0),), HALF)
        rowconv = jnp.einsum(
            "kij,jw->kiw", row_band, padded, preferred_element_type=jnp.float32
        ).astype(jnp.bfloat16)
        blocks = rowconv.reshape(NB, rows, blocks_count, 128)
        empty_rim = jnp.zeros((NB, rows, 1, HALF), jnp.bfloat16)
        previous = jnp.concatenate([empty_rim, blocks[:, :, :-1, 128 - HALF :]], axis=2)
        following = jnp.concatenate([blocks[:, :, 1:, :HALF], empty_rim], axis=2)
        window = jnp.concatenate([previous, blocks, following], axis=3)
        conv = jnp.einsum("krbj,kjc->krbc", window, col_band, preferred_element_type=jnp.float32)
        conv = conv.reshape(NB, rows, width)
        fields = jnp.concatenate(
            [conv, conv * column_pos, jnp.ones((1, rows, width), jnp.float32)], axis=0
        )
        fields = fields.reshape(NU, rows * width)
        exposure_image = science[0, step].astype(jnp.float32).reshape(rows * width)
        normal_local = jnp.dot(fields, fields.T, precision=lax.Precision.HIGHEST)
        project_local = jnp.dot(fields, exposure_image, precision=lax.Precision.HIGHEST)
        normal_matrix, projections = lax.psum((normal_local, project_local), "tile")
        normal_matrix = normal_matrix + RIDGE * (jnp.trace(normal_matrix) / NU) * jnp.eye(
            NU, dtype=jnp.float32
        )
        factor = jnp.linalg.cholesky(normal_matrix)
        coeffs = jax.scipy.linalg.cho_solve((factor, True), projections)
        model = jnp.dot(coeffs, fields, precision=lax.Precision.HIGHEST)
        difference = exposure_image - model
        weight_now = coadd_weight[0, step] * intersection[0, step].astype(jnp.float32)
        pieces.append((weight_now * difference).reshape(rows, width))
        fitted.append(coeffs)
    weighted = jnp.stack(pieces)
    received_parts = lax.all_to_all(weighted[None], "expo", split_axis=3, concat_axis=0, tiled=True)
    coadd = jnp.sum(received_parts, axis=0)
    return (coadd, jnp.stack(fitted)[None])


def per_device(template, science, plan, orders, coadd_weight, intersection):
    expos = lax.axis_size("expo")
    rows, width = template.shape[1:]
    whole_lanes = width % (expos * LANES) == 0 and rows % 16 == 0 and 3 * rows <= LANES
    few = (NU + 1) * expos <= LANES and NU + expos <= LANES
    body = tiled_device if whole_lanes and few else any_device
    return body(template, science, plan, orders, coadd_weight, intersection)


def solution(mesh):
    return jax.shard_map(
        per_device,
        mesh=mesh,
        in_specs=(
            P(("groups", "expo"), "tile", None),
            P(("groups", "expo"), None, "tile", None),
            P("groups"),
            P(),
            P(("groups", "expo"), None),
            P(("groups", "expo"), None),
        ),
        out_specs=(P("groups", "tile", "expo"), P(("groups", "expo"), None, None)),
        check_vma=False,
    )
```

```python
import functools

import jax
import jax.numpy as jnp
import numpy as np
from jax import lax
from jax.experimental import pallas as pl
from jax.experimental.pallas import tpu as pltpu
from jax.sharding import PartitionSpec as P

HALF = 15
NB = 6
NU = 13
LANES = 128
BEYOND = 1000
STAGE_COST = 700_000_000
PAIRS = [(j, k) for j in range(NB) for k in range(j, NB)]

SIGMAS = (0.8, 1.4, 2.2, 3.0, 4.0, 5.5)
RIDGE = 0.05


def power_of(pos, order):
    return jnp.where(order == 0, 1.0, jnp.where(order == 1, pos, pos * pos))


def tap_values(pos, sigma, order):
    value = jnp.exp(-pos * pos / (2.0 * sigma * sigma)) * power_of(pos, order)
    return jnp.where(jnp.abs(pos) <= HALF, value, 0.0)


def tap_norm(sigma, order):
    pos = lax.broadcasted_iota(jnp.int32, (8, LANES), 1).astype(jnp.float32) - HALF
    value = tap_values(pos, sigma, order)
    return jnp.sqrt(jnp.sum(value * value, axis=1, keepdims=True))


def target(me, shift, size):
    return me ^ shift if size & (size - 1) == 0 else (me + shift) % size


def source(me, shift, size):
    return me ^ shift if size & (size - 1) == 0 else (me - shift + size) % size


def crossed(shift, upper, size):
    return shift ^ upper if size >= 4 and size & (size - 1) == 0 and shift >= size // 2 else shift


def science_target(me, shift, size):
    return target(me, crossed(shift, (me >= size // 2) * 1, size), size)


def science_source(me, shift, size):
    return source(me, crossed(shift, (me < size // 2) * 1, size), size)


def middle_first(size):
    return [*range(size // 2, size), *range(1, size // 2), 0] if size > 1 else [0]


def far_first(size):
    return [*range(size - 1, 0, -1), 0]


def joint(shift, size):
    return shift < size // 2


def send_kernel(template_ref, science_ref, plan_ref, orders_ref, *refs, step):
    *out_refs, owner_ref, order_ref, patch_ref, plan_now, orders_now, sems = refs
    size = sems.shape[0] - 4
    rows, width = science_ref.shape
    chunk = width // size
    ext = chunk + LANES
    patch_refs, image_refs = out_refs[:size], out_refs[size:]
    half = size * chunk // 2
    me = lax.axis_index("expo")
    starts = [pl.multiple_of(target(me, shift, size) * chunk, chunk) for shift in range(size)]
    loads = [
        pltpu.make_async_copy(
            template_ref.at[:, pl.ds(i * half, half)], patch_ref.at[:, pl.ds((i * half + LANES), half)], sems.at[i]
        )
        for i in range(2)
    ]
    copies = [
        pltpu.make_async_copy(
            science_ref.at[:, pl.ds(pl.multiple_of(science_target(me, shift, size) * chunk, chunk), chunk)],
            patch_refs[shift].at[:, pl.ds(ext, chunk)]
            if joint(shift, size)
            else image_refs[shift - size // 2].at[:, pl.ds(0, chunk)],
            sems.at[3 + shift],
        )
        for shift in range(size)
    ]
    copies.append(pltpu.make_async_copy(plan_ref, plan_now, sems.at[2]))
    copies.append(pltpu.make_async_copy(orders_ref, orders_now, sems.at[3 + size]))
    for copy in loads + copies:
        copy.start()
    blank = jnp.zeros((rows, LANES), patch_ref.dtype)
    patch_ref[:, :LANES] = blank
    patch_ref[:, size * chunk + LANES :] = blank
    for image_ref in image_refs:
        image_ref[:, chunk:] = blank
    for copy in loads:
        copy.wait()
    lane = lax.broadcasted_iota(jnp.int32, (rows, LANES), 1)
    for shift in range(size):
        start = starts[shift]
        patch_refs[shift][:, :chunk] = patch_ref[:, pl.ds(start + LANES, chunk)]
        before = patch_ref[:, pl.ds(start, LANES)].astype(jnp.float32)
        after = patch_ref[:, pl.ds(start + chunk + LANES, LANES)].astype(jnp.float32)
        rim = jnp.where(lane < LANES // 2, after, before)
        patch_refs[shift][:, chunk:ext] = rim.astype(patch_ref.dtype)
    for copy in copies:
        copy.wait()
    owner_ref[...] = jnp.full(owner_ref.shape, plan_now[step], jnp.int32)
    for way in range(2):
        for k in range(NB):
            order_ref[way, k] = jnp.full((8, LANES), orders_now[way, k], jnp.int32)


def choose_kernel(owner_ref, *refs, shifts, size):
    *recv_refs, out_ref = refs
    me = lax.axis_index("expo")
    for b in range(out_ref.shape[1] // LANES):
        columns = slice(b * LANES, (b + 1) * LANES)
        block = recv_refs[0][:, columns].astype(jnp.float32)
        for shift, ref in zip(shifts, recv_refs[1:]):
            block = jnp.where(
                owner_ref[...] == source(me, shift, size), ref[:, columns].astype(jnp.float32), block
            )
        out_ref[:, columns] = block.astype(out_ref.dtype)


def pick_kernel(owner_ref, *refs, shifts, size):
    *recv_refs, out_ref, block_ref = refs
    ext = out_ref.shape[1]
    choose_kernel(owner_ref, *recv_refs, block_ref, shifts=shifts, size=size)
    whole = jnp.concatenate([block_ref[:, ext - LANES :], block_ref[...]], axis=1)
    out_ref[...] = whole[:, LANES - HALF : LANES - HALF + ext]


def column_positions(first_col, block, width):
    col = lax.broadcasted_iota(jnp.int32, (8, LANES), 1) + (first_col + block * LANES)
    return 2.0 * (col.astype(jnp.float32) + 0.5) / width - 1.0


def band_kernel(order_ref, _, row_ref, col_ref, *, tiles):
    rows = row_ref.shape[0] // NB
    tile_at = lax.axis_index("tile")
    near = 1 - 2 * lax.rem(tile_at, 2)
    near_move = jnp.where(tile_at + near < tiles, near - 1, BEYOND)
    far_move = jnp.where((tile_at >= near) & (tile_at - near < tiles), -near - 2, BEYOND)
    row_from = lax.broadcasted_iota(jnp.int32, (8, LANES), 1)
    moved = jnp.where(row_from < rows, 0, jnp.where(row_from < 2 * rows, near_move, far_move))
    sub = lax.broadcasted_iota(jnp.int32, (8, LANES), 0)
    lane = lax.broadcasted_iota(jnp.int32, (8, LANES), 1)
    shift = (sub - jnp.where(lane < LANES // 2, lane, lane - LANES) - HALF).astype(jnp.float32)
    for k in range(NB):
        norm = tap_norm(SIGMAS[k], order_ref[0, k])
        for r in range(0, rows, 16):
            parts = []
            for half in (r, r + 8):
                offset = (row_from + moved * rows - sub - half).astype(jnp.float32)
                parts.append(tap_values(offset, SIGMAS[k], order_ref[0, k]) / norm)
            both = jnp.concatenate(parts, axis=0).astype(jnp.bfloat16)
            row_ref[k * rows + r : k * rows + r + 16] = both[:, : 3 * rows]
        norm = tap_norm(SIGMAS[k], order_ref[1, k])
        pattern = tap_values(shift, SIGMAS[k], order_ref[1, k]) / norm
        for r in range(0, 2 * LANES, 16):
            parts = []
            for half in (r, r + 8):
                moved_on = pltpu.roll(pattern, half % LANES, 1) if half % LANES else pattern
                inside = lane <= half + 7 if half < LANES else lane >= half - LANES + LANES // 2
                parts.append(jnp.where(inside, moved_on, 0.0))
            col_ref[k, r : r + 16] = jnp.concatenate(parts, axis=0).astype(jnp.bfloat16)


def image_blocks(ref, size, shift, chunk):
    first = chunk + LANES if joint(shift, size) else 0
    return lambda b: ref[:, first + b * LANES : first + (b + 1) * LANES].astype(jnp.float32)


def fit_kernel(weight_ref, hits_ref, row_band_ref, col_band_ref, own_ref, near_ref, far_ref, *refs, width):
    *image_refs, conv_ref, sums_ref, row_ref, parts_ref = refs
    image_refs = dict(zip(middle_first(len(image_refs)), image_refs))
    tile_at = lax.axis_index("tile")
    expo_at = lax.axis_index("expo")
    rows, ext = own_ref.shape
    expos = len(image_refs)
    chunk = ext - LANES
    blocks = chunk // LANES

    patch = jnp.concatenate([own_ref[...], near_ref[...], far_ref[...]], axis=0)
    row_ref[...] = jnp.dot(
        row_band_ref[...], patch, preferred_element_type=jnp.float32
    ).astype(jnp.bfloat16)
    for k in range(NB):
        window = jnp.concatenate(
            [
                row_ref[k * rows : (k + 1) * rows, b * LANES : (b + 2) * LANES]
                for b in range(blocks)
            ],
            axis=0,
        )
        out = jnp.dot(window, col_band_ref[k], preferred_element_type=jnp.float32)
        conv_ref[k] = out.reshape(blocks, rows, LANES)

    first_col = expo_at * chunk
    xs = [column_positions(first_col, b, width) for b in range(blocks)]

    def fold(x):
        total = x[:8]
        for i in range(8, rows, 8):
            total = total + x[i : i + 8]
        return total

    def moments(at, left, right, count):
        total = [None] * count
        for b in range(blocks):
            term = fold(left(b) * right(b)) if right is not None else fold(left(b))
            for i in range(count):
                total[i] = term if total[i] is None else total[i] + term
                if i < count - 1:
                    term = term * xs[b]
        for i in range(count):
            parts_ref[at + i] = total[i]

    def conv(k):
        return lambda b: conv_ref[k, b]

    def sci(shift):
        return image_blocks(image_refs[shift], expos, shift, chunk)

    blank = jnp.zeros((8, LANES), jnp.float32)
    at = 0
    for j, k in PAIRS:
        moments(at, conv(j), conv(k), 3)
        at += 3
    for k in range(NB):
        moments(at, conv(k), None, 2)
        at += 2
    while at % 8:
        parts_ref[at] = blank
        at += 1
    begin = at
    for shift in range(expos):
        row = at + NU * science_source(expo_at, shift, expos)
        for k in range(NB):
            moments(row + 2 * k, conv(k), sci(shift), 2)
        moments(row + NU - 1, sci(shift), None, 1)
    at += NU * expos
    weight = jnp.broadcast_to(weight_ref[...] * hits_ref[...].astype(jnp.float32), (8, LANES))
    weight = jnp.where(tile_at == 0, weight, 0.0)
    spot = (
        (lax.broadcasted_iota(jnp.int32, (8, LANES), 0) == 0)
        & (lax.broadcasted_iota(jnp.int32, (8, LANES), 1) == 0)
    )
    for e in range(expos):
        parts_ref[at + e] = jnp.where(spot & (expo_at == e), weight, 0.0)
    at += expos
    while at % 8:
        parts_ref[at] = blank
        at += 1
    ones = jnp.ones((8, LANES), jnp.float32)
    rows_of = []
    for first, last in ((0, begin), (begin, at)):
        lanes = jnp.sum(parts_ref[first:last], axis=1)
        spare = LANES - (last - first)
        if spare:
            lanes = jnp.concatenate([lanes, jnp.zeros((spare, LANES), jnp.float32)], axis=0)
        rows_of.append(
            lax.dot_general(
                ones,
                lanes,
                (((1,), (1,)), ((), ())),
                precision=lax.Precision.HIGHEST,
                preferred_element_type=jnp.float32,
            )
        )
    both = jnp.where(lax.broadcasted_iota(jnp.int32, (8, LANES), 0) < 4, rows_of[0], rows_of[1])
    for i in range(sums_ref.shape[0]):
        sums_ref[i] = both


def table(expos):
    columns = np.zeros((NU + expos + 1, 16), np.int32)
    for at, (j, k) in enumerate(PAIRS):
        for a, b in ((j, k), (k, j)):
            columns[b, a] = 3 * at
            columns[NB + b, a] = columns[b, NB + a] = 3 * at + 1
            columns[NB + b, NB + a] = 3 * at + 2
    for k in range(NB):
        for x in range(2):
            columns[NU - 1, x * NB + k] = columns[x * NB + k, NU - 1] = 3 * len(PAIRS) + 2 * k + x
    for e in range(expos):
        columns[NU + e, :NU] = [NU * e + 2 * k + x for x in range(2) for k in range(NB)] + [NU * e + NU - 1]
        columns[NU + expos, e] = NU * expos + e
    return np.ascontiguousarray(np.broadcast_to(columns[:, :, None], columns.shape + (LANES,)))


def solve_kernel(table_ref, sums_ref, conv_ref, *refs, width, pixels):
    *image_refs, coadd_ref, coeffs_ref, tile_ref, sems = refs
    expo_at = lax.axis_index("expo")
    expos = len(image_refs)
    rows, chunk = coadd_ref.shape
    blocks = chunk // LANES
    images = [image_blocks(ref, expos, shift, chunk) for shift, ref in enumerate(image_refs)]
    sub = lax.broadcasted_iota(jnp.int32, (16, LANES), 0)
    lane = lax.broadcasted_iota(jnp.int32, (16, LANES), 1)
    sums = sums_ref[0]
    for i in range(1, sums_ref.shape[0]):
        sums = sums + sums_ref[i]
    first = jnp.broadcast_to(sums[0:1], (16, LANES))
    second = jnp.broadcast_to(sums[4:5], (16, LANES))

    columns = [
        jnp.take_along_axis(first if j < NU else second, table_ref[j], axis=1) for j in range(NU + expos)
    ]
    spread = jnp.take_along_axis(second, table_ref[NU + expos], axis=1)
    weight = [jnp.broadcast_to(spread[e : e + 1], (16, LANES)) for e in range(expos)]
    columns[NU - 1] = jnp.where(sub == NU - 1, float(pixels), columns[NU - 1])

    trace = columns[0][0:1]
    for j in range(1, NU):
        trace = trace + columns[j][j : j + 1]
    scale = 1.0 / trace
    for j in range(NU + expos):
        columns[j] = columns[j] * scale
        if j < NU:
            columns[j] = columns[j] + jnp.where(sub == j, RIDGE / NU, 0.0)
    for i in range(NU):
        inverse = 1.0 / columns[i][i : i + 1]
        for j in range(i + 1, NU + expos):
            factor = columns[j][i : i + 1] * inverse
            columns[j] = jnp.where(sub == i, factor, columns[j] - columns[i] * factor)

    solved = columns[NU:]
    own = solved[0]
    mixed = weight[0] * solved[0]
    for e in range(1, expos):
        own = jnp.where(expo_at == e, solved[e], own)
        mixed = mixed + weight[e] * solved[e]
    diagonal = (sub == lane) & (sub < NU)
    coeffs_ref[...] = jnp.sum(jnp.where(diagonal, own, 0.0), axis=0, keepdims=True)[:, :NU]
    scale = [jnp.broadcast_to(mixed[u : u + 1], (8, LANES)) for u in range(NU)]
    gains = []
    for shift in range(expos):
        gain = weight[0][:8]
        for e in range(1, expos):
            gain = jnp.where(science_source(expo_at, shift, expos) == e, weight[e][:8], gain)
        gains.append(gain)
    first_col = expo_at * chunk
    copies = []
    for r in range(0, rows, 8):
        for b in range(blocks):
            x = column_positions(first_col, b, width)
            total = -scale[NU - 1]
            for gain, image in zip(gains, images):
                total = total + gain * image(b)[r : r + 8]
            model = (scale[0] + scale[NB] * x) * conv_ref[0, b, r : r + 8]
            for k in range(1, NB):
                model = model + (scale[k] + scale[NB + k] * x) * conv_ref[k, b, r : r + 8]
            tile_ref[r : r + 8, b * LANES : (b + 1) * LANES] = total - model
        copies.append(
            pltpu.make_async_copy(tile_ref.at[pl.ds(r, 8)], coadd_ref.at[pl.ds(r, 8)], sems.at[r // 8])
        )
        copies[-1].start()
    for copy in copies:
        copy.wait()


def swaps(first, size):
    pairs = [(i, i + 1) for i in range(first, size - 1, 2)]
    if first and size % 2 == 0:
        pairs.append((0, size - 1))
    return [pair for a, b in pairs for pair in ((a, b), (b, a))]


def service_order(expos, tiles):
    early = list(range(tiles // 2))
    late = list(reversed(range(expos // 2 * tiles, expos * tiles)))
    return early + [i for i in late if i not in early] + list(range(len(early), expos // 2 * tiles))


def tiled_device(template, science, plan, orders, coadd_weight, intersection):
    expos = lax.axis_size("expo")
    tiles = lax.axis_size("tile")
    _, rows, width = template.shape
    steps = science.shape[1]
    chunk = width // expos
    ext = chunk + LANES
    blocks = chunk // LANES
    vmem = pl.BlockSpec(memory_space=pltpu.VMEM)
    small = pltpu.CompilerParams(vmem_limit_bytes=16 * 1024 * 1024)
    hbm = pl.BlockSpec(memory_space=pltpu.HBM)
    coadds = []
    fitted = []
    for step in range(steps):
        *blocks_out, owner, order = pl.pallas_call(
            functools.partial(send_kernel, step=step),
            out_shape=tuple(
                pltpu.VMEM((rows, ext + chunk if joint(shift, expos) else ext), template.dtype)
                for shift in range(expos)
            )
            + (pltpu.VMEM((rows, ext), science.dtype),) * (expos - expos // 2)
            + (
                jax.ShapeDtypeStruct((rows, LANES), jnp.int32),
                jax.ShapeDtypeStruct((2, NB, 8, LANES), jnp.int32),
            ),
            in_specs=[hbm] * 4,
            out_specs=(vmem,) * (2 * expos - expos // 2 + 2),
            scratch_shapes=[
                pltpu.VMEM((rows, width + 2 * LANES), template.dtype),
                pltpu.SMEM(plan.shape, jnp.int32),
                pltpu.SMEM((2, NB), jnp.int32),
                pltpu.SemaphoreType.DMA((expos + 4,)),
            ],
            compiler_params=small,
        )(
            pltpu.with_memory_space_constraint(template[0], pltpu.HBM),
            pltpu.with_memory_space_constraint(science[0, step], pltpu.HBM),
            pltpu.with_memory_space_constraint(plan, pltpu.HBM),
            pltpu.with_memory_space_constraint(orders.T, pltpu.HBM),
        )
        patches, images = blocks_out[:expos], blocks_out[expos:]
        for group, first, to in ((patches, 0, target), (images, expos // 2, science_target)):
            for shift in range(max(first, 1), expos):
                pairs = [(e, int(to(e, shift, expos))) for e in range(expos)]
                group[shift - first] = lax.ppermute(group[shift - first], "expo", pairs)
        images = patches[: expos // 2] + images
        across = [shift for shift in far_first(expos)[:-1] if not joint(shift, expos)]
        beside = [shift for shift in far_first(expos)[:-1] if joint(shift, expos)]
        block = pl.pallas_call(
            functools.partial(choose_kernel, shifts=across, size=expos),
            out_shape=jax.ShapeDtypeStruct((rows, ext), template.dtype),
            in_specs=[vmem] * (2 + len(across)),
            out_specs=vmem,
            compiler_params=small,
            cost_estimate=pl.CostEstimate(flops=STAGE_COST, bytes_accessed=500_000, transcendentals=0),
        )(owner, patches[0], *(patches[shift] for shift in across))
        own = pl.pallas_call(
            functools.partial(pick_kernel, shifts=beside, size=expos),
            out_shape=jax.ShapeDtypeStruct((rows, ext), template.dtype),
            in_specs=[vmem] * (2 + len(beside)),
            out_specs=vmem,
            scratch_shapes=[pltpu.VMEM((rows, ext), template.dtype)],
            compiler_params=small,
        )(owner, block, *(patches[shift] for shift in beside))
        row_band, col_band = pl.pallas_call(
            functools.partial(band_kernel, tiles=tiles),
            out_shape=(
                jax.ShapeDtypeStruct((NB * rows, 3 * rows), jnp.bfloat16),
                jax.ShapeDtypeStruct((NB, 2 * LANES, LANES), jnp.bfloat16),
            ),
            in_specs=[vmem, pl.BlockSpec(memory_space=pl.ANY)],
            out_specs=(vmem, vmem),
            compiler_params=small,
            cost_estimate=pl.CostEstimate(flops=4_000_000, bytes_accessed=500_000, transcendentals=200_000),
        )(order, own)
        far = lax.ppermute(own, "tile", swaps(1, tiles))
        near = lax.ppermute(own, "tile", swaps(0, tiles))
        conv, sums = pl.pallas_call(
            functools.partial(fit_kernel, width=width),
            out_shape=(
                jax.ShapeDtypeStruct((NB, blocks, rows, LANES), jnp.float32),
                jax.ShapeDtypeStruct((tiles * expos, 8, LANES), jnp.float32),
            ),
            in_specs=[vmem] * (7 + expos),
            out_specs=(vmem, vmem),
            scratch_shapes=[
                pltpu.VMEM((NB * rows, ext), jnp.bfloat16),
                pltpu.VMEM((80 + 14 * expos + 8, 8, LANES), jnp.float32),
            ],
            compiler_params=small,
        )(
            coadd_weight[:, step : step + 1],
            intersection[:, step : step + 1],
            row_band,
            col_band,
            own,
            near,
            far,
            *(images[shift] for shift in middle_first(expos)),
        )
        group = list(reversed(service_order(expos, tiles)))
        sums = lax.all_to_all(
            sums, ("expo", "tile"), split_axis=0, concat_axis=0, tiled=True, axis_index_groups=[group]
        )
        coadd, coeffs = pl.pallas_call(
            functools.partial(solve_kernel, width=width, pixels=tiles * rows * width),
            out_shape=(
                jax.ShapeDtypeStruct((rows, chunk), jnp.float32),
                jax.ShapeDtypeStruct((1, NU), jnp.float32),
            ),
            in_specs=[vmem] * (3 + expos),
            out_specs=(pl.BlockSpec(memory_space=pl.ANY), vmem),
            scratch_shapes=[
                pltpu.VMEM((rows, chunk), jnp.float32),
                pltpu.SemaphoreType.DMA((rows // 8,)),
            ],
            compiler_params=small,
        )(jnp.asarray(table(expos)), sums, conv, *images)
        coadds.append(coadd[None])
        fitted.append(coeffs)
    return (jnp.concatenate(coadds), jnp.stack(fitted, axis=1))


def broadcast(block, axis, holder):
    block = jnp.where(lax.axis_index(axis) == holder, block, jnp.zeros_like(block))
    return lax.psum(block, axis)


def extended(x, sides, width):
    for axis, dim in sides:
        size, length = (lax.axis_size(axis), x.shape[dim])
        up = [(i, (i + 1) % size) for i in range(size - 1)]
        down = [(j, i) for i, j in up]
        last = lax.slice_in_dim(x, length - width, length, axis=dim)
        first = lax.slice_in_dim(x, 0, width, axis=dim)
        before = lax.ppermute(last, axis, up)
        after = lax.ppermute(first, axis, down)
        x = jnp.concatenate([before, x, after], axis=dim)
    return x


def make_filters(orders):
    taps_pos = jnp.arange(2 * HALF + 1).astype(jnp.float32) - HALF
    row_list = []
    col_list = []
    for basis in range(NB):
        sigma = SIGMAS[basis]
        envelope = jnp.exp(-taps_pos * taps_pos / (2.0 * sigma * sigma))
        row_filter = envelope * power_of(taps_pos, orders[basis, 0])
        col_filter = envelope * power_of(taps_pos, orders[basis, 1])
        row_list.append(row_filter / jnp.sqrt(jnp.sum(row_filter * row_filter)))
        col_list.append(col_filter / jnp.sqrt(jnp.sum(col_filter * col_filter)))
    return (jnp.stack(row_list).astype(jnp.bfloat16), jnp.stack(col_list).astype(jnp.bfloat16))


def band_matrix(filters, out_len, in_len):
    offset = jnp.arange(in_len)[None, :] - jnp.arange(out_len)[:, None]
    taps_idx = jnp.arange(2 * HALF + 1)
    picks = (offset[:, :, None] == taps_idx[None, None, :]).astype(jnp.float32)
    band = jnp.einsum("ijt,kt->kij", picks, filters.astype(jnp.float32))
    return band.astype(jnp.bfloat16)


def any_device(template, science, plan, orders, coadd_weight, intersection):
    row_filters, col_filters = make_filters(orders)
    rows = template.shape[1]
    width = template.shape[2]
    blocks_count = width // 128
    steps_count = science.shape[1]
    row_band = band_matrix(row_filters, rows, rows + 2 * HALF)
    col_band = jnp.transpose(band_matrix(col_filters, 128, 128 + 2 * HALF), (0, 2, 1))
    column_pos = 2.0 * (jnp.arange(width).astype(jnp.float32) + 0.5) / width - 1.0
    pieces = []
    fitted = []
    for step in range(steps_count):
        received = broadcast(template[0], "expo", plan[step])
        padded = extended(received, (("tile", 0),), HALF)
        rowconv = jnp.einsum(
            "kij,jw->kiw", row_band, padded, preferred_element_type=jnp.float32
        ).astype(jnp.bfloat16)
        blocks = rowconv.reshape(NB, rows, blocks_count, 128)
        empty_rim = jnp.zeros((NB, rows, 1, HALF), jnp.bfloat16)
        previous = jnp.concatenate([empty_rim, blocks[:, :, :-1, 128 - HALF :]], axis=2)
        following = jnp.concatenate([blocks[:, :, 1:, :HALF], empty_rim], axis=2)
        window = jnp.concatenate([previous, blocks, following], axis=3)
        conv = jnp.einsum("krbj,kjc->krbc", window, col_band, preferred_element_type=jnp.float32)
        conv = conv.reshape(NB, rows, width)
        fields = jnp.concatenate(
            [conv, conv * column_pos, jnp.ones((1, rows, width), jnp.float32)], axis=0
        )
        fields = fields.reshape(NU, rows * width)
        exposure_image = science[0, step].astype(jnp.float32).reshape(rows * width)
        normal_local = jnp.dot(fields, fields.T, precision=lax.Precision.HIGHEST)
        project_local = jnp.dot(fields, exposure_image, precision=lax.Precision.HIGHEST)
        normal_matrix, projections = lax.psum((normal_local, project_local), "tile")
        normal_matrix = normal_matrix + RIDGE * (jnp.trace(normal_matrix) / NU) * jnp.eye(
            NU, dtype=jnp.float32
        )
        factor = jnp.linalg.cholesky(normal_matrix)
        coeffs = jax.scipy.linalg.cho_solve((factor, True), projections)
        model = jnp.dot(coeffs, fields, precision=lax.Precision.HIGHEST)
        difference = exposure_image - model
        weight_now = coadd_weight[0, step] * intersection[0, step].astype(jnp.float32)
        pieces.append((weight_now * difference).reshape(rows, width))
        fitted.append(coeffs)
    weighted = jnp.stack(pieces)
    received_parts = lax.all_to_all(weighted[None], "expo", split_axis=3, concat_axis=0, tiled=True)
    coadd = jnp.sum(received_parts, axis=0)
    return (coadd, jnp.stack(fitted)[None])


def per_device(template, science, plan, orders, coadd_weight, intersection):
    expos = lax.axis_size("expo")
    rows, width = template.shape[1:]
    whole_lanes = width % (expos * LANES) == 0 and rows % 16 == 0 and 3 * rows <= LANES
    few = (NU + 1) * expos <= LANES and NU + expos <= LANES
    body = tiled_device if whole_lanes and few else any_device
    return body(template, science, plan, orders, coadd_weight, intersection)


def solution(mesh):
    return jax.shard_map(
        per_device,
        mesh=mesh,
        in_specs=(
            P(("groups", "expo"), "tile", None),
            P(("groups", "expo"), None, "tile", None),
            P("groups"),
            P(),
            P(("groups", "expo"), None),
            P(("groups", "expo"), None),
        ),
        out_specs=(P("groups", "tile", "expo"), P(("groups", "expo"), None, None)),
        check_vma=False,
    )
```

```python
import functools

import jax
import jax.numpy as jnp
import numpy as np
from jax import lax
from jax.experimental import pallas as pl
from jax.experimental.pallas import tpu as pltpu
from jax.sharding import PartitionSpec as P

HALF = 15
NB = 6
NU = 13
LANES = 128
BEYOND = 1000
STAGE_COST = 700_000_000
PAIRS = [(j, k) for j in range(NB) for k in range(j, NB)]

SIGMAS = (0.8, 1.4, 2.2, 3.0, 4.0, 5.5)
RIDGE = 0.05


def power_of(pos, order):
    return jnp.where(order == 0, 1.0, jnp.where(order == 1, pos, pos * pos))


def tap_values(pos, sigma, order):
    value = jnp.exp(-pos * pos / (2.0 * sigma * sigma)) * power_of(pos, order)
    return jnp.where(jnp.abs(pos) <= HALF, value, 0.0)


def tap_norm(sigma, order):
    pos = lax.broadcasted_iota(jnp.int32, (8, LANES), 1).astype(jnp.float32) - HALF
    value = tap_values(pos, sigma, order)
    return jnp.sqrt(jnp.sum(value * value, axis=1, keepdims=True))


def target(me, shift, size):
    return me ^ shift if size & (size - 1) == 0 else (me + shift) % size


def source(me, shift, size):
    return me ^ shift if size & (size - 1) == 0 else (me - shift + size) % size


def far_first(size):
    return [*range(size - 1, 0, -1), 0]


def joint(shift, size):
    return shift < size // 2


def send_kernel(template_ref, science_ref, plan_ref, orders_ref, *refs, step):
    *out_refs, owner_ref, order_ref, patch_ref, plan_now, orders_now, sems = refs
    size = sems.shape[0] - 4
    rows, width = science_ref.shape
    chunk = width // size
    ext = chunk + LANES
    patch_refs, image_refs = out_refs[:size], out_refs[size:]
    half = size * chunk // 2
    me = lax.axis_index("expo")
    starts = [pl.multiple_of(target(me, shift, size) * chunk, chunk) for shift in range(size)]
    loads = [
        pltpu.make_async_copy(
            template_ref.at[:, pl.ds(i * half, half)], patch_ref.at[:, pl.ds((i * half + LANES), half)], sems.at[i]
        )
        for i in range(2)
    ]
    copies = [
        pltpu.make_async_copy(
            science_ref.at[:, pl.ds(starts[shift], chunk)],
            patch_refs[shift].at[:, pl.ds(ext, chunk)]
            if joint(shift, size)
            else image_refs[shift - size // 2].at[:, pl.ds(0, chunk)],
            sems.at[3 + shift],
        )
        for shift in range(size)
    ]
    copies.append(pltpu.make_async_copy(plan_ref, plan_now, sems.at[2]))
    copies.append(pltpu.make_async_copy(orders_ref, orders_now, sems.at[3 + size]))
    for copy in loads + copies:
        copy.start()
    blank = jnp.zeros((rows, LANES), patch_ref.dtype)
    patch_ref[:, :LANES] = blank
    patch_ref[:, size * chunk + LANES :] = blank
    for image_ref in image_refs:
        image_ref[:, chunk:] = blank
    for copy in loads:
        copy.wait()
    lane = lax.broadcasted_iota(jnp.int32, (rows, LANES), 1)
    for shift in range(size):
        start = starts[shift]
        patch_refs[shift][:, :chunk] = patch_ref[:, pl.ds(start + LANES, chunk)]
        before = patch_ref[:, pl.ds(start, LANES)].astype(jnp.float32)
        after = patch_ref[:, pl.ds(start + chunk + LANES, LANES)].astype(jnp.float32)
        rim = jnp.where(lane < LANES // 2, after, before)
        patch_refs[shift][:, chunk:ext] = rim.astype(patch_ref.dtype)
    for copy in copies:
        copy.wait()
    owner_ref[...] = jnp.full(owner_ref.shape, plan_now[step], jnp.int32)
    for way in range(2):
        for k in range(NB):
            order_ref[way, k] = jnp.full((8, LANES), orders_now[way, k], jnp.int32)


def choose_kernel(owner_ref, *refs, shifts, size):
    *recv_refs, out_ref = refs
    me = lax.axis_index("expo")
    for b in range(out_ref.shape[1] // LANES):
        columns = slice(b * LANES, (b + 1) * LANES)
        block = recv_refs[0][:, columns].astype(jnp.float32)
        for shift, ref in zip(shifts, recv_refs[1:]):
            block = jnp.where(
                owner_ref[...] == source(me, shift, size), ref[:, columns].astype(jnp.float32), block
            )
        out_ref[:, columns] = block.astype(out_ref.dtype)


def pick_kernel(owner_ref, *refs, shifts, size):
    *recv_refs, out_ref, block_ref = refs
    ext = out_ref.shape[1]
    choose_kernel(owner_ref, *recv_refs, block_ref, shifts=shifts, size=size)
    whole = jnp.concatenate([block_ref[:, ext - LANES :], block_ref[...]], axis=1)
    out_ref[...] = whole[:, LANES - HALF : LANES - HALF + ext]


def column_positions(first_col, block, width):
    col = lax.broadcasted_iota(jnp.int32, (8, LANES), 1) + (first_col + block * LANES)
    return 2.0 * (col.astype(jnp.float32) + 0.5) / width - 1.0


def band_kernel(order_ref, _, row_ref, col_ref, *, tiles):
    rows = row_ref.shape[0] // NB
    tile_at = lax.axis_index("tile")
    near = 1 - 2 * lax.rem(tile_at, 2)
    near_move = jnp.where(tile_at + near < tiles, near - 1, BEYOND)
    far_move = jnp.where((tile_at >= near) & (tile_at - near < tiles), -near - 2, BEYOND)
    row_from = lax.broadcasted_iota(jnp.int32, (8, LANES), 1)
    moved = jnp.where(row_from < rows, 0, jnp.where(row_from < 2 * rows, near_move, far_move))
    sub = lax.broadcasted_iota(jnp.int32, (8, LANES), 0)
    lane = lax.broadcasted_iota(jnp.int32, (8, LANES), 1)
    shift = (sub - jnp.where(lane < LANES // 2, lane, lane - LANES) - HALF).astype(jnp.float32)
    for k in range(NB):
        norm = tap_norm(SIGMAS[k], order_ref[0, k])
        for r in range(0, rows, 16):
            parts = []
            for half in (r, r + 8):
                offset = (row_from + moved * rows - sub - half).astype(jnp.float32)
                parts.append(tap_values(offset, SIGMAS[k], order_ref[0, k]) / norm)
            both = jnp.concatenate(parts, axis=0).astype(jnp.bfloat16)
            row_ref[k * rows + r : k * rows + r + 16] = both[:, : 3 * rows]
        norm = tap_norm(SIGMAS[k], order_ref[1, k])
        pattern = tap_values(shift, SIGMAS[k], order_ref[1, k]) / norm
        for r in range(0, 2 * LANES, 16):
            parts = []
            for half in (r, r + 8):
                moved_on = pltpu.roll(pattern, half % LANES, 1) if half % LANES else pattern
                inside = lane <= half + 7 if half < LANES else lane >= half - LANES + LANES // 2
                parts.append(jnp.where(inside, moved_on, 0.0))
            col_ref[k, r : r + 16] = jnp.concatenate(parts, axis=0).astype(jnp.bfloat16)


def image_blocks(ref, size, shift, chunk):
    first = chunk + LANES if joint(shift, size) else 0
    return lambda b: ref[:, first + b * LANES : first + (b + 1) * LANES].astype(jnp.float32)


def fit_kernel(weight_ref, hits_ref, row_band_ref, col_band_ref, own_ref, near_ref, far_ref, *refs, width):
    *image_refs, conv_ref, sums_ref, row_ref, parts_ref = refs
    image_refs = dict(zip(far_first(len(image_refs)), image_refs))
    tile_at = lax.axis_index("tile")
    expo_at = lax.axis_index("expo")
    rows, ext = own_ref.shape
    expos = len(image_refs)
    chunk = ext - LANES
    blocks = chunk // LANES

    patch = jnp.concatenate([own_ref[...], near_ref[...], far_ref[...]], axis=0)
    row_ref[...] = jnp.dot(
        row_band_ref[...], patch, preferred_element_type=jnp.float32
    ).astype(jnp.bfloat16)
    for k in range(NB):
        window = jnp.concatenate(
            [
                row_ref[k * rows : (k + 1) * rows, b * LANES : (b + 2) * LANES]
                for b in range(blocks)
            ],
            axis=0,
        )
        out = jnp.dot(window, col_band_ref[k], preferred_element_type=jnp.float32)
        conv_ref[k] = out.reshape(blocks, rows, LANES)

    first_col = expo_at * chunk
    xs = [column_positions(first_col, b, width) for b in range(blocks)]

    def fold(x):
        total = x[:8]
        for i in range(8, rows, 8):
            total = total + x[i : i + 8]
        return total

    def moments(at, left, right, count):
        total = [None] * count
        for b in range(blocks):
            term = fold(left(b) * right(b)) if right is not None else fold(left(b))
            for i in range(count):
                total[i] = term if total[i] is None else total[i] + term
                if i < count - 1:
                    term = term * xs[b]
        for i in range(count):
            parts_ref[at + i] = total[i]

    def conv(k):
        return lambda b: conv_ref[k, b]

    def sci(shift):
        return image_blocks(image_refs[shift], expos, shift, chunk)

    blank = jnp.zeros((8, LANES), jnp.float32)
    at = 0
    for j, k in PAIRS:
        moments(at, conv(j), conv(k), 3)
        at += 3
    for k in range(NB):
        moments(at, conv(k), None, 2)
        at += 2
    while at % 8:
        parts_ref[at] = blank
        at += 1
    begin = at
    for shift in range(expos):
        row = at + NU * source(expo_at, shift, expos)
        for k in range(NB):
            moments(row + 2 * k, conv(k), sci(shift), 2)
        moments(row + NU - 1, sci(shift), None, 1)
    at += NU * expos
    weight = jnp.broadcast_to(weight_ref[...] * hits_ref[...].astype(jnp.float32), (8, LANES))
    weight = jnp.where(tile_at == 0, weight, 0.0)
    spot = (
        (lax.broadcasted_iota(jnp.int32, (8, LANES), 0) == 0)
        & (lax.broadcasted_iota(jnp.int32, (8, LANES), 1) == 0)
    )
    for e in range(expos):
        parts_ref[at + e] = jnp.where(spot & (expo_at == e), weight, 0.0)
    at += expos
    while at % 8:
        parts_ref[at] = blank
        at += 1
    ones = jnp.ones((8, LANES), jnp.float32)
    rows_of = []
    for first, last in ((0, begin), (begin, at)):
        lanes = jnp.sum(parts_ref[first:last], axis=1)
        spare = LANES - (last - first)
        if spare:
            lanes = jnp.concatenate([lanes, jnp.zeros((spare, LANES), jnp.float32)], axis=0)
        rows_of.append(
            lax.dot_general(
                ones,
                lanes,
                (((1,), (1,)), ((), ())),
                precision=lax.Precision.HIGHEST,
                preferred_element_type=jnp.float32,
            )
        )
    both = jnp.where(lax.broadcasted_iota(jnp.int32, (8, LANES), 0) < 4, rows_of[0], rows_of[1])
    for i in range(sums_ref.shape[0]):
        sums_ref[i] = both


def table(expos):
    columns = np.zeros((NU + expos + 1, 16), np.int32)
    for at, (j, k) in enumerate(PAIRS):
        for a, b in ((j, k), (k, j)):
            columns[b, a] = 3 * at
            columns[NB + b, a] = columns[b, NB + a] = 3 * at + 1
            columns[NB + b, NB + a] = 3 * at + 2
    for k in range(NB):
        for x in range(2):
            columns[NU - 1, x * NB + k] = columns[x * NB + k, NU - 1] = 3 * len(PAIRS) + 2 * k + x
    for e in range(expos):
        columns[NU + e, :NU] = [NU * e + 2 * k + x for x in range(2) for k in range(NB)] + [NU * e + NU - 1]
        columns[NU + expos, e] = NU * expos + e
    return np.ascontiguousarray(np.broadcast_to(columns[:, :, None], columns.shape + (LANES,)))


def solve_kernel(table_ref, sums_ref, conv_ref, *refs, width, pixels):
    *image_refs, coadd_ref, coeffs_ref, tile_ref, sems = refs
    expo_at = lax.axis_index("expo")
    expos = len(image_refs)
    rows, chunk = coadd_ref.shape
    blocks = chunk // LANES
    images = [image_blocks(ref, expos, shift, chunk) for shift, ref in enumerate(image_refs)]
    sub = lax.broadcasted_iota(jnp.int32, (16, LANES), 0)
    lane = lax.broadcasted_iota(jnp.int32, (16, LANES), 1)
    sums = sums_ref[0]
    for i in range(1, sums_ref.shape[0]):
        sums = sums + sums_ref[i]
    first = jnp.broadcast_to(sums[0:1], (16, LANES))
    second = jnp.broadcast_to(sums[4:5], (16, LANES))

    columns = [
        jnp.take_along_axis(first if j < NU else second, table_ref[j], axis=1) for j in range(NU + expos)
    ]
    spread = jnp.take_along_axis(second, table_ref[NU + expos], axis=1)
    weight = [jnp.broadcast_to(spread[e : e + 1], (16, LANES)) for e in range(expos)]
    columns[NU - 1] = jnp.where(sub == NU - 1, float(pixels), columns[NU - 1])

    trace = columns[0][0:1]
    for j in range(1, NU):
        trace = trace + columns[j][j : j + 1]
    scale = 1.0 / trace
    for j in range(NU + expos):
        columns[j] = columns[j] * scale
        if j < NU:
            columns[j] = columns[j] + jnp.where(sub == j, RIDGE / NU, 0.0)
    for i in range(NU):
        inverse = 1.0 / columns[i][i : i + 1]
        for j in range(i + 1, NU + expos):
            factor = columns[j][i : i + 1] * inverse
            columns[j] = jnp.where(sub == i, factor, columns[j] - columns[i] * factor)

    solved = columns[NU:]
    own = solved[0]
    mixed = weight[0] * solved[0]
    for e in range(1, expos):
        own = jnp.where(expo_at == e, solved[e], own)
        mixed = mixed + weight[e] * solved[e]
    diagonal = (sub == lane) & (sub < NU)
    coeffs_ref[...] = jnp.sum(jnp.where(diagonal, own, 0.0), axis=0, keepdims=True)[:, :NU]
    scale = [jnp.broadcast_to(mixed[u : u + 1], (8, LANES)) for u in range(NU)]
    gains = []
    for shift in range(expos):
        gain = weight[0][:8]
        for e in range(1, expos):
            gain = jnp.where(source(expo_at, shift, expos) == e, weight[e][:8], gain)
        gains.append(gain)
    first_col = expo_at * chunk
    copies = []
    for r in range(0, rows, 8):
        for b in range(blocks):
            x = column_positions(first_col, b, width)
            total = -scale[NU - 1]
            for gain, image in zip(gains, images):
                total = total + gain * image(b)[r : r + 8]
            model = (scale[0] + scale[NB] * x) * conv_ref[0, b, r : r + 8]
            for k in range(1, NB):
                model = model + (scale[k] + scale[NB + k] * x) * conv_ref[k, b, r : r + 8]
            tile_ref[r : r + 8, b * LANES : (b + 1) * LANES] = total - model
        copies.append(
            pltpu.make_async_copy(tile_ref.at[pl.ds(r, 8)], coadd_ref.at[pl.ds(r, 8)], sems.at[r // 8])
        )
        copies[-1].start()
    for copy in copies:
        copy.wait()


def swaps(first, size):
    pairs = [(i, i + 1) for i in range(first, size - 1, 2)]
    if first and size % 2 == 0:
        pairs.append((0, size - 1))
    return [pair for a, b in pairs for pair in ((a, b), (b, a))]


def service_order(expos, tiles):
    early = list(range(tiles // 2))
    late = list(reversed(range(expos // 2 * tiles, expos * tiles)))
    order = late[:tiles] + early + late[tiles:] + list(range(len(early), expos // 2 * tiles))
    return list(dict.fromkeys(order))


def tiled_device(template, science, plan, orders, coadd_weight, intersection):
    expos = lax.axis_size("expo")
    tiles = lax.axis_size("tile")
    _, rows, width = template.shape
    steps = science.shape[1]
    chunk = width // expos
    ext = chunk + LANES
    blocks = chunk // LANES
    vmem = pl.BlockSpec(memory_space=pltpu.VMEM)
    small = pltpu.CompilerParams(vmem_limit_bytes=16 * 1024 * 1024)
    hbm = pl.BlockSpec(memory_space=pltpu.HBM)
    coadds = []
    fitted = []
    for step in range(steps):
        *blocks_out, owner, order = pl.pallas_call(
            functools.partial(send_kernel, step=step),
            out_shape=tuple(
                pltpu.VMEM((rows, ext + chunk if joint(shift, expos) else ext), template.dtype)
                for shift in range(expos)
            )
            + (pltpu.VMEM((rows, ext), science.dtype),) * (expos - expos // 2)
            + (
                jax.ShapeDtypeStruct((rows, LANES), jnp.int32),
                jax.ShapeDtypeStruct((2, NB, 8, LANES), jnp.int32),
            ),
            in_specs=[hbm] * 4,
            out_specs=(vmem,) * (2 * expos - expos // 2 + 2),
            scratch_shapes=[
                pltpu.VMEM((rows, width + 2 * LANES), template.dtype),
                pltpu.SMEM(plan.shape, jnp.int32),
                pltpu.SMEM((2, NB), jnp.int32),
                pltpu.SemaphoreType.DMA((expos + 4,)),
            ],
            compiler_params=small,
        )(
            pltpu.with_memory_space_constraint(template[0], pltpu.HBM),
            pltpu.with_memory_space_constraint(science[0, step], pltpu.HBM),
            pltpu.with_memory_space_constraint(plan, pltpu.HBM),
            pltpu.with_memory_space_constraint(orders.T, pltpu.HBM),
        )
        patches, images = blocks_out[:expos], blocks_out[expos:]
        for group, first in ((patches, 0), (images, expos // 2)):
            for shift in range(max(first, 1), expos):
                pairs = [(e, int(target(e, shift, expos))) for e in range(expos)]
                group[shift - first] = lax.ppermute(group[shift - first], "expo", pairs)
        images = patches[: expos // 2] + images
        across = [shift for shift in far_first(expos)[:-1] if not joint(shift, expos)]
        beside = [shift for shift in far_first(expos)[:-1] if joint(shift, expos)]
        block = pl.pallas_call(
            functools.partial(choose_kernel, shifts=across, size=expos),
            out_shape=jax.ShapeDtypeStruct((rows, ext), template.dtype),
            in_specs=[vmem] * (2 + len(across)),
            out_specs=vmem,
            compiler_params=small,
            cost_estimate=pl.CostEstimate(flops=STAGE_COST, bytes_accessed=500_000, transcendentals=0),
        )(owner, patches[0], *(patches[shift] for shift in across))
        own = pl.pallas_call(
            functools.partial(pick_kernel, shifts=beside, size=expos),
            out_shape=jax.ShapeDtypeStruct((rows, ext), template.dtype),
            in_specs=[vmem] * (2 + len(beside)),
            out_specs=vmem,
            scratch_shapes=[pltpu.VMEM((rows, ext), template.dtype)],
            compiler_params=small,
        )(owner, block, *(patches[shift] for shift in beside))
        row_band, col_band = pl.pallas_call(
            functools.partial(band_kernel, tiles=tiles),
            out_shape=(
                jax.ShapeDtypeStruct((NB * rows, 3 * rows), jnp.bfloat16),
                jax.ShapeDtypeStruct((NB, 2 * LANES, LANES), jnp.bfloat16),
            ),
            in_specs=[vmem, pl.BlockSpec(memory_space=pl.ANY)],
            out_specs=(vmem, vmem),
            compiler_params=small,
            cost_estimate=pl.CostEstimate(flops=4_000_000, bytes_accessed=500_000, transcendentals=200_000),
        )(order, own)
        far = lax.ppermute(own, "tile", swaps(1, tiles))
        near = lax.ppermute(own, "tile", swaps(0, tiles))
        conv, sums = pl.pallas_call(
            functools.partial(fit_kernel, width=width),
            out_shape=(
                jax.ShapeDtypeStruct((NB, blocks, rows, LANES), jnp.float32),
                jax.ShapeDtypeStruct((tiles * expos, 8, LANES), jnp.float32),
            ),
            in_specs=[vmem] * (7 + expos),
            out_specs=(vmem, vmem),
            scratch_shapes=[
                pltpu.VMEM((NB * rows, ext), jnp.bfloat16),
                pltpu.VMEM((80 + 14 * expos + 8, 8, LANES), jnp.float32),
            ],
            compiler_params=small,
        )(
            coadd_weight[:, step : step + 1],
            intersection[:, step : step + 1],
            row_band,
            col_band,
            own,
            near,
            far,
            *(images[shift] for shift in far_first(expos)),
        )
        group = list(reversed(service_order(expos, tiles)))
        sums = lax.all_to_all(
            sums, ("expo", "tile"), split_axis=0, concat_axis=0, tiled=True, axis_index_groups=[group]
        )
        coadd, coeffs = pl.pallas_call(
            functools.partial(solve_kernel, width=width, pixels=tiles * rows * width),
            out_shape=(
                jax.ShapeDtypeStruct((rows, chunk), jnp.float32),
                jax.ShapeDtypeStruct((1, NU), jnp.float32),
            ),
            in_specs=[vmem] * (3 + expos),
            out_specs=(pl.BlockSpec(memory_space=pl.ANY), vmem),
            scratch_shapes=[
                pltpu.VMEM((rows, chunk), jnp.float32),
                pltpu.SemaphoreType.DMA((rows // 8,)),
            ],
            compiler_params=small,
        )(jnp.asarray(table(expos)), sums, conv, *images)
        coadds.append(coadd[None])
        fitted.append(coeffs)
    return (jnp.concatenate(coadds), jnp.stack(fitted, axis=1))


def broadcast(block, axis, holder):
    block = jnp.where(lax.axis_index(axis) == holder, block, jnp.zeros_like(block))
    return lax.psum(block, axis)


def extended(x, sides, width):
    for axis, dim in sides:
        size, length = (lax.axis_size(axis), x.shape[dim])
        up = [(i, (i + 1) % size) for i in range(size - 1)]
        down = [(j, i) for i, j in up]
        last = lax.slice_in_dim(x, length - width, length, axis=dim)
        first = lax.slice_in_dim(x, 0, width, axis=dim)
        before = lax.ppermute(last, axis, up)
        after = lax.ppermute(first, axis, down)
        x = jnp.concatenate([before, x, after], axis=dim)
    return x


def make_filters(orders):
    taps_pos = jnp.arange(2 * HALF + 1).astype(jnp.float32) - HALF
    row_list = []
    col_list = []
    for basis in range(NB):
        sigma = SIGMAS[basis]
        envelope = jnp.exp(-taps_pos * taps_pos / (2.0 * sigma * sigma))
        row_filter = envelope * power_of(taps_pos, orders[basis, 0])
        col_filter = envelope * power_of(taps_pos, orders[basis, 1])
        row_list.append(row_filter / jnp.sqrt(jnp.sum(row_filter * row_filter)))
        col_list.append(col_filter / jnp.sqrt(jnp.sum(col_filter * col_filter)))
    return (jnp.stack(row_list).astype(jnp.bfloat16), jnp.stack(col_list).astype(jnp.bfloat16))


def band_matrix(filters, out_len, in_len):
    offset = jnp.arange(in_len)[None, :] - jnp.arange(out_len)[:, None]
    taps_idx = jnp.arange(2 * HALF + 1)
    picks = (offset[:, :, None] == taps_idx[None, None, :]).astype(jnp.float32)
    band = jnp.einsum("ijt,kt->kij", picks, filters.astype(jnp.float32))
    return band.astype(jnp.bfloat16)


def any_device(template, science, plan, orders, coadd_weight, intersection):
    row_filters, col_filters = make_filters(orders)
    rows = template.shape[1]
    width = template.shape[2]
    blocks_count = width // 128
    steps_count = science.shape[1]
    row_band = band_matrix(row_filters, rows, rows + 2 * HALF)
    col_band = jnp.transpose(band_matrix(col_filters, 128, 128 + 2 * HALF), (0, 2, 1))
    column_pos = 2.0 * (jnp.arange(width).astype(jnp.float32) + 0.5) / width - 1.0
    pieces = []
    fitted = []
    for step in range(steps_count):
        received = broadcast(template[0], "expo", plan[step])
        padded = extended(received, (("tile", 0),), HALF)
        rowconv = jnp.einsum(
            "kij,jw->kiw", row_band, padded, preferred_element_type=jnp.float32
        ).astype(jnp.bfloat16)
        blocks = rowconv.reshape(NB, rows, blocks_count, 128)
        empty_rim = jnp.zeros((NB, rows, 1, HALF), jnp.bfloat16)
        previous = jnp.concatenate([empty_rim, blocks[:, :, :-1, 128 - HALF :]], axis=2)
        following = jnp.concatenate([blocks[:, :, 1:, :HALF], empty_rim], axis=2)
        window = jnp.concatenate([previous, blocks, following], axis=3)
        conv = jnp.einsum("krbj,kjc->krbc", window, col_band, preferred_element_type=jnp.float32)
        conv = conv.reshape(NB, rows, width)
        fields = jnp.concatenate(
            [conv, conv * column_pos, jnp.ones((1, rows, width), jnp.float32)], axis=0
        )
        fields = fields.reshape(NU, rows * width)
        exposure_image = science[0, step].astype(jnp.float32).reshape(rows * width)
        normal_local = jnp.dot(fields, fields.T, precision=lax.Precision.HIGHEST)
        project_local = jnp.dot(fields, exposure_image, precision=lax.Precision.HIGHEST)
        normal_matrix, projections = lax.psum((normal_local, project_local), "tile")
        normal_matrix = normal_matrix + RIDGE * (jnp.trace(normal_matrix) / NU) * jnp.eye(
            NU, dtype=jnp.float32
        )
        factor = jnp.linalg.cholesky(normal_matrix)
        coeffs = jax.scipy.linalg.cho_solve((factor, True), projections)
        model = jnp.dot(coeffs, fields, precision=lax.Precision.HIGHEST)
        difference = exposure_image - model
        weight_now = coadd_weight[0, step] * intersection[0, step].astype(jnp.float32)
        pieces.append((weight_now * difference).reshape(rows, width))
        fitted.append(coeffs)
    weighted = jnp.stack(pieces)
    received_parts = lax.all_to_all(weighted[None], "expo", split_axis=3, concat_axis=0, tiled=True)
    coadd = jnp.sum(received_parts, axis=0)
    return (coadd, jnp.stack(fitted)[None])


def per_device(template, science, plan, orders, coadd_weight, intersection):
    expos = lax.axis_size("expo")
    rows, width = template.shape[1:]
    whole_lanes = width % (expos * LANES) == 0 and rows % 16 == 0 and 3 * rows <= LANES
    few = (NU + 1) * expos <= LANES and NU + expos <= LANES
    body = tiled_device if whole_lanes and few else any_device
    return body(template, science, plan, orders, coadd_weight, intersection)


def solution(mesh):
    return jax.shard_map(
        per_device,
        mesh=mesh,
        in_specs=(
            P(("groups", "expo"), "tile", None),
            P(("groups", "expo"), None, "tile", None),
            P("groups"),
            P(),
            P(("groups", "expo"), None),
            P(("groups", "expo"), None),
        ),
        out_specs=(P("groups", "tile", "expo"), P(("groups", "expo"), None, None)),
        check_vma=False,
    )
```

```python
import functools

import jax
import jax.numpy as jnp
import numpy as np
from jax import lax
from jax.experimental import pallas as pl
from jax.experimental.pallas import tpu as pltpu
from jax.sharding import PartitionSpec as P

HALF = 15
NB = 6
NU = 13
LANES = 128
BEYOND = 1000
PAIRS = [(j, k) for j in range(NB) for k in range(j, NB)]

SIGMAS = (0.8, 1.4, 2.2, 3.0, 4.0, 5.5)
RIDGE = 0.05


def power_of(pos, order):
    return jnp.where(order == 0, 1.0, jnp.where(order == 1, pos, pos * pos))


def tap_values(pos, sigma, order):
    value = jnp.exp(-pos * pos / (2.0 * sigma * sigma)) * power_of(pos, order)
    return jnp.where(jnp.abs(pos) <= HALF, value, 0.0)


def tap_norm(sigma, order):
    pos = lax.broadcasted_iota(jnp.int32, (8, LANES), 1).astype(jnp.float32) - HALF
    value = tap_values(pos, sigma, order)
    return jnp.sqrt(jnp.sum(value * value, axis=1, keepdims=True))


def target(me, shift, size):
    return me ^ shift if size & (size - 1) == 0 else (me + shift) % size


def source(me, shift, size):
    return me ^ shift if size & (size - 1) == 0 else (me - shift + size) % size


def joint(shift, size):
    return shift in (0, size - 1)


def template_order(size):
    return [*range(size - 1, 0, -1), 0]


def send_kernel(template_ref, science_ref, plan_ref, orders_ref, *refs, step):
    *out_refs, owner_ref, order_ref, patch_ref, plan_now, orders_now, sems = refs
    size = sems.shape[0] - 4
    rows, width = science_ref.shape
    chunk = width // size
    ext = chunk + LANES
    patch_refs, apart = out_refs[:size], out_refs[size:]
    image_refs = [
        patch_refs[shift].at[:, pl.ds(ext, chunk)] if joint(shift, size) else apart.pop(0).at[:, pl.ds(0, chunk)]
        for shift in range(size)
    ]
    half = size * chunk // 2
    me = lax.axis_index("expo")
    starts = [pl.multiple_of(target(me, shift, size) * chunk, chunk) for shift in range(size)]
    loads = [
        pltpu.make_async_copy(
            template_ref.at[:, pl.ds(i * half, half)], patch_ref.at[:, pl.ds((i * half + LANES), half)], sems.at[i]
        )
        for i in range(2)
    ]
    copies = [
        pltpu.make_async_copy(
            science_ref.at[:, pl.ds(starts[shift], chunk)],
            image_refs[shift],
            sems.at[3 + shift],
        )
        for shift in range(size)
    ]
    copies.append(pltpu.make_async_copy(plan_ref, plan_now, sems.at[2]))
    copies.append(pltpu.make_async_copy(orders_ref, orders_now, sems.at[3 + size]))
    for copy in loads + copies:
        copy.start()
    blank = jnp.zeros((rows, LANES), patch_ref.dtype)
    patch_ref[:, :LANES] = blank
    patch_ref[:, size * chunk + LANES :] = blank
    for ref in out_refs[size:]:
        ref[:, chunk:] = blank
    for copy in loads:
        copy.wait()
    lane = lax.broadcasted_iota(jnp.int32, (rows, LANES), 1)
    for shift in range(size):
        start = starts[shift]
        patch_refs[shift][:, :chunk] = patch_ref[:, pl.ds(start + LANES, chunk)]
        before = patch_ref[:, pl.ds(start, LANES)].astype(jnp.float32)
        after = patch_ref[:, pl.ds(start + chunk + LANES, LANES)].astype(jnp.float32)
        rim = jnp.where(lane < LANES // 2, after, before)
        patch_refs[shift][:, chunk:ext] = rim.astype(patch_ref.dtype)
    for copy in copies:
        copy.wait()
    owner_ref[...] = jnp.full(owner_ref.shape, plan_now[step], jnp.int32)
    for way in range(2):
        for k in range(NB):
            order_ref[way, k] = jnp.full((8, LANES), orders_now[way, k], jnp.int32)


def pick_kernel(owner_ref, *refs):
    *recv_refs, out_ref, block_ref = refs
    ext = out_ref.shape[1]
    size = len(recv_refs)
    me = lax.axis_index("expo")
    order = template_order(size)
    for b in range(ext // LANES):
        columns = slice(b * LANES, (b + 1) * LANES)
        block = recv_refs[-1][:, columns].astype(jnp.float32)
        for shift, ref in zip(order[:-1], recv_refs):
            block = jnp.where(
                owner_ref[...] == source(me, shift, size), ref[:, columns].astype(jnp.float32), block
            )
        block_ref[:, columns] = block.astype(out_ref.dtype)
    whole = jnp.concatenate([block_ref[:, ext - LANES :], block_ref[...]], axis=1)
    out_ref[...] = whole[:, LANES - HALF : LANES - HALF + ext]


def column_positions(first_col, block, width):
    col = lax.broadcasted_iota(jnp.int32, (8, LANES), 1) + (first_col + block * LANES)
    return 2.0 * (col.astype(jnp.float32) + 0.5) / width - 1.0


def band_kernel(order_ref, _, row_ref, col_ref, *, tiles):
    rows = row_ref.shape[0] // NB
    tile_at = lax.axis_index("tile")
    near = 1 - 2 * lax.rem(tile_at, 2)
    near_move = jnp.where(tile_at + near < tiles, near - 1, BEYOND)
    far_move = jnp.where((tile_at >= near) & (tile_at - near < tiles), -near - 2, BEYOND)
    row_from = lax.broadcasted_iota(jnp.int32, (8, LANES), 1)
    moved = jnp.where(row_from < rows, 0, jnp.where(row_from < 2 * rows, near_move, far_move))
    sub = lax.broadcasted_iota(jnp.int32, (8, LANES), 0)
    lane = lax.broadcasted_iota(jnp.int32, (8, LANES), 1)
    shift = (sub - jnp.where(lane < LANES // 2, lane, lane - LANES) - HALF).astype(jnp.float32)
    for k in range(NB):
        norm = tap_norm(SIGMAS[k], order_ref[0, k])
        for r in range(0, rows, 16):
            parts = []
            for half in (r, r + 8):
                offset = (row_from + moved * rows - sub - half).astype(jnp.float32)
                parts.append(tap_values(offset, SIGMAS[k], order_ref[0, k]) / norm)
            both = jnp.concatenate(parts, axis=0).astype(jnp.bfloat16)
            row_ref[k * rows + r : k * rows + r + 16] = both[:, : 3 * rows]
        norm = tap_norm(SIGMAS[k], order_ref[1, k])
        pattern = tap_values(shift, SIGMAS[k], order_ref[1, k]) / norm
        for r in range(0, 2 * LANES, 16):
            parts = []
            for half in (r, r + 8):
                moved_on = pltpu.roll(pattern, half % LANES, 1) if half % LANES else pattern
                inside = lane <= half + 7 if half < LANES else lane >= half - LANES + LANES // 2
                parts.append(jnp.where(inside, moved_on, 0.0))
            col_ref[k, r : r + 16] = jnp.concatenate(parts, axis=0).astype(jnp.bfloat16)


def image_blocks(ref, size, shift, chunk):
    first = chunk + LANES if joint(shift, size) else 0
    return lambda b: ref[:, first + b * LANES : first + (b + 1) * LANES].astype(jnp.float32)


def fit_kernel(weight_ref, hits_ref, row_band_ref, col_band_ref, own_ref, near_ref, far_ref, *refs, width):
    *image_refs, conv_ref, sums_ref, row_ref, parts_ref = refs
    tile_at = lax.axis_index("tile")
    expo_at = lax.axis_index("expo")
    rows, ext = own_ref.shape
    expos = len(image_refs)
    chunk = ext - LANES
    blocks = chunk // LANES

    patch = jnp.concatenate([own_ref[...], near_ref[...], far_ref[...]], axis=0)
    row_ref[...] = jnp.dot(
        row_band_ref[...], patch, preferred_element_type=jnp.float32
    ).astype(jnp.bfloat16)
    for k in range(NB):
        window = jnp.concatenate(
            [
                row_ref[k * rows : (k + 1) * rows, b * LANES : (b + 2) * LANES]
                for b in range(blocks)
            ],
            axis=0,
        )
        out = jnp.dot(window, col_band_ref[k], preferred_element_type=jnp.float32)
        conv_ref[k] = out.reshape(blocks, rows, LANES)

    first_col = expo_at * chunk
    xs = [column_positions(first_col, b, width) for b in range(blocks)]

    def fold(x):
        total = x[:8]
        for i in range(8, rows, 8):
            total = total + x[i : i + 8]
        return total

    def moments(at, left, right, count):
        total = [None] * count
        for b in range(blocks):
            term = fold(left(b) * right(b)) if right is not None else fold(left(b))
            for i in range(count):
                total[i] = term if total[i] is None else total[i] + term
                if i < count - 1:
                    term = term * xs[b]
        for i in range(count):
            parts_ref[at + i] = total[i]

    def conv(k):
        return lambda b: conv_ref[k, b]

    def sci(shift):
        return image_blocks(image_refs[shift], expos, shift, chunk)

    blank = jnp.zeros((8, LANES), jnp.float32)
    at = 0
    for j, k in PAIRS:
        moments(at, conv(j), conv(k), 3)
        at += 3
    for k in range(NB):
        moments(at, conv(k), None, 2)
        at += 2
    while at % 8:
        parts_ref[at] = blank
        at += 1
    begin = at
    for shift in range(expos):
        row = at + NU * source(expo_at, shift, expos)
        for k in range(NB):
            moments(row + 2 * k, conv(k), sci(shift), 2)
        moments(row + NU - 1, sci(shift), None, 1)
    at += NU * expos
    weight = jnp.broadcast_to(weight_ref[...] * hits_ref[...].astype(jnp.float32), (8, LANES))
    weight = jnp.where(tile_at == 0, weight, 0.0)
    spot = (
        (lax.broadcasted_iota(jnp.int32, (8, LANES), 0) == 0)
        & (lax.broadcasted_iota(jnp.int32, (8, LANES), 1) == 0)
    )
    for e in range(expos):
        parts_ref[at + e] = jnp.where(spot & (expo_at == e), weight, 0.0)
    at += expos
    while at % 8:
        parts_ref[at] = blank
        at += 1
    ones = jnp.ones((8, LANES), jnp.float32)
    rows_of = []
    for first, last in ((0, begin), (begin, at)):
        lanes = jnp.sum(parts_ref[first:last], axis=1)
        spare = LANES - (last - first)
        if spare:
            lanes = jnp.concatenate([lanes, jnp.zeros((spare, LANES), jnp.float32)], axis=0)
        rows_of.append(
            lax.dot_general(
                ones,
                lanes,
                (((1,), (1,)), ((), ())),
                precision=lax.Precision.HIGHEST,
                preferred_element_type=jnp.float32,
            )
        )
    both = jnp.where(lax.broadcasted_iota(jnp.int32, (8, LANES), 0) < 4, rows_of[0], rows_of[1])
    for i in range(sums_ref.shape[0]):
        sums_ref[i] = both


def table(expos):
    columns = np.zeros((NU + expos + 1, 16), np.int32)
    for at, (j, k) in enumerate(PAIRS):
        for a, b in ((j, k), (k, j)):
            columns[b, a] = 3 * at
            columns[NB + b, a] = columns[b, NB + a] = 3 * at + 1
            columns[NB + b, NB + a] = 3 * at + 2
    for k in range(NB):
        for x in range(2):
            columns[NU - 1, x * NB + k] = columns[x * NB + k, NU - 1] = 3 * len(PAIRS) + 2 * k + x
    for e in range(expos):
        columns[NU + e, :NU] = [NU * e + 2 * k + x for x in range(2) for k in range(NB)] + [NU * e + NU - 1]
        columns[NU + expos, e] = NU * expos + e
    return np.ascontiguousarray(np.broadcast_to(columns[:, :, None], columns.shape + (LANES,)))


def solve_kernel(table_ref, sums_ref, conv_ref, *refs, width, pixels):
    *image_refs, coadd_ref, coeffs_ref, tile_ref, sems = refs
    expo_at = lax.axis_index("expo")
    expos = len(image_refs)
    rows, chunk = coadd_ref.shape
    blocks = chunk // LANES
    images = [image_blocks(ref, expos, shift, chunk) for shift, ref in enumerate(image_refs)]
    sub = lax.broadcasted_iota(jnp.int32, (16, LANES), 0)
    lane = lax.broadcasted_iota(jnp.int32, (16, LANES), 1)
    sums = sums_ref[0]
    for i in range(1, sums_ref.shape[0]):
        sums = sums + sums_ref[i]
    first = jnp.broadcast_to(sums[0:1], (16, LANES))
    second = jnp.broadcast_to(sums[4:5], (16, LANES))

    columns = [
        jnp.take_along_axis(first if j < NU else second, table_ref[j], axis=1) for j in range(NU + expos)
    ]
    spread = jnp.take_along_axis(second, table_ref[NU + expos], axis=1)
    weight = [jnp.broadcast_to(spread[e : e + 1], (16, LANES)) for e in range(expos)]
    columns[NU - 1] = jnp.where(sub == NU - 1, float(pixels), columns[NU - 1])

    trace = columns[0][0:1]
    for j in range(1, NU):
        trace = trace + columns[j][j : j + 1]
    scale = 1.0 / trace
    for j in range(NU + expos):
        columns[j] = columns[j] * scale
        if j < NU:
            columns[j] = columns[j] + jnp.where(sub == j, RIDGE / NU, 0.0)
    for i in range(NU):
        inverse = 1.0 / columns[i][i : i + 1]
        for j in range(i + 1, NU + expos):
            factor = columns[j][i : i + 1] * inverse
            columns[j] = jnp.where(sub == i, factor, columns[j] - columns[i] * factor)

    solved = columns[NU:]
    own = solved[0]
    mixed = weight[0] * solved[0]
    for e in range(1, expos):
        own = jnp.where(expo_at == e, solved[e], own)
        mixed = mixed + weight[e] * solved[e]
    diagonal = (sub == lane) & (sub < NU)
    coeffs_ref[...] = jnp.sum(jnp.where(diagonal, own, 0.0), axis=0, keepdims=True)[:, :NU]
    scale = [jnp.broadcast_to(mixed[u : u + 1], (8, LANES)) for u in range(NU)]
    gains = []
    for shift in range(expos):
        gain = weight[0][:8]
        for e in range(1, expos):
            gain = jnp.where(source(expo_at, shift, expos) == e, weight[e][:8], gain)
        gains.append(gain)
    first_col = expo_at * chunk
    copies = []
    for r in range(0, rows, 8):
        for b in range(blocks):
            x = column_positions(first_col, b, width)
            total = -scale[NU - 1]
            for gain, image in zip(gains, images):
                total = total + gain * image(b)[r : r + 8]
            model = (scale[0] + scale[NB] * x) * conv_ref[0, b, r : r + 8]
            for k in range(1, NB):
                model = model + (scale[k] + scale[NB + k] * x) * conv_ref[k, b, r : r + 8]
            tile_ref[r : r + 8, b * LANES : (b + 1) * LANES] = total - model
        copies.append(
            pltpu.make_async_copy(tile_ref.at[pl.ds(r, 8)], coadd_ref.at[pl.ds(r, 8)], sems.at[r // 8])
        )
        copies[-1].start()
    for copy in copies:
        copy.wait()


def swaps(first, size):
    pairs = [(i, i + 1) for i in range(first, size - 1, 2)]
    if first and size % 2 == 0:
        pairs.append((0, size - 1))
    return [pair for a, b in pairs for pair in ((a, b), (b, a))]


def service_order(expos, tiles):
    early = list(range(tiles // 2))
    late = list(reversed(range(expos // 2 * tiles, expos * tiles)))
    return early + [i for i in late if i not in early] + list(range(len(early), expos // 2 * tiles))


def tiled_device(template, science, plan, orders, coadd_weight, intersection):
    expos = lax.axis_size("expo")
    tiles = lax.axis_size("tile")
    _, rows, width = template.shape
    steps = science.shape[1]
    chunk = width // expos
    ext = chunk + LANES
    blocks = chunk // LANES
    vmem = pl.BlockSpec(memory_space=pltpu.VMEM)
    small = pltpu.CompilerParams(vmem_limit_bytes=16 * 1024 * 1024)
    hbm = pl.BlockSpec(memory_space=pltpu.HBM)
    coadds = []
    fitted = []
    for step in range(steps):
        apart = sum(not joint(shift, expos) for shift in range(expos))
        *blocks_out, owner, order = pl.pallas_call(
            functools.partial(send_kernel, step=step),
            out_shape=tuple(
                pltpu.VMEM((rows, ext + chunk if joint(shift, expos) else ext), template.dtype)
                for shift in range(expos)
            )
            + (pltpu.VMEM((rows, ext), science.dtype),) * apart
            + (
                jax.ShapeDtypeStruct((rows, LANES), jnp.int32),
                jax.ShapeDtypeStruct((2, NB, 8, LANES), jnp.int32),
            ),
            in_specs=[hbm] * 4,
            out_specs=(vmem,) * (expos + apart + 2),
            scratch_shapes=[
                pltpu.VMEM((rows, width + 2 * LANES), template.dtype),
                pltpu.SMEM(plan.shape, jnp.int32),
                pltpu.SMEM((2, NB), jnp.int32),
                pltpu.SemaphoreType.DMA((expos + 4,)),
            ],
            compiler_params=small,
        )(
            pltpu.with_memory_space_constraint(template[0], pltpu.HBM),
            pltpu.with_memory_space_constraint(science[0, step], pltpu.HBM),
            pltpu.with_memory_space_constraint(plan, pltpu.HBM),
            pltpu.with_memory_space_constraint(orders.T, pltpu.HBM),
        )
        patches, images = [], []
        for shift in range(expos):
            pairs = [(e, int(target(e, shift, expos))) for e in range(expos)]
            patches.append(lax.ppermute(blocks_out[shift], "expo", pairs) if shift else blocks_out[shift])
        blocks_out = blocks_out[expos:]
        for shift in range(expos):
            pairs = [(e, int(target(e, shift, expos))) for e in range(expos)]
            images.append(
                patches[shift] if joint(shift, expos) else lax.ppermute(blocks_out.pop(0), "expo", pairs)
            )
        own = pl.pallas_call(
            pick_kernel,
            out_shape=jax.ShapeDtypeStruct((rows, ext), template.dtype),
            in_specs=[vmem] * (1 + expos),
            out_specs=vmem,
            scratch_shapes=[pltpu.VMEM((rows, ext), template.dtype)],
            compiler_params=small,
        )(owner, *(patches[shift] for shift in template_order(expos)))
        row_band, col_band = pl.pallas_call(
            functools.partial(band_kernel, tiles=tiles),
            out_shape=(
                jax.ShapeDtypeStruct((NB * rows, 3 * rows), jnp.bfloat16),
                jax.ShapeDtypeStruct((NB, 2 * LANES, LANES), jnp.bfloat16),
            ),
            in_specs=[vmem, pl.BlockSpec(memory_space=pl.ANY)],
            out_specs=(vmem, vmem),
            compiler_params=small,
            cost_estimate=pl.CostEstimate(flops=4_000_000, bytes_accessed=500_000, transcendentals=200_000),
        )(order, own)
        far = lax.ppermute(own, "tile", swaps(1, tiles))
        near = lax.ppermute(own, "tile", swaps(0, tiles))
        conv, sums = pl.pallas_call(
            functools.partial(fit_kernel, width=width),
            out_shape=(
                jax.ShapeDtypeStruct((NB, blocks, rows, LANES), jnp.float32),
                jax.ShapeDtypeStruct((tiles * expos, 8, LANES), jnp.float32),
            ),
            in_specs=[vmem] * (7 + expos),
            out_specs=(vmem, vmem),
            scratch_shapes=[
                pltpu.VMEM((NB * rows, ext), jnp.bfloat16),
                pltpu.VMEM((80 + 14 * expos + 8, 8, LANES), jnp.float32),
            ],
            compiler_params=small,
        )(
            coadd_weight[:, step : step + 1],
            intersection[:, step : step + 1],
            row_band,
            col_band,
            own,
            near,
            far,
            *images,
        )
        group = list(reversed(service_order(expos, tiles)))
        sums = lax.all_to_all(
            sums, ("expo", "tile"), split_axis=0, concat_axis=0, tiled=True, axis_index_groups=[group]
        )
        coadd, coeffs = pl.pallas_call(
            functools.partial(solve_kernel, width=width, pixels=tiles * rows * width),
            out_shape=(
                jax.ShapeDtypeStruct((rows, chunk), jnp.float32),
                jax.ShapeDtypeStruct((1, NU), jnp.float32),
            ),
            in_specs=[vmem] * (3 + expos),
            out_specs=(pl.BlockSpec(memory_space=pl.ANY), vmem),
            scratch_shapes=[
                pltpu.VMEM((rows, chunk), jnp.float32),
                pltpu.SemaphoreType.DMA((rows // 8,)),
            ],
            compiler_params=small,
        )(jnp.asarray(table(expos)), sums, conv, *images)
        coadds.append(coadd[None])
        fitted.append(coeffs)
    return (jnp.concatenate(coadds), jnp.stack(fitted, axis=1))


def broadcast(block, axis, holder):
    block = jnp.where(lax.axis_index(axis) == holder, block, jnp.zeros_like(block))
    return lax.psum(block, axis)


def extended(x, sides, width):
    for axis, dim in sides:
        size, length = (lax.axis_size(axis), x.shape[dim])
        up = [(i, (i + 1) % size) for i in range(size - 1)]
        down = [(j, i) for i, j in up]
        last = lax.slice_in_dim(x, length - width, length, axis=dim)
        first = lax.slice_in_dim(x, 0, width, axis=dim)
        before = lax.ppermute(last, axis, up)
        after = lax.ppermute(first, axis, down)
        x = jnp.concatenate([before, x, after], axis=dim)
    return x


def make_filters(orders):
    taps_pos = jnp.arange(2 * HALF + 1).astype(jnp.float32) - HALF
    row_list = []
    col_list = []
    for basis in range(NB):
        sigma = SIGMAS[basis]
        envelope = jnp.exp(-taps_pos * taps_pos / (2.0 * sigma * sigma))
        row_filter = envelope * power_of(taps_pos, orders[basis, 0])
        col_filter = envelope * power_of(taps_pos, orders[basis, 1])
        row_list.append(row_filter / jnp.sqrt(jnp.sum(row_filter * row_filter)))
        col_list.append(col_filter / jnp.sqrt(jnp.sum(col_filter * col_filter)))
    return (jnp.stack(row_list).astype(jnp.bfloat16), jnp.stack(col_list).astype(jnp.bfloat16))


def band_matrix(filters, out_len, in_len):
    offset = jnp.arange(in_len)[None, :] - jnp.arange(out_len)[:, None]
    taps_idx = jnp.arange(2 * HALF + 1)
    picks = (offset[:, :, None] == taps_idx[None, None, :]).astype(jnp.float32)
    band = jnp.einsum("ijt,kt->kij", picks, filters.astype(jnp.float32))
    return band.astype(jnp.bfloat16)


def any_device(template, science, plan, orders, coadd_weight, intersection):
    row_filters, col_filters = make_filters(orders)
    rows = template.shape[1]
    width = template.shape[2]
    blocks_count = width // 128
    steps_count = science.shape[1]
    row_band = band_matrix(row_filters, rows, rows + 2 * HALF)
    col_band = jnp.transpose(band_matrix(col_filters, 128, 128 + 2 * HALF), (0, 2, 1))
    column_pos = 2.0 * (jnp.arange(width).astype(jnp.float32) + 0.5) / width - 1.0
    pieces = []
    fitted = []
    for step in range(steps_count):
        received = broadcast(template[0], "expo", plan[step])
        padded = extended(received, (("tile", 0),), HALF)
        rowconv = jnp.einsum(
            "kij,jw->kiw", row_band, padded, preferred_element_type=jnp.float32
        ).astype(jnp.bfloat16)
        blocks = rowconv.reshape(NB, rows, blocks_count, 128)
        empty_rim = jnp.zeros((NB, rows, 1, HALF), jnp.bfloat16)
        previous = jnp.concatenate([empty_rim, blocks[:, :, :-1, 128 - HALF :]], axis=2)
        following = jnp.concatenate([blocks[:, :, 1:, :HALF], empty_rim], axis=2)
        window = jnp.concatenate([previous, blocks, following], axis=3)
        conv = jnp.einsum("krbj,kjc->krbc", window, col_band, preferred_element_type=jnp.float32)
        conv = conv.reshape(NB, rows, width)
        fields = jnp.concatenate(
            [conv, conv * column_pos, jnp.ones((1, rows, width), jnp.float32)], axis=0
        )
        fields = fields.reshape(NU, rows * width)
        exposure_image = science[0, step].astype(jnp.float32).reshape(rows * width)
        normal_local = jnp.dot(fields, fields.T, precision=lax.Precision.HIGHEST)
        project_local = jnp.dot(fields, exposure_image, precision=lax.Precision.HIGHEST)
        normal_matrix, projections = lax.psum((normal_local, project_local), "tile")
        normal_matrix = normal_matrix + RIDGE * (jnp.trace(normal_matrix) / NU) * jnp.eye(
            NU, dtype=jnp.float32
        )
        factor = jnp.linalg.cholesky(normal_matrix)
        coeffs = jax.scipy.linalg.cho_solve((factor, True), projections)
        model = jnp.dot(coeffs, fields, precision=lax.Precision.HIGHEST)
        difference = exposure_image - model
        weight_now = coadd_weight[0, step] * intersection[0, step].astype(jnp.float32)
        pieces.append((weight_now * difference).reshape(rows, width))
        fitted.append(coeffs)
    weighted = jnp.stack(pieces)
    received_parts = lax.all_to_all(weighted[None], "expo", split_axis=3, concat_axis=0, tiled=True)
    coadd = jnp.sum(received_parts, axis=0)
    return (coadd, jnp.stack(fitted)[None])


def per_device(template, science, plan, orders, coadd_weight, intersection):
    expos = lax.axis_size("expo")
    rows, width = template.shape[1:]
    whole_lanes = width % (expos * LANES) == 0 and rows % 16 == 0 and 3 * rows <= LANES
    few = (NU + 1) * expos <= LANES and NU + expos <= LANES
    body = tiled_device if whole_lanes and few else any_device
    return body(template, science, plan, orders, coadd_weight, intersection)


def solution(mesh):
    return jax.shard_map(
        per_device,
        mesh=mesh,
        in_specs=(
            P(("groups", "expo"), "tile", None),
            P(("groups", "expo"), None, "tile", None),
            P("groups"),
            P(),
            P(("groups", "expo"), None),
            P(("groups", "expo"), None),
        ),
        out_specs=(P("groups", "tile", "expo"), P(("groups", "expo"), None, None)),
        check_vma=False,
    )
```

```python
import functools

import jax
import jax.numpy as jnp
import numpy as np
from jax import lax
from jax.experimental import pallas as pl
from jax.experimental.pallas import tpu as pltpu
from jax.sharding import PartitionSpec as P

HALF = 15
NB = 6
NU = 13
LANES = 128
BEYOND = 1000
STAGE_COST = 700_000_000
PAIRS = [(j, k) for j in range(NB) for k in range(j, NB)]

SIGMAS = (0.8, 1.4, 2.2, 3.0, 4.0, 5.5)
RIDGE = 0.05


def power_of(pos, order):
    return jnp.where(order == 0, 1.0, jnp.where(order == 1, pos, pos * pos))


def tap_values(pos, sigma, order):
    value = jnp.exp(-pos * pos / (2.0 * sigma * sigma)) * power_of(pos, order)
    return jnp.where(jnp.abs(pos) <= HALF, value, 0.0)


def tap_norm(sigma, order):
    pos = lax.broadcasted_iota(jnp.int32, (8, LANES), 1).astype(jnp.float32) - HALF
    value = tap_values(pos, sigma, order)
    return jnp.sqrt(jnp.sum(value * value, axis=1, keepdims=True))


def target(me, shift, size):
    return me ^ shift if size & (size - 1) == 0 else (me + shift) % size


def source(me, shift, size):
    return me ^ shift if size & (size - 1) == 0 else (me - shift + size) % size


def far_first(size):
    return [*range(size - 1, 0, -1), 0]


def middle_first(size):
    return [*range(size // 2, size), *range(1, size // 2), 0] if size > 1 else [0]


def joint(shift, size):
    return shift < size // 2


def send_kernel(template_ref, science_ref, plan_ref, orders_ref, *refs, step):
    *out_refs, owner_ref, order_ref, patch_ref, plan_now, orders_now, sems = refs
    size = sems.shape[0] - 4
    rows, width = science_ref.shape
    chunk = width // size
    ext = chunk + LANES
    patch_refs, image_refs = out_refs[:size], out_refs[size:]
    half = size * chunk // 2
    me = lax.axis_index("expo")
    starts = [pl.multiple_of(target(me, shift, size) * chunk, chunk) for shift in range(size)]
    loads = [
        pltpu.make_async_copy(
            template_ref.at[:, pl.ds(i * half, half)], patch_ref.at[:, pl.ds((i * half + LANES), half)], sems.at[i]
        )
        for i in range(2)
    ]
    copies = [
        pltpu.make_async_copy(
            science_ref.at[:, pl.ds(starts[shift], chunk)],
            patch_refs[shift].at[:, pl.ds(ext, chunk)]
            if joint(shift, size)
            else image_refs[shift - size // 2].at[:, pl.ds(0, chunk)],
            sems.at[3 + shift],
        )
        for shift in range(size)
    ]
    copies.append(pltpu.make_async_copy(plan_ref, plan_now, sems.at[2]))
    copies.append(pltpu.make_async_copy(orders_ref, orders_now, sems.at[3 + size]))
    for copy in loads + copies:
        copy.start()
    blank = jnp.zeros((rows, LANES), patch_ref.dtype)
    patch_ref[:, :LANES] = blank
    patch_ref[:, size * chunk + LANES :] = blank
    for image_ref in image_refs:
        image_ref[:, chunk:] = blank
    for copy in loads:
        copy.wait()
    lane = lax.broadcasted_iota(jnp.int32, (rows, LANES), 1)
    for shift in range(size):
        start = starts[shift]
        patch_refs[shift][:, :chunk] = patch_ref[:, pl.ds(start + LANES, chunk)]
        before = patch_ref[:, pl.ds(start, LANES)].astype(jnp.float32)
        after = patch_ref[:, pl.ds(start + chunk + LANES, LANES)].astype(jnp.float32)
        rim = jnp.where(lane < LANES // 2, after, before)
        patch_refs[shift][:, chunk:ext] = rim.astype(patch_ref.dtype)
    for copy in copies:
        copy.wait()
    owner_ref[...] = jnp.full(owner_ref.shape, plan_now[step], jnp.int32)
    for way in range(2):
        for k in range(NB):
            order_ref[way, k] = jnp.full((8, LANES), orders_now[way, k], jnp.int32)


def choose_kernel(owner_ref, *refs, shifts, size):
    *recv_refs, out_ref = refs
    me = lax.axis_index("expo")
    for b in range(out_ref.shape[1] // LANES):
        columns = slice(b * LANES, (b + 1) * LANES)
        block = recv_refs[0][:, columns].astype(jnp.float32)
        for shift, ref in zip(shifts, recv_refs[1:]):
            block = jnp.where(
                owner_ref[...] == source(me, shift, size), ref[:, columns].astype(jnp.float32), block
            )
        out_ref[:, columns] = block.astype(out_ref.dtype)


def pick_kernel(owner_ref, *refs, shifts, size):
    *recv_refs, out_ref, block_ref = refs
    ext = out_ref.shape[1]
    choose_kernel(owner_ref, *recv_refs, block_ref, shifts=shifts, size=size)
    whole = jnp.concatenate([block_ref[:, ext - LANES :], block_ref[...]], axis=1)
    out_ref[...] = whole[:, LANES - HALF : LANES - HALF + ext]


def column_positions(first_col, block, width):
    col = lax.broadcasted_iota(jnp.int32, (8, LANES), 1) + (first_col + block * LANES)
    return 2.0 * (col.astype(jnp.float32) + 0.5) / width - 1.0


def band_kernel(order_ref, _, row_ref, col_ref, *, tiles):
    rows = row_ref.shape[0] // NB
    tile_at = lax.axis_index("tile")
    near = 1 - 2 * lax.rem(tile_at, 2)
    near_move = jnp.where(tile_at + near < tiles, near - 1, BEYOND)
    far_move = jnp.where((tile_at >= near) & (tile_at - near < tiles), -near - 2, BEYOND)
    row_from = lax.broadcasted_iota(jnp.int32, (8, LANES), 1)
    moved = jnp.where(row_from < rows, 0, jnp.where(row_from < 2 * rows, near_move, far_move))
    sub = lax.broadcasted_iota(jnp.int32, (8, LANES), 0)
    lane = lax.broadcasted_iota(jnp.int32, (8, LANES), 1)
    shift = (sub - jnp.where(lane < LANES // 2, lane, lane - LANES) - HALF).astype(jnp.float32)
    for k in range(NB):
        norm = tap_norm(SIGMAS[k], order_ref[0, k])
        for r in range(0, rows, 16):
            parts = []
            for half in (r, r + 8):
                offset = (row_from + moved * rows - sub - half).astype(jnp.float32)
                parts.append(tap_values(offset, SIGMAS[k], order_ref[0, k]) / norm)
            both = jnp.concatenate(parts, axis=0).astype(jnp.bfloat16)
            row_ref[k * rows + r : k * rows + r + 16] = both[:, : 3 * rows]
        norm = tap_norm(SIGMAS[k], order_ref[1, k])
        pattern = tap_values(shift, SIGMAS[k], order_ref[1, k]) / norm
        for r in range(0, 2 * LANES, 16):
            parts = []
            for half in (r, r + 8):
                moved_on = pltpu.roll(pattern, half % LANES, 1) if half % LANES else pattern
                inside = lane <= half + 7 if half < LANES else lane >= half - LANES + LANES // 2
                parts.append(jnp.where(inside, moved_on, 0.0))
            col_ref[k, r : r + 16] = jnp.concatenate(parts, axis=0).astype(jnp.bfloat16)


def image_blocks(ref, size, shift, chunk):
    first = chunk + LANES if joint(shift, size) else 0
    return lambda b: ref[:, first + b * LANES : first + (b + 1) * LANES].astype(jnp.float32)


def fit_kernel(weight_ref, hits_ref, row_band_ref, col_band_ref, own_ref, near_ref, far_ref, *refs, width):
    *image_refs, conv_ref, sums_ref, row_ref, parts_ref = refs
    image_refs = dict(zip(middle_first(len(image_refs)), image_refs))
    tile_at = lax.axis_index("tile")
    expo_at = lax.axis_index("expo")
    rows, ext = own_ref.shape
    expos = len(image_refs)
    chunk = ext - LANES
    blocks = chunk // LANES

    patch = jnp.concatenate([own_ref[...], near_ref[...], far_ref[...]], axis=0)
    row_ref[...] = jnp.dot(
        row_band_ref[...], patch, preferred_element_type=jnp.float32
    ).astype(jnp.bfloat16)
    for k in range(NB):
        window = jnp.concatenate(
            [
                row_ref[k * rows : (k + 1) * rows, b * LANES : (b + 2) * LANES]
                for b in range(blocks)
            ],
            axis=0,
        )
        out = jnp.dot(window, col_band_ref[k], preferred_element_type=jnp.float32)
        conv_ref[k] = out.reshape(blocks, rows, LANES)

    first_col = expo_at * chunk
    xs = [column_positions(first_col, b, width) for b in range(blocks)]

    def fold(x):
        total = x[:8]
        for i in range(8, rows, 8):
            total = total + x[i : i + 8]
        return total

    def moments(at, left, right, count):
        total = [None] * count
        for b in range(blocks):
            term = fold(left(b) * right(b)) if right is not None else fold(left(b))
            for i in range(count):
                total[i] = term if total[i] is None else total[i] + term
                if i < count - 1:
                    term = term * xs[b]
        for i in range(count):
            parts_ref[at + i] = total[i]

    def conv(k):
        return lambda b: conv_ref[k, b]

    def sci(shift):
        return image_blocks(image_refs[shift], expos, shift, chunk)

    blank = jnp.zeros((8, LANES), jnp.float32)
    at = 0
    for j, k in PAIRS:
        moments(at, conv(j), conv(k), 3)
        at += 3
    for k in range(NB):
        moments(at, conv(k), None, 2)
        at += 2
    while at % 8:
        parts_ref[at] = blank
        at += 1
    begin = at
    for shift in range(expos):
        row = at + NU * source(expo_at, shift, expos)
        for k in range(NB):
            moments(row + 2 * k, conv(k), sci(shift), 2)
        moments(row + NU - 1, sci(shift), None, 1)
    at += NU * expos
    weight = jnp.broadcast_to(weight_ref[...] * hits_ref[...].astype(jnp.float32), (8, LANES))
    weight = jnp.where(tile_at == 0, weight, 0.0)
    spot = (
        (lax.broadcasted_iota(jnp.int32, (8, LANES), 0) == 0)
        & (lax.broadcasted_iota(jnp.int32, (8, LANES), 1) == 0)
    )
    for e in range(expos):
        parts_ref[at + e] = jnp.where(spot & (expo_at == e), weight, 0.0)
    at += expos
    while at % 8:
        parts_ref[at] = blank
        at += 1
    ones = jnp.ones((8, LANES), jnp.float32)
    rows_of = []
    for first, last in ((0, begin), (begin, at)):
        lanes = jnp.sum(parts_ref[first:last], axis=1)
        spare = LANES - (last - first)
        if spare:
            lanes = jnp.concatenate([lanes, jnp.zeros((spare, LANES), jnp.float32)], axis=0)
        rows_of.append(
            lax.dot_general(
                ones,
                lanes,
                (((1,), (1,)), ((), ())),
                precision=lax.Precision.HIGHEST,
                preferred_element_type=jnp.float32,
            )
        )
    both = jnp.where(lax.broadcasted_iota(jnp.int32, (8, LANES), 0) < 4, rows_of[0], rows_of[1])
    for i in range(sums_ref.shape[0]):
        sums_ref[i] = both


def table(expos):
    columns = np.zeros((NU + expos + 1, 16), np.int32)
    for at, (j, k) in enumerate(PAIRS):
        for a, b in ((j, k), (k, j)):
            columns[b, a] = 3 * at
            columns[NB + b, a] = columns[b, NB + a] = 3 * at + 1
            columns[NB + b, NB + a] = 3 * at + 2
    for k in range(NB):
        for x in range(2):
            columns[NU - 1, x * NB + k] = columns[x * NB + k, NU - 1] = 3 * len(PAIRS) + 2 * k + x
    for e in range(expos):
        columns[NU + e, :NU] = [NU * e + 2 * k + x for x in range(2) for k in range(NB)] + [NU * e + NU - 1]
        columns[NU + expos, e] = NU * expos + e
    return np.ascontiguousarray(np.broadcast_to(columns[:, :, None], columns.shape + (LANES,)))


def solve_kernel(table_ref, sums_ref, conv_ref, *refs, width, pixels):
    *image_refs, coadd_ref, coeffs_ref, tile_ref, sems = refs
    expo_at = lax.axis_index("expo")
    expos = len(image_refs)
    rows, chunk = coadd_ref.shape
    blocks = chunk // LANES
    images = [image_blocks(ref, expos, shift, chunk) for shift, ref in enumerate(image_refs)]
    sub = lax.broadcasted_iota(jnp.int32, (16, LANES), 0)
    lane = lax.broadcasted_iota(jnp.int32, (16, LANES), 1)
    sums = sums_ref[0]
    for i in range(1, sums_ref.shape[0]):
        sums = sums + sums_ref[i]
    first = jnp.broadcast_to(sums[0:1], (16, LANES))
    second = jnp.broadcast_to(sums[4:5], (16, LANES))

    columns = [
        jnp.take_along_axis(first if j < NU else second, table_ref[j], axis=1) for j in range(NU + expos)
    ]
    spread = jnp.take_along_axis(second, table_ref[NU + expos], axis=1)
    weight = [jnp.broadcast_to(spread[e : e + 1], (16, LANES)) for e in range(expos)]
    columns[NU - 1] = jnp.where(sub == NU - 1, float(pixels), columns[NU - 1])

    trace = columns[0][0:1]
    for j in range(1, NU):
        trace = trace + columns[j][j : j + 1]
    scale = 1.0 / trace
    for j in range(NU + expos):
        columns[j] = columns[j] * scale
        if j < NU:
            columns[j] = columns[j] + jnp.where(sub == j, RIDGE / NU, 0.0)
    for i in range(NU):
        inverse = 1.0 / columns[i][i : i + 1]
        for j in range(i + 1, NU + expos):
            factor = columns[j][i : i + 1] * inverse
            columns[j] = jnp.where(sub == i, factor, columns[j] - columns[i] * factor)

    solved = columns[NU:]
    own = solved[0]
    mixed = weight[0] * solved[0]
    for e in range(1, expos):
        own = jnp.where(expo_at == e, solved[e], own)
        mixed = mixed + weight[e] * solved[e]
    diagonal = (sub == lane) & (sub < NU)
    coeffs_ref[...] = jnp.sum(jnp.where(diagonal, own, 0.0), axis=0, keepdims=True)[:, :NU]
    scale = [jnp.broadcast_to(mixed[u : u + 1], (8, LANES)) for u in range(NU)]
    gains = []
    for shift in range(expos):
        gain = weight[0][:8]
        for e in range(1, expos):
            gain = jnp.where(source(expo_at, shift, expos) == e, weight[e][:8], gain)
        gains.append(gain)
    first_col = expo_at * chunk
    copies = []
    for r in range(0, rows, 8):
        for b in range(blocks):
            x = column_positions(first_col, b, width)
            total = -scale[NU - 1]
            for gain, image in zip(gains, images):
                total = total + gain * image(b)[r : r + 8]
            model = (scale[0] + scale[NB] * x) * conv_ref[0, b, r : r + 8]
            for k in range(1, NB):
                model = model + (scale[k] + scale[NB + k] * x) * conv_ref[k, b, r : r + 8]
            tile_ref[r : r + 8, b * LANES : (b + 1) * LANES] = total - model
        copies.append(
            pltpu.make_async_copy(tile_ref.at[pl.ds(r, 8)], coadd_ref.at[pl.ds(r, 8)], sems.at[r // 8])
        )
        copies[-1].start()
    for copy in copies:
        copy.wait()


def swaps(first, size):
    pairs = [(i, i + 1) for i in range(first, size - 1, 2)]
    if first and size % 2 == 0:
        pairs.append((0, size - 1))
    return [pair for a, b in pairs for pair in ((a, b), (b, a))]


def service_order(expos, tiles):
    early = list(range(tiles // 2))
    late = list(reversed(range(expos // 2 * tiles, expos * tiles)))
    return early + [i for i in late if i not in early] + list(range(len(early), expos // 2 * tiles))


def tiled_device(template, science, plan, orders, coadd_weight, intersection):
    expos = lax.axis_size("expo")
    tiles = lax.axis_size("tile")
    _, rows, width = template.shape
    steps = science.shape[1]
    chunk = width // expos
    ext = chunk + LANES
    blocks = chunk // LANES
    vmem = pl.BlockSpec(memory_space=pltpu.VMEM)
    small = pltpu.CompilerParams(vmem_limit_bytes=16 * 1024 * 1024)
    hbm = pl.BlockSpec(memory_space=pltpu.HBM)
    coadds = []
    fitted = []
    for step in range(steps):
        *blocks_out, owner, order = pl.pallas_call(
            functools.partial(send_kernel, step=step),
            out_shape=tuple(
                pltpu.VMEM((rows, ext + chunk if joint(shift, expos) else ext), template.dtype)
                for shift in range(expos)
            )
            + (pltpu.VMEM((rows, ext), science.dtype),) * (expos - expos // 2)
            + (
                jax.ShapeDtypeStruct((rows, LANES), jnp.int32),
                jax.ShapeDtypeStruct((2, NB, 8, LANES), jnp.int32),
            ),
            in_specs=[hbm] * 4,
            out_specs=(vmem,) * (2 * expos - expos // 2 + 2),
            scratch_shapes=[
                pltpu.VMEM((rows, width + 2 * LANES), template.dtype),
                pltpu.SMEM(plan.shape, jnp.int32),
                pltpu.SMEM((2, NB), jnp.int32),
                pltpu.SemaphoreType.DMA((expos + 4,)),
            ],
            compiler_params=small,
        )(
            pltpu.with_memory_space_constraint(template[0], pltpu.HBM),
            pltpu.with_memory_space_constraint(science[0, step], pltpu.HBM),
            pltpu.with_memory_space_constraint(plan, pltpu.HBM),
            pltpu.with_memory_space_constraint(orders.T, pltpu.HBM),
        )
        patches, images = blocks_out[:expos], blocks_out[expos:]
        for group, first in ((patches, 0), (images, expos // 2)):
            for shift in range(max(first, 1), expos):
                pairs = [(e, int(target(e, shift, expos))) for e in range(expos)]
                group[shift - first] = lax.ppermute(group[shift - first], "expo", pairs)
        images = patches[: expos // 2] + images
        across = [shift for shift in far_first(expos)[:-1] if not joint(shift, expos)]
        beside = [shift for shift in far_first(expos)[:-1] if joint(shift, expos)]
        block = pl.pallas_call(
            functools.partial(choose_kernel, shifts=across, size=expos),
            out_shape=jax.ShapeDtypeStruct((rows, ext), template.dtype),
            in_specs=[vmem] * (2 + len(across)),
            out_specs=vmem,
            compiler_params=small,
            cost_estimate=pl.CostEstimate(flops=STAGE_COST, bytes_accessed=500_000, transcendentals=0),
        )(owner, patches[0], *(patches[shift] for shift in across))
        own = pl.pallas_call(
            functools.partial(pick_kernel, shifts=beside, size=expos),
            out_shape=jax.ShapeDtypeStruct((rows, ext), template.dtype),
            in_specs=[vmem] * (2 + len(beside)),
            out_specs=vmem,
            scratch_shapes=[pltpu.VMEM((rows, ext), template.dtype)],
            compiler_params=small,
        )(owner, block, *(patches[shift] for shift in beside))
        row_band, col_band = pl.pallas_call(
            functools.partial(band_kernel, tiles=tiles),
            out_shape=(
                jax.ShapeDtypeStruct((NB * rows, 3 * rows), jnp.bfloat16),
                jax.ShapeDtypeStruct((NB, 2 * LANES, LANES), jnp.bfloat16),
            ),
            in_specs=[vmem, pl.BlockSpec(memory_space=pl.ANY)],
            out_specs=(vmem, vmem),
            compiler_params=small,
            cost_estimate=pl.CostEstimate(flops=4_000_000, bytes_accessed=500_000, transcendentals=200_000),
        )(order, own)
        far = lax.ppermute(own, "tile", swaps(1, tiles))
        near = lax.ppermute(own, "tile", swaps(0, tiles))
        conv, sums = pl.pallas_call(
            functools.partial(fit_kernel, width=width),
            out_shape=(
                jax.ShapeDtypeStruct((NB, blocks, rows, LANES), jnp.float32),
                jax.ShapeDtypeStruct((tiles * expos, 8, LANES), jnp.float32),
            ),
            in_specs=[vmem] * (7 + expos),
            out_specs=(vmem, vmem),
            scratch_shapes=[
                pltpu.VMEM((NB * rows, ext), jnp.bfloat16),
                pltpu.VMEM((80 + 14 * expos + 8, 8, LANES), jnp.float32),
            ],
            compiler_params=small,
        )(
            coadd_weight[:, step : step + 1],
            intersection[:, step : step + 1],
            row_band,
            col_band,
            own,
            near,
            far,
            *(images[shift] for shift in middle_first(expos)),
        )
        group = list(reversed(service_order(expos, tiles)))
        sums = lax.all_to_all(
            sums, ("expo", "tile"), split_axis=0, concat_axis=0, tiled=True, axis_index_groups=[group]
        )
        coadd, coeffs = pl.pallas_call(
            functools.partial(solve_kernel, width=width, pixels=tiles * rows * width),
            out_shape=(
                jax.ShapeDtypeStruct((rows, chunk), jnp.float32),
                jax.ShapeDtypeStruct((1, NU), jnp.float32),
            ),
            in_specs=[vmem] * (3 + expos),
            out_specs=(pl.BlockSpec(memory_space=pl.ANY), vmem),
            scratch_shapes=[
                pltpu.VMEM((rows, chunk), jnp.float32),
                pltpu.SemaphoreType.DMA((rows // 8,)),
            ],
            compiler_params=small,
        )(jnp.asarray(table(expos)), sums, conv, *images)
        coadds.append(coadd[None])
        fitted.append(coeffs)
    return (jnp.concatenate(coadds), jnp.stack(fitted, axis=1))


def broadcast(block, axis, holder):
    block = jnp.where(lax.axis_index(axis) == holder, block, jnp.zeros_like(block))
    return lax.psum(block, axis)


def extended(x, sides, width):
    for axis, dim in sides:
        size, length = (lax.axis_size(axis), x.shape[dim])
        up = [(i, (i + 1) % size) for i in range(size - 1)]
        down = [(j, i) for i, j in up]
        last = lax.slice_in_dim(x, length - width, length, axis=dim)
        first = lax.slice_in_dim(x, 0, width, axis=dim)
        before = lax.ppermute(last, axis, up)
        after = lax.ppermute(first, axis, down)
        x = jnp.concatenate([before, x, after], axis=dim)
    return x


def make_filters(orders):
    taps_pos = jnp.arange(2 * HALF + 1).astype(jnp.float32) - HALF
    row_list = []
    col_list = []
    for basis in range(NB):
        sigma = SIGMAS[basis]
        envelope = jnp.exp(-taps_pos * taps_pos / (2.0 * sigma * sigma))
        row_filter = envelope * power_of(taps_pos, orders[basis, 0])
        col_filter = envelope * power_of(taps_pos, orders[basis, 1])
        row_list.append(row_filter / jnp.sqrt(jnp.sum(row_filter * row_filter)))
        col_list.append(col_filter / jnp.sqrt(jnp.sum(col_filter * col_filter)))
    return (jnp.stack(row_list).astype(jnp.bfloat16), jnp.stack(col_list).astype(jnp.bfloat16))


def band_matrix(filters, out_len, in_len):
    offset = jnp.arange(in_len)[None, :] - jnp.arange(out_len)[:, None]
    taps_idx = jnp.arange(2 * HALF + 1)
    picks = (offset[:, :, None] == taps_idx[None, None, :]).astype(jnp.float32)
    band = jnp.einsum("ijt,kt->kij", picks, filters.astype(jnp.float32))
    return band.astype(jnp.bfloat16)


def any_device(template, science, plan, orders, coadd_weight, intersection):
    row_filters, col_filters = make_filters(orders)
    rows = template.shape[1]
    width = template.shape[2]
    blocks_count = width // 128
    steps_count = science.shape[1]
    row_band = band_matrix(row_filters, rows, rows + 2 * HALF)
    col_band = jnp.transpose(band_matrix(col_filters, 128, 128 + 2 * HALF), (0, 2, 1))
    column_pos = 2.0 * (jnp.arange(width).astype(jnp.float32) + 0.5) / width - 1.0
    pieces = []
    fitted = []
    for step in range(steps_count):
        received = broadcast(template[0], "expo", plan[step])
        padded = extended(received, (("tile", 0),), HALF)
        rowconv = jnp.einsum(
            "kij,jw->kiw", row_band, padded, preferred_element_type=jnp.float32
        ).astype(jnp.bfloat16)
        blocks = rowconv.reshape(NB, rows, blocks_count, 128)
        empty_rim = jnp.zeros((NB, rows, 1, HALF), jnp.bfloat16)
        previous = jnp.concatenate([empty_rim, blocks[:, :, :-1, 128 - HALF :]], axis=2)
        following = jnp.concatenate([blocks[:, :, 1:, :HALF], empty_rim], axis=2)
        window = jnp.concatenate([previous, blocks, following], axis=3)
        conv = jnp.einsum("krbj,kjc->krbc", window, col_band, preferred_element_type=jnp.float32)
        conv = conv.reshape(NB, rows, width)
        fields = jnp.concatenate(
            [conv, conv * column_pos, jnp.ones((1, rows, width), jnp.float32)], axis=0
        )
        fields = fields.reshape(NU, rows * width)
        exposure_image = science[0, step].astype(jnp.float32).reshape(rows * width)
        normal_local = jnp.dot(fields, fields.T, precision=lax.Precision.HIGHEST)
        project_local = jnp.dot(fields, exposure_image, precision=lax.Precision.HIGHEST)
        normal_matrix, projections = lax.psum((normal_local, project_local), "tile")
        normal_matrix = normal_matrix + RIDGE * (jnp.trace(normal_matrix) / NU) * jnp.eye(
            NU, dtype=jnp.float32
        )
        factor = jnp.linalg.cholesky(normal_matrix)
        coeffs = jax.scipy.linalg.cho_solve((factor, True), projections)
        model = jnp.dot(coeffs, fields, precision=lax.Precision.HIGHEST)
        difference = exposure_image - model
        weight_now = coadd_weight[0, step] * intersection[0, step].astype(jnp.float32)
        pieces.append((weight_now * difference).reshape(rows, width))
        fitted.append(coeffs)
    weighted = jnp.stack(pieces)
    received_parts = lax.all_to_all(weighted[None], "expo", split_axis=3, concat_axis=0, tiled=True)
    coadd = jnp.sum(received_parts, axis=0)
    return (coadd, jnp.stack(fitted)[None])


def per_device(template, science, plan, orders, coadd_weight, intersection):
    expos = lax.axis_size("expo")
    rows, width = template.shape[1:]
    whole_lanes = width % (expos * LANES) == 0 and rows % 16 == 0 and 3 * rows <= LANES
    few = (NU + 1) * expos <= LANES and NU + expos <= LANES
    body = tiled_device if whole_lanes and few else any_device
    return body(template, science, plan, orders, coadd_weight, intersection)


def solution(mesh):
    return jax.shard_map(
        per_device,
        mesh=mesh,
        in_specs=(
            P(("groups", "expo"), "tile", None),
            P(("groups", "expo"), None, "tile", None),
            P("groups"),
            P(),
            P(("groups", "expo"), None),
            P(("groups", "expo"), None),
        ),
        out_specs=(P("groups", "tile", "expo"), P(("groups", "expo"), None, None)),
        check_vma=False,
    )
```

```python
import functools

import jax
import jax.numpy as jnp
import numpy as np
from jax import lax
from jax.experimental import pallas as pl
from jax.experimental.pallas import tpu as pltpu
from jax.sharding import PartitionSpec as P

HALF = 15
NB = 6
NU = 13
LANES = 128
BEYOND = 1000
STAGE_COST = 700_000_000
PAIRS = [(j, k) for j in range(NB) for k in range(j, NB)]

SIGMAS = (0.8, 1.4, 2.2, 3.0, 4.0, 5.5)
RIDGE = 0.05


def power_of(pos, order):
    return jnp.where(order == 0, 1.0, jnp.where(order == 1, pos, pos * pos))


def tap_values(pos, sigma, order):
    value = jnp.exp(-pos * pos / (2.0 * sigma * sigma)) * power_of(pos, order)
    return jnp.where(jnp.abs(pos) <= HALF, value, 0.0)


def tap_norm(sigma, order):
    pos = lax.broadcasted_iota(jnp.int32, (8, LANES), 1).astype(jnp.float32) - HALF
    value = tap_values(pos, sigma, order)
    return jnp.sqrt(jnp.sum(value * value, axis=1, keepdims=True))


def target(me, shift, size):
    return me ^ shift if size & (size - 1) == 0 else (me + shift) % size


def source(me, shift, size):
    return me ^ shift if size & (size - 1) == 0 else (me - shift + size) % size


def far_first(size):
    return [*range(size - 1, 0, -1), 0]


def joint(shift, size):
    return shift < size // 2


def send_kernel(template_ref, science_ref, plan_ref, orders_ref, *refs, step):
    *out_refs, owner_ref, order_ref, patch_ref, plan_now, orders_now, sems = refs
    size = sems.shape[0] - 4
    rows, width = science_ref.shape
    chunk = width // size
    ext = chunk + LANES
    patch_refs, image_refs = out_refs[:size], out_refs[size:]
    half = size * chunk // 2
    me = lax.axis_index("expo")
    starts = [pl.multiple_of(target(me, shift, size) * chunk, chunk) for shift in range(size)]
    loads = [
        pltpu.make_async_copy(
            template_ref.at[:, pl.ds(i * half, half)], patch_ref.at[:, pl.ds((i * half + LANES), half)], sems.at[i]
        )
        for i in range(2)
    ]
    copies = [
        pltpu.make_async_copy(
            science_ref.at[:, pl.ds(starts[shift], chunk)],
            patch_refs[shift].at[:, pl.ds(ext, chunk)]
            if joint(shift, size)
            else image_refs[shift - size // 2].at[:, pl.ds(0, chunk)],
            sems.at[3 + shift],
        )
        for shift in range(size)
    ]
    copies.append(pltpu.make_async_copy(plan_ref, plan_now, sems.at[2]))
    copies.append(pltpu.make_async_copy(orders_ref, orders_now, sems.at[3 + size]))
    for copy in loads + copies:
        copy.start()
    blank = jnp.zeros((rows, LANES), patch_ref.dtype)
    patch_ref[:, :LANES] = blank
    patch_ref[:, size * chunk + LANES :] = blank
    for image_ref in image_refs:
        image_ref[:, chunk:] = blank
    for copy in loads:
        copy.wait()
    lane = lax.broadcasted_iota(jnp.int32, (rows, LANES), 1)
    for shift in range(size):
        start = starts[shift]
        patch_refs[shift][:, :chunk] = patch_ref[:, pl.ds(start + LANES, chunk)]
        before = patch_ref[:, pl.ds(start, LANES)].astype(jnp.float32)
        after = patch_ref[:, pl.ds(start + chunk + LANES, LANES)].astype(jnp.float32)
        rim = jnp.where(lane < LANES // 2, after, before)
        patch_refs[shift][:, chunk:ext] = rim.astype(patch_ref.dtype)
    for copy in copies:
        copy.wait()
    owner_ref[...] = jnp.full(owner_ref.shape, plan_now[step], jnp.int32)
    for way in range(2):
        for k in range(NB):
            order_ref[way, k] = jnp.full((8, LANES), orders_now[way, k], jnp.int32)


def choose_kernel(owner_ref, *refs, shifts, size):
    *recv_refs, out_ref = refs
    me = lax.axis_index("expo")
    for b in range(out_ref.shape[1] // LANES):
        columns = slice(b * LANES, (b + 1) * LANES)
        block = recv_refs[0][:, columns].astype(jnp.float32)
        for shift, ref in zip(shifts, recv_refs[1:]):
            block = jnp.where(
                owner_ref[...] == source(me, shift, size), ref[:, columns].astype(jnp.float32), block
            )
        out_ref[:, columns] = block.astype(out_ref.dtype)


def pick_kernel(owner_ref, *refs, shifts, size):
    *recv_refs, out_ref, block_ref = refs
    ext = out_ref.shape[1]
    choose_kernel(owner_ref, *recv_refs, block_ref, shifts=shifts, size=size)
    whole = jnp.concatenate([block_ref[:, ext - LANES :], block_ref[...]], axis=1)
    out_ref[...] = whole[:, LANES - HALF : LANES - HALF + ext]


def column_positions(first_col, block, width):
    col = lax.broadcasted_iota(jnp.int32, (8, LANES), 1) + (first_col + block * LANES)
    return 2.0 * (col.astype(jnp.float32) + 0.5) / width - 1.0


def band_kernel(order_ref, _, row_ref, col_ref, *, tiles):
    rows = row_ref.shape[0] // NB
    tile_at = lax.axis_index("tile")
    near = 1 - 2 * lax.rem(tile_at, 2)
    near_move = jnp.where(tile_at + near < tiles, near - 1, BEYOND)
    far_move = jnp.where((tile_at >= near) & (tile_at - near < tiles), -near - 2, BEYOND)
    row_from = lax.broadcasted_iota(jnp.int32, (8, LANES), 1)
    moved = jnp.where(row_from < rows, 0, jnp.where(row_from < 2 * rows, near_move, far_move))
    sub = lax.broadcasted_iota(jnp.int32, (8, LANES), 0)
    lane = lax.broadcasted_iota(jnp.int32, (8, LANES), 1)
    shift = (sub - jnp.where(lane < LANES // 2, lane, lane - LANES) - HALF).astype(jnp.float32)
    for k in range(NB):
        norm = tap_norm(SIGMAS[k], order_ref[0, k])
        for r in range(0, rows, 16):
            parts = []
            for half in (r, r + 8):
                offset = (row_from + moved * rows - sub - half).astype(jnp.float32)
                parts.append(tap_values(offset, SIGMAS[k], order_ref[0, k]) / norm)
            both = jnp.concatenate(parts, axis=0).astype(jnp.bfloat16)
            row_ref[k * rows + r : k * rows + r + 16] = both[:, : 3 * rows]
        norm = tap_norm(SIGMAS[k], order_ref[1, k])
        pattern = tap_values(shift, SIGMAS[k], order_ref[1, k]) / norm
        for r in range(0, 2 * LANES, 16):
            parts = []
            for half in (r, r + 8):
                moved_on = pltpu.roll(pattern, half % LANES, 1) if half % LANES else pattern
                inside = lane <= half + 7 if half < LANES else lane >= half - LANES + LANES // 2
                parts.append(jnp.where(inside, moved_on, 0.0))
            col_ref[k, r : r + 16] = jnp.concatenate(parts, axis=0).astype(jnp.bfloat16)


def image_blocks(ref, size, shift, chunk):
    first = chunk + LANES if joint(shift, size) else 0
    return lambda b: ref[:, first + b * LANES : first + (b + 1) * LANES].astype(jnp.float32)


def fit_kernel(weight_ref, hits_ref, row_band_ref, col_band_ref, own_ref, near_ref, far_ref, *refs, width):
    *image_refs, conv_ref, sums_ref, row_ref, parts_ref = refs
    image_refs = dict(zip(far_first(len(image_refs)), image_refs))
    tile_at = lax.axis_index("tile")
    expo_at = lax.axis_index("expo")
    rows, ext = own_ref.shape
    expos = len(image_refs)
    chunk = ext - LANES
    blocks = chunk // LANES

    patch = jnp.concatenate([own_ref[...], near_ref[...], far_ref[...]], axis=0)
    row_ref[...] = jnp.dot(
        row_band_ref[...], patch, preferred_element_type=jnp.float32
    ).astype(jnp.bfloat16)
    for k in range(NB):
        window = jnp.concatenate(
            [
                row_ref[k * rows : (k + 1) * rows, b * LANES : (b + 2) * LANES]
                for b in range(blocks)
            ],
            axis=0,
        )
        out = jnp.dot(window, col_band_ref[k], preferred_element_type=jnp.float32)
        conv_ref[k] = out.reshape(blocks, rows, LANES)

    first_col = expo_at * chunk
    xs = [column_positions(first_col, b, width) for b in range(blocks)]

    def fold(x):
        total = x[:8]
        for i in range(8, rows, 8):
            total = total + x[i : i + 8]
        return total

    def moments(at, left, right, count):
        total = [None] * count
        for b in range(blocks):
            term = fold(left(b) * right(b)) if right is not None else fold(left(b))
            for i in range(count):
                total[i] = term if total[i] is None else total[i] + term
                if i < count - 1:
                    term = term * xs[b]
        for i in range(count):
            parts_ref[at + i] = total[i]

    def conv(k):
        return lambda b: conv_ref[k, b]

    def sci(shift):
        return image_blocks(image_refs[shift], expos, shift, chunk)

    blank = jnp.zeros((8, LANES), jnp.float32)
    at = 0
    for j, k in PAIRS:
        moments(at, conv(j), conv(k), 3)
        at += 3
    for k in range(NB):
        moments(at, conv(k), None, 2)
        at += 2
    while at % 8:
        parts_ref[at] = blank
        at += 1
    begin = at
    for shift in range(expos):
        row = at + NU * source(expo_at, shift, expos)
        for k in range(NB):
            moments(row + 2 * k, conv(k), sci(shift), 2)
        moments(row + NU - 1, sci(shift), None, 1)
    at += NU * expos
    weight = jnp.broadcast_to(weight_ref[...] * hits_ref[...].astype(jnp.float32), (8, LANES))
    weight = jnp.where(tile_at == 0, weight, 0.0)
    spot = (
        (lax.broadcasted_iota(jnp.int32, (8, LANES), 0) == 0)
        & (lax.broadcasted_iota(jnp.int32, (8, LANES), 1) == 0)
    )
    for e in range(expos):
        parts_ref[at + e] = jnp.where(spot & (expo_at == e), weight, 0.0)
    at += expos
    while at % 8:
        parts_ref[at] = blank
        at += 1
    lanes = []
    for first, last in ((0, begin), (begin, at)):
        lanes.append(jnp.sum(parts_ref[first:last], axis=1))
        if last - first < LANES:
            lanes.append(jnp.zeros((LANES - (last - first), LANES), jnp.float32))
    rest = jnp.concatenate(lanes, axis=0)
    thirds = []
    for _ in range(3):
        thirds.append(rest.astype(jnp.bfloat16))
        rest = rest - thirds[-1].astype(jnp.float32)
    line = lax.dot_general(
        jnp.ones((16, 3 * LANES), jnp.bfloat16),
        jnp.concatenate(thirds, axis=1),
        (((1,), (1,)), ((), ())),
        preferred_element_type=jnp.float32,
    )[:8]
    both = jnp.where(lax.broadcasted_iota(jnp.int32, (8, LANES), 0) < 4, line[:, :LANES], line[:, LANES:])
    for i in range(sums_ref.shape[0]):
        sums_ref[i] = both


def table(expos):
    columns = np.zeros((NU + expos + 1, 16), np.int32)
    for at, (j, k) in enumerate(PAIRS):
        for a, b in ((j, k), (k, j)):
            columns[b, a] = 3 * at
            columns[NB + b, a] = columns[b, NB + a] = 3 * at + 1
            columns[NB + b, NB + a] = 3 * at + 2
    for k in range(NB):
        for x in range(2):
            columns[NU - 1, x * NB + k] = columns[x * NB + k, NU - 1] = 3 * len(PAIRS) + 2 * k + x
    for e in range(expos):
        columns[NU + e, :NU] = [NU * e + 2 * k + x for x in range(2) for k in range(NB)] + [NU * e + NU - 1]
        columns[NU + expos, e] = NU * expos + e
    return np.ascontiguousarray(np.broadcast_to(columns[:, :, None], columns.shape + (LANES,)))


def solve_kernel(table_ref, sums_ref, conv_ref, *refs, width, pixels):
    *image_refs, coadd_ref, coeffs_ref, tile_ref, sems = refs
    expo_at = lax.axis_index("expo")
    expos = len(image_refs)
    rows, chunk = coadd_ref.shape
    blocks = chunk // LANES
    images = [image_blocks(ref, expos, shift, chunk) for shift, ref in enumerate(image_refs)]
    sub = lax.broadcasted_iota(jnp.int32, (16, LANES), 0)
    lane = lax.broadcasted_iota(jnp.int32, (16, LANES), 1)
    sums = sums_ref[0]
    for i in range(1, sums_ref.shape[0]):
        sums = sums + sums_ref[i]
    first = jnp.broadcast_to(sums[0:1], (16, LANES))
    second = jnp.broadcast_to(sums[4:5], (16, LANES))

    columns = [
        jnp.take_along_axis(first if j < NU else second, table_ref[j], axis=1) for j in range(NU + expos)
    ]
    spread = jnp.take_along_axis(second, table_ref[NU + expos], axis=1)
    weight = [jnp.broadcast_to(spread[e : e + 1], (16, LANES)) for e in range(expos)]
    columns[NU - 1] = jnp.where(sub == NU - 1, float(pixels), columns[NU - 1])

    trace = columns[0][0:1]
    for j in range(1, NU):
        trace = trace + columns[j][j : j + 1]
    scale = 1.0 / trace
    for j in range(NU + expos):
        columns[j] = columns[j] * scale
        if j < NU:
            columns[j] = columns[j] + jnp.where(sub == j, RIDGE / NU, 0.0)
    for i in range(NU):
        inverse = 1.0 / columns[i][i : i + 1]
        for j in range(i + 1, NU + expos):
            factor = columns[j][i : i + 1] * inverse
            columns[j] = jnp.where(sub == i, factor, columns[j] - columns[i] * factor)

    solved = columns[NU:]
    own = solved[0]
    mixed = weight[0] * solved[0]
    for e in range(1, expos):
        own = jnp.where(expo_at == e, solved[e], own)
        mixed = mixed + weight[e] * solved[e]
    diagonal = (sub == lane) & (sub < NU)
    coeffs_ref[...] = jnp.sum(jnp.where(diagonal, own, 0.0), axis=0, keepdims=True)[:, :NU]
    scale = [jnp.broadcast_to(mixed[u : u + 1], (8, LANES)) for u in range(NU)]
    gains = []
    for shift in range(expos):
        gain = weight[0][:8]
        for e in range(1, expos):
            gain = jnp.where(source(expo_at, shift, expos) == e, weight[e][:8], gain)
        gains.append(gain)
    first_col = expo_at * chunk
    copies = []
    for r in range(0, rows, 8):
        for b in range(blocks):
            x = column_positions(first_col, b, width)
            total = -scale[NU - 1]
            for gain, image in zip(gains, images):
                total = total + gain * image(b)[r : r + 8]
            model = (scale[0] + scale[NB] * x) * conv_ref[0, b, r : r + 8]
            for k in range(1, NB):
                model = model + (scale[k] + scale[NB + k] * x) * conv_ref[k, b, r : r + 8]
            tile_ref[r : r + 8, b * LANES : (b + 1) * LANES] = total - model
        copies.append(
            pltpu.make_async_copy(tile_ref.at[pl.ds(r, 8)], coadd_ref.at[pl.ds(r, 8)], sems.at[r // 8])
        )
        copies[-1].start()
    for copy in copies:
        copy.wait()


def swaps(first, size):
    pairs = [(i, i + 1) for i in range(first, size - 1, 2)]
    if first and size % 2 == 0:
        pairs.append((0, size - 1))
    return [pair for a, b in pairs for pair in ((a, b), (b, a))]


def service_order(expos, tiles):
    early = list(range(tiles // 2))
    late = list(reversed(range(expos // 2 * tiles, expos * tiles)))
    return early + [i for i in late if i not in early] + list(range(len(early), expos // 2 * tiles))


def tiled_device(template, science, plan, orders, coadd_weight, intersection):
    expos = lax.axis_size("expo")
    tiles = lax.axis_size("tile")
    _, rows, width = template.shape
    steps = science.shape[1]
    chunk = width // expos
    ext = chunk + LANES
    blocks = chunk // LANES
    vmem = pl.BlockSpec(memory_space=pltpu.VMEM)
    small = pltpu.CompilerParams(vmem_limit_bytes=16 * 1024 * 1024)
    hbm = pl.BlockSpec(memory_space=pltpu.HBM)
    coadds = []
    fitted = []
    for step in range(steps):
        *blocks_out, owner, order = pl.pallas_call(
            functools.partial(send_kernel, step=step),
            out_shape=tuple(
                pltpu.VMEM((rows, ext + chunk if joint(shift, expos) else ext), template.dtype)
                for shift in range(expos)
            )
            + (pltpu.VMEM((rows, ext), science.dtype),) * (expos - expos // 2)
            + (
                jax.ShapeDtypeStruct((rows, LANES), jnp.int32),
                jax.ShapeDtypeStruct((2, NB, 8, LANES), jnp.int32),
            ),
            in_specs=[hbm] * 4,
            out_specs=(vmem,) * (2 * expos - expos // 2 + 2),
            scratch_shapes=[
                pltpu.VMEM((rows, width + 2 * LANES), template.dtype),
                pltpu.SMEM(plan.shape, jnp.int32),
                pltpu.SMEM((2, NB), jnp.int32),
                pltpu.SemaphoreType.DMA((expos + 4,)),
            ],
            compiler_params=small,
        )(
            pltpu.with_memory_space_constraint(template[0], pltpu.HBM),
            pltpu.with_memory_space_constraint(science[0, step], pltpu.HBM),
            pltpu.with_memory_space_constraint(plan, pltpu.HBM),
            pltpu.with_memory_space_constraint(orders.T, pltpu.HBM),
        )
        patches, images = blocks_out[:expos], blocks_out[expos:]
        for group, first in ((patches, 0), (images, expos // 2)):
            for shift in range(max(first, 1), expos):
                pairs = [(e, int(target(e, shift, expos))) for e in range(expos)]
                group[shift - first] = lax.ppermute(group[shift - first], "expo", pairs)
        images = patches[: expos // 2] + images
        across = [shift for shift in far_first(expos)[:-1] if not joint(shift, expos)]
        beside = [shift for shift in far_first(expos)[:-1] if joint(shift, expos)]
        block = pl.pallas_call(
            functools.partial(choose_kernel, shifts=across, size=expos),
            out_shape=jax.ShapeDtypeStruct((rows, ext), template.dtype),
            in_specs=[vmem] * (2 + len(across)),
            out_specs=vmem,
            compiler_params=small,
            cost_estimate=pl.CostEstimate(flops=STAGE_COST, bytes_accessed=500_000, transcendentals=0),
        )(owner, patches[0], *(patches[shift] for shift in across))
        own = pl.pallas_call(
            functools.partial(pick_kernel, shifts=beside, size=expos),
            out_shape=jax.ShapeDtypeStruct((rows, ext), template.dtype),
            in_specs=[vmem] * (2 + len(beside)),
            out_specs=vmem,
            scratch_shapes=[pltpu.VMEM((rows, ext), template.dtype)],
            compiler_params=small,
        )(owner, block, *(patches[shift] for shift in beside))
        row_band, col_band = pl.pallas_call(
            functools.partial(band_kernel, tiles=tiles),
            out_shape=(
                jax.ShapeDtypeStruct((NB * rows, 3 * rows), jnp.bfloat16),
                jax.ShapeDtypeStruct((NB, 2 * LANES, LANES), jnp.bfloat16),
            ),
            in_specs=[vmem, pl.BlockSpec(memory_space=pl.ANY)],
            out_specs=(vmem, vmem),
            compiler_params=small,
            cost_estimate=pl.CostEstimate(flops=4_000_000, bytes_accessed=500_000, transcendentals=200_000),
        )(order, own)
        far = lax.ppermute(own, "tile", swaps(1, tiles))
        near = lax.ppermute(own, "tile", swaps(0, tiles))
        conv, sums = pl.pallas_call(
            functools.partial(fit_kernel, width=width),
            out_shape=(
                jax.ShapeDtypeStruct((NB, blocks, rows, LANES), jnp.float32),
                jax.ShapeDtypeStruct((tiles * expos, 8, LANES), jnp.float32),
            ),
            in_specs=[vmem] * (7 + expos),
            out_specs=(vmem, vmem),
            scratch_shapes=[
                pltpu.VMEM((NB * rows, ext), jnp.bfloat16),
                pltpu.VMEM((80 + 14 * expos + 8, 8, LANES), jnp.float32),
            ],
            compiler_params=small,
        )(
            coadd_weight[:, step : step + 1],
            intersection[:, step : step + 1],
            row_band,
            col_band,
            own,
            near,
            far,
            *(images[shift] for shift in far_first(expos)),
        )
        group = list(reversed(service_order(expos, tiles)))
        sums = lax.all_to_all(
            sums, ("expo", "tile"), split_axis=0, concat_axis=0, tiled=True, axis_index_groups=[group]
        )
        coadd, coeffs = pl.pallas_call(
            functools.partial(solve_kernel, width=width, pixels=tiles * rows * width),
            out_shape=(
                jax.ShapeDtypeStruct((rows, chunk), jnp.float32),
                jax.ShapeDtypeStruct((1, NU), jnp.float32),
            ),
            in_specs=[vmem] * (3 + expos),
            out_specs=(pl.BlockSpec(memory_space=pl.ANY), vmem),
            scratch_shapes=[
                pltpu.VMEM((rows, chunk), jnp.float32),
                pltpu.SemaphoreType.DMA((rows // 8,)),
            ],
            compiler_params=small,
        )(jnp.asarray(table(expos)), sums, conv, *images)
        coadds.append(coadd[None])
        fitted.append(coeffs)
    return (jnp.concatenate(coadds), jnp.stack(fitted, axis=1))


def broadcast(block, axis, holder):
    block = jnp.where(lax.axis_index(axis) == holder, block, jnp.zeros_like(block))
    return lax.psum(block, axis)


def extended(x, sides, width):
    for axis, dim in sides:
        size, length = (lax.axis_size(axis), x.shape[dim])
        up = [(i, (i + 1) % size) for i in range(size - 1)]
        down = [(j, i) for i, j in up]
        last = lax.slice_in_dim(x, length - width, length, axis=dim)
        first = lax.slice_in_dim(x, 0, width, axis=dim)
        before = lax.ppermute(last, axis, up)
        after = lax.ppermute(first, axis, down)
        x = jnp.concatenate([before, x, after], axis=dim)
    return x


def make_filters(orders):
    taps_pos = jnp.arange(2 * HALF + 1).astype(jnp.float32) - HALF
    row_list = []
    col_list = []
    for basis in range(NB):
        sigma = SIGMAS[basis]
        envelope = jnp.exp(-taps_pos * taps_pos / (2.0 * sigma * sigma))
        row_filter = envelope * power_of(taps_pos, orders[basis, 0])
        col_filter = envelope * power_of(taps_pos, orders[basis, 1])
        row_list.append(row_filter / jnp.sqrt(jnp.sum(row_filter * row_filter)))
        col_list.append(col_filter / jnp.sqrt(jnp.sum(col_filter * col_filter)))
    return (jnp.stack(row_list).astype(jnp.bfloat16), jnp.stack(col_list).astype(jnp.bfloat16))


def band_matrix(filters, out_len, in_len):
    offset = jnp.arange(in_len)[None, :] - jnp.arange(out_len)[:, None]
    taps_idx = jnp.arange(2 * HALF + 1)
    picks = (offset[:, :, None] == taps_idx[None, None, :]).astype(jnp.float32)
    band = jnp.einsum("ijt,kt->kij", picks, filters.astype(jnp.float32))
    return band.astype(jnp.bfloat16)


def any_device(template, science, plan, orders, coadd_weight, intersection):
    row_filters, col_filters = make_filters(orders)
    rows = template.shape[1]
    width = template.shape[2]
    blocks_count = width // 128
    steps_count = science.shape[1]
    row_band = band_matrix(row_filters, rows, rows + 2 * HALF)
    col_band = jnp.transpose(band_matrix(col_filters, 128, 128 + 2 * HALF), (0, 2, 1))
    column_pos = 2.0 * (jnp.arange(width).astype(jnp.float32) + 0.5) / width - 1.0
    pieces = []
    fitted = []
    for step in range(steps_count):
        received = broadcast(template[0], "expo", plan[step])
        padded = extended(received, (("tile", 0),), HALF)
        rowconv = jnp.einsum(
            "kij,jw->kiw", row_band, padded, preferred_element_type=jnp.float32
        ).astype(jnp.bfloat16)
        blocks = rowconv.reshape(NB, rows, blocks_count, 128)
        empty_rim = jnp.zeros((NB, rows, 1, HALF), jnp.bfloat16)
        previous = jnp.concatenate([empty_rim, blocks[:, :, :-1, 128 - HALF :]], axis=2)
        following = jnp.concatenate([blocks[:, :, 1:, :HALF], empty_rim], axis=2)
        window = jnp.concatenate([previous, blocks, following], axis=3)
        conv = jnp.einsum("krbj,kjc->krbc", window, col_band, preferred_element_type=jnp.float32)
        conv = conv.reshape(NB, rows, width)
        fields = jnp.concatenate(
            [conv, conv * column_pos, jnp.ones((1, rows, width), jnp.float32)], axis=0
        )
        fields = fields.reshape(NU, rows * width)
        exposure_image = science[0, step].astype(jnp.float32).reshape(rows * width)
        normal_local = jnp.dot(fields, fields.T, precision=lax.Precision.HIGHEST)
        project_local = jnp.dot(fields, exposure_image, precision=lax.Precision.HIGHEST)
        normal_matrix, projections = lax.psum((normal_local, project_local), "tile")
        normal_matrix = normal_matrix + RIDGE * (jnp.trace(normal_matrix) / NU) * jnp.eye(
            NU, dtype=jnp.float32
        )
        factor = jnp.linalg.cholesky(normal_matrix)
        coeffs = jax.scipy.linalg.cho_solve((factor, True), projections)
        model = jnp.dot(coeffs, fields, precision=lax.Precision.HIGHEST)
        difference = exposure_image - model
        weight_now = coadd_weight[0, step] * intersection[0, step].astype(jnp.float32)
        pieces.append((weight_now * difference).reshape(rows, width))
        fitted.append(coeffs)
    weighted = jnp.stack(pieces)
    received_parts = lax.all_to_all(weighted[None], "expo", split_axis=3, concat_axis=0, tiled=True)
    coadd = jnp.sum(received_parts, axis=0)
    return (coadd, jnp.stack(fitted)[None])


def per_device(template, science, plan, orders, coadd_weight, intersection):
    expos = lax.axis_size("expo")
    rows, width = template.shape[1:]
    whole_lanes = width % (expos * LANES) == 0 and rows % 16 == 0 and 3 * rows <= LANES
    few = (NU + 1) * expos <= LANES and NU + expos <= LANES
    body = tiled_device if whole_lanes and few else any_device
    return body(template, science, plan, orders, coadd_weight, intersection)


def solution(mesh):
    return jax.shard_map(
        per_device,
        mesh=mesh,
        in_specs=(
            P(("groups", "expo"), "tile", None),
            P(("groups", "expo"), None, "tile", None),
            P("groups"),
            P(),
            P(("groups", "expo"), None),
            P(("groups", "expo"), None),
        ),
        out_specs=(P("groups", "tile", "expo"), P(("groups", "expo"), None, None)),
        check_vma=False,
    )
```
